32 devices in a mesh: section: 4 (over y, x), rows: 8 (over z, core).
Axes of the slice: x: 2, y: 2, z: 4, core: 2. Of those that a mesh axis runs over, the one named last changes fastest.
Arguments:
- images: bfloat16 [4, 2, 32, 16, 512], P(None, None, 'rows'), may hold values from -40 to 40
- switches: int32 [4, 2, 16, 8], P(None, None, 'rows'), may hold values from 0 to 3
- conv_weights: bfloat16 [4, 3, 3, 512, 512], P('section'), may hold values from -0.09375 to 0.09375
- gains: float32 [4, 512], P('section'), may hold values from 0.5 to 2
- shifts: float32 [4, 512], P('section'), may hold values from -2.5 to 2.5
- cotangent: bfloat16 [4, 2, 32, 16, 512], P(None, None, 'rows'), may hold values from -8 to 8
Outputs:
- section_outputs: bfloat16 [4, 4, 2, 32, 16, 512], P('section', None, None, 'rows')
- input_grads: bfloat16 [4, 4, 2, 32, 16, 512], P('section', None, None, 'rows')
- weight_grads: float32 [4, 3, 3, 512, 512], P('section', None, None, 'rows')
- gain_grads: float32 [4, 512], P('section')
- shift_grads: float32 [4, 512], P('section')
The draws below stay inside these ranges and needn't reach their ends.
All inputs are finite; a program needn't handle non-finite values.
Results may differ from the reference program's by a relative error of at most 0.018.
Values may be sent and summed in bfloat16 or wider, within the bound.
A program may use at most 320 MiB of HBM per device.

```python
import math
import jax
import jax.numpy as jnp
from jax import lax

C = 512
LAYERS = 4
MB = 4
IMG = 2
COLS = 16
HEIGHT = 32


def draw_images(key, part):
    key = jax.random.fold_in(key, 11)
    first_key, second_key = jax.random.split(key, 2)
    height_pos = jnp.arange(HEIGHT, dtype=jnp.float32) / (HEIGHT - 1)
    col_scale = jnp.exp(jnp.log(10.0) * (jax.random.uniform(second_key, (COLS,)) - 0.5))
    row_scale = jnp.exp(jnp.log(10.0) * (height_pos - 0.5))
    values = jnp.clip(jax.random.normal(first_key, (MB, IMG, HEIGHT, COLS, C)), -4.0, 4.0)
    scaled = values * row_scale[:, None, None] * col_scale[None, :, None]
    return scaled.astype(jnp.bfloat16)


def draw_cotangent(key, part):
    key = jax.random.fold_in(key, 23)
    first_key = jax.random.fold_in(key, 0)
    height_pos = jnp.arange(HEIGHT, dtype=jnp.float32) / (HEIGHT - 1)
    row_scale = jnp.exp(jnp.log(3.0) * (height_pos - 0.5))
    values = jnp.clip(jax.random.normal(first_key, (MB, IMG, HEIGHT, COLS, C)), -4.0, 4.0)
    scaled = values * row_scale[:, None, None]
    return scaled.astype(jnp.bfloat16)


def plant(result, own_key, least, top_value):
    index_at = [jax.random.randint(jax.random.fold_in(own_key, axis), (), 0, length) for axis, length in enumerate(result.shape)]
    longest = result.shape.index(max(result.shape))
    next_to = index_at[:longest] + [(index_at[longest] + 1) % result.shape[longest]] + index_at[longest + 1:]
    return result.at[tuple(index_at)].set(least).at[tuple(next_to)].set(top_value)


def levels(key, shape, cuts, low, high):
    factor_of = 1.0
    for axis_at, blocks in cuts:
        draws = jax.random.uniform(jax.random.fold_in(jax.random.fold_in(key, 6), axis_at), (blocks,), jnp.float32, low / len(cuts), high / len(cuts))
        factor_of = factor_of * jnp.repeat(jnp.exp(draws), shape[axis_at] // blocks).reshape((-1,) + (1,) * (len(shape) - 1 - axis_at))
    return factor_of


def gaussian(stream_key, extent, scale, reach, pieces=(), kind=jnp.bfloat16):
    values = scale * jax.random.normal(stream_key, extent, jnp.float32)
    if pieces:
        values = values * levels(stream_key, extent, pieces, -0.22, 0.18)
    return jnp.clip(values, -reach, reach).astype(kind)


def setup_inputs(seed: int = 0) -> dict:
    key_of = jax.random.split(jax.random.key(seed), 7)
    images = draw_images(jax.random.fold_in(key_of[6], 71), 0)
    switches = plant(jax.random.randint(key_of[1], (MB, IMG, HEIGHT // 2, COLS // 2), 0, 4), jax.random.fold_in(key_of[1], 1), 0, 3).astype(jnp.int32)
    conv_weights = gaussian(key_of[2], (LAYERS, 3, 3, C, C), (9 * C) ** -0.5, 0.09375, ((0, 4),))
    gains = jnp.clip(jnp.exp(math.log(2.0) - 1.3862944 * jax.random.uniform(key_of[3], (LAYERS, C), jnp.float32) ** levels(key_of[3], (LAYERS, C), ((0, 4),), -0.2, 0.2)), 0.5, 2.0)
    shifts = gaussian(key_of[4], (LAYERS, C), 0.5, 2.5, ((0, 4),), jnp.float32)
    cotangent = draw_cotangent(jax.random.fold_in(key_of[6], 71), 0)
    return {"images": images, "switches": switches, "conv_weights": conv_weights, "gains": gains, "shifts": shifts, "cotangent": cotangent}


epsilon = 1e-05

@jax.custom_vjp
def low(v):
    return lax.optimization_barrier(v.astype(jnp.bfloat16)).astype(jnp.float32)

@jax.custom_vjp
def low_back(v):
    return v

def low_keep(v):
    return (low(v), None)

def low_pass(kept, grad):
    return (grad,)

def back_keep(v):
    return (v, None)

def back_low(kept, grad):
    return (low(grad),)
low.defvjp(low_keep, low_pass)
low_back.defvjp(back_keep, back_low)

def reference(images, switches, conv_weights, gains, shifts, cotangent):
    source = images.astype(jnp.float32)
    kernels = conv_weights.astype(jnp.float32)
    seed_grad = cotangent.astype(jnp.float32)
    upsampled = jnp.repeat(jnp.repeat(switches, 2, axis=2), 2, axis=3)
    parity = lax.broadcasted_iota(jnp.int32, (HEIGHT, COLS), 0) % 2 * 2 + lax.broadcasted_iota(jnp.int32, (HEIGHT, COLS), 1) % 2
    unpool_mask = (upsampled == parity).astype(jnp.float32)[..., None]

    def forward(kernel_set, gain_set, shift_set, probes):
        activation = source
        outputs = []
        for layer_index in range(LAYERS):
            layer_input = low_back(activation + probes[layer_index])
            if layer_index == LAYERS // 2:
                layer_input = layer_input * unpool_mask
            flat = layer_input.reshape(MB * IMG, HEIGHT, COLS, C)
            conv_out = lax.conv_general_dilated(flat, kernel_set[layer_index], (1, 1), 'SAME', dimension_numbers=('NHWC', 'HWIO', 'NHWC'), precision=lax.Precision.HIGHEST)
            conv_out = low_back(conv_out.reshape(MB, IMG, HEIGHT, COLS, C))
            batch_mean = lax.optimization_barrier(jnp.mean(conv_out, axis=(1, 2, 3), keepdims=True))
            centered = conv_out - batch_mean
            spread = lax.optimization_barrier(jnp.mean(centered * centered, axis=(1, 2, 3), keepdims=True))
            affine = centered * lax.rsqrt(spread + epsilon) * gain_set[layer_index] + shift_set[layer_index]
            activation = low(jax.nn.silu(affine))
            outputs.append(activation)
        return (activation, jnp.stack(outputs))
    probes = jnp.zeros((LAYERS, MB, IMG, HEIGHT, COLS, C), jnp.float32)
    final, backward, stacked = jax.vjp(forward, kernels, gains, shifts, probes, has_aux=True)
    grad_kernels, grad_gains, grad_shifts, grad_probes = backward(seed_grad)
    return (stacked.astype(jnp.bfloat16), grad_probes.astype(jnp.bfloat16), grad_kernels, grad_gains, grad_shifts)
```

```python
import functools

import jax
import jax.numpy as jnp
from jax import lax
from jax.experimental import pallas as pl
from jax.experimental.pallas import tpu as pltpu
from jax.sharding import PartitionSpec as P

EPSILON = 1e-05
MESH = pl.DeviceIdType.MESH
BF16 = jnp.bfloat16
F32 = jnp.float32


def kernel(
    sections, strips, cols,
    images, cotangent, weights, gains, shifts, mask,
    outs, grads_in, weight_part, gain_sum, shift_sum,
    w_v, inp, mask_v, gain_prev, shift_prev, zin, zin_stat, zown, own_stat, zfull, ua, slope_prev, xhat_prev,
    xhat, scale, dyin, dy_stat, dzcat, dzs, dyout, stat_out, sums_out, seed_sums, out_v, gin_v, dw_v,
    w_sem, in_sem, ie_s, ie_r, mk_l, mk_s, mk_r, gp_s, gp_r,
    fz_s, fz_r, fs_s, fs_r, oe_s, oe_r, os_s, os_r, bz_s, bz_r, bs_s, bs_r, ls_s, out_sem, gin_sem, dw_sem,
):
    sec = lax.axis_index("section")
    row = lax.axis_index("rows")
    batches, pictures, tall, ch = inp.shape
    px = tall - 2 * cols
    half = ch // 2
    total = float(pictures * px * strips)
    local = float(pictures * px)
    first, last = sec == 0, sec == sections - 1
    has_up, has_down = row > 0, row < strips - 1

    centre = pl.ds(cols, px)
    top, bottom = pl.ds(0, cols), pl.ds(cols + px, cols)

    def w_copy(r):
        return pltpu.make_async_copy(weights.at[r], w_v.at[r], w_sem.at[r])

    def in_copy(src, m):
        return pltpu.make_async_copy(src.at[m], inp.at[m, :, centre, :], in_sem.at[m])

    for r in range(3):
        w_copy(r).start()

    @pl.when(first)
    def _():
        for m in range(batches):
            in_copy(images, m).start()

    @pl.when(last)
    def _():
        for m in range(batches):
            in_copy(cotangent, m).start()

    mask_copy = pltpu.make_async_copy(mask, mask_v.at[:, :, centre, :], mk_l)
    mask_copy.start()
    gain_sum[...] = jnp.zeros_like(gain_sum)
    shift_sum[...] = jnp.zeros_like(shift_sum)

    barrier = pltpu.get_barrier_semaphore()
    for s in range(sections):
        @pl.when((sec >= s - 1) & (sec <= s + 1))
        def _():
            def greet(i, carry):
                @pl.when((s != sec) | (i != row))
                def _():
                    pl.semaphore_signal(barrier, inc=1, device_id=(jnp.int32(s), i), device_id_type=MESH)
                return carry
            lax.fori_loop(0, strips, greet, 0)
    near = 1 + jnp.where(sec > 0, 1, 0) + jnp.where(sec < sections - 1, 1, 0)
    pl.semaphore_wait(barrier, near * strips - 1)

    def remote(src, dst, send, recv, s, i):
        return pltpu.make_async_remote_copy(
            src_ref=src, dst_ref=dst, send_sem=send, recv_sem=recv, device_id=(s, i), device_id_type=MESH
        )

    def edges(src_at, dst_at, send_at, recv_at, s):
        last_rows, first_rows = pl.ds(px - cols, cols), pl.ds(0, cols)
        return (
            (has_down, lambda: remote(src_at(last_rows), dst_at(top), send_at(0), recv_at(0), s, row + 1)),
            (has_up, lambda: remote(src_at(first_rows), dst_at(bottom), send_at(1), recv_at(1), s, row - 1)),
        )

    def start_edges(pairs):
        for cond, make in pairs:
            @pl.when(cond)
            def _():
                make().start()

    def wait_edges_sent(pairs):
        for cond, make in pairs:
            @pl.when(cond)
            def _():
                make().wait_send()

    def wait_edges_in(pairs):
        (_, down), (_, up) = pairs

        @pl.when(has_up)
        def _():
            down().wait_recv()

        @pl.when(has_down)
        def _():
            up().wait_recv()

    def input_edges(src, m):
        return edges(
            lambda r: src.at[m, :, r, :], lambda r: inp.at[m, :, r, :],
            lambda k: ie_s.at[m, k], lambda k: ie_r.at[m, k], sec,
        )

    mask_edges = edges(
        lambda r: mask.at[:, :, r, :], lambda r: mask_v.at[:, :, r, :],
        lambda k: mk_s.at[k], lambda k: mk_r.at[k], sec,
    )

    @pl.when(first)
    def _():
        for m in range(batches):
            start_edges(input_edges(images, m))

    @pl.when(last)
    def _():
        for m in range(batches):
            start_edges(input_edges(cotangent, m))

    start_edges(mask_edges)

    def affine_sends():
        return (
            remote(gains, gain_prev, gp_s.at[0], gp_r.at[0], sec + 1, row),
            remote(shifts, shift_prev, gp_s.at[1], gp_r.at[1], sec + 1, row),
        )

    @pl.when(sec < sections - 1)
    def _():
        for copy in affine_sends():
            copy.start()

    rows_at = lax.broadcasted_iota(jnp.int32, (pictures, tall, ch), 1)
    inside = (rows_at >= jnp.where(has_up, 0, cols)) & (rows_at < jnp.where(has_down, tall, cols + px))
    column = jnp.bitwise_and(lax.broadcasted_iota(jnp.int32, (pictures * tall, ch), 0), cols - 1)

    def spread(values, dst, dst_at):
        flat = values.reshape(pictures * tall, ch)
        before = jnp.where(column == 0, 0.0, pltpu.roll(flat, 1, 0))
        after = jnp.where(column == cols - 1, 0.0, pltpu.roll(flat, pictures * tall - 1, 0))
        for c, block in enumerate((before, flat, after)):
            dst[dst_at, :, pl.ds(c * ch, ch)] = block.reshape(pictures, tall, ch).astype(BF16)

    def join(stats):
        means, squares = stats[:, 0, :], stats[:, 1, :]
        mean = jnp.sum(means, 0, keepdims=True) / float(strips)
        off = means - mean
        var = (jnp.sum(squares, 0, keepdims=True) + local * jnp.sum(off * off, 0, keepdims=True)) / total
        return mean, lax.rsqrt(var + EPSILON)

    def with_edge_means(stats_ref, m, values, mean):
        up = stats_ref[m, jnp.maximum(row - 1, 0), pl.ds(0, 1), :] - mean
        own = stats_ref[m, row, pl.ds(0, 1), :] - mean
        down = stats_ref[m, jnp.minimum(row + 1, strips - 1), pl.ds(0, 1), :] - mean
        add = jnp.where(rows_at < cols, up[None], jnp.where(rows_at < cols + px, own[None], down[None]))
        return values + add

    def strip_sends(src, dst, send, recv, m, s):
        def one(h):
            part = pl.ds(h * half, half)
            return remote(
                src(m, pl.ds(0, px), part), dst(m, centre, part), send.at[m, h], recv.at[m, h], s, row
            )
        return [functools.partial(one, h) for h in range(2)]

    def z_sends(m, s):
        return strip_sends(
            lambda m, r, c: zown.at[m, :, pl.ds(cols, px), c], lambda m, r, c: zin.at[m, :, r, c], fz_s, fz_r, m, s
        )

    def z_edges(m, s):
        return edges(
            lambda r: zown.at[m, :, pl.ds(r.start + cols, cols), :], lambda r: zin.at[m, :, r, :],
            lambda k: fz_s.at[m, 2 + k], lambda k: fz_r.at[m, 2 + k], s,
        )

    def own_edges(m):
        return edges(
            lambda r: zown.at[m, :, pl.ds(r.start + cols, cols), :], lambda r: zown.at[m, :, r, :],
            lambda k: oe_s.at[m, k], lambda k: oe_r.at[m, k], sec,
        )

    def dy_sends(m, s):
        return strip_sends(
            lambda m, r, c: dyout.at[m, :, r, c], lambda m, r, c: dyin.at[m, :, r, c], bz_s, bz_r, m, s
        )

    def dy_edges(m, s):
        return edges(
            lambda r: dyout.at[m, :, r, :], lambda r: dyin.at[m, :, r, :],
            lambda k: bz_s.at[m, 2 + k], lambda k: bz_r.at[m, 2 + k], s,
        )

    def stat_copy(src, dst, send, recv, m, s, i):
        return remote(src.at[m], dst.at[m, row], send.at[m, i], recv.at[m], s, i)

    def own_copy(src, dst, send, recv, m):
        return pltpu.make_async_copy(src.at[m], dst.at[m, row], recv.at[m])

    def start_stats(src, dst, send, recv, m, s, same):
        def one(i, carry):
            if same:
                @pl.when(i != row)
                def _():
                    stat_copy(src, dst, send, recv, m, s, i).start()
            else:
                stat_copy(src, dst, send, recv, m, s, i).start()
            return carry
        lax.fori_loop(0, strips, one, 0)
        if same:
            own_copy(src, dst, send, recv, m).start()

    def wait_stats_sent(src, dst, send, recv, m, s, same):
        def one(i, carry):
            if same:
                @pl.when(i != row)
                def _():
                    stat_copy(src, dst, send, recv, m, s, i).wait_send()
            else:
                stat_copy(src, dst, send, recv, m, s, i).wait_send()
            return carry
        lax.fori_loop(0, strips, one, 0)

    def wait_stats(dst, recv, m):
        pltpu.make_async_copy(dst.at[m], dst.at[m], recv.at[m]).wait()

    down_stats = (stat_out, zin_stat, fs_s, fs_r)
    same_stats = (stat_out, own_stat, os_s, os_r)
    back_stats = (sums_out, dy_stat, bs_s, bs_r)
    seed_stats = (seed_sums, dy_stat, ls_s, bs_r)

    def forward(m):
        @pl.when(m == 0)
        def _():
            mask_copy.wait()
            wait_edges_in(mask_edges)

        @pl.when(first)
        def _():
            in_copy(images, m).wait()
            wait_edges_in(input_edges(images, m))
            values = jnp.where(inside, inp[m].astype(F32), 0.0)
            spread(values, ua.at[m], slice(None))

        @pl.when(sec > 0)
        def _():
            @pl.when(m == 0)
            def _():
                for copy in affine_sends():
                    copy.wait_recv()
            wait_stats(zin_stat, fs_r, m)
            for make in z_sends(m, sec):
                make().wait_recv()
            wait_edges_in(z_edges(m, sec))
            mean, inv = join(zin_stat[m])
            normed = with_edge_means(zin_stat, m, zin[m].astype(F32), mean) * inv
            y = normed * gain_prev[...] + shift_prev[...]
            sig = 1.0 / (1.0 + jnp.exp(-y))
            gate = jnp.concatenate([mask_v[m].astype(F32)] * (ch // 128), axis=2)
            values = jnp.where(inside, (y * sig) .astype(BF16).astype(F32) * gate, 0.0)
            spread(values, ua.at[m], slice(None))
            slope = sig * (1.0 + y * (1.0 - sig))
            slope_prev[m] = slope[:, cols : cols + px]
            xhat_prev[m] = normed[:, cols : cols + px]

        for h in range(2):
            acc = jnp.zeros((pictures * px, half), F32)
            for r in range(3):
                if h == 0:
                    @pl.when(weights_due(m))
                    def _():
                        w_copy(r).wait()
                left = ua[m, :, pl.ds(r * cols, px), :].reshape(pictures * px, 3 * ch)
                acc += jnp.dot(left, w_v[r, :, pl.ds(h * half, half)], preferred_element_type=F32)
            mean = jnp.sum(acc, 0, keepdims=True) / local
            centred = acc - mean
            stat_out[m, pl.ds(0, 1), pl.ds(h * half, half)] = mean
            stat_out[m, pl.ds(1, 1), pl.ds(h * half, half)] = jnp.sum(centred * centred, 0, keepdims=True)
            centred = centred.reshape(pictures, px, half)
            zfull[m, :, :, pl.ds(h * half, half)] = centred
            zown[m, :, centre, pl.ds(h * half, half)] = centred.astype(BF16)

            @pl.when(sec < sections - 1)
            def _():
                if h == 1:
                    start_stats(*down_stats, m, sec + 1, False)
                z_sends(m, sec + 1)[h]().start()
                if h == 1:
                    start_edges(z_edges(m, sec + 1))

        start_stats(*same_stats, m, sec, True)
        start_edges(own_edges(m))

    def weights_due(m):
        return m == 0

    def finish(m):
        wait_stats(own_stat, os_r, m)
        wait_edges_in(own_edges(m))
        mean, inv = join(own_stat[m])
        gain, shift = gains[...], shifts[...]
        scale[m] = inv * gain
        normed = with_edge_means(own_stat, m, zown[m].astype(F32), mean) * inv
        xhat[m] = normed
        y = normed * gain + shift
        sig = 1.0 / (1.0 + jnp.exp(-y))

        @pl.when(last)
        def _():
            in_copy(cotangent, m).wait()
            wait_edges_in(input_edges(cotangent, m))
            dy = inp[m].astype(F32) * sig * (1.0 + y * (1.0 - sig))
            dyin[m] = dy.astype(BF16)
            own = dy[:, cols : cols + px].reshape(pictures * px, ch)
            other = normed[:, cols : cols + px].reshape(pictures * px, ch)
            seed_sums[m, pl.ds(0, 1), :] = jnp.sum(own, 0, keepdims=True)
            seed_sums[m, pl.ds(1, 1), :] = jnp.sum(own * other, 0, keepdims=True)
            start_stats(*seed_stats, m, sec, True)

        off = own_stat[m, row, pl.ds(0, 1), :] - mean
        y = (zfull[m] + off[None]) * scale[m][None] + shift[None]
        out_v[m] = (y / (1.0 + jnp.exp(-y))).astype(BF16)
        pltpu.make_async_copy(out_v.at[m], outs.at[m], out_sem.at[m]).start()

    def backward(m):
        wait_stats(dy_stat, bs_r, m)

        @pl.when(sec < sections - 1)
        def _():
            for make in dy_sends(m, sec):
                make().wait_recv()
            wait_edges_in(dy_edges(m, sec))

        sums = dy_stat[m]
        first_sum = jnp.sum(sums[:, 0, :], 0, keepdims=True)
        cross_sum = jnp.sum(sums[:, 1, :], 0, keepdims=True)
        shift_sum[...] += first_sum
        gain_sum[...] += cross_sum
        dz = scale[m][None] * (dyin[m].astype(F32) - first_sum[None] / total - xhat[m] * (cross_sum[None] / total))
        dz = jnp.where(inside, dz, 0.0).astype(BF16)
        dzs[m] = dz[:, cols : cols + px]
        spread(dz.astype(F32), dzcat, slice(None))
        gate = mask_v[m, :, centre, :].astype(F32)
        gate = jnp.concatenate([gate] * (half // 128), axis=2)
        for h in range(2):
            acc = jnp.zeros((pictures * px, half), F32)
            for r in range(3):
                for c in range(3):
                    left = dzcat[:, pl.ds((2 - r) * cols, px), pl.ds((2 - c) * ch, ch)].reshape(pictures * px, ch)
                    acc += lax.dot_general(
                        left, w_v[r, pl.ds(c * ch + h * half, half), :], (((1,), (1,)), ((), ())),
                        preferred_element_type=F32,
                    )
            du = (acc.reshape(pictures, px, half) * gate).astype(BF16)
            gin_v[m, :, :, pl.ds(h * half, half)] = du

            @pl.when(sec > 0)
            def _():
                part = pl.ds(h * half, half)
                dy = du.astype(F32) * slope_prev[m, :, :, part]
                dyout[m, :, :, part] = dy.astype(BF16)
                own = dy.reshape(pictures * px, half)
                other = xhat_prev[m, :, :, part].reshape(pictures * px, half)
                sums_out[m, pl.ds(0, 1), part] = jnp.sum(own, 0, keepdims=True)
                sums_out[m, pl.ds(1, 1), part] = jnp.sum(own * other, 0, keepdims=True)
                if h == 1:
                    start_stats(*back_stats, m, sec - 1, False)
                dy_sends(m, sec - 1)[h]().start()
                if h == 1:
                    start_edges(dy_edges(m, sec - 1))

        pltpu.make_async_copy(gin_v.at[m], grads_in.at[m], gin_sem.at[m]).start()

    def step(t, carry):
        ahead = t - sec
        behind = t - (2 * sections - 1 - sec)

        @pl.when((ahead >= 0) & (ahead < batches))
        def _():
            forward(ahead)

        @pl.when((behind >= 0) & (behind < batches))
        def _():
            backward(behind)

        @pl.when((ahead >= 0) & (ahead < batches))
        def _():
            finish(ahead)

        return carry

    lax.fori_loop(0, 2 * sections - 1 + batches, step, 0)

    def dw_copy(r, c):
        return pltpu.make_async_copy(dw_v.at[r, c], weight_part.at[r, c], dw_sem.at[r, c])

    def taps(r, carry):
        for c in range(3):
            left = ua[:, :, pl.ds(pl.multiple_of(r * cols, cols), px), pl.ds(c * ch, ch)]
            left = left.reshape(batches * pictures * px, ch)
            right = dzs[...].reshape(batches * pictures * px, ch)
            for h in range(2):
                part = lax.dot_general(
                    left[:, h * half : (h + 1) * half], right, (((0,), (0,)), ((), ())), preferred_element_type=F32
                )
                dw_v[r, c, pl.ds(h * half, half), :] = part.astype(BF16)
            dw_copy(r, c).start()
        return carry

    lax.fori_loop(0, 3, taps, 0)

    for r in range(3):
        for c in range(3):
            dw_copy(r, c).wait()

    wait_edges_sent(mask_edges)

    @pl.when(sec < sections - 1)
    def _():
        for copy in affine_sends():
            copy.wait_send()

    def drain(m, carry):
        pltpu.make_async_copy(out_v.at[m], outs.at[m], out_sem.at[m]).wait()
        pltpu.make_async_copy(gin_v.at[m], grads_in.at[m], gin_sem.at[m]).wait()

        @pl.when(first)
        def _():
            wait_edges_sent(input_edges(images, m))

        @pl.when(last)
        def _():
            wait_edges_sent(input_edges(cotangent, m))
            wait_stats_sent(*seed_stats, m, sec, True)

        @pl.when(sec < sections - 1)
        def _():
            wait_stats_sent(*down_stats, m, sec + 1, False)
            for make in z_sends(m, sec + 1):
                make().wait_send()
            wait_edges_sent(z_edges(m, sec + 1))

        wait_stats_sent(*same_stats, m, sec, True)
        wait_edges_sent(own_edges(m))

        @pl.when(sec > 0)
        def _():
            wait_stats_sent(*back_stats, m, sec - 1, False)
            for make in dy_sends(m, sec - 1):
                make().wait_send()
            wait_edges_sent(dy_edges(m, sec - 1))

        return carry

    lax.fori_loop(0, batches, drain, 0)


def body(images, switches, conv_weights, gains, shifts, cotangent):
    sections = lax.axis_size("section")
    strips = lax.axis_size("rows")
    batches, pictures, strip_rows, cols, ch = images.shape
    px = strip_rows * cols
    tall = px + 2 * cols
    parity = (
        lax.broadcasted_iota(jnp.int32, (strip_rows, cols), 0) % 2 * 2
        + lax.broadcasted_iota(jnp.int32, (strip_rows, cols), 1) % 2
    )
    upsampled = jnp.repeat(jnp.repeat(switches, 2, axis=2), 2, axis=3)
    chosen = (upsampled == parity) | (lax.axis_index("section") != sections // 2)
    mask = jnp.broadcast_to(
        chosen.astype(BF16).reshape(batches, pictures, px, 1), (batches, pictures, px, 128)
    )
    anywhere = pl.BlockSpec(memory_space=pl.ANY)
    vmem = pl.BlockSpec(memory_space=pltpu.VMEM)
    dma = pltpu.SemaphoreType.DMA
    flops = 3 * 2 * 9 * ch * ch * batches * pictures * px
    outs, grads_in, weight_part, gain_sum, shift_sum = pl.pallas_call(
        functools.partial(kernel, sections, strips, cols),
        out_shape=(
            jax.ShapeDtypeStruct((batches, pictures, px, ch), BF16),
            jax.ShapeDtypeStruct((batches, pictures, px, ch), BF16),
            jax.ShapeDtypeStruct((3, 3, ch, ch), BF16),
            jax.ShapeDtypeStruct((1, ch), F32),
            jax.ShapeDtypeStruct((1, ch), F32),
        ),
        in_specs=[anywhere, anywhere, anywhere, vmem, vmem, anywhere],
        out_specs=(anywhere, anywhere, anywhere, vmem, vmem),
        scratch_shapes=[
            pltpu.VMEM((3, 3 * ch, ch), BF16),
            pltpu.VMEM((batches, pictures, tall, ch), BF16),
            pltpu.VMEM((batches, pictures, tall, 128), BF16),
            pltpu.VMEM((1, ch), F32),
            pltpu.VMEM((1, ch), F32),
            pltpu.VMEM((batches, pictures, tall, ch), BF16),
            pltpu.VMEM((batches, strips, 2, ch), F32),
            pltpu.VMEM((batches, pictures, tall, ch), BF16),
            pltpu.VMEM((batches, strips, 2, ch), F32),
            pltpu.VMEM((batches, pictures, px, ch), F32),
            pltpu.VMEM((batches, pictures, tall, 3 * ch), BF16),
            pltpu.VMEM((batches, pictures, px, ch), F32),
            pltpu.VMEM((batches, pictures, px, ch), F32),
            pltpu.VMEM((batches, pictures, tall, ch), F32),
            pltpu.VMEM((batches, 1, ch), F32),
            pltpu.VMEM((batches, pictures, tall, ch), BF16),
            pltpu.VMEM((batches, strips, 2, ch), F32),
            pltpu.VMEM((pictures, tall, 3 * ch), BF16),
            pltpu.VMEM((batches, pictures, px, ch), BF16),
            pltpu.VMEM((batches, pictures, px, ch), BF16),
            pltpu.VMEM((batches, 2, ch), F32),
            pltpu.VMEM((batches, 2, ch), F32),
            pltpu.VMEM((batches, 2, ch), F32),
            pltpu.VMEM((batches, pictures, px, ch), BF16),
            pltpu.VMEM((batches, pictures, px, ch), BF16),
            pltpu.VMEM((3, 3, ch, ch), BF16),
            dma((3,)),
            dma((batches,)),
            dma((batches, 2)), dma((batches, 2)),
            dma, dma((2,)), dma((2,)),
            dma((2,)), dma((2,)),
            dma((batches, 4)), dma((batches, 4)),
            dma((batches, strips)), dma((batches,)),
            dma((batches, 2)), dma((batches, 2)),
            dma((batches, strips)), dma((batches,)),
            dma((batches, 4)), dma((batches, 4)),
            dma((batches, strips)), dma((batches,)),
            dma((batches, strips)),
            dma((batches,)), dma((batches,)), dma((3, 3)),
        ],
        compiler_params=pltpu.CompilerParams(
            collective_id=0, has_side_effects=True, vmem_limit_bytes=56 * 2**20
        ),
        cost_estimate=pl.CostEstimate(
            flops=flops, bytes_accessed=2 * 9 * ch * ch * 2, transcendentals=0
        ),
    )(
        images.reshape(batches, pictures, px, ch),
        cotangent.reshape(batches, pictures, px, ch),
        conv_weights.reshape(3, 3 * ch, ch),
        gains,
        shifts,
        mask,
    )
    weight_grad = lax.psum_scatter(weight_part, "rows", scatter_dimension=2, tiled=True).astype(F32)
    shape = (1, batches, pictures, strip_rows, cols, ch)
    return (outs.reshape(shape), grads_in.reshape(shape), weight_grad[None], gain_sum, shift_sum)


def solution(mesh):
    return jax.shard_map(
        body,
        mesh=mesh,
        in_specs=(
            P(None, None, "rows", None, None),
            P(None, None, "rows", None),
            P("section", None, None, None, None),
            P("section", None),
            P("section", None),
            P(None, None, "rows", None, None),
        ),
        out_specs=(
            P("section", None, None, "rows", None, None),
            P("section", None, None, "rows", None, None),
            P("section", None, None, "rows", None),
            P("section", None),
            P("section", None),
        ),
        check_vma=False,
    )
```

```python
import functools

import jax
import jax.numpy as jnp
from jax import lax
from jax.experimental import pallas as pl
from jax.experimental.pallas import tpu as pltpu
from jax.sharding import PartitionSpec as P

EPSILON = 1e-05
MESH = pl.DeviceIdType.MESH
BF16 = jnp.bfloat16
F32 = jnp.float32


def kernel(
    sections, strips, cols,
    images, cotangent, weights, gains, shifts, switches,
    outs, grads_in, weight_part, gain_sum, shift_sum,
    w_v, inp, mask_own, mask_v, gain_prev, shift_prev, zin, zin_stat, zown, own_stat, ub, slope_prev,
    prev_coef, own_coef, dyin, dy_stat, dzb, dzside, dyout, stat_out, sums_out, seed_sums, out_v, gin_v, dw_v,
    w_sem, in_sem, pi_s, pi_r, ie_s, ie_r, mp_s, mp_r, me_s, me_r, gp_s, gp_r,
    fz_s, fz_r, fs_s, fs_r, oe_s, oe_r, os_s, os_r, bz_s, bz_r, bs_s, bs_r, ls_s,
    out_sem, po_s, po_r, gin_sem, pg_s, pg_r, dw_sem,
):
    sec = lax.axis_index("section")
    row = lax.axis_index("rows")
    batches, tall, ch = inp.shape
    px = tall - 2 * cols
    strip = px // 2
    groups = tall // cols
    half = ch // 2
    total = float(px * strips)
    local = float(px)
    first, last, decoder = sec == 0, sec == sections - 1, sec == sections // 2
    core = row % 2
    partner = row + 1 - 2 * core
    has_up, has_down = row >= 2, row < strips - 2
    centre = pl.ds(cols, px)
    mine = pl.multiple_of(cols + strip * core, cols)

    def w_copy(r):
        return pltpu.make_async_copy(weights.at[r], w_v.at[r], w_sem.at[r])

    def in_copy(src, m):
        return pltpu.make_async_copy(src.at[m, core], inp.at[m, pl.ds(mine, strip), :], in_sem.at[m])

    for r in range(3):
        w_copy(r).start()

    @pl.when(first)
    def _():
        for m in range(batches):
            in_copy(images, m).start()

    @pl.when(last)
    def _():
        for m in range(batches):
            in_copy(cotangent, m).start()

    barrier = pltpu.get_barrier_semaphore()
    for s in range(sections):
        @pl.when((sec >= s - 1) & (sec <= s + 1))
        def _():
            def greet(i, carry):
                @pl.when((s != sec) | (i != row))
                def _():
                    pl.semaphore_signal(barrier, inc=1, device_id=(jnp.int32(s), i), device_id_type=MESH)
                return carry
            lax.fori_loop(0, strips, greet, 0)

    gain_sum[...] = jnp.zeros_like(gain_sum)
    shift_sum[...] = jnp.zeros_like(shift_sum)

    @pl.when(decoder)
    def _():
        wide = cols // 2
        lanes = lax.broadcasted_iota(jnp.int32, (cols, wide), 1)
        places = lax.broadcasted_iota(jnp.int32, (cols, wide), 0)
        pick = (lax.shift_right_logical(places, 1) == lanes).astype(F32)
        table = lax.dot_general(
            pick, switches[...].astype(F32), (((1,), (1,)), ((), ())), preferred_element_type=F32
        )
        odd = jnp.bitwise_and(lax.broadcasted_iota(jnp.int32, (cols, 128), 0), 1).astype(F32)
        windows = strip // cols // 2
        for m in range(batches):
            for i in range(2):
                for w in range(windows):
                    at = (m * 2 + i) * windows + w
                    value = jnp.broadcast_to(table[:, at : at + 1], (cols, 128))
                    for p in range(2):
                        hit = (jnp.abs(value - (2.0 * p + odd)) < 0.5).astype(F32).astype(BF16)
                        mask_own[m, i, pl.ds((2 * w + p) * cols, cols), :] = hit
        for m in range(batches):
            mask_v[m, pl.ds(mine, strip), :] = mask_own[m, core]

    @pl.when(jnp.logical_not(decoder))
    def _():
        mask_v[...] = jnp.ones_like(mask_v)

    near = 1 + jnp.where(sec > 0, 1, 0) + jnp.where(sec < sections - 1, 1, 0)
    pl.semaphore_wait(barrier, near * strips - 1)

    def remote(src, dst, send, recv, s, i):
        return pltpu.make_async_remote_copy(
            src_ref=src, dst_ref=dst, send_sem=send, recv_sem=recv, device_id=(s, i), device_id_type=MESH
        )

    def to_partner(src_at, dst_at, send, recv):
        return remote(src_at(1 - core), dst_at(pl.ds(mine, strip)), send, recv, sec, partner)

    def start_argument(src_at, dst_at, pair_sems, edge_sems):
        to_partner(src_at, dst_at, *pair_sems).start()

        @pl.when((core == 1) & has_down)
        def _():
            for i in range(2):
                remote(
                    src_at(i, pl.ds(strip - cols, cols)), dst_at(pl.ds(0, cols)),
                    edge_sems[0].at[i], edge_sems[1].at[0], sec, row + 1 + i,
                ).start()

        @pl.when((core == 0) & has_up)
        def _():
            for i in range(2):
                remote(
                    src_at(i, pl.ds(0, cols)), dst_at(pl.ds(cols + px, cols)),
                    edge_sems[0].at[i], edge_sems[1].at[1], sec, row - 2 + i,
                ).start()

    def argument_arrived(src_at, dst_at, pair_sems, edge_sems):
        to_partner(src_at, dst_at, *pair_sems).wait_recv()

        @pl.when(has_up)
        def _():
            remote(
                src_at(0, pl.ds(0, cols)), dst_at(pl.ds(0, cols)), edge_sems[0].at[0], edge_sems[1].at[0], sec, row
            ).wait_recv()

        @pl.when(has_down)
        def _():
            remote(
                src_at(0, pl.ds(0, cols)), dst_at(pl.ds(cols + px, cols)), edge_sems[0].at[0], edge_sems[1].at[1],
                sec, row,
            ).wait_recv()

    def argument_sent(src_at, dst_at, pair_sems, edge_sems):
        to_partner(src_at, dst_at, *pair_sems).wait_send()

        @pl.when(((core == 1) & has_down) | ((core == 0) & has_up))
        def _():
            for i in range(2):
                remote(
                    src_at(i, pl.ds(0, cols)), dst_at(pl.ds(0, cols)), edge_sems[0].at[i], edge_sems[1].at[0], sec, row
                ).wait_send()

    def input_parts(src, m):
        return (
            lambda i, r=pl.ds(0, strip): src.at[m, i, r, :],
            lambda r: inp.at[m, r, :],
            (pi_s.at[m], pi_r.at[m]),
            (ie_s.at[m], ie_r.at[m]),
        )

    mask_parts = (
        lambda i, r=pl.ds(0, strip): mask_own.at[:, i, r, :],
        lambda r: mask_v.at[:, r, :],
        (mp_s, mp_r),
        (me_s, me_r),
    )

    @pl.when(first)
    def _():
        for m in range(batches):
            start_argument(*input_parts(images, m))

    @pl.when(last)
    def _():
        for m in range(batches):
            start_argument(*input_parts(cotangent, m))

    @pl.when(decoder)
    def _():
        start_argument(*mask_parts)

    def affine_sends():
        return (
            remote(gains, gain_prev, gp_s.at[0], gp_r.at[0], sec + 1, row),
            remote(shifts, shift_prev, gp_s.at[1], gp_r.at[1], sec + 1, row),
        )

    @pl.when(sec < sections - 1)
    def _():
        for copy in affine_sends():
            copy.start()

    def block_sends(src, src_from, dst, send, recv, m, s):
        def one(k, h, src_row, dst_row, rows, i):
            part = pl.ds(h * half, half)
            return remote(
                src.at[m, pl.ds(src_from + src_row, rows), part], dst.at[m, pl.ds(dst_row, rows), part],
                send.at[m, k, h], recv.at[m, k, h], s, i,
            )
        return (
            (None, lambda h: one(0, h, 0, cols, px, row)),
            (has_down, lambda h: one(1, h, px - cols, 0, cols, row + 2)),
            (has_up, lambda h: one(2, h, 0, cols + px, cols, row - 2)),
        )

    def each(parts, h, act):
        for cond, make in parts:
            if cond is None:
                act(make(h))
            else:
                @pl.when(cond)
                def _():
                    act(make(h))

    def arrived(parts):
        (_, body), (_, to_down), (_, to_up) = parts
        for h in range(2):
            body(h).wait_recv()
        edges_arrived(to_down, to_up)

    def edges_arrived(to_down, to_up):
        @pl.when(has_up)
        def _():
            for h in range(2):
                to_down(h).wait_recv()

        @pl.when(has_down)
        def _():
            for h in range(2):
                to_up(h).wait_recv()

    def start(copy):
        copy.start()

    def sent(copy):
        copy.wait_send()

    def z_sends(m, s):
        return block_sends(zown, cols, zin, fz_s, fz_r, m, s)

    def own_edges(m):
        return block_sends(zown, cols, zown, oe_s, oe_r, m, sec)[1:]

    def dy_sends(m, s):
        return block_sends(dyout, 0, dyin, bz_s, bz_r, m, s)

    def stat_copy(src, dst, send, recv, m, s, i):
        return remote(src.at[m], dst.at[m, row], send.at[m, i], recv.at[m], s, i)

    def stats_each(src, dst, send, recv, m, s, same, act):
        def one(d, carry):
            i = row + d
            act(stat_copy(src, dst, send, recv, m, s, jnp.where(i >= strips, i - strips, i)))
            return carry
        lax.fori_loop(1 if same else 0, strips, one, 0)

    def start_stats(src, dst, send, recv, m, s, same):
        stats_each(src, dst, send, recv, m, s, same, start)
        if same:
            pltpu.make_async_copy(src.at[m], dst.at[m, row], recv.at[m]).start()

    def wait_stats(dst, recv, m):
        pltpu.make_async_copy(dst.at[m], dst.at[m], recv.at[m]).wait()

    down_stats = (stat_out, zin_stat, fs_s, fs_r)
    same_stats = (stat_out, own_stat, os_s, os_r)
    back_stats = (sums_out, dy_stat, bs_s, bs_r)
    seed_stats = (seed_sums, dy_stat, ls_s, bs_r)

    def join(stats_ref, m):
        means, squares = stats_ref[m, :, 0, :], stats_ref[m, :, 1, :]
        mean = jnp.sum(means, 0, keepdims=True) / float(strips)
        off = means - mean
        var = (jnp.sum(squares, 0, keepdims=True) + local * jnp.sum(off * off, 0, keepdims=True)) / total
        at = (jnp.maximum(row - 2, 0), row, jnp.minimum(row + 2, strips - 1))
        return lax.rsqrt(var + EPSILON), [stats_ref[m, i, pl.ds(0, 1), :] - mean for i in at]

    def kind(g):
        return 0 if g == 0 else 2 if g == groups - 1 else 1

    def inside(g, values):
        if kind(g) == 1:
            return values
        return jnp.where(has_up if kind(g) == 0 else has_down, values, jnp.zeros_like(values))

    def group(g):
        return pl.ds(g * cols, cols)

    column = lax.broadcasted_iota(jnp.int32, (1, cols, half), 1)

    def taps_joined(parts, left, right):
        def moved(values, by, edge):
            turned = pltpu.roll(values, by % px, 0).reshape(px // cols, cols, half)
            return jnp.where(column == edge, 0.0, turned).reshape(px, half)
        return parts[1] + moved(parts[left], 1, 0) + moved(parts[right], -1, cols - 1)

    def forward(m):
        @pl.when(first)
        def _():
            in_copy(images, m).wait()
            argument_arrived(*input_parts(images, m))
            for g in range(groups):
                ub[m, group(g), :] = inside(g, inp[m, group(g), :])

        @pl.when(sec > 0)
        def _():
            @pl.when(m == 0)
            def _():
                for copy in affine_sends():
                    copy.wait_recv()

                @pl.when(decoder)
                def _():
                    argument_arrived(*mask_parts)

            wait_stats(zin_stat, fs_r, m)
            inv, offs = join(zin_stat, m)
            prev_coef[m, pl.ds(0, 1), :] = inv
            prev_coef[m, pl.ds(1, 1), :] = offs[1]
            slant = 0.5 * inv * gain_prev[...]
            level = [slant * off + 0.5 * shift_prev[...] for off in offs]
            arrived(z_sends(m, sec))
            for g in range(groups):
                halved = zin[m, group(g), :].astype(F32) * slant + level[kind(g)]
                turn = jnp.tanh(halved)
                bent = halved * turn
                gate = jnp.concatenate([mask_v[m, group(g), :].astype(F32)] * (ch // 128), axis=1)
                ub[m, group(g), :] = inside(g, ((halved + bent) * gate).astype(BF16))
                if kind(g) == 1:
                    slope_prev[m, pl.ds((g - 1) * cols, cols), :] = (0.5 + 0.5 * turn) * (1.0 + halved - bent)

        @pl.when(m == 0)
        def _():
            for r in range(3):
                w_copy(r).wait()

        for h in range(2):
            part = pl.ds(h * half, half)
            parts = []
            for c in range(3):
                acc = jnp.zeros((px, half), F32)
                for r in range(3):
                    acc += jnp.dot(
                        ub[m, pl.ds(r * cols, px), :], w_v[r, pl.ds(c * ch, ch), part], preferred_element_type=F32
                    )
                parts.append(acc)
            conv = taps_joined(parts, 0, 2)
            mean = jnp.sum(conv, 0, keepdims=True) / local
            conv = conv - mean
            stat_out[m, pl.ds(0, 1), part] = mean
            stat_out[m, pl.ds(1, 1), part] = jnp.sum(conv * conv, 0, keepdims=True)
            zown[m, centre, part] = conv.astype(BF16)

            @pl.when(sec < sections - 1)
            def _():
                if h == 1:
                    start_stats(*down_stats, m, sec + 1, False)
                each(z_sends(m, sec + 1), h, start)

        start_stats(*same_stats, m, sec, True)
        for h in range(2):
            each(own_edges(m), h, start)

    def finish(m):
        wait_stats(own_stat, os_r, m)
        inv, offs = join(own_stat, m)
        scale = inv * gains[...]
        own_coef[m, pl.ds(0, 1), :] = inv
        own_coef[m, pl.ds(1, 1), :] = scale
        for k in range(3):
            own_coef[m, pl.ds(2 + k, 1), :] = offs[k]
        slant = 0.5 * scale
        level = [slant * off + 0.5 * shifts[...] for off in offs]
        (_, to_down), (_, to_up) = own_edges(m)
        edges_arrived(to_down, to_up)

        @pl.when(last)
        def _():
            in_copy(cotangent, m).wait()
            argument_arrived(*input_parts(cotangent, m))
            sums = jnp.zeros((cols, ch), F32)
            cross = jnp.zeros((cols, ch), F32)
            for g in range(groups):
                z = zown[m, group(g), :].astype(F32)
                halved = z * slant + level[kind(g)]
                turn = jnp.tanh(halved)
                bent = halved * turn
                dy = inp[m, group(g), :].astype(F32) * ((0.5 + 0.5 * turn) * (1.0 + halved - bent))
                dyin[m, group(g), :] = dy.astype(BF16)
                if kind(g) == 1:
                    out_v[m, pl.ds((g - 1) * cols, cols), :] = (halved + bent).astype(BF16)
                    sums += dy
                    cross += dy * z
            one = jnp.sum(sums, 0, keepdims=True)
            seed_sums[m, pl.ds(0, 1), :] = one
            seed_sums[m, pl.ds(1, 1), :] = inv * (jnp.sum(cross, 0, keepdims=True) + offs[1] * one)
            start_stats(*seed_stats, m, sec, True)

        @pl.when(jnp.logical_not(last))
        def _():
            for g in range(1, groups - 1):
                halved = zown[m, group(g), :].astype(F32) * slant + level[1]
                out_v[m, pl.ds((g - 1) * cols, cols), :] = (halved + halved * jnp.tanh(halved)).astype(BF16)

        for copy in result_copies(out_v, outs, out_sem, po_s, po_r, m):
            copy.start()

    def result_copies(src, dst, sem, send, recv, m):
        here, there = pl.multiple_of(strip * core, cols), pl.multiple_of(strip * (1 - core), cols)
        return (
            pltpu.make_async_copy(src.at[m, pl.ds(here, strip), :], dst.at[m, core], sem.at[m]),
            remote(src.at[m, pl.ds(there, strip), :], dst.at[m, core], send.at[m], recv.at[m], sec, partner),
        )

    def backward(m):
        wait_stats(dy_stat, bs_r, m)
        first_sum = jnp.sum(dy_stat[m, :, 0, :], 0, keepdims=True)
        cross_sum = jnp.sum(dy_stat[m, :, 1, :], 0, keepdims=True)
        shift_sum[...] += first_sum
        gain_sum[...] += cross_sum
        inv = own_coef[m, pl.ds(0, 1), :]
        scale = own_coef[m, pl.ds(1, 1), :]
        tilt = scale * inv * (cross_sum / total)
        base = [scale * (first_sum / total) + tilt * own_coef[m, pl.ds(2 + k, 1), :] for k in range(3)]

        @pl.when(sec < sections - 1)
        def _():
            arrived(dy_sends(m, sec))

        for g in range(groups):
            dz = dyin[m, group(g), :].astype(F32) * scale - zown[m, group(g), :].astype(F32) * tilt - base[kind(g)]
            dzb[m, group(g), :] = inside(g, dz.astype(BF16))

        for h in range(2):
            part = pl.ds(h * half, half)
            parts = []
            for c in range(3):
                acc = jnp.zeros((px, half), F32)
                for r in range(3):
                    acc += lax.dot_general(
                        dzb[m, pl.ds((2 - r) * cols, px), :], w_v[r, pl.ds(c * ch + h * half, half), :],
                        (((1,), (1,)), ((), ())), preferred_element_type=F32,
                    )
                parts.append(acc)
            gate = jnp.concatenate([mask_v[m, centre, :].astype(F32)] * (half // 128), axis=1)
            du = (taps_joined(parts, 2, 0) * gate).astype(BF16)
            gin_v[m, :, part] = du

            @pl.when(sec > 0)
            def _():
                dy = du.astype(F32) * slope_prev[m, :, part]
                dyout[m, :, part] = dy.astype(BF16)
                one = jnp.sum(dy, 0, keepdims=True)
                cross = jnp.sum(dy * zin[m, centre, part].astype(F32), 0, keepdims=True)
                sums_out[m, pl.ds(0, 1), part] = one
                sums_out[m, pl.ds(1, 1), part] = prev_coef[m, pl.ds(0, 1), part] * (
                    cross + prev_coef[m, pl.ds(1, 1), part] * one
                )
                if h == 1:
                    start_stats(*back_stats, m, sec - 1, False)
                each(dy_sends(m, sec - 1), h, start)

        for copy in result_copies(gin_v, grads_in, gin_sem, pg_s, pg_r, m):
            copy.start()

    def step(t, carry):
        ahead = t - sec
        behind = t - (2 * sections - 1 - sec)

        @pl.when((ahead >= 0) & (ahead < batches))
        def _():
            forward(ahead)

        @pl.when((behind >= 0) & (behind < batches))
        def _():
            backward(behind)

        @pl.when((ahead >= 0) & (ahead < batches))
        def _():
            finish(ahead)

        return carry

    lax.fori_loop(0, 2 * sections - 1 + batches, step, 0)

    place = lax.broadcasted_iota(jnp.int32, (cols, ch), 0)
    for m in range(batches):
        for g in range(1, groups - 1):
            values = dzb[m, group(g), :].astype(F32)
            at = pl.ds((m * (groups - 2) + g - 1) * cols, cols)
            dzside[0, at, :] = jnp.where(place == cols - 1, 0.0, pltpu.roll(values, cols - 1, 0)).astype(BF16)
            dzside[1, at, :] = values.astype(BF16)
            dzside[2, at, :] = jnp.where(place == 0, 0.0, pltpu.roll(values, 1, 0)).astype(BF16)

    def dw_copy(r, c):
        return pltpu.make_async_copy(dw_v.at[r, c], weight_part.at[r, c], dw_sem.at[r, c])

    def taps(r, carry):
        left = ub[:, pl.ds(pl.multiple_of(r * cols, cols), px), :].reshape(batches * px, ch)
        for c in range(3):
            for h in range(2):
                part = lax.dot_general(
                    left[:, h * half : (h + 1) * half], dzside[c], (((0,), (0,)), ((), ())),
                    preferred_element_type=F32,
                )
                dw_v[r, c, pl.ds(h * half, half), :] = part.astype(BF16)
            dw_copy(r, c).start()
        return carry

    lax.fori_loop(0, 3, taps, 0)

    for r in range(3):
        for c in range(3):
            dw_copy(r, c).wait()

    @pl.when(decoder)
    def _():
        argument_sent(*mask_parts)

    @pl.when(sec < sections - 1)
    def _():
        for copy in affine_sends():
            copy.wait_send()

    def drain(m, carry):
        for src, dst, sems in ((out_v, outs, (out_sem, po_s, po_r)), (gin_v, grads_in, (gin_sem, pg_s, pg_r))):
            here, there = result_copies(src, dst, *sems, m)
            here.wait()
            there.wait_send()
            remote(
                src.at[m, pl.ds(0, strip), :], dst.at[m, 1 - core], sems[1].at[m], sems[2].at[m], sec, partner
            ).wait_recv()

        @pl.when(first)
        def _():
            argument_sent(*input_parts(images, m))

        @pl.when(last)
        def _():
            argument_sent(*input_parts(cotangent, m))
            stats_each(*seed_stats, m, sec, True, sent)

        @pl.when(sec < sections - 1)
        def _():
            stats_each(*down_stats, m, sec + 1, False, sent)
            for h in range(2):
                each(z_sends(m, sec + 1), h, sent)

        stats_each(*same_stats, m, sec, True, sent)
        for h in range(2):
            each(own_edges(m), h, sent)

        @pl.when(sec > 0)
        def _():
            stats_each(*back_stats, m, sec - 1, False, sent)
            for h in range(2):
                each(dy_sends(m, sec - 1), h, sent)

        return carry

    lax.fori_loop(0, batches, drain, 0)


def body(images, switches, conv_weights, gains, shifts, cotangent):
    sections = lax.axis_size("section")
    strips = lax.axis_size("rows")
    batches, pictures, strip_rows, cols, ch = images.shape
    strip = strip_rows * cols
    px = 2 * strip
    tall = px + 2 * cols
    anywhere = pl.BlockSpec(memory_space=pl.ANY)
    vmem = pl.BlockSpec(memory_space=pltpu.VMEM)
    dma = pltpu.SemaphoreType.DMA
    flops = 3 * 2 * 9 * ch * ch * batches * px
    outs, grads_in, weight_part, gain_sum, shift_sum = pl.pallas_call(
        functools.partial(kernel, sections, strips, cols),
        out_shape=(
            jax.ShapeDtypeStruct((batches, pictures, strip, ch), BF16),
            jax.ShapeDtypeStruct((batches, pictures, strip, ch), BF16),
            jax.ShapeDtypeStruct((3, 3, ch, ch), BF16),
            jax.ShapeDtypeStruct((1, ch), F32),
            jax.ShapeDtypeStruct((1, ch), F32),
        ),
        in_specs=[anywhere, anywhere, anywhere, vmem, vmem, vmem],
        out_specs=(anywhere, anywhere, anywhere, vmem, vmem),
        scratch_shapes=[
            pltpu.VMEM((3, 3 * ch, ch), BF16),
            pltpu.VMEM((batches, tall, ch), BF16),
            pltpu.VMEM((batches, 2, strip, 128), BF16),
            pltpu.VMEM((batches, tall, 128), BF16),
            pltpu.VMEM((1, ch), F32),
            pltpu.VMEM((1, ch), F32),
            pltpu.VMEM((batches, tall, ch), BF16),
            pltpu.VMEM((batches, strips, 2, ch), F32),
            pltpu.VMEM((batches, tall, ch), BF16),
            pltpu.VMEM((batches, strips, 2, ch), F32),
            pltpu.VMEM((batches, tall, ch), BF16),
            pltpu.VMEM((batches, px, ch), F32),
            pltpu.VMEM((batches, 2, ch), F32),
            pltpu.VMEM((batches, 8, ch), F32),
            pltpu.VMEM((batches, tall, ch), BF16),
            pltpu.VMEM((batches, strips, 2, ch), F32),
            pltpu.VMEM((batches, tall, ch), BF16),
            pltpu.VMEM((3, batches * px, ch), BF16),
            pltpu.VMEM((batches, px, ch), BF16),
            pltpu.VMEM((batches, 2, ch), F32),
            pltpu.VMEM((batches, 2, ch), F32),
            pltpu.VMEM((batches, 2, ch), F32),
            pltpu.VMEM((batches, px, ch), BF16),
            pltpu.VMEM((batches, px, ch), BF16),
            pltpu.VMEM((3, 3, ch, ch), BF16),
            dma((3,)),
            dma((batches,)),
            dma((batches,)), dma((batches,)),
            dma((batches, 2)), dma((batches, 2)),
            dma, dma,
            dma((2,)), dma((2,)),
            dma((2,)), dma((2,)),
            dma((batches, 3, 2)), dma((batches, 3, 2)),
            dma((batches, strips)), dma((batches,)),
            dma((batches, 3, 2)), dma((batches, 3, 2)),
            dma((batches, strips)), dma((batches,)),
            dma((batches, 3, 2)), dma((batches, 3, 2)),
            dma((batches, strips)), dma((batches,)),
            dma((batches, strips)),
            dma((batches,)), dma((batches,)), dma((batches,)),
            dma((batches,)), dma((batches,)), dma((batches,)),
            dma((3, 3)),
        ],
        compiler_params=pltpu.CompilerParams(
            collective_id=0, has_side_effects=True, vmem_limit_bytes=56 * 2**20
        ),
        cost_estimate=pl.CostEstimate(
            flops=flops, bytes_accessed=2 * 9 * ch * ch * 2, transcendentals=0
        ),
    )(
        images.reshape(batches, pictures, strip, ch),
        cotangent.reshape(batches, pictures, strip, ch),
        conv_weights.reshape(3, 3 * ch, ch),
        gains,
        shifts,
        switches.reshape(-1, switches.shape[-1]),
    )
    weight_grad = lax.psum_scatter(weight_part, "rows", scatter_dimension=2, tiled=True).astype(F32)
    shape = (1, batches, pictures, strip_rows, cols, ch)
    return (outs.reshape(shape), grads_in.reshape(shape), weight_grad[None], gain_sum, shift_sum)


def solution(mesh):
    return jax.shard_map(
        body,
        mesh=mesh,
        in_specs=(
            P(None, None, "rows", None, None),
            P(None, None, "rows", None),
            P("section", None, None, None, None),
            P("section", None),
            P("section", None),
            P(None, None, "rows", None, None),
        ),
        out_specs=(
            P("section", None, None, "rows", None, None),
            P("section", None, None, "rows", None, None),
            P("section", None, None, "rows", None),
            P("section", None),
            P("section", None),
        ),
        check_vma=False,
    )
```

```python
import functools

import jax
import jax.numpy as jnp
from jax import lax
from jax.experimental import pallas as pl
from jax.experimental.pallas import tpu as pltpu
from jax.sharding import PartitionSpec as P

EPSILON = 1e-05
MESH = pl.DeviceIdType.MESH
BF16 = jnp.bfloat16
F32 = jnp.float32


def kernel(
    sections, strips, cols,
    images, cotangent, weights, gains, shifts, switches,
    outs, grads_in, weight_part, gain_sum, shift_sum,
    w_v, inp, mask_own, mask_v, gain_prev, shift_prev, zin, zin_stat, zown, own_stat, ub, slope_prev,
    prev_coef, own_coef, dyin, dy_stat, dzb, dzside, dyout, stat_out, sums_out, seed_sums, out_v, gin_v, dw_v,
    w_sem, in_sem, pi_s, pi_r, ie_s, ie_r, mp_s, mp_r, me_s, me_r, gp_s, gp_r,
    fz_s, fz_r, fs_s, fs_r, oe_s, oe_r, os_s, os_r, bz_s, bz_r, bs_s, bs_r, ls_s,
    out_sem, po_s, po_r, gin_sem, pg_s, pg_r, dw_sem,
):
    sec = lax.axis_index("section")
    row = lax.axis_index("rows")
    batches, tall, ch = inp.shape
    px = tall - 2 * cols
    strip = px // 2
    groups = tall // cols
    half = ch // 2
    total = float(px * strips)
    local = float(px)
    first, last, decoder = sec == 0, sec == sections - 1, sec == sections // 2
    core = row % 2
    partner = row + 1 - 2 * core
    has_up, has_down = row >= 2, row < strips - 2
    centre = pl.ds(cols, px)
    mine = pl.multiple_of(cols + strip * core, cols)

    def w_copy(r):
        return pltpu.make_async_copy(weights.at[r], w_v.at[r], w_sem.at[r])

    def in_copy(src, m):
        return pltpu.make_async_copy(src.at[m, core], inp.at[m, pl.ds(mine, strip), :], in_sem.at[m])

    for r in range(3):
        w_copy(r).start()

    @pl.when(first)
    def _():
        for m in range(batches):
            in_copy(images, m).start()

    @pl.when(last)
    def _():
        for m in range(batches):
            in_copy(cotangent, m).start()

    barrier = pltpu.get_barrier_semaphore()
    for s in range(sections):
        @pl.when((sec >= s - 1) & (sec <= s + 1))
        def _():
            def greet(i, carry):
                @pl.when((s != sec) | (i != row))
                def _():
                    pl.semaphore_signal(barrier, inc=1, device_id=(jnp.int32(s), i), device_id_type=MESH)
                return carry
            lax.fori_loop(0, strips, greet, 0)

    gain_sum[...] = jnp.zeros_like(gain_sum)
    shift_sum[...] = jnp.zeros_like(shift_sum)

    @pl.when(decoder)
    def _():
        wide = cols // 2
        lanes = lax.broadcasted_iota(jnp.int32, (cols, wide), 1)
        places = lax.broadcasted_iota(jnp.int32, (cols, wide), 0)
        pick = (lax.shift_right_logical(places, 1) == lanes).astype(F32)
        table = lax.dot_general(
            pick, switches[...].astype(F32), (((1,), (1,)), ((), ())), preferred_element_type=F32
        )
        odd = jnp.bitwise_and(lax.broadcasted_iota(jnp.int32, (cols, 128), 0), 1).astype(F32)
        windows = strip // cols // 2
        for m in range(batches):
            for i in range(2):
                for w in range(windows):
                    at = (m * 2 + i) * windows + w
                    value = jnp.broadcast_to(table[:, at : at + 1], (cols, 128))
                    for p in range(2):
                        hit = (jnp.abs(value - (2.0 * p + odd)) < 0.5).astype(F32).astype(BF16)
                        mask_own[m, i, pl.ds((2 * w + p) * cols, cols), :] = hit
        for m in range(batches):
            mask_v[m, pl.ds(mine, strip), :] = mask_own[m, core]

    @pl.when(jnp.logical_not(decoder))
    def _():
        mask_v[...] = jnp.ones_like(mask_v)

    near = 1 + jnp.where(sec > 0, 1, 0) + jnp.where(sec < sections - 1, 1, 0)
    pl.semaphore_wait(barrier, near * strips - 1)

    def remote(src, dst, send, recv, s, i):
        return pltpu.make_async_remote_copy(
            src_ref=src, dst_ref=dst, send_sem=send, recv_sem=recv, device_id=(s, i), device_id_type=MESH
        )

    def to_partner(src_at, dst_at, send, recv):
        return remote(src_at(1 - core), dst_at(pl.ds(mine, strip)), send, recv, sec, partner)

    def start_argument(src_at, dst_at, pair_sems, edge_sems):
        to_partner(src_at, dst_at, *pair_sems).start()

        @pl.when((core == 1) & has_down)
        def _():
            for i in range(2):
                remote(
                    src_at(i, pl.ds(strip - cols, cols)), dst_at(pl.ds(0, cols)),
                    edge_sems[0].at[i], edge_sems[1].at[0], sec, row + 1 + i,
                ).start()

        @pl.when((core == 0) & has_up)
        def _():
            for i in range(2):
                remote(
                    src_at(i, pl.ds(0, cols)), dst_at(pl.ds(cols + px, cols)),
                    edge_sems[0].at[i], edge_sems[1].at[1], sec, row - 2 + i,
                ).start()

    def argument_arrived(src_at, dst_at, pair_sems, edge_sems):
        to_partner(src_at, dst_at, *pair_sems).wait_recv()

        @pl.when(has_up)
        def _():
            remote(
                src_at(0, pl.ds(0, cols)), dst_at(pl.ds(0, cols)), edge_sems[0].at[0], edge_sems[1].at[0], sec, row
            ).wait_recv()

        @pl.when(has_down)
        def _():
            remote(
                src_at(0, pl.ds(0, cols)), dst_at(pl.ds(cols + px, cols)), edge_sems[0].at[0], edge_sems[1].at[1],
                sec, row,
            ).wait_recv()

    def argument_sent(src_at, dst_at, pair_sems, edge_sems):
        to_partner(src_at, dst_at, *pair_sems).wait_send()

        @pl.when(((core == 1) & has_down) | ((core == 0) & has_up))
        def _():
            for i in range(2):
                remote(
                    src_at(i, pl.ds(0, cols)), dst_at(pl.ds(0, cols)), edge_sems[0].at[i], edge_sems[1].at[0], sec, row
                ).wait_send()

    def input_parts(src, m):
        return (
            lambda i, r=pl.ds(0, strip): src.at[m, i, r, :],
            lambda r: inp.at[m, r, :],
            (pi_s.at[m], pi_r.at[m]),
            (ie_s.at[m], ie_r.at[m]),
        )

    mask_parts = (
        lambda i, r=pl.ds(0, strip): mask_own.at[:, i, r, :],
        lambda r: mask_v.at[:, r, :],
        (mp_s, mp_r),
        (me_s, me_r),
    )

    @pl.when(first)
    def _():
        for m in range(batches):
            start_argument(*input_parts(images, m))

    @pl.when(last)
    def _():
        for m in range(batches):
            start_argument(*input_parts(cotangent, m))

    @pl.when(decoder)
    def _():
        start_argument(*mask_parts)

    def affine_sends():
        return (
            remote(gains, gain_prev, gp_s.at[0], gp_r.at[0], sec + 1, row),
            remote(shifts, shift_prev, gp_s.at[1], gp_r.at[1], sec + 1, row),
        )

    @pl.when(sec < sections - 1)
    def _():
        for copy in affine_sends():
            copy.start()

    def block_sends(src, src_from, dst, send, recv, m, s):
        def one(k, h, src_row, dst_row, rows, i):
            part = pl.ds(h * half, half)
            return remote(
                src.at[m, pl.ds(src_from + src_row, rows), part], dst.at[m, pl.ds(dst_row, rows), part],
                send.at[m, k, h], recv.at[m, k, h], s, i,
            )
        return (
            (None, lambda h: one(0, h, 0, cols, px, row)),
            (has_down, lambda h: one(1, h, px - cols, 0, cols, row + 2)),
            (has_up, lambda h: one(2, h, 0, cols + px, cols, row - 2)),
        )

    def each(parts, h, act):
        for cond, make in parts:
            if cond is None:
                act(make(h))
            else:
                @pl.when(cond)
                def _():
                    act(make(h))

    def arrived(parts):
        (_, body), (_, to_down), (_, to_up) = parts
        for h in range(2):
            body(h).wait_recv()
        edges_arrived(to_down, to_up)

    def edges_arrived(to_down, to_up):
        @pl.when(has_up)
        def _():
            for h in range(2):
                to_down(h).wait_recv()

        @pl.when(has_down)
        def _():
            for h in range(2):
                to_up(h).wait_recv()

    def start(copy):
        copy.start()

    def sent(copy):
        copy.wait_send()

    def z_sends(m, s):
        return block_sends(zown, cols, zin, fz_s, fz_r, m, s)

    def own_edges(m):
        return block_sends(zown, cols, zown, oe_s, oe_r, m, sec)[1:]

    def dy_sends(m, s):
        return block_sends(dyout, 0, dyin, bz_s, bz_r, m, s)

    def stat_copy(src, dst, send, recv, m, s, i):
        return remote(src.at[m], dst.at[m, row], send.at[m, i], recv.at[m], s, i)

    def stats_each(src, dst, send, recv, m, s, same, act):
        def one(d, carry):
            i = row + d
            act(stat_copy(src, dst, send, recv, m, s, jnp.where(i >= strips, i - strips, i)))
            return carry
        lax.fori_loop(1 if same else 0, strips, one, 0)

    def start_stats(src, dst, send, recv, m, s, same):
        stats_each(src, dst, send, recv, m, s, same, start)
        if same:
            pltpu.make_async_copy(src.at[m], dst.at[m, row], recv.at[m]).start()

    def wait_stats(dst, recv, m):
        pltpu.make_async_copy(dst.at[m], dst.at[m], recv.at[m]).wait()

    down_stats = (stat_out, zin_stat, fs_s, fs_r)
    same_stats = (stat_out, own_stat, os_s, os_r)
    back_stats = (sums_out, dy_stat, bs_s, bs_r)
    seed_stats = (seed_sums, dy_stat, ls_s, bs_r)

    def join(stats_ref, m):
        means, squares = stats_ref[m, :, 0, :], stats_ref[m, :, 1, :]
        mean = jnp.sum(means, 0, keepdims=True) / float(strips)
        off = means - mean
        var = (jnp.sum(squares, 0, keepdims=True) + local * jnp.sum(off * off, 0, keepdims=True)) / total
        at = (jnp.maximum(row - 2, 0), row, jnp.minimum(row + 2, strips - 1))
        return lax.rsqrt(var + EPSILON), [stats_ref[m, i, pl.ds(0, 1), :] - mean for i in at]

    def kind(g):
        return 0 if g == 0 else 2 if g == groups - 1 else 1

    def inside(g, values):
        if kind(g) == 1:
            return values
        return jnp.where(has_up if kind(g) == 0 else has_down, values, jnp.zeros_like(values))

    def group(g):
        return pl.ds(g * cols, cols)

    column = lax.broadcasted_iota(jnp.int32, (1, cols, half), 1)

    def taps_joined(parts, left, right):
        def moved(values, by, edge):
            turned = pltpu.roll(values, by % px, 0).reshape(px // cols, cols, half)
            return jnp.where(column == edge, 0.0, turned).reshape(px, half)
        return parts[1] + moved(parts[left], 1, 0) + moved(parts[right], -1, cols - 1)

    def forward(m):
        @pl.when(first)
        def _():
            in_copy(images, m).wait()
            argument_arrived(*input_parts(images, m))
            for g in range(groups):
                ub[m, group(g), :] = inside(g, inp[m, group(g), :])

        @pl.when(sec > 0)
        def _():
            @pl.when(m == 0)
            def _():
                for copy in affine_sends():
                    copy.wait_recv()

                @pl.when(decoder)
                def _():
                    argument_arrived(*mask_parts)

            wait_stats(zin_stat, fs_r, m)
            inv, offs = join(zin_stat, m)
            prev_coef[m, pl.ds(0, 1), :] = inv
            prev_coef[m, pl.ds(1, 1), :] = offs[1]
            slant = 0.5 * inv * gain_prev[...]
            level = [slant * off + 0.5 * shift_prev[...] for off in offs]
            arrived(z_sends(m, sec))
            for g in range(groups):
                halved = zin[m, group(g), :].astype(F32) * slant + level[kind(g)]
                turn = jnp.tanh(halved)
                bent = halved * turn
                gate = jnp.concatenate([mask_v[m, group(g), :].astype(F32)] * (ch // 128), axis=1)
                ub[m, group(g), :] = inside(g, ((halved + bent) * gate).astype(BF16))
                if kind(g) == 1:
                    slope_prev[m, pl.ds((g - 1) * cols, cols), :] = (0.5 + 0.5 * turn) * (1.0 + halved - bent)

        @pl.when(m == 0)
        def _():
            for r in range(3):
                w_copy(r).wait()

        for h in range(2):
            part = pl.ds(h * half, half)
            parts = []
            for c in range(3):
                acc = jnp.zeros((px, half), F32)
                for r in range(3):
                    acc += jnp.dot(
                        ub[m, pl.ds(r * cols, px), :], w_v[r, pl.ds(c * ch, ch), part], preferred_element_type=F32
                    )
                parts.append(acc)
            conv = taps_joined(parts, 0, 2)
            mean = jnp.sum(conv, 0, keepdims=True) / local
            conv = conv - mean
            stat_out[m, pl.ds(0, 1), part] = mean
            stat_out[m, pl.ds(1, 1), part] = jnp.sum(conv * conv, 0, keepdims=True)
            zown[m, centre, part] = conv.astype(BF16)

            @pl.when(sec < sections - 1)
            def _():
                each(z_sends(m, sec + 1), h, start)
                if h == 1:
                    start_stats(*down_stats, m, sec + 1, False)

        start_stats(*same_stats, m, sec, True)
        for h in range(2):
            each(own_edges(m), h, start)

    def finish(m):
        wait_stats(own_stat, os_r, m)
        inv, offs = join(own_stat, m)
        scale = inv * gains[...]
        own_coef[m, pl.ds(0, 1), :] = inv
        own_coef[m, pl.ds(1, 1), :] = scale
        for k in range(3):
            own_coef[m, pl.ds(2 + k, 1), :] = offs[k]
        slant = 0.5 * scale
        level = [slant * off + 0.5 * shifts[...] for off in offs]
        (_, to_down), (_, to_up) = own_edges(m)
        edges_arrived(to_down, to_up)

        @pl.when(last)
        def _():
            in_copy(cotangent, m).wait()
            argument_arrived(*input_parts(cotangent, m))
            sums = jnp.zeros((cols, ch), F32)
            cross = jnp.zeros((cols, ch), F32)
            for g in range(groups):
                z = zown[m, group(g), :].astype(F32)
                halved = z * slant + level[kind(g)]
                turn = jnp.tanh(halved)
                bent = halved * turn
                dy = inp[m, group(g), :].astype(F32) * ((0.5 + 0.5 * turn) * (1.0 + halved - bent))
                dyin[m, group(g), :] = dy.astype(BF16)
                if kind(g) == 1:
                    out_v[m, pl.ds((g - 1) * cols, cols), :] = (halved + bent).astype(BF16)
                    sums += dy
                    cross += dy * z
            one = jnp.sum(sums, 0, keepdims=True)
            seed_sums[m, pl.ds(0, 1), :] = one
            seed_sums[m, pl.ds(1, 1), :] = inv * (jnp.sum(cross, 0, keepdims=True) + offs[1] * one)
            start_stats(*seed_stats, m, sec, True)

        @pl.when(jnp.logical_not(last))
        def _():
            for g in range(1, groups - 1):
                halved = zown[m, group(g), :].astype(F32) * slant + level[1]
                out_v[m, pl.ds((g - 1) * cols, cols), :] = (halved + halved * jnp.tanh(halved)).astype(BF16)

        for copy in result_copies(out_v, outs, out_sem, po_s, po_r, m):
            copy.start()

    def result_copies(src, dst, sem, send, recv, m):
        here, there = pl.multiple_of(strip * core, cols), pl.multiple_of(strip * (1 - core), cols)
        return (
            pltpu.make_async_copy(src.at[m, pl.ds(here, strip), :], dst.at[m, core], sem.at[m]),
            remote(src.at[m, pl.ds(there, strip), :], dst.at[m, core], send.at[m], recv.at[m], sec, partner),
        )

    def backward(m):
        wait_stats(dy_stat, bs_r, m)
        first_sum = jnp.sum(dy_stat[m, :, 0, :], 0, keepdims=True)
        cross_sum = jnp.sum(dy_stat[m, :, 1, :], 0, keepdims=True)
        shift_sum[...] += first_sum
        gain_sum[...] += cross_sum
        inv = own_coef[m, pl.ds(0, 1), :]
        scale = own_coef[m, pl.ds(1, 1), :]
        tilt = scale * inv * (cross_sum / total)
        base = [scale * (first_sum / total) + tilt * own_coef[m, pl.ds(2 + k, 1), :] for k in range(3)]

        @pl.when(sec < sections - 1)
        def _():
            arrived(dy_sends(m, sec))

        for g in range(groups):
            dz = dyin[m, group(g), :].astype(F32) * scale - zown[m, group(g), :].astype(F32) * tilt - base[kind(g)]
            dzb[m, group(g), :] = inside(g, dz.astype(BF16))

        for h in range(2):
            part = pl.ds(h * half, half)
            parts = []
            for c in range(3):
                acc = jnp.zeros((px, half), F32)
                for r in range(3):
                    acc += lax.dot_general(
                        dzb[m, pl.ds((2 - r) * cols, px), :], w_v[r, pl.ds(c * ch + h * half, half), :],
                        (((1,), (1,)), ((), ())), preferred_element_type=F32,
                    )
                parts.append(acc)
            gate = jnp.concatenate([mask_v[m, centre, :].astype(F32)] * (half // 128), axis=1)
            du = (taps_joined(parts, 2, 0) * gate).astype(BF16)
            gin_v[m, :, part] = du

            @pl.when(sec > 0)
            def _():
                dy = du.astype(F32) * slope_prev[m, :, part]
                dyout[m, :, part] = dy.astype(BF16)
                one = jnp.sum(dy, 0, keepdims=True)
                cross = jnp.sum(dy * zin[m, centre, part].astype(F32), 0, keepdims=True)
                sums_out[m, pl.ds(0, 1), part] = one
                sums_out[m, pl.ds(1, 1), part] = prev_coef[m, pl.ds(0, 1), part] * (
                    cross + prev_coef[m, pl.ds(1, 1), part] * one
                )
                each(dy_sends(m, sec - 1), h, start)
                if h == 1:
                    start_stats(*back_stats, m, sec - 1, False)

        for copy in result_copies(gin_v, grads_in, gin_sem, pg_s, pg_r, m):
            copy.start()

    def step(t, carry):
        ahead = t - sec
        behind = t - (2 * sections - 1 - sec)

        @pl.when((ahead >= 0) & (ahead < batches))
        def _():
            forward(ahead)

        done = ahead - jnp.where(last, 0, 1)

        @pl.when((behind >= 0) & (behind < batches))
        def _():
            backward(behind)

        @pl.when((done >= 0) & (done < batches))
        def _():
            finish(done)

        return carry

    lax.fori_loop(0, 2 * sections - 1 + batches, step, 0)

    place = lax.broadcasted_iota(jnp.int32, (cols, ch), 0)
    for m in range(batches):
        for g in range(1, groups - 1):
            values = dzb[m, group(g), :].astype(F32)
            at = pl.ds((m * (groups - 2) + g - 1) * cols, cols)
            dzside[0, at, :] = jnp.where(place == cols - 1, 0.0, pltpu.roll(values, cols - 1, 0)).astype(BF16)
            dzside[1, at, :] = values.astype(BF16)
            dzside[2, at, :] = jnp.where(place == 0, 0.0, pltpu.roll(values, 1, 0)).astype(BF16)

    def dw_copy(r, c):
        return pltpu.make_async_copy(dw_v.at[r, c], weight_part.at[r, c], dw_sem.at[r, c])

    def taps(r, carry):
        left = ub[:, pl.ds(pl.multiple_of(r * cols, cols), px), :].reshape(batches * px, ch)
        for c in range(3):
            for h in range(2):
                part = lax.dot_general(
                    left[:, h * half : (h + 1) * half], dzside[c], (((0,), (0,)), ((), ())),
                    preferred_element_type=F32,
                )
                dw_v[r, c, pl.ds(h * half, half), :] = part.astype(BF16)
            dw_copy(r, c).start()
        return carry

    lax.fori_loop(0, 3, taps, 0)

    for r in range(3):
        for c in range(3):
            dw_copy(r, c).wait()

    @pl.when(decoder)
    def _():
        argument_sent(*mask_parts)

    @pl.when(sec < sections - 1)
    def _():
        for copy in affine_sends():
            copy.wait_send()

    def drain(m, carry):
        for src, dst, sems in ((out_v, outs, (out_sem, po_s, po_r)), (gin_v, grads_in, (gin_sem, pg_s, pg_r))):
            here, there = result_copies(src, dst, *sems, m)
            here.wait()
            there.wait_send()
            remote(
                src.at[m, pl.ds(0, strip), :], dst.at[m, 1 - core], sems[1].at[m], sems[2].at[m], sec, partner
            ).wait_recv()

        @pl.when(first)
        def _():
            argument_sent(*input_parts(images, m))

        @pl.when(last)
        def _():
            argument_sent(*input_parts(cotangent, m))
            stats_each(*seed_stats, m, sec, True, sent)

        @pl.when(sec < sections - 1)
        def _():
            stats_each(*down_stats, m, sec + 1, False, sent)
            for h in range(2):
                each(z_sends(m, sec + 1), h, sent)

        stats_each(*same_stats, m, sec, True, sent)
        for h in range(2):
            each(own_edges(m), h, sent)

        @pl.when(sec > 0)
        def _():
            stats_each(*back_stats, m, sec - 1, False, sent)
            for h in range(2):
                each(dy_sends(m, sec - 1), h, sent)

        return carry

    lax.fori_loop(0, batches, drain, 0)


def body(images, switches, conv_weights, gains, shifts, cotangent):
    sections = lax.axis_size("section")
    strips = lax.axis_size("rows")
    batches, pictures, strip_rows, cols, ch = images.shape
    strip = strip_rows * cols
    px = 2 * strip
    tall = px + 2 * cols
    anywhere = pl.BlockSpec(memory_space=pl.ANY)
    vmem = pl.BlockSpec(memory_space=pltpu.VMEM)
    dma = pltpu.SemaphoreType.DMA
    flops = 3 * 2 * 9 * ch * ch * batches * px
    outs, grads_in, weight_part, gain_sum, shift_sum = pl.pallas_call(
        functools.partial(kernel, sections, strips, cols),
        out_shape=(
            jax.ShapeDtypeStruct((batches, pictures, strip, ch), BF16),
            jax.ShapeDtypeStruct((batches, pictures, strip, ch), BF16),
            jax.ShapeDtypeStruct((3, 3, ch, ch), BF16),
            jax.ShapeDtypeStruct((1, ch), F32),
            jax.ShapeDtypeStruct((1, ch), F32),
        ),
        in_specs=[anywhere, anywhere, anywhere, vmem, vmem, vmem],
        out_specs=(anywhere, anywhere, anywhere, vmem, vmem),
        scratch_shapes=[
            pltpu.VMEM((3, 3 * ch, ch), BF16),
            pltpu.VMEM((batches, tall, ch), BF16),
            pltpu.VMEM((batches, 2, strip, 128), BF16),
            pltpu.VMEM((batches, tall, 128), BF16),
            pltpu.VMEM((1, ch), F32),
            pltpu.VMEM((1, ch), F32),
            pltpu.VMEM((batches, tall, ch), BF16),
            pltpu.VMEM((batches, strips, 2, ch), F32),
            pltpu.VMEM((batches, tall, ch), BF16),
            pltpu.VMEM((batches, strips, 2, ch), F32),
            pltpu.VMEM((batches, tall, ch), BF16),
            pltpu.VMEM((batches, px, ch), F32),
            pltpu.VMEM((batches, 2, ch), F32),
            pltpu.VMEM((batches, 8, ch), F32),
            pltpu.VMEM((batches, tall, ch), BF16),
            pltpu.VMEM((batches, strips, 2, ch), F32),
            pltpu.VMEM((batches, tall, ch), BF16),
            pltpu.VMEM((3, batches * px, ch), BF16),
            pltpu.VMEM((batches, px, ch), BF16),
            pltpu.VMEM((batches, 2, ch), F32),
            pltpu.VMEM((batches, 2, ch), F32),
            pltpu.VMEM((batches, 2, ch), F32),
            pltpu.VMEM((batches, px, ch), BF16),
            pltpu.VMEM((batches, px, ch), BF16),
            pltpu.VMEM((3, 3, ch, ch), BF16),
            dma((3,)),
            dma((batches,)),
            dma((batches,)), dma((batches,)),
            dma((batches, 2)), dma((batches, 2)),
            dma, dma,
            dma((2,)), dma((2,)),
            dma((2,)), dma((2,)),
            dma((batches, 3, 2)), dma((batches, 3, 2)),
            dma((batches, strips)), dma((batches,)),
            dma((batches, 3, 2)), dma((batches, 3, 2)),
            dma((batches, strips)), dma((batches,)),
            dma((batches, 3, 2)), dma((batches, 3, 2)),
            dma((batches, strips)), dma((batches,)),
            dma((batches, strips)),
            dma((batches,)), dma((batches,)), dma((batches,)),
            dma((batches,)), dma((batches,)), dma((batches,)),
            dma((3, 3)),
        ],
        compiler_params=pltpu.CompilerParams(
            collective_id=0, has_side_effects=True, vmem_limit_bytes=56 * 2**20
        ),
        cost_estimate=pl.CostEstimate(
            flops=flops, bytes_accessed=2 * 9 * ch * ch * 2, transcendentals=0
        ),
    )(
        images.reshape(batches, pictures, strip, ch),
        cotangent.reshape(batches, pictures, strip, ch),
        conv_weights.reshape(3, 3 * ch, ch),
        gains,
        shifts,
        switches.reshape(-1, switches.shape[-1]),
    )
    weight_grad = lax.psum_scatter(weight_part, "rows", scatter_dimension=2, tiled=True).astype(F32)
    shape = (1, batches, pictures, strip_rows, cols, ch)
    return (outs.reshape(shape), grads_in.reshape(shape), weight_grad[None], gain_sum, shift_sum)


def solution(mesh):
    return jax.shard_map(
        body,
        mesh=mesh,
        in_specs=(
            P(None, None, "rows", None, None),
            P(None, None, "rows", None),
            P("section", None, None, None, None),
            P("section", None),
            P("section", None),
            P(None, None, "rows", None, None),
        ),
        out_specs=(
            P("section", None, None, "rows", None, None),
            P("section", None, None, "rows", None, None),
            P("section", None, None, "rows", None),
            P("section", None),
            P("section", None),
        ),
        check_vma=False,
    )
```

```python
import functools

import jax
import jax.numpy as jnp
from jax import lax
from jax.experimental import pallas as pl
from jax.experimental.pallas import tpu as pltpu
from jax.sharding import PartitionSpec as P

EPSILON = 1e-05
MESH = pl.DeviceIdType.MESH
BF16 = jnp.bfloat16
F32 = jnp.float32


def kernel(
    sections, strips, cols,
    images, cotangent, weights, gains, shifts, switches,
    outs, grads_in, weight_part, gain_sum, shift_sum,
    w_v, wt_v, inp, mask_own, mask_v, gain_prev, shift_prev, zin, zin_stat, zown, own_stat, ub, slope_prev,
    prev_coef, own_coef, dyin, dy_stat, dzb, dzside, dyout, stat_out, sums_out, seed_sums, out_v, gin_v, dw_v,
    w_sem, in_sem, pi_s, pi_r, ie_s, ie_r, mp_s, mp_r, me_s, me_r, gp_s, gp_r,
    fz_s, fz_r, fs_s, fs_r, oe_s, oe_r, os_s, os_r, bz_s, bz_r, bs_s, bs_r, ls_s,
    out_sem, po_s, po_r, gin_sem, pg_s, pg_r, dw_sem,
):
    sec = lax.axis_index("section")
    row = lax.axis_index("rows")
    batches, tall, ch = inp.shape
    px = tall - 2 * cols
    strip = px // 2
    groups = tall // cols
    half = ch // 2
    total = float(px * strips)
    local = float(px)
    first, last, decoder = sec == 0, sec == sections - 1, sec == sections // 2
    core = row % 2
    partner = row + 1 - 2 * core
    has_up, has_down = row >= 2, row < strips - 2
    centre = pl.ds(cols, px)
    mine = pl.multiple_of(cols + strip * core, cols)

    def w_copy(r):
        return pltpu.make_async_copy(weights.at[r], w_v.at[r], w_sem.at[r])

    def in_copy(src, m):
        return pltpu.make_async_copy(src.at[m, core], inp.at[m, pl.ds(mine, strip), :], in_sem.at[m])

    for r in range(3):
        w_copy(r).start()

    @pl.when(first)
    def _():
        for m in range(batches):
            in_copy(images, m).start()

    @pl.when(last)
    def _():
        for m in range(batches):
            in_copy(cotangent, m).start()

    barrier = pltpu.get_barrier_semaphore()
    for s in range(sections):
        @pl.when((sec >= s - 1) & (sec <= s + 1))
        def _():
            def greet(i, carry):
                @pl.when((s != sec) | (i != row))
                def _():
                    pl.semaphore_signal(barrier, inc=1, device_id=(jnp.int32(s), i), device_id_type=MESH)
                return carry
            lax.fori_loop(0, strips, greet, 0)

    gain_sum[...] = jnp.zeros_like(gain_sum)
    shift_sum[...] = jnp.zeros_like(shift_sum)

    @pl.when(decoder)
    def _():
        wide = cols // 2
        lanes = lax.broadcasted_iota(jnp.int32, (cols, wide), 1)
        places = lax.broadcasted_iota(jnp.int32, (cols, wide), 0)
        pick = (lax.shift_right_logical(places, 1) == lanes).astype(F32)
        table = lax.dot_general(
            pick, switches[...].astype(F32), (((1,), (1,)), ((), ())), preferred_element_type=F32
        )
        odd = jnp.bitwise_and(lax.broadcasted_iota(jnp.int32, (cols, 128), 0), 1).astype(F32)
        windows = strip // cols // 2
        for m in range(batches):
            for i in range(2):
                for w in range(windows):
                    at = (m * 2 + i) * windows + w
                    value = jnp.broadcast_to(table[:, at : at + 1], (cols, 128))
                    for p in range(2):
                        hit = (jnp.abs(value - (2.0 * p + odd)) < 0.5).astype(F32).astype(BF16)
                        mask_own[m, i, pl.ds((2 * w + p) * cols, cols), :] = hit
        for m in range(batches):
            mask_v[m, pl.ds(mine, strip), :] = mask_own[m, core]

    @pl.when(jnp.logical_not(decoder))
    def _():
        mask_v[...] = jnp.ones_like(mask_v)

    near = 1 + jnp.where(sec > 0, 1, 0) + jnp.where(sec < sections - 1, 1, 0)
    pl.semaphore_wait(barrier, near * strips - 1)

    def remote(src, dst, send, recv, s, i):
        return pltpu.make_async_remote_copy(
            src_ref=src, dst_ref=dst, send_sem=send, recv_sem=recv, device_id=(s, i), device_id_type=MESH
        )

    def to_partner(src_at, dst_at, send, recv):
        return remote(src_at(1 - core), dst_at(pl.ds(mine, strip)), send, recv, sec, partner)

    def start_argument(src_at, dst_at, pair_sems, edge_sems):
        to_partner(src_at, dst_at, *pair_sems).start()

        @pl.when((core == 1) & has_down)
        def _():
            for i in range(2):
                remote(
                    src_at(i, pl.ds(strip - cols, cols)), dst_at(pl.ds(0, cols)),
                    edge_sems[0].at[i], edge_sems[1].at[0], sec, row + 1 + i,
                ).start()

        @pl.when((core == 0) & has_up)
        def _():
            for i in range(2):
                remote(
                    src_at(i, pl.ds(0, cols)), dst_at(pl.ds(cols + px, cols)),
                    edge_sems[0].at[i], edge_sems[1].at[1], sec, row - 2 + i,
                ).start()

    def argument_arrived(src_at, dst_at, pair_sems, edge_sems):
        to_partner(src_at, dst_at, *pair_sems).wait_recv()

        @pl.when(has_up)
        def _():
            remote(
                src_at(0, pl.ds(0, cols)), dst_at(pl.ds(0, cols)), edge_sems[0].at[0], edge_sems[1].at[0], sec, row
            ).wait_recv()

        @pl.when(has_down)
        def _():
            remote(
                src_at(0, pl.ds(0, cols)), dst_at(pl.ds(cols + px, cols)), edge_sems[0].at[0], edge_sems[1].at[1],
                sec, row,
            ).wait_recv()

    def argument_sent(src_at, dst_at, pair_sems, edge_sems):
        to_partner(src_at, dst_at, *pair_sems).wait_send()

        @pl.when(((core == 1) & has_down) | ((core == 0) & has_up))
        def _():
            for i in range(2):
                remote(
                    src_at(i, pl.ds(0, cols)), dst_at(pl.ds(0, cols)), edge_sems[0].at[i], edge_sems[1].at[0], sec, row
                ).wait_send()

    def input_parts(src, m):
        return (
            lambda i, r=pl.ds(0, strip): src.at[m, i, r, :],
            lambda r: inp.at[m, r, :],
            (pi_s.at[m], pi_r.at[m]),
            (ie_s.at[m], ie_r.at[m]),
        )

    mask_parts = (
        lambda i, r=pl.ds(0, strip): mask_own.at[:, i, r, :],
        lambda r: mask_v.at[:, r, :],
        (mp_s, mp_r),
        (me_s, me_r),
    )

    @pl.when(first)
    def _():
        for m in range(batches):
            start_argument(*input_parts(images, m))

    @pl.when(last)
    def _():
        for m in range(batches):
            start_argument(*input_parts(cotangent, m))

    @pl.when(decoder)
    def _():
        start_argument(*mask_parts)

    def affine_sends():
        return (
            remote(gains, gain_prev, gp_s.at[0], gp_r.at[0], sec + 1, row),
            remote(shifts, shift_prev, gp_s.at[1], gp_r.at[1], sec + 1, row),
        )

    @pl.when(sec < sections - 1)
    def _():
        for copy in affine_sends():
            copy.start()

    def block_sends(src, src_from, dst, send, recv, m, s):
        def one(k, h, src_row, dst_row, rows, i):
            part = pl.ds(h * half, half)
            return remote(
                src.at[m, pl.ds(src_from + src_row, rows), part], dst.at[m, pl.ds(dst_row, rows), part],
                send.at[m, k, h], recv.at[m, k, h], s, i,
            )
        return (
            (None, lambda h: one(0, h, 0, cols, px, row)),
            (has_down, lambda h: one(1, h, px - cols, 0, cols, row + 2)),
            (has_up, lambda h: one(2, h, 0, cols + px, cols, row - 2)),
        )

    def each(parts, h, act):
        for cond, make in parts:
            if cond is None:
                act(make(h))
            else:
                @pl.when(cond)
                def _():
                    act(make(h))

    def arrived(parts):
        (_, body), (_, to_down), (_, to_up) = parts
        for h in range(2):
            body(h).wait_recv()
        edges_arrived(to_down, to_up)

    def edges_arrived(to_down, to_up):
        @pl.when(has_up)
        def _():
            for h in range(2):
                to_down(h).wait_recv()

        @pl.when(has_down)
        def _():
            for h in range(2):
                to_up(h).wait_recv()

    def start(copy):
        copy.start()

    def sent(copy):
        copy.wait_send()

    def z_sends(m, s):
        return block_sends(zown, cols, zin, fz_s, fz_r, m, s)

    def own_edges(m):
        return block_sends(zown, cols, zown, oe_s, oe_r, m, sec)[1:]

    def dy_sends(m, s):
        return block_sends(dyout, 0, dyin, bz_s, bz_r, m, s)

    def stat_copy(src, dst, send, recv, m, s, i):
        return remote(src.at[m], dst.at[m, row], send.at[m, i], recv.at[m], s, i)

    def stats_each(src, dst, send, recv, m, s, same, act):
        def one(d, carry):
            i = row + d
            act(stat_copy(src, dst, send, recv, m, s, jnp.where(i >= strips, i - strips, i)))
            return carry
        lax.fori_loop(1 if same else 0, strips, one, 0)

    def start_stats(src, dst, send, recv, m, s, same):
        stats_each(src, dst, send, recv, m, s, same, start)
        if same:
            pltpu.make_async_copy(src.at[m], dst.at[m, row], recv.at[m]).start()

    def wait_stats(dst, recv, m):
        pltpu.make_async_copy(dst.at[m], dst.at[m], recv.at[m]).wait()

    down_stats = (stat_out, zin_stat, fs_s, fs_r)
    same_stats = (stat_out, own_stat, os_s, os_r)
    back_stats = (sums_out, dy_stat, bs_s, bs_r)
    seed_stats = (seed_sums, dy_stat, ls_s, bs_r)

    def join(stats_ref, m):
        means, squares = stats_ref[m, :, 0, :], stats_ref[m, :, 1, :]
        mean = jnp.sum(means, 0, keepdims=True) / float(strips)
        off = means - mean
        var = (jnp.sum(squares, 0, keepdims=True) + local * jnp.sum(off * off, 0, keepdims=True)) / total
        at = (jnp.maximum(row - 2, 0), row, jnp.minimum(row + 2, strips - 1))
        return lax.rsqrt(var + EPSILON), [stats_ref[m, i, pl.ds(0, 1), :] - mean for i in at]

    def kind(g):
        return 0 if g == 0 else 2 if g == groups - 1 else 1

    def inside(g, values):
        if kind(g) == 1:
            return values
        return jnp.where(has_up if kind(g) == 0 else has_down, values, jnp.zeros_like(values))

    def group(g):
        return pl.ds(g * cols, cols)

    column = lax.broadcasted_iota(jnp.int32, (1, cols, half), 1)

    def taps_joined(parts, left, right):
        def moved(values, by, edge):
            turned = pltpu.roll(values, by % px, 0).reshape(px // cols, cols, half)
            return jnp.where(column == edge, 0.0, turned).reshape(px, half)
        return parts[1] + moved(parts[left], 1, 0) + moved(parts[right], -1, cols - 1)

    def forward(m):
        @pl.when(first)
        def _():
            in_copy(images, m).wait()
            argument_arrived(*input_parts(images, m))
            for g in range(groups):
                ub[m, group(g), :] = inside(g, inp[m, group(g), :])

        @pl.when(sec > 0)
        def _():
            @pl.when(m == 0)
            def _():
                for copy in affine_sends():
                    copy.wait_recv()

                @pl.when(decoder)
                def _():
                    argument_arrived(*mask_parts)

            wait_stats(zin_stat, fs_r, m)
            inv, offs = join(zin_stat, m)
            prev_coef[m, pl.ds(0, 1), :] = inv
            prev_coef[m, pl.ds(1, 1), :] = offs[1]
            slant = 0.5 * inv * gain_prev[...]
            level = [slant * off + 0.5 * shift_prev[...] for off in offs]
            arrived(z_sends(m, sec))
            for g in range(groups):
                halved = zin[m, group(g), :].astype(F32) * slant + level[kind(g)]
                turn = jnp.tanh(halved)
                bent = halved * turn
                gate = jnp.concatenate([mask_v[m, group(g), :].astype(F32)] * (ch // 128), axis=1)
                ub[m, group(g), :] = inside(g, ((halved + bent) * gate).astype(BF16))
                if kind(g) == 1:
                    slope_prev[m, pl.ds((g - 1) * cols, cols), :] = (0.5 + 0.5 * turn) * (1.0 + halved - bent)

        @pl.when(first & (m == 0))
        def _():
            for r in range(3):
                w_copy(r).wait()

        for h in range(2):
            part = pl.ds(h * half, half)
            parts = []
            for c in range(3):
                acc = jnp.zeros((px, half), F32)
                for r in range(3):
                    acc += jnp.dot(
                        ub[m, pl.ds(r * cols, px), :], w_v[r, pl.ds(c * ch, ch), part], preferred_element_type=F32
                    )
                parts.append(acc)
            conv = taps_joined(parts, 0, 2)
            mean = jnp.sum(conv, 0, keepdims=True) / local
            conv = conv - mean
            stat_out[m, pl.ds(0, 1), part] = mean
            stat_out[m, pl.ds(1, 1), part] = jnp.sum(conv * conv, 0, keepdims=True)
            zown[m, centre, part] = conv.astype(BF16)

            @pl.when(sec < sections - 1)
            def _():
                if h == 1:
                    start_stats(*down_stats, m, sec + 1, False)
                each(z_sends(m, sec + 1), h, start)

        start_stats(*same_stats, m, sec, True)
        for h in range(2):
            each(own_edges(m), h, start)

    def finish(m):
        wait_stats(own_stat, os_r, m)
        inv, offs = join(own_stat, m)
        scale = inv * gains[...]
        own_coef[m, pl.ds(0, 1), :] = inv
        own_coef[m, pl.ds(1, 1), :] = scale
        for k in range(3):
            own_coef[m, pl.ds(2 + k, 1), :] = offs[k]
        slant = 0.5 * scale
        level = [slant * off + 0.5 * shifts[...] for off in offs]
        (_, to_down), (_, to_up) = own_edges(m)
        edges_arrived(to_down, to_up)

        @pl.when(last)
        def _():
            in_copy(cotangent, m).wait()
            argument_arrived(*input_parts(cotangent, m))
            sums = jnp.zeros((cols, ch), F32)
            cross = jnp.zeros((cols, ch), F32)
            for g in range(groups):
                z = zown[m, group(g), :].astype(F32)
                halved = z * slant + level[kind(g)]
                turn = jnp.tanh(halved)
                bent = halved * turn
                dy = inp[m, group(g), :].astype(F32) * ((0.5 + 0.5 * turn) * (1.0 + halved - bent))
                dyin[m, group(g), :] = dy.astype(BF16)
                if kind(g) == 1:
                    out_v[m, pl.ds((g - 1) * cols, cols), :] = (halved + bent).astype(BF16)
                    sums += dy
                    cross += dy * z
            one = jnp.sum(sums, 0, keepdims=True)
            seed_sums[m, pl.ds(0, 1), :] = one
            seed_sums[m, pl.ds(1, 1), :] = inv * (jnp.sum(cross, 0, keepdims=True) + offs[1] * one)
            start_stats(*seed_stats, m, sec, True)

        @pl.when(jnp.logical_not(last))
        def _():
            for g in range(1, groups - 1):
                halved = zown[m, group(g), :].astype(F32) * slant + level[1]
                out_v[m, pl.ds((g - 1) * cols, cols), :] = (halved + halved * jnp.tanh(halved)).astype(BF16)

        for copy in result_copies(out_v, outs, out_sem, po_s, po_r, m):
            copy.start()

    def result_copies(src, dst, sem, send, recv, m):
        here, there = pl.multiple_of(strip * core, cols), pl.multiple_of(strip * (1 - core), cols)
        return (
            pltpu.make_async_copy(src.at[m, pl.ds(here, strip), :], dst.at[m, core], sem.at[m]),
            remote(src.at[m, pl.ds(there, strip), :], dst.at[m, core], send.at[m], recv.at[m], sec, partner),
        )

    def backward(m):
        wait_stats(dy_stat, bs_r, m)
        first_sum = jnp.sum(dy_stat[m, :, 0, :], 0, keepdims=True)
        cross_sum = jnp.sum(dy_stat[m, :, 1, :], 0, keepdims=True)
        shift_sum[...] += first_sum
        gain_sum[...] += cross_sum
        inv = own_coef[m, pl.ds(0, 1), :]
        scale = own_coef[m, pl.ds(1, 1), :]
        tilt = scale * inv * (cross_sum / total)
        base = [scale * (first_sum / total) + tilt * own_coef[m, pl.ds(2 + k, 1), :] for k in range(3)]

        @pl.when(sec < sections - 1)
        def _():
            arrived(dy_sends(m, sec))

        for g in range(groups):
            dz = dyin[m, group(g), :].astype(F32) * scale - zown[m, group(g), :].astype(F32) * tilt - base[kind(g)]
            dzb[m, group(g), :] = inside(g, dz.astype(BF16))

        for h in range(2):
            part = pl.ds(h * half, half)
            parts = []
            for c in range(3):
                acc = jnp.zeros((px, half), F32)
                for r in range(3):
                    acc += jnp.dot(
                        dzb[m, pl.ds((2 - r) * cols, px), :], wt_v[r, pl.ds(c * ch, ch), part],
                        preferred_element_type=F32,
                    )
                parts.append(acc)
            gate = jnp.concatenate([mask_v[m, centre, :].astype(F32)] * (half // 128), axis=1)
            du = (taps_joined(parts, 2, 0) * gate).astype(BF16)
            gin_v[m, :, part] = du

            @pl.when(sec > 0)
            def _():
                dy = du.astype(F32) * slope_prev[m, :, part]
                dyout[m, :, part] = dy.astype(BF16)
                one = jnp.sum(dy, 0, keepdims=True)
                cross = jnp.sum(dy * zin[m, centre, part].astype(F32), 0, keepdims=True)
                sums_out[m, pl.ds(0, 1), part] = one
                sums_out[m, pl.ds(1, 1), part] = prev_coef[m, pl.ds(0, 1), part] * (
                    cross + prev_coef[m, pl.ds(1, 1), part] * one
                )
                if h == 1:
                    start_stats(*back_stats, m, sec - 1, False)
                each(dy_sends(m, sec - 1), h, start)

        for copy in result_copies(gin_v, grads_in, gin_sem, pg_s, pg_r, m):
            copy.start()

    def turn_weights():
        def one(i, carry):
            at = pl.ds(pl.multiple_of(lax.rem(i, 3) * ch, ch), ch)
            wt_v[lax.div(i, 3), at, :] = w_v[lax.div(i, 3), at, :].T
            return carry
        lax.fori_loop(0, 9, one, 0)

    @pl.when(jnp.logical_not(first))
    def _():
        for r in range(3):
            w_copy(r).wait()
        turn_weights()

    def step(t, carry):
        @pl.when(first & (t == batches))
        def _():
            turn_weights()

        ahead = t - sec
        behind = t - (2 * sections - 1 - sec)

        @pl.when((ahead >= 0) & (ahead < batches))
        def _():
            forward(ahead)

        done = ahead - jnp.where(last, 0, 1)

        @pl.when((behind >= 0) & (behind < batches))
        def _():
            backward(behind)

        @pl.when((done >= 0) & (done < batches))
        def _():
            finish(done)

        return carry

    lax.fori_loop(0, 2 * sections - 1 + batches, step, 0)

    place = lax.broadcasted_iota(jnp.int32, (cols, ch), 0)
    for m in range(batches):
        for g in range(1, groups - 1):
            values = dzb[m, group(g), :].astype(F32)
            at = pl.ds((m * (groups - 2) + g - 1) * cols, cols)
            dzside[0, at, :] = jnp.where(place == cols - 1, 0.0, pltpu.roll(values, cols - 1, 0)).astype(BF16)
            dzside[1, at, :] = values.astype(BF16)
            dzside[2, at, :] = jnp.where(place == 0, 0.0, pltpu.roll(values, 1, 0)).astype(BF16)

    def dw_copy(r, c):
        return pltpu.make_async_copy(dw_v.at[r, c], weight_part.at[r, c], dw_sem.at[r, c])

    def taps(r, carry):
        left = ub[:, pl.ds(pl.multiple_of(r * cols, cols), px), :].reshape(batches * px, ch)
        for c in range(3):
            for h in range(2):
                part = lax.dot_general(
                    left[:, h * half : (h + 1) * half], dzside[c], (((0,), (0,)), ((), ())),
                    preferred_element_type=F32,
                )
                dw_v[r, c, pl.ds(h * half, half), :] = part.astype(BF16)
            dw_copy(r, c).start()
        return carry

    lax.fori_loop(0, 3, taps, 0)

    for r in range(3):
        for c in range(3):
            dw_copy(r, c).wait()

    @pl.when(decoder)
    def _():
        argument_sent(*mask_parts)

    @pl.when(sec < sections - 1)
    def _():
        for copy in affine_sends():
            copy.wait_send()

    def drain(m, carry):
        for src, dst, sems in ((out_v, outs, (out_sem, po_s, po_r)), (gin_v, grads_in, (gin_sem, pg_s, pg_r))):
            here, there = result_copies(src, dst, *sems, m)
            here.wait()
            there.wait_send()
            remote(
                src.at[m, pl.ds(0, strip), :], dst.at[m, 1 - core], sems[1].at[m], sems[2].at[m], sec, partner
            ).wait_recv()

        @pl.when(first)
        def _():
            argument_sent(*input_parts(images, m))

        @pl.when(last)
        def _():
            argument_sent(*input_parts(cotangent, m))
            stats_each(*seed_stats, m, sec, True, sent)

        @pl.when(sec < sections - 1)
        def _():
            stats_each(*down_stats, m, sec + 1, False, sent)
            for h in range(2):
                each(z_sends(m, sec + 1), h, sent)

        stats_each(*same_stats, m, sec, True, sent)
        for h in range(2):
            each(own_edges(m), h, sent)

        @pl.when(sec > 0)
        def _():
            stats_each(*back_stats, m, sec - 1, False, sent)
            for h in range(2):
                each(dy_sends(m, sec - 1), h, sent)

        return carry

    lax.fori_loop(0, batches, drain, 0)


def body(images, switches, conv_weights, gains, shifts, cotangent):
    sections = lax.axis_size("section")
    strips = lax.axis_size("rows")
    batches, pictures, strip_rows, cols, ch = images.shape
    strip = strip_rows * cols
    px = 2 * strip
    tall = px + 2 * cols
    anywhere = pl.BlockSpec(memory_space=pl.ANY)
    vmem = pl.BlockSpec(memory_space=pltpu.VMEM)
    dma = pltpu.SemaphoreType.DMA
    flops = 3 * 2 * 9 * ch * ch * batches * px
    outs, grads_in, weight_part, gain_sum, shift_sum = pl.pallas_call(
        functools.partial(kernel, sections, strips, cols),
        out_shape=(
            jax.ShapeDtypeStruct((batches, pictures, strip, ch), BF16),
            jax.ShapeDtypeStruct((batches, pictures, strip, ch), BF16),
            jax.ShapeDtypeStruct((3, 3, ch, ch), BF16),
            jax.ShapeDtypeStruct((1, ch), F32),
            jax.ShapeDtypeStruct((1, ch), F32),
        ),
        in_specs=[anywhere, anywhere, anywhere, vmem, vmem, vmem],
        out_specs=(anywhere, anywhere, anywhere, vmem, vmem),
        scratch_shapes=[
            pltpu.VMEM((3, 3 * ch, ch), BF16),
            pltpu.VMEM((3, 3 * ch, ch), BF16),
            pltpu.VMEM((batches, tall, ch), BF16),
            pltpu.VMEM((batches, 2, strip, 128), BF16),
            pltpu.VMEM((batches, tall, 128), BF16),
            pltpu.VMEM((1, ch), F32),
            pltpu.VMEM((1, ch), F32),
            pltpu.VMEM((batches, tall, ch), BF16),
            pltpu.VMEM((batches, strips, 2, ch), F32),
            pltpu.VMEM((batches, tall, ch), BF16),
            pltpu.VMEM((batches, strips, 2, ch), F32),
            pltpu.VMEM((batches, tall, ch), BF16),
            pltpu.VMEM((batches, px, ch), F32),
            pltpu.VMEM((batches, 2, ch), F32),
            pltpu.VMEM((batches, 8, ch), F32),
            pltpu.VMEM((batches, tall, ch), BF16),
            pltpu.VMEM((batches, strips, 2, ch), F32),
            pltpu.VMEM((batches, tall, ch), BF16),
            pltpu.VMEM((3, batches * px, ch), BF16),
            pltpu.VMEM((batches, px, ch), BF16),
            pltpu.VMEM((batches, 2, ch), F32),
            pltpu.VMEM((batches, 2, ch), F32),
            pltpu.VMEM((batches, 2, ch), F32),
            pltpu.VMEM((batches, px, ch), BF16),
            pltpu.VMEM((batches, px, ch), BF16),
            pltpu.VMEM((3, 3, ch, ch), BF16),
            dma((3,)),
            dma((batches,)),
            dma((batches,)), dma((batches,)),
            dma((batches, 2)), dma((batches, 2)),
            dma, dma,
            dma((2,)), dma((2,)),
            dma((2,)), dma((2,)),
            dma((batches, 3, 2)), dma((batches, 3, 2)),
            dma((batches, strips)), dma((batches,)),
            dma((batches, 3, 2)), dma((batches, 3, 2)),
            dma((batches, strips)), dma((batches,)),
            dma((batches, 3, 2)), dma((batches, 3, 2)),
            dma((batches, strips)), dma((batches,)),
            dma((batches, strips)),
            dma((batches,)), dma((batches,)), dma((batches,)),
            dma((batches,)), dma((batches,)), dma((batches,)),
            dma((3, 3)),
        ],
        compiler_params=pltpu.CompilerParams(
            collective_id=0, has_side_effects=True, vmem_limit_bytes=56 * 2**20
        ),
        cost_estimate=pl.CostEstimate(
            flops=flops, bytes_accessed=2 * 9 * ch * ch * 2, transcendentals=0
        ),
    )(
        images.reshape(batches, pictures, strip, ch),
        cotangent.reshape(batches, pictures, strip, ch),
        conv_weights.reshape(3, 3 * ch, ch),
        gains,
        shifts,
        switches.reshape(-1, switches.shape[-1]),
    )
    weight_grad = lax.psum_scatter(weight_part, "rows", scatter_dimension=2, tiled=True).astype(F32)
    shape = (1, batches, pictures, strip_rows, cols, ch)
    return (outs.reshape(shape), grads_in.reshape(shape), weight_grad[None], gain_sum, shift_sum)


def solution(mesh):
    return jax.shard_map(
        body,
        mesh=mesh,
        in_specs=(
            P(None, None, "rows", None, None),
            P(None, None, "rows", None),
            P("section", None, None, None, None),
            P("section", None),
            P("section", None),
            P(None, None, "rows", None, None),
        ),
        out_specs=(
            P("section", None, None, "rows", None, None),
            P("section", None, None, "rows", None, None),
            P("section", None, None, "rows", None),
            P("section", None),
            P("section", None),
        ),
        check_vma=False,
    )
```

```python
import functools

import jax
import jax.numpy as jnp
from jax import lax
from jax.experimental import pallas as pl
from jax.experimental.pallas import tpu as pltpu
from jax.sharding import PartitionSpec as P

EPSILON = 1e-05
MESH = pl.DeviceIdType.MESH
BF16 = jnp.bfloat16
F32 = jnp.float32


def kernel(
    sections, strips, cols,
    images, cotangent, weights, gains, shifts, switches,
    outs, grads_in, weight_grad, gain_sum, shift_sum,
    w_v, wt_v, inp, mask_own, mask_v, gain_prev, shift_prev, zin, zin_stat, zown, own_stat, ub, slope_prev,
    prev_coef, own_coef, dyin, dy_stat, dzb, dyout, stat_out, sums_out, seed_sums, out_v, gin_v,
    ut_own, ut_all, dz_all, dz_taps, acc_v, swap_out, swap_in, dw_v,
    w_sem, in_sem, pi_s, pi_r, ie_s, ie_r, mp_s, mp_r, me_s, me_r, gp_s, gp_r,
    fz_s, fz_r, fs_s, fs_r, oe_s, oe_r, os_s, os_r, bz_s, bz_r, bs_s, bs_r, ls_s,
    out_sem, po_s, po_r, gin_sem, pg_s, pg_r,
    ut_s, ut_r, uf_s, uf_r, dz_s, dz_r, sw_s, sw_r, dw_sem,
):
    sec = lax.axis_index("section")
    row = lax.axis_index("rows")
    batches, tall, ch = inp.shape
    px = tall - 2 * cols
    strip = px // 2
    groups = tall // cols
    half = ch // 2
    total = float(px * strips)
    local = float(px)
    first, last, decoder = sec == 0, sec == sections - 1, sec == sections // 2
    core = row % 2
    partner = row + 1 - 2 * core
    has_up, has_down = row >= 2, row < strips - 2
    centre = pl.ds(cols, px)
    chip = row // 2
    team, seat = row // 4, row % 4
    lanes = dz_all.shape[3]
    block = ut_all.shape[2]
    share = block // 4
    mine = pl.multiple_of(cols + strip * core, cols)

    def w_copy(r):
        return pltpu.make_async_copy(weights.at[r], w_v.at[r], w_sem.at[r])

    def in_copy(src, m):
        return pltpu.make_async_copy(src.at[m, core], inp.at[m, pl.ds(mine, strip), :], in_sem.at[m])

    for r in range(3):
        w_copy(r).start()

    @pl.when(first)
    def _():
        for m in range(batches):
            in_copy(images, m).start()

    @pl.when(last)
    def _():
        for m in range(batches):
            in_copy(cotangent, m).start()

    barrier = pltpu.get_barrier_semaphore()
    for s in range(sections):
        @pl.when((sec >= s - 1) & (sec <= s + 1))
        def _():
            def greet(i, carry):
                @pl.when((s != sec) | (i != row))
                def _():
                    pl.semaphore_signal(barrier, inc=1, device_id=(jnp.int32(s), i), device_id_type=MESH)
                return carry
            lax.fori_loop(0, strips, greet, 0)

    acc_v[...] = jnp.zeros_like(acc_v)
    gain_sum[...] = jnp.zeros_like(gain_sum)
    shift_sum[...] = jnp.zeros_like(shift_sum)

    for m in range(batches):
        for i in range(2):
            for at in (0, dz_all.shape[2] - cols):
                dz_all[m, i, pl.ds(at, cols), :] = jnp.zeros((cols, lanes), BF16)

    @pl.when(decoder)
    def _():
        wide = cols // 2
        windows_at = lax.broadcasted_iota(jnp.int32, (cols, wide), 1)
        places = lax.broadcasted_iota(jnp.int32, (cols, wide), 0)
        pick = (lax.shift_right_logical(places, 1) == windows_at).astype(F32)
        table = lax.dot_general(
            pick, switches[...].astype(F32), (((1,), (1,)), ((), ())), preferred_element_type=F32
        )
        odd = jnp.bitwise_and(lax.broadcasted_iota(jnp.int32, (cols, 128), 0), 1).astype(F32)
        windows = strip // cols // 2
        for m in range(batches):
            for i in range(2):
                for w in range(windows):
                    at = (m * 2 + i) * windows + w
                    value = jnp.broadcast_to(table[:, at : at + 1], (cols, 128))
                    for p in range(2):
                        hit = (jnp.abs(value - (2.0 * p + odd)) < 0.5).astype(F32).astype(BF16)
                        mask_own[m, i, pl.ds((2 * w + p) * cols, cols), :] = hit
        for m in range(batches):
            mask_v[m, pl.ds(mine, strip), :] = mask_own[m, core]

    @pl.when(jnp.logical_not(decoder))
    def _():
        mask_v[...] = jnp.ones_like(mask_v)

    near = 1 + jnp.where(sec > 0, 1, 0) + jnp.where(sec < sections - 1, 1, 0)
    pl.semaphore_wait(barrier, near * strips - 1)

    def remote(src, dst, send, recv, s, i):
        return pltpu.make_async_remote_copy(
            src_ref=src, dst_ref=dst, send_sem=send, recv_sem=recv, device_id=(s, i), device_id_type=MESH
        )

    def to_partner(src_at, dst_at, send, recv):
        return remote(src_at(1 - core), dst_at(pl.ds(mine, strip)), send, recv, sec, partner)

    def start_argument(src_at, dst_at, pair_sems, edge_sems):
        to_partner(src_at, dst_at, *pair_sems).start()

        @pl.when((core == 1) & has_down)
        def _():
            for i in range(2):
                remote(
                    src_at(i, pl.ds(strip - cols, cols)), dst_at(pl.ds(0, cols)),
                    edge_sems[0].at[i], edge_sems[1].at[0], sec, row + 1 + i,
                ).start()

        @pl.when((core == 0) & has_up)
        def _():
            for i in range(2):
                remote(
                    src_at(i, pl.ds(0, cols)), dst_at(pl.ds(cols + px, cols)),
                    edge_sems[0].at[i], edge_sems[1].at[1], sec, row - 2 + i,
                ).start()

    def argument_arrived(src_at, dst_at, pair_sems, edge_sems):
        to_partner(src_at, dst_at, *pair_sems).wait_recv()

        @pl.when(has_up)
        def _():
            remote(
                src_at(0, pl.ds(0, cols)), dst_at(pl.ds(0, cols)), edge_sems[0].at[0], edge_sems[1].at[0], sec, row
            ).wait_recv()

        @pl.when(has_down)
        def _():
            remote(
                src_at(0, pl.ds(0, cols)), dst_at(pl.ds(cols + px, cols)), edge_sems[0].at[0], edge_sems[1].at[1],
                sec, row,
            ).wait_recv()

    def argument_sent(src_at, dst_at, pair_sems, edge_sems):
        to_partner(src_at, dst_at, *pair_sems).wait_send()

        @pl.when(((core == 1) & has_down) | ((core == 0) & has_up))
        def _():
            for i in range(2):
                remote(
                    src_at(i, pl.ds(0, cols)), dst_at(pl.ds(0, cols)), edge_sems[0].at[i], edge_sems[1].at[0], sec, row
                ).wait_send()

    def input_parts(src, m):
        return (
            lambda i, r=pl.ds(0, strip): src.at[m, i, r, :],
            lambda r: inp.at[m, r, :],
            (pi_s.at[m], pi_r.at[m]),
            (ie_s.at[m], ie_r.at[m]),
        )

    mask_parts = (
        lambda i, r=pl.ds(0, strip): mask_own.at[:, i, r, :],
        lambda r: mask_v.at[:, r, :],
        (mp_s, mp_r),
        (me_s, me_r),
    )

    @pl.when(first)
    def _():
        for m in range(batches):
            start_argument(*input_parts(images, m))

    @pl.when(last)
    def _():
        for m in range(batches):
            start_argument(*input_parts(cotangent, m))

    @pl.when(decoder)
    def _():
        start_argument(*mask_parts)

    def affine_sends():
        return (
            remote(gains, gain_prev, gp_s.at[0], gp_r.at[0], sec + 1, row),
            remote(shifts, shift_prev, gp_s.at[1], gp_r.at[1], sec + 1, row),
        )

    @pl.when(sec < sections - 1)
    def _():
        for copy in affine_sends():
            copy.start()

    def block_sends(src, src_from, dst, send, recv, m, s):
        def one(k, h, src_row, dst_row, rows, i):
            part = pl.ds(h * half, half)
            return remote(
                src.at[m, pl.ds(src_from + src_row, rows), part], dst.at[m, pl.ds(dst_row, rows), part],
                send.at[m, k, h], recv.at[m, k, h], s, i,
            )
        return (
            (None, lambda h: one(0, h, 0, cols, px, row)),
            (has_down, lambda h: one(1, h, px - cols, 0, cols, row + 2)),
            (has_up, lambda h: one(2, h, 0, cols + px, cols, row - 2)),
        )

    def each(parts, h, act):
        for cond, make in parts:
            if cond is None:
                act(make(h))
            else:
                @pl.when(cond)
                def _():
                    act(make(h))

    def arrived(parts):
        (_, body), (_, to_down), (_, to_up) = parts
        for h in range(2):
            body(h).wait_recv()
        edges_arrived(to_down, to_up)

    def edges_arrived(to_down, to_up):
        @pl.when(has_up)
        def _():
            for h in range(2):
                to_down(h).wait_recv()

        @pl.when(has_down)
        def _():
            for h in range(2):
                to_up(h).wait_recv()

    def start(copy):
        copy.start()

    def sent(copy):
        copy.wait_send()

    def z_sends(m, s):
        return block_sends(zown, cols, zin, fz_s, fz_r, m, s)

    def own_edges(m):
        return block_sends(zown, cols, zown, oe_s, oe_r, m, sec)[1:]

    def dy_sends(m, s):
        return block_sends(dyout, 0, dyin, bz_s, bz_r, m, s)

    def stat_copy(src, dst, send, recv, m, s, i):
        return remote(src.at[m], dst.at[m, row], send.at[m, i], recv.at[m], s, i)

    def stats_each(src, dst, send, recv, m, s, same, act):
        def one(d, carry):
            i = row + d
            act(stat_copy(src, dst, send, recv, m, s, jnp.where(i >= strips, i - strips, i)))
            return carry
        lax.fori_loop(1 if same else 0, strips, one, 0)

    def start_stats(src, dst, send, recv, m, s, same):
        stats_each(src, dst, send, recv, m, s, same, start)
        if same:
            pltpu.make_async_copy(src.at[m], dst.at[m, row], recv.at[m]).start()

    def wait_stats(dst, recv, m):
        pltpu.make_async_copy(dst.at[m], dst.at[m], recv.at[m]).wait()

    down_stats = (stat_out, zin_stat, fs_s, fs_r)
    same_stats = (stat_out, own_stat, os_s, os_r)
    back_stats = (sums_out, dy_stat, bs_s, bs_r)
    seed_stats = (seed_sums, dy_stat, ls_s, bs_r)

    def join(stats_ref, m):
        means, squares = stats_ref[m, :, 0, :], stats_ref[m, :, 1, :]
        mean = jnp.sum(means, 0, keepdims=True) / float(strips)
        off = means - mean
        var = (jnp.sum(squares, 0, keepdims=True) + local * jnp.sum(off * off, 0, keepdims=True)) / total
        at = (jnp.maximum(row - 2, 0), row, jnp.minimum(row + 2, strips - 1))
        return lax.rsqrt(var + EPSILON), [stats_ref[m, i, pl.ds(0, 1), :] - mean for i in at]

    def kind(g):
        return 0 if g == 0 else 2 if g == groups - 1 else 1

    def inside(g, values):
        if kind(g) == 1:
            return values
        return jnp.where(has_up if kind(g) == 0 else has_down, values, jnp.zeros_like(values))

    def group(g):
        return pl.ds(g * cols, cols)

    column = lax.broadcasted_iota(jnp.int32, (1, cols, half), 1)

    def taps_joined(parts, left, right):
        def moved(values, by, edge):
            turned = pltpu.roll(values, by % px, 0).reshape(px // cols, cols, half)
            return jnp.where(column == edge, 0.0, turned).reshape(px, half)
        return parts[1] + moved(parts[left], 1, 0) + moved(parts[right], -1, cols - 1)

    def turned_copy(m, q):
        src = ut_own.at[m, pl.ds(pl.multiple_of((q // 2) * block, block), block), :]
        dst = ut_all.at[m, core, :, pl.ds(pl.multiple_of(chip * px, px), px)]
        return src, dst

    def turned_each(m, act):
        def one(d, carry):
            q = chip + d
            q = jnp.where(q >= strips // 2, q - strips // 2, q)
            src, dst = turned_copy(m, q)
            act(remote(src, dst, ut_s.at[m, d], ut_r.at[m], sec, 2 * q + core))
            return carry
        lax.fori_loop(1, strips // 2, one, 0)

    def send_turned(m):
        ut_own[m] = ub[m, centre, :].T
        turned_each(m, start)
        src, dst = turned_copy(m, chip)
        pltpu.make_async_copy(src, dst, ut_r.at[m]).start()

    def turned_relay(m):
        return remote(ut_all.at[m, core], ut_all.at[m, core], uf_s.at[m], uf_r.at[m], sec, partner)

    def relay_turned(m):
        pltpu.make_async_copy(ut_all.at[m, core], ut_all.at[m, core], ut_r.at[m]).wait()
        turned_relay(m).start()

    def dz_copy(m, i):
        src = dzb.at[m, centre, pl.ds(pl.multiple_of((i % 4) * lanes, lanes), lanes)]
        dst = dz_all.at[m, core, pl.ds(pl.multiple_of(cols + chip * px, cols), px), :]
        return src, dst

    def dz_each(m, act):
        def one(d, carry):
            i = row + d
            i = jnp.where(i >= strips, i - strips, i)
            src, dst = dz_copy(m, i)
            act(remote(src, dst, dz_s.at[m, d], dz_r.at[m], sec, i))
            return carry
        lax.fori_loop(1, strips, one, 0)

    def send_dz(m):
        dz_each(m, start)
        src, dst = dz_copy(m, row)
        pltpu.make_async_copy(src, dst, dz_r.at[m]).start()

    def gather_taps(m):
        whole = dz_all.at[m, :, pl.ds(cols, px * (strips // 2)), :]
        pltpu.make_async_copy(whole, whole, dz_r.at[m]).wait()
        relayed = ut_all.at[m, 1 - core]
        pltpu.make_async_copy(relayed, relayed, uf_r.at[m]).wait()
        rows = dz_all.shape[2]
        edge = lax.broadcasted_iota(jnp.int32, (1, cols, lanes), 1)
        for i in range(2):
            values = dz_all[m, i].astype(F32)
            for c, by, gone in ((0, rows - 1, cols - 1), (2, 1, 0)):
                turned = pltpu.roll(values, by, 0).reshape(rows // cols, cols, lanes)
                turned = jnp.where(edge == gone, 0.0, turned).reshape(rows, lanes)
                dz_taps[i, :, pl.ds(c * lanes, lanes)] = turned.astype(BF16)
            dz_taps[i, :, pl.ds(lanes, lanes)] = dz_all[m, i]

    def kernel_row(m, r):
        part = jnp.zeros((block, 3 * lanes), F32)
        for i in range(2):
            part += jnp.dot(
                ut_all[m, i], dz_taps[i, pl.ds((2 - r) * cols, px * (strips // 2)), :], preferred_element_type=F32
            )
        return part

    def add_gradients(m):
        gather_taps(m)
        for r in range(3):
            acc_v[r] = acc_v[r] + kernel_row(m, r)

    def forward(m):
        @pl.when(first)
        def _():
            in_copy(images, m).wait()
            argument_arrived(*input_parts(images, m))
            for g in range(groups):
                ub[m, group(g), :] = inside(g, inp[m, group(g), :])

        @pl.when(sec > 0)
        def _():
            @pl.when(m == 0)
            def _():
                for copy in affine_sends():
                    copy.wait_recv()

                @pl.when(decoder)
                def _():
                    argument_arrived(*mask_parts)

            wait_stats(zin_stat, fs_r, m)
            inv, offs = join(zin_stat, m)
            prev_coef[m, pl.ds(0, 1), :] = inv
            prev_coef[m, pl.ds(1, 1), :] = offs[1]
            slant = 0.5 * inv * gain_prev[...]
            level = [slant * off + 0.5 * shift_prev[...] for off in offs]
            arrived(z_sends(m, sec))
            for g in range(groups):
                halved = zin[m, group(g), :].astype(F32) * slant + level[kind(g)]
                turn = jnp.tanh(halved)
                bent = halved * turn
                gate = jnp.concatenate([mask_v[m, group(g), :].astype(F32)] * (ch // 128), axis=1)
                ub[m, group(g), :] = inside(g, ((halved + bent) * gate).astype(BF16))
                if kind(g) == 1:
                    slope_prev[m, pl.ds((g - 1) * cols, cols), :] = (0.5 + 0.5 * turn) * (1.0 + halved - bent)

        @pl.when(first & (m == 0))
        def _():
            for r in range(3):
                w_copy(r).wait()

        for h in range(2):
            part = pl.ds(h * half, half)
            parts = []
            for c in range(3):
                acc = jnp.zeros((px, half), F32)
                for r in range(3):
                    acc += jnp.dot(
                        ub[m, pl.ds(r * cols, px), :], w_v[r, pl.ds(c * ch, ch), part], preferred_element_type=F32
                    )
                parts.append(acc)
            conv = taps_joined(parts, 0, 2)
            mean = jnp.sum(conv, 0, keepdims=True) / local
            conv = conv - mean
            stat_out[m, pl.ds(0, 1), part] = mean
            stat_out[m, pl.ds(1, 1), part] = jnp.sum(conv * conv, 0, keepdims=True)
            zown[m, centre, part] = conv.astype(BF16)

            @pl.when(sec < sections - 1)
            def _():
                if h == 1:
                    start_stats(*down_stats, m, sec + 1, False)
                each(z_sends(m, sec + 1), h, start)

        start_stats(*same_stats, m, sec, True)
        for h in range(2):
            each(own_edges(m), h, start)
        send_turned(m)

    def finish(m):
        wait_stats(own_stat, os_r, m)
        inv, offs = join(own_stat, m)
        scale = inv * gains[...]
        own_coef[m, pl.ds(0, 1), :] = inv
        own_coef[m, pl.ds(1, 1), :] = scale
        for k in range(3):
            own_coef[m, pl.ds(2 + k, 1), :] = offs[k]
        slant = 0.5 * scale
        level = [slant * off + 0.5 * shifts[...] for off in offs]
        (_, to_down), (_, to_up) = own_edges(m)
        edges_arrived(to_down, to_up)

        @pl.when(last)
        def _():
            in_copy(cotangent, m).wait()
            argument_arrived(*input_parts(cotangent, m))
            sums = jnp.zeros((cols, ch), F32)
            cross = jnp.zeros((cols, ch), F32)
            for g in range(groups):
                z = zown[m, group(g), :].astype(F32)
                halved = z * slant + level[kind(g)]
                turn = jnp.tanh(halved)
                bent = halved * turn
                dy = inp[m, group(g), :].astype(F32) * ((0.5 + 0.5 * turn) * (1.0 + halved - bent))
                dyin[m, group(g), :] = dy.astype(BF16)
                if kind(g) == 1:
                    out_v[m, pl.ds((g - 1) * cols, cols), :] = (halved + bent).astype(BF16)
                    sums += dy
                    cross += dy * z
            one = jnp.sum(sums, 0, keepdims=True)
            seed_sums[m, pl.ds(0, 1), :] = one
            seed_sums[m, pl.ds(1, 1), :] = inv * (jnp.sum(cross, 0, keepdims=True) + offs[1] * one)
            start_stats(*seed_stats, m, sec, True)

        @pl.when(jnp.logical_not(last))
        def _():
            for g in range(1, groups - 1):
                halved = zown[m, group(g), :].astype(F32) * slant + level[1]
                out_v[m, pl.ds((g - 1) * cols, cols), :] = (halved + halved * jnp.tanh(halved)).astype(BF16)

        for copy in result_copies(out_v, outs, out_sem, po_s, po_r, m):
            copy.start()

    def result_copies(src, dst, sem, send, recv, m):
        here, there = pl.multiple_of(strip * core, cols), pl.multiple_of(strip * (1 - core), cols)
        return (
            pltpu.make_async_copy(src.at[m, pl.ds(here, strip), :], dst.at[m, core], sem.at[m]),
            remote(src.at[m, pl.ds(there, strip), :], dst.at[m, core], send.at[m], recv.at[m], sec, partner),
        )

    def backward(m):
        wait_stats(dy_stat, bs_r, m)
        first_sum = jnp.sum(dy_stat[m, :, 0, :], 0, keepdims=True)
        cross_sum = jnp.sum(dy_stat[m, :, 1, :], 0, keepdims=True)
        shift_sum[...] += first_sum
        gain_sum[...] += cross_sum
        inv = own_coef[m, pl.ds(0, 1), :]
        scale = own_coef[m, pl.ds(1, 1), :]
        tilt = scale * inv * (cross_sum / total)
        base = [scale * (first_sum / total) + tilt * own_coef[m, pl.ds(2 + k, 1), :] for k in range(3)]

        @pl.when(sec < sections - 1)
        def _():
            arrived(dy_sends(m, sec))

        for g in range(groups):
            dz = dyin[m, group(g), :].astype(F32) * scale - zown[m, group(g), :].astype(F32) * tilt - base[kind(g)]
            dzb[m, group(g), :] = inside(g, dz.astype(BF16))

        @pl.when(first)
        def _():
            send_dz(m)

        for h in range(2):
            part = pl.ds(h * half, half)
            parts = []
            for c in range(3):
                acc = jnp.zeros((px, half), F32)
                for r in range(3):
                    acc += jnp.dot(
                        dzb[m, pl.ds((2 - r) * cols, px), :], wt_v[r, pl.ds(c * ch, ch), part],
                        preferred_element_type=F32,
                    )
                parts.append(acc)
            gate = jnp.concatenate([mask_v[m, centre, :].astype(F32)] * (half // 128), axis=1)
            du = (taps_joined(parts, 2, 0) * gate).astype(BF16)
            gin_v[m, :, part] = du

            @pl.when(sec > 0)
            def _():
                dy = du.astype(F32) * slope_prev[m, :, part]
                dyout[m, :, part] = dy.astype(BF16)
                one = jnp.sum(dy, 0, keepdims=True)
                cross = jnp.sum(dy * zin[m, centre, part].astype(F32), 0, keepdims=True)
                sums_out[m, pl.ds(0, 1), part] = one
                sums_out[m, pl.ds(1, 1), part] = prev_coef[m, pl.ds(0, 1), part] * (
                    cross + prev_coef[m, pl.ds(1, 1), part] * one
                )
                if h == 1:
                    start_stats(*back_stats, m, sec - 1, False)
                each(dy_sends(m, sec - 1), h, start)

        for copy in result_copies(gin_v, grads_in, gin_sem, pg_s, pg_r, m):
            copy.start()

        @pl.when((sec > 0) & (sec < sections - 1))
        def _():
            send_dz(m)

    def turn_weights():
        def one(i, carry):
            at = pl.ds(pl.multiple_of(lax.rem(i, 3) * ch, ch), ch)
            wt_v[lax.div(i, 3), at, :] = w_v[lax.div(i, 3), at, :].T
            return carry
        lax.fori_loop(0, 9, one, 0)

    @pl.when(jnp.logical_not(first))
    def _():
        for r in range(3):
            w_copy(r).wait()
        turn_weights()

    def step(t, carry):
        @pl.when(first & (t == batches))
        def _():
            turn_weights()

        ahead = t - sec
        behind = t - (2 * sections - 1 - sec)

        @pl.when((ahead >= 0) & (ahead < batches))
        def _():
            forward(ahead)

        done = ahead - jnp.where(last, 0, 1)

        @pl.when((behind >= 0) & (behind < batches))
        def _():
            backward(behind)

        @pl.when((done >= 0) & (done < batches))
        def _():
            finish(done)

        @pl.when((ahead >= 2) & (ahead < batches + 2))
        def _():
            relay_turned(ahead - 2)

        @pl.when((behind >= 1) & (behind < batches) & jnp.logical_not(last))
        def _():
            add_gradients(behind - 1)

        return carry

    lax.fori_loop(0, 2 * sections - 1 + batches, step, 0)

    @pl.when(last)
    def _():
        def send(m, carry):
            send_dz(m)
            return carry

        def add(m, carry):
            add_gradients(m)
            return carry

        lax.fori_loop(0, batches, send, 0)
        lax.fori_loop(0, batches - 1, add, 0)

    def swap(r, d):
        other = (seat + d) % 4
        return remote(
            swap_out.at[r, pl.ds(pl.multiple_of(other * share, share), share), :], swap_in.at[r, 4 - d - 1],
            sw_s.at[r, d - 1], sw_r.at[r, 4 - d - 1], sec, 4 * team + other,
        )

    gather_taps(batches - 1)
    for r in range(3):
        part = acc_v[r] + kernel_row(batches - 1, r)
        acc_v[r] = part
        swap_out[r] = part.astype(BF16)
        for d in range(1, 4):
            swap(r, d).start()

    def dw_copy(r):
        return pltpu.make_async_copy(dw_v.at[r], weight_grad.at[r], dw_sem.at[r])

    own_rows = pl.ds(pl.multiple_of(seat * share, share), share)
    for r in range(3):
        for c in range(3):
            dw_v[r, c, :, pl.ds(pl.multiple_of(seat * lanes, lanes), lanes)] = acc_v[r, own_rows, pl.ds(c * lanes, lanes)]
        for d in range(1, 4):
            swap(r, 4 - d).wait_recv()
            source = (seat + d) % 4
            for c in range(3):
                dw_v[r, c, :, pl.ds(pl.multiple_of(source * lanes, lanes), lanes)] = swap_in[
                    r, d - 1, :, pl.ds(c * lanes, lanes)
                ].astype(F32)
        dw_copy(r).start()

    for r in range(3):
        dw_copy(r).wait()
        for d in range(1, 4):
            swap(r, d).wait_send()

    @pl.when(decoder)
    def _():
        argument_sent(*mask_parts)

    @pl.when(sec < sections - 1)
    def _():
        for copy in affine_sends():
            copy.wait_send()

    def drain(m, carry):
        for src, dst, sems in ((out_v, outs, (out_sem, po_s, po_r)), (gin_v, grads_in, (gin_sem, pg_s, pg_r))):
            here, there = result_copies(src, dst, *sems, m)
            here.wait()
            there.wait_send()
            remote(
                src.at[m, pl.ds(0, strip), :], dst.at[m, 1 - core], sems[1].at[m], sems[2].at[m], sec, partner
            ).wait_recv()

        turned_each(m, sent)
        turned_relay(m).wait_send()
        dz_each(m, sent)

        @pl.when(first)
        def _():
            argument_sent(*input_parts(images, m))

        @pl.when(last)
        def _():
            argument_sent(*input_parts(cotangent, m))
            stats_each(*seed_stats, m, sec, True, sent)

        @pl.when(sec < sections - 1)
        def _():
            stats_each(*down_stats, m, sec + 1, False, sent)
            for h in range(2):
                each(z_sends(m, sec + 1), h, sent)

        stats_each(*same_stats, m, sec, True, sent)
        for h in range(2):
            each(own_edges(m), h, sent)

        @pl.when(sec > 0)
        def _():
            stats_each(*back_stats, m, sec - 1, False, sent)
            for h in range(2):
                each(dy_sends(m, sec - 1), h, sent)

        return carry

    lax.fori_loop(0, batches, drain, 0)


def body(images, switches, conv_weights, gains, shifts, cotangent):
    sections = lax.axis_size("section")
    strips = lax.axis_size("rows")
    batches, pictures, strip_rows, cols, ch = images.shape
    strip = strip_rows * cols
    px = 2 * strip
    tall = px + 2 * cols
    anywhere = pl.BlockSpec(memory_space=pl.ANY)
    vmem = pl.BlockSpec(memory_space=pltpu.VMEM)
    dma = pltpu.SemaphoreType.DMA
    flops = 3 * 2 * 9 * ch * ch * batches * px
    share = ch // strips
    outs, grads_in, weight_grad, gain_sum, shift_sum = pl.pallas_call(
        functools.partial(kernel, sections, strips, cols),
        out_shape=(
            jax.ShapeDtypeStruct((batches, pictures, strip, ch), BF16),
            jax.ShapeDtypeStruct((batches, pictures, strip, ch), BF16),
            jax.ShapeDtypeStruct((3, 3, share, ch), F32),
            jax.ShapeDtypeStruct((1, ch), F32),
            jax.ShapeDtypeStruct((1, ch), F32),
        ),
        in_specs=[anywhere, anywhere, anywhere, vmem, vmem, vmem],
        out_specs=(anywhere, anywhere, anywhere, vmem, vmem),
        scratch_shapes=[
            pltpu.VMEM((3, 3 * ch, ch), BF16),
            pltpu.VMEM((3, 3 * ch, ch), BF16),
            pltpu.VMEM((batches, tall, ch), BF16),
            pltpu.VMEM((batches, 2, strip, 128), BF16),
            pltpu.VMEM((batches, tall, 128), BF16),
            pltpu.VMEM((1, ch), F32),
            pltpu.VMEM((1, ch), F32),
            pltpu.VMEM((batches, tall, ch), BF16),
            pltpu.VMEM((batches, strips, 2, ch), F32),
            pltpu.VMEM((batches, tall, ch), BF16),
            pltpu.VMEM((batches, strips, 2, ch), F32),
            pltpu.VMEM((batches, tall, ch), BF16),
            pltpu.VMEM((batches, px, ch), F32),
            pltpu.VMEM((batches, 2, ch), F32),
            pltpu.VMEM((batches, 8, ch), F32),
            pltpu.VMEM((batches, tall, ch), BF16),
            pltpu.VMEM((batches, strips, 2, ch), F32),
            pltpu.VMEM((batches, tall, ch), BF16),
            pltpu.VMEM((batches, px, ch), BF16),
            pltpu.VMEM((batches, 2, ch), F32),
            pltpu.VMEM((batches, 2, ch), F32),
            pltpu.VMEM((batches, 2, ch), F32),
            pltpu.VMEM((batches, px, ch), BF16),
            pltpu.VMEM((batches, px, ch), BF16),
            pltpu.VMEM((batches, ch, px), BF16),
            pltpu.VMEM((batches, 2, 4 * share, px * strips // 2), BF16),
            pltpu.VMEM((batches, 2, px * strips // 2 + 2 * cols, ch // 4), BF16),
            pltpu.VMEM((2, px * strips // 2 + 2 * cols, 3 * ch // 4), BF16),
            pltpu.VMEM((3, 4 * share, 3 * ch // 4), F32),
            pltpu.VMEM((3, 4 * share, 3 * ch // 4), BF16),
            pltpu.VMEM((3, 3, share, 3 * ch // 4), BF16),
            pltpu.VMEM((3, 3, share, ch), F32),
            dma((3,)),
            dma((batches,)),
            dma((batches,)), dma((batches,)),
            dma((batches, 2)), dma((batches, 2)),
            dma, dma,
            dma((2,)), dma((2,)),
            dma((2,)), dma((2,)),
            dma((batches, 3, 2)), dma((batches, 3, 2)),
            dma((batches, strips)), dma((batches,)),
            dma((batches, 3, 2)), dma((batches, 3, 2)),
            dma((batches, strips)), dma((batches,)),
            dma((batches, 3, 2)), dma((batches, 3, 2)),
            dma((batches, strips)), dma((batches,)),
            dma((batches, strips)),
            dma((batches,)), dma((batches,)), dma((batches,)),
            dma((batches,)), dma((batches,)), dma((batches,)),
            dma((batches, strips // 2)), dma((batches,)),
            dma((batches,)), dma((batches,)),
            dma((batches, strips)), dma((batches,)),
            dma((3, 3)), dma((3, 3)),
            dma((3,)),
        ],
        compiler_params=pltpu.CompilerParams(
            collective_id=0, has_side_effects=True, vmem_limit_bytes=56 * 2**20
        ),
        cost_estimate=pl.CostEstimate(
            flops=flops, bytes_accessed=2 * 9 * ch * ch * 2, transcendentals=0
        ),
    )(
        images.reshape(batches, pictures, strip, ch),
        cotangent.reshape(batches, pictures, strip, ch),
        conv_weights.reshape(3, 3 * ch, ch),
        gains,
        shifts,
        switches.reshape(-1, switches.shape[-1]),
    )
    shape = (1, batches, pictures, strip_rows, cols, ch)
    return (outs.reshape(shape), grads_in.reshape(shape), weight_grad[None], gain_sum, shift_sum)


def solution(mesh):
    return jax.shard_map(
        body,
        mesh=mesh,
        in_specs=(
            P(None, None, "rows", None, None),
            P(None, None, "rows", None),
            P("section", None, None, None, None),
            P("section", None),
            P("section", None),
            P(None, None, "rows", None, None),
        ),
        out_specs=(
            P("section", None, None, "rows", None, None),
            P("section", None, None, "rows", None, None),
            P("section", None, None, "rows", None),
            P("section", None),
            P("section", None),
        ),
        check_vma=False,
    )
```

```python
import functools

import jax
import jax.numpy as jnp
from jax import lax
from jax.experimental import pallas as pl
from jax.experimental.pallas import tpu as pltpu
from jax.sharding import PartitionSpec as P

EPSILON = 1e-05
MESH = pl.DeviceIdType.MESH
BF16 = jnp.bfloat16
F32 = jnp.float32


def kernel(
    sections, strips, cols,
    images, cotangent, weights, gains, shifts, switches,
    outs, grads_in, weight_grad, gain_sum, shift_sum,
    w_v, wt_v, inp, mask_own, mask_v, gain_prev, shift_prev, zin, zin_stat, zown, own_stat, ub, slope_prev,
    prev_coef, own_coef, dyin, dy_stat, dzb, dyout, stat_out, sums_out, seed_sums, out_v, gin_v,
    ut_own, ut_all, dz_all, dz_taps, acc_v, swap_out, swap_in, dw_v,
    w_sem, in_sem, pi_s, pi_r, ie_s, ie_r, mp_s, mp_r, me_s, me_r, gp_s, gp_r,
    fz_s, fz_r, fs_s, fs_r, oe_s, oe_r, os_s, os_r, bz_s, bz_r, bs_s, bs_r, ls_s,
    out_sem, po_s, po_r, gin_sem, pg_s, pg_r,
    ut_s, ut_r, uf_s, uf_r, dz_s, dz_r, sw_s, sw_r, dw_sem,
):
    sec = lax.axis_index("section")
    row = lax.axis_index("rows")
    batches, tall, ch = inp.shape
    px = tall - 2 * cols
    strip = px // 2
    groups = tall // cols
    half = ch // 2
    total = float(px * strips)
    local = float(px)
    first, last, decoder = sec == 0, sec == sections - 1, sec == sections // 2
    late = sec >= sections // 2
    core = row % 2
    partner = row + 1 - 2 * core
    has_up, has_down = row >= 2, row < strips - 2
    centre = pl.ds(cols, px)
    chip = row // 2
    team, seat = row // 4, row % 4
    lanes = dz_all.shape[3]
    block = ut_all.shape[2]
    share = block // 4
    mine = pl.multiple_of(cols + strip * core, cols)

    def w_copy(r):
        return pltpu.make_async_copy(weights.at[r], w_v.at[r], w_sem.at[r])

    def in_copy(src, m):
        return pltpu.make_async_copy(src.at[m, core], inp.at[m, pl.ds(mine, strip), :], in_sem.at[m])

    for r in range(3):
        w_copy(r).start()

    @pl.when(first)
    def _():
        for m in range(batches):
            in_copy(images, m).start()

    @pl.when(last)
    def _():
        for m in range(batches):
            in_copy(cotangent, m).start()

    barrier = pltpu.get_barrier_semaphore()
    for s in range(sections):
        @pl.when((sec >= s - 1) & (sec <= s + 1))
        def _():
            def greet(i, carry):
                @pl.when((s != sec) | (i != row))
                def _():
                    pl.semaphore_signal(barrier, inc=1, device_id=(jnp.int32(s), i), device_id_type=MESH)
                return carry
            lax.fori_loop(0, strips, greet, 0)

    acc_v[...] = jnp.zeros_like(acc_v)
    gain_sum[...] = jnp.zeros_like(gain_sum)
    shift_sum[...] = jnp.zeros_like(shift_sum)

    for m in range(batches):
        for i in range(2):
            for at in (0, dz_all.shape[2] - cols):
                dz_all[m, i, pl.ds(at, cols), :] = jnp.zeros((cols, lanes), BF16)

    @pl.when(decoder)
    def _():
        wide = cols // 2
        windows_at = lax.broadcasted_iota(jnp.int32, (cols, wide), 1)
        places = lax.broadcasted_iota(jnp.int32, (cols, wide), 0)
        pick = (lax.shift_right_logical(places, 1) == windows_at).astype(F32)
        table = lax.dot_general(
            pick, switches[...].astype(F32), (((1,), (1,)), ((), ())), preferred_element_type=F32
        )
        odd = jnp.bitwise_and(lax.broadcasted_iota(jnp.int32, (cols, 128), 0), 1).astype(F32)
        windows = strip // cols // 2
        for m in range(batches):
            for i in range(2):
                for w in range(windows):
                    at = (m * 2 + i) * windows + w
                    value = jnp.broadcast_to(table[:, at : at + 1], (cols, 128))
                    for p in range(2):
                        hit = (jnp.abs(value - (2.0 * p + odd)) < 0.5).astype(F32).astype(BF16)
                        mask_own[m, i, pl.ds((2 * w + p) * cols, cols), :] = hit
        for m in range(batches):
            mask_v[m, pl.ds(mine, strip), :] = mask_own[m, core]

    @pl.when(jnp.logical_not(decoder))
    def _():
        mask_v[...] = jnp.ones_like(mask_v)

    near = 1 + jnp.where(sec > 0, 1, 0) + jnp.where(sec < sections - 1, 1, 0)
    pl.semaphore_wait(barrier, near * strips - 1)

    def remote(src, dst, send, recv, s, i):
        return pltpu.make_async_remote_copy(
            src_ref=src, dst_ref=dst, send_sem=send, recv_sem=recv, device_id=(s, i), device_id_type=MESH
        )

    def to_partner(src_at, dst_at, send, recv):
        return remote(src_at(1 - core), dst_at(pl.ds(mine, strip)), send, recv, sec, partner)

    def start_argument(src_at, dst_at, pair_sems, edge_sems):
        to_partner(src_at, dst_at, *pair_sems).start()

        @pl.when((core == 1) & has_down)
        def _():
            for i in range(2):
                remote(
                    src_at(i, pl.ds(strip - cols, cols)), dst_at(pl.ds(0, cols)),
                    edge_sems[0].at[i], edge_sems[1].at[0], sec, row + 1 + i,
                ).start()

        @pl.when((core == 0) & has_up)
        def _():
            for i in range(2):
                remote(
                    src_at(i, pl.ds(0, cols)), dst_at(pl.ds(cols + px, cols)),
                    edge_sems[0].at[i], edge_sems[1].at[1], sec, row - 2 + i,
                ).start()

    def argument_arrived(src_at, dst_at, pair_sems, edge_sems):
        to_partner(src_at, dst_at, *pair_sems).wait_recv()

        @pl.when(has_up)
        def _():
            remote(
                src_at(0, pl.ds(0, cols)), dst_at(pl.ds(0, cols)), edge_sems[0].at[0], edge_sems[1].at[0], sec, row
            ).wait_recv()

        @pl.when(has_down)
        def _():
            remote(
                src_at(0, pl.ds(0, cols)), dst_at(pl.ds(cols + px, cols)), edge_sems[0].at[0], edge_sems[1].at[1],
                sec, row,
            ).wait_recv()

    def argument_sent(src_at, dst_at, pair_sems, edge_sems):
        to_partner(src_at, dst_at, *pair_sems).wait_send()

        @pl.when(((core == 1) & has_down) | ((core == 0) & has_up))
        def _():
            for i in range(2):
                remote(
                    src_at(i, pl.ds(0, cols)), dst_at(pl.ds(0, cols)), edge_sems[0].at[i], edge_sems[1].at[0], sec, row
                ).wait_send()

    def input_parts(src, m):
        return (
            lambda i, r=pl.ds(0, strip): src.at[m, i, r, :],
            lambda r: inp.at[m, r, :],
            (pi_s.at[m], pi_r.at[m]),
            (ie_s.at[m], ie_r.at[m]),
        )

    mask_parts = (
        lambda i, r=pl.ds(0, strip): mask_own.at[:, i, r, :],
        lambda r: mask_v.at[:, r, :],
        (mp_s, mp_r),
        (me_s, me_r),
    )

    @pl.when(first)
    def _():
        for m in range(batches):
            start_argument(*input_parts(images, m))

    @pl.when(last)
    def _():
        for m in range(batches):
            start_argument(*input_parts(cotangent, m))

    @pl.when(decoder)
    def _():
        start_argument(*mask_parts)

    def affine_sends():
        return (
            remote(gains, gain_prev, gp_s.at[0], gp_r.at[0], sec + 1, row),
            remote(shifts, shift_prev, gp_s.at[1], gp_r.at[1], sec + 1, row),
        )

    @pl.when(sec < sections - 1)
    def _():
        for copy in affine_sends():
            copy.start()

    def block_sends(src, src_from, dst, send, recv, m, s):
        def one(k, h, src_row, dst_row, rows, i):
            part = pl.ds(h * half, half)
            return remote(
                src.at[m, pl.ds(src_from + src_row, rows), part], dst.at[m, pl.ds(dst_row, rows), part],
                send.at[m, k, h], recv.at[m, k, h], s, i,
            )
        return (
            (None, lambda h: one(0, h, 0, cols, px, row)),
            (has_down, lambda h: one(1, h, px - cols, 0, cols, row + 2)),
            (has_up, lambda h: one(2, h, 0, cols + px, cols, row - 2)),
        )

    def each(parts, h, act):
        for cond, make in parts:
            if cond is None:
                act(make(h))
            else:
                @pl.when(cond)
                def _():
                    act(make(h))

    def arrived(parts):
        (_, body), (_, to_down), (_, to_up) = parts
        for h in range(2):
            body(h).wait_recv()
        edges_arrived(to_down, to_up)

    def edges_arrived(to_down, to_up):
        @pl.when(has_up)
        def _():
            for h in range(2):
                to_down(h).wait_recv()

        @pl.when(has_down)
        def _():
            for h in range(2):
                to_up(h).wait_recv()

    def start(copy):
        copy.start()

    def sent(copy):
        copy.wait_send()

    def z_sends(m, s):
        return block_sends(zown, cols, zin, fz_s, fz_r, m, s)

    def own_edges(m):
        return block_sends(zown, cols, zown, oe_s, oe_r, m, sec)[1:]

    def dy_sends(m, s):
        return block_sends(dyout, 0, dyin, bz_s, bz_r, m, s)

    def stat_copy(src, dst, send, recv, m, s, i):
        return remote(src.at[m], dst.at[m, row], send.at[m, i], recv.at[m], s, i)

    def stats_each(src, dst, send, recv, m, s, same, act):
        def one(d, carry):
            i = row + d
            act(stat_copy(src, dst, send, recv, m, s, jnp.where(i >= strips, i - strips, i)))
            return carry
        lax.fori_loop(1 if same else 0, strips, one, 0)

    def start_stats(src, dst, send, recv, m, s, same):
        stats_each(src, dst, send, recv, m, s, same, start)
        if same:
            pltpu.make_async_copy(src.at[m], dst.at[m, row], recv.at[m]).start()

    def wait_stats(dst, recv, m):
        pltpu.make_async_copy(dst.at[m], dst.at[m], recv.at[m]).wait()

    down_stats = (stat_out, zin_stat, fs_s, fs_r)
    same_stats = (stat_out, own_stat, os_s, os_r)
    back_stats = (sums_out, dy_stat, bs_s, bs_r)
    seed_stats = (seed_sums, dy_stat, ls_s, bs_r)

    def join(stats_ref, m):
        means, squares = stats_ref[m, :, 0, :], stats_ref[m, :, 1, :]
        mean = jnp.sum(means, 0, keepdims=True) / float(strips)
        off = means - mean
        var = (jnp.sum(squares, 0, keepdims=True) + local * jnp.sum(off * off, 0, keepdims=True)) / total
        at = (jnp.maximum(row - 2, 0), row, jnp.minimum(row + 2, strips - 1))
        return lax.rsqrt(var + EPSILON), [stats_ref[m, i, pl.ds(0, 1), :] - mean for i in at]

    def kind(g):
        return 0 if g == 0 else 2 if g == groups - 1 else 1

    def inside(g, values):
        if kind(g) == 1:
            return values
        return jnp.where(has_up if kind(g) == 0 else has_down, values, jnp.zeros_like(values))

    def group(g):
        return pl.ds(g * cols, cols)

    column = lax.broadcasted_iota(jnp.int32, (1, cols, half), 1)

    def taps_joined(parts, left, right):
        def moved(values, by, edge):
            turned = pltpu.roll(values, by % px, 0).reshape(px // cols, cols, half)
            return jnp.where(column == edge, 0.0, turned).reshape(px, half)
        return parts[1] + moved(parts[left], 1, 0) + moved(parts[right], -1, cols - 1)

    def turned_copy(m, q):
        src = ut_own.at[m, pl.ds(pl.multiple_of((q // 2) * block, block), block), :]
        dst = ut_all.at[m, core, :, pl.ds(pl.multiple_of(chip * px, px), px)]
        return src, dst

    chips = strips // 2
    thirds = [1 + (chips - 1) * i // 3 for i in range(4)]

    def turned_each(m, act, low=1, high=chips):
        def one(d, carry):
            q = chip + d
            q = jnp.where(q >= chips, q - chips, q)
            src, dst = turned_copy(m, q)
            act(remote(src, dst, ut_s.at[m, d], ut_r.at[m], sec, 2 * q + core))
            return carry
        lax.fori_loop(low, high, one, 0)

    def turn_inputs(m):
        ut_own[m] = ub[m, centre, :].T
        src, dst = turned_copy(m, chip)
        pltpu.make_async_copy(src, dst, ut_r.at[m]).start()

    def send_turned_third(m, i):
        @pl.when(late & (m >= 0) & (m < batches))
        def _():
            if i == 0:
                turn_inputs(m)
            turned_each(m, start, thirds[i], thirds[i + 1])

    def turned_relay(m):
        return remote(ut_all.at[m, core], ut_all.at[m, core], uf_s.at[m], uf_r.at[m], sec, partner)

    def relay_turned(m):
        pltpu.make_async_copy(ut_all.at[m, core], ut_all.at[m, core], ut_r.at[m]).wait()
        turned_relay(m).start()

    def dz_copy(m, i):
        src = dzb.at[m, centre, pl.ds(pl.multiple_of((i % 4) * lanes, lanes), lanes)]
        dst = dz_all.at[m, core, pl.ds(pl.multiple_of(cols + chip * px, cols), px), :]
        return src, dst

    def dz_each(m, act):
        def one(d, carry):
            i = row + d
            i = jnp.where(i >= strips, i - strips, i)
            src, dst = dz_copy(m, i)
            act(remote(src, dst, dz_s.at[m, d], dz_r.at[m], sec, i))
            return carry
        lax.fori_loop(1, strips, one, 0)

    def send_dz(m):
        dz_each(m, start)
        src, dst = dz_copy(m, row)
        pltpu.make_async_copy(src, dst, dz_r.at[m]).start()

    def gather_taps(m):
        whole = dz_all.at[m, :, pl.ds(cols, px * (strips // 2)), :]
        pltpu.make_async_copy(whole, whole, dz_r.at[m]).wait()
        relayed = ut_all.at[m, 1 - core]
        pltpu.make_async_copy(relayed, relayed, uf_r.at[m]).wait()
        rows = dz_all.shape[2]
        edge = lax.broadcasted_iota(jnp.int32, (1, cols, lanes), 1)
        for i in range(2):
            values = dz_all[m, i].astype(F32)
            for c, by, gone in ((0, rows - 1, cols - 1), (2, 1, 0)):
                turned = pltpu.roll(values, by, 0).reshape(rows // cols, cols, lanes)
                turned = jnp.where(edge == gone, 0.0, turned).reshape(rows, lanes)
                dz_taps[i, :, pl.ds(c * lanes, lanes)] = turned.astype(BF16)
            dz_taps[i, :, pl.ds(lanes, lanes)] = dz_all[m, i]

    def kernel_row(m, r):
        part = jnp.zeros((block, 3 * lanes), F32)
        for i in range(2):
            part += jnp.dot(
                ut_all[m, i], dz_taps[i, pl.ds((2 - r) * cols, px * (strips // 2)), :], preferred_element_type=F32
            )
        return part

    def add_gradients(m):
        gather_taps(m)
        for r in range(3):
            acc_v[r] = acc_v[r] + kernel_row(m, r)

    def forward(m):
        @pl.when(first)
        def _():
            in_copy(images, m).wait()
            argument_arrived(*input_parts(images, m))
            for g in range(groups):
                ub[m, group(g), :] = inside(g, inp[m, group(g), :])

        @pl.when(sec > 0)
        def _():
            @pl.when(m == 0)
            def _():
                for copy in affine_sends():
                    copy.wait_recv()

                @pl.when(decoder)
                def _():
                    argument_arrived(*mask_parts)

            wait_stats(zin_stat, fs_r, m)
            inv, offs = join(zin_stat, m)
            prev_coef[m, pl.ds(0, 1), :] = inv
            prev_coef[m, pl.ds(1, 1), :] = offs[1]
            slant = 0.5 * inv * gain_prev[...]
            level = [slant * off + 0.5 * shift_prev[...] for off in offs]
            arrived(z_sends(m, sec))
            for g in range(groups):
                halved = zin[m, group(g), :].astype(F32) * slant + level[kind(g)]
                turn = jnp.tanh(halved)
                bent = halved * turn
                gate = jnp.concatenate([mask_v[m, group(g), :].astype(F32)] * (ch // 128), axis=1)
                ub[m, group(g), :] = inside(g, ((halved + bent) * gate).astype(BF16))
                if kind(g) == 1:
                    slope_prev[m, pl.ds((g - 1) * cols, cols), :] = (0.5 + 0.5 * turn) * (1.0 + halved - bent)

        @pl.when(first & (m == 0))
        def _():
            for r in range(3):
                w_copy(r).wait()

        for h in range(2):
            part = pl.ds(h * half, half)
            parts = []
            for c in range(3):
                acc = jnp.zeros((px, half), F32)
                for r in range(3):
                    acc += jnp.dot(
                        ub[m, pl.ds(r * cols, px), :], w_v[r, pl.ds(c * ch, ch), part], preferred_element_type=F32
                    )
                parts.append(acc)
            conv = taps_joined(parts, 0, 2)
            mean = jnp.sum(conv, 0, keepdims=True) / local
            conv = conv - mean
            stat_out[m, pl.ds(0, 1), part] = mean
            stat_out[m, pl.ds(1, 1), part] = jnp.sum(conv * conv, 0, keepdims=True)
            zown[m, centre, part] = conv.astype(BF16)

            @pl.when(sec < sections - 1)
            def _():
                if h == 1:
                    start_stats(*down_stats, m, sec + 1, False)
                each(z_sends(m, sec + 1), h, start)

        start_stats(*same_stats, m, sec, True)
        for h in range(2):
            each(own_edges(m), h, start)

    def finish(m):
        wait_stats(own_stat, os_r, m)
        inv, offs = join(own_stat, m)
        scale = inv * gains[...]
        own_coef[m, pl.ds(0, 1), :] = inv
        own_coef[m, pl.ds(1, 1), :] = scale
        for k in range(3):
            own_coef[m, pl.ds(2 + k, 1), :] = offs[k]
        slant = 0.5 * scale
        level = [slant * off + 0.5 * shifts[...] for off in offs]
        (_, to_down), (_, to_up) = own_edges(m)
        edges_arrived(to_down, to_up)

        @pl.when(last)
        def _():
            in_copy(cotangent, m).wait()
            argument_arrived(*input_parts(cotangent, m))
            sums = jnp.zeros((cols, ch), F32)
            cross = jnp.zeros((cols, ch), F32)
            for g in range(groups):
                z = zown[m, group(g), :].astype(F32)
                halved = z * slant + level[kind(g)]
                turn = jnp.tanh(halved)
                bent = halved * turn
                dy = inp[m, group(g), :].astype(F32) * ((0.5 + 0.5 * turn) * (1.0 + halved - bent))
                dyin[m, group(g), :] = dy.astype(BF16)
                if kind(g) == 1:
                    out_v[m, pl.ds((g - 1) * cols, cols), :] = (halved + bent).astype(BF16)
                    sums += dy
                    cross += dy * z
            one = jnp.sum(sums, 0, keepdims=True)
            seed_sums[m, pl.ds(0, 1), :] = one
            seed_sums[m, pl.ds(1, 1), :] = inv * (jnp.sum(cross, 0, keepdims=True) + offs[1] * one)
            start_stats(*seed_stats, m, sec, True)

        @pl.when(jnp.logical_not(last))
        def _():
            for g in range(1, groups - 1):
                halved = zown[m, group(g), :].astype(F32) * slant + level[1]
                out_v[m, pl.ds((g - 1) * cols, cols), :] = (halved + halved * jnp.tanh(halved)).astype(BF16)

        for copy in result_copies(out_v, outs, out_sem, po_s, po_r, m):
            copy.start()

    def result_copies(src, dst, sem, send, recv, m):
        here, there = pl.multiple_of(strip * core, cols), pl.multiple_of(strip * (1 - core), cols)
        return (
            pltpu.make_async_copy(src.at[m, pl.ds(here, strip), :], dst.at[m, core], sem.at[m]),
            remote(src.at[m, pl.ds(there, strip), :], dst.at[m, core], send.at[m], recv.at[m], sec, partner),
        )

    def backward(m):
        wait_stats(dy_stat, bs_r, m)
        first_sum = jnp.sum(dy_stat[m, :, 0, :], 0, keepdims=True)
        cross_sum = jnp.sum(dy_stat[m, :, 1, :], 0, keepdims=True)
        shift_sum[...] += first_sum
        gain_sum[...] += cross_sum
        inv = own_coef[m, pl.ds(0, 1), :]
        scale = own_coef[m, pl.ds(1, 1), :]
        tilt = scale * inv * (cross_sum / total)
        base = [scale * (first_sum / total) + tilt * own_coef[m, pl.ds(2 + k, 1), :] for k in range(3)]

        @pl.when(sec < sections - 1)
        def _():
            arrived(dy_sends(m, sec))

        for g in range(groups):
            dz = dyin[m, group(g), :].astype(F32) * scale - zown[m, group(g), :].astype(F32) * tilt - base[kind(g)]
            dzb[m, group(g), :] = inside(g, dz.astype(BF16))

        @pl.when(first)
        def _():
            send_dz(m)

        for h in range(2):
            part = pl.ds(h * half, half)
            parts = []
            for c in range(3):
                acc = jnp.zeros((px, half), F32)
                for r in range(3):
                    acc += jnp.dot(
                        dzb[m, pl.ds((2 - r) * cols, px), :], wt_v[r, pl.ds(c * ch, ch), part],
                        preferred_element_type=F32,
                    )
                parts.append(acc)
            gate = jnp.concatenate([mask_v[m, centre, :].astype(F32)] * (half // 128), axis=1)
            du = (taps_joined(parts, 2, 0) * gate).astype(BF16)
            gin_v[m, :, part] = du

            @pl.when(sec > 0)
            def _():
                dy = du.astype(F32) * slope_prev[m, :, part]
                dyout[m, :, part] = dy.astype(BF16)
                one = jnp.sum(dy, 0, keepdims=True)
                cross = jnp.sum(dy * zin[m, centre, part].astype(F32), 0, keepdims=True)
                sums_out[m, pl.ds(0, 1), part] = one
                sums_out[m, pl.ds(1, 1), part] = prev_coef[m, pl.ds(0, 1), part] * (
                    cross + prev_coef[m, pl.ds(1, 1), part] * one
                )
                if h == 1:
                    start_stats(*back_stats, m, sec - 1, False)
                each(dy_sends(m, sec - 1), h, start)

        for copy in result_copies(gin_v, grads_in, gin_sem, pg_s, pg_r, m):
            copy.start()

        @pl.when((sec > 0) & (sec < sections - 1))
        def _():
            send_dz(m)

    def turn_weights():
        def one(i, carry):
            at = pl.ds(pl.multiple_of(lax.rem(i, 3) * ch, ch), ch)
            wt_v[lax.div(i, 3), at, :] = w_v[lax.div(i, 3), at, :].T
            return carry
        lax.fori_loop(0, 9, one, 0)

    @pl.when(jnp.logical_not(first))
    def _():
        for r in range(3):
            w_copy(r).wait()
        turn_weights()

    def step(t, carry):
        @pl.when(first & (t == batches))
        def _():
            turn_weights()

        ahead = t - sec
        behind = t - (2 * sections - 1 - sec)

        @pl.when((ahead >= 0) & (ahead < batches))
        def _():
            forward(ahead)

        send_turned_third(ahead, 0)

        @pl.when(jnp.logical_not(late) & (ahead == batches))
        def _():
            def turned(m, carry):
                turn_inputs(m)
                turned_each(m, start)
                return carry
            lax.fori_loop(0, batches, turned, 0)

        done = ahead - jnp.where(last, 0, 1)

        @pl.when((behind >= 0) & (behind < batches))
        def _():
            backward(behind)

        send_turned_third(ahead, 1)

        @pl.when((done >= 0) & (done < batches))
        def _():
            finish(done)

        send_turned_third(ahead, 2)

        @pl.when(late & (ahead >= 2) & (ahead < batches + 2))
        def _():
            relay_turned(ahead - 2)

        @pl.when(jnp.logical_not(late) & (ahead == batches + 1))
        def _():
            def relay(m, carry):
                relay_turned(m)
                return carry
            lax.fori_loop(0, batches, relay, 0)

        @pl.when((behind >= 1) & (behind < batches) & jnp.logical_not(last))
        def _():
            add_gradients(behind - 1)

        return carry

    lax.fori_loop(0, 2 * sections - 1 + batches, step, 0)

    @pl.when(last)
    def _():
        def send(m, carry):
            send_dz(m)
            return carry

        def add(m, carry):
            add_gradients(m)
            return carry

        lax.fori_loop(0, batches, send, 0)
        lax.fori_loop(0, batches - 1, add, 0)

    def swap(r, d):
        other = (seat + d) % 4
        return remote(
            swap_out.at[r, pl.ds(pl.multiple_of(other * share, share), share), :], swap_in.at[r, 4 - d - 1],
            sw_s.at[r, d - 1], sw_r.at[r, 4 - d - 1], sec, 4 * team + other,
        )

    gather_taps(batches - 1)
    for r in range(3):
        part = acc_v[r] + kernel_row(batches - 1, r)
        acc_v[r] = part
        swap_out[r] = part.astype(BF16)
        for d in range(1, 4):
            swap(r, d).start()

    def dw_copy(r):
        return pltpu.make_async_copy(dw_v.at[r], weight_grad.at[r], dw_sem.at[r])

    own_rows = pl.ds(pl.multiple_of(seat * share, share), share)
    for r in range(3):
        for c in range(3):
            dw_v[r, c, :, pl.ds(pl.multiple_of(seat * lanes, lanes), lanes)] = acc_v[r, own_rows, pl.ds(c * lanes, lanes)]
        for d in range(1, 4):
            swap(r, 4 - d).wait_recv()
            source = (seat + d) % 4
            for c in range(3):
                dw_v[r, c, :, pl.ds(pl.multiple_of(source * lanes, lanes), lanes)] = swap_in[
                    r, d - 1, :, pl.ds(c * lanes, lanes)
                ].astype(F32)
        dw_copy(r).start()

    for r in range(3):
        dw_copy(r).wait()
        for d in range(1, 4):
            swap(r, d).wait_send()

    @pl.when(decoder)
    def _():
        argument_sent(*mask_parts)

    @pl.when(sec < sections - 1)
    def _():
        for copy in affine_sends():
            copy.wait_send()

    def drain(m, carry):
        for src, dst, sems in ((out_v, outs, (out_sem, po_s, po_r)), (gin_v, grads_in, (gin_sem, pg_s, pg_r))):
            here, there = result_copies(src, dst, *sems, m)
            here.wait()
            there.wait_send()
            remote(
                src.at[m, pl.ds(0, strip), :], dst.at[m, 1 - core], sems[1].at[m], sems[2].at[m], sec, partner
            ).wait_recv()

        turned_each(m, sent)
        turned_relay(m).wait_send()
        dz_each(m, sent)

        @pl.when(first)
        def _():
            argument_sent(*input_parts(images, m))

        @pl.when(last)
        def _():
            argument_sent(*input_parts(cotangent, m))
            stats_each(*seed_stats, m, sec, True, sent)

        @pl.when(sec < sections - 1)
        def _():
            stats_each(*down_stats, m, sec + 1, False, sent)
            for h in range(2):
                each(z_sends(m, sec + 1), h, sent)

        stats_each(*same_stats, m, sec, True, sent)
        for h in range(2):
            each(own_edges(m), h, sent)

        @pl.when(sec > 0)
        def _():
            stats_each(*back_stats, m, sec - 1, False, sent)
            for h in range(2):
                each(dy_sends(m, sec - 1), h, sent)

        return carry

    lax.fori_loop(0, batches, drain, 0)


def settle(*refs):
    count = len(refs) // 2
    sources, targets, sems = refs[:count], refs[count : 2 * count], refs[-1]
    copies = []
    for src, dst in zip(sources, targets):
        if len(src.shape) == 2:
            copies.append((src, dst))
        else:
            copies += [(src.at[i], dst.at[i]) for i in range(src.shape[0])]
    copies = [pltpu.make_async_copy(src, dst, sems.at[i]) for i, (src, dst) in enumerate(copies)]
    for copy in copies:
        copy.start()
    for copy in copies:
        copy.wait()


def body(images, switches, conv_weights, gains, shifts, cotangent):
    sections = lax.axis_size("section")
    strips = lax.axis_size("rows")
    batches, pictures, strip_rows, cols, ch = images.shape
    strip = strip_rows * cols
    px = 2 * strip
    tall = px + 2 * cols
    anywhere = pl.BlockSpec(memory_space=pl.ANY)
    vmem = pl.BlockSpec(memory_space=pltpu.VMEM)
    dma = pltpu.SemaphoreType.DMA
    flops = 3 * 2 * 9 * ch * ch * batches * px
    share = ch // strips
    outs, grads_in, weight_grad, gain_sum, shift_sum = pl.pallas_call(
        functools.partial(kernel, sections, strips, cols),
        out_shape=(
            jax.ShapeDtypeStruct((batches, pictures, strip, ch), BF16),
            jax.ShapeDtypeStruct((batches, pictures, strip, ch), BF16),
            jax.ShapeDtypeStruct((3, 3, share, ch), F32),
            jax.ShapeDtypeStruct((1, ch), F32),
            jax.ShapeDtypeStruct((1, ch), F32),
        ),
        in_specs=[anywhere, anywhere, anywhere, vmem, vmem, vmem],
        out_specs=(anywhere, anywhere, anywhere, vmem, vmem),
        scratch_shapes=[
            pltpu.VMEM((3, 3 * ch, ch), BF16),
            pltpu.VMEM((3, 3 * ch, ch), BF16),
            pltpu.VMEM((batches, tall, ch), BF16),
            pltpu.VMEM((batches, 2, strip, 128), BF16),
            pltpu.VMEM((batches, tall, 128), BF16),
            pltpu.VMEM((1, ch), F32),
            pltpu.VMEM((1, ch), F32),
            pltpu.VMEM((batches, tall, ch), BF16),
            pltpu.VMEM((batches, strips, 2, ch), F32),
            pltpu.VMEM((batches, tall, ch), BF16),
            pltpu.VMEM((batches, strips, 2, ch), F32),
            pltpu.VMEM((batches, tall, ch), BF16),
            pltpu.VMEM((batches, px, ch), F32),
            pltpu.VMEM((batches, 2, ch), F32),
            pltpu.VMEM((batches, 8, ch), F32),
            pltpu.VMEM((batches, tall, ch), BF16),
            pltpu.VMEM((batches, strips, 2, ch), F32),
            pltpu.VMEM((batches, tall, ch), BF16),
            pltpu.VMEM((batches, px, ch), BF16),
            pltpu.VMEM((batches, 2, ch), F32),
            pltpu.VMEM((batches, 2, ch), F32),
            pltpu.VMEM((batches, 2, ch), F32),
            pltpu.VMEM((batches, px, ch), BF16),
            pltpu.VMEM((batches, px, ch), BF16),
            pltpu.VMEM((batches, ch, px), BF16),
            pltpu.VMEM((batches, 2, 4 * share, px * strips // 2), BF16),
            pltpu.VMEM((batches, 2, px * strips // 2 + 2 * cols, ch // 4), BF16),
            pltpu.VMEM((2, px * strips // 2 + 2 * cols, 3 * ch // 4), BF16),
            pltpu.VMEM((3, 4 * share, 3 * ch // 4), F32),
            pltpu.VMEM((3, 4 * share, 3 * ch // 4), BF16),
            pltpu.VMEM((3, 3, share, 3 * ch // 4), BF16),
            pltpu.VMEM((3, 3, share, ch), F32),
            dma((3,)),
            dma((batches,)),
            dma((batches,)), dma((batches,)),
            dma((batches, 2)), dma((batches, 2)),
            dma, dma,
            dma((2,)), dma((2,)),
            dma((2,)), dma((2,)),
            dma((batches, 3, 2)), dma((batches, 3, 2)),
            dma((batches, strips)), dma((batches,)),
            dma((batches, 3, 2)), dma((batches, 3, 2)),
            dma((batches, strips)), dma((batches,)),
            dma((batches, 3, 2)), dma((batches, 3, 2)),
            dma((batches, strips)), dma((batches,)),
            dma((batches, strips)),
            dma((batches,)), dma((batches,)), dma((batches,)),
            dma((batches,)), dma((batches,)), dma((batches,)),
            dma((batches, strips // 2)), dma((batches,)),
            dma((batches,)), dma((batches,)),
            dma((batches, strips)), dma((batches,)),
            dma((3, 3)), dma((3, 3)),
            dma((3,)),
        ],
        compiler_params=pltpu.CompilerParams(
            collective_id=0, has_side_effects=True, vmem_limit_bytes=56 * 2**20
        ),
        cost_estimate=pl.CostEstimate(
            flops=flops, bytes_accessed=2 * 9 * ch * ch * 2, transcendentals=0
        ),
    )(
        images.reshape(batches, pictures, strip, ch),
        cotangent.reshape(batches, pictures, strip, ch),
        conv_weights.reshape(3, 3 * ch, ch),
        gains,
        shifts,
        switches.reshape(-1, switches.shape[-1]),
    )
    results = (outs, grads_in, weight_grad, gain_sum, shift_sum)
    outs, grads_in, weight_grad, gain_sum, shift_sum = pl.pallas_call(
        settle,
        out_shape=tuple(jax.ShapeDtypeStruct(r.shape, r.dtype) for r in results),
        in_specs=[pl.BlockSpec(memory_space=pltpu.HBM)] * 5,
        out_specs=(pl.BlockSpec(memory_space=pltpu.HBM),) * 5,
        scratch_shapes=[dma((2 * batches + 3 + 2,))],
    )(*results)
    shape = (1, batches, pictures, strip_rows, cols, ch)
    return (outs.reshape(shape), grads_in.reshape(shape), weight_grad[None], gain_sum, shift_sum)


def solution(mesh):
    return jax.shard_map(
        body,
        mesh=mesh,
        in_specs=(
            P(None, None, "rows", None, None),
            P(None, None, "rows", None),
            P("section", None, None, None, None),
            P("section", None),
            P("section", None),
            P(None, None, "rows", None, None),
        ),
        out_specs=(
            P("section", None, None, "rows", None, None),
            P("section", None, None, "rows", None, None),
            P("section", None, None, "rows", None),
            P("section", None),
            P("section", None),
        ),
        check_vma=False,
    )
```

```python
import functools

import jax
import jax.numpy as jnp
from jax import lax
from jax.experimental import pallas as pl
from jax.experimental.pallas import tpu as pltpu
from jax.sharding import PartitionSpec as P

EPSILON = 1e-05
MESH = pl.DeviceIdType.MESH
BF16 = jnp.bfloat16
F32 = jnp.float32


def kernel(
    sections, strips, cols,
    images, cotangent, weights, gains, shifts, switches,
    outs, grads_in, weight_grad, gain_sum, shift_sum,
    w_v, wt_v, inp, mask_own, mask_v, gain_prev, shift_prev, zin, zin_stat, zown, own_stat, ub, slope_prev,
    prev_coef, own_coef, dyin, dy_stat, dzb, dyout, stat_out, sums_out, seed_sums, out_v, gin_v,
    ut_own, ut_all, dz_all, dz_taps, acc_v, swap_out, swap_in, dw_v,
    w_sem, in_sem, pi_s, pi_r, ie_s, ie_r, mp_s, mp_r, me_s, me_r, gp_s, gp_r,
    fz_s, fz_r, fs_s, fs_r, oe_s, oe_r, os_s, os_r, bz_s, bz_r, bs_s, bs_r, ls_s,
    out_sem, po_s, po_r, gin_sem, pg_s, pg_r,
    ut_s, ut_r, uf_s, uf_r, dz_s, dz_r, sw_s, sw_r, dw_sem,
):
    sec = lax.axis_index("section")
    row = lax.axis_index("rows")
    batches, tall, ch = inp.shape
    px = tall - 2 * cols
    strip = px // 2
    groups = tall // cols
    half = ch // 2
    total = float(px * strips)
    local = float(px)
    first, last, decoder = sec == 0, sec == sections - 1, sec == sections // 2
    late = sec >= sections // 2
    core = row % 2
    partner = row + 1 - 2 * core
    has_up, has_down = row >= 2, row < strips - 2
    centre = pl.ds(cols, px)
    chip = row // 2
    team, seat = row // 4, row % 4
    lanes = dz_all.shape[3]
    block = ut_all.shape[2]
    share = block // 4
    mine = pl.multiple_of(cols + strip * core, cols)

    def w_copy(r):
        return pltpu.make_async_copy(weights.at[r], w_v.at[r], w_sem.at[r])

    def in_copy(src, m):
        return pltpu.make_async_copy(src.at[m, core], inp.at[m, pl.ds(mine, strip), :], in_sem.at[m])

    for r in range(3):
        w_copy(r).start()

    @pl.when(first)
    def _():
        for m in range(batches):
            in_copy(images, m).start()

    @pl.when(last)
    def _():
        for m in range(batches):
            in_copy(cotangent, m).start()

    barrier = pltpu.get_barrier_semaphore()
    for s in range(sections):
        @pl.when((sec >= s - 1) & (sec <= s + 1))
        def _():
            def greet(i, carry):
                @pl.when((s != sec) | (i != row))
                def _():
                    pl.semaphore_signal(barrier, inc=1, device_id=(jnp.int32(s), i), device_id_type=MESH)
                return carry
            lax.fori_loop(0, strips, greet, 0)

    acc_v[...] = jnp.zeros_like(acc_v)
    gain_sum[...] = jnp.zeros_like(gain_sum)
    shift_sum[...] = jnp.zeros_like(shift_sum)

    for m in range(batches):
        for i in range(2):
            for at in (0, dz_all.shape[2] - cols):
                dz_all[m, i, pl.ds(at, cols), :] = jnp.zeros((cols, lanes), BF16)

    @pl.when(decoder)
    def _():
        wide = cols // 2
        windows_at = lax.broadcasted_iota(jnp.int32, (cols, wide), 1)
        places = lax.broadcasted_iota(jnp.int32, (cols, wide), 0)
        pick = (lax.shift_right_logical(places, 1) == windows_at).astype(F32)
        table = lax.dot_general(
            pick, switches[...].astype(F32), (((1,), (1,)), ((), ())), preferred_element_type=F32
        )
        odd = jnp.bitwise_and(lax.broadcasted_iota(jnp.int32, (cols, 128), 0), 1).astype(F32)
        windows = strip // cols // 2
        for m in range(batches):
            for i in range(2):
                for w in range(windows):
                    at = (m * 2 + i) * windows + w
                    value = jnp.broadcast_to(table[:, at : at + 1], (cols, 128))
                    for p in range(2):
                        hit = (jnp.abs(value - (2.0 * p + odd)) < 0.5).astype(F32).astype(BF16)
                        mask_own[m, i, pl.ds((2 * w + p) * cols, cols), :] = hit
        for m in range(batches):
            mask_v[m, pl.ds(mine, strip), :] = mask_own[m, core]

    @pl.when(jnp.logical_not(decoder))
    def _():
        mask_v[...] = jnp.ones_like(mask_v)

    near = 1 + jnp.where(sec > 0, 1, 0) + jnp.where(sec < sections - 1, 1, 0)
    pl.semaphore_wait(barrier, near * strips - 1)

    def remote(src, dst, send, recv, s, i):
        return pltpu.make_async_remote_copy(
            src_ref=src, dst_ref=dst, send_sem=send, recv_sem=recv, device_id=(s, i), device_id_type=MESH
        )

    def to_partner(src_at, dst_at, send, recv):
        return remote(src_at(1 - core), dst_at(pl.ds(mine, strip)), send, recv, sec, partner)

    def start_argument(src_at, dst_at, pair_sems, edge_sems):
        to_partner(src_at, dst_at, *pair_sems).start()

        @pl.when((core == 1) & has_down)
        def _():
            for i in range(2):
                remote(
                    src_at(i, pl.ds(strip - cols, cols)), dst_at(pl.ds(0, cols)),
                    edge_sems[0].at[i], edge_sems[1].at[0], sec, row + 1 + i,
                ).start()

        @pl.when((core == 0) & has_up)
        def _():
            for i in range(2):
                remote(
                    src_at(i, pl.ds(0, cols)), dst_at(pl.ds(cols + px, cols)),
                    edge_sems[0].at[i], edge_sems[1].at[1], sec, row - 2 + i,
                ).start()

    def argument_arrived(src_at, dst_at, pair_sems, edge_sems):
        to_partner(src_at, dst_at, *pair_sems).wait_recv()

        @pl.when(has_up)
        def _():
            remote(
                src_at(0, pl.ds(0, cols)), dst_at(pl.ds(0, cols)), edge_sems[0].at[0], edge_sems[1].at[0], sec, row
            ).wait_recv()

        @pl.when(has_down)
        def _():
            remote(
                src_at(0, pl.ds(0, cols)), dst_at(pl.ds(cols + px, cols)), edge_sems[0].at[0], edge_sems[1].at[1],
                sec, row,
            ).wait_recv()

    def argument_sent(src_at, dst_at, pair_sems, edge_sems):
        to_partner(src_at, dst_at, *pair_sems).wait_send()

        @pl.when(((core == 1) & has_down) | ((core == 0) & has_up))
        def _():
            for i in range(2):
                remote(
                    src_at(i, pl.ds(0, cols)), dst_at(pl.ds(0, cols)), edge_sems[0].at[i], edge_sems[1].at[0], sec, row
                ).wait_send()

    def input_parts(src, m):
        return (
            lambda i, r=pl.ds(0, strip): src.at[m, i, r, :],
            lambda r: inp.at[m, r, :],
            (pi_s.at[m], pi_r.at[m]),
            (ie_s.at[m], ie_r.at[m]),
        )

    mask_parts = (
        lambda i, r=pl.ds(0, strip): mask_own.at[:, i, r, :],
        lambda r: mask_v.at[:, r, :],
        (mp_s, mp_r),
        (me_s, me_r),
    )

    @pl.when(first)
    def _():
        for m in range(batches):
            start_argument(*input_parts(images, m))

    @pl.when(last)
    def _():
        for m in range(batches):
            start_argument(*input_parts(cotangent, m))

    @pl.when(decoder)
    def _():
        start_argument(*mask_parts)

    def affine_sends():
        return (
            remote(gains, gain_prev, gp_s.at[0], gp_r.at[0], sec + 1, row),
            remote(shifts, shift_prev, gp_s.at[1], gp_r.at[1], sec + 1, row),
        )

    @pl.when(sec < sections - 1)
    def _():
        for copy in affine_sends():
            copy.start()

    def block_sends(src, src_from, dst, send, recv, m, s):
        def one(k, h, src_row, dst_row, rows, i):
            part = pl.ds(h * half, half)
            return remote(
                src.at[m, pl.ds(src_from + src_row, rows), part], dst.at[m, pl.ds(dst_row, rows), part],
                send.at[m, k, h], recv.at[m, k, h], s, i,
            )
        return (
            (None, lambda h: one(0, h, 0, cols, px, row)),
            (has_down, lambda h: one(1, h, px - cols, 0, cols, row + 2)),
            (has_up, lambda h: one(2, h, 0, cols + px, cols, row - 2)),
        )

    def each(parts, h, act):
        for cond, make in parts:
            if cond is None:
                act(make(h))
            else:
                @pl.when(cond)
                def _():
                    act(make(h))

    def arrived(parts):
        (_, body), (_, to_down), (_, to_up) = parts
        for h in range(2):
            body(h).wait_recv()
        edges_arrived(to_down, to_up)

    def edges_arrived(to_down, to_up):
        @pl.when(has_up)
        def _():
            for h in range(2):
                to_down(h).wait_recv()

        @pl.when(has_down)
        def _():
            for h in range(2):
                to_up(h).wait_recv()

    def start(copy):
        copy.start()

    def sent(copy):
        copy.wait_send()

    def came(copy):
        copy.wait_recv()

    def z_sends(m, s):
        return block_sends(zown, cols, zin, fz_s, fz_r, m, s)

    def own_edges(m):
        return block_sends(zown, cols, zown, oe_s, oe_r, m, sec)[1:]

    def dy_sends(m, s):
        return block_sends(dyout, 0, dyin, bz_s, bz_r, m, s)

    def stat_copy(src, dst, send, recv, m, s, i):
        return remote(src.at[m], dst.at[m, row], send.at[m, i], recv.at[m], s, i)

    def stats_each(src, dst, send, recv, m, s, same, act):
        def one(d, carry):
            i = row + d
            act(stat_copy(src, dst, send, recv, m, s, jnp.where(i >= strips, i - strips, i)))
            return carry
        lax.fori_loop(1 if same else 0, strips, one, 0)

    def start_stats(src, dst, send, recv, m, s, same):
        stats_each(src, dst, send, recv, m, s, same, start)
        if same:
            pltpu.make_async_copy(src.at[m], dst.at[m, row], recv.at[m]).start()

    def wait_stats(dst, recv, m):
        pltpu.make_async_copy(dst.at[m], dst.at[m], recv.at[m]).wait()

    down_stats = (stat_out, zin_stat, fs_s, fs_r)
    same_stats = (stat_out, own_stat, os_s, os_r)
    back_stats = (sums_out, dy_stat, bs_s, bs_r)
    seed_stats = (seed_sums, dy_stat, ls_s, bs_r)

    def join(stats_ref, m):
        means, squares = stats_ref[m, :, 0, :], stats_ref[m, :, 1, :]
        mean = jnp.sum(means, 0, keepdims=True) / float(strips)
        off = means - mean
        var = (jnp.sum(squares, 0, keepdims=True) + local * jnp.sum(off * off, 0, keepdims=True)) / total
        at = (jnp.maximum(row - 2, 0), row, jnp.minimum(row + 2, strips - 1))
        return lax.rsqrt(var + EPSILON), [stats_ref[m, i, pl.ds(0, 1), :] - mean for i in at]

    def kind(g):
        return 0 if g == 0 else 2 if g == groups - 1 else 1

    def inside(g, values):
        if kind(g) == 1:
            return values
        return jnp.where(has_up if kind(g) == 0 else has_down, values, jnp.zeros_like(values))

    def group(g):
        return pl.ds(g * cols, cols)

    column = lax.broadcasted_iota(jnp.int32, (1, cols, half), 1)

    def taps_joined(parts, left, right):
        def moved(values, by, edge):
            turned = pltpu.roll(values, by % px, 0).reshape(px // cols, cols, half)
            return jnp.where(column == edge, 0.0, turned).reshape(px, half)
        return parts[1] + moved(parts[left], 1, 0) + moved(parts[right], -1, cols - 1)

    def turned_copy(m, q):
        src = ut_own.at[m, pl.ds(pl.multiple_of((q // 2) * block, block), block), :]
        dst = ut_all.at[m, core, :, pl.ds(pl.multiple_of(chip * px, px), px)]
        return src, dst

    chips = strips // 2
    thirds = [1 + (chips - 1) * i // 3 for i in range(4)]

    def turned_each(m, act, low=1, high=chips):
        def one(d, carry):
            q = chip + d
            q = jnp.where(q >= chips, q - chips, q)
            src, dst = turned_copy(m, q)
            act(remote(src, dst, ut_s.at[m, d], ut_r.at[m, d], sec, 2 * q + core))
            return carry
        lax.fori_loop(low, high, one, 0)

    def turn_inputs(m):
        ut_own[m] = ub[m, centre, :].T
        mine_at = pl.ds(pl.multiple_of(team * block, block), block)
        ut_all[m, core, :, pl.ds(pl.multiple_of(chip * px, px), px)] = ut_own[m, mine_at, :]

    def send_turned_third(m, i):
        @pl.when(late & (m >= 0) & (m < batches))
        def _():
            if i == 0:
                turn_inputs(m)
            turned_each(m, start, thirds[i], thirds[i + 1])

    def turned_relay(m):
        return remote(ut_all.at[m, core], ut_all.at[m, core], uf_s.at[m], uf_r.at[m], sec, partner)

    def relay_turned(m):
        turned_each(m, came)
        turned_relay(m).start()

    def dz_copy(m, i):
        src = dzb.at[m, centre, pl.ds(pl.multiple_of((i % 4) * lanes, lanes), lanes)]
        dst = dz_all.at[m, core, pl.ds(pl.multiple_of(cols + chip * px, cols), px), :]
        return src, dst

    def dz_each(m, act):
        def one(d, carry):
            i = row + d
            i = jnp.where(i >= strips, i - strips, i)
            src, dst = dz_copy(m, i)
            act(remote(src, dst, dz_s.at[m, d], dz_r.at[m, d], sec, i))
            return carry
        lax.fori_loop(1, strips, one, 0)

    def send_dz(m):
        dz_each(m, start)
        quarter = pl.ds(pl.multiple_of(seat * lanes, lanes), lanes)
        dz_all[m, core, pl.ds(pl.multiple_of(cols + chip * px, cols), px), :] = dzb[m, centre, quarter]

    def gather_taps(m):
        dz_each(m, came)
        relayed = ut_all.at[m, 1 - core]
        pltpu.make_async_copy(relayed, relayed, uf_r.at[m]).wait()
        rows = dz_all.shape[2]
        edge = lax.broadcasted_iota(jnp.int32, (1, cols, lanes), 1)
        for i in range(2):
            values = dz_all[m, i].astype(F32)
            for c, by, gone in ((0, rows - 1, cols - 1), (2, 1, 0)):
                turned = pltpu.roll(values, by, 0).reshape(rows // cols, cols, lanes)
                turned = jnp.where(edge == gone, 0.0, turned).reshape(rows, lanes)
                dz_taps[i, :, pl.ds(c * lanes, lanes)] = turned.astype(BF16)
            dz_taps[i, :, pl.ds(lanes, lanes)] = dz_all[m, i]

    def kernel_row(m, r):
        part = jnp.zeros((block, 3 * lanes), F32)
        for i in range(2):
            part += jnp.dot(
                ut_all[m, i], dz_taps[i, pl.ds((2 - r) * cols, px * (strips // 2)), :], preferred_element_type=F32
            )
        return part

    def add_gradients(m):
        gather_taps(m)
        for r in range(3):
            acc_v[r] = acc_v[r] + kernel_row(m, r)

    def forward(m):
        @pl.when(first)
        def _():
            in_copy(images, m).wait()
            argument_arrived(*input_parts(images, m))
            for g in range(groups):
                ub[m, group(g), :] = inside(g, inp[m, group(g), :])

        @pl.when(sec > 0)
        def _():
            @pl.when(m == 0)
            def _():
                for copy in affine_sends():
                    copy.wait_recv()

                @pl.when(decoder)
                def _():
                    argument_arrived(*mask_parts)

            wait_stats(zin_stat, fs_r, m)
            inv, offs = join(zin_stat, m)
            prev_coef[m, pl.ds(0, 1), :] = inv
            prev_coef[m, pl.ds(1, 1), :] = offs[1]
            slant = 0.5 * inv * gain_prev[...]
            level = [slant * off + 0.5 * shift_prev[...] for off in offs]
            arrived(z_sends(m, sec))
            for g in range(groups):
                halved = zin[m, group(g), :].astype(F32) * slant + level[kind(g)]
                turn = jnp.tanh(halved)
                bent = halved * turn
                gate = jnp.concatenate([mask_v[m, group(g), :].astype(F32)] * (ch // 128), axis=1)
                ub[m, group(g), :] = inside(g, ((halved + bent) * gate).astype(BF16))
                if kind(g) == 1:
                    slope_prev[m, pl.ds((g - 1) * cols, cols), :] = (0.5 + 0.5 * turn) * (1.0 + halved - bent)

        @pl.when(jnp.logical_not(late) & (m == 0))
        def _():
            for r in range(3):
                w_copy(r).wait()

        for h in range(2):
            part = pl.ds(h * half, half)
            parts = []
            for c in range(3):
                acc = jnp.zeros((px, half), F32)
                for r in range(3):
                    acc += jnp.dot(
                        ub[m, pl.ds(r * cols, px), :], w_v[r, pl.ds(c * ch, ch), part], preferred_element_type=F32
                    )
                parts.append(acc)
            conv = taps_joined(parts, 0, 2)
            mean = jnp.sum(conv, 0, keepdims=True) / local
            conv = conv - mean
            stat_out[m, pl.ds(0, 1), part] = mean
            stat_out[m, pl.ds(1, 1), part] = jnp.sum(conv * conv, 0, keepdims=True)
            zown[m, centre, part] = conv.astype(BF16)

            @pl.when(sec < sections - 1)
            def _():
                if h == 1:
                    start_stats(*down_stats, m, sec + 1, False)
                each(z_sends(m, sec + 1), h, start)

        start_stats(*same_stats, m, sec, True)
        for h in range(2):
            each(own_edges(m), h, start)

    def finish(m):
        wait_stats(own_stat, os_r, m)
        inv, offs = join(own_stat, m)
        scale = inv * gains[...]
        own_coef[m, pl.ds(0, 1), :] = inv
        own_coef[m, pl.ds(1, 1), :] = scale
        for k in range(3):
            own_coef[m, pl.ds(2 + k, 1), :] = offs[k]
        slant = 0.5 * scale
        level = [slant * off + 0.5 * shifts[...] for off in offs]
        (_, to_down), (_, to_up) = own_edges(m)
        edges_arrived(to_down, to_up)

        @pl.when(last)
        def _():
            in_copy(cotangent, m).wait()
            argument_arrived(*input_parts(cotangent, m))
            sums = jnp.zeros((cols, ch), F32)
            cross = jnp.zeros((cols, ch), F32)
            for g in range(groups):
                z = zown[m, group(g), :].astype(F32)
                halved = z * slant + level[kind(g)]
                turn = jnp.tanh(halved)
                bent = halved * turn
                dy = inp[m, group(g), :].astype(F32) * ((0.5 + 0.5 * turn) * (1.0 + halved - bent))
                dyin[m, group(g), :] = dy.astype(BF16)
                if kind(g) == 1:
                    out_v[m, pl.ds((g - 1) * cols, cols), :] = (halved + bent).astype(BF16)
                    sums += dy
                    cross += dy * z
            one = jnp.sum(sums, 0, keepdims=True)
            seed_sums[m, pl.ds(0, 1), :] = one
            seed_sums[m, pl.ds(1, 1), :] = inv * (jnp.sum(cross, 0, keepdims=True) + offs[1] * one)
            start_stats(*seed_stats, m, sec, True)

        @pl.when(jnp.logical_not(last))
        def _():
            for g in range(1, groups - 1):
                halved = zown[m, group(g), :].astype(F32) * slant + level[1]
                out_v[m, pl.ds((g - 1) * cols, cols), :] = (halved + halved * jnp.tanh(halved)).astype(BF16)

        for copy in result_copies(out_v, outs, out_sem, po_s, po_r, m):
            copy.start()

    def result_copies(src, dst, sem, send, recv, m):
        here, there = pl.multiple_of(strip * core, cols), pl.multiple_of(strip * (1 - core), cols)
        return (
            pltpu.make_async_copy(src.at[m, pl.ds(here, strip), :], dst.at[m, core], sem.at[m]),
            remote(src.at[m, pl.ds(there, strip), :], dst.at[m, core], send.at[m], recv.at[m], sec, partner),
        )

    def backward(m):
        wait_stats(dy_stat, bs_r, m)
        first_sum = jnp.sum(dy_stat[m, :, 0, :], 0, keepdims=True)
        cross_sum = jnp.sum(dy_stat[m, :, 1, :], 0, keepdims=True)
        shift_sum[...] += first_sum
        gain_sum[...] += cross_sum
        inv = own_coef[m, pl.ds(0, 1), :]
        scale = own_coef[m, pl.ds(1, 1), :]
        tilt = scale * inv * (cross_sum / total)
        base = [scale * (first_sum / total) + tilt * own_coef[m, pl.ds(2 + k, 1), :] for k in range(3)]

        @pl.when(sec < sections - 1)
        def _():
            arrived(dy_sends(m, sec))

        for g in range(groups):
            dz = dyin[m, group(g), :].astype(F32) * scale - zown[m, group(g), :].astype(F32) * tilt - base[kind(g)]
            dzb[m, group(g), :] = inside(g, dz.astype(BF16))

        @pl.when(first)
        def _():
            send_dz(m)

        for h in range(2):
            part = pl.ds(h * half, half)
            parts = []
            for c in range(3):
                acc = jnp.zeros((px, half), F32)
                for r in range(3):
                    acc += jnp.dot(
                        dzb[m, pl.ds((2 - r) * cols, px), :], wt_v[r, pl.ds(c * ch, ch), part],
                        preferred_element_type=F32,
                    )
                parts.append(acc)
            gate = jnp.concatenate([mask_v[m, centre, :].astype(F32)] * (half // 128), axis=1)
            du = (taps_joined(parts, 2, 0) * gate).astype(BF16)
            gin_v[m, :, part] = du

            @pl.when(sec > 0)
            def _():
                dy = du.astype(F32) * slope_prev[m, :, part]
                dyout[m, :, part] = dy.astype(BF16)
                one = jnp.sum(dy, 0, keepdims=True)
                cross = jnp.sum(dy * zin[m, centre, part].astype(F32), 0, keepdims=True)
                sums_out[m, pl.ds(0, 1), part] = one
                sums_out[m, pl.ds(1, 1), part] = prev_coef[m, pl.ds(0, 1), part] * (
                    cross + prev_coef[m, pl.ds(1, 1), part] * one
                )
                if h == 1:
                    start_stats(*back_stats, m, sec - 1, False)
                each(dy_sends(m, sec - 1), h, start)

        for copy in result_copies(gin_v, grads_in, gin_sem, pg_s, pg_r, m):
            copy.start()

        @pl.when((sec > 0) & (sec < sections - 1))
        def _():
            send_dz(m)

    def turn_weights():
        def one(i, carry):
            at = pl.ds(pl.multiple_of(lax.rem(i, 3) * ch, ch), ch)
            wt_v[lax.div(i, 3), at, :] = w_v[lax.div(i, 3), at, :].T
            return carry
        lax.fori_loop(0, 9, one, 0)

    @pl.when(late)
    def _():
        for r in range(3):
            w_copy(r).wait()
        turn_weights()

    def step(t, carry):
        ahead = t - sec
        behind = t - (2 * sections - 1 - sec)

        @pl.when((ahead >= 0) & (ahead < batches))
        def _():
            forward(ahead)

        send_turned_third(ahead, 0)

        @pl.when(jnp.logical_not(late) & (ahead == batches))
        def _():
            def turned(m, carry):
                turn_inputs(m)
                turned_each(m, start)
                return carry
            lax.fori_loop(0, batches, turned, 0)
            turn_weights()

        done = ahead - jnp.where(last, 0, 1)

        @pl.when((behind >= 0) & (behind < batches))
        def _():
            backward(behind)

        send_turned_third(ahead, 1)

        @pl.when((done >= 0) & (done < batches))
        def _():
            finish(done)

        send_turned_third(ahead, 2)

        @pl.when(jnp.logical_not(late) & (ahead == batches + 1))
        def _():
            def relay(m, carry):
                relay_turned(m)
                return carry
            lax.fori_loop(0, batches, relay, 0)

        @pl.when((behind >= 1) & (behind < batches) & jnp.logical_not(late))
        def _():
            add_gradients(behind - 1)

        return carry

    lax.fori_loop(0, 2 * sections - 1 + batches, step, 0)

    @pl.when(last)
    def _():
        def send(m, carry):
            send_dz(m)
            return carry

        lax.fori_loop(0, batches, send, 0)

    @pl.when(late)
    def _():
        def relay(m, carry):
            relay_turned(m)
            return carry

        def add(m, carry):
            add_gradients(m)
            return carry

        lax.fori_loop(0, batches, relay, 0)
        lax.fori_loop(0, batches - 1, add, 0)

    def swap(r, d):
        other = (seat + d) % 4
        return remote(
            swap_out.at[r, pl.ds(pl.multiple_of(other * share, share), share), :], swap_in.at[r, 4 - d - 1],
            sw_s.at[r, d - 1], sw_r.at[r, 4 - d - 1], sec, 4 * team + other,
        )

    gather_taps(batches - 1)
    for r in range(3):
        part = acc_v[r] + kernel_row(batches - 1, r)
        acc_v[r] = part
        swap_out[r] = part.astype(BF16)
        for d in range(1, 4):
            swap(r, d).start()

    def dw_copy(r):
        return pltpu.make_async_copy(dw_v.at[r], weight_grad.at[r], dw_sem.at[r])

    own_rows = pl.ds(pl.multiple_of(seat * share, share), share)
    for r in range(3):
        for c in range(3):
            dw_v[r, c, :, pl.ds(pl.multiple_of(seat * lanes, lanes), lanes)] = acc_v[r, own_rows, pl.ds(c * lanes, lanes)]
        for d in range(1, 4):
            swap(r, 4 - d).wait_recv()
            source = (seat + d) % 4
            for c in range(3):
                dw_v[r, c, :, pl.ds(pl.multiple_of(source * lanes, lanes), lanes)] = swap_in[
                    r, d - 1, :, pl.ds(c * lanes, lanes)
                ].astype(F32)
        dw_copy(r).start()

    for r in range(3):
        dw_copy(r).wait()
        for d in range(1, 4):
            swap(r, d).wait_send()

    @pl.when(decoder)
    def _():
        argument_sent(*mask_parts)

    @pl.when(sec < sections - 1)
    def _():
        for copy in affine_sends():
            copy.wait_send()

    def drain(m, carry):
        for src, dst, sems in ((out_v, outs, (out_sem, po_s, po_r)), (gin_v, grads_in, (gin_sem, pg_s, pg_r))):
            here, there = result_copies(src, dst, *sems, m)
            here.wait()
            there.wait_send()
            remote(
                src.at[m, pl.ds(0, strip), :], dst.at[m, 1 - core], sems[1].at[m], sems[2].at[m], sec, partner
            ).wait_recv()

        turned_each(m, sent)
        turned_relay(m).wait_send()
        dz_each(m, sent)

        @pl.when(first)
        def _():
            argument_sent(*input_parts(images, m))

        @pl.when(last)
        def _():
            argument_sent(*input_parts(cotangent, m))
            stats_each(*seed_stats, m, sec, True, sent)

        @pl.when(sec < sections - 1)
        def _():
            stats_each(*down_stats, m, sec + 1, False, sent)
            for h in range(2):
                each(z_sends(m, sec + 1), h, sent)

        stats_each(*same_stats, m, sec, True, sent)
        for h in range(2):
            each(own_edges(m), h, sent)

        @pl.when(sec > 0)
        def _():
            stats_each(*back_stats, m, sec - 1, False, sent)
            for h in range(2):
                each(dy_sends(m, sec - 1), h, sent)

        return carry

    lax.fori_loop(0, batches, drain, 0)


def settle(*refs):
    count = (len(refs) - 2) // 3
    sources, targets, stages = refs[:count], refs[count : 2 * count], refs[2 * count : 3 * count]
    moves = []
    for src, dst, stage in zip(sources, targets, stages):
        if len(src.shape) == 2:
            moves.append((src, dst, stage))
        else:
            moves += [(src.at[i], dst.at[i], stage.at[i]) for i in range(src.shape[0])]
    ins = [pltpu.make_async_copy(src, stage, refs[-2].at[i]) for i, (src, dst, stage) in enumerate(moves)]
    outs = [pltpu.make_async_copy(stage, dst, refs[-1].at[i]) for i, (src, dst, stage) in enumerate(moves)]
    for copy in ins:
        copy.start()
    for come, go in zip(ins, outs):
        come.wait()
        go.start()
    for copy in outs:
        copy.wait()


def body(images, switches, conv_weights, gains, shifts, cotangent):
    sections = lax.axis_size("section")
    strips = lax.axis_size("rows")
    batches, pictures, strip_rows, cols, ch = images.shape
    strip = strip_rows * cols
    px = 2 * strip
    tall = px + 2 * cols
    anywhere = pl.BlockSpec(memory_space=pl.ANY)
    vmem = pl.BlockSpec(memory_space=pltpu.VMEM)
    dma = pltpu.SemaphoreType.DMA
    flops = 3 * 2 * 9 * ch * ch * batches * px
    share = ch // strips
    outs, grads_in, weight_grad, gain_sum, shift_sum = pl.pallas_call(
        functools.partial(kernel, sections, strips, cols),
        out_shape=(
            jax.ShapeDtypeStruct((batches, pictures, strip, ch), BF16),
            jax.ShapeDtypeStruct((batches, pictures, strip, ch), BF16),
            jax.ShapeDtypeStruct((3, 3, share, ch), F32),
            jax.ShapeDtypeStruct((1, ch), F32),
            jax.ShapeDtypeStruct((1, ch), F32),
        ),
        in_specs=[anywhere, anywhere, anywhere, vmem, vmem, vmem],
        out_specs=(anywhere, anywhere, anywhere, vmem, vmem),
        scratch_shapes=[
            pltpu.VMEM((3, 3 * ch, ch), BF16),
            pltpu.VMEM((3, 3 * ch, ch), BF16),
            pltpu.VMEM((batches, tall, ch), BF16),
            pltpu.VMEM((batches, 2, strip, 128), BF16),
            pltpu.VMEM((batches, tall, 128), BF16),
            pltpu.VMEM((1, ch), F32),
            pltpu.VMEM((1, ch), F32),
            pltpu.VMEM((batches, tall, ch), BF16),
            pltpu.VMEM((batches, strips, 2, ch), F32),
            pltpu.VMEM((batches, tall, ch), BF16),
            pltpu.VMEM((batches, strips, 2, ch), F32),
            pltpu.VMEM((batches, tall, ch), BF16),
            pltpu.VMEM((batches, px, ch), F32),
            pltpu.VMEM((batches, 2, ch), F32),
            pltpu.VMEM((batches, 8, ch), F32),
            pltpu.VMEM((batches, tall, ch), BF16),
            pltpu.VMEM((batches, strips, 2, ch), F32),
            pltpu.VMEM((batches, tall, ch), BF16),
            pltpu.VMEM((batches, px, ch), BF16),
            pltpu.VMEM((batches, 2, ch), F32),
            pltpu.VMEM((batches, 2, ch), F32),
            pltpu.VMEM((batches, 2, ch), F32),
            pltpu.VMEM((batches, px, ch), BF16),
            pltpu.VMEM((batches, px, ch), BF16),
            pltpu.VMEM((batches, ch, px), BF16),
            pltpu.VMEM((batches, 2, 4 * share, px * strips // 2), BF16),
            pltpu.VMEM((batches, 2, px * strips // 2 + 2 * cols, ch // 4), BF16),
            pltpu.VMEM((2, px * strips // 2 + 2 * cols, 3 * ch // 4), BF16),
            pltpu.VMEM((3, 4 * share, 3 * ch // 4), F32),
            pltpu.VMEM((3, 4 * share, 3 * ch // 4), BF16),
            pltpu.VMEM((3, 3, share, 3 * ch // 4), BF16),
            pltpu.VMEM((3, 3, share, ch), F32),
            dma((3,)),
            dma((batches,)),
            dma((batches,)), dma((batches,)),
            dma((batches, 2)), dma((batches, 2)),
            dma, dma,
            dma((2,)), dma((2,)),
            dma((2,)), dma((2,)),
            dma((batches, 3, 2)), dma((batches, 3, 2)),
            dma((batches, strips)), dma((batches,)),
            dma((batches, 3, 2)), dma((batches, 3, 2)),
            dma((batches, strips)), dma((batches,)),
            dma((batches, 3, 2)), dma((batches, 3, 2)),
            dma((batches, strips)), dma((batches,)),
            dma((batches, strips)),
            dma((batches,)), dma((batches,)), dma((batches,)),
            dma((batches,)), dma((batches,)), dma((batches,)),
            dma((batches, strips // 2)), dma((batches, strips // 2)),
            dma((batches,)), dma((batches,)),
            dma((batches, strips)), dma((batches, strips)),
            dma((3, 3)), dma((3, 3)),
            dma((3,)),
        ],
        compiler_params=pltpu.CompilerParams(
            collective_id=0, has_side_effects=True, vmem_limit_bytes=56 * 2**20
        ),
        cost_estimate=pl.CostEstimate(
            flops=flops, bytes_accessed=2 * 9 * ch * ch * 2, transcendentals=0
        ),
    )(
        images.reshape(batches, pictures, strip, ch),
        cotangent.reshape(batches, pictures, strip, ch),
        conv_weights.reshape(3, 3 * ch, ch),
        gains,
        shifts,
        switches.reshape(-1, switches.shape[-1]),
    )
    results = (outs, grads_in, weight_grad, gain_sum, shift_sum)
    outs, grads_in, weight_grad, gain_sum, shift_sum = pl.pallas_call(
        settle,
        out_shape=tuple(jax.ShapeDtypeStruct(r.shape, r.dtype) for r in results),
        in_specs=[anywhere] * 5,
        out_specs=(anywhere,) * 5,
        scratch_shapes=[pltpu.VMEM(r.shape, r.dtype) for r in results] + [dma((2 * batches + 5,))] * 2,
        compiler_params=pltpu.CompilerParams(vmem_limit_bytes=60 * 2**20),
    )(*results)
    shape = (1, batches, pictures, strip_rows, cols, ch)
    return (outs.reshape(shape), grads_in.reshape(shape), weight_grad[None], gain_sum, shift_sum)


def solution(mesh):
    return jax.shard_map(
        body,
        mesh=mesh,
        in_specs=(
            P(None, None, "rows", None, None),
            P(None, None, "rows", None),
            P("section", None, None, None, None),
            P("section", None),
            P("section", None),
            P(None, None, "rows", None, None),
        ),
        out_specs=(
            P("section", None, None, "rows", None, None),
            P("section", None, None, "rows", None, None),
            P("section", None, None, "rows", None),
            P("section", None),
            P("section", None),
        ),
        check_vma=False,
    )
```

```python
import functools

import jax
import jax.numpy as jnp
from jax import lax
from jax.experimental import pallas as pl
from jax.experimental.pallas import tpu as pltpu
from jax.sharding import PartitionSpec as P

EPSILON = 1e-05
MESH = pl.DeviceIdType.MESH
BF16 = jnp.bfloat16
F32 = jnp.float32


def kernel(
    sections, strips, cols,
    images, cotangent, weights, gains, shifts, switches,
    outs, grads_in, weight_grad, gain_sum, shift_sum,
    w_v, wt_v, inp, mask_own, mask_v, gain_prev, shift_prev, zin, zin_stat, zown, own_stat, ub, slope_prev,
    prev_coef, own_coef, dyin, dy_stat, dzb, dz_out, dyout, stat_out, sums_out, seed_sums, out_v, gin_v,
    ut_own, ut_all, dz_all, dz_taps, acc_v, swap_out, swap_in, dw_v,
    w_sem, in_sem, pi_s, pi_r, ie_s, ie_r, mp_s, mp_r, me_s, me_r, gp_s, gp_r,
    fz_s, fz_r, fs_s, fs_r, oe_s, oe_r, os_s, os_r, bz_s, bz_r, bs_s, bs_r, ls_s,
    out_sem, po_s, po_r, gin_sem, pg_s, pg_r,
    ut_s, ut_r, uf_s, uf_r, dz_s, dz_r, sw_s, sw_r, dw_sem,
):
    sec = lax.axis_index("section")
    row = lax.axis_index("rows")
    batches, tall, ch = inp.shape
    px = tall - 2 * cols
    strip = px // 2
    groups = tall // cols
    half = ch // 2
    total = float(px * strips)
    local = float(px)
    first, last, decoder = sec == 0, sec == sections - 1, sec == sections // 2
    late = sec >= sections // 2
    core = row % 2
    partner = row + 1 - 2 * core
    has_up, has_down = row >= 2, row < strips - 2
    centre = pl.ds(cols, px)
    chip = row // 2
    team, seat = row // 4, row % 4
    lanes = dz_all.shape[3]
    block = ut_all.shape[3]
    share = block // 4
    mine = pl.multiple_of(cols + strip * core, cols)

    def w_copy(r):
        return pltpu.make_async_copy(weights.at[r], w_v.at[r], w_sem.at[r])

    def in_copy(src, m):
        return pltpu.make_async_copy(src.at[m, core], inp.at[m, pl.ds(mine, strip), :], in_sem.at[m])

    for r in range(3):
        w_copy(r).start()

    @pl.when(first)
    def _():
        for m in range(batches):
            in_copy(images, m).start()

    @pl.when(last)
    def _():
        for m in range(batches):
            in_copy(cotangent, m).start()

    barrier = pltpu.get_barrier_semaphore()
    for s in range(sections):
        @pl.when((sec >= s - 1) & (sec <= s + 1))
        def _():
            def greet(i, carry):
                @pl.when((s != sec) | (i != row))
                def _():
                    pl.semaphore_signal(barrier, inc=1, device_id=(jnp.int32(s), i), device_id_type=MESH)
                return carry
            lax.fori_loop(0, strips, greet, 0)

    acc_v[...] = jnp.zeros_like(acc_v)
    gain_sum[...] = jnp.zeros_like(gain_sum)
    shift_sum[...] = jnp.zeros_like(shift_sum)

    for m in range(batches):
        for i in range(2):
            for at in (0, dz_all.shape[2] - cols):
                dz_all[m, i, pl.ds(at, cols), :] = jnp.zeros((cols, lanes), BF16)

    @pl.when(decoder)
    def _():
        wide = cols // 2
        windows_at = lax.broadcasted_iota(jnp.int32, (cols, wide), 1)
        places = lax.broadcasted_iota(jnp.int32, (cols, wide), 0)
        pick = (lax.shift_right_logical(places, 1) == windows_at).astype(F32)
        table = lax.dot_general(
            pick, switches[...].astype(F32), (((1,), (1,)), ((), ())), preferred_element_type=F32
        )
        odd = jnp.bitwise_and(lax.broadcasted_iota(jnp.int32, (cols, 128), 0), 1).astype(F32)
        windows = strip // cols // 2
        for m in range(batches):
            for i in range(2):
                for w in range(windows):
                    at = (m * 2 + i) * windows + w
                    value = jnp.broadcast_to(table[:, at : at + 1], (cols, 128))
                    for p in range(2):
                        hit = (jnp.abs(value - (2.0 * p + odd)) < 0.5).astype(F32).astype(BF16)
                        mask_own[m, i, pl.ds((2 * w + p) * cols, cols), :] = hit
        for m in range(batches):
            mask_v[m, pl.ds(mine, strip), :] = mask_own[m, core]

    @pl.when(jnp.logical_not(decoder))
    def _():
        mask_v[...] = jnp.ones_like(mask_v)

    near = 1 + jnp.where(sec > 0, 1, 0) + jnp.where(sec < sections - 1, 1, 0)
    pl.semaphore_wait(barrier, near * strips - 1)

    def remote(src, dst, send, recv, s, i):
        return pltpu.make_async_remote_copy(
            src_ref=src, dst_ref=dst, send_sem=send, recv_sem=recv, device_id=(s, i), device_id_type=MESH
        )

    def to_partner(src_at, dst_at, send, recv):
        return remote(src_at(1 - core), dst_at(pl.ds(mine, strip)), send, recv, sec, partner)

    def start_argument(src_at, dst_at, pair_sems, edge_sems):
        to_partner(src_at, dst_at, *pair_sems).start()

        @pl.when((core == 1) & has_down)
        def _():
            for i in range(2):
                remote(
                    src_at(i, pl.ds(strip - cols, cols)), dst_at(pl.ds(0, cols)),
                    edge_sems[0].at[i], edge_sems[1].at[0], sec, row + 1 + i,
                ).start()

        @pl.when((core == 0) & has_up)
        def _():
            for i in range(2):
                remote(
                    src_at(i, pl.ds(0, cols)), dst_at(pl.ds(cols + px, cols)),
                    edge_sems[0].at[i], edge_sems[1].at[1], sec, row - 2 + i,
                ).start()

    def argument_arrived(src_at, dst_at, pair_sems, edge_sems):
        to_partner(src_at, dst_at, *pair_sems).wait_recv()

        @pl.when(has_up)
        def _():
            remote(
                src_at(0, pl.ds(0, cols)), dst_at(pl.ds(0, cols)), edge_sems[0].at[0], edge_sems[1].at[0], sec, row
            ).wait_recv()

        @pl.when(has_down)
        def _():
            remote(
                src_at(0, pl.ds(0, cols)), dst_at(pl.ds(cols + px, cols)), edge_sems[0].at[0], edge_sems[1].at[1],
                sec, row,
            ).wait_recv()

    def argument_sent(src_at, dst_at, pair_sems, edge_sems):
        to_partner(src_at, dst_at, *pair_sems).wait_send()

        @pl.when(((core == 1) & has_down) | ((core == 0) & has_up))
        def _():
            for i in range(2):
                remote(
                    src_at(i, pl.ds(0, cols)), dst_at(pl.ds(0, cols)), edge_sems[0].at[i], edge_sems[1].at[0], sec, row
                ).wait_send()

    def input_parts(src, m):
        return (
            lambda i, r=pl.ds(0, strip): src.at[m, i, r, :],
            lambda r: inp.at[m, r, :],
            (pi_s.at[m], pi_r.at[m]),
            (ie_s.at[m], ie_r.at[m]),
        )

    mask_parts = (
        lambda i, r=pl.ds(0, strip): mask_own.at[:, i, r, :],
        lambda r: mask_v.at[:, r, :],
        (mp_s, mp_r),
        (me_s, me_r),
    )

    @pl.when(first)
    def _():
        for m in range(batches):
            start_argument(*input_parts(images, m))

    @pl.when(last)
    def _():
        for m in range(batches):
            start_argument(*input_parts(cotangent, m))

    @pl.when(decoder)
    def _():
        start_argument(*mask_parts)

    def affine_sends():
        return (
            remote(gains, gain_prev, gp_s.at[0], gp_r.at[0], sec + 1, row),
            remote(shifts, shift_prev, gp_s.at[1], gp_r.at[1], sec + 1, row),
        )

    @pl.when(sec < sections - 1)
    def _():
        for copy in affine_sends():
            copy.start()

    def block_sends(src, src_from, dst, send, recv, m, s):
        def one(k, h, src_row, dst_row, rows, i):
            return remote(
                src.at[m, h, pl.ds(src_from + src_row, rows), :], dst.at[m, h, pl.ds(dst_row, rows), :],
                send.at[m, k, h], recv.at[m, k, h], s, i,
            )
        return (
            (None, lambda h: one(0, h, 0, cols, px, row)),
            (has_down, lambda h: one(1, h, px - cols, 0, cols, row + 2)),
            (has_up, lambda h: one(2, h, 0, cols + px, cols, row - 2)),
        )

    def each(parts, h, act):
        for cond, make in parts:
            if cond is None:
                act(make(h))
            else:
                @pl.when(cond)
                def _():
                    act(make(h))

    def arrived(parts):
        (_, body), (_, to_down), (_, to_up) = parts
        for h in range(2):
            body(h).wait_recv()
        edges_arrived(to_down, to_up)

    def edges_arrived(to_down, to_up):
        @pl.when(has_up)
        def _():
            for h in range(2):
                to_down(h).wait_recv()

        @pl.when(has_down)
        def _():
            for h in range(2):
                to_up(h).wait_recv()

    def start(copy):
        copy.start()

    def sent(copy):
        copy.wait_send()

    def came(copy):
        copy.wait_recv()

    def z_sends(m, s):
        return block_sends(zown, cols, zin, fz_s, fz_r, m, s)

    def own_edges(m):
        return block_sends(zown, cols, zown, oe_s, oe_r, m, sec)[1:]

    def dy_sends(m, s):
        return block_sends(dyout, 0, dyin, bz_s, bz_r, m, s)

    def stat_copy(src, dst, send, recv, m, s, i):
        return remote(src.at[m], dst.at[m, row], send.at[m, i], recv.at[m], s, i)

    def stats_each(src, dst, send, recv, m, s, same, act):
        def one(d, carry):
            i = row + d
            act(stat_copy(src, dst, send, recv, m, s, jnp.where(i >= strips, i - strips, i)))
            return carry
        lax.fori_loop(1 if same else 0, strips, one, 0)

    def start_stats(src, dst, send, recv, m, s, same):
        stats_each(src, dst, send, recv, m, s, same, start)
        if same:
            pltpu.make_async_copy(src.at[m], dst.at[m, row], recv.at[m]).start()

    def wait_stats(dst, recv, m):
        pltpu.make_async_copy(dst.at[m], dst.at[m], recv.at[m]).wait()

    down_stats = (stat_out, zin_stat, fs_s, fs_r)
    same_stats = (stat_out, own_stat, os_s, os_r)
    back_stats = (sums_out, dy_stat, bs_s, bs_r)
    seed_stats = (seed_sums, dy_stat, ls_s, bs_r)

    def join(stats_ref, m):
        means, squares = stats_ref[m, :, 0, :], stats_ref[m, :, 1, :]
        mean = jnp.sum(means, 0, keepdims=True) / float(strips)
        off = means - mean
        var = (jnp.sum(squares, 0, keepdims=True) + local * jnp.sum(off * off, 0, keepdims=True)) / total
        at = (jnp.maximum(row - 2, 0), row, jnp.minimum(row + 2, strips - 1))
        return lax.rsqrt(var + EPSILON), [stats_ref[m, i, pl.ds(0, 1), :] - mean for i in at]

    def kind(g):
        return 0 if g == 0 else 2 if g == groups - 1 else 1

    def inside(g, values):
        if kind(g) == 1:
            return values
        return jnp.where(has_up if kind(g) == 0 else has_down, values, jnp.zeros_like(values))

    def group(g):
        return pl.ds(g * cols, cols)

    column = lax.broadcasted_iota(jnp.int32, (1, cols, half), 1)

    def taps_joined(parts, left, right):
        def moved(values, by, edge):
            turned = pltpu.roll(values, by % px, 0).reshape(px // cols, cols, half)
            return jnp.where(column == edge, 0.0, turned).reshape(px, half)
        return parts[1] + moved(parts[left], 1, 0) + moved(parts[right], -1, cols - 1)

    def turned_copy(m, q):
        src = ut_own.at[m, pl.ds(pl.multiple_of((q // 2) * block, block), block), :]
        return src, ut_all.at[m, core, chip]

    chips = strips // 2
    thirds = [1 + (chips - 1) * i // 3 for i in range(4)]

    def turned_each(m, act, low=1, high=chips):
        def one(d, carry):
            q = chip + d
            q = jnp.where(q >= chips, q - chips, q)
            src, dst = turned_copy(m, q)
            act(remote(src, dst, ut_s.at[m, d], ut_r.at[m, d], sec, 2 * q + core))
            return carry
        lax.fori_loop(low, high, one, 0)

    def turn_inputs(m):
        ut_own[m] = ub[m, centre, :].T
        mine_at = pl.ds(pl.multiple_of(team * block, block), block)
        ut_all[m, core, chip] = ut_own[m, mine_at, :]

    def send_turned_third(m, i):
        @pl.when(late & (m >= 0) & (m < batches))
        def _():
            if i == 0:
                turn_inputs(m)
            turned_each(m, start, thirds[i], thirds[i + 1])

    def turned_relay(m):
        return remote(ut_all.at[m, core], ut_all.at[m, core], uf_s.at[m], uf_r.at[m], sec, partner)

    def relay_turned(m):
        turned_each(m, came)
        turned_relay(m).start()

    def dz_copy(m, i):
        src = dz_out.at[m, i % 4]
        dst = dz_all.at[m, core, pl.ds(pl.multiple_of(cols + chip * px, cols), px), :]
        return src, dst

    def dz_each(m, act):
        def one(d, carry):
            i = row + d
            i = jnp.where(i >= strips, i - strips, i)
            src, dst = dz_copy(m, i)
            act(remote(src, dst, dz_s.at[m, d], dz_r.at[m, d], sec, i))
            return carry
        lax.fori_loop(1, strips, one, 0)

    def send_dz(m):
        dz_each(m, start)
        dz_all[m, core, pl.ds(pl.multiple_of(cols + chip * px, cols), px), :] = dz_out[m, seat]

    def gather_taps(m):
        dz_each(m, came)
        relayed = ut_all.at[m, 1 - core]
        pltpu.make_async_copy(relayed, relayed, uf_r.at[m]).wait()
        rows = dz_all.shape[2]
        edge = lax.broadcasted_iota(jnp.int32, (1, cols, lanes), 1)
        for i in range(2):
            values = dz_all[m, i].astype(F32)
            for c, by, gone in ((0, rows - 1, cols - 1), (2, 1, 0)):
                turned = pltpu.roll(values, by, 0).reshape(rows // cols, cols, lanes)
                turned = jnp.where(edge == gone, 0.0, turned).reshape(rows, lanes)
                dz_taps[i, :, pl.ds(c * lanes, lanes)] = turned.astype(BF16)
            dz_taps[i, :, pl.ds(lanes, lanes)] = dz_all[m, i]

    def kernel_row(m, r):
        part = jnp.zeros((block, 3 * lanes), F32)
        for i in range(2):
            left = jnp.concatenate([ut_all[m, i, q] for q in range(chips)], axis=1)
            part += jnp.dot(
                left, dz_taps[i, pl.ds((2 - r) * cols, px * (strips // 2)), :], preferred_element_type=F32
            )
        return part

    def add_gradients(m):
        gather_taps(m)
        for r in range(3):
            acc_v[r] = acc_v[r] + kernel_row(m, r)

    def forward(m):
        @pl.when(first)
        def _():
            in_copy(images, m).wait()
            argument_arrived(*input_parts(images, m))
            for g in range(groups):
                ub[m, group(g), :] = inside(g, inp[m, group(g), :])

        @pl.when(sec > 0)
        def _():
            @pl.when(m == 0)
            def _():
                for copy in affine_sends():
                    copy.wait_recv()

                @pl.when(decoder)
                def _():
                    argument_arrived(*mask_parts)

            wait_stats(zin_stat, fs_r, m)
            inv, offs = join(zin_stat, m)
            prev_coef[m, pl.ds(0, 1), :] = inv
            prev_coef[m, pl.ds(1, 1), :] = offs[1]
            slant = 0.5 * inv * gain_prev[...]
            level = [slant * off + 0.5 * shift_prev[...] for off in offs]
            arrived(z_sends(m, sec))
            for g in range(groups):
                gate = jnp.concatenate([mask_v[m, group(g), :].astype(F32)] * (half // 128), axis=1)
                for h in range(2):
                    part = slice(h * half, (h + 1) * half)
                    halved = zin[m, h, group(g), :].astype(F32) * slant[:, part] + level[kind(g)][:, part]
                    turn = jnp.tanh(halved)
                    bent = halved * turn
                    ub[m, group(g), part] = inside(g, ((halved + bent) * gate).astype(BF16))
                    if kind(g) == 1:
                        slope_prev[m, pl.ds((g - 1) * cols, cols), part] = (0.5 + 0.5 * turn) * (1.0 + halved - bent)

        @pl.when(jnp.logical_not(late) & (m == 0))
        def _():
            for r in range(3):
                w_copy(r).wait()

        for h in range(2):
            part = pl.ds(h * half, half)
            parts = []
            for c in range(3):
                acc = jnp.zeros((px, half), F32)
                for r in range(3):
                    acc += jnp.dot(
                        ub[m, pl.ds(r * cols, px), :], w_v[r, pl.ds(c * ch, ch), part], preferred_element_type=F32
                    )
                parts.append(acc)
            conv = taps_joined(parts, 0, 2)
            mean = jnp.sum(conv, 0, keepdims=True) / local
            conv = conv - mean
            stat_out[m, pl.ds(0, 1), part] = mean
            stat_out[m, pl.ds(1, 1), part] = jnp.sum(conv * conv, 0, keepdims=True)
            zown[m, h, centre, :] = conv.astype(BF16)

            @pl.when(sec < sections - 1)
            def _():
                if h == 1:
                    start_stats(*down_stats, m, sec + 1, False)
                each(z_sends(m, sec + 1), h, start)

        start_stats(*same_stats, m, sec, True)
        for h in range(2):
            each(own_edges(m), h, start)

    def finish(m):
        wait_stats(own_stat, os_r, m)
        inv, offs = join(own_stat, m)
        scale = inv * gains[...]
        own_coef[m, pl.ds(0, 1), :] = inv
        own_coef[m, pl.ds(1, 1), :] = scale
        for k in range(3):
            own_coef[m, pl.ds(2 + k, 1), :] = offs[k]
        slant = 0.5 * scale
        level = [slant * off + 0.5 * shifts[...] for off in offs]
        (_, to_down), (_, to_up) = own_edges(m)
        edges_arrived(to_down, to_up)

        @pl.when(last)
        def _():
            in_copy(cotangent, m).wait()
            argument_arrived(*input_parts(cotangent, m))
            for h in range(2):
                part = slice(h * half, (h + 1) * half)
                sums = jnp.zeros((cols, half), F32)
                cross = jnp.zeros((cols, half), F32)
                for g in range(groups):
                    z = zown[m, h, group(g), :].astype(F32)
                    halved = z * slant[:, part] + level[kind(g)][:, part]
                    turn = jnp.tanh(halved)
                    bent = halved * turn
                    dy = inp[m, group(g), part].astype(F32) * ((0.5 + 0.5 * turn) * (1.0 + halved - bent))
                    dyin[m, h, group(g), :] = dy.astype(BF16)
                    if kind(g) == 1:
                        out_v[m, pl.ds((g - 1) * cols, cols), part] = (halved + bent).astype(BF16)
                        sums += dy
                        cross += dy * z
                one = jnp.sum(sums, 0, keepdims=True)
                cross = jnp.sum(cross, 0, keepdims=True)
                seed_sums[m, pl.ds(0, 1), part] = one
                seed_sums[m, pl.ds(1, 1), part] = inv[:, part] * (cross + offs[1][:, part] * one)
            start_stats(*seed_stats, m, sec, True)

        @pl.when(jnp.logical_not(last))
        def _():
            for h in range(2):
                part = slice(h * half, (h + 1) * half)
                for g in range(1, groups - 1):
                    halved = zown[m, h, group(g), :].astype(F32) * slant[:, part] + level[1][:, part]
                    out_v[m, pl.ds((g - 1) * cols, cols), part] = (halved + halved * jnp.tanh(halved)).astype(BF16)

        for copy in result_copies(out_v, outs, out_sem, po_s, po_r, m):
            copy.start()

    def result_copies(src, dst, sem, send, recv, m):
        here, there = pl.multiple_of(strip * core, cols), pl.multiple_of(strip * (1 - core), cols)
        return (
            pltpu.make_async_copy(src.at[m, pl.ds(here, strip), :], dst.at[m, core], sem.at[m]),
            remote(src.at[m, pl.ds(there, strip), :], dst.at[m, core], send.at[m], recv.at[m], sec, partner),
        )

    def backward(m):
        wait_stats(dy_stat, bs_r, m)
        first_sum = jnp.sum(dy_stat[m, :, 0, :], 0, keepdims=True)
        cross_sum = jnp.sum(dy_stat[m, :, 1, :], 0, keepdims=True)
        shift_sum[...] += first_sum
        gain_sum[...] += cross_sum
        inv = own_coef[m, pl.ds(0, 1), :]
        scale = own_coef[m, pl.ds(1, 1), :]
        tilt = scale * inv * (cross_sum / total)
        base = [scale * (first_sum / total) + tilt * own_coef[m, pl.ds(2 + k, 1), :] for k in range(3)]

        @pl.when(sec < sections - 1)
        def _():
            arrived(dy_sends(m, sec))

        for g in range(groups):
            for h in range(2):
                part = slice(h * half, (h + 1) * half)
                dz = dyin[m, h, group(g), :].astype(F32) * scale[:, part]
                dz = dz - zown[m, h, group(g), :].astype(F32) * tilt[:, part] - base[kind(g)][:, part]
                dz = inside(g, dz.astype(BF16))
                dzb[m, group(g), part] = dz
                if kind(g) == 1:
                    for k in range(half // lanes):
                        dz_out[m, h * (half // lanes) + k, pl.ds((g - 1) * cols, cols), :] = dz[
                            :, k * lanes : (k + 1) * lanes
                        ]

        @pl.when(first)
        def _():
            send_dz(m)

        for h in range(2):
            part = pl.ds(h * half, half)
            parts = []
            for c in range(3):
                acc = jnp.zeros((px, half), F32)
                for r in range(3):
                    acc += jnp.dot(
                        dzb[m, pl.ds((2 - r) * cols, px), :], wt_v[r, pl.ds(c * ch, ch), part],
                        preferred_element_type=F32,
                    )
                parts.append(acc)
            gate = jnp.concatenate([mask_v[m, centre, :].astype(F32)] * (half // 128), axis=1)
            du = (taps_joined(parts, 2, 0) * gate).astype(BF16)
            gin_v[m, :, part] = du

            @pl.when(sec > 0)
            def _():
                dy = du.astype(F32) * slope_prev[m, :, part]
                dyout[m, h] = dy.astype(BF16)
                one = jnp.sum(dy, 0, keepdims=True)
                cross = jnp.sum(dy * zin[m, h, centre, :].astype(F32), 0, keepdims=True)
                sums_out[m, pl.ds(0, 1), part] = one
                sums_out[m, pl.ds(1, 1), part] = prev_coef[m, pl.ds(0, 1), part] * (
                    cross + prev_coef[m, pl.ds(1, 1), part] * one
                )
                if h == 1:
                    start_stats(*back_stats, m, sec - 1, False)
                each(dy_sends(m, sec - 1), h, start)

        for copy in result_copies(gin_v, grads_in, gin_sem, pg_s, pg_r, m):
            copy.start()

        @pl.when((sec > 0) & (sec < sections - 1))
        def _():
            send_dz(m)

    def turn_weights():
        def one(i, carry):
            at = pl.ds(pl.multiple_of(lax.rem(i, 3) * ch, ch), ch)
            wt_v[lax.div(i, 3), at, :] = w_v[lax.div(i, 3), at, :].T
            return carry
        lax.fori_loop(0, 9, one, 0)

    @pl.when(late)
    def _():
        for r in range(3):
            w_copy(r).wait()
        turn_weights()

    def step(t, carry):
        ahead = t - sec
        behind = t - (2 * sections - 1 - sec)

        @pl.when((ahead >= 0) & (ahead < batches))
        def _():
            forward(ahead)

        send_turned_third(ahead, 0)

        @pl.when(jnp.logical_not(late) & (ahead == batches))
        def _():
            def turned(m, carry):
                turn_inputs(m)
                turned_each(m, start)
                return carry
            lax.fori_loop(0, batches, turned, 0)
            turn_weights()

        done = ahead - jnp.where(last, 0, 1)

        @pl.when((behind >= 0) & (behind < batches))
        def _():
            backward(behind)

        send_turned_third(ahead, 1)

        @pl.when((done >= 0) & (done < batches))
        def _():
            finish(done)

        send_turned_third(ahead, 2)

        @pl.when(jnp.logical_not(late) & (ahead == batches + 1))
        def _():
            def relay(m, carry):
                relay_turned(m)
                return carry
            lax.fori_loop(0, batches, relay, 0)

        @pl.when((behind >= 1) & (behind < batches) & jnp.logical_not(late))
        def _():
            add_gradients(behind - 1)

        return carry

    lax.fori_loop(0, 2 * sections - 1 + batches, step, 0)

    @pl.when(last)
    def _():
        def send(m, carry):
            send_dz(m)
            return carry

        lax.fori_loop(0, batches, send, 0)

    @pl.when(late)
    def _():
        def relay(m, carry):
            relay_turned(m)
            return carry

        def add(m, carry):
            add_gradients(m)
            return carry

        lax.fori_loop(0, batches, relay, 0)
        lax.fori_loop(0, batches - 1, add, 0)

    def swap(r, d):
        other = (seat + d) % 4
        return remote(
            swap_out.at[r, pl.ds(pl.multiple_of(other * share, share), share), :], swap_in.at[r, 4 - d - 1],
            sw_s.at[r, d - 1], sw_r.at[r, 4 - d - 1], sec, 4 * team + other,
        )

    gather_taps(batches - 1)
    for r in range(3):
        part = acc_v[r] + kernel_row(batches - 1, r)
        acc_v[r] = part
        swap_out[r] = part.astype(BF16)
        for d in range(1, 4):
            swap(r, d).start()

    def dw_copy(r):
        return pltpu.make_async_copy(dw_v.at[r], weight_grad.at[r], dw_sem.at[r])

    own_rows = pl.ds(pl.multiple_of(seat * share, share), share)
    for r in range(3):
        for c in range(3):
            dw_v[r, c, :, pl.ds(pl.multiple_of(seat * lanes, lanes), lanes)] = acc_v[r, own_rows, pl.ds(c * lanes, lanes)]
        for d in range(1, 4):
            swap(r, 4 - d).wait_recv()
            source = (seat + d) % 4
            for c in range(3):
                dw_v[r, c, :, pl.ds(pl.multiple_of(source * lanes, lanes), lanes)] = swap_in[
                    r, d - 1, :, pl.ds(c * lanes, lanes)
                ].astype(F32)
        dw_copy(r).start()

    for r in range(3):
        dw_copy(r).wait()
        for d in range(1, 4):
            swap(r, d).wait_send()

    @pl.when(decoder)
    def _():
        argument_sent(*mask_parts)

    @pl.when(sec < sections - 1)
    def _():
        for copy in affine_sends():
            copy.wait_send()

    def drain(m, carry):
        for src, dst, sems in ((out_v, outs, (out_sem, po_s, po_r)), (gin_v, grads_in, (gin_sem, pg_s, pg_r))):
            here, there = result_copies(src, dst, *sems, m)
            here.wait()
            there.wait_send()
            remote(
                src.at[m, pl.ds(0, strip), :], dst.at[m, 1 - core], sems[1].at[m], sems[2].at[m], sec, partner
            ).wait_recv()

        turned_each(m, sent)
        turned_relay(m).wait_send()
        dz_each(m, sent)

        @pl.when(first)
        def _():
            argument_sent(*input_parts(images, m))

        @pl.when(last)
        def _():
            argument_sent(*input_parts(cotangent, m))
            stats_each(*seed_stats, m, sec, True, sent)

        @pl.when(sec < sections - 1)
        def _():
            stats_each(*down_stats, m, sec + 1, False, sent)
            for h in range(2):
                each(z_sends(m, sec + 1), h, sent)

        stats_each(*same_stats, m, sec, True, sent)
        for h in range(2):
            each(own_edges(m), h, sent)

        @pl.when(sec > 0)
        def _():
            stats_each(*back_stats, m, sec - 1, False, sent)
            for h in range(2):
                each(dy_sends(m, sec - 1), h, sent)

        return carry

    lax.fori_loop(0, batches, drain, 0)


def settle(*refs):
    count = (len(refs) - 2) // 3
    sources, targets, stages = refs[:count], refs[count : 2 * count], refs[2 * count : 3 * count]
    moves = []
    for src, dst, stage in zip(sources, targets, stages):
        if len(src.shape) == 2:
            moves.append((src, dst, stage))
        else:
            moves += [(src.at[i], dst.at[i], stage.at[i]) for i in range(src.shape[0])]
    ins = [pltpu.make_async_copy(src, stage, refs[-2].at[i]) for i, (src, dst, stage) in enumerate(moves)]
    outs = [pltpu.make_async_copy(stage, dst, refs[-1].at[i]) for i, (src, dst, stage) in enumerate(moves)]
    for copy in ins:
        copy.start()
    for come, go in zip(ins, outs):
        come.wait()
        go.start()
    for copy in outs:
        copy.wait()


def body(images, switches, conv_weights, gains, shifts, cotangent):
    sections = lax.axis_size("section")
    strips = lax.axis_size("rows")
    batches, pictures, strip_rows, cols, ch = images.shape
    strip = strip_rows * cols
    px = 2 * strip
    tall = px + 2 * cols
    anywhere = pl.BlockSpec(memory_space=pl.ANY)
    vmem = pl.BlockSpec(memory_space=pltpu.VMEM)
    dma = pltpu.SemaphoreType.DMA
    flops = 3 * 2 * 9 * ch * ch * batches * px
    share = ch // strips
    outs, grads_in, weight_grad, gain_sum, shift_sum = pl.pallas_call(
        functools.partial(kernel, sections, strips, cols),
        out_shape=(
            jax.ShapeDtypeStruct((batches, pictures, strip, ch), BF16),
            jax.ShapeDtypeStruct((batches, pictures, strip, ch), BF16),
            jax.ShapeDtypeStruct((3, 3, share, ch), F32),
            jax.ShapeDtypeStruct((1, ch), F32),
            jax.ShapeDtypeStruct((1, ch), F32),
        ),
        in_specs=[anywhere, anywhere, anywhere, vmem, vmem, vmem],
        out_specs=(anywhere, anywhere, anywhere, vmem, vmem),
        scratch_shapes=[
            pltpu.VMEM((3, 3 * ch, ch), BF16),
            pltpu.VMEM((3, 3 * ch, ch), BF16),
            pltpu.VMEM((batches, tall, ch), BF16),
            pltpu.VMEM((batches, 2, strip, 128), BF16),
            pltpu.VMEM((batches, tall, 128), BF16),
            pltpu.VMEM((1, ch), F32),
            pltpu.VMEM((1, ch), F32),
            pltpu.VMEM((batches, 2, tall, ch // 2), BF16),
            pltpu.VMEM((batches, strips, 2, ch), F32),
            pltpu.VMEM((batches, 2, tall, ch // 2), BF16),
            pltpu.VMEM((batches, strips, 2, ch), F32),
            pltpu.VMEM((batches, tall, ch), BF16),
            pltpu.VMEM((batches, px, ch), F32),
            pltpu.VMEM((batches, 2, ch), F32),
            pltpu.VMEM((batches, 8, ch), F32),
            pltpu.VMEM((batches, 2, tall, ch // 2), BF16),
            pltpu.VMEM((batches, strips, 2, ch), F32),
            pltpu.VMEM((batches, tall, ch), BF16),
            pltpu.VMEM((batches, 4, px, ch // 4), BF16),
            pltpu.VMEM((batches, 2, px, ch // 2), BF16),
            pltpu.VMEM((batches, 2, ch), F32),
            pltpu.VMEM((batches, 2, ch), F32),
            pltpu.VMEM((batches, 2, ch), F32),
            pltpu.VMEM((batches, px, ch), BF16),
            pltpu.VMEM((batches, px, ch), BF16),
            pltpu.VMEM((batches, ch, px), BF16),
            pltpu.VMEM((batches, 2, strips // 2, 4 * share, px), BF16),
            pltpu.VMEM((batches, 2, px * strips // 2 + 2 * cols, ch // 4), BF16),
            pltpu.VMEM((2, px * strips // 2 + 2 * cols, 3 * ch // 4), BF16),
            pltpu.VMEM((3, 4 * share, 3 * ch // 4), F32),
            pltpu.VMEM((3, 4 * share, 3 * ch // 4), BF16),
            pltpu.VMEM((3, 3, share, 3 * ch // 4), BF16),
            pltpu.VMEM((3, 3, share, ch), F32),
            dma((3,)),
            dma((batches,)),
            dma((batches,)), dma((batches,)),
            dma((batches, 2)), dma((batches, 2)),
            dma, dma,
            dma((2,)), dma((2,)),
            dma((2,)), dma((2,)),
            dma((batches, 3, 2)), dma((batches, 3, 2)),
            dma((batches, strips)), dma((batches,)),
            dma((batches, 3, 2)), dma((batches, 3, 2)),
            dma((batches, strips)), dma((batches,)),
            dma((batches, 3, 2)), dma((batches, 3, 2)),
            dma((batches, strips)), dma((batches,)),
            dma((batches, strips)),
            dma((batches,)), dma((batches,)), dma((batches,)),
            dma((batches,)), dma((batches,)), dma((batches,)),
            dma((batches, strips // 2)), dma((batches, strips // 2)),
            dma((batches,)), dma((batches,)),
            dma((batches, strips)), dma((batches, strips)),
            dma((3, 3)), dma((3, 3)),
            dma((3,)),
        ],
        compiler_params=pltpu.CompilerParams(
            collective_id=0, has_side_effects=True, vmem_limit_bytes=56 * 2**20
        ),
        cost_estimate=pl.CostEstimate(
            flops=flops, bytes_accessed=2 * 9 * ch * ch * 2, transcendentals=0
        ),
    )(
        images.reshape(batches, pictures, strip, ch),
        cotangent.reshape(batches, pictures, strip, ch),
        conv_weights.reshape(3, 3 * ch, ch),
        gains,
        shifts,
        switches.reshape(-1, switches.shape[-1]),
    )
    results = (outs, grads_in, weight_grad, gain_sum, shift_sum)
    outs, grads_in, weight_grad, gain_sum, shift_sum = pl.pallas_call(
        settle,
        out_shape=tuple(jax.ShapeDtypeStruct(r.shape, r.dtype) for r in results),
        in_specs=[anywhere] * 5,
        out_specs=(anywhere,) * 5,
        scratch_shapes=[pltpu.VMEM(r.shape, r.dtype) for r in results] + [dma((2 * batches + 5,))] * 2,
        compiler_params=pltpu.CompilerParams(vmem_limit_bytes=60 * 2**20),
    )(*results)
    shape = (1, batches, pictures, strip_rows, cols, ch)
    return (outs.reshape(shape), grads_in.reshape(shape), weight_grad[None], gain_sum, shift_sum)


def solution(mesh):
    return jax.shard_map(
        body,
        mesh=mesh,
        in_specs=(
            P(None, None, "rows", None, None),
            P(None, None, "rows", None),
            P("section", None, None, None, None),
            P("section", None),
            P("section", None),
            P(None, None, "rows", None, None),
        ),
        out_specs=(
            P("section", None, None, "rows", None, None),
            P("section", None, None, "rows", None, None),
            P("section", None, None, "rows", None),
            P("section", None),
            P("section", None),
        ),
        check_vma=False,
    )
```

```python
import functools

import jax
import jax.numpy as jnp
from jax import lax
from jax.experimental import pallas as pl
from jax.experimental.pallas import tpu as pltpu
from jax.sharding import PartitionSpec as P

EPSILON = 1e-05
MESH = pl.DeviceIdType.MESH
BF16 = jnp.bfloat16
F32 = jnp.float32


def kernel(
    sections, strips, cols,
    images, cotangent, weights, gains, shifts, switches,
    outs, grads_in, own_part, part_1, part_2, part_3, gain_sum, shift_sum,
    w_v, wt_v, inp, mask_own, mask_v, gain_prev, shift_prev, zin, zin_stat, zown, own_stat, ub, slope_prev,
    prev_coef, own_coef, dyin, dy_stat, dzb, dz_out, dyout, stat_out, sums_out, seed_sums, out_v, gin_v,
    ut_own, ut_all, dz_all, dz_taps, acc_v, swap_out, own_v,
    w_sem, in_sem, pi_s, pi_r, ie_s, ie_r, mp_s, mp_r, me_s, me_r, gp_s, gp_r,
    fz_s, fz_r, fs_s, fs_r, oe_s, oe_r, os_s, os_r, bz_s, bz_r, bs_s, bs_r, ls_s,
    out_sem, po_s, po_r, gin_sem, pg_s, pg_r,
    ut_s, ut_r, uf_s, uf_r, dz_s, dz_r, dw_sem,
):
    sent_parts = (part_1, part_2, part_3)
    sec = lax.axis_index("section")
    row = lax.axis_index("rows")
    batches, tall, ch = inp.shape
    px = tall - 2 * cols
    strip = px // 2
    groups = tall // cols
    half = ch // 2
    total = float(px * strips)
    local = float(px)
    first, last, decoder = sec == 0, sec == sections - 1, sec == sections // 2
    late = sec >= sections // 2
    core = row % 2
    partner = row + 1 - 2 * core
    has_up, has_down = row >= 2, row < strips - 2
    centre = pl.ds(cols, px)
    chip = row // 2
    team, seat = row // 4, row % 4
    lanes = dz_all.shape[3]
    block = ut_all.shape[3]
    share = block // 4
    mine = pl.multiple_of(cols + strip * core, cols)

    def w_copy(r):
        return pltpu.make_async_copy(weights.at[r], w_v.at[r], w_sem.at[r])

    def in_copy(src, m):
        return pltpu.make_async_copy(src.at[m, core], inp.at[m, pl.ds(mine, strip), :], in_sem.at[m])

    for r in range(3):
        w_copy(r).start()

    @pl.when(first)
    def _():
        for m in range(batches):
            in_copy(images, m).start()

    @pl.when(last)
    def _():
        for m in range(batches):
            in_copy(cotangent, m).start()

    barrier = pltpu.get_barrier_semaphore()
    for s in range(sections):
        @pl.when((sec >= s - 1) & (sec <= s + 1))
        def _():
            def greet(i, carry):
                @pl.when((s != sec) | (i != row))
                def _():
                    pl.semaphore_signal(barrier, inc=1, device_id=(jnp.int32(s), i), device_id_type=MESH)
                return carry
            lax.fori_loop(0, strips, greet, 0)

    acc_v[...] = jnp.zeros_like(acc_v)
    gain_sum[...] = jnp.zeros_like(gain_sum)
    shift_sum[...] = jnp.zeros_like(shift_sum)

    for m in range(batches):
        for i in range(2):
            for at in (0, dz_all.shape[2] - cols):
                dz_all[m, i, pl.ds(at, cols), :] = jnp.zeros((cols, lanes), BF16)

    @pl.when(decoder)
    def _():
        wide = cols // 2
        windows_at = lax.broadcasted_iota(jnp.int32, (cols, wide), 1)
        places = lax.broadcasted_iota(jnp.int32, (cols, wide), 0)
        pick = (lax.shift_right_logical(places, 1) == windows_at).astype(F32)
        table = lax.dot_general(
            pick, switches[...].astype(F32), (((1,), (1,)), ((), ())), preferred_element_type=F32
        )
        odd = jnp.bitwise_and(lax.broadcasted_iota(jnp.int32, (cols, 128), 0), 1).astype(F32)
        windows = strip // cols // 2
        for m in range(batches):
            for i in range(2):
                for w in range(windows):
                    at = (m * 2 + i) * windows + w
                    value = jnp.broadcast_to(table[:, at : at + 1], (cols, 128))
                    for p in range(2):
                        hit = (jnp.abs(value - (2.0 * p + odd)) < 0.5).astype(F32).astype(BF16)
                        mask_own[m, i, pl.ds((2 * w + p) * cols, cols), :] = hit
        for m in range(batches):
            mask_v[m, pl.ds(mine, strip), :] = mask_own[m, core]

    @pl.when(jnp.logical_not(decoder))
    def _():
        mask_v[...] = jnp.ones_like(mask_v)

    near = 1 + jnp.where(sec > 0, 1, 0) + jnp.where(sec < sections - 1, 1, 0)
    pl.semaphore_wait(barrier, near * strips - 1)

    def remote(src, dst, send, recv, s, i):
        return pltpu.make_async_remote_copy(
            src_ref=src, dst_ref=dst, send_sem=send, recv_sem=recv, device_id=(s, i), device_id_type=MESH
        )

    def to_partner(src_at, dst_at, send, recv):
        return remote(src_at(1 - core), dst_at(pl.ds(mine, strip)), send, recv, sec, partner)

    def start_argument(src_at, dst_at, pair_sems, edge_sems):
        to_partner(src_at, dst_at, *pair_sems).start()

        @pl.when((core == 1) & has_down)
        def _():
            for i in range(2):
                remote(
                    src_at(i, pl.ds(strip - cols, cols)), dst_at(pl.ds(0, cols)),
                    edge_sems[0].at[i], edge_sems[1].at[0], sec, row + 1 + i,
                ).start()

        @pl.when((core == 0) & has_up)
        def _():
            for i in range(2):
                remote(
                    src_at(i, pl.ds(0, cols)), dst_at(pl.ds(cols + px, cols)),
                    edge_sems[0].at[i], edge_sems[1].at[1], sec, row - 2 + i,
                ).start()

    def argument_arrived(src_at, dst_at, pair_sems, edge_sems):
        to_partner(src_at, dst_at, *pair_sems).wait_recv()

        @pl.when(has_up)
        def _():
            remote(
                src_at(0, pl.ds(0, cols)), dst_at(pl.ds(0, cols)), edge_sems[0].at[0], edge_sems[1].at[0], sec, row
            ).wait_recv()

        @pl.when(has_down)
        def _():
            remote(
                src_at(0, pl.ds(0, cols)), dst_at(pl.ds(cols + px, cols)), edge_sems[0].at[0], edge_sems[1].at[1],
                sec, row,
            ).wait_recv()

    def argument_sent(src_at, dst_at, pair_sems, edge_sems):
        to_partner(src_at, dst_at, *pair_sems).wait_send()

        @pl.when(((core == 1) & has_down) | ((core == 0) & has_up))
        def _():
            for i in range(2):
                remote(
                    src_at(i, pl.ds(0, cols)), dst_at(pl.ds(0, cols)), edge_sems[0].at[i], edge_sems[1].at[0], sec, row
                ).wait_send()

    def input_parts(src, m):
        return (
            lambda i, r=pl.ds(0, strip): src.at[m, i, r, :],
            lambda r: inp.at[m, r, :],
            (pi_s.at[m], pi_r.at[m]),
            (ie_s.at[m], ie_r.at[m]),
        )

    mask_parts = (
        lambda i, r=pl.ds(0, strip): mask_own.at[:, i, r, :],
        lambda r: mask_v.at[:, r, :],
        (mp_s, mp_r),
        (me_s, me_r),
    )

    @pl.when(first)
    def _():
        for m in range(batches):
            start_argument(*input_parts(images, m))

    @pl.when(last)
    def _():
        for m in range(batches):
            start_argument(*input_parts(cotangent, m))

    @pl.when(decoder)
    def _():
        start_argument(*mask_parts)

    def affine_sends():
        return (
            remote(gains, gain_prev, gp_s.at[0], gp_r.at[0], sec + 1, row),
            remote(shifts, shift_prev, gp_s.at[1], gp_r.at[1], sec + 1, row),
        )

    @pl.when(sec < sections - 1)
    def _():
        for copy in affine_sends():
            copy.start()

    def block_sends(src, src_from, dst, send, recv, m, s):
        def one(k, h, src_row, dst_row, rows, i):
            return remote(
                src.at[m, h, pl.ds(src_from + src_row, rows), :], dst.at[m, h, pl.ds(dst_row, rows), :],
                send.at[m, k, h], recv.at[m, k, h], s, i,
            )
        return (
            (None, lambda h: one(0, h, 0, cols, px, row)),
            (has_down, lambda h: one(1, h, px - cols, 0, cols, row + 2)),
            (has_up, lambda h: one(2, h, 0, cols + px, cols, row - 2)),
        )

    def each(parts, h, act):
        for cond, make in parts:
            if cond is None:
                act(make(h))
            else:
                @pl.when(cond)
                def _():
                    act(make(h))

    def arrived(parts):
        (_, body), (_, to_down), (_, to_up) = parts
        for h in range(2):
            body(h).wait_recv()
        edges_arrived(to_down, to_up)

    def edges_arrived(to_down, to_up):
        @pl.when(has_up)
        def _():
            for h in range(2):
                to_down(h).wait_recv()

        @pl.when(has_down)
        def _():
            for h in range(2):
                to_up(h).wait_recv()

    def start(copy):
        copy.start()

    def sent(copy):
        copy.wait_send()

    def came(copy):
        copy.wait_recv()

    def z_sends(m, s):
        return block_sends(zown, cols, zin, fz_s, fz_r, m, s)

    def own_edges(m):
        return block_sends(zown, cols, zown, oe_s, oe_r, m, sec)[1:]

    def dy_sends(m, s):
        return block_sends(dyout, 0, dyin, bz_s, bz_r, m, s)

    def stat_copy(src, dst, send, recv, m, s, i):
        return remote(src.at[m], dst.at[m, row], send.at[m, i], recv.at[m], s, i)

    def stats_each(src, dst, send, recv, m, s, same, act):
        def one(d, carry):
            i = row + d
            act(stat_copy(src, dst, send, recv, m, s, jnp.where(i >= strips, i - strips, i)))
            return carry
        lax.fori_loop(1 if same else 0, strips, one, 0)

    def start_stats(src, dst, send, recv, m, s, same):
        stats_each(src, dst, send, recv, m, s, same, start)
        if same:
            pltpu.make_async_copy(src.at[m], dst.at[m, row], recv.at[m]).start()

    def wait_stats(dst, recv, m):
        pltpu.make_async_copy(dst.at[m], dst.at[m], recv.at[m]).wait()

    down_stats = (stat_out, zin_stat, fs_s, fs_r)
    same_stats = (stat_out, own_stat, os_s, os_r)
    back_stats = (sums_out, dy_stat, bs_s, bs_r)
    seed_stats = (seed_sums, dy_stat, ls_s, bs_r)

    def join(stats_ref, m):
        means, squares = stats_ref[m, :, 0, :], stats_ref[m, :, 1, :]
        mean = jnp.sum(means, 0, keepdims=True) / float(strips)
        off = means - mean
        var = (jnp.sum(squares, 0, keepdims=True) + local * jnp.sum(off * off, 0, keepdims=True)) / total
        at = (jnp.maximum(row - 2, 0), row, jnp.minimum(row + 2, strips - 1))
        return lax.rsqrt(var + EPSILON), [stats_ref[m, i, pl.ds(0, 1), :] - mean for i in at]

    def kind(g):
        return 0 if g == 0 else 2 if g == groups - 1 else 1

    def inside(g, values):
        if kind(g) == 1:
            return values
        return jnp.where(has_up if kind(g) == 0 else has_down, values, jnp.zeros_like(values))

    def group(g):
        return pl.ds(g * cols, cols)

    column = lax.broadcasted_iota(jnp.int32, (1, cols, half), 1)

    def taps_joined(parts, left, right):
        def moved(values, by, edge):
            turned = pltpu.roll(values, by % px, 0).reshape(px // cols, cols, half)
            return jnp.where(column == edge, 0.0, turned).reshape(px, half)
        return parts[1] + moved(parts[left], 1, 0) + moved(parts[right], -1, cols - 1)

    def turned_copy(m, q):
        src = ut_own.at[m, pl.ds(pl.multiple_of((q // 2) * block, block), block), :]
        return src, ut_all.at[m, core, chip]

    chips = strips // 2
    thirds = [1 + (chips - 1) * i // 3 for i in range(4)]

    def turned_each(m, act, low=1, high=chips):
        def one(d, carry):
            q = chip + d
            q = jnp.where(q >= chips, q - chips, q)
            src, dst = turned_copy(m, q)
            act(remote(src, dst, ut_s.at[m, d], ut_r.at[m, d], sec, 2 * q + core))
            return carry
        lax.fori_loop(low, high, one, 0)

    def turn_inputs(m):
        ut_own[m] = ub[m, centre, :].T
        mine_at = pl.ds(pl.multiple_of(team * block, block), block)
        ut_all[m, core, chip] = ut_own[m, mine_at, :]

    def send_turned_third(m, i):
        @pl.when(late & (m >= 0) & (m < batches))
        def _():
            if i == 0:
                turn_inputs(m)
            turned_each(m, start, thirds[i], thirds[i + 1])

    def turned_relay(m):
        return remote(ut_all.at[m, core], ut_all.at[m, core], uf_s.at[m], uf_r.at[m], sec, partner)

    def relay_turned(m):
        turned_each(m, came)
        turned_relay(m).start()

    def dz_copy(m, i):
        src = dz_out.at[m, i % 4]
        dst = dz_all.at[m, core, pl.ds(pl.multiple_of(cols + chip * px, cols), px), :]
        return src, dst

    def dz_each(m, act):
        def one(d, carry):
            i = row + d
            i = jnp.where(i >= strips, i - strips, i)
            src, dst = dz_copy(m, i)
            act(remote(src, dst, dz_s.at[m, d], dz_r.at[m, d], sec, i))
            return carry
        lax.fori_loop(1, strips, one, 0)

    def send_dz(m):
        dz_each(m, start)
        dz_all[m, core, pl.ds(pl.multiple_of(cols + chip * px, cols), px), :] = dz_out[m, seat]

    def gather_taps(m):
        dz_each(m, came)
        relayed = ut_all.at[m, 1 - core]
        pltpu.make_async_copy(relayed, relayed, uf_r.at[m]).wait()
        rows = dz_all.shape[2]
        edge = lax.broadcasted_iota(jnp.int32, (1, cols, lanes), 1)
        for i in range(2):
            values = dz_all[m, i].astype(F32)
            for c, by, gone in ((0, rows - 1, cols - 1), (2, 1, 0)):
                turned = pltpu.roll(values, by, 0).reshape(rows // cols, cols, lanes)
                turned = jnp.where(edge == gone, 0.0, turned).reshape(rows, lanes)
                dz_taps[i, :, pl.ds(c * lanes, lanes)] = turned.astype(BF16)
            dz_taps[i, :, pl.ds(lanes, lanes)] = dz_all[m, i]

    def kernel_row(m, r):
        part = jnp.zeros((block, 3 * lanes), F32)
        for i in range(2):
            left = jnp.concatenate([ut_all[m, i, q] for q in range(chips)], axis=1)
            part += jnp.dot(
                left, dz_taps[i, pl.ds((2 - r) * cols, px * (strips // 2)), :], preferred_element_type=F32
            )
        return part

    def add_gradients(m):
        gather_taps(m)
        for r in range(3):
            acc_v[r] = acc_v[r] + kernel_row(m, r)

    def forward(m):
        @pl.when(first)
        def _():
            in_copy(images, m).wait()
            argument_arrived(*input_parts(images, m))
            for g in range(groups):
                ub[m, group(g), :] = inside(g, inp[m, group(g), :])

        @pl.when(sec > 0)
        def _():
            @pl.when(m == 0)
            def _():
                for copy in affine_sends():
                    copy.wait_recv()

                @pl.when(decoder)
                def _():
                    argument_arrived(*mask_parts)

            wait_stats(zin_stat, fs_r, m)
            inv, offs = join(zin_stat, m)
            prev_coef[m, pl.ds(0, 1), :] = inv
            prev_coef[m, pl.ds(1, 1), :] = offs[1]
            slant = 0.5 * inv * gain_prev[...]
            level = [slant * off + 0.5 * shift_prev[...] for off in offs]
            arrived(z_sends(m, sec))
            for g in range(groups):
                gate = jnp.concatenate([mask_v[m, group(g), :].astype(F32)] * (half // 128), axis=1)
                for h in range(2):
                    part = slice(h * half, (h + 1) * half)
                    halved = zin[m, h, group(g), :].astype(F32) * slant[:, part] + level[kind(g)][:, part]
                    turn = jnp.tanh(halved)
                    bent = halved * turn
                    ub[m, group(g), part] = inside(g, ((halved + bent) * gate).astype(BF16))
                    if kind(g) == 1:
                        slope_prev[m, pl.ds((g - 1) * cols, cols), part] = (0.5 + 0.5 * turn) * (1.0 + halved - bent)

        @pl.when(jnp.logical_not(late) & (m == 0))
        def _():
            for r in range(3):
                w_copy(r).wait()

        for h in range(2):
            part = pl.ds(h * half, half)
            parts = []
            for c in range(3):
                acc = jnp.zeros((px, half), F32)
                for r in range(3):
                    acc += jnp.dot(
                        ub[m, pl.ds(r * cols, px), :], w_v[r, pl.ds(c * ch, ch), part], preferred_element_type=F32
                    )
                parts.append(acc)
            conv = taps_joined(parts, 0, 2)
            mean = jnp.sum(conv, 0, keepdims=True) / local
            conv = conv - mean
            stat_out[m, pl.ds(0, 1), part] = mean
            stat_out[m, pl.ds(1, 1), part] = jnp.sum(conv * conv, 0, keepdims=True)
            zown[m, h, centre, :] = conv.astype(BF16)

            @pl.when(sec < sections - 1)
            def _():
                if h == 1:
                    start_stats(*down_stats, m, sec + 1, False)
                each(z_sends(m, sec + 1), h, start)

        start_stats(*same_stats, m, sec, True)
        for h in range(2):
            each(own_edges(m), h, start)

    def finish(m):
        wait_stats(own_stat, os_r, m)
        inv, offs = join(own_stat, m)
        scale = inv * gains[...]
        own_coef[m, pl.ds(0, 1), :] = inv
        own_coef[m, pl.ds(1, 1), :] = scale
        for k in range(3):
            own_coef[m, pl.ds(2 + k, 1), :] = offs[k]
        slant = 0.5 * scale
        level = [slant * off + 0.5 * shifts[...] for off in offs]
        (_, to_down), (_, to_up) = own_edges(m)
        edges_arrived(to_down, to_up)

        @pl.when(last)
        def _():
            in_copy(cotangent, m).wait()
            argument_arrived(*input_parts(cotangent, m))
            for h in range(2):
                part = slice(h * half, (h + 1) * half)
                sums = jnp.zeros((cols, half), F32)
                cross = jnp.zeros((cols, half), F32)
                for g in range(groups):
                    z = zown[m, h, group(g), :].astype(F32)
                    halved = z * slant[:, part] + level[kind(g)][:, part]
                    turn = jnp.tanh(halved)
                    bent = halved * turn
                    dy = inp[m, group(g), part].astype(F32) * ((0.5 + 0.5 * turn) * (1.0 + halved - bent))
                    dyin[m, h, group(g), :] = dy.astype(BF16)
                    if kind(g) == 1:
                        out_v[m, pl.ds((g - 1) * cols, cols), part] = (halved + bent).astype(BF16)
                        sums += dy
                        cross += dy * z
                one = jnp.sum(sums, 0, keepdims=True)
                cross = jnp.sum(cross, 0, keepdims=True)
                seed_sums[m, pl.ds(0, 1), part] = one
                seed_sums[m, pl.ds(1, 1), part] = inv[:, part] * (cross + offs[1][:, part] * one)
            start_stats(*seed_stats, m, sec, True)

        @pl.when(jnp.logical_not(last))
        def _():
            for h in range(2):
                part = slice(h * half, (h + 1) * half)
                for g in range(1, groups - 1):
                    halved = zown[m, h, group(g), :].astype(F32) * slant[:, part] + level[1][:, part]
                    out_v[m, pl.ds((g - 1) * cols, cols), part] = (halved + halved * jnp.tanh(halved)).astype(BF16)

        for copy in result_copies(out_v, outs, out_sem, po_s, po_r, m):
            copy.start()

    def result_copies(src, dst, sem, send, recv, m):
        here, there = pl.multiple_of(strip * core, cols), pl.multiple_of(strip * (1 - core), cols)
        return (
            pltpu.make_async_copy(src.at[m, pl.ds(here, strip), :], dst.at[m, core], sem.at[m]),
            remote(src.at[m, pl.ds(there, strip), :], dst.at[m, core], send.at[m], recv.at[m], sec, partner),
        )

    def backward(m):
        wait_stats(dy_stat, bs_r, m)
        first_sum = jnp.sum(dy_stat[m, :, 0, :], 0, keepdims=True)
        cross_sum = jnp.sum(dy_stat[m, :, 1, :], 0, keepdims=True)
        shift_sum[...] += first_sum
        gain_sum[...] += cross_sum
        inv = own_coef[m, pl.ds(0, 1), :]
        scale = own_coef[m, pl.ds(1, 1), :]
        tilt = scale * inv * (cross_sum / total)
        base = [scale * (first_sum / total) + tilt * own_coef[m, pl.ds(2 + k, 1), :] for k in range(3)]

        @pl.when(sec < sections - 1)
        def _():
            arrived(dy_sends(m, sec))

        for g in range(groups):
            for h in range(2):
                part = slice(h * half, (h + 1) * half)
                dz = dyin[m, h, group(g), :].astype(F32) * scale[:, part]
                dz = dz - zown[m, h, group(g), :].astype(F32) * tilt[:, part] - base[kind(g)][:, part]
                dz = inside(g, dz.astype(BF16))
                dzb[m, group(g), part] = dz
                if kind(g) == 1:
                    for k in range(half // lanes):
                        dz_out[m, h * (half // lanes) + k, pl.ds((g - 1) * cols, cols), :] = dz[
                            :, k * lanes : (k + 1) * lanes
                        ]

        @pl.when(first)
        def _():
            send_dz(m)

        for h in range(2):
            part = pl.ds(h * half, half)
            parts = []
            for c in range(3):
                acc = jnp.zeros((px, half), F32)
                for r in range(3):
                    acc += jnp.dot(
                        dzb[m, pl.ds((2 - r) * cols, px), :], wt_v[r, pl.ds(c * ch, ch), part],
                        preferred_element_type=F32,
                    )
                parts.append(acc)
            gate = jnp.concatenate([mask_v[m, centre, :].astype(F32)] * (half // 128), axis=1)
            du = (taps_joined(parts, 2, 0) * gate).astype(BF16)
            gin_v[m, :, part] = du

            @pl.when(sec > 0)
            def _():
                dy = du.astype(F32) * slope_prev[m, :, part]
                dyout[m, h] = dy.astype(BF16)
                one = jnp.sum(dy, 0, keepdims=True)
                cross = jnp.sum(dy * zin[m, h, centre, :].astype(F32), 0, keepdims=True)
                sums_out[m, pl.ds(0, 1), part] = one
                sums_out[m, pl.ds(1, 1), part] = prev_coef[m, pl.ds(0, 1), part] * (
                    cross + prev_coef[m, pl.ds(1, 1), part] * one
                )
                if h == 1:
                    start_stats(*back_stats, m, sec - 1, False)
                each(dy_sends(m, sec - 1), h, start)

        for copy in result_copies(gin_v, grads_in, gin_sem, pg_s, pg_r, m):
            copy.start()

        @pl.when((sec > 0) & (sec < sections - 1))
        def _():
            send_dz(m)

    def turn_weights():
        def one(i, carry):
            at = pl.ds(pl.multiple_of(lax.rem(i, 3) * ch, ch), ch)
            wt_v[lax.div(i, 3), at, :] = w_v[lax.div(i, 3), at, :].T
            return carry
        lax.fori_loop(0, 9, one, 0)

    @pl.when(late)
    def _():
        for r in range(3):
            w_copy(r).wait()
        turn_weights()

    def step(t, carry):
        ahead = t - sec
        behind = t - (2 * sections - 1 - sec)

        @pl.when((ahead >= 0) & (ahead < batches))
        def _():
            forward(ahead)

        send_turned_third(ahead, 0)

        @pl.when(jnp.logical_not(late) & (ahead == batches))
        def _():
            def turned(m, carry):
                turn_inputs(m)
                turned_each(m, start)
                return carry
            lax.fori_loop(0, batches, turned, 0)
            turn_weights()

        done = ahead - jnp.where(last, 0, 1)

        @pl.when((behind >= 0) & (behind < batches))
        def _():
            backward(behind)

        send_turned_third(ahead, 1)

        @pl.when((done >= 0) & (done < batches))
        def _():
            finish(done)

        send_turned_third(ahead, 2)

        @pl.when(jnp.logical_not(late) & (ahead == batches + 1))
        def _():
            def relay(m, carry):
                relay_turned(m)
                return carry
            lax.fori_loop(0, batches, relay, 0)

        @pl.when((behind >= 1) & (behind < batches) & jnp.logical_not(late))
        def _():
            add_gradients(behind - 1)

        return carry

    lax.fori_loop(0, 2 * sections - 1 + batches, step, 0)

    @pl.when(last)
    def _():
        def send(m, carry):
            send_dz(m)
            return carry

        lax.fori_loop(0, batches, send, 0)

    @pl.when(late)
    def _():
        def relay(m, carry):
            relay_turned(m)
            return carry

        def add(m, carry):
            add_gradients(m)
            return carry

        lax.fori_loop(0, batches, relay, 0)
        lax.fori_loop(0, batches - 1, add, 0)

    gather_taps(batches - 1)
    for r in range(3):
        acc_v[r] = acc_v[r] + kernel_row(batches - 1, r)
        for d in range(4):
            rows = pl.ds(pl.multiple_of(((seat + d) % 4) * share, share), share)
            if d == 0:
                own_v[r] = acc_v[r, rows, :]
            else:
                swap_out[d - 1, r] = acc_v[r, rows, :].astype(BF16)

    def part_copies():
        return [pltpu.make_async_copy(own_v, own_part, dw_sem.at[0])] + [
            pltpu.make_async_copy(swap_out.at[d], ref, dw_sem.at[d + 1]) for d, ref in enumerate(sent_parts)
        ]

    for copy in part_copies():
        copy.start()

    for copy in part_copies():
        copy.wait()

    @pl.when(decoder)
    def _():
        argument_sent(*mask_parts)

    @pl.when(sec < sections - 1)
    def _():
        for copy in affine_sends():
            copy.wait_send()

    def drain(m, carry):
        for src, dst, sems in ((out_v, outs, (out_sem, po_s, po_r)), (gin_v, grads_in, (gin_sem, pg_s, pg_r))):
            here, there = result_copies(src, dst, *sems, m)
            here.wait()
            there.wait_send()
            remote(
                src.at[m, pl.ds(0, strip), :], dst.at[m, 1 - core], sems[1].at[m], sems[2].at[m], sec, partner
            ).wait_recv()

        turned_each(m, sent)
        turned_relay(m).wait_send()
        dz_each(m, sent)

        @pl.when(first)
        def _():
            argument_sent(*input_parts(images, m))

        @pl.when(last)
        def _():
            argument_sent(*input_parts(cotangent, m))
            stats_each(*seed_stats, m, sec, True, sent)

        @pl.when(sec < sections - 1)
        def _():
            stats_each(*down_stats, m, sec + 1, False, sent)
            for h in range(2):
                each(z_sends(m, sec + 1), h, sent)

        stats_each(*same_stats, m, sec, True, sent)
        for h in range(2):
            each(own_edges(m), h, sent)

        @pl.when(sec > 0)
        def _():
            stats_each(*back_stats, m, sec - 1, False, sent)
            for h in range(2):
                each(dy_sends(m, sec - 1), h, sent)

        return carry

    lax.fori_loop(0, batches, drain, 0)


def settle(outs, grads_in, gain_sum, shift_sum, own, part_1, part_2, part_3, *refs):
    targets, stages, (quarters, others, whole, in_sem, out_sem) = refs[:5], refs[5:9], refs[9:]
    moves = []
    for src, dst, stage in zip((outs, grads_in, gain_sum, shift_sum), targets[:4], stages):
        if len(src.shape) == 2:
            moves.append((src, dst, stage))
        else:
            moves += [(src.at[i], dst.at[i], stage.at[i]) for i in range(src.shape[0])]
    count = len(moves)
    pieces = [(own, quarters)] + [(ref, others.at[d]) for d, ref in enumerate((part_1, part_2, part_3))]
    parts = [pltpu.make_async_copy(src, dst, in_sem.at[count + i]) for i, (src, dst) in enumerate(pieces)]
    ins = [pltpu.make_async_copy(src, stage, in_sem.at[i]) for i, (src, dst, stage) in enumerate(moves)]
    outs = [pltpu.make_async_copy(stage, dst, out_sem.at[i]) for i, (src, dst, stage) in enumerate(moves)]
    outs.append(pltpu.make_async_copy(whole, targets[4], out_sem.at[count]))
    for copy in parts + ins:
        copy.start()
    for copy in parts:
        copy.wait()
    seat = lax.axis_index("rows") % 4
    lanes = whole.shape[3] // 4
    for d in range(4):
        at = pl.ds(pl.multiple_of(((seat + d) % 4) * lanes, lanes), lanes)
        for r in range(3):
            for c in range(3):
                part = pl.ds(c * lanes, lanes)
                whole[r, c, :, at] = quarters[r, :, part] if d == 0 else others[3 - d, r, :, part].astype(F32)
    outs[count].start()
    for come, go in zip(ins, outs):
        come.wait()
        go.start()
    for copy in outs:
        copy.wait()


def body(images, switches, conv_weights, gains, shifts, cotangent):
    sections = lax.axis_size("section")
    strips = lax.axis_size("rows")
    batches, pictures, strip_rows, cols, ch = images.shape
    strip = strip_rows * cols
    px = 2 * strip
    tall = px + 2 * cols
    anywhere = pl.BlockSpec(memory_space=pl.ANY)
    vmem = pl.BlockSpec(memory_space=pltpu.VMEM)
    dma = pltpu.SemaphoreType.DMA
    flops = 3 * 2 * 9 * ch * ch * batches * px
    share = ch // strips
    outs, grads_in, own, part_1, part_2, part_3, gain_sum, shift_sum = pl.pallas_call(
        functools.partial(kernel, sections, strips, cols),
        out_shape=(
            jax.ShapeDtypeStruct((batches, pictures, strip, ch), BF16),
            jax.ShapeDtypeStruct((batches, pictures, strip, ch), BF16),
            jax.ShapeDtypeStruct((3, share, 3 * ch // 4), F32),
            jax.ShapeDtypeStruct((3, share, 3 * ch // 4), BF16),
            jax.ShapeDtypeStruct((3, share, 3 * ch // 4), BF16),
            jax.ShapeDtypeStruct((3, share, 3 * ch // 4), BF16),
            jax.ShapeDtypeStruct((1, ch), F32),
            jax.ShapeDtypeStruct((1, ch), F32),
        ),
        in_specs=[anywhere, anywhere, anywhere, vmem, vmem, vmem],
        out_specs=(anywhere,) * 6 + (vmem, vmem),
        scratch_shapes=[
            pltpu.VMEM((3, 3 * ch, ch), BF16),
            pltpu.VMEM((3, 3 * ch, ch), BF16),
            pltpu.VMEM((batches, tall, ch), BF16),
            pltpu.VMEM((batches, 2, strip, 128), BF16),
            pltpu.VMEM((batches, tall, 128), BF16),
            pltpu.VMEM((1, ch), F32),
            pltpu.VMEM((1, ch), F32),
            pltpu.VMEM((batches, 2, tall, ch // 2), BF16),
            pltpu.VMEM((batches, strips, 2, ch), F32),
            pltpu.VMEM((batches, 2, tall, ch // 2), BF16),
            pltpu.VMEM((batches, strips, 2, ch), F32),
            pltpu.VMEM((batches, tall, ch), BF16),
            pltpu.VMEM((batches, px, ch), F32),
            pltpu.VMEM((batches, 2, ch), F32),
            pltpu.VMEM((batches, 8, ch), F32),
            pltpu.VMEM((batches, 2, tall, ch // 2), BF16),
            pltpu.VMEM((batches, strips, 2, ch), F32),
            pltpu.VMEM((batches, tall, ch), BF16),
            pltpu.VMEM((batches, 4, px, ch // 4), BF16),
            pltpu.VMEM((batches, 2, px, ch // 2), BF16),
            pltpu.VMEM((batches, 2, ch), F32),
            pltpu.VMEM((batches, 2, ch), F32),
            pltpu.VMEM((batches, 2, ch), F32),
            pltpu.VMEM((batches, px, ch), BF16),
            pltpu.VMEM((batches, px, ch), BF16),
            pltpu.VMEM((batches, ch, px), BF16),
            pltpu.VMEM((batches, 2, strips // 2, 4 * share, px), BF16),
            pltpu.VMEM((batches, 2, px * strips // 2 + 2 * cols, ch // 4), BF16),
            pltpu.VMEM((2, px * strips // 2 + 2 * cols, 3 * ch // 4), BF16),
            pltpu.VMEM((3, 4 * share, 3 * ch // 4), F32),
            pltpu.VMEM((3, 3, share, 3 * ch // 4), BF16),
            pltpu.VMEM((3, share, 3 * ch // 4), F32),
            dma((3,)),
            dma((batches,)),
            dma((batches,)), dma((batches,)),
            dma((batches, 2)), dma((batches, 2)),
            dma, dma,
            dma((2,)), dma((2,)),
            dma((2,)), dma((2,)),
            dma((batches, 3, 2)), dma((batches, 3, 2)),
            dma((batches, strips)), dma((batches,)),
            dma((batches, 3, 2)), dma((batches, 3, 2)),
            dma((batches, strips)), dma((batches,)),
            dma((batches, 3, 2)), dma((batches, 3, 2)),
            dma((batches, strips)), dma((batches,)),
            dma((batches, strips)),
            dma((batches,)), dma((batches,)), dma((batches,)),
            dma((batches,)), dma((batches,)), dma((batches,)),
            dma((batches, strips // 2)), dma((batches, strips // 2)),
            dma((batches,)), dma((batches,)),
            dma((batches, strips)), dma((batches, strips)),
            dma((4,)),
        ],
        compiler_params=pltpu.CompilerParams(
            collective_id=0, has_side_effects=True, vmem_limit_bytes=56 * 2**20
        ),
        cost_estimate=pl.CostEstimate(
            flops=flops, bytes_accessed=2 * 9 * ch * ch * 2, transcendentals=0
        ),
    )(
        images.reshape(batches, pictures, strip, ch),
        cotangent.reshape(batches, pictures, strip, ch),
        conv_weights.reshape(3, 3 * ch, ch),
        gains,
        shifts,
        switches.reshape(-1, switches.shape[-1]),
    )
    def seats_on(d):
        return [(i, i // 4 * 4 + (i + d) % 4) for i in range(strips)]

    parts = [lax.ppermute(part, "rows", seats_on(d + 1)) for d, part in enumerate((part_1, part_2, part_3))]
    results = (outs, grads_in, gain_sum, shift_sum)
    whole = jax.ShapeDtypeStruct((3, 3, share, ch), F32)
    outs, grads_in, gain_sum, shift_sum, weight_grad = pl.pallas_call(
        settle,
        out_shape=tuple(jax.ShapeDtypeStruct(r.shape, r.dtype) for r in results) + (whole,),
        in_specs=[anywhere] * 8,
        out_specs=(anywhere,) * 5,
        scratch_shapes=[pltpu.VMEM(r.shape, r.dtype) for r in results]
        + [
            pltpu.VMEM(own.shape, F32),
            pltpu.VMEM((3, *part_1.shape), BF16),
            pltpu.VMEM(whole.shape, F32),
            dma((2 * batches + 6,)),
            dma((2 * batches + 3,)),
        ],
        compiler_params=pltpu.CompilerParams(vmem_limit_bytes=60 * 2**20),
    )(*results, own, *parts)
    shape = (1, batches, pictures, strip_rows, cols, ch)
    return (outs.reshape(shape), grads_in.reshape(shape), weight_grad[None], gain_sum, shift_sum)


def solution(mesh):
    return jax.shard_map(
        body,
        mesh=mesh,
        in_specs=(
            P(None, None, "rows", None, None),
            P(None, None, "rows", None),
            P("section", None, None, None, None),
            P("section", None),
            P("section", None),
            P(None, None, "rows", None, None),
        ),
        out_specs=(
            P("section", None, None, "rows", None, None),
            P("section", None, None, "rows", None, None),
            P("section", None, None, "rows", None),
            P("section", None),
            P("section", None),
        ),
        check_vma=False,
    )
```

```python
import functools

import jax
import jax.numpy as jnp
from jax import lax
from jax.experimental import pallas as pl
from jax.experimental.pallas import tpu as pltpu
from jax.sharding import PartitionSpec as P

EPSILON = 1e-05
MESH = pl.DeviceIdType.MESH
BF16 = jnp.bfloat16
F32 = jnp.float32


def kernel(
    sections, strips, cols,
    images, cotangent, weights, gains, shifts, switches,
    outs, grads_in, weight_grad, gain_sum, shift_sum,
    w_v, wt_v, inp, mask_own, mask_v, gain_prev, shift_prev, zin, zin_stat, zown, own_stat, ub, slope_prev,
    prev_coef, own_coef, dyin, dy_stat, dzb, dz_out, dyout, stat_out, sums_out, seed_sums, out_v, gin_v,
    ut_own, ut_all, dz_all, dz_taps, acc_v, swap_out, swap_in, dw_v,
    w_sem, in_sem, pi_s, pi_r, ie_s, ie_r, mp_s, mp_r, me_s, me_r, gp_s, gp_r,
    fz_s, fz_r, fs_s, fs_r, oe_s, oe_r, os_s, os_r, bz_s, bz_r, bs_s, bs_r, ls_s,
    out_sem, po_s, po_r, gin_sem, pg_s, pg_r,
    ut_s, ut_r, uf_s, uf_r, dz_s, dz_r, sw_s, sw_r, dw_sem,
):
    sec = lax.axis_index("section")
    row = lax.axis_index("rows")
    batches, tall, ch = inp.shape
    px = tall - 2 * cols
    strip = px // 2
    groups = tall // cols
    half = ch // 2
    total = float(px * strips)
    local = float(px)
    first, last, decoder = sec == 0, sec == sections - 1, sec == sections // 2
    late = sec >= sections // 2
    core = row % 2
    partner = row + 1 - 2 * core
    has_up, has_down = row >= 2, row < strips - 2
    centre = pl.ds(cols, px)
    chip = row // 2
    team, seat = row // 4, row % 4
    lanes = dz_all.shape[3]
    block = ut_all.shape[3]
    share = block // 4
    mine = pl.multiple_of(cols + strip * core, cols)

    def w_copy(r):
        return pltpu.make_async_copy(weights.at[r], w_v.at[r], w_sem.at[r])

    def in_copy(src, m):
        return pltpu.make_async_copy(src.at[m, core], inp.at[m, pl.ds(mine, strip), :], in_sem.at[m])

    for r in range(3):
        w_copy(r).start()

    @pl.when(first)
    def _():
        for m in range(batches):
            in_copy(images, m).start()

    @pl.when(last)
    def _():
        for m in range(batches):
            in_copy(cotangent, m).start()

    barrier = pltpu.get_barrier_semaphore()
    for s in range(sections):
        @pl.when((sec >= s - 1) & (sec <= s + 1))
        def _():
            def greet(i, carry):
                @pl.when((s != sec) | (i != row))
                def _():
                    pl.semaphore_signal(barrier, inc=1, device_id=(jnp.int32(s), i), device_id_type=MESH)
                return carry
            lax.fori_loop(0, strips, greet, 0)

    acc_v[...] = jnp.zeros_like(acc_v)
    gain_sum[...] = jnp.zeros_like(gain_sum)
    shift_sum[...] = jnp.zeros_like(shift_sum)

    for m in range(batches):
        for i in range(2):
            for at in (0, dz_all.shape[2] - cols):
                dz_all[m, i, pl.ds(at, cols), :] = jnp.zeros((cols, lanes), BF16)

    @pl.when(decoder)
    def _():
        wide = cols // 2
        windows_at = lax.broadcasted_iota(jnp.int32, (cols, wide), 1)
        places = lax.broadcasted_iota(jnp.int32, (cols, wide), 0)
        pick = (lax.shift_right_logical(places, 1) == windows_at).astype(F32)
        table = lax.dot_general(
            pick, switches[...].astype(F32), (((1,), (1,)), ((), ())), preferred_element_type=F32
        )
        odd = jnp.bitwise_and(lax.broadcasted_iota(jnp.int32, (cols, 128), 0), 1).astype(F32)
        windows = strip // cols // 2
        for m in range(batches):
            for i in range(2):
                for w in range(windows):
                    at = (m * 2 + i) * windows + w
                    value = jnp.broadcast_to(table[:, at : at + 1], (cols, 128))
                    for p in range(2):
                        hit = (jnp.abs(value - (2.0 * p + odd)) < 0.5).astype(F32).astype(BF16)
                        mask_own[m, i, pl.ds((2 * w + p) * cols, cols), :] = hit
        for m in range(batches):
            mask_v[m, pl.ds(mine, strip), :] = mask_own[m, core]

    @pl.when(jnp.logical_not(decoder))
    def _():
        mask_v[...] = jnp.ones_like(mask_v)

    near = 1 + jnp.where(sec > 0, 1, 0) + jnp.where(sec < sections - 1, 1, 0)
    pl.semaphore_wait(barrier, near * strips - 1)

    def remote(src, dst, send, recv, s, i):
        return pltpu.make_async_remote_copy(
            src_ref=src, dst_ref=dst, send_sem=send, recv_sem=recv, device_id=(s, i), device_id_type=MESH
        )

    def to_partner(src_at, dst_at, send, recv):
        return remote(src_at(1 - core), dst_at(pl.ds(mine, strip)), send, recv, sec, partner)

    def start_argument(src_at, dst_at, pair_sems, edge_sems):
        to_partner(src_at, dst_at, *pair_sems).start()

        @pl.when((core == 1) & has_down)
        def _():
            for i in range(2):
                remote(
                    src_at(i, pl.ds(strip - cols, cols)), dst_at(pl.ds(0, cols)),
                    edge_sems[0].at[i], edge_sems[1].at[0], sec, row + 1 + i,
                ).start()

        @pl.when((core == 0) & has_up)
        def _():
            for i in range(2):
                remote(
                    src_at(i, pl.ds(0, cols)), dst_at(pl.ds(cols + px, cols)),
                    edge_sems[0].at[i], edge_sems[1].at[1], sec, row - 2 + i,
                ).start()

    def argument_arrived(src_at, dst_at, pair_sems, edge_sems):
        to_partner(src_at, dst_at, *pair_sems).wait_recv()

        @pl.when(has_up)
        def _():
            remote(
                src_at(0, pl.ds(0, cols)), dst_at(pl.ds(0, cols)), edge_sems[0].at[0], edge_sems[1].at[0], sec, row
            ).wait_recv()

        @pl.when(has_down)
        def _():
            remote(
                src_at(0, pl.ds(0, cols)), dst_at(pl.ds(cols + px, cols)), edge_sems[0].at[0], edge_sems[1].at[1],
                sec, row,
            ).wait_recv()

    def argument_sent(src_at, dst_at, pair_sems, edge_sems):
        to_partner(src_at, dst_at, *pair_sems).wait_send()

        @pl.when(((core == 1) & has_down) | ((core == 0) & has_up))
        def _():
            for i in range(2):
                remote(
                    src_at(i, pl.ds(0, cols)), dst_at(pl.ds(0, cols)), edge_sems[0].at[i], edge_sems[1].at[0], sec, row
                ).wait_send()

    def input_parts(src, m):
        return (
            lambda i, r=pl.ds(0, strip): src.at[m, i, r, :],
            lambda r: inp.at[m, r, :],
            (pi_s.at[m], pi_r.at[m]),
            (ie_s.at[m], ie_r.at[m]),
        )

    mask_parts = (
        lambda i, r=pl.ds(0, strip): mask_own.at[:, i, r, :],
        lambda r: mask_v.at[:, r, :],
        (mp_s, mp_r),
        (me_s, me_r),
    )

    @pl.when(first)
    def _():
        for m in range(batches):
            start_argument(*input_parts(images, m))

    @pl.when(last)
    def _():
        for m in range(batches):
            start_argument(*input_parts(cotangent, m))

    @pl.when(decoder)
    def _():
        start_argument(*mask_parts)

    def affine_sends():
        return (
            remote(gains, gain_prev, gp_s.at[0], gp_r.at[0], sec + 1, row),
            remote(shifts, shift_prev, gp_s.at[1], gp_r.at[1], sec + 1, row),
        )

    @pl.when(sec < sections - 1)
    def _():
        for copy in affine_sends():
            copy.start()

    def block_sends(src, src_from, dst, send, recv, m, s):
        def one(k, h, src_row, dst_row, rows, i):
            return remote(
                src.at[m, h, pl.ds(src_from + src_row, rows), :], dst.at[m, h, pl.ds(dst_row, rows), :],
                send.at[m, k, h], recv.at[m, k, h], s, i,
            )
        return (
            (None, lambda h: one(0, h, 0, cols, px, row)),
            (has_down, lambda h: one(1, h, px - cols, 0, cols, row + 2)),
            (has_up, lambda h: one(2, h, 0, cols + px, cols, row - 2)),
        )

    def each(parts, h, act):
        for cond, make in parts:
            if cond is None:
                act(make(h))
            else:
                @pl.when(cond)
                def _():
                    act(make(h))

    def arrived(parts):
        (_, body), (_, to_down), (_, to_up) = parts
        for h in range(2):
            body(h).wait_recv()
        edges_arrived(to_down, to_up)

    def edges_arrived(to_down, to_up):
        @pl.when(has_up)
        def _():
            for h in range(2):
                to_down(h).wait_recv()

        @pl.when(has_down)
        def _():
            for h in range(2):
                to_up(h).wait_recv()

    def start(copy):
        copy.start()

    def sent(copy):
        copy.wait_send()

    def came(copy):
        copy.wait_recv()

    def z_sends(m, s):
        return block_sends(zown, cols, zin, fz_s, fz_r, m, s)

    def own_edges(m):
        return block_sends(zown, cols, zown, oe_s, oe_r, m, sec)[1:]

    def dy_sends(m, s):
        return block_sends(dyout, 0, dyin, bz_s, bz_r, m, s)

    def stat_copy(src, dst, send, recv, m, s, i):
        return remote(src.at[m], dst.at[m, row], send.at[m, i], recv.at[m], s, i)

    def stats_each(src, dst, send, recv, m, s, same, act):
        def one(d, carry):
            i = row + d
            act(stat_copy(src, dst, send, recv, m, s, jnp.where(i >= strips, i - strips, i)))
            return carry
        lax.fori_loop(1 if same else 0, strips, one, 0)

    def start_stats(src, dst, send, recv, m, s, same):
        stats_each(src, dst, send, recv, m, s, same, start)
        if same:
            pltpu.make_async_copy(src.at[m], dst.at[m, row], recv.at[m]).start()

    def wait_stats(dst, recv, m):
        pltpu.make_async_copy(dst.at[m], dst.at[m], recv.at[m]).wait()

    down_stats = (stat_out, zin_stat, fs_s, fs_r)
    same_stats = (stat_out, own_stat, os_s, os_r)
    back_stats = (sums_out, dy_stat, bs_s, bs_r)
    seed_stats = (seed_sums, dy_stat, ls_s, bs_r)

    def join(stats_ref, m):
        means, squares = stats_ref[m, :, 0, :], stats_ref[m, :, 1, :]
        mean = jnp.sum(means, 0, keepdims=True) / float(strips)
        off = means - mean
        var = (jnp.sum(squares, 0, keepdims=True) + local * jnp.sum(off * off, 0, keepdims=True)) / total
        at = (jnp.maximum(row - 2, 0), row, jnp.minimum(row + 2, strips - 1))
        return lax.rsqrt(var + EPSILON), [stats_ref[m, i, pl.ds(0, 1), :] - mean for i in at]

    def kind(g):
        return 0 if g == 0 else 2 if g == groups - 1 else 1

    def inside(g, values):
        if kind(g) == 1:
            return values
        return jnp.where(has_up if kind(g) == 0 else has_down, values, jnp.zeros_like(values))

    def group(g):
        return pl.ds(g * cols, cols)

    column = lax.broadcasted_iota(jnp.int32, (1, cols, half), 1)

    def taps_joined(parts, left, right):
        def moved(values, by, edge):
            turned = pltpu.roll(values, by % px, 0).reshape(px // cols, cols, half)
            return jnp.where(column == edge, 0.0, turned).reshape(px, half)
        return parts[1] + moved(parts[left], 1, 0) + moved(parts[right], -1, cols - 1)

    def turned_copy(m, q):
        src = ut_own.at[m, pl.ds(pl.multiple_of((q // 2) * block, block), block), :]
        return src, ut_all.at[m, core, chip]

    chips = strips // 2
    thirds = [1 + (chips - 1) * i // 3 for i in range(4)]

    def turned_each(m, act, low=1, high=chips):
        def one(d, carry):
            q = chip + d
            q = jnp.where(q >= chips, q - chips, q)
            src, dst = turned_copy(m, q)
            act(remote(src, dst, ut_s.at[m, d], ut_r.at[m, d], sec, 2 * q + core))
            return carry
        lax.fori_loop(low, high, one, 0)

    def turn_inputs(m):
        ut_own[m] = ub[m, centre, :].T
        mine_at = pl.ds(pl.multiple_of(team * block, block), block)
        ut_all[m, core, chip] = ut_own[m, mine_at, :]

    def send_turned_third(m, i):
        @pl.when(late & (m >= 0) & (m < batches))
        def _():
            if i == 0:
                turn_inputs(m)
            turned_each(m, start, thirds[i], thirds[i + 1])

    def turned_relay(m):
        return remote(ut_all.at[m, core], ut_all.at[m, core], uf_s.at[m], uf_r.at[m], sec, partner)

    def relay_turned(m):
        turned_each(m, came)
        turned_relay(m).start()

    def dz_copy(m, i):
        src = dz_out.at[m, i % 4]
        dst = dz_all.at[m, core, pl.ds(pl.multiple_of(cols + chip * px, cols), px), :]
        return src, dst

    def dz_each(m, act):
        def one(d, carry):
            i = row + d
            i = jnp.where(i >= strips, i - strips, i)
            src, dst = dz_copy(m, i)
            act(remote(src, dst, dz_s.at[m, d], dz_r.at[m, d], sec, i))
            return carry
        lax.fori_loop(1, strips, one, 0)

    def send_dz(m):
        dz_each(m, start)
        dz_all[m, core, pl.ds(pl.multiple_of(cols + chip * px, cols), px), :] = dz_out[m, seat]

    def gather_taps(m):
        dz_each(m, came)
        relayed = ut_all.at[m, 1 - core]
        pltpu.make_async_copy(relayed, relayed, uf_r.at[m]).wait()
        rows = dz_all.shape[2]
        edge = lax.broadcasted_iota(jnp.int32, (1, cols, lanes), 1)
        for i in range(2):
            values = dz_all[m, i].astype(F32)
            for c, by, gone in ((0, rows - 1, cols - 1), (2, 1, 0)):
                turned = pltpu.roll(values, by, 0).reshape(rows // cols, cols, lanes)
                turned = jnp.where(edge == gone, 0.0, turned).reshape(rows, lanes)
                dz_taps[i, :, pl.ds(c * lanes, lanes)] = turned.astype(BF16)
            dz_taps[i, :, pl.ds(lanes, lanes)] = dz_all[m, i]

    def kernel_row(m, r):
        part = jnp.zeros((block, 3 * lanes), F32)
        for i in range(2):
            left = jnp.concatenate([ut_all[m, i, q] for q in range(chips)], axis=1)
            part += jnp.dot(
                left, dz_taps[i, pl.ds((2 - r) * cols, px * (strips // 2)), :], preferred_element_type=F32
            )
        return part

    def add_gradients(m):
        gather_taps(m)
        for r in range(3):
            acc_v[r] = acc_v[r] + kernel_row(m, r)

    def forward(m):
        @pl.when(first)
        def _():
            in_copy(images, m).wait()
            argument_arrived(*input_parts(images, m))
            for g in range(groups):
                ub[m, group(g), :] = inside(g, inp[m, group(g), :])

        @pl.when(sec > 0)
        def _():
            @pl.when(m == 0)
            def _():
                for copy in affine_sends():
                    copy.wait_recv()

                @pl.when(decoder)
                def _():
                    argument_arrived(*mask_parts)

            wait_stats(zin_stat, fs_r, m)
            inv, offs = join(zin_stat, m)
            prev_coef[m, pl.ds(0, 1), :] = inv
            prev_coef[m, pl.ds(1, 1), :] = offs[1]
            slant = 0.5 * inv * gain_prev[...]
            level = [slant * off + 0.5 * shift_prev[...] for off in offs]
            arrived(z_sends(m, sec))
            for g in range(groups):
                gate = jnp.concatenate([mask_v[m, group(g), :].astype(F32)] * (half // 128), axis=1)
                for h in range(2):
                    part = slice(h * half, (h + 1) * half)
                    halved = zin[m, h, group(g), :].astype(F32) * slant[:, part] + level[kind(g)][:, part]
                    turn = jnp.tanh(halved)
                    bent = halved * turn
                    ub[m, group(g), part] = inside(g, ((halved + bent) * gate).astype(BF16))
                    if kind(g) == 1:
                        slope_prev[m, pl.ds((g - 1) * cols, cols), part] = (0.5 + 0.5 * turn) * (1.0 + halved - bent)

        @pl.when(jnp.logical_not(late) & (m == 0))
        def _():
            for r in range(3):
                w_copy(r).wait()

        for h in range(2):
            part = pl.ds(h * half, half)
            parts = []
            for c in range(3):
                acc = jnp.zeros((px, half), F32)
                for r in range(3):
                    acc += jnp.dot(
                        ub[m, pl.ds(r * cols, px), :], w_v[r, pl.ds(c * ch, ch), part], preferred_element_type=F32
                    )
                parts.append(acc)
            conv = taps_joined(parts, 0, 2)
            mean = jnp.sum(conv, 0, keepdims=True) / local
            conv = conv - mean
            stat_out[m, pl.ds(0, 1), part] = mean
            stat_out[m, pl.ds(1, 1), part] = jnp.sum(conv * conv, 0, keepdims=True)
            zown[m, h, centre, :] = conv.astype(BF16)

            @pl.when(sec < sections - 1)
            def _():
                if h == 1:
                    start_stats(*down_stats, m, sec + 1, False)
                each(z_sends(m, sec + 1), h, start)

        start_stats(*same_stats, m, sec, True)
        for h in range(2):
            each(own_edges(m), h, start)

    def finish(m):
        wait_stats(own_stat, os_r, m)
        inv, offs = join(own_stat, m)
        scale = inv * gains[...]
        own_coef[m, pl.ds(0, 1), :] = inv
        own_coef[m, pl.ds(1, 1), :] = scale
        for k in range(3):
            own_coef[m, pl.ds(2 + k, 1), :] = offs[k]
        slant = 0.5 * scale
        level = [slant * off + 0.5 * shifts[...] for off in offs]
        (_, to_down), (_, to_up) = own_edges(m)
        edges_arrived(to_down, to_up)

        @pl.when(last)
        def _():
            in_copy(cotangent, m).wait()
            argument_arrived(*input_parts(cotangent, m))
            for h in range(2):
                part = slice(h * half, (h + 1) * half)
                sums = jnp.zeros((cols, half), F32)
                cross = jnp.zeros((cols, half), F32)
                for g in range(groups):
                    z = zown[m, h, group(g), :].astype(F32)
                    halved = z * slant[:, part] + level[kind(g)][:, part]
                    turn = jnp.tanh(halved)
                    bent = halved * turn
                    dy = inp[m, group(g), part].astype(F32) * ((0.5 + 0.5 * turn) * (1.0 + halved - bent))
                    dyin[m, h, group(g), :] = dy.astype(BF16)
                    if kind(g) == 1:
                        out_v[m, pl.ds((g - 1) * cols, cols), part] = (halved + bent).astype(BF16)
                        sums += dy
                        cross += dy * z
                one = jnp.sum(sums, 0, keepdims=True)
                cross = jnp.sum(cross, 0, keepdims=True)
                seed_sums[m, pl.ds(0, 1), part] = one
                seed_sums[m, pl.ds(1, 1), part] = inv[:, part] * (cross + offs[1][:, part] * one)
            start_stats(*seed_stats, m, sec, True)

        @pl.when(jnp.logical_not(last))
        def _():
            for h in range(2):
                part = slice(h * half, (h + 1) * half)
                for g in range(1, groups - 1):
                    halved = zown[m, h, group(g), :].astype(F32) * slant[:, part] + level[1][:, part]
                    out_v[m, pl.ds((g - 1) * cols, cols), part] = (halved + halved * jnp.tanh(halved)).astype(BF16)

        for copy in result_copies(out_v, outs, out_sem, po_s, po_r, m):
            copy.start()

    def result_copies(src, dst, sem, send, recv, m):
        here, there = pl.multiple_of(strip * core, cols), pl.multiple_of(strip * (1 - core), cols)
        return (
            pltpu.make_async_copy(src.at[m, pl.ds(here, strip), :], dst.at[m, core], sem.at[m]),
            remote(src.at[m, pl.ds(there, strip), :], dst.at[m, core], send.at[m], recv.at[m], sec, partner),
        )

    def backward(m):
        wait_stats(dy_stat, bs_r, m)
        first_sum = jnp.sum(dy_stat[m, :, 0, :], 0, keepdims=True)
        cross_sum = jnp.sum(dy_stat[m, :, 1, :], 0, keepdims=True)
        shift_sum[...] += first_sum
        gain_sum[...] += cross_sum
        inv = own_coef[m, pl.ds(0, 1), :]
        scale = own_coef[m, pl.ds(1, 1), :]
        tilt = scale * inv * (cross_sum / total)
        base = [scale * (first_sum / total) + tilt * own_coef[m, pl.ds(2 + k, 1), :] for k in range(3)]

        @pl.when(sec < sections - 1)
        def _():
            arrived(dy_sends(m, sec))

        for g in range(groups):
            for h in range(2):
                part = slice(h * half, (h + 1) * half)
                dz = dyin[m, h, group(g), :].astype(F32) * scale[:, part]
                dz = dz - zown[m, h, group(g), :].astype(F32) * tilt[:, part] - base[kind(g)][:, part]
                dz = inside(g, dz.astype(BF16))
                dzb[m, group(g), part] = dz
                if kind(g) == 1:
                    for k in range(half // lanes):
                        dz_out[m, h * (half // lanes) + k, pl.ds((g - 1) * cols, cols), :] = dz[
                            :, k * lanes : (k + 1) * lanes
                        ]

        @pl.when(first)
        def _():
            send_dz(m)

        for h in range(2):
            part = pl.ds(h * half, half)
            parts = []
            for c in range(3):
                acc = jnp.zeros((px, half), F32)
                for r in range(3):
                    acc += jnp.dot(
                        dzb[m, pl.ds((2 - r) * cols, px), :], wt_v[r, pl.ds(c * ch, ch), part],
                        preferred_element_type=F32,
                    )
                parts.append(acc)
            gate = jnp.concatenate([mask_v[m, centre, :].astype(F32)] * (half // 128), axis=1)
            du = (taps_joined(parts, 2, 0) * gate).astype(BF16)
            gin_v[m, :, part] = du

            @pl.when(sec > 0)
            def _():
                dy = du.astype(F32) * slope_prev[m, :, part]
                dyout[m, h] = dy.astype(BF16)
                one = jnp.sum(dy, 0, keepdims=True)
                cross = jnp.sum(dy * zin[m, h, centre, :].astype(F32), 0, keepdims=True)
                sums_out[m, pl.ds(0, 1), part] = one
                sums_out[m, pl.ds(1, 1), part] = prev_coef[m, pl.ds(0, 1), part] * (
                    cross + prev_coef[m, pl.ds(1, 1), part] * one
                )
                if h == 1:
                    start_stats(*back_stats, m, sec - 1, False)
                each(dy_sends(m, sec - 1), h, start)

        for copy in result_copies(gin_v, grads_in, gin_sem, pg_s, pg_r, m):
            copy.start()

        @pl.when((sec > 0) & (sec < sections - 1))
        def _():
            send_dz(m)

    def turn_weights():
        def one(i, carry):
            at = pl.ds(pl.multiple_of(lax.rem(i, 3) * ch, ch), ch)
            wt_v[lax.div(i, 3), at, :] = w_v[lax.div(i, 3), at, :].T
            return carry
        lax.fori_loop(0, 9, one, 0)

    @pl.when(late)
    def _():
        for r in range(3):
            w_copy(r).wait()
        turn_weights()

    def step(t, carry):
        ahead = t - sec
        behind = t - (2 * sections - 1 - sec) - jnp.where(last, 1, 0)

        @pl.when((ahead >= 0) & (ahead < batches))
        def _():
            forward(ahead)

        send_turned_third(ahead, 0)

        @pl.when(jnp.logical_not(late) & (ahead == batches))
        def _():
            def turned(m, carry):
                turn_inputs(m)
                turned_each(m, start)
                return carry
            lax.fori_loop(0, batches, turned, 0)
            turn_weights()

        @pl.when((ahead >= 1) & (ahead <= batches))
        def _():
            finish(ahead - 1)

        send_turned_third(ahead, 1)

        @pl.when((behind >= 0) & (behind < batches))
        def _():
            backward(behind)

        send_turned_third(ahead, 2)

        @pl.when(jnp.logical_not(late) & (ahead == batches + 1))
        def _():
            def relay(m, carry):
                relay_turned(m)
                return carry
            lax.fori_loop(0, batches, relay, 0)

        @pl.when((behind >= 1) & (behind < batches) & jnp.logical_not(late))
        def _():
            add_gradients(behind - 1)

        return carry

    lax.fori_loop(0, 2 * sections - 1 + batches, step, 0)

    @pl.when(last)
    def _():
        def send(m, carry):
            send_dz(m)
            return carry

        lax.fori_loop(0, batches, send, 0)

    @pl.when(late)
    def _():
        def relay(m, carry):
            relay_turned(m)
            return carry

        def add(m, carry):
            add_gradients(m)
            return carry

        lax.fori_loop(0, batches, relay, 0)
        lax.fori_loop(0, batches - 1, add, 0)

    def swap(r, d):
        other = (seat + d) % 4
        return remote(
            swap_out.at[r, pl.ds(pl.multiple_of(other * share, share), share), :], swap_in.at[r, 4 - d - 1],
            sw_s.at[r, d - 1], sw_r.at[r, 4 - d - 1], sec, 4 * team + other,
        )

    gather_taps(batches - 1)
    for r in range(3):
        part = acc_v[r] + kernel_row(batches - 1, r)
        acc_v[r] = part
        swap_out[r] = part.astype(BF16)
        for d in range(1, 4):
            swap(r, d).start()

    def dw_copy(r):
        return pltpu.make_async_copy(dw_v.at[r], weight_grad.at[r], dw_sem.at[r])

    own_rows = pl.ds(pl.multiple_of(seat * share, share), share)
    for r in range(3):
        for c in range(3):
            dw_v[r, c, :, pl.ds(pl.multiple_of(seat * lanes, lanes), lanes)] = acc_v[r, own_rows, pl.ds(c * lanes, lanes)]
        for d in range(1, 4):
            swap(r, 4 - d).wait_recv()
            source = (seat + d) % 4
            for c in range(3):
                dw_v[r, c, :, pl.ds(pl.multiple_of(source * lanes, lanes), lanes)] = swap_in[
                    r, d - 1, :, pl.ds(c * lanes, lanes)
                ].astype(F32)
        dw_copy(r).start()

    for r in range(3):
        dw_copy(r).wait()
        for d in range(1, 4):
            swap(r, d).wait_send()

    @pl.when(decoder)
    def _():
        argument_sent(*mask_parts)

    @pl.when(sec < sections - 1)
    def _():
        for copy in affine_sends():
            copy.wait_send()

    def drain(m, carry):
        for src, dst, sems in ((out_v, outs, (out_sem, po_s, po_r)), (gin_v, grads_in, (gin_sem, pg_s, pg_r))):
            here, there = result_copies(src, dst, *sems, m)
            here.wait()
            there.wait_send()
            remote(
                src.at[m, pl.ds(0, strip), :], dst.at[m, 1 - core], sems[1].at[m], sems[2].at[m], sec, partner
            ).wait_recv()

        turned_each(m, sent)
        turned_relay(m).wait_send()
        dz_each(m, sent)

        @pl.when(first)
        def _():
            argument_sent(*input_parts(images, m))

        @pl.when(last)
        def _():
            argument_sent(*input_parts(cotangent, m))
            stats_each(*seed_stats, m, sec, True, sent)

        @pl.when(sec < sections - 1)
        def _():
            stats_each(*down_stats, m, sec + 1, False, sent)
            for h in range(2):
                each(z_sends(m, sec + 1), h, sent)

        stats_each(*same_stats, m, sec, True, sent)
        for h in range(2):
            each(own_edges(m), h, sent)

        @pl.when(sec > 0)
        def _():
            stats_each(*back_stats, m, sec - 1, False, sent)
            for h in range(2):
                each(dy_sends(m, sec - 1), h, sent)

        return carry

    lax.fori_loop(0, batches, drain, 0)


def settle(*refs):
    count = (len(refs) - 2) // 3
    sources, targets, stages = refs[:count], refs[count : 2 * count], refs[2 * count : 3 * count]
    moves = []
    for src, dst, stage in zip(sources, targets, stages):
        if len(src.shape) == 2:
            moves.append((src, dst, stage))
        else:
            moves += [(src.at[i], dst.at[i], stage.at[i]) for i in range(src.shape[0])]
    ins = [pltpu.make_async_copy(src, stage, refs[-2].at[i]) for i, (src, dst, stage) in enumerate(moves)]
    outs = [pltpu.make_async_copy(stage, dst, refs[-1].at[i]) for i, (src, dst, stage) in enumerate(moves)]
    for copy in ins:
        copy.start()
    for come, go in zip(ins, outs):
        come.wait()
        go.start()
    for copy in outs:
        copy.wait()


def body(images, switches, conv_weights, gains, shifts, cotangent):
    sections = lax.axis_size("section")
    strips = lax.axis_size("rows")
    batches, pictures, strip_rows, cols, ch = images.shape
    strip = strip_rows * cols
    px = 2 * strip
    tall = px + 2 * cols
    anywhere = pl.BlockSpec(memory_space=pl.ANY)
    vmem = pl.BlockSpec(memory_space=pltpu.VMEM)
    dma = pltpu.SemaphoreType.DMA
    flops = 3 * 2 * 9 * ch * ch * batches * px
    share = ch // strips
    outs, grads_in, weight_grad, gain_sum, shift_sum = pl.pallas_call(
        functools.partial(kernel, sections, strips, cols),
        out_shape=(
            jax.ShapeDtypeStruct((batches, pictures, strip, ch), BF16),
            jax.ShapeDtypeStruct((batches, pictures, strip, ch), BF16),
            jax.ShapeDtypeStruct((3, 3, share, ch), F32),
            jax.ShapeDtypeStruct((1, ch), F32),
            jax.ShapeDtypeStruct((1, ch), F32),
        ),
        in_specs=[anywhere, anywhere, anywhere, vmem, vmem, vmem],
        out_specs=(anywhere, anywhere, anywhere, vmem, vmem),
        scratch_shapes=[
            pltpu.VMEM((3, 3 * ch, ch), BF16),
            pltpu.VMEM((3, 3 * ch, ch), BF16),
            pltpu.VMEM((batches, tall, ch), BF16),
            pltpu.VMEM((batches, 2, strip, 128), BF16),
            pltpu.VMEM((batches, tall, 128), BF16),
            pltpu.VMEM((1, ch), F32),
            pltpu.VMEM((1, ch), F32),
            pltpu.VMEM((batches, 2, tall, ch // 2), BF16),
            pltpu.VMEM((batches, strips, 2, ch), F32),
            pltpu.VMEM((batches, 2, tall, ch // 2), BF16),
            pltpu.VMEM((batches, strips, 2, ch), F32),
            pltpu.VMEM((batches, tall, ch), BF16),
            pltpu.VMEM((batches, px, ch), F32),
            pltpu.VMEM((batches, 2, ch), F32),
            pltpu.VMEM((batches, 8, ch), F32),
            pltpu.VMEM((batches, 2, tall, ch // 2), BF16),
            pltpu.VMEM((batches, strips, 2, ch), F32),
            pltpu.VMEM((batches, tall, ch), BF16),
            pltpu.VMEM((batches, 4, px, ch // 4), BF16),
            pltpu.VMEM((batches, 2, px, ch // 2), BF16),
            pltpu.VMEM((batches, 2, ch), F32),
            pltpu.VMEM((batches, 2, ch), F32),
            pltpu.VMEM((batches, 2, ch), F32),
            pltpu.VMEM((batches, px, ch), BF16),
            pltpu.VMEM((batches, px, ch), BF16),
            pltpu.VMEM((batches, ch, px), BF16),
            pltpu.VMEM((batches, 2, strips // 2, 4 * share, px), BF16),
            pltpu.VMEM((batches, 2, px * strips // 2 + 2 * cols, ch // 4), BF16),
            pltpu.VMEM((2, px * strips // 2 + 2 * cols, 3 * ch // 4), BF16),
            pltpu.VMEM((3, 4 * share, 3 * ch // 4), F32),
            pltpu.VMEM((3, 4 * share, 3 * ch // 4), BF16),
            pltpu.VMEM((3, 3, share, 3 * ch // 4), BF16),
            pltpu.VMEM((3, 3, share, ch), F32),
            dma((3,)),
            dma((batches,)),
            dma((batches,)), dma((batches,)),
            dma((batches, 2)), dma((batches, 2)),
            dma, dma,
            dma((2,)), dma((2,)),
            dma((2,)), dma((2,)),
            dma((batches, 3, 2)), dma((batches, 3, 2)),
            dma((batches, strips)), dma((batches,)),
            dma((batches, 3, 2)), dma((batches, 3, 2)),
            dma((batches, strips)), dma((batches,)),
            dma((batches, 3, 2)), dma((batches, 3, 2)),
            dma((batches, strips)), dma((batches,)),
            dma((batches, strips)),
            dma((batches,)), dma((batches,)), dma((batches,)),
            dma((batches,)), dma((batches,)), dma((batches,)),
            dma((batches, strips // 2)), dma((batches, strips // 2)),
            dma((batches,)), dma((batches,)),
            dma((batches, strips)), dma((batches, strips)),
            dma((3, 3)), dma((3, 3)),
            dma((3,)),
        ],
        compiler_params=pltpu.CompilerParams(
            collective_id=0, has_side_effects=True, vmem_limit_bytes=56 * 2**20
        ),
        cost_estimate=pl.CostEstimate(
            flops=flops, bytes_accessed=2 * 9 * ch * ch * 2, transcendentals=0
        ),
    )(
        images.reshape(batches, pictures, strip, ch),
        cotangent.reshape(batches, pictures, strip, ch),
        conv_weights.reshape(3, 3 * ch, ch),
        gains,
        shifts,
        switches.reshape(-1, switches.shape[-1]),
    )
    results = (outs, grads_in, weight_grad, gain_sum, shift_sum)
    outs, grads_in, weight_grad, gain_sum, shift_sum = pl.pallas_call(
        settle,
        out_shape=tuple(jax.ShapeDtypeStruct(r.shape, r.dtype) for r in results),
        in_specs=[anywhere] * 5,
        out_specs=(anywhere,) * 5,
        scratch_shapes=[pltpu.VMEM(r.shape, r.dtype) for r in results] + [dma((2 * batches + 5,))] * 2,
        compiler_params=pltpu.CompilerParams(vmem_limit_bytes=60 * 2**20),
    )(*results)
    shape = (1, batches, pictures, strip_rows, cols, ch)
    return (outs.reshape(shape), grads_in.reshape(shape), weight_grad[None], gain_sum, shift_sum)


def solution(mesh):
    return jax.shard_map(
        body,
        mesh=mesh,
        in_specs=(
            P(None, None, "rows", None, None),
            P(None, None, "rows", None),
            P("section", None, None, None, None),
            P("section", None),
            P("section", None),
            P(None, None, "rows", None, None),
        ),
        out_specs=(
            P("section", None, None, "rows", None, None),
            P("section", None, None, "rows", None, None),
            P("section", None, None, "rows", None),
            P("section", None),
            P("section", None),
        ),
        check_vma=False,
    )
```

```python
import functools

import jax
import jax.numpy as jnp
from jax import lax
from jax.experimental import pallas as pl
from jax.experimental.pallas import tpu as pltpu
from jax.sharding import PartitionSpec as P

EPSILON = 1e-05
MESH = pl.DeviceIdType.MESH
BF16 = jnp.bfloat16
F32 = jnp.float32


def kernel(
    sections, strips, cols,
    images, cotangent, weights, gains, shifts, switches,
    outs, grads_in, weight_grad, gain_sum, shift_sum,
    w_v, wt_v, inp, mask_own, mask_v, gain_prev, shift_prev, zin, zin_stat, zown, own_stat, ub, slope_prev,
    prev_coef, own_coef, dyin, dy_stat, dzb, dz_out, dyout, stat_out, sums_out, seed_sums, out_v, gin_v,
    ut_own, ut_all, dz_all, dz_taps, acc_v, swap_out, swap_in, dw_v,
    w_sem, in_sem, pi_s, pi_r, ie_s, ie_r, mp_s, mp_r, me_s, me_r, gp_s, gp_r,
    fz_s, fz_r, fs_s, fs_r, oe_s, oe_r, os_s, os_r, bz_s, bz_r, bs_s, bs_r, ls_s,
    out_sem, po_s, po_r, gin_sem, pg_s, pg_r,
    ut_s, ut_r, uf_s, uf_r, dz_s, dz_r, sw_s, sw_r, dw_sem,
):
    sec = lax.axis_index("section")
    row = lax.axis_index("rows")
    batches, tall, ch = inp.shape
    px = tall - 2 * cols
    strip = px // 2
    groups = tall // cols
    half = ch // 2
    total = float(px * strips)
    local = float(px)
    first, last, decoder = sec == 0, sec == sections - 1, sec == sections // 2
    late = sec >= sections // 2
    core = row % 2
    partner = row + 1 - 2 * core
    has_up, has_down = row >= 2, row < strips - 2
    centre = pl.ds(cols, px)
    chip = row // 2
    team, seat = row // 4, row % 4
    lanes = dz_all.shape[3]
    block = ut_all.shape[3]
    share = block // 4
    mine = pl.multiple_of(cols + strip * core, cols)

    def w_copy(r):
        return pltpu.make_async_copy(weights.at[r], w_v.at[r], w_sem.at[r])

    def in_copy(src, m):
        return pltpu.make_async_copy(src.at[m, core], inp.at[m, pl.ds(mine, strip), :], in_sem.at[m])

    for r in range(3):
        w_copy(r).start()

    @pl.when(first)
    def _():
        for m in range(batches):
            in_copy(images, m).start()

    @pl.when(last)
    def _():
        for m in range(batches):
            in_copy(cotangent, m).start()

    barrier = pltpu.get_barrier_semaphore()
    for s in range(sections):
        @pl.when((sec >= s - 1) & (sec <= s + 1))
        def _():
            def greet(i, carry):
                @pl.when((s != sec) | (i != row))
                def _():
                    pl.semaphore_signal(barrier, inc=1, device_id=(jnp.int32(s), i), device_id_type=MESH)
                return carry
            lax.fori_loop(0, strips, greet, 0)

    acc_v[...] = jnp.zeros_like(acc_v)
    gain_sum[...] = jnp.zeros_like(gain_sum)
    shift_sum[...] = jnp.zeros_like(shift_sum)

    for m in range(batches):
        for i in range(2):
            for at in (0, dz_all.shape[2] - cols):
                dz_all[m, i, pl.ds(at, cols), :] = jnp.zeros((cols, lanes), BF16)

    @pl.when(decoder)
    def _():
        wide = cols // 2
        windows_at = lax.broadcasted_iota(jnp.int32, (cols, wide), 1)
        places = lax.broadcasted_iota(jnp.int32, (cols, wide), 0)
        pick = (lax.shift_right_logical(places, 1) == windows_at).astype(F32)
        table = lax.dot_general(
            pick, switches[...].astype(F32), (((1,), (1,)), ((), ())), preferred_element_type=F32
        )
        odd = jnp.bitwise_and(lax.broadcasted_iota(jnp.int32, (cols, 128), 0), 1).astype(F32)
        windows = strip // cols // 2
        for m in range(batches):
            for i in range(2):
                for w in range(windows):
                    at = (m * 2 + i) * windows + w
                    value = jnp.broadcast_to(table[:, at : at + 1], (cols, 128))
                    for p in range(2):
                        hit = (jnp.abs(value - (2.0 * p + odd)) < 0.5).astype(F32).astype(BF16)
                        mask_own[m, i, pl.ds((2 * w + p) * cols, cols), :] = hit
        for m in range(batches):
            mask_v[m, pl.ds(mine, strip), :] = mask_own[m, core]

    @pl.when(jnp.logical_not(decoder))
    def _():
        mask_v[...] = jnp.ones_like(mask_v)

    near = 1 + jnp.where(sec > 0, 1, 0) + jnp.where(sec < sections - 1, 1, 0)
    pl.semaphore_wait(barrier, near * strips - 1)

    def remote(src, dst, send, recv, s, i):
        return pltpu.make_async_remote_copy(
            src_ref=src, dst_ref=dst, send_sem=send, recv_sem=recv, device_id=(s, i), device_id_type=MESH
        )

    def to_partner(src_at, dst_at, send, recv):
        return remote(src_at(1 - core), dst_at(pl.ds(mine, strip)), send, recv, sec, partner)

    def start_argument(src_at, dst_at, pair_sems, edge_sems):
        to_partner(src_at, dst_at, *pair_sems).start()

        @pl.when((core == 1) & has_down)
        def _():
            for i in range(2):
                remote(
                    src_at(i, pl.ds(strip - cols, cols)), dst_at(pl.ds(0, cols)),
                    edge_sems[0].at[i], edge_sems[1].at[0], sec, row + 1 + i,
                ).start()

        @pl.when((core == 0) & has_up)
        def _():
            for i in range(2):
                remote(
                    src_at(i, pl.ds(0, cols)), dst_at(pl.ds(cols + px, cols)),
                    edge_sems[0].at[i], edge_sems[1].at[1], sec, row - 2 + i,
                ).start()

    def argument_arrived(src_at, dst_at, pair_sems, edge_sems):
        to_partner(src_at, dst_at, *pair_sems).wait_recv()

        @pl.when(has_up)
        def _():
            remote(
                src_at(0, pl.ds(0, cols)), dst_at(pl.ds(0, cols)), edge_sems[0].at[0], edge_sems[1].at[0], sec, row
            ).wait_recv()

        @pl.when(has_down)
        def _():
            remote(
                src_at(0, pl.ds(0, cols)), dst_at(pl.ds(cols + px, cols)), edge_sems[0].at[0], edge_sems[1].at[1],
                sec, row,
            ).wait_recv()

    def argument_sent(src_at, dst_at, pair_sems, edge_sems):
        to_partner(src_at, dst_at, *pair_sems).wait_send()

        @pl.when(((core == 1) & has_down) | ((core == 0) & has_up))
        def _():
            for i in range(2):
                remote(
                    src_at(i, pl.ds(0, cols)), dst_at(pl.ds(0, cols)), edge_sems[0].at[i], edge_sems[1].at[0], sec, row
                ).wait_send()

    def input_parts(src, m):
        return (
            lambda i, r=pl.ds(0, strip): src.at[m, i, r, :],
            lambda r: inp.at[m, r, :],
            (pi_s.at[m], pi_r.at[m]),
            (ie_s.at[m], ie_r.at[m]),
        )

    mask_parts = (
        lambda i, r=pl.ds(0, strip): mask_own.at[:, i, r, :],
        lambda r: mask_v.at[:, r, :],
        (mp_s, mp_r),
        (me_s, me_r),
    )

    @pl.when(first)
    def _():
        for m in range(batches):
            start_argument(*input_parts(images, m))

    @pl.when(last)
    def _():
        for m in range(batches):
            start_argument(*input_parts(cotangent, m))

    @pl.when(decoder)
    def _():
        start_argument(*mask_parts)

    def affine_sends():
        return (
            remote(gains, gain_prev, gp_s.at[0], gp_r.at[0], sec + 1, row),
            remote(shifts, shift_prev, gp_s.at[1], gp_r.at[1], sec + 1, row),
        )

    @pl.when(sec < sections - 1)
    def _():
        for copy in affine_sends():
            copy.start()

    def block_sends(src, src_from, dst, send, recv, m, s):
        def one(k, h, src_row, dst_row, rows, i):
            return remote(
                src.at[m, h, pl.ds(src_from + src_row, rows), :], dst.at[m, h, pl.ds(dst_row, rows), :],
                send.at[m, k, h], recv.at[m, k, h], s, i,
            )
        return (
            (None, lambda h: one(0, h, 0, cols, px, row)),
            (has_down, lambda h: one(1, h, px - cols, 0, cols, row + 2)),
            (has_up, lambda h: one(2, h, 0, cols + px, cols, row - 2)),
        )

    def each(parts, h, act):
        for cond, make in parts:
            if cond is None:
                act(make(h))
            else:
                @pl.when(cond)
                def _():
                    act(make(h))

    def arrived(parts):
        (_, body), (_, to_down), (_, to_up) = parts
        for h in range(2):
            body(h).wait_recv()
        edges_arrived(to_down, to_up)

    def edges_arrived(to_down, to_up):
        @pl.when(has_up)
        def _():
            for h in range(2):
                to_down(h).wait_recv()

        @pl.when(has_down)
        def _():
            for h in range(2):
                to_up(h).wait_recv()

    def start(copy):
        copy.start()

    def sent(copy):
        copy.wait_send()

    def came(copy):
        copy.wait_recv()

    def z_sends(m, s):
        return block_sends(zown, cols, zin, fz_s, fz_r, m, s)

    def own_edges(m):
        return block_sends(zown, cols, zown, oe_s, oe_r, m, sec)[1:]

    def dy_sends(m, s):
        return block_sends(dyout, 0, dyin, bz_s, bz_r, m, s)

    def stat_copy(src, dst, send, recv, m, s, i):
        return remote(src.at[m], dst.at[m, row], send.at[m, i], recv.at[m], s, i)

    def stats_each(src, dst, send, recv, m, s, same, act):
        def one(d, carry):
            i = row + d
            act(stat_copy(src, dst, send, recv, m, s, jnp.where(i >= strips, i - strips, i)))
            return carry
        lax.fori_loop(1 if same else 0, strips, one, 0)

    def start_stats(src, dst, send, recv, m, s, same):
        stats_each(src, dst, send, recv, m, s, same, start)
        if same:
            pltpu.make_async_copy(src.at[m], dst.at[m, row], recv.at[m]).start()

    def wait_stats(dst, recv, m):
        pltpu.make_async_copy(dst.at[m], dst.at[m], recv.at[m]).wait()

    down_stats = (stat_out, zin_stat, fs_s, fs_r)
    same_stats = (stat_out, own_stat, os_s, os_r)
    back_stats = (sums_out, dy_stat, bs_s, bs_r)
    seed_stats = (seed_sums, dy_stat, ls_s, bs_r)

    def join(stats_ref, m):
        means, squares = stats_ref[m, :, 0, :], stats_ref[m, :, 1, :]
        mean = jnp.sum(means, 0, keepdims=True) / float(strips)
        off = means - mean
        var = (jnp.sum(squares, 0, keepdims=True) + local * jnp.sum(off * off, 0, keepdims=True)) / total
        at = (jnp.maximum(row - 2, 0), row, jnp.minimum(row + 2, strips - 1))
        return lax.rsqrt(var + EPSILON), [stats_ref[m, i, pl.ds(0, 1), :] - mean for i in at]

    def kind(g):
        return 0 if g == 0 else 2 if g == groups - 1 else 1

    def inside(g, values):
        if kind(g) == 1:
            return values
        return jnp.where(has_up if kind(g) == 0 else has_down, values, jnp.zeros_like(values))

    def group(g):
        return pl.ds(g * cols, cols)

    column = lax.broadcasted_iota(jnp.int32, (1, cols, half), 1)

    def taps_joined(parts, left, right):
        def moved(values, by, edge):
            turned = pltpu.roll(values, by % px, 0).reshape(px // cols, cols, half)
            return jnp.where(column == edge, 0.0, turned).reshape(px, half)
        return parts[1] + moved(parts[left], 1, 0) + moved(parts[right], -1, cols - 1)

    def turned_copy(m, q):
        src = ut_own.at[m, pl.ds(pl.multiple_of((q // 2) * block, block), block), :]
        return src, ut_all.at[m, core, chip]

    chips = strips // 2

    def turned_each(m, act):
        def one(d, carry):
            q = chip + d
            q = jnp.where(q >= chips, q - chips, q)
            src, dst = turned_copy(m, q)
            act(remote(src, dst, ut_s.at[m, d], ut_r.at[m, d], sec, 2 * q + core))
            return carry
        lax.fori_loop(1, chips, one, 0)

    def turn_inputs(m):
        ut_own[m] = ub[m, centre, :].T
        mine_at = pl.ds(pl.multiple_of(team * block, block), block)
        ut_all[m, core, chip] = ut_own[m, mine_at, :]

    def send_turned():
        def one(m, carry):
            turn_inputs(m)
            turned_each(m, start)
            return carry
        lax.fori_loop(0, batches, one, 0)

    def turned_relay(m):
        return remote(ut_all.at[m, core], ut_all.at[m, core], uf_s.at[m], uf_r.at[m], sec, partner)

    def relay_turned(m):
        turned_each(m, came)
        turned_relay(m).start()

    def dz_copy(m, i):
        src = dz_out.at[m, i % 4]
        dst = dz_all.at[m, core, pl.ds(pl.multiple_of(cols + chip * px, cols), px), :]
        return src, dst

    def dz_each(m, act):
        def one(d, carry):
            i = row + d
            i = jnp.where(i >= strips, i - strips, i)
            src, dst = dz_copy(m, i)
            act(remote(src, dst, dz_s.at[m, d], dz_r.at[m, d], sec, i))
            return carry
        lax.fori_loop(1, strips, one, 0)

    def send_dz(m):
        dz_each(m, start)
        dz_all[m, core, pl.ds(pl.multiple_of(cols + chip * px, cols), px), :] = dz_out[m, seat]

    def gather_taps(m):
        dz_each(m, came)
        relayed = ut_all.at[m, 1 - core]
        pltpu.make_async_copy(relayed, relayed, uf_r.at[m]).wait()
        rows = dz_all.shape[2]
        edge = lax.broadcasted_iota(jnp.int32, (1, cols, lanes), 1)
        for i in range(2):
            values = dz_all[m, i].astype(F32)
            for c, by, gone in ((0, rows - 1, cols - 1), (2, 1, 0)):
                turned = pltpu.roll(values, by, 0).reshape(rows // cols, cols, lanes)
                turned = jnp.where(edge == gone, 0.0, turned).reshape(rows, lanes)
                dz_taps[i, :, pl.ds(c * lanes, lanes)] = turned.astype(BF16)
            dz_taps[i, :, pl.ds(lanes, lanes)] = dz_all[m, i]

    def kernel_row(m, r):
        part = jnp.zeros((block, 3 * lanes), F32)
        for i in range(2):
            left = jnp.concatenate([ut_all[m, i, q] for q in range(chips)], axis=1)
            part += jnp.dot(
                left, dz_taps[i, pl.ds((2 - r) * cols, px * (strips // 2)), :], preferred_element_type=F32
            )
        return part

    def add_gradients(m):
        gather_taps(m)
        for r in range(3):
            acc_v[r] = acc_v[r] + kernel_row(m, r)

    def forward(m):
        @pl.when(first)
        def _():
            in_copy(images, m).wait()
            argument_arrived(*input_parts(images, m))
            for g in range(groups):
                ub[m, group(g), :] = inside(g, inp[m, group(g), :])

        @pl.when(sec > 0)
        def _():
            @pl.when(m == 0)
            def _():
                for copy in affine_sends():
                    copy.wait_recv()

                @pl.when(decoder)
                def _():
                    argument_arrived(*mask_parts)

            wait_stats(zin_stat, fs_r, m)
            inv, offs = join(zin_stat, m)
            prev_coef[m, pl.ds(0, 1), :] = inv
            prev_coef[m, pl.ds(1, 1), :] = offs[1]
            slant = 0.5 * inv * gain_prev[...]
            level = [slant * off + 0.5 * shift_prev[...] for off in offs]
            arrived(z_sends(m, sec))
            for g in range(groups):
                gate = jnp.concatenate([mask_v[m, group(g), :].astype(F32)] * (half // 128), axis=1)
                for h in range(2):
                    part = slice(h * half, (h + 1) * half)
                    halved = zin[m, h, group(g), :].astype(F32) * slant[:, part] + level[kind(g)][:, part]
                    turn = jnp.tanh(halved)
                    bent = halved * turn
                    ub[m, group(g), part] = inside(g, ((halved + bent) * gate).astype(BF16))
                    if kind(g) == 1:
                        slope_prev[m, pl.ds((g - 1) * cols, cols), part] = (0.5 + 0.5 * turn) * (1.0 + halved - bent)

        @pl.when(jnp.logical_not(late) & (m == 0))
        def _():
            for r in range(3):
                w_copy(r).wait()

        for h in range(2):
            part = pl.ds(h * half, half)
            parts = []
            for c in range(3):
                acc = jnp.zeros((px, half), F32)
                for r in range(3):
                    acc += jnp.dot(
                        ub[m, pl.ds(r * cols, px), :], w_v[r, pl.ds(c * ch, ch), part], preferred_element_type=F32
                    )
                parts.append(acc)
            conv = taps_joined(parts, 0, 2)
            mean = jnp.sum(conv, 0, keepdims=True) / local
            conv = conv - mean
            stat_out[m, pl.ds(0, 1), part] = mean
            stat_out[m, pl.ds(1, 1), part] = jnp.sum(conv * conv, 0, keepdims=True)
            zown[m, h, centre, :] = conv.astype(BF16)

            @pl.when(sec < sections - 1)
            def _():
                if h == 1:
                    start_stats(*down_stats, m, sec + 1, False)
                each(z_sends(m, sec + 1), h, start)

        start_stats(*same_stats, m, sec, True)
        for h in range(2):
            each(own_edges(m), h, start)

    def finish(m):
        wait_stats(own_stat, os_r, m)
        inv, offs = join(own_stat, m)
        scale = inv * gains[...]
        own_coef[m, pl.ds(0, 1), :] = inv
        own_coef[m, pl.ds(1, 1), :] = scale
        for k in range(3):
            own_coef[m, pl.ds(2 + k, 1), :] = offs[k]
        slant = 0.5 * scale
        level = [slant * off + 0.5 * shifts[...] for off in offs]
        (_, to_down), (_, to_up) = own_edges(m)
        edges_arrived(to_down, to_up)

        @pl.when(last)
        def _():
            in_copy(cotangent, m).wait()
            argument_arrived(*input_parts(cotangent, m))
            for h in range(2):
                part = slice(h * half, (h + 1) * half)
                sums = jnp.zeros((cols, half), F32)
                cross = jnp.zeros((cols, half), F32)
                for g in range(groups):
                    z = zown[m, h, group(g), :].astype(F32)
                    halved = z * slant[:, part] + level[kind(g)][:, part]
                    turn = jnp.tanh(halved)
                    bent = halved * turn
                    dy = inp[m, group(g), part].astype(F32) * ((0.5 + 0.5 * turn) * (1.0 + halved - bent))
                    dyin[m, h, group(g), :] = dy.astype(BF16)
                    if kind(g) == 1:
                        out_v[m, pl.ds((g - 1) * cols, cols), part] = (halved + bent).astype(BF16)
                        sums += dy
                        cross += dy * z
                one = jnp.sum(sums, 0, keepdims=True)
                cross = jnp.sum(cross, 0, keepdims=True)
                seed_sums[m, pl.ds(0, 1), part] = one
                seed_sums[m, pl.ds(1, 1), part] = inv[:, part] * (cross + offs[1][:, part] * one)
            start_stats(*seed_stats, m, sec, True)

        @pl.when(jnp.logical_not(last))
        def _():
            for h in range(2):
                part = slice(h * half, (h + 1) * half)
                for g in range(1, groups - 1):
                    halved = zown[m, h, group(g), :].astype(F32) * slant[:, part] + level[1][:, part]
                    out_v[m, pl.ds((g - 1) * cols, cols), part] = (halved + halved * jnp.tanh(halved)).astype(BF16)

        for copy in result_copies(out_v, outs, out_sem, po_s, po_r, m):
            copy.start()

    def result_copies(src, dst, sem, send, recv, m):
        here, there = pl.multiple_of(strip * core, cols), pl.multiple_of(strip * (1 - core), cols)
        return (
            pltpu.make_async_copy(src.at[m, pl.ds(here, strip), :], dst.at[m, core], sem.at[m]),
            remote(src.at[m, pl.ds(there, strip), :], dst.at[m, core], send.at[m], recv.at[m], sec, partner),
        )

    def backward(m):
        wait_stats(dy_stat, bs_r, m)
        first_sum = jnp.sum(dy_stat[m, :, 0, :], 0, keepdims=True)
        cross_sum = jnp.sum(dy_stat[m, :, 1, :], 0, keepdims=True)
        shift_sum[...] += first_sum
        gain_sum[...] += cross_sum
        inv = own_coef[m, pl.ds(0, 1), :]
        scale = own_coef[m, pl.ds(1, 1), :]
        tilt = scale * inv * (cross_sum / total)
        base = [scale * (first_sum / total) + tilt * own_coef[m, pl.ds(2 + k, 1), :] for k in range(3)]

        @pl.when(sec < sections - 1)
        def _():
            arrived(dy_sends(m, sec))

        for g in range(groups):
            for h in range(2):
                part = slice(h * half, (h + 1) * half)
                dz = dyin[m, h, group(g), :].astype(F32) * scale[:, part]
                dz = dz - zown[m, h, group(g), :].astype(F32) * tilt[:, part] - base[kind(g)][:, part]
                dz = inside(g, dz.astype(BF16))
                dzb[m, group(g), part] = dz
                if kind(g) == 1:
                    for k in range(half // lanes):
                        dz_out[m, h * (half // lanes) + k, pl.ds((g - 1) * cols, cols), :] = dz[
                            :, k * lanes : (k + 1) * lanes
                        ]

        @pl.when(first)
        def _():
            send_dz(m)

        for h in range(2):
            part = pl.ds(h * half, half)
            parts = []
            for c in range(3):
                acc = jnp.zeros((px, half), F32)
                for r in range(3):
                    acc += jnp.dot(
                        dzb[m, pl.ds((2 - r) * cols, px), :], wt_v[r, pl.ds(c * ch, ch), part],
                        preferred_element_type=F32,
                    )
                parts.append(acc)
            gate = jnp.concatenate([mask_v[m, centre, :].astype(F32)] * (half // 128), axis=1)
            du = (taps_joined(parts, 2, 0) * gate).astype(BF16)
            gin_v[m, :, part] = du

            @pl.when(sec > 0)
            def _():
                dy = du.astype(F32) * slope_prev[m, :, part]
                dyout[m, h] = dy.astype(BF16)
                one = jnp.sum(dy, 0, keepdims=True)
                cross = jnp.sum(dy * zin[m, h, centre, :].astype(F32), 0, keepdims=True)
                sums_out[m, pl.ds(0, 1), part] = one
                sums_out[m, pl.ds(1, 1), part] = prev_coef[m, pl.ds(0, 1), part] * (
                    cross + prev_coef[m, pl.ds(1, 1), part] * one
                )
                if h == 1:
                    start_stats(*back_stats, m, sec - 1, False)
                each(dy_sends(m, sec - 1), h, start)

        for copy in result_copies(gin_v, grads_in, gin_sem, pg_s, pg_r, m):
            copy.start()

        @pl.when((sec > 0) & (sec < sections - 1))
        def _():
            send_dz(m)

    def turn_weights():
        def one(i, carry):
            at = pl.ds(pl.multiple_of(lax.rem(i, 3) * ch, ch), ch)
            wt_v[lax.div(i, 3), at, :] = w_v[lax.div(i, 3), at, :].T
            return carry
        lax.fori_loop(0, 9, one, 0)

    @pl.when(late)
    def _():
        for r in range(3):
            w_copy(r).wait()
        turn_weights()

    def step(t, carry):
        ahead = t - sec
        behind = t - (2 * sections - 1 - sec)

        @pl.when((ahead >= 0) & (ahead < batches))
        def _():
            forward(ahead)

        @pl.when(jnp.logical_not(late) & (ahead == batches))
        def _():
            send_turned()
            turn_weights()

        done = ahead - jnp.where(last, 0, 1)

        @pl.when((behind >= 0) & (behind < batches))
        def _():
            backward(behind)

        @pl.when((done >= 0) & (done < batches))
        def _():
            finish(done)

        @pl.when(jnp.logical_not(late) & (ahead == batches + 1))
        def _():
            def relay(m, carry):
                relay_turned(m)
                return carry
            lax.fori_loop(0, batches, relay, 0)

        @pl.when((behind >= 1) & (behind < batches) & jnp.logical_not(late))
        def _():
            add_gradients(behind - 1)

        return carry

    lax.fori_loop(0, 2 * sections - 1 + batches, step, 0)

    @pl.when(late)
    def _():
        send_turned()

    @pl.when(last)
    def _():
        def send(m, carry):
            send_dz(m)
            return carry

        lax.fori_loop(0, batches, send, 0)

    @pl.when(late)
    def _():
        def relay(m, carry):
            relay_turned(m)
            return carry

        def add(m, carry):
            add_gradients(m)
            return carry

        lax.fori_loop(0, batches, relay, 0)
        lax.fori_loop(0, batches - 1, add, 0)

    def swap(r, d):
        other = (seat + d) % 4
        return remote(
            swap_out.at[r, pl.ds(pl.multiple_of(other * share, share), share), :], swap_in.at[r, 4 - d - 1],
            sw_s.at[r, d - 1], sw_r.at[r, 4 - d - 1], sec, 4 * team + other,
        )

    gather_taps(batches - 1)
    for r in range(3):
        part = acc_v[r] + kernel_row(batches - 1, r)
        acc_v[r] = part
        swap_out[r] = part.astype(BF16)
        for d in range(1, 4):
            swap(r, d).start()

    def dw_copy(r):
        return pltpu.make_async_copy(dw_v.at[r], weight_grad.at[r], dw_sem.at[r])

    own_rows = pl.ds(pl.multiple_of(seat * share, share), share)
    for r in range(3):
        for c in range(3):
            dw_v[r, c, :, pl.ds(pl.multiple_of(seat * lanes, lanes), lanes)] = acc_v[r, own_rows, pl.ds(c * lanes, lanes)]
        for d in range(1, 4):
            swap(r, 4 - d).wait_recv()
            source = (seat + d) % 4
            for c in range(3):
                dw_v[r, c, :, pl.ds(pl.multiple_of(source * lanes, lanes), lanes)] = swap_in[
                    r, d - 1, :, pl.ds(c * lanes, lanes)
                ].astype(F32)
        dw_copy(r).start()

    for r in range(3):
        dw_copy(r).wait()
        for d in range(1, 4):
            swap(r, d).wait_send()

    @pl.when(decoder)
    def _():
        argument_sent(*mask_parts)

    @pl.when(sec < sections - 1)
    def _():
        for copy in affine_sends():
            copy.wait_send()

    def drain(m, carry):
        for src, dst, sems in ((out_v, outs, (out_sem, po_s, po_r)), (gin_v, grads_in, (gin_sem, pg_s, pg_r))):
            here, there = result_copies(src, dst, *sems, m)
            here.wait()
            there.wait_send()
            remote(
                src.at[m, pl.ds(0, strip), :], dst.at[m, 1 - core], sems[1].at[m], sems[2].at[m], sec, partner
            ).wait_recv()

        turned_each(m, sent)
        turned_relay(m).wait_send()
        dz_each(m, sent)

        @pl.when(first)
        def _():
            argument_sent(*input_parts(images, m))

        @pl.when(last)
        def _():
            argument_sent(*input_parts(cotangent, m))
            stats_each(*seed_stats, m, sec, True, sent)

        @pl.when(sec < sections - 1)
        def _():
            stats_each(*down_stats, m, sec + 1, False, sent)
            for h in range(2):
                each(z_sends(m, sec + 1), h, sent)

        stats_each(*same_stats, m, sec, True, sent)
        for h in range(2):
            each(own_edges(m), h, sent)

        @pl.when(sec > 0)
        def _():
            stats_each(*back_stats, m, sec - 1, False, sent)
            for h in range(2):
                each(dy_sends(m, sec - 1), h, sent)

        return carry

    lax.fori_loop(0, batches, drain, 0)


def settle(*refs):
    count = (len(refs) - 2) // 3
    sources, targets, stages = refs[:count], refs[count : 2 * count], refs[2 * count : 3 * count]
    moves = []
    for src, dst, stage in zip(sources, targets, stages):
        if len(src.shape) == 2:
            moves.append((src, dst, stage))
        else:
            moves += [(src.at[i], dst.at[i], stage.at[i]) for i in range(src.shape[0])]
    ins = [pltpu.make_async_copy(src, stage, refs[-2].at[i]) for i, (src, dst, stage) in enumerate(moves)]
    outs = [pltpu.make_async_copy(stage, dst, refs[-1].at[i]) for i, (src, dst, stage) in enumerate(moves)]
    for copy in ins:
        copy.start()
    for come, go in zip(ins, outs):
        come.wait()
        go.start()
    for copy in outs:
        copy.wait()


def body(images, switches, conv_weights, gains, shifts, cotangent):
    sections = lax.axis_size("section")
    strips = lax.axis_size("rows")
    batches, pictures, strip_rows, cols, ch = images.shape
    strip = strip_rows * cols
    px = 2 * strip
    tall = px + 2 * cols
    anywhere = pl.BlockSpec(memory_space=pl.ANY)
    vmem = pl.BlockSpec(memory_space=pltpu.VMEM)
    dma = pltpu.SemaphoreType.DMA
    flops = 3 * 2 * 9 * ch * ch * batches * px
    share = ch // strips
    outs, grads_in, weight_grad, gain_sum, shift_sum = pl.pallas_call(
        functools.partial(kernel, sections, strips, cols),
        out_shape=(
            jax.ShapeDtypeStruct((batches, pictures, strip, ch), BF16),
            jax.ShapeDtypeStruct((batches, pictures, strip, ch), BF16),
            jax.ShapeDtypeStruct((3, 3, share, ch), F32),
            jax.ShapeDtypeStruct((1, ch), F32),
            jax.ShapeDtypeStruct((1, ch), F32),
        ),
        in_specs=[anywhere, anywhere, anywhere, vmem, vmem, vmem],
        out_specs=(anywhere, anywhere, anywhere, vmem, vmem),
        scratch_shapes=[
            pltpu.VMEM((3, 3 * ch, ch), BF16),
            pltpu.VMEM((3, 3 * ch, ch), BF16),
            pltpu.VMEM((batches, tall, ch), BF16),
            pltpu.VMEM((batches, 2, strip, 128), BF16),
            pltpu.VMEM((batches, tall, 128), BF16),
            pltpu.VMEM((1, ch), F32),
            pltpu.VMEM((1, ch), F32),
            pltpu.VMEM((batches, 2, tall, ch // 2), BF16),
            pltpu.VMEM((batches, strips, 2, ch), F32),
            pltpu.VMEM((batches, 2, tall, ch // 2), BF16),
            pltpu.VMEM((batches, strips, 2, ch), F32),
            pltpu.VMEM((batches, tall, ch), BF16),
            pltpu.VMEM((batches, px, ch), F32),
            pltpu.VMEM((batches, 2, ch), F32),
            pltpu.VMEM((batches, 8, ch), F32),
            pltpu.VMEM((batches, 2, tall, ch // 2), BF16),
            pltpu.VMEM((batches, strips, 2, ch), F32),
            pltpu.VMEM((batches, tall, ch), BF16),
            pltpu.VMEM((batches, 4, px, ch // 4), BF16),
            pltpu.VMEM((batches, 2, px, ch // 2), BF16),
            pltpu.VMEM((batches, 2, ch), F32),
            pltpu.VMEM((batches, 2, ch), F32),
            pltpu.VMEM((batches, 2, ch), F32),
            pltpu.VMEM((batches, px, ch), BF16),
            pltpu.VMEM((batches, px, ch), BF16),
            pltpu.VMEM((batches, ch, px), BF16),
            pltpu.VMEM((batches, 2, strips // 2, 4 * share, px), BF16),
            pltpu.VMEM((batches, 2, px * strips // 2 + 2 * cols, ch // 4), BF16),
            pltpu.VMEM((2, px * strips // 2 + 2 * cols, 3 * ch // 4), BF16),
            pltpu.VMEM((3, 4 * share, 3 * ch // 4), F32),
            pltpu.VMEM((3, 4 * share, 3 * ch // 4), BF16),
            pltpu.VMEM((3, 3, share, 3 * ch // 4), BF16),
            pltpu.VMEM((3, 3, share, ch), F32),
            dma((3,)),
            dma((batches,)),
            dma((batches,)), dma((batches,)),
            dma((batches, 2)), dma((batches, 2)),
            dma, dma,
            dma((2,)), dma((2,)),
            dma((2,)), dma((2,)),
            dma((batches, 3, 2)), dma((batches, 3, 2)),
            dma((batches, strips)), dma((batches,)),
            dma((batches, 3, 2)), dma((batches, 3, 2)),
            dma((batches, strips)), dma((batches,)),
            dma((batches, 3, 2)), dma((batches, 3, 2)),
            dma((batches, strips)), dma((batches,)),
            dma((batches, strips)),
            dma((batches,)), dma((batches,)), dma((batches,)),
            dma((batches,)), dma((batches,)), dma((batches,)),
            dma((batches, strips // 2)), dma((batches, strips // 2)),
            dma((batches,)), dma((batches,)),
            dma((batches, strips)), dma((batches, strips)),
            dma((3, 3)), dma((3, 3)),
            dma((3,)),
        ],
        compiler_params=pltpu.CompilerParams(
            collective_id=0, has_side_effects=True, vmem_limit_bytes=56 * 2**20
        ),
        cost_estimate=pl.CostEstimate(
            flops=flops, bytes_accessed=2 * 9 * ch * ch * 2, transcendentals=0
        ),
    )(
        images.reshape(batches, pictures, strip, ch),
        cotangent.reshape(batches, pictures, strip, ch),
        conv_weights.reshape(3, 3 * ch, ch),
        gains,
        shifts,
        switches.reshape(-1, switches.shape[-1]),
    )
    results = (outs, grads_in, weight_grad, gain_sum, shift_sum)
    outs, grads_in, weight_grad, gain_sum, shift_sum = pl.pallas_call(
        settle,
        out_shape=tuple(jax.ShapeDtypeStruct(r.shape, r.dtype) for r in results),
        in_specs=[anywhere] * 5,
        out_specs=(anywhere,) * 5,
        scratch_shapes=[pltpu.VMEM(r.shape, r.dtype) for r in results] + [dma((2 * batches + 5,))] * 2,
        compiler_params=pltpu.CompilerParams(vmem_limit_bytes=60 * 2**20),
    )(*results)
    shape = (1, batches, pictures, strip_rows, cols, ch)
    return (outs.reshape(shape), grads_in.reshape(shape), weight_grad[None], gain_sum, shift_sum)


def solution(mesh):
    return jax.shard_map(
        body,
        mesh=mesh,
        in_specs=(
            P(None, None, "rows", None, None),
            P(None, None, "rows", None),
            P("section", None, None, None, None),
            P("section", None),
            P("section", None),
            P(None, None, "rows", None, None),
        ),
        out_specs=(
            P("section", None, None, "rows", None, None),
            P("section", None, None, "rows", None, None),
            P("section", None, None, "rows", None),
            P("section", None),
            P("section", None),
        ),
        check_vma=False,
    )
```

```python
import functools

import jax
import jax.numpy as jnp
from jax import lax
from jax.experimental import pallas as pl
from jax.experimental.pallas import tpu as pltpu
from jax.sharding import PartitionSpec as P

EPSILON = 1e-05
MESH = pl.DeviceIdType.MESH
BF16 = jnp.bfloat16
F32 = jnp.float32


def kernel(
    sections, strips, cols,
    images, cotangent, weights, gains, shifts, switches,
    outs, grads_in, weight_grad, gain_sum, shift_sum,
    w_v, wt_v, inp, mask_own, mask_v, gain_prev, shift_prev, zin, zin_stat, zown, own_stat, ub, slope_prev,
    prev_coef, own_coef, dyin, dy_stat, dzb, dz_out, dyout, stat_out, sums_out, seed_sums, out_v, gin_v,
    ut_own, ut_all, dz_all, dz_taps, acc_v, swap_out, swap_in, dw_v,
    w_sem, in_sem, pi_s, pi_r, ie_s, ie_r, mp_s, mp_r, me_s, me_r, gp_s, gp_r,
    fz_s, fz_r, fs_s, fs_r, oe_s, oe_r, os_s, os_r, bz_s, bz_r, bs_s, bs_r, ls_s, jb_s, jb_r,
    out_sem, po_s, po_r, gin_sem, pg_s, pg_r,
    ut_s, ut_r, uf_s, uf_r, dz_s, dz_r, sw_s, sw_r, dw_sem,
):
    sec = lax.axis_index("section")
    row = lax.axis_index("rows")
    batches, tall, ch = inp.shape
    px = tall - 2 * cols
    strip = px // 2
    groups = tall // cols
    half = ch // 2
    total = float(px * strips)
    local = float(px)
    first, last, decoder = sec == 0, sec == sections - 1, sec == sections // 2
    late = sec >= sections // 2
    core = row % 2
    partner = row + 1 - 2 * core
    has_up, has_down = row >= 2, row < strips - 2
    centre = pl.ds(cols, px)
    chip = row // 2
    team, seat = row // 4, row % 4
    lanes = dz_all.shape[3]
    block = ut_all.shape[3]
    share = block // 4
    mine = pl.multiple_of(cols + strip * core, cols)

    def w_copy(r):
        return pltpu.make_async_copy(weights.at[r], w_v.at[r], w_sem.at[r])

    def in_copy(src, m):
        return pltpu.make_async_copy(src.at[m, core], inp.at[m, pl.ds(mine, strip), :], in_sem.at[m])

    for r in range(3):
        w_copy(r).start()

    @pl.when(first)
    def _():
        for m in range(batches):
            in_copy(images, m).start()

    @pl.when(last)
    def _():
        for m in range(batches):
            in_copy(cotangent, m).start()

    barrier = pltpu.get_barrier_semaphore()
    for s in range(sections):
        @pl.when((sec >= s - 1) & (sec <= s + 1))
        def _():
            def greet(i, carry):
                @pl.when((s != sec) | (i != row))
                def _():
                    pl.semaphore_signal(barrier, inc=1, device_id=(jnp.int32(s), i), device_id_type=MESH)
                return carry
            lax.fori_loop(0, strips, greet, 0)

    acc_v[...] = jnp.zeros_like(acc_v)
    gain_sum[...] = jnp.zeros_like(gain_sum)
    shift_sum[...] = jnp.zeros_like(shift_sum)

    for m in range(batches):
        for i in range(2):
            for at in (0, dz_all.shape[2] - cols):
                dz_all[m, i, pl.ds(at, cols), :] = jnp.zeros((cols, lanes), BF16)

    @pl.when(decoder)
    def _():
        wide = cols // 2
        windows_at = lax.broadcasted_iota(jnp.int32, (cols, wide), 1)
        places = lax.broadcasted_iota(jnp.int32, (cols, wide), 0)
        pick = (lax.shift_right_logical(places, 1) == windows_at).astype(F32)
        table = lax.dot_general(
            pick, switches[...].astype(F32), (((1,), (1,)), ((), ())), preferred_element_type=F32
        )
        odd = jnp.bitwise_and(lax.broadcasted_iota(jnp.int32, (cols, 128), 0), 1).astype(F32)
        windows = strip // cols // 2
        for m in range(batches):
            for i in range(2):
                for w in range(windows):
                    at = (m * 2 + i) * windows + w
                    value = jnp.broadcast_to(table[:, at : at + 1], (cols, 128))
                    for p in range(2):
                        hit = (jnp.abs(value - (2.0 * p + odd)) < 0.5).astype(F32).astype(BF16)
                        mask_own[m, i, pl.ds((2 * w + p) * cols, cols), :] = hit
        for m in range(batches):
            mask_v[m, pl.ds(mine, strip), :] = mask_own[m, core]

    @pl.when(jnp.logical_not(decoder))
    def _():
        mask_v[...] = jnp.ones_like(mask_v)

    near = 1 + jnp.where(sec > 0, 1, 0) + jnp.where(sec < sections - 1, 1, 0)
    pl.semaphore_wait(barrier, near * strips - 1)

    def remote(src, dst, send, recv, s, i):
        return pltpu.make_async_remote_copy(
            src_ref=src, dst_ref=dst, send_sem=send, recv_sem=recv, device_id=(s, i), device_id_type=MESH
        )

    def to_partner(src_at, dst_at, send, recv):
        return remote(src_at(1 - core), dst_at(pl.ds(mine, strip)), send, recv, sec, partner)

    def start_argument(src_at, dst_at, pair_sems, edge_sems):
        to_partner(src_at, dst_at, *pair_sems).start()

        @pl.when((core == 1) & has_down)
        def _():
            for i in range(2):
                remote(
                    src_at(i, pl.ds(strip - cols, cols)), dst_at(pl.ds(0, cols)),
                    edge_sems[0].at[i], edge_sems[1].at[0], sec, row + 1 + i,
                ).start()

        @pl.when((core == 0) & has_up)
        def _():
            for i in range(2):
                remote(
                    src_at(i, pl.ds(0, cols)), dst_at(pl.ds(cols + px, cols)),
                    edge_sems[0].at[i], edge_sems[1].at[1], sec, row - 2 + i,
                ).start()

    def argument_arrived(src_at, dst_at, pair_sems, edge_sems):
        to_partner(src_at, dst_at, *pair_sems).wait_recv()

        @pl.when(has_up)
        def _():
            remote(
                src_at(0, pl.ds(0, cols)), dst_at(pl.ds(0, cols)), edge_sems[0].at[0], edge_sems[1].at[0], sec, row
            ).wait_recv()

        @pl.when(has_down)
        def _():
            remote(
                src_at(0, pl.ds(0, cols)), dst_at(pl.ds(cols + px, cols)), edge_sems[0].at[0], edge_sems[1].at[1],
                sec, row,
            ).wait_recv()

    def argument_sent(src_at, dst_at, pair_sems, edge_sems):
        to_partner(src_at, dst_at, *pair_sems).wait_send()

        @pl.when(((core == 1) & has_down) | ((core == 0) & has_up))
        def _():
            for i in range(2):
                remote(
                    src_at(i, pl.ds(0, cols)), dst_at(pl.ds(0, cols)), edge_sems[0].at[i], edge_sems[1].at[0], sec, row
                ).wait_send()

    def input_parts(src, m):
        return (
            lambda i, r=pl.ds(0, strip): src.at[m, i, r, :],
            lambda r: inp.at[m, r, :],
            (pi_s.at[m], pi_r.at[m]),
            (ie_s.at[m], ie_r.at[m]),
        )

    mask_parts = (
        lambda i, r=pl.ds(0, strip): mask_own.at[:, i, r, :],
        lambda r: mask_v.at[:, r, :],
        (mp_s, mp_r),
        (me_s, me_r),
    )

    @pl.when(first)
    def _():
        for m in range(batches):
            start_argument(*input_parts(images, m))

    @pl.when(last)
    def _():
        for m in range(batches):
            start_argument(*input_parts(cotangent, m))

    @pl.when(decoder)
    def _():
        start_argument(*mask_parts)

    def affine_sends():
        return (
            remote(gains, gain_prev, gp_s.at[0], gp_r.at[0], sec + 1, row),
            remote(shifts, shift_prev, gp_s.at[1], gp_r.at[1], sec + 1, row),
        )

    @pl.when(sec < sections - 1)
    def _():
        for copy in affine_sends():
            copy.start()

    def block_sends(src, src_from, dst, send, recv, m, s):
        def body(h):
            return remote(
                src.at[m, h, pl.ds(src_from, px), :], dst.at[m, h, centre, :], send.at[m, h], recv.at[m, h], s, row
            )

        def edge(k, src_row, dst_row, i):
            return remote(
                src.at[m, :, pl.ds(src_from + src_row, cols), :], dst.at[m, :, pl.ds(dst_row, cols), :],
                send.at[m, 2 + k], recv.at[m, 2 + k], s, i,
            )

        return body, lambda: edge(0, px - cols, 0, row + 2), lambda: edge(1, 0, cols + px, row - 2)

    def each_edge(parts, act):
        _, to_down, to_up = parts

        @pl.when(has_down)
        def _():
            act(to_down())

        @pl.when(has_up)
        def _():
            act(to_up())

    def edges_arrived(parts):
        _, to_down, to_up = parts

        @pl.when(has_up)
        def _():
            to_down().wait_recv()

        @pl.when(has_down)
        def _():
            to_up().wait_recv()

    def arrived(parts):
        for h in range(2):
            parts[0](h).wait_recv()
        edges_arrived(parts)

    def all_sent(parts):
        for h in range(2):
            parts[0](h).wait_send()
        each_edge(parts, sent)

    def start(copy):
        copy.start()

    def sent(copy):
        copy.wait_send()

    def came(copy):
        copy.wait_recv()

    def z_sends(m, s):
        return block_sends(zown, cols, zin, fz_s, fz_r, m, s)

    def own_edges(m):
        return block_sends(zown, cols, zown, oe_s, oe_r, m, sec)

    def dy_sends(m, s):
        return block_sends(dyout, 0, dyin, bz_s, bz_r, m, s)

    def stat_copy(src, dst, send, recv, m, s, i):
        return remote(src.at[m], dst.at[m, row], send.at[m, i], recv.at[m], s, i)

    def stats_each(src, dst, send, recv, m, s, same, act):
        def one(d, carry):
            i = row + d
            act(stat_copy(src, dst, send, recv, m, s, jnp.where(i >= strips, i - strips, i)))
            return carry
        lax.fori_loop(1 if same else 0, strips, one, 0)

    def start_stats(src, dst, send, recv, m, s, same):
        stats_each(src, dst, send, recv, m, s, same, start)
        if same:
            pltpu.make_async_copy(src.at[m], dst.at[m, row], recv.at[m]).start()

    def wait_stats(dst, recv, m):
        pltpu.make_async_copy(dst.at[m], dst.at[m], recv.at[m]).wait()

    down_stats = (stat_out, zin_stat, fs_s, fs_r)
    same_stats = (stat_out, own_stat, os_s, os_r)
    back_stats = (sums_out, dy_stat, bs_s, bs_r)
    seed_stats = (seed_sums, dy_stat, ls_s, bs_r)

    def join(stats_ref, m):
        means, squares = stats_ref[m, :, 0, :], stats_ref[m, :, 1, :]
        mean = jnp.sum(means, 0, keepdims=True) / float(strips)
        off = means - mean
        var = (jnp.sum(squares, 0, keepdims=True) + local * jnp.sum(off * off, 0, keepdims=True)) / total
        at = (jnp.maximum(row - 2, 0), row, jnp.minimum(row + 2, strips - 1))
        return lax.rsqrt(var + EPSILON), [stats_ref[m, i, pl.ds(0, 1), :] - mean for i in at]

    def joined_back(m, s):
        return remote(prev_coef.at[m], own_coef.at[m], jb_s.at[m], jb_r.at[m], s, row)

    def kind(g):
        return 0 if g == 0 else 2 if g == groups - 1 else 1

    def inside(g, values):
        if kind(g) == 1:
            return values
        return jnp.where(has_up if kind(g) == 0 else has_down, values, jnp.zeros_like(values))

    def group(g):
        return pl.ds(g * cols, cols)

    column = lax.broadcasted_iota(jnp.int32, (1, cols, half), 1)

    def taps_joined(parts, left, right):
        def moved(values, by, edge):
            turned = pltpu.roll(values, by % px, 0).reshape(px // cols, cols, half)
            return jnp.where(column == edge, 0.0, turned).reshape(px, half)
        return parts[1] + moved(parts[left], 1, 0) + moved(parts[right], -1, cols - 1)

    def turned_copy(m, q):
        src = ut_own.at[m, pl.ds(pl.multiple_of((q // 2) * block, block), block), :]
        return src, ut_all.at[m, core, chip]

    chips = strips // 2

    def turned_each(m, act):
        def one(d, carry):
            q = chip + d
            q = jnp.where(q >= chips, q - chips, q)
            src, dst = turned_copy(m, q)
            act(remote(src, dst, ut_s.at[m, d], ut_r.at[m, d], sec, 2 * q + core))
            return carry
        lax.fori_loop(1, chips, one, 0)

    def turn_inputs(m):
        ut_own[m] = ub[m, centre, :].T
        mine_at = pl.ds(pl.multiple_of(team * block, block), block)
        ut_all[m, core, chip] = ut_own[m, mine_at, :]

    def send_turned():
        def one(m, carry):
            turn_inputs(m)
            turned_each(m, start)
            return carry
        lax.fori_loop(0, batches, one, 0)

    def turned_relay(m):
        return remote(ut_all.at[m, core], ut_all.at[m, core], uf_s.at[m], uf_r.at[m], sec, partner)

    def relay_turned(m):
        turned_each(m, came)
        turned_relay(m).start()

    def dz_copy(m, i):
        src = dz_out.at[m, i % 4]
        dst = dz_all.at[m, core, pl.ds(pl.multiple_of(cols + chip * px, cols), px), :]
        return src, dst

    def dz_each(m, act):
        def one(d, carry):
            i = row + d
            i = jnp.where(i >= strips, i - strips, i)
            src, dst = dz_copy(m, i)
            act(remote(src, dst, dz_s.at[m, d], dz_r.at[m, d], sec, i))
            return carry
        lax.fori_loop(1, strips, one, 0)

    def send_dz(m):
        dz_each(m, start)
        dz_all[m, core, pl.ds(pl.multiple_of(cols + chip * px, cols), px), :] = dz_out[m, seat]

    def gather_taps(m):
        dz_each(m, came)
        relayed = ut_all.at[m, 1 - core]
        pltpu.make_async_copy(relayed, relayed, uf_r.at[m]).wait()
        rows = dz_all.shape[2]
        edge = lax.broadcasted_iota(jnp.int32, (1, cols, lanes), 1)
        for i in range(2):
            values = dz_all[m, i].astype(F32)
            for c, by, gone in ((0, rows - 1, cols - 1), (2, 1, 0)):
                turned = pltpu.roll(values, by, 0).reshape(rows // cols, cols, lanes)
                turned = jnp.where(edge == gone, 0.0, turned).reshape(rows, lanes)
                dz_taps[i, :, pl.ds(c * lanes, lanes)] = turned.astype(BF16)
            dz_taps[i, :, pl.ds(lanes, lanes)] = dz_all[m, i]

    def kernel_row(m, r):
        part = jnp.zeros((block, 3 * lanes), F32)
        for i in range(2):
            left = jnp.concatenate([ut_all[m, i, q] for q in range(chips)], axis=1)
            part += jnp.dot(
                left, dz_taps[i, pl.ds((2 - r) * cols, px * (strips // 2)), :], preferred_element_type=F32
            )
        return part

    def add_gradients(m):
        gather_taps(m)
        for r in range(3):
            acc_v[r] = acc_v[r] + kernel_row(m, r)

    def forward(m):
        @pl.when(first)
        def _():
            in_copy(images, m).wait()
            argument_arrived(*input_parts(images, m))
            for g in range(groups):
                ub[m, group(g), :] = inside(g, inp[m, group(g), :])

        @pl.when(sec > 0)
        def _():
            @pl.when(m == 0)
            def _():
                for copy in affine_sends():
                    copy.wait_recv()

                @pl.when(decoder)
                def _():
                    argument_arrived(*mask_parts)

            wait_stats(zin_stat, fs_r, m)
            inv, offs = join(zin_stat, m)
            for k, value in enumerate((inv, *offs)):
                prev_coef[m, pl.ds(k, 1), :] = value
            joined_back(m, sec - 1).start()
            slant = 0.5 * inv * gain_prev[...]
            level = [slant * off + 0.5 * shift_prev[...] for off in offs]
            arrived(z_sends(m, sec))
            for g in range(groups):
                gate = jnp.concatenate([mask_v[m, group(g), :].astype(F32)] * (half // 128), axis=1)
                for h in range(2):
                    part = slice(h * half, (h + 1) * half)
                    halved = zin[m, h, group(g), :].astype(F32) * slant[:, part] + level[kind(g)][:, part]
                    turn = jnp.tanh(halved)
                    bent = halved * turn
                    ub[m, group(g), part] = inside(g, ((halved + bent) * gate).astype(BF16))
                    if kind(g) == 1:
                        slope_prev[m, pl.ds((g - 1) * cols, cols), part] = (0.5 + 0.5 * turn) * (1.0 + halved - bent)

        @pl.when(jnp.logical_not(late) & (m == 0))
        def _():
            for r in range(3):
                w_copy(r).wait()

        for h in range(2):
            part = pl.ds(h * half, half)
            parts = []
            for c in range(3):
                acc = jnp.zeros((px, half), F32)
                for r in range(3):
                    acc += jnp.dot(
                        ub[m, pl.ds(r * cols, px), :], w_v[r, pl.ds(c * ch, ch), part], preferred_element_type=F32
                    )
                parts.append(acc)
            conv = taps_joined(parts, 0, 2)
            mean = jnp.sum(conv, 0, keepdims=True) / local
            conv = conv - mean
            stat_out[m, pl.ds(0, 1), part] = mean
            stat_out[m, pl.ds(1, 1), part] = jnp.sum(conv * conv, 0, keepdims=True)
            zown[m, h, centre, :] = conv.astype(BF16)

            @pl.when(sec < sections - 1)
            def _():
                if h == 1:
                    start_stats(*down_stats, m, sec + 1, False)
                z_sends(m, sec + 1)[0](h).start()
                if h == 1:
                    each_edge(z_sends(m, sec + 1), start)

        @pl.when(last)
        def _():
            start_stats(*same_stats, m, sec, True)

        each_edge(own_edges(m), start)

    def finish(m):
        @pl.when(last)
        def _():
            wait_stats(own_stat, os_r, m)
            inv, offs = join(own_stat, m)
            for k, value in enumerate((inv, *offs)):
                own_coef[m, pl.ds(k, 1), :] = value

        @pl.when(jnp.logical_not(last))
        def _():
            joined_back(m, sec).wait_recv()

        inv = own_coef[m, pl.ds(0, 1), :]
        offs = [own_coef[m, pl.ds(1 + k, 1), :] for k in range(3)]
        scale = inv * gains[...]
        slant = 0.5 * scale
        level = [slant * off + 0.5 * shifts[...] for off in offs]
        edges_arrived(own_edges(m))

        @pl.when(last)
        def _():
            in_copy(cotangent, m).wait()
            argument_arrived(*input_parts(cotangent, m))
            for h in range(2):
                part = slice(h * half, (h + 1) * half)
                sums = jnp.zeros((cols, half), F32)
                cross = jnp.zeros((cols, half), F32)
                for g in range(groups):
                    z = zown[m, h, group(g), :].astype(F32)
                    halved = z * slant[:, part] + level[kind(g)][:, part]
                    turn = jnp.tanh(halved)
                    bent = halved * turn
                    dy = inp[m, group(g), part].astype(F32) * ((0.5 + 0.5 * turn) * (1.0 + halved - bent))
                    dyin[m, h, group(g), :] = dy.astype(BF16)
                    if kind(g) == 1:
                        out_v[m, pl.ds((g - 1) * cols, cols), part] = (halved + bent).astype(BF16)
                        sums += dy
                        cross += dy * z
                one = jnp.sum(sums, 0, keepdims=True)
                cross = jnp.sum(cross, 0, keepdims=True)
                seed_sums[m, pl.ds(0, 1), part] = one
                seed_sums[m, pl.ds(1, 1), part] = inv[:, part] * (cross + offs[1][:, part] * one)
            start_stats(*seed_stats, m, sec, True)

        @pl.when(jnp.logical_not(last))
        def _():
            for h in range(2):
                part = slice(h * half, (h + 1) * half)
                for g in range(1, groups - 1):
                    halved = zown[m, h, group(g), :].astype(F32) * slant[:, part] + level[1][:, part]
                    out_v[m, pl.ds((g - 1) * cols, cols), part] = (halved + halved * jnp.tanh(halved)).astype(BF16)

        for copy in result_copies(out_v, outs, out_sem, po_s, po_r, m):
            copy.start()

    def result_copies(src, dst, sem, send, recv, m):
        here, there = pl.multiple_of(strip * core, cols), pl.multiple_of(strip * (1 - core), cols)
        return (
            pltpu.make_async_copy(src.at[m, pl.ds(here, strip), :], dst.at[m, core], sem.at[m]),
            remote(src.at[m, pl.ds(there, strip), :], dst.at[m, core], send.at[m], recv.at[m], sec, partner),
        )

    def backward(m):
        wait_stats(dy_stat, bs_r, m)
        first_sum = jnp.sum(dy_stat[m, :, 0, :], 0, keepdims=True)
        cross_sum = jnp.sum(dy_stat[m, :, 1, :], 0, keepdims=True)
        shift_sum[...] += first_sum
        gain_sum[...] += cross_sum
        inv = own_coef[m, pl.ds(0, 1), :]
        scale = inv * gains[...]
        tilt = scale * inv * (cross_sum / total)
        base = [scale * (first_sum / total) + tilt * own_coef[m, pl.ds(1 + k, 1), :] for k in range(3)]

        @pl.when(sec < sections - 1)
        def _():
            arrived(dy_sends(m, sec))

        for g in range(groups):
            for h in range(2):
                part = slice(h * half, (h + 1) * half)
                dz = dyin[m, h, group(g), :].astype(F32) * scale[:, part]
                dz = dz - zown[m, h, group(g), :].astype(F32) * tilt[:, part] - base[kind(g)][:, part]
                dz = inside(g, dz.astype(BF16))
                dzb[m, group(g), part] = dz
                if kind(g) == 1:
                    for k in range(half // lanes):
                        dz_out[m, h * (half // lanes) + k, pl.ds((g - 1) * cols, cols), :] = dz[
                            :, k * lanes : (k + 1) * lanes
                        ]

        @pl.when(first)
        def _():
            send_dz(m)

        for h in range(2):
            part = pl.ds(h * half, half)
            parts = []
            for c in range(3):
                acc = jnp.zeros((px, half), F32)
                for r in range(3):
                    acc += jnp.dot(
                        dzb[m, pl.ds((2 - r) * cols, px), :], wt_v[r, pl.ds(c * ch, ch), part],
                        preferred_element_type=F32,
                    )
                parts.append(acc)
            gate = jnp.concatenate([mask_v[m, centre, :].astype(F32)] * (half // 128), axis=1)
            du = (taps_joined(parts, 2, 0) * gate).astype(BF16)
            gin_v[m, :, part] = du

            @pl.when(sec > 0)
            def _():
                dy = du.astype(F32) * slope_prev[m, :, part]
                dyout[m, h] = dy.astype(BF16)
                one = jnp.sum(dy, 0, keepdims=True)
                cross = jnp.sum(dy * zin[m, h, centre, :].astype(F32), 0, keepdims=True)
                sums_out[m, pl.ds(0, 1), part] = one
                sums_out[m, pl.ds(1, 1), part] = prev_coef[m, pl.ds(0, 1), part] * (
                    cross + prev_coef[m, pl.ds(2, 1), part] * one
                )
                if h == 1:
                    start_stats(*back_stats, m, sec - 1, False)
                dy_sends(m, sec - 1)[0](h).start()
                if h == 1:
                    each_edge(dy_sends(m, sec - 1), start)

        for copy in result_copies(gin_v, grads_in, gin_sem, pg_s, pg_r, m):
            copy.start()

        @pl.when((sec > 0) & (sec < sections - 1))
        def _():
            send_dz(m)

    def turn_weights():
        def one(i, carry):
            at = pl.ds(pl.multiple_of(lax.rem(i, 3) * ch, ch), ch)
            wt_v[lax.div(i, 3), at, :] = w_v[lax.div(i, 3), at, :].T
            return carry
        lax.fori_loop(0, 9, one, 0)

    @pl.when(late)
    def _():
        for r in range(3):
            w_copy(r).wait()
        turn_weights()

    def step(t, carry):
        ahead = t - sec
        behind = t - (2 * sections - 1 - sec)

        @pl.when((ahead >= 0) & (ahead < batches))
        def _():
            forward(ahead)

        @pl.when(jnp.logical_not(late) & (ahead == batches))
        def _():
            send_turned()
            turn_weights()

        done = ahead - jnp.where(last, 0, 2)

        @pl.when((behind >= 0) & (behind < batches))
        def _():
            backward(behind)

        @pl.when((done >= 0) & (done < batches))
        def _():
            finish(done)

        @pl.when(jnp.logical_not(late) & (ahead == batches + 1))
        def _():
            def relay(m, carry):
                relay_turned(m)
                return carry
            lax.fori_loop(0, batches, relay, 0)

        @pl.when((behind >= 1) & (behind < batches) & jnp.logical_not(late))
        def _():
            add_gradients(behind - 1)

        return carry

    lax.fori_loop(0, 2 * sections - 1 + batches, step, 0)

    @pl.when(late)
    def _():
        send_turned()

    @pl.when(last)
    def _():
        def send(m, carry):
            send_dz(m)
            return carry

        lax.fori_loop(0, batches, send, 0)

    @pl.when(late)
    def _():
        def relay(m, carry):
            relay_turned(m)
            return carry

        def add(m, carry):
            add_gradients(m)
            return carry

        lax.fori_loop(0, batches, relay, 0)
        lax.fori_loop(0, batches - 1, add, 0)

    def swap(r, d):
        other = (seat + d) % 4
        return remote(
            swap_out.at[r, pl.ds(pl.multiple_of(other * share, share), share), :], swap_in.at[r, 4 - d - 1],
            sw_s.at[r, d - 1], sw_r.at[r, 4 - d - 1], sec, 4 * team + other,
        )

    gather_taps(batches - 1)
    for r in range(3):
        part = acc_v[r] + kernel_row(batches - 1, r)
        acc_v[r] = part
        swap_out[r] = part.astype(BF16)
        for d in range(1, 4):
            swap(r, d).start()

    def dw_copy(r):
        return pltpu.make_async_copy(dw_v.at[r], weight_grad.at[r], dw_sem.at[r])

    own_rows = pl.ds(pl.multiple_of(seat * share, share), share)
    for r in range(3):
        for c in range(3):
            dw_v[r, c, :, pl.ds(pl.multiple_of(seat * lanes, lanes), lanes)] = acc_v[r, own_rows, pl.ds(c * lanes, lanes)]
        for d in range(1, 4):
            swap(r, 4 - d).wait_recv()
            source = (seat + d) % 4
            for c in range(3):
                dw_v[r, c, :, pl.ds(pl.multiple_of(source * lanes, lanes), lanes)] = swap_in[
                    r, d - 1, :, pl.ds(c * lanes, lanes)
                ].astype(F32)
        dw_copy(r).start()

    for r in range(3):
        dw_copy(r).wait()
        for d in range(1, 4):
            swap(r, d).wait_send()

    @pl.when(decoder)
    def _():
        argument_sent(*mask_parts)

    @pl.when(sec < sections - 1)
    def _():
        for copy in affine_sends():
            copy.wait_send()

    def drain(m, carry):
        for src, dst, sems in ((out_v, outs, (out_sem, po_s, po_r)), (gin_v, grads_in, (gin_sem, pg_s, pg_r))):
            here, there = result_copies(src, dst, *sems, m)
            here.wait()
            there.wait_send()
            remote(
                src.at[m, pl.ds(0, strip), :], dst.at[m, 1 - core], sems[1].at[m], sems[2].at[m], sec, partner
            ).wait_recv()

        turned_each(m, sent)
        turned_relay(m).wait_send()
        dz_each(m, sent)

        @pl.when(first)
        def _():
            argument_sent(*input_parts(images, m))

        @pl.when(last)
        def _():
            argument_sent(*input_parts(cotangent, m))
            stats_each(*seed_stats, m, sec, True, sent)
            stats_each(*same_stats, m, sec, True, sent)

        @pl.when(sec < sections - 1)
        def _():
            stats_each(*down_stats, m, sec + 1, False, sent)
            all_sent(z_sends(m, sec + 1))

        each_edge(own_edges(m), sent)

        @pl.when(sec > 0)
        def _():
            stats_each(*back_stats, m, sec - 1, False, sent)
            all_sent(dy_sends(m, sec - 1))
            joined_back(m, sec - 1).wait_send()

        return carry

    lax.fori_loop(0, batches, drain, 0)


def settle(*refs):
    count = (len(refs) - 2) // 3
    sources, targets, stages = refs[:count], refs[count : 2 * count], refs[2 * count : 3 * count]
    moves = []
    for src, dst, stage in zip(sources, targets, stages):
        if len(src.shape) == 2:
            moves.append((src, dst, stage))
        else:
            moves += [(src.at[i], dst.at[i], stage.at[i]) for i in range(src.shape[0])]
    ins = [pltpu.make_async_copy(src, stage, refs[-2].at[i]) for i, (src, dst, stage) in enumerate(moves)]
    outs = [pltpu.make_async_copy(stage, dst, refs[-1].at[i]) for i, (src, dst, stage) in enumerate(moves)]
    for copy in ins:
        copy.start()
    for come, go in zip(ins, outs):
        come.wait()
        go.start()
    for copy in outs:
        copy.wait()


def body(images, switches, conv_weights, gains, shifts, cotangent):
    sections = lax.axis_size("section")
    strips = lax.axis_size("rows")
    batches, pictures, strip_rows, cols, ch = images.shape
    strip = strip_rows * cols
    px = 2 * strip
    tall = px + 2 * cols
    anywhere = pl.BlockSpec(memory_space=pl.ANY)
    vmem = pl.BlockSpec(memory_space=pltpu.VMEM)
    dma = pltpu.SemaphoreType.DMA
    flops = 3 * 2 * 9 * ch * ch * batches * px
    share = ch // strips
    outs, grads_in, weight_grad, gain_sum, shift_sum = pl.pallas_call(
        functools.partial(kernel, sections, strips, cols),
        out_shape=(
            jax.ShapeDtypeStruct((batches, pictures, strip, ch), BF16),
            jax.ShapeDtypeStruct((batches, pictures, strip, ch), BF16),
            jax.ShapeDtypeStruct((3, 3, share, ch), F32),
            jax.ShapeDtypeStruct((1, ch), F32),
            jax.ShapeDtypeStruct((1, ch), F32),
        ),
        in_specs=[anywhere, anywhere, anywhere, vmem, vmem, vmem],
        out_specs=(anywhere, anywhere, anywhere, vmem, vmem),
        scratch_shapes=[
            pltpu.VMEM((3, 3 * ch, ch), BF16),
            pltpu.VMEM((3, 3 * ch, ch), BF16),
            pltpu.VMEM((batches, tall, ch), BF16),
            pltpu.VMEM((batches, 2, strip, 128), BF16),
            pltpu.VMEM((batches, tall, 128), BF16),
            pltpu.VMEM((1, ch), F32),
            pltpu.VMEM((1, ch), F32),
            pltpu.VMEM((batches, 2, tall, ch // 2), BF16),
            pltpu.VMEM((batches, strips, 2, ch), F32),
            pltpu.VMEM((batches, 2, tall, ch // 2), BF16),
            pltpu.VMEM((batches, strips, 2, ch), F32),
            pltpu.VMEM((batches, tall, ch), BF16),
            pltpu.VMEM((batches, px, ch), F32),
            pltpu.VMEM((batches, 4, ch), F32),
            pltpu.VMEM((batches, 4, ch), F32),
            pltpu.VMEM((batches, 2, tall, ch // 2), BF16),
            pltpu.VMEM((batches, strips, 2, ch), F32),
            pltpu.VMEM((batches, tall, ch), BF16),
            pltpu.VMEM((batches, 4, px, ch // 4), BF16),
            pltpu.VMEM((batches, 2, px, ch // 2), BF16),
            pltpu.VMEM((batches, 2, ch), F32),
            pltpu.VMEM((batches, 2, ch), F32),
            pltpu.VMEM((batches, 2, ch), F32),
            pltpu.VMEM((batches, px, ch), BF16),
            pltpu.VMEM((batches, px, ch), BF16),
            pltpu.VMEM((batches, ch, px), BF16),
            pltpu.VMEM((batches, 2, strips // 2, 4 * share, px), BF16),
            pltpu.VMEM((batches, 2, px * strips // 2 + 2 * cols, ch // 4), BF16),
            pltpu.VMEM((2, px * strips // 2 + 2 * cols, 3 * ch // 4), BF16),
            pltpu.VMEM((3, 4 * share, 3 * ch // 4), F32),
            pltpu.VMEM((3, 4 * share, 3 * ch // 4), BF16),
            pltpu.VMEM((3, 3, share, 3 * ch // 4), BF16),
            pltpu.VMEM((3, 3, share, ch), F32),
            dma((3,)),
            dma((batches,)),
            dma((batches,)), dma((batches,)),
            dma((batches, 2)), dma((batches, 2)),
            dma, dma,
            dma((2,)), dma((2,)),
            dma((2,)), dma((2,)),
            dma((batches, 4)), dma((batches, 4)),
            dma((batches, strips)), dma((batches,)),
            dma((batches, 4)), dma((batches, 4)),
            dma((batches, strips)), dma((batches,)),
            dma((batches, 4)), dma((batches, 4)),
            dma((batches, strips)), dma((batches,)),
            dma((batches, strips)),
            dma((batches,)), dma((batches,)),
            dma((batches,)), dma((batches,)), dma((batches,)),
            dma((batches,)), dma((batches,)), dma((batches,)),
            dma((batches, strips // 2)), dma((batches, strips // 2)),
            dma((batches,)), dma((batches,)),
            dma((batches, strips)), dma((batches, strips)),
            dma((3, 3)), dma((3, 3)),
            dma((3,)),
        ],
        compiler_params=pltpu.CompilerParams(
            collective_id=0, has_side_effects=True, vmem_limit_bytes=56 * 2**20
        ),
        cost_estimate=pl.CostEstimate(
            flops=flops, bytes_accessed=2 * 9 * ch * ch * 2, transcendentals=0
        ),
    )(
        images.reshape(batches, pictures, strip, ch),
        cotangent.reshape(batches, pictures, strip, ch),
        conv_weights.reshape(3, 3 * ch, ch),
        gains,
        shifts,
        switches.reshape(-1, switches.shape[-1]),
    )
    results = (outs, grads_in, weight_grad, gain_sum, shift_sum)
    outs, grads_in, weight_grad, gain_sum, shift_sum = pl.pallas_call(
        settle,
        out_shape=tuple(jax.ShapeDtypeStruct(r.shape, r.dtype) for r in results),
        in_specs=[anywhere] * 5,
        out_specs=(anywhere,) * 5,
        scratch_shapes=[pltpu.VMEM(r.shape, r.dtype) for r in results] + [dma((2 * batches + 5,))] * 2,
        compiler_params=pltpu.CompilerParams(vmem_limit_bytes=60 * 2**20),
    )(*results)
    shape = (1, batches, pictures, strip_rows, cols, ch)
    return (outs.reshape(shape), grads_in.reshape(shape), weight_grad[None], gain_sum, shift_sum)


def solution(mesh):
    return jax.shard_map(
        body,
        mesh=mesh,
        in_specs=(
            P(None, None, "rows", None, None),
            P(None, None, "rows", None),
            P("section", None, None, None, None),
            P("section", None),
            P("section", None),
            P(None, None, "rows", None, None),
        ),
        out_specs=(
            P("section", None, None, "rows", None, None),
            P("section", None, None, "rows", None, None),
            P("section", None, None, "rows", None),
            P("section", None),
            P("section", None),
        ),
        check_vma=False,
    )
```

```python
import functools

import jax
import jax.numpy as jnp
from jax import lax
from jax.experimental import pallas as pl
from jax.experimental.pallas import tpu as pltpu
from jax.sharding import PartitionSpec as P

EPSILON = 1e-05
MESH = pl.DeviceIdType.MESH
BF16 = jnp.bfloat16
F32 = jnp.float32


def kernel(
    sections, strips, cols,
    images, cotangent, weights, gains, shifts, switches,
    outs, grads_in, weight_grad, gain_sum, shift_sum,
    w_v, wt_v, inp, mask_own, mask_v, gain_prev, shift_prev, zin, zin_stat, zown, own_stat, ub, slope_prev,
    prev_coef, own_coef, dyin, dy_stat, dzb, dyout, product_v, sums_v, stat_out, sums_out, seed_sums, out_v, gin_v,
    ut_own, ut_all, dz_all, dz_taps, acc_v, swap_out, swap_in, dw_v,
    w_sem, wt_sem, in_sem, pi_s, pi_r, ie_s, ie_r, mp_s, mp_r, me_s, me_r, gp_s, gp_r,
    ux_s, ux_r, dx_s, dx_r, sv_s, sv_r,
    fz_s, fz_r, fs_s, fs_r, oe_s, oe_r, os_s, os_r, bz_s, bz_r, bs_s, bs_r, ls_s,
    out_sem, po_s, po_r, gin_sem, pg_s, pg_r,
    ut_s, ut_r, uf_s, uf_r, dz_s, dz_r, sw_s, sw_r, dw_sem,
):
    sec = lax.axis_index("section")
    row = lax.axis_index("rows")
    batches, _, tall, half = inp.shape
    ch = 2 * half
    px = tall - 2 * cols
    strip = px // 2
    groups = tall // cols
    chips = strips // 2
    local = float(2 * px)
    total = local * chips
    first, last, decoder = sec == 0, sec == sections - 1, sec == sections // 2
    late = sec >= sections // 2
    core = row % 2
    partner = row + 1 - 2 * core
    has_up, has_down = row >= 2, row < strips - 2
    centre = pl.ds(cols, px)
    chip = row // 2
    team, seat = row // 4, row % 4
    lanes = dz_all.shape[3]
    block = ut_all.shape[3]
    share = block // 4
    mine = pl.multiple_of(cols + strip * core, cols)

    def channels(h):
        return pl.ds(pl.multiple_of(h * half, half), half)

    def w_copies():
        return [
            pltpu.make_async_copy(weights.at[:, channels(h), channels(core)], w_v.at[h], w_sem.at[h]) for h in range(2)
        ]

    def wt_copies():
        return [
            pltpu.make_async_copy(weights.at[:, channels(core), channels(h)], wt_v.at[h], wt_sem.at[h]) for h in range(2)
        ]

    def in_copy(src, m):
        return pltpu.make_async_copy(src.at[m, :, :, channels(core)], inp.at[m, :, pl.ds(mine, strip), :], in_sem.at[m])

    for copy in w_copies() + wt_copies():
        copy.start()

    @pl.when(first)
    def _():
        for m in range(batches):
            in_copy(images, m).start()

    @pl.when(last)
    def _():
        for m in range(batches):
            in_copy(cotangent, m).start()

    barrier = pltpu.get_barrier_semaphore()
    for s in range(sections):
        @pl.when((sec >= s - 1) & (sec <= s + 1))
        def _():
            def greet(i, carry):
                @pl.when((s != sec) | (i != row))
                def _():
                    pl.semaphore_signal(barrier, inc=1, device_id=(jnp.int32(s), i), device_id_type=MESH)
                return carry
            lax.fori_loop(0, strips, greet, 0)

    acc_v[...] = jnp.zeros_like(acc_v)
    sums_v[...] = jnp.zeros_like(sums_v)

    for m in range(batches):
        for i in range(2):
            for at in (0, dz_all.shape[2] - cols):
                dz_all[m, i, pl.ds(at, cols), :] = jnp.zeros((cols, lanes), BF16)

    @pl.when(decoder)
    def _():
        wide = cols // 2
        windows_at = lax.broadcasted_iota(jnp.int32, (cols, wide), 1)
        places = lax.broadcasted_iota(jnp.int32, (cols, wide), 0)
        pick = (lax.shift_right_logical(places, 1) == windows_at).astype(F32)
        table = lax.dot_general(
            pick, switches[...].astype(F32), (((1,), (1,)), ((), ())), preferred_element_type=F32
        )
        odd = jnp.bitwise_and(lax.broadcasted_iota(jnp.int32, (cols, 128), 0), 1).astype(F32)
        windows = strip // cols // 2
        for m in range(batches):
            for i in range(2):
                for w in range(windows):
                    at = (m * 2 + i) * windows + w
                    value = jnp.broadcast_to(table[:, at : at + 1], (cols, 128))
                    for p in range(2):
                        hit = (jnp.abs(value - (2.0 * p + odd)) < 0.5).astype(F32).astype(BF16)
                        mask_own[m, i, pl.ds((2 * w + p) * cols, cols), :] = hit
        for m in range(batches):
            mask_v[m, :, pl.ds(mine, strip), :] = mask_own[m]

    @pl.when(jnp.logical_not(decoder))
    def _():
        mask_v[...] = jnp.ones_like(mask_v)

    near = 1 + jnp.where(sec > 0, 1, 0) + jnp.where(sec < sections - 1, 1, 0)
    pl.semaphore_wait(barrier, near * strips - 1)

    def remote(src, dst, send, recv, s, i):
        return pltpu.make_async_remote_copy(
            src_ref=src, dst_ref=dst, send_sem=send, recv_sem=recv, device_id=(s, i), device_id_type=MESH
        )

    def to_partner(src_at, dst_at, send, recv):
        return remote(src_at(1 - core), dst_at(pl.ds(mine, strip)), send, recv, sec, partner)

    def start_argument(src_at, dst_at, pair_sems, edge_sems):
        to_partner(src_at, dst_at, *pair_sems).start()

        @pl.when((core == 1) & has_down)
        def _():
            for i in range(2):
                remote(
                    src_at(i, pl.ds(strip - cols, cols)), dst_at(pl.ds(0, cols)),
                    edge_sems[0].at[i], edge_sems[1].at[0], sec, row + 1 + i,
                ).start()

        @pl.when((core == 0) & has_up)
        def _():
            for i in range(2):
                remote(
                    src_at(i, pl.ds(0, cols)), dst_at(pl.ds(cols + px, cols)),
                    edge_sems[0].at[i], edge_sems[1].at[1], sec, row - 2 + i,
                ).start()

    def argument_arrived(src_at, dst_at, pair_sems, edge_sems):
        to_partner(src_at, dst_at, *pair_sems).wait_recv()

        @pl.when(has_up)
        def _():
            remote(
                src_at(0, pl.ds(0, cols)), dst_at(pl.ds(0, cols)), edge_sems[0].at[0], edge_sems[1].at[0], sec, row
            ).wait_recv()

        @pl.when(has_down)
        def _():
            remote(
                src_at(0, pl.ds(0, cols)), dst_at(pl.ds(cols + px, cols)), edge_sems[0].at[0], edge_sems[1].at[1],
                sec, row,
            ).wait_recv()

    def argument_sent(src_at, dst_at, pair_sems, edge_sems):
        to_partner(src_at, dst_at, *pair_sems).wait_send()

        @pl.when(((core == 1) & has_down) | ((core == 0) & has_up))
        def _():
            for i in range(2):
                remote(
                    src_at(i, pl.ds(0, cols)), dst_at(pl.ds(0, cols)), edge_sems[0].at[i], edge_sems[1].at[0], sec, row
                ).wait_send()

    def input_parts(src, m):
        return (
            lambda i, r=pl.ds(0, strip): src.at[m, :, r, channels(i)],
            lambda r: inp.at[m, :, r, :],
            (pi_s.at[m], pi_r.at[m]),
            (ie_s.at[m], ie_r.at[m]),
        )

    mask_parts = (
        lambda i, r=pl.ds(0, strip): mask_own.at[:, :, r, :],
        lambda r: mask_v.at[:, :, r, :],
        (mp_s, mp_r),
        (me_s, me_r),
    )

    @pl.when(first)
    def _():
        for m in range(batches):
            start_argument(*input_parts(images, m))

    @pl.when(last)
    def _():
        for m in range(batches):
            start_argument(*input_parts(cotangent, m))

    @pl.when(decoder)
    def _():
        start_argument(*mask_parts)

    def affine_sends():
        return (
            remote(gains, gain_prev, gp_s.at[0], gp_r.at[0], sec + 1, row),
            remote(shifts, shift_prev, gp_s.at[1], gp_r.at[1], sec + 1, row),
        )

    @pl.when(sec < sections - 1)
    def _():
        for copy in affine_sends():
            copy.start()

    def block_sends(src, src_from, dst, send, recv, m, s):
        def body(i):
            return remote(
                src.at[m, i, pl.ds(src_from, px), :], dst.at[m, i, centre, :], send.at[m, i], recv.at[m, i], s, row
            )

        def edge(e, src_row, dst_row, i):
            return remote(
                src.at[m, :, pl.ds(src_from + src_row, cols), :], dst.at[m, :, pl.ds(dst_row, cols), :],
                send.at[m, 2 + e], recv.at[m, 2 + e], s, i,
            )

        return body, lambda: edge(0, px - cols, 0, row + 2), lambda: edge(1, 0, cols + px, row - 2)

    def each_edge(parts, act):
        _, to_down, to_up = parts

        @pl.when(has_down)
        def _():
            act(to_down())

        @pl.when(has_up)
        def _():
            act(to_up())

    def edges_arrived(parts):
        _, to_down, to_up = parts

        @pl.when(has_up)
        def _():
            to_down().wait_recv()

        @pl.when(has_down)
        def _():
            to_up().wait_recv()

    def send_block(parts):
        each_edge(parts, start)
        for i in range(2):
            parts[0](i).start()

    def block_sent(parts):
        each_edge(parts, sent)
        for i in range(2):
            parts[0](i).wait_send()

    def start(copy):
        copy.start()

    def sent(copy):
        copy.wait_send()

    def came(copy):
        copy.wait_recv()

    def z_sends(m, s):
        return block_sends(zown, cols, zin, fz_s, fz_r, m, s)

    def own_edges(m):
        return block_sends(zown, cols, zown, oe_s, oe_r, m, sec)

    def dy_sends(m, s):
        return block_sends(dyout, 0, dyin, bz_s, bz_r, m, s)

    def stats_each(src, dst, send, recv, m, s, same, act):
        def one(d, carry):
            q = chip + d
            q = jnp.where(q >= chips, q - chips, q)
            act(remote(src.at[m], dst.at[m, chip], send.at[m, d], recv.at[m, d], s, 2 * q + core))
            return carry
        lax.fori_loop(1 if same else 0, chips, one, 0)

    def start_stats(src, dst, send, recv, m, s, same):
        stats_each(src, dst, send, recv, m, s, same, start)
        if same:
            dst[m, chip] = src[m]

    def wait_stats(src, dst, send, recv, m, same):
        stats_each(src, dst, send, recv, m, sec, same, came)

    down_stats = (stat_out, zin_stat, fs_s, fs_r)
    same_stats = (stat_out, own_stat, os_s, os_r)
    back_stats = (sums_out, dy_stat, bs_s, bs_r)
    seed_stats = (seed_sums, dy_stat, ls_s, bs_r)

    def join(stats_ref, m):
        means, squares = stats_ref[m, :, 0, :], stats_ref[m, :, 1, :]
        mean = jnp.sum(means, 0, keepdims=True) / float(chips)
        off = means - mean
        var = (jnp.sum(squares, 0, keepdims=True) + local * jnp.sum(off * off, 0, keepdims=True)) / total
        at = (jnp.maximum(chip - 1, 0), chip, jnp.minimum(chip + 1, chips - 1))
        return lax.rsqrt(var + EPSILON), [stats_ref[m, i, pl.ds(0, 1), :] - mean for i in at]

    def kind(g):
        return 0 if g == 0 else 2 if g == groups - 1 else 1

    def inside(g, values):
        if kind(g) == 1:
            return values
        return jnp.where(has_up if kind(g) == 0 else has_down, values, jnp.zeros_like(values))

    def group(g):
        return pl.ds(g * cols, cols)

    column = lax.broadcasted_iota(jnp.int32, (1, cols, half), 1)

    def taps_joined(parts, left, right):
        def moved(values, by, edge):
            turned = pltpu.roll(values, by % (2 * px), 0).reshape(2 * px // cols, cols, half)
            return jnp.where(column == edge, 0.0, turned).reshape(2 * px, half)
        return parts[1] + moved(parts[left], 1, 0) + moved(parts[right], -1, cols - 1)

    def pass_on(operand, send, recv, m, i):
        return remote(operand.at[m, core, i], operand.at[m, core, i], send.at[m, i], recv.at[m, i], sec, partner)

    def products(operand, w, m, h, r_at):
        def one(c):
            acc = jnp.zeros((2 * px, half), F32)
            for r in range(3):
                left = operand[m, h, :, pl.ds(r_at(r) * cols, px), :].reshape(2 * px, half)
                acc += jnp.dot(left, w[h, 3 * r + c], preferred_element_type=F32)
            return acc
        return one

    def convolve(operand, w, send, recv, m, r_at, before_second=None):
        mine_first = products(operand, w, m, core, r_at)
        for c in range(3):
            product_v[c] = mine_first(c)
        for i in range(2):
            pass_on(operand, send, recv, m, i).wait_recv()
        if before_second is not None:
            before_second()
        then = products(operand, w, m, 1 - core, r_at)
        return [product_v[c] + then(c) for c in range(3)]

    def turned_copy(m, q):
        src = ut_own.at[m, pl.ds(pl.multiple_of((q // 2) * block, block), block), :]
        return src, ut_all.at[m, core, chip]

    thirds = [1 + (chips - 1) * i // 3 for i in range(4)]

    def turned_each(m, act, low=1, high=chips):
        def one(d, carry):
            q = chip + d
            q = jnp.where(q >= chips, q - chips, q)
            src, dst = turned_copy(m, q)
            act(remote(src, dst, ut_s.at[m, d], ut_r.at[m, d], sec, 2 * q + core))
            return carry
        lax.fori_loop(low, high, one, 0)

    def turn_inputs(m):
        for h in range(2):
            ut_own[m, pl.ds(h * half, half), :] = ub[m, h, core, centre, :].T
        mine_at = pl.ds(pl.multiple_of(team * block, block), block)
        ut_all[m, core, chip] = ut_own[m, mine_at, :]

    def send_turned_third(m, i):
        @pl.when(late & (m >= 0) & (m < batches))
        def _():
            if i == 0:
                turn_inputs(m)
            turned_each(m, start, thirds[i], thirds[i + 1])

    def turned_relay(m):
        return remote(ut_all.at[m, core], ut_all.at[m, core], uf_s.at[m], uf_r.at[m], sec, partner)

    def relay_turned(m):
        turned_each(m, came)
        turned_relay(m).start()

    def dz_copy(m, i):
        src = dzb.at[m, (i % 4) // 2, core, centre, pl.ds(pl.multiple_of(i % 2 * lanes, lanes), lanes)]
        dst = dz_all.at[m, core, pl.ds(pl.multiple_of(cols + chip * px, cols), px), :]
        return src, dst

    def dz_each(m, act):
        def one(d, carry):
            i = row + d
            i = jnp.where(i >= strips, i - strips, i)
            src, dst = dz_copy(m, i)
            act(remote(src, dst, dz_s.at[m, d], dz_r.at[m, d], sec, i))
            return carry
        lax.fori_loop(1, strips, one, 0)

    def send_dz(m):
        dz_each(m, start)
        dz_all[m, core, pl.ds(pl.multiple_of(cols + chip * px, cols), px), :] = dzb[
            m, seat // 2, core, centre, pl.ds(pl.multiple_of(seat % 2 * lanes, lanes), lanes)
        ]

    def gather_taps(m):
        dz_each(m, came)
        relayed = ut_all.at[m, 1 - core]
        pltpu.make_async_copy(relayed, relayed, uf_r.at[m]).wait()
        rows = dz_all.shape[2]
        edge = lax.broadcasted_iota(jnp.int32, (1, cols, lanes), 1)
        for i in range(2):
            values = dz_all[m, i].astype(F32)
            for c, by, gone in ((0, rows - 1, cols - 1), (2, 1, 0)):
                turned = pltpu.roll(values, by, 0).reshape(rows // cols, cols, lanes)
                turned = jnp.where(edge == gone, 0.0, turned).reshape(rows, lanes)
                dz_taps[i, :, pl.ds(c * lanes, lanes)] = turned.astype(BF16)
            dz_taps[i, :, pl.ds(lanes, lanes)] = dz_all[m, i]

    def kernel_row(m, r):
        part = jnp.zeros((block, 3 * lanes), F32)
        for i in range(2):
            left = jnp.concatenate([ut_all[m, i, q] for q in range(chips)], axis=1)
            part += jnp.dot(
                left, dz_taps[i, pl.ds((2 - r) * cols, px * (strips // 2)), :], preferred_element_type=F32
            )
        return part

    def add_gradients(m):
        gather_taps(m)
        for r in range(3):
            acc_v[r] = acc_v[r] + kernel_row(m, r)

    def forward(m):
        @pl.when(first)
        def _():
            in_copy(images, m).wait()
            argument_arrived(*input_parts(images, m))
            for i in range(2):
                for g in range(groups):
                    ub[m, core, i, group(g), :] = inside(g, inp[m, i, group(g), :])
                pass_on(ub, ux_s, ux_r, m, i).start()

        @pl.when(sec > 0)
        def _():
            @pl.when(m == 0)
            def _():
                for copy in affine_sends():
                    copy.wait_recv()

                @pl.when(decoder)
                def _():
                    argument_arrived(*mask_parts)

            wait_stats(*down_stats, m, False)
            inv, offs = join(zin_stat, m)
            prev_coef[m, pl.ds(0, 1), :] = inv
            prev_coef[m, pl.ds(1, 1), :] = offs[1]
            slant = 0.5 * inv * gain_prev[:, channels(core)]
            level = [slant * off + 0.5 * shift_prev[:, channels(core)] for off in offs]
            sends = z_sends(m, sec)
            edges_arrived(sends)
            for i in range(2):
                sends[0](i).wait_recv()
                for g in range(groups):
                    gate = jnp.concatenate([mask_v[m, i, group(g), :].astype(F32)] * (half // 128), axis=1)
                    halved = zin[m, i, group(g), :].astype(F32) * slant + level[kind(g)]
                    turn = jnp.tanh(halved)
                    bent = halved * turn
                    ub[m, core, i, group(g), :] = inside(g, ((halved + bent) * gate).astype(BF16))
                    if kind(g) == 1:
                        slope_prev[m, i, pl.ds((g - 1) * cols, cols), :] = (0.5 + 0.5 * turn) * (1.0 + halved - bent)
                pass_on(ub, ux_s, ux_r, m, i).start()

        @pl.when(m == 0)
        def _():
            for copy in w_copies():
                copy.wait()

        conv = taps_joined(convolve(ub, w_v, ux_s, ux_r, m, lambda r: r), 0, 2)
        mean = jnp.sum(conv, 0, keepdims=True) / local
        conv = conv - mean
        stat_out[m, pl.ds(0, 1), :] = mean
        stat_out[m, pl.ds(1, 1), :] = jnp.sum(conv * conv, 0, keepdims=True)
        zown[m, :, centre, :] = conv.reshape(2, px, half).astype(BF16)

        @pl.when(sec < sections - 1)
        def _():
            start_stats(*down_stats, m, sec + 1, False)
            send_block(z_sends(m, sec + 1))

        start_stats(*same_stats, m, sec, True)
        each_edge(own_edges(m), start)

    def finish(m):
        wait_stats(*same_stats, m, True)
        inv, offs = join(own_stat, m)
        scale = inv * gains[:, channels(core)]
        own_coef[m, pl.ds(0, 1), :] = inv
        own_coef[m, pl.ds(1, 1), :] = scale
        for e in range(3):
            own_coef[m, pl.ds(2 + e, 1), :] = offs[e]
        slant = 0.5 * scale
        level = [slant * off + 0.5 * shifts[:, channels(core)] for off in offs]
        edges_arrived(own_edges(m))

        @pl.when(last)
        def _():
            in_copy(cotangent, m).wait()
            argument_arrived(*input_parts(cotangent, m))
            sums = jnp.zeros((cols, half), F32)
            cross = jnp.zeros((cols, half), F32)
            for i in range(2):
                for g in range(groups):
                    z = zown[m, i, group(g), :].astype(F32)
                    halved = z * slant + level[kind(g)]
                    turn = jnp.tanh(halved)
                    bent = halved * turn
                    dy = inp[m, i, group(g), :].astype(F32) * ((0.5 + 0.5 * turn) * (1.0 + halved - bent))
                    dyin[m, i, group(g), :] = dy.astype(BF16)
                    if kind(g) == 1:
                        out_v[m, i, pl.ds((g - 1) * cols, cols), :] = (halved + bent).astype(BF16)
                        sums += dy
                        cross += dy * z
            one = jnp.sum(sums, 0, keepdims=True)
            cross = jnp.sum(cross, 0, keepdims=True)
            seed_sums[m, pl.ds(0, 1), :] = one
            seed_sums[m, pl.ds(1, 1), :] = inv * (cross + offs[1] * one)
            start_stats(*seed_stats, m, sec, True)

        @pl.when(jnp.logical_not(last))
        def _():
            for i in range(2):
                for g in range(1, groups - 1):
                    halved = zown[m, i, group(g), :].astype(F32) * slant + level[1]
                    out_v[m, i, pl.ds((g - 1) * cols, cols), :] = (halved + halved * jnp.tanh(halved)).astype(BF16)

        for copy in result_copies(out_v, outs, out_sem, po_s, po_r, m):
            copy.start()

    def result_copies(src, dst, sem, send, recv, m):
        here, there = pl.multiple_of(strip * core, cols), pl.multiple_of(strip * (1 - core), cols)
        place = dst.at[m, :, :, channels(core)]
        return (
            pltpu.make_async_copy(src.at[m, :, pl.ds(here, strip), :], place, sem.at[m]),
            remote(src.at[m, :, pl.ds(there, strip), :], place, send.at[m], recv.at[m], sec, partner),
        )

    def backward(m):
        @pl.when(last)
        def _():
            wait_stats(*seed_stats, m, True)

        @pl.when(jnp.logical_not(last))
        def _():
            wait_stats(*back_stats, m, False)

        first_sum = jnp.sum(dy_stat[m, :, 0, :], 0, keepdims=True)
        cross_sum = jnp.sum(dy_stat[m, :, 1, :], 0, keepdims=True)
        sums_v[core, pl.ds(0, 1), :] = sums_v[core, pl.ds(0, 1), :] + first_sum
        sums_v[core, pl.ds(1, 1), :] = sums_v[core, pl.ds(1, 1), :] + cross_sum
        inv = own_coef[m, pl.ds(0, 1), :]
        scale = own_coef[m, pl.ds(1, 1), :]
        tilt = scale * inv * (cross_sum / total)
        base = [scale * (first_sum / total) + tilt * own_coef[m, pl.ds(2 + e, 1), :] for e in range(3)]
        sends = dy_sends(m, sec)

        @pl.when(jnp.logical_not(last))
        def _():
            edges_arrived(sends)

        for i in range(2):
            @pl.when(jnp.logical_not(last))
            def _():
                sends[0](i).wait_recv()

            for g in range(groups):
                dz = dyin[m, i, group(g), :].astype(F32) * scale
                dz = dz - zown[m, i, group(g), :].astype(F32) * tilt - base[kind(g)]
                dzb[m, core, i, group(g), :] = inside(g, dz.astype(BF16))
            pass_on(dzb, dx_s, dx_r, m, i).start()

        def early():
            @pl.when(first)
            def _():
                send_dz(m)

        gate = jnp.concatenate([mask_v[m, :, centre, :].astype(F32)] * (half // 128), axis=2)
        conv = taps_joined(convolve(dzb, wt_v, dx_s, dx_r, m, lambda r: 2 - r, early), 2, 0)
        du = (conv.reshape(2, px, half) * gate).astype(BF16)
        gin_v[m] = du

        @pl.when(sec > 0)
        def _():
            dy = du.astype(F32) * slope_prev[m]
            dyout[m] = dy.astype(BF16)
            one = jnp.sum(dy.reshape(2 * px, half), 0, keepdims=True)
            cross = jnp.sum((dy * zin[m, :, centre, :].astype(F32)).reshape(2 * px, half), 0, keepdims=True)
            sums_out[m, pl.ds(0, 1), :] = one
            sums_out[m, pl.ds(1, 1), :] = prev_coef[m, pl.ds(0, 1), :] * (cross + prev_coef[m, pl.ds(1, 1), :] * one)
            start_stats(*back_stats, m, sec - 1, False)
            send_block(dy_sends(m, sec - 1))

        for copy in result_copies(gin_v, grads_in, gin_sem, pg_s, pg_r, m):
            copy.start()

        @pl.when((sec > 0) & (sec < sections - 1))
        def _():
            send_dz(m)

    def turn_weights():
        for copy in wt_copies():
            copy.wait()

        def one(i, carry):
            for h in range(2):
                wt_v[h, i] = wt_v[h, i].T
            return carry
        lax.fori_loop(0, 9, one, 0)

    @pl.when(late)
    def _():
        turn_weights()

    def step(t, carry):
        ahead = t - sec
        behind = t - (2 * sections - 1 - sec)

        @pl.when((ahead >= 0) & (ahead < batches))
        def _():
            forward(ahead)

        send_turned_third(ahead, 0)

        @pl.when(jnp.logical_not(late) & (ahead == batches))
        def _():
            def turned(m, carry):
                turn_inputs(m)
                turned_each(m, start)
                return carry
            lax.fori_loop(0, batches, turned, 0)
            turn_weights()

        done = ahead - jnp.where(last, 0, 1)

        @pl.when((behind >= 0) & (behind < batches))
        def _():
            backward(behind)

        send_turned_third(ahead, 1)

        @pl.when((done >= 0) & (done < batches))
        def _():
            finish(done)

        send_turned_third(ahead, 2)

        @pl.when(jnp.logical_not(late) & (ahead == batches + 1))
        def _():
            def relay(m, carry):
                relay_turned(m)
                return carry
            lax.fori_loop(0, batches, relay, 0)

        @pl.when((behind >= 1) & (behind < batches) & jnp.logical_not(late))
        def _():
            add_gradients(behind - 1)

        return carry

    lax.fori_loop(0, 2 * sections - 1 + batches, step, 0)

    remote(sums_v.at[core], sums_v.at[core], sv_s, sv_r, sec, partner).start()

    @pl.when(last)
    def _():
        def send(m, carry):
            send_dz(m)
            return carry

        lax.fori_loop(0, batches, send, 0)

    @pl.when(late)
    def _():
        def relay(m, carry):
            relay_turned(m)
            return carry

        def add(m, carry):
            add_gradients(m)
            return carry

        lax.fori_loop(0, batches, relay, 0)
        lax.fori_loop(0, batches - 1, add, 0)

    def swap(r, d):
        other = (seat + d) % 4
        return remote(
            swap_out.at[r, pl.ds(pl.multiple_of(other * share, share), share), :], swap_in.at[r, 4 - d - 1],
            sw_s.at[r, d - 1], sw_r.at[r, 4 - d - 1], sec, 4 * team + other,
        )

    gather_taps(batches - 1)
    for r in range(3):
        part = acc_v[r] + kernel_row(batches - 1, r)
        acc_v[r] = part
        swap_out[r] = part.astype(BF16)
        for d in range(1, 4):
            swap(r, d).start()

    def dw_copy(r):
        return pltpu.make_async_copy(dw_v.at[r], weight_grad.at[r], dw_sem.at[r])

    own_rows = pl.ds(pl.multiple_of(seat * share, share), share)
    for r in range(3):
        for c in range(3):
            dw_v[r, c, :, pl.ds(pl.multiple_of(seat * lanes, lanes), lanes)] = acc_v[r, own_rows, pl.ds(c * lanes, lanes)]
        for d in range(1, 4):
            swap(r, 4 - d).wait_recv()
            source = (seat + d) % 4
            for c in range(3):
                dw_v[r, c, :, pl.ds(pl.multiple_of(source * lanes, lanes), lanes)] = swap_in[
                    r, d - 1, :, pl.ds(c * lanes, lanes)
                ].astype(F32)
        dw_copy(r).start()

    for r in range(3):
        dw_copy(r).wait()
        for d in range(1, 4):
            swap(r, d).wait_send()

    @pl.when(decoder)
    def _():
        argument_sent(*mask_parts)

    @pl.when(sec < sections - 1)
    def _():
        for copy in affine_sends():
            copy.wait_send()

    def sums_copy():
        return remote(sums_v.at[core], sums_v.at[core], sv_s, sv_r, sec, partner)

    sums_copy().wait_recv()
    sums_copy().wait_send()
    for h in range(2):
        shift_sum[:, pl.ds(h * half, half)] = sums_v[h, pl.ds(0, 1), :]
        gain_sum[:, pl.ds(h * half, half)] = sums_v[h, pl.ds(1, 1), :]

    def drain(m, carry):
        for src, dst, sems in ((out_v, outs, (out_sem, po_s, po_r)), (gin_v, grads_in, (gin_sem, pg_s, pg_r))):
            here, there = result_copies(src, dst, *sems, m)
            here.wait()
            there.wait_send()
            remote(
                src.at[m, :, pl.ds(0, strip), :], dst.at[m, :, :, channels(1 - core)], sems[1].at[m], sems[2].at[m],
                sec, partner,
            ).wait_recv()

        turned_each(m, sent)
        turned_relay(m).wait_send()
        dz_each(m, sent)
        for i in range(2):
            pass_on(ub, ux_s, ux_r, m, i).wait_send()
            pass_on(dzb, dx_s, dx_r, m, i).wait_send()

        @pl.when(first)
        def _():
            argument_sent(*input_parts(images, m))

        @pl.when(last)
        def _():
            argument_sent(*input_parts(cotangent, m))
            stats_each(*seed_stats, m, sec, True, sent)

        @pl.when(sec < sections - 1)
        def _():
            stats_each(*down_stats, m, sec + 1, False, sent)
            block_sent(z_sends(m, sec + 1))

        stats_each(*same_stats, m, sec, True, sent)
        each_edge(own_edges(m), sent)

        @pl.when(sec > 0)
        def _():
            stats_each(*back_stats, m, sec - 1, False, sent)
            block_sent(dy_sends(m, sec - 1))

        return carry

    lax.fori_loop(0, batches, drain, 0)


def settle(*refs):
    count = (len(refs) - 2) // 3
    sources, targets, stages = refs[:count], refs[count : 2 * count], refs[2 * count : 3 * count]
    moves = []
    for src, dst, stage in zip(sources, targets, stages):
        if len(src.shape) == 2:
            moves.append((src, dst, stage))
        else:
            moves += [(src.at[i], dst.at[i], stage.at[i]) for i in range(src.shape[0])]
    ins = [pltpu.make_async_copy(src, stage, refs[-2].at[i]) for i, (src, dst, stage) in enumerate(moves)]
    outs = [pltpu.make_async_copy(stage, dst, refs[-1].at[i]) for i, (src, dst, stage) in enumerate(moves)]
    for copy in ins:
        copy.start()
    for come, go in zip(ins, outs):
        come.wait()
        go.start()
    for copy in outs:
        copy.wait()


def body(images, switches, conv_weights, gains, shifts, cotangent):
    sections = lax.axis_size("section")
    strips = lax.axis_size("rows")
    batches, pictures, strip_rows, cols, ch = images.shape
    strip = strip_rows * cols
    px = 2 * strip
    tall = px + 2 * cols
    anywhere = pl.BlockSpec(memory_space=pl.ANY)
    vmem = pl.BlockSpec(memory_space=pltpu.VMEM)
    dma = pltpu.SemaphoreType.DMA
    flops = 3 * 2 * 9 * ch * ch * batches * px
    share = ch // strips
    chips = strips // 2
    outs, grads_in, weight_grad, gain_sum, shift_sum = pl.pallas_call(
        functools.partial(kernel, sections, strips, cols),
        out_shape=(
            jax.ShapeDtypeStruct((batches, pictures, strip, ch), BF16),
            jax.ShapeDtypeStruct((batches, pictures, strip, ch), BF16),
            jax.ShapeDtypeStruct((3, 3, share, ch), F32),
            jax.ShapeDtypeStruct((1, ch), F32),
            jax.ShapeDtypeStruct((1, ch), F32),
        ),
        in_specs=[anywhere, anywhere, anywhere, vmem, vmem, vmem],
        out_specs=(anywhere, anywhere, anywhere, vmem, vmem),
        scratch_shapes=[
            pltpu.VMEM((2, 9, ch // 2, ch // 2), BF16),
            pltpu.VMEM((2, 9, ch // 2, ch // 2), BF16),
            pltpu.VMEM((batches, 2, tall, ch // 2), BF16),
            pltpu.VMEM((batches, 2, strip, 128), BF16),
            pltpu.VMEM((batches, 2, tall, 128), BF16),
            pltpu.VMEM((1, ch), F32),
            pltpu.VMEM((1, ch), F32),
            pltpu.VMEM((batches, 2, tall, ch // 2), BF16),
            pltpu.VMEM((batches, chips, 2, ch // 2), F32),
            pltpu.VMEM((batches, 2, tall, ch // 2), BF16),
            pltpu.VMEM((batches, chips, 2, ch // 2), F32),
            pltpu.VMEM((batches, 2, 2, tall, ch // 2), BF16),
            pltpu.VMEM((batches, 2, px, ch // 2), F32),
            pltpu.VMEM((batches, 2, ch // 2), F32),
            pltpu.VMEM((batches, 8, ch // 2), F32),
            pltpu.VMEM((batches, 2, tall, ch // 2), BF16),
            pltpu.VMEM((batches, chips, 2, ch // 2), F32),
            pltpu.VMEM((batches, 2, 2, tall, ch // 2), BF16),
            pltpu.VMEM((batches, 2, px, ch // 2), BF16),
            pltpu.VMEM((3, 2 * px, ch // 2), F32),
            pltpu.VMEM((2, 2, ch // 2), F32),
            pltpu.VMEM((batches, 2, ch // 2), F32),
            pltpu.VMEM((batches, 2, ch // 2), F32),
            pltpu.VMEM((batches, 2, ch // 2), F32),
            pltpu.VMEM((batches, 2, px, ch // 2), BF16),
            pltpu.VMEM((batches, 2, px, ch // 2), BF16),
            pltpu.VMEM((batches, ch, px), BF16),
            pltpu.VMEM((batches, 2, strips // 2, 4 * share, px), BF16),
            pltpu.VMEM((batches, 2, px * strips // 2 + 2 * cols, ch // 4), BF16),
            pltpu.VMEM((2, px * strips // 2 + 2 * cols, 3 * ch // 4), BF16),
            pltpu.VMEM((3, 4 * share, 3 * ch // 4), F32),
            pltpu.VMEM((3, 4 * share, 3 * ch // 4), BF16),
            pltpu.VMEM((3, 3, share, 3 * ch // 4), BF16),
            pltpu.VMEM((3, 3, share, ch), F32),
            dma((2,)), dma((2,)),
            dma((batches,)),
            dma((batches,)), dma((batches,)),
            dma((batches, 2)), dma((batches, 2)),
            dma, dma,
            dma((2,)), dma((2,)),
            dma((2,)), dma((2,)),
            dma((batches, 2)), dma((batches, 2)),
            dma((batches, 2)), dma((batches, 2)),
            dma, dma,
            dma((batches, 4)), dma((batches, 4)),
            dma((batches, chips)), dma((batches, chips)),
            dma((batches, 4)), dma((batches, 4)),
            dma((batches, chips)), dma((batches, chips)),
            dma((batches, 4)), dma((batches, 4)),
            dma((batches, chips)), dma((batches, chips)),
            dma((batches, chips)),
            dma((batches,)), dma((batches,)), dma((batches,)),
            dma((batches,)), dma((batches,)), dma((batches,)),
            dma((batches, strips // 2)), dma((batches, strips // 2)),
            dma((batches,)), dma((batches,)),
            dma((batches, strips)), dma((batches, strips)),
            dma((3, 3)), dma((3, 3)),
            dma((3,)),
        ],
        compiler_params=pltpu.CompilerParams(
            collective_id=0, has_side_effects=True, vmem_limit_bytes=56 * 2**20
        ),
        cost_estimate=pl.CostEstimate(
            flops=flops, bytes_accessed=2 * 9 * ch * ch * 2, transcendentals=0
        ),
    )(
        images.reshape(batches, pictures, strip, ch),
        cotangent.reshape(batches, pictures, strip, ch),
        conv_weights.reshape(9, ch, ch),
        gains,
        shifts,
        switches.reshape(-1, switches.shape[-1]),
    )
    results = (outs, grads_in, weight_grad, gain_sum, shift_sum)
    outs, grads_in, weight_grad, gain_sum, shift_sum = pl.pallas_call(
        settle,
        out_shape=tuple(jax.ShapeDtypeStruct(r.shape, r.dtype) for r in results),
        in_specs=[anywhere] * 5,
        out_specs=(anywhere,) * 5,
        scratch_shapes=[pltpu.VMEM(r.shape, r.dtype) for r in results] + [dma((2 * batches + 5,))] * 2,
        compiler_params=pltpu.CompilerParams(vmem_limit_bytes=60 * 2**20),
    )(*results)
    shape = (1, batches, pictures, strip_rows, cols, ch)
    return (outs.reshape(shape), grads_in.reshape(shape), weight_grad[None], gain_sum, shift_sum)


def solution(mesh):
    return jax.shard_map(
        body,
        mesh=mesh,
        in_specs=(
            P(None, None, "rows", None, None),
            P(None, None, "rows", None),
            P("section", None, None, None, None),
            P("section", None),
            P("section", None),
            P(None, None, "rows", None, None),
        ),
        out_specs=(
            P("section", None, None, "rows", None, None),
            P("section", None, None, "rows", None, None),
            P("section", None, None, "rows", None),
            P("section", None),
            P("section", None),
        ),
        check_vma=False,
    )
```

```python
import functools

import jax
import jax.numpy as jnp
from jax import lax
from jax.experimental import pallas as pl
from jax.experimental.pallas import tpu as pltpu
from jax.sharding import PartitionSpec as P

EPSILON = 1e-05
MESH = pl.DeviceIdType.MESH
BF16 = jnp.bfloat16
F32 = jnp.float32


def kernel(
    sections, strips, cols,
    images, cotangent, weights, gains, shifts, switches,
    outs, grads_in, weight_grad, gain_sum, shift_sum,
    w_v, wt_v, inp, mask_own, mask_v, gain_prev, shift_prev, zin, zin_stat, zown, own_stat, ub, slope_prev,
    prev_coef, own_coef, dyin, dy_stat, dzb, dyout, product_v, sums_v, stat_out, sums_out, seed_sums, out_v, gin_v,
    ut_own, ut_all, dz_all, dz_taps, acc_v, swap_out, swap_in, dw_v,
    w_sem, wt_sem, in_sem, pi_s, pi_r, ie_s, ie_r, mp_s, mp_r, me_s, me_r, gp_s, gp_r,
    ux_s, ux_r, dx_s, dx_r, sv_s, sv_r,
    fz_s, fz_r, fs_s, fs_r, oe_s, oe_r, os_s, os_r, bz_s, bz_r, bs_s, bs_r, ls_s,
    out_sem, po_s, po_r, gin_sem, pg_s, pg_r,
    ut_s, ut_r, uw_s, uf_s, uf_r, dz_s, dz_r, sw_s, sw_r, dw_sem,
):
    sec = lax.axis_index("section")
    row = lax.axis_index("rows")
    batches, _, tall, half = inp.shape
    ch = 2 * half
    px = tall - 2 * cols
    strip = px // 2
    groups = tall // cols
    chips = strips // 2
    local = float(2 * px)
    total = local * chips
    first, last, decoder = sec == 0, sec == sections - 1, sec == sections // 2
    late = sec >= sections // 2
    core = row % 2
    partner = row + 1 - 2 * core
    has_up, has_down = row >= 2, row < strips - 2
    centre = pl.ds(cols, px)
    chip = row // 2
    team, seat = row // 4, row % 4
    lanes = dz_all.shape[3]
    block = ut_all.shape[3]
    share = block // 4
    mine = pl.multiple_of(cols + strip * core, cols)

    def channels(h):
        return pl.ds(pl.multiple_of(h * half, half), half)

    def w_copies():
        return [
            pltpu.make_async_copy(weights.at[:, channels(h), channels(core)], w_v.at[h], w_sem.at[h]) for h in range(2)
        ]

    def wt_copies():
        return [
            pltpu.make_async_copy(weights.at[:, channels(core), channels(h)], wt_v.at[h], wt_sem.at[h]) for h in range(2)
        ]

    def in_copy(src, m):
        return pltpu.make_async_copy(src.at[m, :, :, channels(core)], inp.at[m, :, pl.ds(mine, strip), :], in_sem.at[m])

    for copy in w_copies() + wt_copies():
        copy.start()

    @pl.when(first)
    def _():
        for m in range(batches):
            in_copy(images, m).start()

    @pl.when(last)
    def _():
        for m in range(batches):
            in_copy(cotangent, m).start()

    barrier = pltpu.get_barrier_semaphore()
    for s in range(sections):
        @pl.when((sec >= s - 1) & (sec <= s + 1))
        def _():
            def greet(i, carry):
                @pl.when((s != sec) | (i != row))
                def _():
                    pl.semaphore_signal(barrier, inc=1, device_id=(jnp.int32(s), i), device_id_type=MESH)
                return carry
            lax.fori_loop(0, strips, greet, 0)

    acc_v[...] = jnp.zeros_like(acc_v)
    sums_v[...] = jnp.zeros_like(sums_v)

    for m in range(batches):
        for i in range(2):
            for at in (0, dz_all.shape[2] - cols):
                dz_all[m, i, pl.ds(at, cols), :] = jnp.zeros((cols, lanes), BF16)

    @pl.when(decoder)
    def _():
        wide = cols // 2
        windows_at = lax.broadcasted_iota(jnp.int32, (cols, wide), 1)
        places = lax.broadcasted_iota(jnp.int32, (cols, wide), 0)
        pick = (lax.shift_right_logical(places, 1) == windows_at).astype(F32)
        table = lax.dot_general(
            pick, switches[...].astype(F32), (((1,), (1,)), ((), ())), preferred_element_type=F32
        )
        odd = jnp.bitwise_and(lax.broadcasted_iota(jnp.int32, (cols, 128), 0), 1).astype(F32)
        windows = strip // cols // 2
        for m in range(batches):
            for i in range(2):
                for w in range(windows):
                    at = (m * 2 + i) * windows + w
                    value = jnp.broadcast_to(table[:, at : at + 1], (cols, 128))
                    for p in range(2):
                        hit = (jnp.abs(value - (2.0 * p + odd)) < 0.5).astype(F32).astype(BF16)
                        mask_own[m, i, pl.ds((2 * w + p) * cols, cols), :] = hit
        for m in range(batches):
            mask_v[m, :, pl.ds(mine, strip), :] = mask_own[m]

    @pl.when(jnp.logical_not(decoder))
    def _():
        mask_v[...] = jnp.ones_like(mask_v)

    near = 1 + jnp.where(sec > 0, 1, 0) + jnp.where(sec < sections - 1, 1, 0)
    pl.semaphore_wait(barrier, near * strips - 1)

    def remote(src, dst, send, recv, s, i):
        return pltpu.make_async_remote_copy(
            src_ref=src, dst_ref=dst, send_sem=send, recv_sem=recv, device_id=(s, i), device_id_type=MESH
        )

    def to_partner(src_at, dst_at, send, recv):
        return remote(src_at(1 - core), dst_at(pl.ds(mine, strip)), send, recv, sec, partner)

    def start_argument(src_at, dst_at, pair_sems, edge_sems):
        to_partner(src_at, dst_at, *pair_sems).start()

        @pl.when((core == 1) & has_down)
        def _():
            for i in range(2):
                remote(
                    src_at(i, pl.ds(strip - cols, cols)), dst_at(pl.ds(0, cols)),
                    edge_sems[0].at[i], edge_sems[1].at[0], sec, row + 1 + i,
                ).start()

        @pl.when((core == 0) & has_up)
        def _():
            for i in range(2):
                remote(
                    src_at(i, pl.ds(0, cols)), dst_at(pl.ds(cols + px, cols)),
                    edge_sems[0].at[i], edge_sems[1].at[1], sec, row - 2 + i,
                ).start()

    def argument_arrived(src_at, dst_at, pair_sems, edge_sems):
        to_partner(src_at, dst_at, *pair_sems).wait_recv()

        @pl.when(has_up)
        def _():
            remote(
                src_at(0, pl.ds(0, cols)), dst_at(pl.ds(0, cols)), edge_sems[0].at[0], edge_sems[1].at[0], sec, row
            ).wait_recv()

        @pl.when(has_down)
        def _():
            remote(
                src_at(0, pl.ds(0, cols)), dst_at(pl.ds(cols + px, cols)), edge_sems[0].at[0], edge_sems[1].at[1],
                sec, row,
            ).wait_recv()

    def argument_sent(src_at, dst_at, pair_sems, edge_sems):
        to_partner(src_at, dst_at, *pair_sems).wait_send()

        @pl.when(((core == 1) & has_down) | ((core == 0) & has_up))
        def _():
            for i in range(2):
                remote(
                    src_at(i, pl.ds(0, cols)), dst_at(pl.ds(0, cols)), edge_sems[0].at[i], edge_sems[1].at[0], sec, row
                ).wait_send()

    def input_parts(src, m):
        return (
            lambda i, r=pl.ds(0, strip): src.at[m, :, r, channels(i)],
            lambda r: inp.at[m, :, r, :],
            (pi_s.at[m], pi_r.at[m]),
            (ie_s.at[m], ie_r.at[m]),
        )

    mask_parts = (
        lambda i, r=pl.ds(0, strip): mask_own.at[:, :, r, :],
        lambda r: mask_v.at[:, :, r, :],
        (mp_s, mp_r),
        (me_s, me_r),
    )

    @pl.when(first)
    def _():
        for m in range(batches):
            start_argument(*input_parts(images, m))

    @pl.when(last)
    def _():
        for m in range(batches):
            start_argument(*input_parts(cotangent, m))

    @pl.when(decoder)
    def _():
        start_argument(*mask_parts)

    def affine_sends():
        return (
            remote(gains, gain_prev, gp_s.at[0], gp_r.at[0], sec + 1, row),
            remote(shifts, shift_prev, gp_s.at[1], gp_r.at[1], sec + 1, row),
        )

    @pl.when(sec < sections - 1)
    def _():
        for copy in affine_sends():
            copy.start()

    def block_sends(src, src_from, dst, send, recv, m, s):
        def body(i):
            return remote(
                src.at[m, i, pl.ds(src_from, px), :], dst.at[m, i, centre, :], send.at[m, i], recv.at[m, i], s, row
            )

        def edge(e, src_row, dst_row, i):
            return remote(
                src.at[m, :, pl.ds(src_from + src_row, cols), :], dst.at[m, :, pl.ds(dst_row, cols), :],
                send.at[m, 2 + e], recv.at[m, 2 + e], s, i,
            )

        return body, lambda: edge(0, px - cols, 0, row + 2), lambda: edge(1, 0, cols + px, row - 2)

    def each_edge(parts, act):
        _, to_down, to_up = parts

        @pl.when(has_down)
        def _():
            act(to_down())

        @pl.when(has_up)
        def _():
            act(to_up())

    def edges_arrived(parts):
        _, to_down, to_up = parts

        @pl.when(has_up)
        def _():
            to_down().wait_recv()

        @pl.when(has_down)
        def _():
            to_up().wait_recv()

    def send_block(parts):
        each_edge(parts, start)
        for i in range(2):
            parts[0](i).start()

    def block_sent(parts):
        each_edge(parts, sent)
        for i in range(2):
            parts[0](i).wait_send()

    def start(copy):
        copy.start()

    def sent(copy):
        copy.wait_send()

    def came(copy):
        copy.wait_recv()

    def z_sends(m, s):
        return block_sends(zown, cols, zin, fz_s, fz_r, m, s)

    def own_edges(m):
        return block_sends(zown, cols, zown, oe_s, oe_r, m, sec)

    def dy_sends(m, s):
        return block_sends(dyout, 0, dyin, bz_s, bz_r, m, s)

    def stats_each(src, dst, send, recv, m, s, same, act):
        def one(d, carry):
            q = chip + d
            q = jnp.where(q >= chips, q - chips, q)
            act(remote(src.at[m], dst.at[m, chip], send.at[m, d], recv.at[m, d], s, 2 * q + core))
            return carry
        lax.fori_loop(1 if same else 0, chips, one, 0)

    def start_stats(src, dst, send, recv, m, s, same):
        stats_each(src, dst, send, recv, m, s, same, start)
        if same:
            dst[m, chip] = src[m]

    def wait_stats(src, dst, send, recv, m, same):
        stats_each(src, dst, send, recv, m, sec, same, came)

    down_stats = (stat_out, zin_stat, fs_s, fs_r)
    same_stats = (stat_out, own_stat, os_s, os_r)
    back_stats = (sums_out, dy_stat, bs_s, bs_r)
    seed_stats = (seed_sums, dy_stat, ls_s, bs_r)

    def join(stats_ref, m):
        means, squares = stats_ref[m, :, 0, :], stats_ref[m, :, 1, :]
        mean = jnp.sum(means, 0, keepdims=True) / float(chips)
        off = means - mean
        var = (jnp.sum(squares, 0, keepdims=True) + local * jnp.sum(off * off, 0, keepdims=True)) / total
        at = (jnp.maximum(chip - 1, 0), chip, jnp.minimum(chip + 1, chips - 1))
        return lax.rsqrt(var + EPSILON), [stats_ref[m, i, pl.ds(0, 1), :] - mean for i in at]

    def kind(g):
        return 0 if g == 0 else 2 if g == groups - 1 else 1

    def inside(g, values):
        if kind(g) == 1:
            return values
        return jnp.where(has_up if kind(g) == 0 else has_down, values, jnp.zeros_like(values))

    def group(g):
        return pl.ds(g * cols, cols)

    column = lax.broadcasted_iota(jnp.int32, (1, cols, half), 1)

    def taps_joined(parts, left, right):
        def moved(values, by, edge):
            turned = pltpu.roll(values, by % (2 * px), 0).reshape(2 * px // cols, cols, half)
            return jnp.where(column == edge, 0.0, turned).reshape(2 * px, half)
        return parts[1] + moved(parts[left], 1, 0) + moved(parts[right], -1, cols - 1)

    def pass_on(operand, send, recv, m, i):
        return remote(operand.at[m, core, i], operand.at[m, core, i], send.at[m, i], recv.at[m, i], sec, partner)

    def products(operand, w, m, h, r_at):
        def one(c):
            acc = jnp.zeros((2 * px, half), F32)
            for r in range(3):
                left = operand[m, h, :, pl.ds(r_at(r) * cols, px), :].reshape(2 * px, half)
                acc += jnp.dot(left, w[h, 3 * r + c], preferred_element_type=F32)
            return acc
        return one

    def convolve(operand, w, send, recv, m, r_at, before_second=None):
        mine_first = products(operand, w, m, core, r_at)
        for c in range(3):
            product_v[c] = mine_first(c)
        for i in range(2):
            pass_on(operand, send, recv, m, i).wait_recv()
        if before_second is not None:
            before_second()
        then = products(operand, w, m, 1 - core, r_at)
        return [product_v[c] + then(c) for c in range(3)]

    def turned_copy(m, q):
        src = ut_own.at[m, pl.ds(pl.multiple_of((q // 2) * block, block), block), :]
        return src, ut_all.at[m, core, chip]

    thirds = [1 + (chips - 1) * i // 3 for i in range(4)]

    def turned_each(m, act, low=1, high=chips):
        def one(d, carry):
            q = chip + d
            q = jnp.where(q >= chips, q - chips, q)
            its_team = q // 2
            nearest = 2 * its_team + jnp.where(chip > q, 1, 0)

            @pl.when((its_team == team) | (q == nearest))
            def _():
                src, dst = turned_copy(m, q)
                act(remote(src, dst, ut_s.at[m, d], ut_r.at[m, d], sec, 2 * q + core))
            return carry
        lax.fori_loop(low, high, one, 0)

    def entry_for(p):
        return (p // 2 != team) & (jnp.where(p > chip, 1, 0) == chip % 2)

    def turned_arrived(m):
        def one(d, carry):
            p = chip - d
            p = jnp.where(p < 0, p + chips, p)

            @pl.when(jnp.logical_not(entry_for(p)))
            def _():
                piece = ut_all.at[m, core, p]
                remote(piece, piece, ut_s.at[m, d], ut_r.at[m, d], sec, row).wait_recv()
            return carry
        lax.fori_loop(1, chips, one, 0)

    def turned_onward(m, act, arrive):
        other = chip + 1 - 2 * (chip % 2)

        def one(d, carry):
            p = chip - d
            p = jnp.where(p < 0, p + chips, p)

            @pl.when(entry_for(p))
            def _():
                piece = ut_all.at[m, core, p]
                if arrive:
                    remote(piece, piece, ut_s.at[m, d], ut_r.at[m, d], sec, row).wait_recv()
                there = other - p
                there = jnp.where(there < 0, there + chips, there)
                act(remote(piece, piece, uw_s.at[m, d], ut_r.at[m, there], sec, 2 * other + core))

            return carry
        lax.fori_loop(1, chips, one, 0)

    def turn_inputs(m):
        for h in range(2):
            ut_own[m, pl.ds(h * half, half), :] = ub[m, h, core, centre, :].T
        mine_at = pl.ds(pl.multiple_of(team * block, block), block)
        ut_all[m, core, chip] = ut_own[m, mine_at, :]

    def send_turned_third(m, i):
        @pl.when(last & (m >= 0) & (m < batches))
        def _():
            if i == 0:
                turn_inputs(m)
            turned_each(m, start, thirds[i], thirds[i + 1])

    def send_turned():
        def one(m, carry):
            turn_inputs(m)
            turned_each(m, start)
            return carry
        lax.fori_loop(0, batches, one, 0)

    def turned_relay(m):
        return remote(ut_all.at[m, core], ut_all.at[m, core], uf_s.at[m], uf_r.at[m], sec, partner)

    def relay_turned():
        def onward(m, carry):
            turned_onward(m, start, True)
            return carry

        def relay(m, carry):
            turned_arrived(m)
            turned_relay(m).start()
            return carry

        lax.fori_loop(0, batches, onward, 0)
        lax.fori_loop(0, batches, relay, 0)

    def dz_copy(m, i):
        src = dzb.at[m, (i % 4) // 2, core, centre, pl.ds(pl.multiple_of(i % 2 * lanes, lanes), lanes)]
        dst = dz_all.at[m, core, pl.ds(pl.multiple_of(cols + chip * px, cols), px), :]
        return src, dst

    def dz_each(m, act):
        def one(d, carry):
            i = row + d
            i = jnp.where(i >= strips, i - strips, i)
            src, dst = dz_copy(m, i)
            act(remote(src, dst, dz_s.at[m, d], dz_r.at[m, d], sec, i))
            return carry
        lax.fori_loop(1, strips, one, 0)

    def send_dz(m):
        dz_each(m, start)
        dz_all[m, core, pl.ds(pl.multiple_of(cols + chip * px, cols), px), :] = dzb[
            m, seat // 2, core, centre, pl.ds(pl.multiple_of(seat % 2 * lanes, lanes), lanes)
        ]

    def gather_taps(m):
        dz_each(m, came)
        relayed = ut_all.at[m, 1 - core]
        pltpu.make_async_copy(relayed, relayed, uf_r.at[m]).wait()
        rows = dz_all.shape[2]
        edge = lax.broadcasted_iota(jnp.int32, (1, cols, lanes), 1)
        for i in range(2):
            values = dz_all[m, i].astype(F32)
            for c, by, gone in ((0, rows - 1, cols - 1), (2, 1, 0)):
                turned = pltpu.roll(values, by, 0).reshape(rows // cols, cols, lanes)
                turned = jnp.where(edge == gone, 0.0, turned).reshape(rows, lanes)
                dz_taps[i, :, pl.ds(c * lanes, lanes)] = turned.astype(BF16)
            dz_taps[i, :, pl.ds(lanes, lanes)] = dz_all[m, i]

    def kernel_row(m, r):
        part = jnp.zeros((block, 3 * lanes), F32)
        for i in range(2):
            left = jnp.concatenate([ut_all[m, i, q] for q in range(chips)], axis=1)
            part += jnp.dot(
                left, dz_taps[i, pl.ds((2 - r) * cols, px * (strips // 2)), :], preferred_element_type=F32
            )
        return part

    def add_gradients(m):
        gather_taps(m)
        for r in range(3):
            acc_v[r] = acc_v[r] + kernel_row(m, r)

    def forward(m):
        @pl.when(first)
        def _():
            in_copy(images, m).wait()
            argument_arrived(*input_parts(images, m))
            for i in range(2):
                for g in range(groups):
                    ub[m, core, i, group(g), :] = inside(g, inp[m, i, group(g), :])
                pass_on(ub, ux_s, ux_r, m, i).start()

        @pl.when(sec > 0)
        def _():
            @pl.when(m == 0)
            def _():
                for copy in affine_sends():
                    copy.wait_recv()

                @pl.when(decoder)
                def _():
                    argument_arrived(*mask_parts)

            wait_stats(*down_stats, m, False)
            inv, offs = join(zin_stat, m)
            prev_coef[m, pl.ds(0, 1), :] = inv
            prev_coef[m, pl.ds(1, 1), :] = offs[1]
            slant = 0.5 * inv * gain_prev[:, channels(core)]
            level = [slant * off + 0.5 * shift_prev[:, channels(core)] for off in offs]
            sends = z_sends(m, sec)
            edges_arrived(sends)
            for i in range(2):
                sends[0](i).wait_recv()
                for g in range(groups):
                    gate = jnp.concatenate([mask_v[m, i, group(g), :].astype(F32)] * (half // 128), axis=1)
                    halved = zin[m, i, group(g), :].astype(F32) * slant + level[kind(g)]
                    turn = jnp.tanh(halved)
                    bent = halved * turn
                    ub[m, core, i, group(g), :] = inside(g, ((halved + bent) * gate).astype(BF16))
                    if kind(g) == 1:
                        slope_prev[m, i, pl.ds((g - 1) * cols, cols), :] = (0.5 + 0.5 * turn) * (1.0 + halved - bent)
                pass_on(ub, ux_s, ux_r, m, i).start()

        @pl.when(m == 0)
        def _():
            for copy in w_copies():
                copy.wait()

        conv = taps_joined(convolve(ub, w_v, ux_s, ux_r, m, lambda r: r), 0, 2)
        mean = jnp.sum(conv, 0, keepdims=True) / local
        conv = conv - mean
        stat_out[m, pl.ds(0, 1), :] = mean
        stat_out[m, pl.ds(1, 1), :] = jnp.sum(conv * conv, 0, keepdims=True)
        zown[m, :, centre, :] = conv.reshape(2, px, half).astype(BF16)

        @pl.when(sec < sections - 1)
        def _():
            start_stats(*down_stats, m, sec + 1, False)
            send_block(z_sends(m, sec + 1))

        start_stats(*same_stats, m, sec, True)
        each_edge(own_edges(m), start)

    def finish(m):
        wait_stats(*same_stats, m, True)
        inv, offs = join(own_stat, m)
        scale = inv * gains[:, channels(core)]
        own_coef[m, pl.ds(0, 1), :] = inv
        own_coef[m, pl.ds(1, 1), :] = scale
        for e in range(3):
            own_coef[m, pl.ds(2 + e, 1), :] = offs[e]
        slant = 0.5 * scale
        level = [slant * off + 0.5 * shifts[:, channels(core)] for off in offs]
        edges_arrived(own_edges(m))

        @pl.when(last)
        def _():
            in_copy(cotangent, m).wait()
            argument_arrived(*input_parts(cotangent, m))
            sums = jnp.zeros((cols, half), F32)
            cross = jnp.zeros((cols, half), F32)
            for i in range(2):
                for g in range(groups):
                    z = zown[m, i, group(g), :].astype(F32)
                    halved = z * slant + level[kind(g)]
                    turn = jnp.tanh(halved)
                    bent = halved * turn
                    dy = inp[m, i, group(g), :].astype(F32) * ((0.5 + 0.5 * turn) * (1.0 + halved - bent))
                    dyin[m, i, group(g), :] = dy.astype(BF16)
                    if kind(g) == 1:
                        out_v[m, i, pl.ds((g - 1) * cols, cols), :] = (halved + bent).astype(BF16)
                        sums += dy
                        cross += dy * z
            one = jnp.sum(sums, 0, keepdims=True)
            cross = jnp.sum(cross, 0, keepdims=True)
            seed_sums[m, pl.ds(0, 1), :] = one
            seed_sums[m, pl.ds(1, 1), :] = inv * (cross + offs[1] * one)
            start_stats(*seed_stats, m, sec, True)

        @pl.when(jnp.logical_not(last))
        def _():
            for i in range(2):
                for g in range(1, groups - 1):
                    halved = zown[m, i, group(g), :].astype(F32) * slant + level[1]
                    out_v[m, i, pl.ds((g - 1) * cols, cols), :] = (halved + halved * jnp.tanh(halved)).astype(BF16)

        for copy in result_copies(out_v, outs, out_sem, po_s, po_r, m):
            copy.start()

    def result_copies(src, dst, sem, send, recv, m):
        here, there = pl.multiple_of(strip * core, cols), pl.multiple_of(strip * (1 - core), cols)
        place = dst.at[m, :, :, channels(core)]
        return (
            pltpu.make_async_copy(src.at[m, :, pl.ds(here, strip), :], place, sem.at[m]),
            remote(src.at[m, :, pl.ds(there, strip), :], place, send.at[m], recv.at[m], sec, partner),
        )

    def backward(m):
        @pl.when(last)
        def _():
            wait_stats(*seed_stats, m, True)

        @pl.when(jnp.logical_not(last))
        def _():
            wait_stats(*back_stats, m, False)

        first_sum = jnp.sum(dy_stat[m, :, 0, :], 0, keepdims=True)
        cross_sum = jnp.sum(dy_stat[m, :, 1, :], 0, keepdims=True)
        sums_v[core, pl.ds(0, 1), :] = sums_v[core, pl.ds(0, 1), :] + first_sum
        sums_v[core, pl.ds(1, 1), :] = sums_v[core, pl.ds(1, 1), :] + cross_sum
        inv = own_coef[m, pl.ds(0, 1), :]
        scale = own_coef[m, pl.ds(1, 1), :]
        tilt = scale * inv * (cross_sum / total)
        base = [scale * (first_sum / total) + tilt * own_coef[m, pl.ds(2 + e, 1), :] for e in range(3)]
        sends = dy_sends(m, sec)

        @pl.when(jnp.logical_not(last))
        def _():
            edges_arrived(sends)

        for i in range(2):
            @pl.when(jnp.logical_not(last))
            def _():
                sends[0](i).wait_recv()

            for g in range(groups):
                dz = dyin[m, i, group(g), :].astype(F32) * scale
                dz = dz - zown[m, i, group(g), :].astype(F32) * tilt - base[kind(g)]
                dzb[m, core, i, group(g), :] = inside(g, dz.astype(BF16))
            pass_on(dzb, dx_s, dx_r, m, i).start()

        def early():
            @pl.when(first)
            def _():
                send_dz(m)

        gate = jnp.concatenate([mask_v[m, :, centre, :].astype(F32)] * (half // 128), axis=2)
        conv = taps_joined(convolve(dzb, wt_v, dx_s, dx_r, m, lambda r: 2 - r, early), 2, 0)
        du = (conv.reshape(2, px, half) * gate).astype(BF16)
        gin_v[m] = du

        @pl.when(sec > 0)
        def _():
            dy = du.astype(F32) * slope_prev[m]
            dyout[m] = dy.astype(BF16)
            one = jnp.sum(dy.reshape(2 * px, half), 0, keepdims=True)
            cross = jnp.sum((dy * zin[m, :, centre, :].astype(F32)).reshape(2 * px, half), 0, keepdims=True)
            sums_out[m, pl.ds(0, 1), :] = one
            sums_out[m, pl.ds(1, 1), :] = prev_coef[m, pl.ds(0, 1), :] * (cross + prev_coef[m, pl.ds(1, 1), :] * one)
            start_stats(*back_stats, m, sec - 1, False)
            send_block(dy_sends(m, sec - 1))

        for copy in result_copies(gin_v, grads_in, gin_sem, pg_s, pg_r, m):
            copy.start()

        @pl.when((sec > 0) & (sec < sections - 1))
        def _():
            send_dz(m)

    def turn_weights():
        for copy in wt_copies():
            copy.wait()

        def one(i, carry):
            for h in range(2):
                wt_v[h, i] = wt_v[h, i].T
            return carry
        lax.fori_loop(0, 9, one, 0)

    @pl.when(late)
    def _():
        turn_weights()

    def step(t, carry):
        ahead = t - sec
        behind = t - (2 * sections - 1 - sec)

        @pl.when((ahead >= 0) & (ahead < batches))
        def _():
            forward(ahead)

        send_turned_third(ahead, 0)

        @pl.when(jnp.logical_not(late) & (ahead == batches))
        def _():
            send_turned()
            turn_weights()

        done = ahead - jnp.where(last, 0, 1)

        @pl.when((behind >= 0) & (behind < batches))
        def _():
            backward(behind)

        send_turned_third(ahead, 1)

        @pl.when((done >= 0) & (done < batches))
        def _():
            finish(done)

        send_turned_third(ahead, 2)

        @pl.when(jnp.logical_not(late) & (ahead == batches + 1))
        def _():
            relay_turned()

        @pl.when((behind >= 1) & (behind < batches) & jnp.logical_not(late))
        def _():
            add_gradients(behind - 1)

        return carry

    lax.fori_loop(0, 2 * sections - 1 + batches, step, 0)

    remote(sums_v.at[core], sums_v.at[core], sv_s, sv_r, sec, partner).start()

    @pl.when(late & jnp.logical_not(last))
    def _():
        send_turned()

    @pl.when(last)
    def _():
        def send(m, carry):
            send_dz(m)
            return carry

        lax.fori_loop(0, batches, send, 0)

    @pl.when(late)
    def _():
        def add(m, carry):
            add_gradients(m)
            return carry

        relay_turned()
        lax.fori_loop(0, batches - 1, add, 0)

    def swap(r, d):
        other = (seat + d) % 4
        return remote(
            swap_out.at[r, pl.ds(pl.multiple_of(other * share, share), share), :], swap_in.at[r, 4 - d - 1],
            sw_s.at[r, d - 1], sw_r.at[r, 4 - d - 1], sec, 4 * team + other,
        )

    gather_taps(batches - 1)
    for r in range(3):
        part = acc_v[r] + kernel_row(batches - 1, r)
        acc_v[r] = part
        swap_out[r] = part.astype(BF16)
        for d in range(1, 4):
            swap(r, d).start()

    def dw_copy(r):
        return pltpu.make_async_copy(dw_v.at[r], weight_grad.at[r], dw_sem.at[r])

    own_rows = pl.ds(pl.multiple_of(seat * share, share), share)
    for r in range(3):
        for c in range(3):
            dw_v[r, c, :, pl.ds(pl.multiple_of(seat * lanes, lanes), lanes)] = acc_v[r, own_rows, pl.ds(c * lanes, lanes)]
        for d in range(1, 4):
            swap(r, 4 - d).wait_recv()
            source = (seat + d) % 4
            for c in range(3):
                dw_v[r, c, :, pl.ds(pl.multiple_of(source * lanes, lanes), lanes)] = swap_in[
                    r, d - 1, :, pl.ds(c * lanes, lanes)
                ].astype(F32)
        dw_copy(r).start()

    for r in range(3):
        dw_copy(r).wait()
        for d in range(1, 4):
            swap(r, d).wait_send()

    @pl.when(decoder)
    def _():
        argument_sent(*mask_parts)

    @pl.when(sec < sections - 1)
    def _():
        for copy in affine_sends():
            copy.wait_send()

    def sums_copy():
        return remote(sums_v.at[core], sums_v.at[core], sv_s, sv_r, sec, partner)

    sums_copy().wait_recv()
    sums_copy().wait_send()
    for h in range(2):
        shift_sum[:, pl.ds(h * half, half)] = sums_v[h, pl.ds(0, 1), :]
        gain_sum[:, pl.ds(h * half, half)] = sums_v[h, pl.ds(1, 1), :]

    def drain(m, carry):
        for src, dst, sems in ((out_v, outs, (out_sem, po_s, po_r)), (gin_v, grads_in, (gin_sem, pg_s, pg_r))):
            here, there = result_copies(src, dst, *sems, m)
            here.wait()
            there.wait_send()
            remote(
                src.at[m, :, pl.ds(0, strip), :], dst.at[m, :, :, channels(1 - core)], sems[1].at[m], sems[2].at[m],
                sec, partner,
            ).wait_recv()

        turned_each(m, sent)
        turned_onward(m, sent, False)
        turned_relay(m).wait_send()
        dz_each(m, sent)
        for i in range(2):
            pass_on(ub, ux_s, ux_r, m, i).wait_send()
            pass_on(dzb, dx_s, dx_r, m, i).wait_send()

        @pl.when(first)
        def _():
            argument_sent(*input_parts(images, m))

        @pl.when(last)
        def _():
            argument_sent(*input_parts(cotangent, m))
            stats_each(*seed_stats, m, sec, True, sent)

        @pl.when(sec < sections - 1)
        def _():
            stats_each(*down_stats, m, sec + 1, False, sent)
            block_sent(z_sends(m, sec + 1))

        stats_each(*same_stats, m, sec, True, sent)
        each_edge(own_edges(m), sent)

        @pl.when(sec > 0)
        def _():
            stats_each(*back_stats, m, sec - 1, False, sent)
            block_sent(dy_sends(m, sec - 1))

        return carry

    lax.fori_loop(0, batches, drain, 0)


def settle(*refs):
    count = (len(refs) - 2) // 3
    sources, targets, stages = refs[:count], refs[count : 2 * count], refs[2 * count : 3 * count]
    moves = []
    for src, dst, stage in zip(sources, targets, stages):
        if len(src.shape) == 2:
            moves.append((src, dst, stage))
        else:
            moves += [(src.at[i], dst.at[i], stage.at[i]) for i in range(src.shape[0])]
    ins = [pltpu.make_async_copy(src, stage, refs[-2].at[i]) for i, (src, dst, stage) in enumerate(moves)]
    outs = [pltpu.make_async_copy(stage, dst, refs[-1].at[i]) for i, (src, dst, stage) in enumerate(moves)]
    for copy in ins:
        copy.start()
    for come, go in zip(ins, outs):
        come.wait()
        go.start()
    for copy in outs:
        copy.wait()


def body(images, switches, conv_weights, gains, shifts, cotangent):
    sections = lax.axis_size("section")
    strips = lax.axis_size("rows")
    batches, pictures, strip_rows, cols, ch = images.shape
    strip = strip_rows * cols
    px = 2 * strip
    tall = px + 2 * cols
    anywhere = pl.BlockSpec(memory_space=pl.ANY)
    vmem = pl.BlockSpec(memory_space=pltpu.VMEM)
    dma = pltpu.SemaphoreType.DMA
    flops = 3 * 2 * 9 * ch * ch * batches * px
    share = ch // strips
    chips = strips // 2
    outs, grads_in, weight_grad, gain_sum, shift_sum = pl.pallas_call(
        functools.partial(kernel, sections, strips, cols),
        out_shape=(
            jax.ShapeDtypeStruct((batches, pictures, strip, ch), BF16),
            jax.ShapeDtypeStruct((batches, pictures, strip, ch), BF16),
            jax.ShapeDtypeStruct((3, 3, share, ch), F32),
            jax.ShapeDtypeStruct((1, ch), F32),
            jax.ShapeDtypeStruct((1, ch), F32),
        ),
        in_specs=[anywhere, anywhere, anywhere, vmem, vmem, vmem],
        out_specs=(anywhere, anywhere, anywhere, vmem, vmem),
        scratch_shapes=[
            pltpu.VMEM((2, 9, ch // 2, ch // 2), BF16),
            pltpu.VMEM((2, 9, ch // 2, ch // 2), BF16),
            pltpu.VMEM((batches, 2, tall, ch // 2), BF16),
            pltpu.VMEM((batches, 2, strip, 128), BF16),
            pltpu.VMEM((batches, 2, tall, 128), BF16),
            pltpu.VMEM((1, ch), F32),
            pltpu.VMEM((1, ch), F32),
            pltpu.VMEM((batches, 2, tall, ch // 2), BF16),
            pltpu.VMEM((batches, chips, 2, ch // 2), F32),
            pltpu.VMEM((batches, 2, tall, ch // 2), BF16),
            pltpu.VMEM((batches, chips, 2, ch // 2), F32),
            pltpu.VMEM((batches, 2, 2, tall, ch // 2), BF16),
            pltpu.VMEM((batches, 2, px, ch // 2), F32),
            pltpu.VMEM((batches, 2, ch // 2), F32),
            pltpu.VMEM((batches, 8, ch // 2), F32),
            pltpu.VMEM((batches, 2, tall, ch // 2), BF16),
            pltpu.VMEM((batches, chips, 2, ch // 2), F32),
            pltpu.VMEM((batches, 2, 2, tall, ch // 2), BF16),
            pltpu.VMEM((batches, 2, px, ch // 2), BF16),
            pltpu.VMEM((3, 2 * px, ch // 2), F32),
            pltpu.VMEM((2, 2, ch // 2), F32),
            pltpu.VMEM((batches, 2, ch // 2), F32),
            pltpu.VMEM((batches, 2, ch // 2), F32),
            pltpu.VMEM((batches, 2, ch // 2), F32),
            pltpu.VMEM((batches, 2, px, ch // 2), BF16),
            pltpu.VMEM((batches, 2, px, ch // 2), BF16),
            pltpu.VMEM((batches, ch, px), BF16),
            pltpu.VMEM((batches, 2, strips // 2, 4 * share, px), BF16),
            pltpu.VMEM((batches, 2, px * strips // 2 + 2 * cols, ch // 4), BF16),
            pltpu.VMEM((2, px * strips // 2 + 2 * cols, 3 * ch // 4), BF16),
            pltpu.VMEM((3, 4 * share, 3 * ch // 4), F32),
            pltpu.VMEM((3, 4 * share, 3 * ch // 4), BF16),
            pltpu.VMEM((3, 3, share, 3 * ch // 4), BF16),
            pltpu.VMEM((3, 3, share, ch), F32),
            dma((2,)), dma((2,)),
            dma((batches,)),
            dma((batches,)), dma((batches,)),
            dma((batches, 2)), dma((batches, 2)),
            dma, dma,
            dma((2,)), dma((2,)),
            dma((2,)), dma((2,)),
            dma((batches, 2)), dma((batches, 2)),
            dma((batches, 2)), dma((batches, 2)),
            dma, dma,
            dma((batches, 4)), dma((batches, 4)),
            dma((batches, chips)), dma((batches, chips)),
            dma((batches, 4)), dma((batches, 4)),
            dma((batches, chips)), dma((batches, chips)),
            dma((batches, 4)), dma((batches, 4)),
            dma((batches, chips)), dma((batches, chips)),
            dma((batches, chips)),
            dma((batches,)), dma((batches,)), dma((batches,)),
            dma((batches,)), dma((batches,)), dma((batches,)),
            dma((batches, chips)), dma((batches, chips)), dma((batches, chips)),
            dma((batches,)), dma((batches,)),
            dma((batches, strips)), dma((batches, strips)),
            dma((3, 3)), dma((3, 3)),
            dma((3,)),
        ],
        compiler_params=pltpu.CompilerParams(
            collective_id=0, has_side_effects=True, vmem_limit_bytes=56 * 2**20
        ),
        cost_estimate=pl.CostEstimate(
            flops=flops, bytes_accessed=2 * 9 * ch * ch * 2, transcendentals=0
        ),
    )(
        images.reshape(batches, pictures, strip, ch),
        cotangent.reshape(batches, pictures, strip, ch),
        conv_weights.reshape(9, ch, ch),
        gains,
        shifts,
        switches.reshape(-1, switches.shape[-1]),
    )
    results = (outs, grads_in, weight_grad, gain_sum, shift_sum)
    outs, grads_in, weight_grad, gain_sum, shift_sum = pl.pallas_call(
        settle,
        out_shape=tuple(jax.ShapeDtypeStruct(r.shape, r.dtype) for r in results),
        in_specs=[anywhere] * 5,
        out_specs=(anywhere,) * 5,
        scratch_shapes=[pltpu.VMEM(r.shape, r.dtype) for r in results] + [dma((2 * batches + 5,))] * 2,
        compiler_params=pltpu.CompilerParams(vmem_limit_bytes=60 * 2**20),
    )(*results)
    shape = (1, batches, pictures, strip_rows, cols, ch)
    return (outs.reshape(shape), grads_in.reshape(shape), weight_grad[None], gain_sum, shift_sum)


def solution(mesh):
    return jax.shard_map(
        body,
        mesh=mesh,
        in_specs=(
            P(None, None, "rows", None, None),
            P(None, None, "rows", None),
            P("section", None, None, None, None),
            P("section", None),
            P("section", None),
            P(None, None, "rows", None, None),
        ),
        out_specs=(
            P("section", None, None, "rows", None, None),
            P("section", None, None, "rows", None, None),
            P("section", None, None, "rows", None),
            P("section", None),
            P("section", None),
        ),
        check_vma=False,
    )
```

```python
import functools

import jax
import jax.numpy as jnp
from jax import lax
from jax.experimental import pallas as pl
from jax.experimental.pallas import tpu as pltpu
from jax.sharding import PartitionSpec as P

EPSILON = 1e-05
MESH = pl.DeviceIdType.MESH
BF16 = jnp.bfloat16
F32 = jnp.float32


def kernel(
    sections, strips, cols,
    images, cotangent, weights, gains, shifts, switches,
    outs, grads_in, weight_grad, gain_sum, shift_sum,
    w_v, wt_v, inp, mask_own, mask_v, gain_prev, shift_prev, zin, zin_stat, zown, own_stat, ub, slope_prev,
    prev_coef, own_coef, dyin, dy_stat, dzb, dyout, product_v, sums_v, stat_out, sums_out, seed_sums, out_v, gin_v,
    ut_own, ut_all, dz_all, dz_taps, acc_v, swap_out, swap_in, dw_v,
    w_sem, wt_sem, in_sem, pi_s, pi_r, ie_s, ie_r, mp_s, mp_r, me_s, me_r, gp_s, gp_r,
    ux_s, ux_r, dx_s, dx_r, sv_s, sv_r,
    fz_s, fz_r, fs_s, fs_r, oe_s, oe_r, os_s, os_r, bz_s, bz_r, bs_s, bs_r, ls_s,
    out_sem, po_s, po_r, gin_sem, pg_s, pg_r,
    ut_s, ut_r, uf_s, uf_r, dz_s, dz_r, sw_s, sw_r, dw_sem,
):
    sec = lax.axis_index("section")
    row = lax.axis_index("rows")
    batches, _, tall, half = inp.shape
    ch = 2 * half
    px = tall - 2 * cols
    strip = px // 2
    groups = tall // cols
    chips = strips // 2
    local = float(2 * px)
    total = local * chips
    first, last, decoder = sec == 0, sec == sections - 1, sec == sections // 2
    late = sec >= sections // 2
    core = row % 2
    partner = row + 1 - 2 * core
    has_up, has_down = row >= 2, row < strips - 2
    centre = pl.ds(cols, px)
    chip = row // 2
    team, seat = row // 4, row % 4
    lanes = dz_all.shape[3]
    block = ut_all.shape[3]
    share = block // 4
    mine = pl.multiple_of(cols + strip * core, cols)

    def channels(h):
        return pl.ds(pl.multiple_of(h * half, half), half)

    def w_copies():
        return [
            pltpu.make_async_copy(weights.at[:, channels(h), channels(core)], w_v.at[h], w_sem.at[h]) for h in range(2)
        ]

    def wt_copies():
        return [
            pltpu.make_async_copy(weights.at[:, channels(core), channels(h)], wt_v.at[h], wt_sem.at[h]) for h in range(2)
        ]

    def in_copy(src, m):
        return pltpu.make_async_copy(src.at[m, :, :, channels(core)], inp.at[m, :, pl.ds(mine, strip), :], in_sem.at[m])

    for copy in w_copies() + wt_copies():
        copy.start()

    @pl.when(first)
    def _():
        for m in range(batches):
            in_copy(images, m).start()

    @pl.when(last)
    def _():
        for m in range(batches):
            in_copy(cotangent, m).start()

    barrier = pltpu.get_barrier_semaphore()
    for s in range(sections):
        @pl.when((sec >= s - 1) & (sec <= s + 1))
        def _():
            def greet(i, carry):
                @pl.when((s != sec) | (i != row))
                def _():
                    pl.semaphore_signal(barrier, inc=1, device_id=(jnp.int32(s), i), device_id_type=MESH)
                return carry
            lax.fori_loop(0, strips, greet, 0)

    acc_v[...] = jnp.zeros_like(acc_v)
    sums_v[...] = jnp.zeros_like(sums_v)

    for m in range(batches):
        for i in range(2):
            for at in (0, dz_all.shape[2] - cols):
                dz_all[m, i, pl.ds(at, cols), :] = jnp.zeros((cols, lanes), BF16)

    @pl.when(decoder)
    def _():
        wide = cols // 2
        windows_at = lax.broadcasted_iota(jnp.int32, (cols, wide), 1)
        places = lax.broadcasted_iota(jnp.int32, (cols, wide), 0)
        pick = (lax.shift_right_logical(places, 1) == windows_at).astype(F32)
        table = lax.dot_general(
            pick, switches[...].astype(F32), (((1,), (1,)), ((), ())), preferred_element_type=F32
        )
        odd = jnp.bitwise_and(lax.broadcasted_iota(jnp.int32, (cols, 128), 0), 1).astype(F32)
        windows = strip // cols // 2
        for m in range(batches):
            for i in range(2):
                for w in range(windows):
                    at = (m * 2 + i) * windows + w
                    value = jnp.broadcast_to(table[:, at : at + 1], (cols, 128))
                    for p in range(2):
                        hit = (jnp.abs(value - (2.0 * p + odd)) < 0.5).astype(F32).astype(BF16)
                        mask_own[m, i, pl.ds((2 * w + p) * cols, cols), :] = hit
        for m in range(batches):
            mask_v[m, :, pl.ds(mine, strip), :] = mask_own[m]

    @pl.when(jnp.logical_not(decoder))
    def _():
        mask_v[...] = jnp.ones_like(mask_v)

    near = 1 + jnp.where(sec > 0, 1, 0) + jnp.where(sec < sections - 1, 1, 0)
    pl.semaphore_wait(barrier, near * strips - 1)

    def remote(src, dst, send, recv, s, i):
        return pltpu.make_async_remote_copy(
            src_ref=src, dst_ref=dst, send_sem=send, recv_sem=recv, device_id=(s, i), device_id_type=MESH
        )

    def to_partner(src_at, dst_at, send, recv):
        return remote(src_at(1 - core), dst_at(pl.ds(mine, strip)), send, recv, sec, partner)

    def start_argument(src_at, dst_at, pair_sems, edge_sems):
        to_partner(src_at, dst_at, *pair_sems).start()

        @pl.when((core == 1) & has_down)
        def _():
            for i in range(2):
                remote(
                    src_at(i, pl.ds(strip - cols, cols)), dst_at(pl.ds(0, cols)),
                    edge_sems[0].at[i], edge_sems[1].at[0], sec, row + 1 + i,
                ).start()

        @pl.when((core == 0) & has_up)
        def _():
            for i in range(2):
                remote(
                    src_at(i, pl.ds(0, cols)), dst_at(pl.ds(cols + px, cols)),
                    edge_sems[0].at[i], edge_sems[1].at[1], sec, row - 2 + i,
                ).start()

    def argument_arrived(src_at, dst_at, pair_sems, edge_sems):
        to_partner(src_at, dst_at, *pair_sems).wait_recv()

        @pl.when(has_up)
        def _():
            remote(
                src_at(0, pl.ds(0, cols)), dst_at(pl.ds(0, cols)), edge_sems[0].at[0], edge_sems[1].at[0], sec, row
            ).wait_recv()

        @pl.when(has_down)
        def _():
            remote(
                src_at(0, pl.ds(0, cols)), dst_at(pl.ds(cols + px, cols)), edge_sems[0].at[0], edge_sems[1].at[1],
                sec, row,
            ).wait_recv()

    def argument_sent(src_at, dst_at, pair_sems, edge_sems):
        to_partner(src_at, dst_at, *pair_sems).wait_send()

        @pl.when(((core == 1) & has_down) | ((core == 0) & has_up))
        def _():
            for i in range(2):
                remote(
                    src_at(i, pl.ds(0, cols)), dst_at(pl.ds(0, cols)), edge_sems[0].at[i], edge_sems[1].at[0], sec, row
                ).wait_send()

    def input_parts(src, m):
        return (
            lambda i, r=pl.ds(0, strip): src.at[m, :, r, channels(i)],
            lambda r: inp.at[m, :, r, :],
            (pi_s.at[m], pi_r.at[m]),
            (ie_s.at[m], ie_r.at[m]),
        )

    mask_parts = (
        lambda i, r=pl.ds(0, strip): mask_own.at[:, :, r, :],
        lambda r: mask_v.at[:, :, r, :],
        (mp_s, mp_r),
        (me_s, me_r),
    )

    @pl.when(first)
    def _():
        for m in range(batches):
            start_argument(*input_parts(images, m))

    @pl.when(last)
    def _():
        for m in range(batches):
            start_argument(*input_parts(cotangent, m))

    @pl.when(decoder)
    def _():
        start_argument(*mask_parts)

    def affine_sends():
        return (
            remote(gains, gain_prev, gp_s.at[0], gp_r.at[0], sec + 1, row),
            remote(shifts, shift_prev, gp_s.at[1], gp_r.at[1], sec + 1, row),
        )

    @pl.when(sec < sections - 1)
    def _():
        for copy in affine_sends():
            copy.start()

    def block_sends(src, src_from, dst, send, recv, m, s):
        def body(i):
            return remote(
                src.at[m, i, pl.ds(src_from, px), :], dst.at[m, i, centre, :], send.at[m, i], recv.at[m, i], s, row
            )

        def edge(e, src_row, dst_row, i):
            return remote(
                src.at[m, :, pl.ds(src_from + src_row, cols), :], dst.at[m, :, pl.ds(dst_row, cols), :],
                send.at[m, 2 + e], recv.at[m, 2 + e], s, i,
            )

        return body, lambda: edge(0, px - cols, 0, row + 2), lambda: edge(1, 0, cols + px, row - 2)

    def each_edge(parts, act):
        _, to_down, to_up = parts

        @pl.when(has_down)
        def _():
            act(to_down())

        @pl.when(has_up)
        def _():
            act(to_up())

    def edges_arrived(parts):
        _, to_down, to_up = parts

        @pl.when(has_up)
        def _():
            to_down().wait_recv()

        @pl.when(has_down)
        def _():
            to_up().wait_recv()

    def send_block(parts):
        each_edge(parts, start)
        for i in range(2):
            parts[0](i).start()

    def block_sent(parts):
        each_edge(parts, sent)
        for i in range(2):
            parts[0](i).wait_send()

    def start(copy):
        copy.start()

    def sent(copy):
        copy.wait_send()

    def came(copy):
        copy.wait_recv()

    def z_sends(m, s):
        return block_sends(zown, cols, zin, fz_s, fz_r, m, s)

    def own_edges(m):
        return block_sends(zown, cols, zown, oe_s, oe_r, m, sec)

    def dy_sends(m, s):
        return block_sends(dyout, 0, dyin, bz_s, bz_r, m, s)

    def stats_each(src, dst, send, recv, m, s, same, act):
        def one(d, carry):
            q = chip + d
            q = jnp.where(q >= chips, q - chips, q)
            act(remote(src.at[m], dst.at[m, chip], send.at[m, d], recv.at[m, d], s, 2 * q + core))
            return carry
        lax.fori_loop(1 if same else 0, chips, one, 0)

    def start_stats(src, dst, send, recv, m, s, same):
        stats_each(src, dst, send, recv, m, s, same, start)
        if same:
            dst[m, chip] = src[m]

    def wait_stats(src, dst, send, recv, m, same):
        stats_each(src, dst, send, recv, m, sec, same, came)

    down_stats = (stat_out, zin_stat, fs_s, fs_r)
    same_stats = (stat_out, own_stat, os_s, os_r)
    back_stats = (sums_out, dy_stat, bs_s, bs_r)
    seed_stats = (seed_sums, dy_stat, ls_s, bs_r)

    def join(stats_ref, m):
        means, squares = stats_ref[m, :, 0, :], stats_ref[m, :, 1, :]
        mean = jnp.sum(means, 0, keepdims=True) / float(chips)
        off = means - mean
        var = (jnp.sum(squares, 0, keepdims=True) + local * jnp.sum(off * off, 0, keepdims=True)) / total
        at = (jnp.maximum(chip - 1, 0), chip, jnp.minimum(chip + 1, chips - 1))
        return lax.rsqrt(var + EPSILON), [stats_ref[m, i, pl.ds(0, 1), :] - mean for i in at]

    def kind(g):
        return 0 if g == 0 else 2 if g == groups - 1 else 1

    def inside(g, values):
        if kind(g) == 1:
            return values
        return jnp.where(has_up if kind(g) == 0 else has_down, values, jnp.zeros_like(values))

    def group(g):
        return pl.ds(g * cols, cols)

    column = lax.broadcasted_iota(jnp.int32, (1, cols, half), 1)

    def taps_joined(parts, left, right):
        def moved(values, by, edge):
            turned = pltpu.roll(values, by % (2 * px), 0).reshape(2 * px // cols, cols, half)
            return jnp.where(column == edge, 0.0, turned).reshape(2 * px, half)
        return parts[1] + moved(parts[left], 1, 0) + moved(parts[right], -1, cols - 1)

    def pass_on(operand, send, recv, m, i):
        return remote(operand.at[m, core, i], operand.at[m, core, i], send.at[m, i], recv.at[m, i], sec, partner)

    def products(operand, w, m, h, r_at):
        def one(c):
            acc = jnp.zeros((2 * px, half), F32)
            for r in range(3):
                left = operand[m, h, :, pl.ds(r_at(r) * cols, px), :].reshape(2 * px, half)
                acc += jnp.dot(left, w[h, 3 * r + c], preferred_element_type=F32)
            return acc
        return one

    def convolve(operand, w, send, recv, m, r_at, before_second=None):
        mine_first = products(operand, w, m, core, r_at)
        for c in range(3):
            product_v[c] = mine_first(c)
        for i in range(2):
            pass_on(operand, send, recv, m, i).wait_recv()
        if before_second is not None:
            before_second()
        then = products(operand, w, m, 1 - core, r_at)
        return [product_v[c] + then(c) for c in range(3)]

    def turned_copy(m, q):
        src = ut_own.at[m, pl.ds(pl.multiple_of((q // 2) * block, block), block), :]
        return src, ut_all.at[m, core, chip]

    thirds = [1 + (chips - 1) * i // 3 for i in range(4)]

    def turned_each(m, act, low=1, high=chips):
        def one(d, carry):
            q = chip + d
            q = jnp.where(q >= chips, q - chips, q)
            src, dst = turned_copy(m, q)
            act(remote(src, dst, ut_s.at[m, d], ut_r.at[m, d], sec, 2 * q + core))
            return carry
        lax.fori_loop(low, high, one, 0)

    def turn_inputs(m):
        for h in range(2):
            ut_own[m, pl.ds(h * half, half), :] = ub[m, h, core, centre, :].T
        mine_at = pl.ds(pl.multiple_of(team * block, block), block)
        ut_all[m, core, chip] = ut_own[m, mine_at, :]

    def send_turned_third(m, i):
        @pl.when(late & (m >= 0) & (m < batches))
        def _():
            if i == 0:
                turn_inputs(m)
            turned_each(m, start, thirds[i], thirds[i + 1])

    def turned_relay(m):
        return remote(ut_all.at[m, core], ut_all.at[m, core], uf_s.at[m], uf_r.at[m], sec, partner)

    def relay_turned(m):
        turned_each(m, came)
        turned_relay(m).start()

    def relay_all():
        def one(m, carry):
            relay_turned(m)
            return carry
        lax.fori_loop(0, batches, one, 0)

    def dz_copy(m, i):
        src = dzb.at[m, (i % 4) // 2, core, centre, pl.ds(pl.multiple_of(i % 2 * lanes, lanes), lanes)]
        dst = dz_all.at[m, core, pl.ds(pl.multiple_of(cols + chip * px, cols), px), :]
        return src, dst

    def dz_each(m, act):
        def one(d, carry):
            i = row + d
            i = jnp.where(i >= strips, i - strips, i)
            src, dst = dz_copy(m, i)
            act(remote(src, dst, dz_s.at[m, d], dz_r.at[m, d], sec, i))
            return carry
        lax.fori_loop(1, strips, one, 0)

    def send_dz(m):
        dz_each(m, start)
        dz_all[m, core, pl.ds(pl.multiple_of(cols + chip * px, cols), px), :] = dzb[
            m, seat // 2, core, centre, pl.ds(pl.multiple_of(seat % 2 * lanes, lanes), lanes)
        ]

    def gather_taps(m):
        dz_each(m, came)
        relayed = ut_all.at[m, 1 - core]
        pltpu.make_async_copy(relayed, relayed, uf_r.at[m]).wait()
        rows = dz_all.shape[2]
        edge = lax.broadcasted_iota(jnp.int32, (1, cols, lanes), 1)
        for i in range(2):
            values = dz_all[m, i].astype(F32)
            for c, by, gone in ((0, rows - 1, cols - 1), (2, 1, 0)):
                turned = pltpu.roll(values, by, 0).reshape(rows // cols, cols, lanes)
                turned = jnp.where(edge == gone, 0.0, turned).reshape(rows, lanes)
                dz_taps[i, :, pl.ds(c * lanes, lanes)] = turned.astype(BF16)
            dz_taps[i, :, pl.ds(lanes, lanes)] = dz_all[m, i]

    def kernel_row(m, r):
        part = jnp.zeros((block, 3 * lanes), F32)
        for i in range(2):
            left = jnp.concatenate([ut_all[m, i, q] for q in range(chips)], axis=1)
            part += jnp.dot(
                left, dz_taps[i, pl.ds((2 - r) * cols, px * (strips // 2)), :], preferred_element_type=F32
            )
        return part

    def add_gradients(m):
        gather_taps(m)
        for r in range(3):
            acc_v[r] = acc_v[r] + kernel_row(m, r)

    def forward(m):
        @pl.when(first)
        def _():
            in_copy(images, m).wait()
            argument_arrived(*input_parts(images, m))
            for i in range(2):
                for g in range(groups):
                    ub[m, core, i, group(g), :] = inside(g, inp[m, i, group(g), :])
                pass_on(ub, ux_s, ux_r, m, i).start()

        @pl.when(sec > 0)
        def _():
            @pl.when(m == 0)
            def _():
                for copy in affine_sends():
                    copy.wait_recv()

                @pl.when(decoder)
                def _():
                    argument_arrived(*mask_parts)

            wait_stats(*down_stats, m, False)
            inv, offs = join(zin_stat, m)
            prev_coef[m, pl.ds(0, 1), :] = inv
            prev_coef[m, pl.ds(1, 1), :] = offs[1]
            slant = 0.5 * inv * gain_prev[:, channels(core)]
            level = [slant * off + 0.5 * shift_prev[:, channels(core)] for off in offs]
            sends = z_sends(m, sec)
            edges_arrived(sends)
            for i in range(2):
                sends[0](i).wait_recv()
                for g in range(groups):
                    gate = jnp.concatenate([mask_v[m, i, group(g), :].astype(F32)] * (half // 128), axis=1)
                    halved = zin[m, i, group(g), :].astype(F32) * slant + level[kind(g)]
                    turn = jnp.tanh(halved)
                    bent = halved * turn
                    ub[m, core, i, group(g), :] = inside(g, ((halved + bent) * gate).astype(BF16))
                    if kind(g) == 1:
                        slope_prev[m, i, pl.ds((g - 1) * cols, cols), :] = (0.5 + 0.5 * turn) * (1.0 + halved - bent)
                pass_on(ub, ux_s, ux_r, m, i).start()

        @pl.when(m == 0)
        def _():
            for copy in w_copies():
                copy.wait()

        conv = taps_joined(convolve(ub, w_v, ux_s, ux_r, m, lambda r: r), 0, 2)
        mean = jnp.sum(conv, 0, keepdims=True) / local
        conv = conv - mean
        stat_out[m, pl.ds(0, 1), :] = mean
        stat_out[m, pl.ds(1, 1), :] = jnp.sum(conv * conv, 0, keepdims=True)
        zown[m, :, centre, :] = conv.reshape(2, px, half).astype(BF16)

        @pl.when(sec < sections - 1)
        def _():
            start_stats(*down_stats, m, sec + 1, False)
            send_block(z_sends(m, sec + 1))

        start_stats(*same_stats, m, sec, True)
        each_edge(own_edges(m), start)

    def finish(m):
        wait_stats(*same_stats, m, True)
        inv, offs = join(own_stat, m)
        scale = inv * gains[:, channels(core)]
        own_coef[m, pl.ds(0, 1), :] = inv
        own_coef[m, pl.ds(1, 1), :] = scale
        for e in range(3):
            own_coef[m, pl.ds(2 + e, 1), :] = offs[e]
        slant = 0.5 * scale
        level = [slant * off + 0.5 * shifts[:, channels(core)] for off in offs]
        edges_arrived(own_edges(m))

        @pl.when(last)
        def _():
            in_copy(cotangent, m).wait()
            argument_arrived(*input_parts(cotangent, m))
            sums = jnp.zeros((cols, half), F32)
            cross = jnp.zeros((cols, half), F32)
            for i in range(2):
                for g in range(groups):
                    z = zown[m, i, group(g), :].astype(F32)
                    halved = z * slant + level[kind(g)]
                    turn = jnp.tanh(halved)
                    bent = halved * turn
                    dy = inp[m, i, group(g), :].astype(F32) * ((0.5 + 0.5 * turn) * (1.0 + halved - bent))
                    dyin[m, i, group(g), :] = dy.astype(BF16)
                    if kind(g) == 1:
                        out_v[m, i, pl.ds((g - 1) * cols, cols), :] = (halved + bent).astype(BF16)
                        sums += dy
                        cross += dy * z
            one = jnp.sum(sums, 0, keepdims=True)
            cross = jnp.sum(cross, 0, keepdims=True)
            seed_sums[m, pl.ds(0, 1), :] = one
            seed_sums[m, pl.ds(1, 1), :] = inv * (cross + offs[1] * one)
            start_stats(*seed_stats, m, sec, True)

        @pl.when(jnp.logical_not(last))
        def _():
            for i in range(2):
                for g in range(1, groups - 1):
                    halved = zown[m, i, group(g), :].astype(F32) * slant + level[1]
                    out_v[m, i, pl.ds((g - 1) * cols, cols), :] = (halved + halved * jnp.tanh(halved)).astype(BF16)

        for copy in result_copies(out_v, outs, out_sem, po_s, po_r, m):
            copy.start()

    def result_copies(src, dst, sem, send, recv, m):
        here, there = pl.multiple_of(strip * core, cols), pl.multiple_of(strip * (1 - core), cols)
        place = dst.at[m, :, :, channels(core)]
        return (
            pltpu.make_async_copy(src.at[m, :, pl.ds(here, strip), :], place, sem.at[m]),
            remote(src.at[m, :, pl.ds(there, strip), :], place, send.at[m], recv.at[m], sec, partner),
        )

    def backward(m):
        @pl.when(last)
        def _():
            wait_stats(*seed_stats, m, True)

        @pl.when(jnp.logical_not(last))
        def _():
            wait_stats(*back_stats, m, False)

        first_sum = jnp.sum(dy_stat[m, :, 0, :], 0, keepdims=True)
        cross_sum = jnp.sum(dy_stat[m, :, 1, :], 0, keepdims=True)
        sums_v[core, pl.ds(0, 1), :] = sums_v[core, pl.ds(0, 1), :] + first_sum
        sums_v[core, pl.ds(1, 1), :] = sums_v[core, pl.ds(1, 1), :] + cross_sum
        inv = own_coef[m, pl.ds(0, 1), :]
        scale = own_coef[m, pl.ds(1, 1), :]
        tilt = scale * inv * (cross_sum / total)
        base = [scale * (first_sum / total) + tilt * own_coef[m, pl.ds(2 + e, 1), :] for e in range(3)]
        sends = dy_sends(m, sec)

        @pl.when(jnp.logical_not(last))
        def _():
            edges_arrived(sends)

        for i in range(2):
            @pl.when(jnp.logical_not(last))
            def _():
                sends[0](i).wait_recv()

            for g in range(groups):
                dz = dyin[m, i, group(g), :].astype(F32) * scale
                dz = dz - zown[m, i, group(g), :].astype(F32) * tilt - base[kind(g)]
                dzb[m, core, i, group(g), :] = inside(g, dz.astype(BF16))
            pass_on(dzb, dx_s, dx_r, m, i).start()

        def early():
            @pl.when(first)
            def _():
                send_dz(m)

        gate = jnp.concatenate([mask_v[m, :, centre, :].astype(F32)] * (half // 128), axis=2)
        conv = taps_joined(convolve(dzb, wt_v, dx_s, dx_r, m, lambda r: 2 - r, early), 2, 0)
        du = (conv.reshape(2, px, half) * gate).astype(BF16)
        gin_v[m] = du

        @pl.when(sec > 0)
        def _():
            dy = du.astype(F32) * slope_prev[m]
            dyout[m] = dy.astype(BF16)
            one = jnp.sum(dy.reshape(2 * px, half), 0, keepdims=True)
            cross = jnp.sum((dy * zin[m, :, centre, :].astype(F32)).reshape(2 * px, half), 0, keepdims=True)
            sums_out[m, pl.ds(0, 1), :] = one
            sums_out[m, pl.ds(1, 1), :] = prev_coef[m, pl.ds(0, 1), :] * (cross + prev_coef[m, pl.ds(1, 1), :] * one)
            start_stats(*back_stats, m, sec - 1, False)
            send_block(dy_sends(m, sec - 1))

        for copy in result_copies(gin_v, grads_in, gin_sem, pg_s, pg_r, m):
            copy.start()

        @pl.when((sec > 0) & (sec < sections - 1))
        def _():
            send_dz(m)

    def turn_weights():
        for copy in wt_copies():
            copy.wait()

        def one(i, carry):
            for h in range(2):
                wt_v[h, i] = wt_v[h, i].T
            return carry
        lax.fori_loop(0, 9, one, 0)

    @pl.when(late)
    def _():
        turn_weights()

    def step(t, carry):
        ahead = t - sec
        behind = t - (2 * sections - 1 - sec)

        @pl.when((ahead >= 0) & (ahead < batches))
        def _():
            forward(ahead)

        send_turned_third(ahead, 0)

        @pl.when(jnp.logical_not(late) & (ahead == batches))
        def _():
            def turned(m, carry):
                turn_inputs(m)
                turned_each(m, start)
                return carry
            lax.fori_loop(0, batches, turned, 0)
            turn_weights()

        done = ahead - jnp.where(last, 0, 1)

        @pl.when((behind >= 0) & (behind < batches))
        def _():
            backward(behind)

        send_turned_third(ahead, 1)

        @pl.when((done >= 0) & (done < batches))
        def _():
            finish(done)

        send_turned_third(ahead, 2)

        @pl.when(first & (ahead == batches + 1))
        def _():
            relay_all()

        return carry

    lax.fori_loop(0, 2 * sections - 1 + batches, step, 0)

    remote(sums_v.at[core], sums_v.at[core], sv_s, sv_r, sec, partner).start()

    @pl.when(last)
    def _():
        def send(m, carry):
            send_dz(m)
            return carry

        lax.fori_loop(0, batches, send, 0)

    @pl.when(jnp.logical_not(first))
    def _():
        relay_all()

    def add(m, carry):
        add_gradients(m)
        return carry

    lax.fori_loop(0, batches - 1, add, 0)

    def swap(r, d):
        other = (seat + d) % 4
        return remote(
            swap_out.at[r, pl.ds(pl.multiple_of(other * share, share), share), :], swap_in.at[r, 4 - d - 1],
            sw_s.at[r, d - 1], sw_r.at[r, 4 - d - 1], sec, 4 * team + other,
        )

    gather_taps(batches - 1)
    for r in range(3):
        part = acc_v[r] + kernel_row(batches - 1, r)
        acc_v[r] = part
        swap_out[r] = part.astype(BF16)
        for d in range(1, 4):
            swap(r, d).start()

    def dw_copy(r):
        return pltpu.make_async_copy(dw_v.at[r], weight_grad.at[r], dw_sem.at[r])

    own_rows = pl.ds(pl.multiple_of(seat * share, share), share)
    for r in range(3):
        for c in range(3):
            dw_v[r, c, :, pl.ds(pl.multiple_of(seat * lanes, lanes), lanes)] = acc_v[r, own_rows, pl.ds(c * lanes, lanes)]
        for d in range(1, 4):
            swap(r, 4 - d).wait_recv()
            source = (seat + d) % 4
            for c in range(3):
                dw_v[r, c, :, pl.ds(pl.multiple_of(source * lanes, lanes), lanes)] = swap_in[
                    r, d - 1, :, pl.ds(c * lanes, lanes)
                ].astype(F32)
        dw_copy(r).start()

    for r in range(3):
        dw_copy(r).wait()
        for d in range(1, 4):
            swap(r, d).wait_send()

    @pl.when(decoder)
    def _():
        argument_sent(*mask_parts)

    @pl.when(sec < sections - 1)
    def _():
        for copy in affine_sends():
            copy.wait_send()

    def sums_copy():
        return remote(sums_v.at[core], sums_v.at[core], sv_s, sv_r, sec, partner)

    sums_copy().wait_recv()
    sums_copy().wait_send()
    for h in range(2):
        shift_sum[:, pl.ds(h * half, half)] = sums_v[h, pl.ds(0, 1), :]
        gain_sum[:, pl.ds(h * half, half)] = sums_v[h, pl.ds(1, 1), :]

    def drain(m, carry):
        for src, dst, sems in ((out_v, outs, (out_sem, po_s, po_r)), (gin_v, grads_in, (gin_sem, pg_s, pg_r))):
            here, there = result_copies(src, dst, *sems, m)
            here.wait()
            there.wait_send()
            remote(
                src.at[m, :, pl.ds(0, strip), :], dst.at[m, :, :, channels(1 - core)], sems[1].at[m], sems[2].at[m],
                sec, partner,
            ).wait_recv()

        turned_each(m, sent)
        turned_relay(m).wait_send()
        dz_each(m, sent)
        for i in range(2):
            pass_on(ub, ux_s, ux_r, m, i).wait_send()
            pass_on(dzb, dx_s, dx_r, m, i).wait_send()

        @pl.when(first)
        def _():
            argument_sent(*input_parts(images, m))

        @pl.when(last)
        def _():
            argument_sent(*input_parts(cotangent, m))
            stats_each(*seed_stats, m, sec, True, sent)

        @pl.when(sec < sections - 1)
        def _():
            stats_each(*down_stats, m, sec + 1, False, sent)
            block_sent(z_sends(m, sec + 1))

        stats_each(*same_stats, m, sec, True, sent)
        each_edge(own_edges(m), sent)

        @pl.when(sec > 0)
        def _():
            stats_each(*back_stats, m, sec - 1, False, sent)
            block_sent(dy_sends(m, sec - 1))

        return carry

    lax.fori_loop(0, batches, drain, 0)


def settle(*refs):
    count = (len(refs) - 2) // 3
    sources, targets, stages = refs[:count], refs[count : 2 * count], refs[2 * count : 3 * count]
    moves = []
    for src, dst, stage in zip(sources, targets, stages):
        if len(src.shape) == 2:
            moves.append((src, dst, stage))
        else:
            moves += [(src.at[i], dst.at[i], stage.at[i]) for i in range(src.shape[0])]
    ins = [pltpu.make_async_copy(src, stage, refs[-2].at[i]) for i, (src, dst, stage) in enumerate(moves)]
    outs = [pltpu.make_async_copy(stage, dst, refs[-1].at[i]) for i, (src, dst, stage) in enumerate(moves)]
    for copy in ins:
        copy.start()
    for come, go in zip(ins, outs):
        come.wait()
        go.start()
    for copy in outs:
        copy.wait()


def body(images, switches, conv_weights, gains, shifts, cotangent):
    sections = lax.axis_size("section")
    strips = lax.axis_size("rows")
    batches, pictures, strip_rows, cols, ch = images.shape
    strip = strip_rows * cols
    px = 2 * strip
    tall = px + 2 * cols
    anywhere = pl.BlockSpec(memory_space=pl.ANY)
    vmem = pl.BlockSpec(memory_space=pltpu.VMEM)
    dma = pltpu.SemaphoreType.DMA
    flops = 3 * 2 * 9 * ch * ch * batches * px
    share = ch // strips
    chips = strips // 2
    outs, grads_in, weight_grad, gain_sum, shift_sum = pl.pallas_call(
        functools.partial(kernel, sections, strips, cols),
        out_shape=(
            jax.ShapeDtypeStruct((batches, pictures, strip, ch), BF16),
            jax.ShapeDtypeStruct((batches, pictures, strip, ch), BF16),
            jax.ShapeDtypeStruct((3, 3, share, ch), F32),
            jax.ShapeDtypeStruct((1, ch), F32),
            jax.ShapeDtypeStruct((1, ch), F32),
        ),
        in_specs=[anywhere, anywhere, anywhere, vmem, vmem, vmem],
        out_specs=(anywhere, anywhere, anywhere, vmem, vmem),
        scratch_shapes=[
            pltpu.VMEM((2, 9, ch // 2, ch // 2), BF16),
            pltpu.VMEM((2, 9, ch // 2, ch // 2), BF16),
            pltpu.VMEM((batches, 2, tall, ch // 2), BF16),
            pltpu.VMEM((batches, 2, strip, 128), BF16),
            pltpu.VMEM((batches, 2, tall, 128), BF16),
            pltpu.VMEM((1, ch), F32),
            pltpu.VMEM((1, ch), F32),
            pltpu.VMEM((batches, 2, tall, ch // 2), BF16),
            pltpu.VMEM((batches, chips, 2, ch // 2), F32),
            pltpu.VMEM((batches, 2, tall, ch // 2), BF16),
            pltpu.VMEM((batches, chips, 2, ch // 2), F32),
            pltpu.VMEM((batches, 2, 2, tall, ch // 2), BF16),
            pltpu.VMEM((batches, 2, px, ch // 2), F32),
            pltpu.VMEM((batches, 2, ch // 2), F32),
            pltpu.VMEM((batches, 8, ch // 2), F32),
            pltpu.VMEM((batches, 2, tall, ch // 2), BF16),
            pltpu.VMEM((batches, chips, 2, ch // 2), F32),
            pltpu.VMEM((batches, 2, 2, tall, ch // 2), BF16),
            pltpu.VMEM((batches, 2, px, ch // 2), BF16),
            pltpu.VMEM((3, 2 * px, ch // 2), F32),
            pltpu.VMEM((2, 2, ch // 2), F32),
            pltpu.VMEM((batches, 2, ch // 2), F32),
            pltpu.VMEM((batches, 2, ch // 2), F32),
            pltpu.VMEM((batches, 2, ch // 2), F32),
            pltpu.VMEM((batches, 2, px, ch // 2), BF16),
            pltpu.VMEM((batches, 2, px, ch // 2), BF16),
            pltpu.VMEM((batches, ch, px), BF16),
            pltpu.VMEM((batches, 2, strips // 2, 4 * share, px), BF16),
            pltpu.VMEM((batches, 2, px * strips // 2 + 2 * cols, ch // 4), BF16),
            pltpu.VMEM((2, px * strips // 2 + 2 * cols, 3 * ch // 4), BF16),
            pltpu.VMEM((3, 4 * share, 3 * ch // 4), F32),
            pltpu.VMEM((3, 4 * share, 3 * ch // 4), BF16),
            pltpu.VMEM((3, 3, share, 3 * ch // 4), BF16),
            pltpu.VMEM((3, 3, share, ch), F32),
            dma((2,)), dma((2,)),
            dma((batches,)),
            dma((batches,)), dma((batches,)),
            dma((batches, 2)), dma((batches, 2)),
            dma, dma,
            dma((2,)), dma((2,)),
            dma((2,)), dma((2,)),
            dma((batches, 2)), dma((batches, 2)),
            dma((batches, 2)), dma((batches, 2)),
            dma, dma,
            dma((batches, 4)), dma((batches, 4)),
            dma((batches, chips)), dma((batches, chips)),
            dma((batches, 4)), dma((batches, 4)),
            dma((batches, chips)), dma((batches, chips)),
            dma((batches, 4)), dma((batches, 4)),
            dma((batches, chips)), dma((batches, chips)),
            dma((batches, chips)),
            dma((batches,)), dma((batches,)), dma((batches,)),
            dma((batches,)), dma((batches,)), dma((batches,)),
            dma((batches, strips // 2)), dma((batches, strips // 2)),
            dma((batches,)), dma((batches,)),
            dma((batches, strips)), dma((batches, strips)),
            dma((3, 3)), dma((3, 3)),
            dma((3,)),
        ],
        compiler_params=pltpu.CompilerParams(
            collective_id=0, has_side_effects=True, vmem_limit_bytes=56 * 2**20
        ),
        cost_estimate=pl.CostEstimate(
            flops=flops, bytes_accessed=2 * 9 * ch * ch * 2, transcendentals=0
        ),
    )(
        images.reshape(batches, pictures, strip, ch),
        cotangent.reshape(batches, pictures, strip, ch),
        conv_weights.reshape(9, ch, ch),
        gains,
        shifts,
        switches.reshape(-1, switches.shape[-1]),
    )
    results = (outs, grads_in, weight_grad, gain_sum, shift_sum)
    outs, grads_in, weight_grad, gain_sum, shift_sum = pl.pallas_call(
        settle,
        out_shape=tuple(jax.ShapeDtypeStruct(r.shape, r.dtype) for r in results),
        in_specs=[anywhere] * 5,
        out_specs=(anywhere,) * 5,
        scratch_shapes=[pltpu.VMEM(r.shape, r.dtype) for r in results] + [dma((2 * batches + 5,))] * 2,
        compiler_params=pltpu.CompilerParams(vmem_limit_bytes=60 * 2**20),
    )(*results)
    shape = (1, batches, pictures, strip_rows, cols, ch)
    return (outs.reshape(shape), grads_in.reshape(shape), weight_grad[None], gain_sum, shift_sum)


def solution(mesh):
    return jax.shard_map(
        body,
        mesh=mesh,
        in_specs=(
            P(None, None, "rows", None, None),
            P(None, None, "rows", None),
            P("section", None, None, None, None),
            P("section", None),
            P("section", None),
            P(None, None, "rows", None, None),
        ),
        out_specs=(
            P("section", None, None, "rows", None, None),
            P("section", None, None, "rows", None, None),
            P("section", None, None, "rows", None),
            P("section", None),
            P("section", None),
        ),
        check_vma=False,
    )
```

```python
import functools

import jax
import jax.numpy as jnp
from jax import lax
from jax.experimental import pallas as pl
from jax.experimental.pallas import tpu as pltpu
from jax.sharding import PartitionSpec as P

EPSILON = 1e-05
MESH = pl.DeviceIdType.MESH
BF16 = jnp.bfloat16
F32 = jnp.float32


def kernel(
    sections, strips, cols,
    images, cotangent, weights, gains, shifts, switches,
    outs, grads_in, weight_grad, gain_sum, shift_sum,
    w_v, wt_v, inp, mask_own, mask_v, gain_prev, shift_prev, zin, zin_stat, zown, own_stat, ub, slope_prev,
    prev_coef, own_coef, dyin, dy_stat, dzb, dyout, product_v, sums_v, stat_out, sums_out, seed_sums, out_v, gin_v,
    ut_own, ut_all, dz_all, dz_taps, acc_v, swap_out, swap_in, dw_v,
    w_sem, wt_sem, in_sem, pi_s, pi_r, ie_s, ie_r, mp_s, mp_r, me_s, me_r, gp_s, gp_r,
    ux_s, ux_r, dx_s, dx_r, sv_s, sv_r,
    fz_s, fz_r, fs_s, fs_r, oe_s, oe_r, os_s, os_r, bz_s, bz_r, bs_s, bs_r, ls_s,
    out_sem, po_s, po_r, gin_sem, pg_s, pg_r,
    ut_s, ut_r, uf_s, uf_r, dz_s, dz_r, sw_s, sw_r, dw_sem,
):
    sec = lax.axis_index("section")
    row = lax.axis_index("rows")
    batches, _, tall, half = inp.shape
    ch = 2 * half
    px = tall - 2 * cols
    strip = px // 2
    groups = tall // cols
    chips = strips // 2
    local = float(2 * px)
    total = local * chips
    first, last, decoder = sec == 0, sec == sections - 1, sec == sections // 2
    late = sec >= sections // 2
    core = row % 2
    partner = row + 1 - 2 * core
    has_up, has_down = row >= 2, row < strips - 2
    centre = pl.ds(cols, px)
    chip = row // 2
    team, seat = row // 4, row % 4
    lanes = dz_all.shape[3]
    block = ut_all.shape[3]
    share = block // 4
    mine = pl.multiple_of(cols + strip * core, cols)

    def channels(h):
        return pl.ds(pl.multiple_of(h * half, half), half)

    def w_copies():
        return [
            pltpu.make_async_copy(weights.at[:, channels(h), channels(core)], w_v.at[h], w_sem.at[h]) for h in range(2)
        ]

    def wt_copies():
        return [
            pltpu.make_async_copy(weights.at[:, channels(core), channels(h)], wt_v.at[h], wt_sem.at[h]) for h in range(2)
        ]

    def in_copy(src, m):
        return pltpu.make_async_copy(src.at[m, :, :, channels(core)], inp.at[m, :, pl.ds(mine, strip), :], in_sem.at[m])

    for copy in w_copies() + wt_copies():
        copy.start()

    @pl.when(first)
    def _():
        for m in range(batches):
            in_copy(images, m).start()

    @pl.when(last)
    def _():
        for m in range(batches):
            in_copy(cotangent, m).start()

    barrier = pltpu.get_barrier_semaphore()
    for s in range(sections):
        @pl.when((sec >= s - 1) & (sec <= s + 1))
        def _():
            def greet(i, carry):
                @pl.when((s != sec) | (i != row))
                def _():
                    pl.semaphore_signal(barrier, inc=1, device_id=(jnp.int32(s), i), device_id_type=MESH)
                return carry
            lax.fori_loop(0, strips, greet, 0)

    acc_v[...] = jnp.zeros_like(acc_v)
    sums_v[...] = jnp.zeros_like(sums_v)

    for m in range(batches):
        for i in range(2):
            for at in (0, dz_all.shape[2] - cols):
                dz_all[m, i, pl.ds(at, cols), :] = jnp.zeros((cols, lanes), BF16)

    @pl.when(decoder)
    def _():
        wide = cols // 2
        windows_at = lax.broadcasted_iota(jnp.int32, (cols, wide), 1)
        places = lax.broadcasted_iota(jnp.int32, (cols, wide), 0)
        pick = (lax.shift_right_logical(places, 1) == windows_at).astype(F32)
        table = lax.dot_general(
            pick, switches[...].astype(F32), (((1,), (1,)), ((), ())), preferred_element_type=F32
        )
        odd = jnp.bitwise_and(lax.broadcasted_iota(jnp.int32, (cols, 128), 0), 1).astype(F32)
        windows = strip // cols // 2
        for m in range(batches):
            for i in range(2):
                for w in range(windows):
                    at = (m * 2 + i) * windows + w
                    value = jnp.broadcast_to(table[:, at : at + 1], (cols, 128))
                    for p in range(2):
                        hit = (jnp.abs(value - (2.0 * p + odd)) < 0.5).astype(F32).astype(BF16)
                        mask_own[m, i, pl.ds((2 * w + p) * cols, cols), :] = hit
        for m in range(batches):
            mask_v[m, :, pl.ds(mine, strip), :] = mask_own[m]

    @pl.when(jnp.logical_not(decoder))
    def _():
        mask_v[...] = jnp.ones_like(mask_v)

    near = 1 + jnp.where(sec > 0, 1, 0) + jnp.where(sec < sections - 1, 1, 0)
    pl.semaphore_wait(barrier, near * strips - 1)

    def remote(src, dst, send, recv, s, i):
        return pltpu.make_async_remote_copy(
            src_ref=src, dst_ref=dst, send_sem=send, recv_sem=recv, device_id=(s, i), device_id_type=MESH
        )

    def to_partner(src_at, dst_at, send, recv):
        return remote(src_at(1 - core), dst_at(pl.ds(mine, strip)), send, recv, sec, partner)

    def start_argument(src_at, dst_at, pair_sems, edge_sems):
        to_partner(src_at, dst_at, *pair_sems).start()

        @pl.when((core == 1) & has_down)
        def _():
            for i in range(2):
                remote(
                    src_at(i, pl.ds(strip - cols, cols)), dst_at(pl.ds(0, cols)),
                    edge_sems[0].at[i], edge_sems[1].at[0], sec, row + 1 + i,
                ).start()

        @pl.when((core == 0) & has_up)
        def _():
            for i in range(2):
                remote(
                    src_at(i, pl.ds(0, cols)), dst_at(pl.ds(cols + px, cols)),
                    edge_sems[0].at[i], edge_sems[1].at[1], sec, row - 2 + i,
                ).start()

    def argument_arrived(src_at, dst_at, pair_sems, edge_sems):
        to_partner(src_at, dst_at, *pair_sems).wait_recv()

        @pl.when(has_up)
        def _():
            remote(
                src_at(0, pl.ds(0, cols)), dst_at(pl.ds(0, cols)), edge_sems[0].at[0], edge_sems[1].at[0], sec, row
            ).wait_recv()

        @pl.when(has_down)
        def _():
            remote(
                src_at(0, pl.ds(0, cols)), dst_at(pl.ds(cols + px, cols)), edge_sems[0].at[0], edge_sems[1].at[1],
                sec, row,
            ).wait_recv()

    def argument_sent(src_at, dst_at, pair_sems, edge_sems):
        to_partner(src_at, dst_at, *pair_sems).wait_send()

        @pl.when(((core == 1) & has_down) | ((core == 0) & has_up))
        def _():
            for i in range(2):
                remote(
                    src_at(i, pl.ds(0, cols)), dst_at(pl.ds(0, cols)), edge_sems[0].at[i], edge_sems[1].at[0], sec, row
                ).wait_send()

    def input_parts(src, m):
        return (
            lambda i, r=pl.ds(0, strip): src.at[m, :, r, channels(i)],
            lambda r: inp.at[m, :, r, :],
            (pi_s.at[m], pi_r.at[m]),
            (ie_s.at[m], ie_r.at[m]),
        )

    mask_parts = (
        lambda i, r=pl.ds(0, strip): mask_own.at[:, :, r, :],
        lambda r: mask_v.at[:, :, r, :],
        (mp_s, mp_r),
        (me_s, me_r),
    )

    @pl.when(first)
    def _():
        for m in range(batches):
            start_argument(*input_parts(images, m))

    @pl.when(last)
    def _():
        for m in range(batches):
            start_argument(*input_parts(cotangent, m))

    @pl.when(decoder)
    def _():
        start_argument(*mask_parts)

    def affine_sends():
        return (
            remote(gains, gain_prev, gp_s.at[0], gp_r.at[0], sec + 1, row),
            remote(shifts, shift_prev, gp_s.at[1], gp_r.at[1], sec + 1, row),
        )

    @pl.when(sec < sections - 1)
    def _():
        for copy in affine_sends():
            copy.start()

    quarter = half // 2

    def block_sends(src, src_from, dst, send, recv, m, s):
        def piece(k, src_row, dst_row, rows, i):
            def one(h):
                part = pl.ds(h * quarter, quarter)
                return remote(
                    src.at[m, :, pl.ds(src_from + src_row, rows), part], dst.at[m, :, pl.ds(dst_row, rows), part],
                    send.at[m, k, h], recv.at[m, k, h], s, i,
                )
            return one

        return (
            piece(0, 0, cols, px, row), piece(1, px - cols, 0, cols, row + 2), piece(2, 0, cols + px, cols, row - 2)
        )

    def each_edge(parts, h, act):
        _, to_down, to_up = parts

        @pl.when(has_down)
        def _():
            act(to_down(h))

        @pl.when(has_up)
        def _():
            act(to_up(h))

    def edges_arrived(parts, h):
        _, to_down, to_up = parts

        @pl.when(has_up)
        def _():
            to_down(h).wait_recv()

        @pl.when(has_down)
        def _():
            to_up(h).wait_recv()

    def send_block(parts, h):
        each_edge(parts, h, start)
        parts[0](h).start()

    def block_sent(parts):
        for h in range(2):
            each_edge(parts, h, sent)
            parts[0](h).wait_send()

    def start(copy):
        copy.start()

    def sent(copy):
        copy.wait_send()

    def came(copy):
        copy.wait_recv()

    def z_sends(m, s):
        return block_sends(zown, cols, zin, fz_s, fz_r, m, s)

    def own_edges(m):
        return block_sends(zown, cols, zown, oe_s, oe_r, m, sec)

    def dy_sends(m, s):
        return block_sends(dyout, 0, dyin, bz_s, bz_r, m, s)

    def stats_each(src, dst, send, recv, m, s, same, act):
        def one(d, carry):
            q = chip + d
            q = jnp.where(q >= chips, q - chips, q)
            act(remote(src.at[m], dst.at[m, chip], send.at[m, d], recv.at[m, d], s, 2 * q + core))
            return carry
        lax.fori_loop(1 if same else 0, chips, one, 0)

    def start_stats(src, dst, send, recv, m, s, same):
        stats_each(src, dst, send, recv, m, s, same, start)
        if same:
            dst[m, chip] = src[m]

    def wait_stats(src, dst, send, recv, m, same):
        stats_each(src, dst, send, recv, m, sec, same, came)

    down_stats = (stat_out, zin_stat, fs_s, fs_r)
    same_stats = (stat_out, own_stat, os_s, os_r)
    back_stats = (sums_out, dy_stat, bs_s, bs_r)
    seed_stats = (seed_sums, dy_stat, ls_s, bs_r)

    def join(stats_ref, m):
        means, squares = stats_ref[m, :, 0, :], stats_ref[m, :, 1, :]
        mean = jnp.sum(means, 0, keepdims=True) / float(chips)
        off = means - mean
        var = (jnp.sum(squares, 0, keepdims=True) + local * jnp.sum(off * off, 0, keepdims=True)) / total
        at = (jnp.maximum(chip - 1, 0), chip, jnp.minimum(chip + 1, chips - 1))
        return lax.rsqrt(var + EPSILON), [stats_ref[m, i, pl.ds(0, 1), :] - mean for i in at]

    def kind(g):
        return 0 if g == 0 else 2 if g == groups - 1 else 1

    def inside(g, values):
        if kind(g) == 1:
            return values
        return jnp.where(has_up if kind(g) == 0 else has_down, values, jnp.zeros_like(values))

    def group(g):
        return pl.ds(g * cols, cols)

    column = lax.broadcasted_iota(jnp.int32, (1, cols, quarter), 1)

    def taps_joined(parts, left, right):
        def moved(values, by, edge):
            turned = pltpu.roll(values, by % (2 * px), 0).reshape(2 * px // cols, cols, quarter)
            return jnp.where(column == edge, 0.0, turned).reshape(2 * px, quarter)
        return parts[1] + moved(parts[left], 1, 0) + moved(parts[right], -1, cols - 1)

    def pass_on(operand, send, recv, m, h):
        part = operand.at[m, core, :, :, pl.ds(h * quarter, quarter)]
        return remote(part, part, send.at[m, h], recv.at[m, h], sec, partner)

    def products(operand, w, m, h, r_at, part):
        def one(c):
            acc = jnp.zeros((2 * px, part.size), F32)
            for r in range(3):
                left = operand[m, h, :, pl.ds(r_at(r) * cols, px), :].reshape(2 * px, half)
                acc += jnp.dot(left, w[h, 3 * r + c, :, part], preferred_element_type=F32)
            return acc
        return one

    def convolve(operand, w, send, recv, m, r_at, left, right, between, use):
        mine_first = products(operand, w, m, core, r_at, pl.ds(0, half))
        for c in range(3):
            product_v[c] = mine_first(c)
        for h in range(2):
            pass_on(operand, send, recv, m, h).wait_recv()
        between()
        for h in range(2):
            part = pl.ds(h * quarter, quarter)
            then = products(operand, w, m, 1 - core, r_at, part)
            use(h, part, taps_joined([product_v[c, :, part] + then(c) for c in range(3)], left, right))

    def turned_copy(m, q):
        src = ut_own.at[m, pl.ds(pl.multiple_of((q // 2) * block, block), block), :]
        return src, ut_all.at[m, core, chip]

    thirds = [1 + (chips - 1) * i // 3 for i in range(4)]

    def turned_each(m, act, low=1, high=chips):
        def one(d, carry):
            q = chip + d
            q = jnp.where(q >= chips, q - chips, q)
            src, dst = turned_copy(m, q)
            act(remote(src, dst, ut_s.at[m, d], ut_r.at[m, d], sec, 2 * q + core))
            return carry
        lax.fori_loop(low, high, one, 0)

    def turn_inputs(m):
        for h in range(2):
            ut_own[m, pl.ds(h * half, half), :] = ub[m, h, core, centre, :].T
        mine_at = pl.ds(pl.multiple_of(team * block, block), block)
        ut_all[m, core, chip] = ut_own[m, mine_at, :]

    def send_turned_third(m, i):
        @pl.when(late & (m >= 0) & (m < batches))
        def _():
            if i == 0:
                turn_inputs(m)
            turned_each(m, start, thirds[i], thirds[i + 1])

    def turned_relay(m):
        return remote(ut_all.at[m, core], ut_all.at[m, core], uf_s.at[m], uf_r.at[m], sec, partner)

    def relay_turned(m):
        turned_each(m, came)
        turned_relay(m).start()

    def relay_all():
        def one(m, carry):
            relay_turned(m)
            return carry
        lax.fori_loop(0, batches, one, 0)

    def dz_copy(m, i):
        src = dzb.at[m, (i % 4) // 2, core, centre, pl.ds(pl.multiple_of(i % 2 * lanes, lanes), lanes)]
        dst = dz_all.at[m, core, pl.ds(pl.multiple_of(cols + chip * px, cols), px), :]
        return src, dst

    def dz_each(m, act):
        def one(d, carry):
            i = row + d
            i = jnp.where(i >= strips, i - strips, i)
            src, dst = dz_copy(m, i)
            act(remote(src, dst, dz_s.at[m, d], dz_r.at[m, d], sec, i))
            return carry
        lax.fori_loop(1, strips, one, 0)

    def send_dz(m):
        dz_each(m, start)
        dz_all[m, core, pl.ds(pl.multiple_of(cols + chip * px, cols), px), :] = dzb[
            m, seat // 2, core, centre, pl.ds(pl.multiple_of(seat % 2 * lanes, lanes), lanes)
        ]

    def gather_taps(m):
        dz_each(m, came)
        relayed = ut_all.at[m, 1 - core]
        pltpu.make_async_copy(relayed, relayed, uf_r.at[m]).wait()
        rows = dz_all.shape[2]
        edge = lax.broadcasted_iota(jnp.int32, (1, cols, lanes), 1)
        for i in range(2):
            values = dz_all[m, i].astype(F32)
            for c, by, gone in ((0, rows - 1, cols - 1), (2, 1, 0)):
                turned = pltpu.roll(values, by, 0).reshape(rows // cols, cols, lanes)
                turned = jnp.where(edge == gone, 0.0, turned).reshape(rows, lanes)
                dz_taps[i, :, pl.ds(c * lanes, lanes)] = turned.astype(BF16)
            dz_taps[i, :, pl.ds(lanes, lanes)] = dz_all[m, i]

    def kernel_row(m, r):
        part = jnp.zeros((block, 3 * lanes), F32)
        for i in range(2):
            left = jnp.concatenate([ut_all[m, i, q] for q in range(chips)], axis=1)
            part += jnp.dot(
                left, dz_taps[i, pl.ds((2 - r) * cols, px * (strips // 2)), :], preferred_element_type=F32
            )
        return part

    def add_gradients(m):
        gather_taps(m)
        for r in range(3):
            acc_v[r] = acc_v[r] + kernel_row(m, r)

    def forward(m):
        @pl.when(first)
        def _():
            in_copy(images, m).wait()
            argument_arrived(*input_parts(images, m))
            for i in range(2):
                for g in range(groups):
                    ub[m, core, i, group(g), :] = inside(g, inp[m, i, group(g), :])
            for h in range(2):
                pass_on(ub, ux_s, ux_r, m, h).start()

        @pl.when(sec > 0)
        def _():
            @pl.when(m == 0)
            def _():
                for copy in affine_sends():
                    copy.wait_recv()

                @pl.when(decoder)
                def _():
                    argument_arrived(*mask_parts)

            wait_stats(*down_stats, m, False)
            inv, offs = join(zin_stat, m)
            prev_coef[m, pl.ds(0, 1), :] = inv
            prev_coef[m, pl.ds(1, 1), :] = offs[1]
            slant = 0.5 * inv * gain_prev[:, channels(core)]
            level = [slant * off + 0.5 * shift_prev[:, channels(core)] for off in offs]
            sends = z_sends(m, sec)
            for h in range(2):
                at, part = pl.ds(h * quarter, quarter), slice(h * quarter, (h + 1) * quarter)
                edges_arrived(sends, h)
                sends[0](h).wait_recv()
                for i in range(2):
                    for g in range(groups):
                        gate = jnp.concatenate([mask_v[m, i, group(g), :].astype(F32)] * (quarter // 128), axis=1)
                        halved = zin[m, i, group(g), at].astype(F32) * slant[:, part] + level[kind(g)][:, part]
                        turn = jnp.tanh(halved)
                        bent = halved * turn
                        ub[m, core, i, group(g), at] = inside(g, ((halved + bent) * gate).astype(BF16))
                        if kind(g) == 1:
                            slope = (0.5 + 0.5 * turn) * (1.0 + halved - bent)
                            slope_prev[m, i, pl.ds((g - 1) * cols, cols), at] = slope
                pass_on(ub, ux_s, ux_r, m, h).start()

        @pl.when(m == 0)
        def _():
            for copy in w_copies():
                copy.wait()

        def use(h, part, conv):
            mean = jnp.sum(conv, 0, keepdims=True) / local
            conv = conv - mean
            stat_out[m, pl.ds(0, 1), part] = mean
            stat_out[m, pl.ds(1, 1), part] = jnp.sum(conv * conv, 0, keepdims=True)
            zown[m, :, centre, part] = conv.reshape(2, px, quarter).astype(BF16)

            @pl.when(sec < sections - 1)
            def _():
                if h == 1:
                    start_stats(*down_stats, m, sec + 1, False)
                send_block(z_sends(m, sec + 1), h)

        convolve(ub, w_v, ux_s, ux_r, m, lambda r: r, 0, 2, lambda: None, use)
        start_stats(*same_stats, m, sec, True)
        for h in range(2):
            each_edge(own_edges(m), h, start)

    def finish(m):
        wait_stats(*same_stats, m, True)
        inv, offs = join(own_stat, m)
        scale = inv * gains[:, channels(core)]
        own_coef[m, pl.ds(0, 1), :] = inv
        own_coef[m, pl.ds(1, 1), :] = scale
        for e in range(3):
            own_coef[m, pl.ds(2 + e, 1), :] = offs[e]
        slant = 0.5 * scale
        level = [slant * off + 0.5 * shifts[:, channels(core)] for off in offs]
        for h in range(2):
            edges_arrived(own_edges(m), h)

        @pl.when(last)
        def _():
            in_copy(cotangent, m).wait()
            argument_arrived(*input_parts(cotangent, m))
            sums = jnp.zeros((cols, half), F32)
            cross = jnp.zeros((cols, half), F32)
            for i in range(2):
                for g in range(groups):
                    z = zown[m, i, group(g), :].astype(F32)
                    halved = z * slant + level[kind(g)]
                    turn = jnp.tanh(halved)
                    bent = halved * turn
                    dy = inp[m, i, group(g), :].astype(F32) * ((0.5 + 0.5 * turn) * (1.0 + halved - bent))
                    dyin[m, i, group(g), :] = dy.astype(BF16)
                    if kind(g) == 1:
                        out_v[m, i, pl.ds((g - 1) * cols, cols), :] = (halved + bent).astype(BF16)
                        sums += dy
                        cross += dy * z
            one = jnp.sum(sums, 0, keepdims=True)
            cross = jnp.sum(cross, 0, keepdims=True)
            seed_sums[m, pl.ds(0, 1), :] = one
            seed_sums[m, pl.ds(1, 1), :] = inv * (cross + offs[1] * one)
            start_stats(*seed_stats, m, sec, True)

        @pl.when(jnp.logical_not(last))
        def _():
            for i in range(2):
                for g in range(1, groups - 1):
                    halved = zown[m, i, group(g), :].astype(F32) * slant + level[1]
                    out_v[m, i, pl.ds((g - 1) * cols, cols), :] = (halved + halved * jnp.tanh(halved)).astype(BF16)

        for copy in result_copies(out_v, outs, out_sem, po_s, po_r, m):
            copy.start()

    def result_copies(src, dst, sem, send, recv, m):
        here, there = pl.multiple_of(strip * core, cols), pl.multiple_of(strip * (1 - core), cols)
        place = dst.at[m, :, :, channels(core)]
        return (
            pltpu.make_async_copy(src.at[m, :, pl.ds(here, strip), :], place, sem.at[m]),
            remote(src.at[m, :, pl.ds(there, strip), :], place, send.at[m], recv.at[m], sec, partner),
        )

    def backward(m):
        @pl.when(last)
        def _():
            wait_stats(*seed_stats, m, True)

        @pl.when(jnp.logical_not(last))
        def _():
            wait_stats(*back_stats, m, False)

        first_sum = jnp.sum(dy_stat[m, :, 0, :], 0, keepdims=True)
        cross_sum = jnp.sum(dy_stat[m, :, 1, :], 0, keepdims=True)
        sums_v[core, pl.ds(0, 1), :] = sums_v[core, pl.ds(0, 1), :] + first_sum
        sums_v[core, pl.ds(1, 1), :] = sums_v[core, pl.ds(1, 1), :] + cross_sum
        inv = own_coef[m, pl.ds(0, 1), :]
        scale = own_coef[m, pl.ds(1, 1), :]
        tilt = scale * inv * (cross_sum / total)
        base = [scale * (first_sum / total) + tilt * own_coef[m, pl.ds(2 + e, 1), :] for e in range(3)]
        sends = dy_sends(m, sec)

        for h in range(2):
            at, part = pl.ds(h * quarter, quarter), slice(h * quarter, (h + 1) * quarter)

            @pl.when(jnp.logical_not(last))
            def _():
                edges_arrived(sends, h)
                sends[0](h).wait_recv()

            for i in range(2):
                for g in range(groups):
                    dz = dyin[m, i, group(g), at].astype(F32) * scale[:, part]
                    dz = dz - zown[m, i, group(g), at].astype(F32) * tilt[:, part] - base[kind(g)][:, part]
                    dzb[m, core, i, group(g), at] = inside(g, dz.astype(BF16))
            pass_on(dzb, dx_s, dx_r, m, h).start()

        def between():
            @pl.when(first)
            def _():
                send_dz(m)

        def use(h, part, conv):
            gate = jnp.concatenate([mask_v[m, :, centre, :].astype(F32)] * (quarter // 128), axis=2)
            du = (conv.reshape(2, px, quarter) * gate).astype(BF16)
            gin_v[m, :, :, part] = du

            @pl.when(sec > 0)
            def _():
                dy = du.astype(F32) * slope_prev[m, :, :, part]
                dyout[m, :, :, part] = dy.astype(BF16)
                one = jnp.sum(dy.reshape(2 * px, quarter), 0, keepdims=True)
                cross = dy * zin[m, :, centre, part].astype(F32)
                cross = jnp.sum(cross.reshape(2 * px, quarter), 0, keepdims=True)
                sums_out[m, pl.ds(0, 1), part] = one
                sums_out[m, pl.ds(1, 1), part] = prev_coef[m, pl.ds(0, 1), part] * (
                    cross + prev_coef[m, pl.ds(1, 1), part] * one
                )
                if h == 1:
                    start_stats(*back_stats, m, sec - 1, False)
                send_block(dy_sends(m, sec - 1), h)

        convolve(dzb, wt_v, dx_s, dx_r, m, lambda r: 2 - r, 2, 0, between, use)

        for copy in result_copies(gin_v, grads_in, gin_sem, pg_s, pg_r, m):
            copy.start()

        @pl.when((sec > 0) & (sec < sections - 1))
        def _():
            send_dz(m)

    def turn_weights():
        for copy in wt_copies():
            copy.wait()

        def one(i, carry):
            for h in range(2):
                wt_v[h, i] = wt_v[h, i].T
            return carry
        lax.fori_loop(0, 9, one, 0)

    @pl.when(late)
    def _():
        turn_weights()

    def step(t, carry):
        ahead = t - sec
        behind = t - (2 * sections - 1 - sec)

        @pl.when((ahead >= 0) & (ahead < batches))
        def _():
            forward(ahead)

        send_turned_third(ahead, 0)

        @pl.when(jnp.logical_not(late) & (ahead == batches))
        def _():
            def turned(m, carry):
                turn_inputs(m)
                turned_each(m, start)
                return carry
            lax.fori_loop(0, batches, turned, 0)
            turn_weights()

        done = ahead - jnp.where(last, 0, 1)

        @pl.when((behind >= 0) & (behind < batches))
        def _():
            backward(behind)

        send_turned_third(ahead, 1)

        @pl.when((done >= 0) & (done < batches))
        def _():
            finish(done)

        send_turned_third(ahead, 2)

        @pl.when(first & (ahead == batches + 1))
        def _():
            relay_all()

        return carry

    lax.fori_loop(0, 2 * sections - 1 + batches, step, 0)

    remote(sums_v.at[core], sums_v.at[core], sv_s, sv_r, sec, partner).start()

    @pl.when(last)
    def _():
        def send(m, carry):
            send_dz(m)
            return carry

        lax.fori_loop(0, batches, send, 0)

    @pl.when(jnp.logical_not(first))
    def _():
        relay_all()

    def add(m, carry):
        add_gradients(m)
        return carry

    lax.fori_loop(0, batches - 1, add, 0)

    def swap(r, d):
        other = (seat + d) % 4
        return remote(
            swap_out.at[r, pl.ds(pl.multiple_of(other * share, share), share), :], swap_in.at[r, 4 - d - 1],
            sw_s.at[r, d - 1], sw_r.at[r, 4 - d - 1], sec, 4 * team + other,
        )

    gather_taps(batches - 1)
    for r in range(3):
        part = acc_v[r] + kernel_row(batches - 1, r)
        acc_v[r] = part
        swap_out[r] = part.astype(BF16)
        for d in range(1, 4):
            swap(r, d).start()

    def dw_copy(r):
        return pltpu.make_async_copy(dw_v.at[r], weight_grad.at[r], dw_sem.at[r])

    own_rows = pl.ds(pl.multiple_of(seat * share, share), share)
    for r in range(3):
        for c in range(3):
            dw_v[r, c, :, pl.ds(pl.multiple_of(seat * lanes, lanes), lanes)] = acc_v[r, own_rows, pl.ds(c * lanes, lanes)]
        for d in range(1, 4):
            swap(r, 4 - d).wait_recv()
            source = (seat + d) % 4
            for c in range(3):
                dw_v[r, c, :, pl.ds(pl.multiple_of(source * lanes, lanes), lanes)] = swap_in[
                    r, d - 1, :, pl.ds(c * lanes, lanes)
                ].astype(F32)
        dw_copy(r).start()

    for r in range(3):
        dw_copy(r).wait()
        for d in range(1, 4):
            swap(r, d).wait_send()

    @pl.when(decoder)
    def _():
        argument_sent(*mask_parts)

    @pl.when(sec < sections - 1)
    def _():
        for copy in affine_sends():
            copy.wait_send()

    def sums_copy():
        return remote(sums_v.at[core], sums_v.at[core], sv_s, sv_r, sec, partner)

    sums_copy().wait_recv()
    sums_copy().wait_send()
    for h in range(2):
        shift_sum[:, pl.ds(h * half, half)] = sums_v[h, pl.ds(0, 1), :]
        gain_sum[:, pl.ds(h * half, half)] = sums_v[h, pl.ds(1, 1), :]

    def drain(m, carry):
        for src, dst, sems in ((out_v, outs, (out_sem, po_s, po_r)), (gin_v, grads_in, (gin_sem, pg_s, pg_r))):
            here, there = result_copies(src, dst, *sems, m)
            here.wait()
            there.wait_send()
            remote(
                src.at[m, :, pl.ds(0, strip), :], dst.at[m, :, :, channels(1 - core)], sems[1].at[m], sems[2].at[m],
                sec, partner,
            ).wait_recv()

        turned_each(m, sent)
        turned_relay(m).wait_send()
        dz_each(m, sent)
        for h in range(2):
            pass_on(ub, ux_s, ux_r, m, h).wait_send()
            pass_on(dzb, dx_s, dx_r, m, h).wait_send()

        @pl.when(first)
        def _():
            argument_sent(*input_parts(images, m))

        @pl.when(last)
        def _():
            argument_sent(*input_parts(cotangent, m))
            stats_each(*seed_stats, m, sec, True, sent)

        @pl.when(sec < sections - 1)
        def _():
            stats_each(*down_stats, m, sec + 1, False, sent)
            block_sent(z_sends(m, sec + 1))

        stats_each(*same_stats, m, sec, True, sent)
        for h in range(2):
            each_edge(own_edges(m), h, sent)

        @pl.when(sec > 0)
        def _():
            stats_each(*back_stats, m, sec - 1, False, sent)
            block_sent(dy_sends(m, sec - 1))

        return carry

    lax.fori_loop(0, batches, drain, 0)


def settle(*refs):
    count = (len(refs) - 2) // 3
    sources, targets, stages = refs[:count], refs[count : 2 * count], refs[2 * count : 3 * count]
    moves = []
    for src, dst, stage in zip(sources, targets, stages):
        if len(src.shape) == 2:
            moves.append((src, dst, stage))
        else:
            moves += [(src.at[i], dst.at[i], stage.at[i]) for i in range(src.shape[0])]
    ins = [pltpu.make_async_copy(src, stage, refs[-2].at[i]) for i, (src, dst, stage) in enumerate(moves)]
    outs = [pltpu.make_async_copy(stage, dst, refs[-1].at[i]) for i, (src, dst, stage) in enumerate(moves)]
    for copy in ins:
        copy.start()
    for come, go in zip(ins, outs):
        come.wait()
        go.start()
    for copy in outs:
        copy.wait()


def body(images, switches, conv_weights, gains, shifts, cotangent):
    sections = lax.axis_size("section")
    strips = lax.axis_size("rows")
    batches, pictures, strip_rows, cols, ch = images.shape
    strip = strip_rows * cols
    px = 2 * strip
    tall = px + 2 * cols
    anywhere = pl.BlockSpec(memory_space=pl.ANY)
    vmem = pl.BlockSpec(memory_space=pltpu.VMEM)
    dma = pltpu.SemaphoreType.DMA
    flops = 3 * 2 * 9 * ch * ch * batches * px
    share = ch // strips
    chips = strips // 2
    outs, grads_in, weight_grad, gain_sum, shift_sum = pl.pallas_call(
        functools.partial(kernel, sections, strips, cols),
        out_shape=(
            jax.ShapeDtypeStruct((batches, pictures, strip, ch), BF16),
            jax.ShapeDtypeStruct((batches, pictures, strip, ch), BF16),
            jax.ShapeDtypeStruct((3, 3, share, ch), F32),
            jax.ShapeDtypeStruct((1, ch), F32),
            jax.ShapeDtypeStruct((1, ch), F32),
        ),
        in_specs=[anywhere, anywhere, anywhere, vmem, vmem, vmem],
        out_specs=(anywhere, anywhere, anywhere, vmem, vmem),
        scratch_shapes=[
            pltpu.VMEM((2, 9, ch // 2, ch // 2), BF16),
            pltpu.VMEM((2, 9, ch // 2, ch // 2), BF16),
            pltpu.VMEM((batches, 2, tall, ch // 2), BF16),
            pltpu.VMEM((batches, 2, strip, 128), BF16),
            pltpu.VMEM((batches, 2, tall, 128), BF16),
            pltpu.VMEM((1, ch), F32),
            pltpu.VMEM((1, ch), F32),
            pltpu.VMEM((batches, 2, tall, ch // 2), BF16),
            pltpu.VMEM((batches, chips, 2, ch // 2), F32),
            pltpu.VMEM((batches, 2, tall, ch // 2), BF16),
            pltpu.VMEM((batches, chips, 2, ch // 2), F32),
            pltpu.VMEM((batches, 2, 2, tall, ch // 2), BF16),
            pltpu.VMEM((batches, 2, px, ch // 2), F32),
            pltpu.VMEM((batches, 2, ch // 2), F32),
            pltpu.VMEM((batches, 8, ch // 2), F32),
            pltpu.VMEM((batches, 2, tall, ch // 2), BF16),
            pltpu.VMEM((batches, chips, 2, ch // 2), F32),
            pltpu.VMEM((batches, 2, 2, tall, ch // 2), BF16),
            pltpu.VMEM((batches, 2, px, ch // 2), BF16),
            pltpu.VMEM((3, 2 * px, ch // 2), F32),
            pltpu.VMEM((2, 2, ch // 2), F32),
            pltpu.VMEM((batches, 2, ch // 2), F32),
            pltpu.VMEM((batches, 2, ch // 2), F32),
            pltpu.VMEM((batches, 2, ch // 2), F32),
            pltpu.VMEM((batches, 2, px, ch // 2), BF16),
            pltpu.VMEM((batches, 2, px, ch // 2), BF16),
            pltpu.VMEM((batches, ch, px), BF16),
            pltpu.VMEM((batches, 2, strips // 2, 4 * share, px), BF16),
            pltpu.VMEM((batches, 2, px * strips // 2 + 2 * cols, ch // 4), BF16),
            pltpu.VMEM((2, px * strips // 2 + 2 * cols, 3 * ch // 4), BF16),
            pltpu.VMEM((3, 4 * share, 3 * ch // 4), F32),
            pltpu.VMEM((3, 4 * share, 3 * ch // 4), BF16),
            pltpu.VMEM((3, 3, share, 3 * ch // 4), BF16),
            pltpu.VMEM((3, 3, share, ch), F32),
            dma((2,)), dma((2,)),
            dma((batches,)),
            dma((batches,)), dma((batches,)),
            dma((batches, 2)), dma((batches, 2)),
            dma, dma,
            dma((2,)), dma((2,)),
            dma((2,)), dma((2,)),
            dma((batches, 2)), dma((batches, 2)),
            dma((batches, 2)), dma((batches, 2)),
            dma, dma,
            dma((batches, 3, 2)), dma((batches, 3, 2)),
            dma((batches, chips)), dma((batches, chips)),
            dma((batches, 3, 2)), dma((batches, 3, 2)),
            dma((batches, chips)), dma((batches, chips)),
            dma((batches, 3, 2)), dma((batches, 3, 2)),
            dma((batches, chips)), dma((batches, chips)),
            dma((batches, chips)),
            dma((batches,)), dma((batches,)), dma((batches,)),
            dma((batches,)), dma((batches,)), dma((batches,)),
            dma((batches, strips // 2)), dma((batches, strips // 2)),
            dma((batches,)), dma((batches,)),
            dma((batches, strips)), dma((batches, strips)),
            dma((3, 3)), dma((3, 3)),
            dma((3,)),
        ],
        compiler_params=pltpu.CompilerParams(
            collective_id=0, has_side_effects=True, vmem_limit_bytes=56 * 2**20
        ),
        cost_estimate=pl.CostEstimate(
            flops=flops, bytes_accessed=2 * 9 * ch * ch * 2, transcendentals=0
        ),
    )(
        images.reshape(batches, pictures, strip, ch),
        cotangent.reshape(batches, pictures, strip, ch),
        conv_weights.reshape(9, ch, ch),
        gains,
        shifts,
        switches.reshape(-1, switches.shape[-1]),
    )
    results = (outs, grads_in, weight_grad, gain_sum, shift_sum)
    outs, grads_in, weight_grad, gain_sum, shift_sum = pl.pallas_call(
        settle,
        out_shape=tuple(jax.ShapeDtypeStruct(r.shape, r.dtype) for r in results),
        in_specs=[anywhere] * 5,
        out_specs=(anywhere,) * 5,
        scratch_shapes=[pltpu.VMEM(r.shape, r.dtype) for r in results] + [dma((2 * batches + 5,))] * 2,
        compiler_params=pltpu.CompilerParams(vmem_limit_bytes=60 * 2**20),
    )(*results)
    shape = (1, batches, pictures, strip_rows, cols, ch)
    return (outs.reshape(shape), grads_in.reshape(shape), weight_grad[None], gain_sum, shift_sum)


def solution(mesh):
    return jax.shard_map(
        body,
        mesh=mesh,
        in_specs=(
            P(None, None, "rows", None, None),
            P(None, None, "rows", None),
            P("section", None, None, None, None),
            P("section", None),
            P("section", None),
            P(None, None, "rows", None, None),
        ),
        out_specs=(
            P("section", None, None, "rows", None, None),
            P("section", None, None, "rows", None, None),
            P("section", None, None, "rows", None),
            P("section", None),
            P("section", None),
        ),
        check_vma=False,
    )
```

```python
import functools

import jax
import jax.numpy as jnp
from jax import lax
from jax.experimental import pallas as pl
from jax.experimental.pallas import tpu as pltpu
from jax.sharding import PartitionSpec as P

EPSILON = 1e-05
MESH = pl.DeviceIdType.MESH
BF16 = jnp.bfloat16
F32 = jnp.float32


def kernel(
    sections, strips, cols,
    images, cotangent, weights, gains, shifts, switches,
    outs, grads_in, weight_grad, gain_sum, shift_sum,
    w_v, wt_v, inp, mask_own, mask_v, gain_prev, shift_prev, zin, zin_stat, zown, own_stat, ub, slope_prev,
    prev_coef, own_coef, dyin, dy_stat, dzb, dyout, product_v, sums_v, stat_out, sums_out, seed_sums, out_v, gin_v,
    ut_own, ut_all, dz_all, dz_taps, acc_v, swap_out, swap_in, dw_v,
    w_sem, wt_sem, in_sem, pi_s, pi_r, ie_s, ie_r, mp_s, mp_r, me_s, me_r, gp_s, gp_r,
    ux_s, ux_r, dx_s, dx_r, sv_s, sv_r,
    fz_s, fz_r, fs_s, fs_r, oe_s, oe_r, os_s, os_r, bz_s, bz_r, bs_s, bs_r, ls_s,
    out_sem, po_s, po_r, gin_sem, pg_s, pg_r,
    ut_s, ut_r, uf_s, uf_r, dz_s, dz_r, sw_s, sw_r, dw_sem,
):
    sec = lax.axis_index("section")
    row = lax.axis_index("rows")
    batches, _, tall, half = inp.shape
    ch = 2 * half
    px = tall - 2 * cols
    strip = px // 2
    groups = tall // cols
    chips = strips // 2
    local = float(2 * px)
    total = local * chips
    first, last, decoder = sec == 0, sec == sections - 1, sec == sections // 2
    late = sec >= sections // 2
    core = row % 2
    partner = row + 1 - 2 * core
    has_up, has_down = row >= 2, row < strips - 2
    centre = pl.ds(cols, px)
    chip = row // 2
    team, seat = row // 4, row % 4
    lanes = dz_all.shape[3]
    block = ut_all.shape[3]
    share = block // 4
    mine = pl.multiple_of(cols + strip * core, cols)

    def channels(h):
        return pl.ds(pl.multiple_of(h * half, half), half)

    def w_copies():
        return [
            pltpu.make_async_copy(weights.at[:, channels(h), channels(core)], w_v.at[h], w_sem.at[h]) for h in range(2)
        ]

    def wt_copies():
        return [
            pltpu.make_async_copy(weights.at[:, channels(core), channels(h)], wt_v.at[h], wt_sem.at[h]) for h in range(2)
        ]

    def in_copy(src, m):
        return pltpu.make_async_copy(src.at[m, :, :, channels(core)], inp.at[m, :, pl.ds(mine, strip), :], in_sem.at[m])

    for copy in w_copies() + wt_copies():
        copy.start()

    @pl.when(first)
    def _():
        for m in range(batches):
            in_copy(images, m).start()

    @pl.when(last)
    def _():
        for m in range(batches):
            in_copy(cotangent, m).start()

    barrier = pltpu.get_barrier_semaphore()
    for s in range(sections):
        @pl.when((sec >= s - 1) & (sec <= s + 1))
        def _():
            def greet(i, carry):
                @pl.when((s != sec) | (i != row))
                def _():
                    pl.semaphore_signal(barrier, inc=1, device_id=(jnp.int32(s), i), device_id_type=MESH)
                return carry
            lax.fori_loop(0, strips, greet, 0)

    acc_v[...] = jnp.zeros_like(acc_v)
    sums_v[...] = jnp.zeros_like(sums_v)

    for m in range(batches):
        for i in range(2):
            for at in (0, dz_all.shape[2] - cols):
                dz_all[m, i, pl.ds(at, cols), :] = jnp.zeros((cols, lanes), BF16)

    @pl.when(decoder)
    def _():
        wide = cols // 2
        windows_at = lax.broadcasted_iota(jnp.int32, (cols, wide), 1)
        places = lax.broadcasted_iota(jnp.int32, (cols, wide), 0)
        pick = (lax.shift_right_logical(places, 1) == windows_at).astype(F32)
        table = lax.dot_general(
            pick, switches[...].astype(F32), (((1,), (1,)), ((), ())), preferred_element_type=F32
        )
        odd = jnp.bitwise_and(lax.broadcasted_iota(jnp.int32, (cols, 128), 0), 1).astype(F32)
        windows = strip // cols // 2
        for m in range(batches):
            for i in range(2):
                for w in range(windows):
                    at = (m * 2 + i) * windows + w
                    value = jnp.broadcast_to(table[:, at : at + 1], (cols, 128))
                    for p in range(2):
                        hit = (jnp.abs(value - (2.0 * p + odd)) < 0.5).astype(F32).astype(BF16)
                        mask_own[m, i, pl.ds((2 * w + p) * cols, cols), :] = hit
        for m in range(batches):
            mask_v[m, :, pl.ds(mine, strip), :] = mask_own[m]

    @pl.when(jnp.logical_not(decoder))
    def _():
        mask_v[...] = jnp.ones_like(mask_v)

    near = 1 + jnp.where(sec > 0, 1, 0) + jnp.where(sec < sections - 1, 1, 0)
    pl.semaphore_wait(barrier, near * strips - 1)

    def remote(src, dst, send, recv, s, i):
        return pltpu.make_async_remote_copy(
            src_ref=src, dst_ref=dst, send_sem=send, recv_sem=recv, device_id=(s, i), device_id_type=MESH
        )

    def to_partner(src_at, dst_at, send, recv):
        return remote(src_at(1 - core), dst_at(pl.ds(mine, strip)), send, recv, sec, partner)

    def start_argument(src_at, dst_at, pair_sems, edge_sems):
        to_partner(src_at, dst_at, *pair_sems).start()

        @pl.when((core == 1) & has_down)
        def _():
            for i in range(2):
                remote(
                    src_at(i, pl.ds(strip - cols, cols)), dst_at(pl.ds(0, cols)),
                    edge_sems[0].at[i], edge_sems[1].at[0], sec, row + 1 + i,
                ).start()

        @pl.when((core == 0) & has_up)
        def _():
            for i in range(2):
                remote(
                    src_at(i, pl.ds(0, cols)), dst_at(pl.ds(cols + px, cols)),
                    edge_sems[0].at[i], edge_sems[1].at[1], sec, row - 2 + i,
                ).start()

    def argument_arrived(src_at, dst_at, pair_sems, edge_sems):
        to_partner(src_at, dst_at, *pair_sems).wait_recv()

        @pl.when(has_up)
        def _():
            remote(
                src_at(0, pl.ds(0, cols)), dst_at(pl.ds(0, cols)), edge_sems[0].at[0], edge_sems[1].at[0], sec, row
            ).wait_recv()

        @pl.when(has_down)
        def _():
            remote(
                src_at(0, pl.ds(0, cols)), dst_at(pl.ds(cols + px, cols)), edge_sems[0].at[0], edge_sems[1].at[1],
                sec, row,
            ).wait_recv()

    def argument_sent(src_at, dst_at, pair_sems, edge_sems):
        to_partner(src_at, dst_at, *pair_sems).wait_send()

        @pl.when(((core == 1) & has_down) | ((core == 0) & has_up))
        def _():
            for i in range(2):
                remote(
                    src_at(i, pl.ds(0, cols)), dst_at(pl.ds(0, cols)), edge_sems[0].at[i], edge_sems[1].at[0], sec, row
                ).wait_send()

    def input_parts(src, m):
        return (
            lambda i, r=pl.ds(0, strip): src.at[m, :, r, channels(i)],
            lambda r: inp.at[m, :, r, :],
            (pi_s.at[m], pi_r.at[m]),
            (ie_s.at[m], ie_r.at[m]),
        )

    mask_parts = (
        lambda i, r=pl.ds(0, strip): mask_own.at[:, :, r, :],
        lambda r: mask_v.at[:, :, r, :],
        (mp_s, mp_r),
        (me_s, me_r),
    )

    @pl.when(first)
    def _():
        for m in range(batches):
            start_argument(*input_parts(images, m))

    @pl.when(last)
    def _():
        for m in range(batches):
            start_argument(*input_parts(cotangent, m))

    @pl.when(decoder)
    def _():
        start_argument(*mask_parts)

    def affine_sends():
        return (
            remote(gains, gain_prev, gp_s.at[0], gp_r.at[0], sec + 1, row),
            remote(shifts, shift_prev, gp_s.at[1], gp_r.at[1], sec + 1, row),
        )

    @pl.when(sec < sections - 1)
    def _():
        for copy in affine_sends():
            copy.start()

    def block_sends(src, src_from, dst, send, recv, m, s):
        def body(i):
            return remote(
                src.at[m, i, pl.ds(src_from, px), :], dst.at[m, i, centre, :], send.at[m, i], recv.at[m, i], s, row
            )

        def edge(e, src_row, dst_row, i):
            return remote(
                src.at[m, :, pl.ds(src_from + src_row, cols), :], dst.at[m, :, pl.ds(dst_row, cols), :],
                send.at[m, 2 + e], recv.at[m, 2 + e], s, i,
            )

        return body, lambda: edge(0, px - cols, 0, row + 2), lambda: edge(1, 0, cols + px, row - 2)

    def each_edge(parts, act):
        _, to_down, to_up = parts

        @pl.when(has_down)
        def _():
            act(to_down())

        @pl.when(has_up)
        def _():
            act(to_up())

    def edges_arrived(parts):
        _, to_down, to_up = parts

        @pl.when(has_up)
        def _():
            to_down().wait_recv()

        @pl.when(has_down)
        def _():
            to_up().wait_recv()

    def send_block(parts):
        each_edge(parts, start)
        for i in range(2):
            parts[0](i).start()

    def block_sent(parts):
        each_edge(parts, sent)
        for i in range(2):
            parts[0](i).wait_send()

    def start(copy):
        copy.start()

    def sent(copy):
        copy.wait_send()

    def came(copy):
        copy.wait_recv()

    def z_sends(m, s):
        return block_sends(zown, cols, zin, fz_s, fz_r, m, s)

    def own_edges(m):
        return block_sends(zown, cols, zown, oe_s, oe_r, m, sec)

    def dy_sends(m, s):
        return block_sends(dyout, 0, dyin, bz_s, bz_r, m, s)

    def stats_each(src, dst, send, recv, m, s, same, act):
        def one(d, carry):
            q = chip + d
            q = jnp.where(q >= chips, q - chips, q)
            act(remote(src.at[m], dst.at[m, chip], send.at[m, d], recv.at[m, d], s, 2 * q + core))
            return carry
        lax.fori_loop(1 if same else 0, chips, one, 0)

    def start_stats(src, dst, send, recv, m, s, same):
        stats_each(src, dst, send, recv, m, s, same, start)
        if same:
            dst[m, chip] = src[m]

    def wait_stats(src, dst, send, recv, m, same):
        stats_each(src, dst, send, recv, m, sec, same, came)

    down_stats = (stat_out, zin_stat, fs_s, fs_r)
    same_stats = (stat_out, own_stat, os_s, os_r)
    back_stats = (sums_out, dy_stat, bs_s, bs_r)
    seed_stats = (seed_sums, dy_stat, ls_s, bs_r)

    def join(stats_ref, m):
        means, squares = stats_ref[m, :, 0, :], stats_ref[m, :, 1, :]
        mean = jnp.sum(means, 0, keepdims=True) / float(chips)
        off = means - mean
        var = (jnp.sum(squares, 0, keepdims=True) + local * jnp.sum(off * off, 0, keepdims=True)) / total
        at = (jnp.maximum(chip - 1, 0), chip, jnp.minimum(chip + 1, chips - 1))
        return lax.rsqrt(var + EPSILON), [stats_ref[m, i, pl.ds(0, 1), :] - mean for i in at]

    def kind(g):
        return 0 if g == 0 else 2 if g == groups - 1 else 1

    def inside(g, values):
        if kind(g) == 1:
            return values
        return jnp.where(has_up if kind(g) == 0 else has_down, values, jnp.zeros_like(values))

    def group(g):
        return pl.ds(g * cols, cols)

    column = lax.broadcasted_iota(jnp.int32, (1, cols, half), 1)

    def taps_joined(parts, left, right):
        def moved(values, by, edge):
            turned = pltpu.roll(values, by % (2 * px), 0).reshape(2 * px // cols, cols, half)
            return jnp.where(column == edge, 0.0, turned).reshape(2 * px, half)
        return parts[1] + moved(parts[left], 1, 0) + moved(parts[right], -1, cols - 1)

    def pass_on(operand, send, recv, m, i):
        return remote(operand.at[m, core, i], operand.at[m, core, i], send.at[m, i], recv.at[m, i], sec, partner)

    def products(operand, w, m, h, r_at):
        def one(c):
            acc = jnp.zeros((2 * px, half), F32)
            for r in range(3):
                left = operand[m, h, :, pl.ds(r_at(r) * cols, px), :].reshape(2 * px, half)
                acc += jnp.dot(left, w[h, 3 * r + c], preferred_element_type=F32)
            return acc
        return one

    def convolve(operand, w, send, recv, m, r_at, before_second=None):
        mine_first = products(operand, w, m, core, r_at)
        for c in range(3):
            product_v[c] = mine_first(c)
        for i in range(2):
            pass_on(operand, send, recv, m, i).wait_recv()
        if before_second is not None:
            before_second()
        then = products(operand, w, m, 1 - core, r_at)
        return [product_v[c] + then(c) for c in range(3)]

    def turned_copy(m, q):
        src = ut_own.at[m, pl.ds(pl.multiple_of((q // 2) * block, block), block), :]
        return src, ut_all.at[m, core, chip]

    first_piece = 2

    def turned_each(m, act, low=1, high=chips):
        def one(d, carry):
            q = chip + d
            q = jnp.where(q >= chips, q - chips, q)
            src, dst = turned_copy(m, q)
            act(remote(src, dst, ut_s.at[m, d], ut_r.at[m, d], sec, 2 * q + core))
            return carry
        lax.fori_loop(low, high, one, 0)

    def turn_inputs(m):
        for h in range(2):
            ut_own[m, pl.ds(h * half, half), :] = ub[m, h, core, centre, :].T
        mine_at = pl.ds(pl.multiple_of(team * block, block), block)
        ut_all[m, core, chip] = ut_own[m, mine_at, :]

    def send_turned(m):
        turn_inputs(m)
        turned_each(m, start)

    def turned_relay(m):
        return remote(ut_all.at[m, core], ut_all.at[m, core], uf_s.at[m], uf_r.at[m], sec, partner)

    def relay_turned(m):
        turned_each(m, came)
        turned_relay(m).start()

    def relay_all():
        def one(m, carry):
            relay_turned(m)
            return carry
        lax.fori_loop(0, batches, one, 0)

    def dz_copy(m, i):
        src = dzb.at[m, (i % 4) // 2, core, centre, pl.ds(pl.multiple_of(i % 2 * lanes, lanes), lanes)]
        dst = dz_all.at[m, core, pl.ds(pl.multiple_of(cols + chip * px, cols), px), :]
        return src, dst

    def dz_each(m, act):
        def one(d, carry):
            i = row + d
            i = jnp.where(i >= strips, i - strips, i)
            src, dst = dz_copy(m, i)
            act(remote(src, dst, dz_s.at[m, d], dz_r.at[m, d], sec, i))
            return carry
        lax.fori_loop(1, strips, one, 0)

    def send_dz(m):
        dz_each(m, start)
        dz_all[m, core, pl.ds(pl.multiple_of(cols + chip * px, cols), px), :] = dzb[
            m, seat // 2, core, centre, pl.ds(pl.multiple_of(seat % 2 * lanes, lanes), lanes)
        ]

    def gather_taps(m):
        dz_each(m, came)
        relayed = ut_all.at[m, 1 - core]
        pltpu.make_async_copy(relayed, relayed, uf_r.at[m]).wait()
        rows = dz_all.shape[2]
        edge = lax.broadcasted_iota(jnp.int32, (1, cols, lanes), 1)
        for i in range(2):
            values = dz_all[m, i].astype(F32)
            for c, by, gone in ((0, rows - 1, cols - 1), (2, 1, 0)):
                turned = pltpu.roll(values, by, 0).reshape(rows // cols, cols, lanes)
                turned = jnp.where(edge == gone, 0.0, turned).reshape(rows, lanes)
                dz_taps[i, :, pl.ds(c * lanes, lanes)] = turned.astype(BF16)
            dz_taps[i, :, pl.ds(lanes, lanes)] = dz_all[m, i]

    def kernel_row(m, r):
        part = jnp.zeros((block, 3 * lanes), F32)
        for i in range(2):
            left = jnp.concatenate([ut_all[m, i, q] for q in range(chips)], axis=1)
            part += jnp.dot(
                left, dz_taps[i, pl.ds((2 - r) * cols, px * (strips // 2)), :], preferred_element_type=F32
            )
        return part

    def add_gradients(m):
        gather_taps(m)
        for r in range(3):
            acc_v[r] = acc_v[r] + kernel_row(m, r)

    def forward(m):
        @pl.when(first)
        def _():
            in_copy(images, m).wait()
            argument_arrived(*input_parts(images, m))
            for i in range(2):
                for g in range(groups):
                    ub[m, core, i, group(g), :] = inside(g, inp[m, i, group(g), :])
                pass_on(ub, ux_s, ux_r, m, i).start()

        @pl.when(sec > 0)
        def _():
            @pl.when(m == 0)
            def _():
                for copy in affine_sends():
                    copy.wait_recv()

                @pl.when(decoder)
                def _():
                    argument_arrived(*mask_parts)

            wait_stats(*down_stats, m, False)
            inv, offs = join(zin_stat, m)
            prev_coef[m, pl.ds(0, 1), :] = inv
            prev_coef[m, pl.ds(1, 1), :] = offs[1]
            slant = 0.5 * inv * gain_prev[:, channels(core)]
            level = [slant * off + 0.5 * shift_prev[:, channels(core)] for off in offs]
            sends = z_sends(m, sec)
            edges_arrived(sends)
            for i in range(2):
                sends[0](i).wait_recv()
                for g in range(groups):
                    gate = jnp.concatenate([mask_v[m, i, group(g), :].astype(F32)] * (half // 128), axis=1)
                    halved = zin[m, i, group(g), :].astype(F32) * slant + level[kind(g)]
                    turn = jnp.tanh(halved)
                    bent = halved * turn
                    ub[m, core, i, group(g), :] = inside(g, ((halved + bent) * gate).astype(BF16))
                    if kind(g) == 1:
                        slope_prev[m, i, pl.ds((g - 1) * cols, cols), :] = (0.5 + 0.5 * turn) * (1.0 + halved - bent)
                pass_on(ub, ux_s, ux_r, m, i).start()

        @pl.when(m == 0)
        def _():
            for copy in w_copies():
                copy.wait()

        def early():
            @pl.when(last & (m >= 1))
            def _():
                turn_inputs(m - 1)
                turned_each(m - 1, start, 1, first_piece)

        conv = taps_joined(convolve(ub, w_v, ux_s, ux_r, m, lambda r: r, early), 0, 2)
        mean = jnp.sum(conv, 0, keepdims=True) / local
        conv = conv - mean
        stat_out[m, pl.ds(0, 1), :] = mean
        stat_out[m, pl.ds(1, 1), :] = jnp.sum(conv * conv, 0, keepdims=True)
        zown[m, :, centre, :] = conv.reshape(2, px, half).astype(BF16)

        @pl.when(sec < sections - 1)
        def _():
            start_stats(*down_stats, m, sec + 1, False)
            send_block(z_sends(m, sec + 1))

        start_stats(*same_stats, m, sec, True)
        each_edge(own_edges(m), start)

    def finish(m):
        wait_stats(*same_stats, m, True)
        inv, offs = join(own_stat, m)
        scale = inv * gains[:, channels(core)]
        own_coef[m, pl.ds(0, 1), :] = inv
        own_coef[m, pl.ds(1, 1), :] = scale
        for e in range(3):
            own_coef[m, pl.ds(2 + e, 1), :] = offs[e]
        slant = 0.5 * scale
        level = [slant * off + 0.5 * shifts[:, channels(core)] for off in offs]
        edges_arrived(own_edges(m))

        @pl.when(last)
        def _():
            in_copy(cotangent, m).wait()
            argument_arrived(*input_parts(cotangent, m))
            sums = jnp.zeros((cols, half), F32)
            cross = jnp.zeros((cols, half), F32)
            for i in range(2):
                for g in range(groups):
                    z = zown[m, i, group(g), :].astype(F32)
                    halved = z * slant + level[kind(g)]
                    turn = jnp.tanh(halved)
                    bent = halved * turn
                    dy = inp[m, i, group(g), :].astype(F32) * ((0.5 + 0.5 * turn) * (1.0 + halved - bent))
                    dyin[m, i, group(g), :] = dy.astype(BF16)
                    if kind(g) == 1:
                        out_v[m, i, pl.ds((g - 1) * cols, cols), :] = (halved + bent).astype(BF16)
                        sums += dy
                        cross += dy * z
            one = jnp.sum(sums, 0, keepdims=True)
            cross = jnp.sum(cross, 0, keepdims=True)
            seed_sums[m, pl.ds(0, 1), :] = one
            seed_sums[m, pl.ds(1, 1), :] = inv * (cross + offs[1] * one)
            start_stats(*seed_stats, m, sec, True)

        @pl.when(jnp.logical_not(last))
        def _():
            for i in range(2):
                for g in range(1, groups - 1):
                    halved = zown[m, i, group(g), :].astype(F32) * slant + level[1]
                    out_v[m, i, pl.ds((g - 1) * cols, cols), :] = (halved + halved * jnp.tanh(halved)).astype(BF16)

        for copy in result_copies(out_v, outs, out_sem, po_s, po_r, m):
            copy.start()

    def result_copies(src, dst, sem, send, recv, m):
        here, there = pl.multiple_of(strip * core, cols), pl.multiple_of(strip * (1 - core), cols)
        place = dst.at[m, :, :, channels(core)]
        return (
            pltpu.make_async_copy(src.at[m, :, pl.ds(here, strip), :], place, sem.at[m]),
            remote(src.at[m, :, pl.ds(there, strip), :], place, send.at[m], recv.at[m], sec, partner),
        )

    def backward(m):
        @pl.when(last)
        def _():
            wait_stats(*seed_stats, m, True)

        @pl.when(jnp.logical_not(last))
        def _():
            wait_stats(*back_stats, m, False)

        first_sum = jnp.sum(dy_stat[m, :, 0, :], 0, keepdims=True)
        cross_sum = jnp.sum(dy_stat[m, :, 1, :], 0, keepdims=True)
        sums_v[core, pl.ds(0, 1), :] = sums_v[core, pl.ds(0, 1), :] + first_sum
        sums_v[core, pl.ds(1, 1), :] = sums_v[core, pl.ds(1, 1), :] + cross_sum
        inv = own_coef[m, pl.ds(0, 1), :]
        scale = own_coef[m, pl.ds(1, 1), :]
        tilt = scale * inv * (cross_sum / total)
        base = [scale * (first_sum / total) + tilt * own_coef[m, pl.ds(2 + e, 1), :] for e in range(3)]
        sends = dy_sends(m, sec)

        @pl.when(jnp.logical_not(last))
        def _():
            edges_arrived(sends)

        for i in range(2):
            @pl.when(jnp.logical_not(last))
            def _():
                sends[0](i).wait_recv()

            for g in range(groups):
                dz = dyin[m, i, group(g), :].astype(F32) * scale
                dz = dz - zown[m, i, group(g), :].astype(F32) * tilt - base[kind(g)]
                dzb[m, core, i, group(g), :] = inside(g, dz.astype(BF16))
            pass_on(dzb, dx_s, dx_r, m, i).start()

        def early():
            @pl.when(first)
            def _():
                send_dz(m)

            @pl.when(last & (m == batches - 1))
            def _():
                turn_inputs(m)
                turned_each(m, start, 1, first_piece)

            @pl.when(last)
            def _():
                turned_each(m, start, first_piece, chips)

        gate = jnp.concatenate([mask_v[m, :, centre, :].astype(F32)] * (half // 128), axis=2)
        conv = taps_joined(convolve(dzb, wt_v, dx_s, dx_r, m, lambda r: 2 - r, early), 2, 0)
        du = (conv.reshape(2, px, half) * gate).astype(BF16)
        gin_v[m] = du

        @pl.when(sec > 0)
        def _():
            dy = du.astype(F32) * slope_prev[m]
            dyout[m] = dy.astype(BF16)
            one = jnp.sum(dy.reshape(2 * px, half), 0, keepdims=True)
            cross = jnp.sum((dy * zin[m, :, centre, :].astype(F32)).reshape(2 * px, half), 0, keepdims=True)
            sums_out[m, pl.ds(0, 1), :] = one
            sums_out[m, pl.ds(1, 1), :] = prev_coef[m, pl.ds(0, 1), :] * (cross + prev_coef[m, pl.ds(1, 1), :] * one)
            start_stats(*back_stats, m, sec - 1, False)
            send_block(dy_sends(m, sec - 1))

        for copy in result_copies(gin_v, grads_in, gin_sem, pg_s, pg_r, m):
            copy.start()

        @pl.when((sec > 0) & (sec < sections - 1))
        def _():
            send_dz(m)

    def turn_weights():
        for copy in wt_copies():
            copy.wait()

        def one(i, carry):
            for h in range(2):
                wt_v[h, i] = wt_v[h, i].T
            return carry
        lax.fori_loop(0, 9, one, 0)

    @pl.when(late)
    def _():
        turn_weights()

    def step(t, carry):
        ahead = t - sec
        behind = t - (2 * sections - 1 - sec)

        @pl.when((ahead >= 0) & (ahead < batches))
        def _():
            forward(ahead)

        @pl.when(late & jnp.logical_not(last) & (ahead >= 0) & (ahead < batches))
        def _():
            send_turned(ahead)

        @pl.when(jnp.logical_not(late) & (ahead == batches))
        def _():
            def turned(m, carry):
                send_turned(m)
                return carry
            lax.fori_loop(0, batches, turned, 0)
            turn_weights()

        done = ahead - jnp.where(last, 0, 1)

        @pl.when((behind >= 0) & (behind < batches))
        def _():
            backward(behind)

        @pl.when((done >= 0) & (done < batches))
        def _():
            finish(done)

        @pl.when(first & (ahead == batches + 1))
        def _():
            relay_all()

        return carry

    lax.fori_loop(0, 2 * sections - 1 + batches, step, 0)

    remote(sums_v.at[core], sums_v.at[core], sv_s, sv_r, sec, partner).start()

    @pl.when(last)
    def _():
        def send(m, carry):
            send_dz(m)
            return carry

        lax.fori_loop(0, batches, send, 0)

    @pl.when(jnp.logical_not(first))
    def _():
        relay_all()

    def add(m, carry):
        add_gradients(m)
        return carry

    lax.fori_loop(0, batches - 1, add, 0)

    def swap(r, d):
        other = (seat + d) % 4
        return remote(
            swap_out.at[r, pl.ds(pl.multiple_of(other * share, share), share), :], swap_in.at[r, 4 - d - 1],
            sw_s.at[r, d - 1], sw_r.at[r, 4 - d - 1], sec, 4 * team + other,
        )

    gather_taps(batches - 1)
    for r in range(3):
        part = acc_v[r] + kernel_row(batches - 1, r)
        acc_v[r] = part
        swap_out[r] = part.astype(BF16)
        for d in range(1, 4):
            swap(r, d).start()

    def dw_copy(r):
        return pltpu.make_async_copy(dw_v.at[r], weight_grad.at[r], dw_sem.at[r])

    own_rows = pl.ds(pl.multiple_of(seat * share, share), share)
    for r in range(3):
        for c in range(3):
            dw_v[r, c, :, pl.ds(pl.multiple_of(seat * lanes, lanes), lanes)] = acc_v[r, own_rows, pl.ds(c * lanes, lanes)]
        for d in range(1, 4):
            swap(r, 4 - d).wait_recv()
            source = (seat + d) % 4
            for c in range(3):
                dw_v[r, c, :, pl.ds(pl.multiple_of(source * lanes, lanes), lanes)] = swap_in[
                    r, d - 1, :, pl.ds(c * lanes, lanes)
                ].astype(F32)
        dw_copy(r).start()

    for r in range(3):
        dw_copy(r).wait()
        for d in range(1, 4):
            swap(r, d).wait_send()

    @pl.when(decoder)
    def _():
        argument_sent(*mask_parts)

    @pl.when(sec < sections - 1)
    def _():
        for copy in affine_sends():
            copy.wait_send()

    def sums_copy():
        return remote(sums_v.at[core], sums_v.at[core], sv_s, sv_r, sec, partner)

    sums_copy().wait_recv()
    sums_copy().wait_send()
    for h in range(2):
        shift_sum[:, pl.ds(h * half, half)] = sums_v[h, pl.ds(0, 1), :]
        gain_sum[:, pl.ds(h * half, half)] = sums_v[h, pl.ds(1, 1), :]

    def drain(m, carry):
        for src, dst, sems in ((out_v, outs, (out_sem, po_s, po_r)), (gin_v, grads_in, (gin_sem, pg_s, pg_r))):
            here, there = result_copies(src, dst, *sems, m)
            here.wait()
            there.wait_send()
            remote(
                src.at[m, :, pl.ds(0, strip), :], dst.at[m, :, :, channels(1 - core)], sems[1].at[m], sems[2].at[m],
                sec, partner,
            ).wait_recv()

        turned_each(m, sent)
        turned_relay(m).wait_send()
        dz_each(m, sent)
        for i in range(2):
            pass_on(ub, ux_s, ux_r, m, i).wait_send()
            pass_on(dzb, dx_s, dx_r, m, i).wait_send()

        @pl.when(first)
        def _():
            argument_sent(*input_parts(images, m))

        @pl.when(last)
        def _():
            argument_sent(*input_parts(cotangent, m))
            stats_each(*seed_stats, m, sec, True, sent)

        @pl.when(sec < sections - 1)
        def _():
            stats_each(*down_stats, m, sec + 1, False, sent)
            block_sent(z_sends(m, sec + 1))

        stats_each(*same_stats, m, sec, True, sent)
        each_edge(own_edges(m), sent)

        @pl.when(sec > 0)
        def _():
            stats_each(*back_stats, m, sec - 1, False, sent)
            block_sent(dy_sends(m, sec - 1))

        return carry

    lax.fori_loop(0, batches, drain, 0)


def settle(*refs):
    count = (len(refs) - 2) // 3
    sources, targets, stages = refs[:count], refs[count : 2 * count], refs[2 * count : 3 * count]
    moves = []
    for src, dst, stage in zip(sources, targets, stages):
        if len(src.shape) == 2:
            moves.append((src, dst, stage))
        else:
            moves += [(src.at[i], dst.at[i], stage.at[i]) for i in range(src.shape[0])]
    ins = [pltpu.make_async_copy(src, stage, refs[-2].at[i]) for i, (src, dst, stage) in enumerate(moves)]
    outs = [pltpu.make_async_copy(stage, dst, refs[-1].at[i]) for i, (src, dst, stage) in enumerate(moves)]
    for copy in ins:
        copy.start()
    for come, go in zip(ins, outs):
        come.wait()
        go.start()
    for copy in outs:
        copy.wait()


def body(images, switches, conv_weights, gains, shifts, cotangent):
    sections = lax.axis_size("section")
    strips = lax.axis_size("rows")
    batches, pictures, strip_rows, cols, ch = images.shape
    strip = strip_rows * cols
    px = 2 * strip
    tall = px + 2 * cols
    anywhere = pl.BlockSpec(memory_space=pl.ANY)
    vmem = pl.BlockSpec(memory_space=pltpu.VMEM)
    dma = pltpu.SemaphoreType.DMA
    flops = 3 * 2 * 9 * ch * ch * batches * px
    share = ch // strips
    chips = strips // 2
    outs, grads_in, weight_grad, gain_sum, shift_sum = pl.pallas_call(
        functools.partial(kernel, sections, strips, cols),
        out_shape=(
            jax.ShapeDtypeStruct((batches, pictures, strip, ch), BF16),
            jax.ShapeDtypeStruct((batches, pictures, strip, ch), BF16),
            jax.ShapeDtypeStruct((3, 3, share, ch), F32),
            jax.ShapeDtypeStruct((1, ch), F32),
            jax.ShapeDtypeStruct((1, ch), F32),
        ),
        in_specs=[anywhere, anywhere, anywhere, vmem, vmem, vmem],
        out_specs=(anywhere, anywhere, anywhere, vmem, vmem),
        scratch_shapes=[
            pltpu.VMEM((2, 9, ch // 2, ch // 2), BF16),
            pltpu.VMEM((2, 9, ch // 2, ch // 2), BF16),
            pltpu.VMEM((batches, 2, tall, ch // 2), BF16),
            pltpu.VMEM((batches, 2, strip, 128), BF16),
            pltpu.VMEM((batches, 2, tall, 128), BF16),
            pltpu.VMEM((1, ch), F32),
            pltpu.VMEM((1, ch), F32),
            pltpu.VMEM((batches, 2, tall, ch // 2), BF16),
            pltpu.VMEM((batches, chips, 2, ch // 2), F32),
            pltpu.VMEM((batches, 2, tall, ch // 2), BF16),
            pltpu.VMEM((batches, chips, 2, ch // 2), F32),
            pltpu.VMEM((batches, 2, 2, tall, ch // 2), BF16),
            pltpu.VMEM((batches, 2, px, ch // 2), F32),
            pltpu.VMEM((batches, 2, ch // 2), F32),
            pltpu.VMEM((batches, 8, ch // 2), F32),
            pltpu.VMEM((batches, 2, tall, ch // 2), BF16),
            pltpu.VMEM((batches, chips, 2, ch // 2), F32),
            pltpu.VMEM((batches, 2, 2, tall, ch // 2), BF16),
            pltpu.VMEM((batches, 2, px, ch // 2), BF16),
            pltpu.VMEM((3, 2 * px, ch // 2), F32),
            pltpu.VMEM((2, 2, ch // 2), F32),
            pltpu.VMEM((batches, 2, ch // 2), F32),
            pltpu.VMEM((batches, 2, ch // 2), F32),
            pltpu.VMEM((batches, 2, ch // 2), F32),
            pltpu.VMEM((batches, 2, px, ch // 2), BF16),
            pltpu.VMEM((batches, 2, px, ch // 2), BF16),
            pltpu.VMEM((batches, ch, px), BF16),
            pltpu.VMEM((batches, 2, strips // 2, 4 * share, px), BF16),
            pltpu.VMEM((batches, 2, px * strips // 2 + 2 * cols, ch // 4), BF16),
            pltpu.VMEM((2, px * strips // 2 + 2 * cols, 3 * ch // 4), BF16),
            pltpu.VMEM((3, 4 * share, 3 * ch // 4), F32),
            pltpu.VMEM((3, 4 * share, 3 * ch // 4), BF16),
            pltpu.VMEM((3, 3, share, 3 * ch // 4), BF16),
            pltpu.VMEM((3, 3, share, ch), F32),
            dma((2,)), dma((2,)),
            dma((batches,)),
            dma((batches,)), dma((batches,)),
            dma((batches, 2)), dma((batches, 2)),
            dma, dma,
            dma((2,)), dma((2,)),
            dma((2,)), dma((2,)),
            dma((batches, 2)), dma((batches, 2)),
            dma((batches, 2)), dma((batches, 2)),
            dma, dma,
            dma((batches, 4)), dma((batches, 4)),
            dma((batches, chips)), dma((batches, chips)),
            dma((batches, 4)), dma((batches, 4)),
            dma((batches, chips)), dma((batches, chips)),
            dma((batches, 4)), dma((batches, 4)),
            dma((batches, chips)), dma((batches, chips)),
            dma((batches, chips)),
            dma((batches,)), dma((batches,)), dma((batches,)),
            dma((batches,)), dma((batches,)), dma((batches,)),
            dma((batches, strips // 2)), dma((batches, strips // 2)),
            dma((batches,)), dma((batches,)),
            dma((batches, strips)), dma((batches, strips)),
            dma((3, 3)), dma((3, 3)),
            dma((3,)),
        ],
        compiler_params=pltpu.CompilerParams(
            collective_id=0, has_side_effects=True, vmem_limit_bytes=56 * 2**20
        ),
        cost_estimate=pl.CostEstimate(
            flops=flops, bytes_accessed=2 * 9 * ch * ch * 2, transcendentals=0
        ),
    )(
        images.reshape(batches, pictures, strip, ch),
        cotangent.reshape(batches, pictures, strip, ch),
        conv_weights.reshape(9, ch, ch),
        gains,
        shifts,
        switches.reshape(-1, switches.shape[-1]),
    )
    results = (outs, grads_in, weight_grad, gain_sum, shift_sum)
    outs, grads_in, weight_grad, gain_sum, shift_sum = pl.pallas_call(
        settle,
        out_shape=tuple(jax.ShapeDtypeStruct(r.shape, r.dtype) for r in results),
        in_specs=[anywhere] * 5,
        out_specs=(anywhere,) * 5,
        scratch_shapes=[pltpu.VMEM(r.shape, r.dtype) for r in results] + [dma((2 * batches + 5,))] * 2,
        compiler_params=pltpu.CompilerParams(vmem_limit_bytes=60 * 2**20),
    )(*results)
    shape = (1, batches, pictures, strip_rows, cols, ch)
    return (outs.reshape(shape), grads_in.reshape(shape), weight_grad[None], gain_sum, shift_sum)


def solution(mesh):
    return jax.shard_map(
        body,
        mesh=mesh,
        in_specs=(
            P(None, None, "rows", None, None),
            P(None, None, "rows", None),
            P("section", None, None, None, None),
            P("section", None),
            P("section", None),
            P(None, None, "rows", None, None),
        ),
        out_specs=(
            P("section", None, None, "rows", None, None),
            P("section", None, None, "rows", None, None),
            P("section", None, None, "rows", None),
            P("section", None),
            P("section", None),
        ),
        check_vma=False,
    )
```

```python
import functools

import jax
import jax.numpy as jnp
from jax import lax
from jax.experimental import pallas as pl
from jax.experimental.pallas import tpu as pltpu
from jax.sharding import PartitionSpec as P

EPSILON = 1e-05
MESH = pl.DeviceIdType.MESH
BF16 = jnp.bfloat16
F32 = jnp.float32


def kernel(
    sections, strips, cols,
    images, cotangent, weights, gains, shifts, switches,
    outs, grads_in, weight_grad, gain_sum, shift_sum,
    w_v, wt_v, inp, mask_own, mask_v, gain_prev, shift_prev, zin, zin_stat, zown, own_stat, ub, slope_prev,
    prev_coef, own_coef, dyin, dy_stat, dzb, dyout, product_v, sums_v, stat_out, sums_out, seed_sums, out_v, gin_v,
    ut_own, ut_all, dz_all, dz_taps, acc_v, swap_out, swap_in, dw_v,
    w_sem, wt_sem, in_sem, pi_s, pi_r, ie_s, ie_r, mp_s, mp_r, me_s, me_r, gp_s, gp_r,
    ux_s, ux_r, dx_s, dx_r, sv_s, sv_r,
    fz_s, fz_r, fs_s, fs_r, oe_s, oe_r, os_s, os_r, bz_s, bz_r, bs_s, bs_r, ls_s,
    out_sem, po_s, po_r, gin_sem, pg_s, pg_r,
    ut_s, ut_r, uw_s, uf_s, uf_r, dz_s, dz_r, sw_s, sw_r, dw_sem,
):
    sec = lax.axis_index("section")
    row = lax.axis_index("rows")
    batches, _, tall, half = inp.shape
    ch = 2 * half
    px = tall - 2 * cols
    strip = px // 2
    groups = tall // cols
    chips = strips // 2
    local = float(2 * px)
    total = local * chips
    first, last, decoder = sec == 0, sec == sections - 1, sec == sections // 2
    late = sec >= sections // 2
    core = row % 2
    partner = row + 1 - 2 * core
    has_up, has_down = row >= 2, row < strips - 2
    centre = pl.ds(cols, px)
    chip = row // 2
    team, seat = row // 4, row % 4
    lanes = dz_all.shape[3]
    block = ut_all.shape[3]
    share = block // 4
    mine = pl.multiple_of(cols + strip * core, cols)

    def channels(h):
        return pl.ds(pl.multiple_of(h * half, half), half)

    def w_copies():
        return [
            pltpu.make_async_copy(weights.at[:, channels(h), channels(core)], w_v.at[h], w_sem.at[h]) for h in range(2)
        ]

    def wt_copies():
        return [
            pltpu.make_async_copy(weights.at[:, channels(core), channels(h)], wt_v.at[h], wt_sem.at[h]) for h in range(2)
        ]

    def in_copy(src, m):
        return pltpu.make_async_copy(src.at[m, :, :, channels(core)], inp.at[m, :, pl.ds(mine, strip), :], in_sem.at[m])

    for copy in w_copies() + wt_copies():
        copy.start()

    @pl.when(first)
    def _():
        for m in range(batches):
            in_copy(images, m).start()

    @pl.when(last)
    def _():
        for m in range(batches):
            in_copy(cotangent, m).start()

    barrier = pltpu.get_barrier_semaphore()
    for s in range(sections):
        @pl.when((sec >= s - 1) & (sec <= s + 1))
        def _():
            def greet(i, carry):
                @pl.when((s != sec) | (i != row))
                def _():
                    pl.semaphore_signal(barrier, inc=1, device_id=(jnp.int32(s), i), device_id_type=MESH)
                return carry
            lax.fori_loop(0, strips, greet, 0)

    acc_v[...] = jnp.zeros_like(acc_v)
    sums_v[...] = jnp.zeros_like(sums_v)

    for m in range(batches):
        for i in range(2):
            for at in (0, dz_all.shape[2] - cols):
                dz_all[m, i, pl.ds(at, cols), :] = jnp.zeros((cols, lanes), BF16)

    @pl.when(decoder)
    def _():
        wide = cols // 2
        windows_at = lax.broadcasted_iota(jnp.int32, (cols, wide), 1)
        places = lax.broadcasted_iota(jnp.int32, (cols, wide), 0)
        pick = (lax.shift_right_logical(places, 1) == windows_at).astype(F32)
        table = lax.dot_general(
            pick, switches[...].astype(F32), (((1,), (1,)), ((), ())), preferred_element_type=F32
        )
        odd = jnp.bitwise_and(lax.broadcasted_iota(jnp.int32, (cols, 128), 0), 1).astype(F32)
        windows = strip // cols // 2
        for m in range(batches):
            for i in range(2):
                for w in range(windows):
                    at = (m * 2 + i) * windows + w
                    value = jnp.broadcast_to(table[:, at : at + 1], (cols, 128))
                    for p in range(2):
                        hit = (jnp.abs(value - (2.0 * p + odd)) < 0.5).astype(F32).astype(BF16)
                        mask_own[m, i, pl.ds((2 * w + p) * cols, cols), :] = hit
        for m in range(batches):
            mask_v[m, :, pl.ds(mine, strip), :] = mask_own[m]

    @pl.when(jnp.logical_not(decoder))
    def _():
        mask_v[...] = jnp.ones_like(mask_v)

    near = 1 + jnp.where(sec > 0, 1, 0) + jnp.where(sec < sections - 1, 1, 0)
    pl.semaphore_wait(barrier, near * strips - 1)

    def remote(src, dst, send, recv, s, i):
        return pltpu.make_async_remote_copy(
            src_ref=src, dst_ref=dst, send_sem=send, recv_sem=recv, device_id=(s, i), device_id_type=MESH
        )

    def to_partner(src_at, dst_at, send, recv):
        return remote(src_at(1 - core), dst_at(pl.ds(mine, strip)), send, recv, sec, partner)

    def start_argument(src_at, dst_at, pair_sems, edge_sems):
        to_partner(src_at, dst_at, *pair_sems).start()

        @pl.when((core == 1) & has_down)
        def _():
            for i in range(2):
                remote(
                    src_at(i, pl.ds(strip - cols, cols)), dst_at(pl.ds(0, cols)),
                    edge_sems[0].at[i], edge_sems[1].at[0], sec, row + 1 + i,
                ).start()

        @pl.when((core == 0) & has_up)
        def _():
            for i in range(2):
                remote(
                    src_at(i, pl.ds(0, cols)), dst_at(pl.ds(cols + px, cols)),
                    edge_sems[0].at[i], edge_sems[1].at[1], sec, row - 2 + i,
                ).start()

    def argument_arrived(src_at, dst_at, pair_sems, edge_sems):
        to_partner(src_at, dst_at, *pair_sems).wait_recv()

        @pl.when(has_up)
        def _():
            remote(
                src_at(0, pl.ds(0, cols)), dst_at(pl.ds(0, cols)), edge_sems[0].at[0], edge_sems[1].at[0], sec, row
            ).wait_recv()

        @pl.when(has_down)
        def _():
            remote(
                src_at(0, pl.ds(0, cols)), dst_at(pl.ds(cols + px, cols)), edge_sems[0].at[0], edge_sems[1].at[1],
                sec, row,
            ).wait_recv()

    def argument_sent(src_at, dst_at, pair_sems, edge_sems):
        to_partner(src_at, dst_at, *pair_sems).wait_send()

        @pl.when(((core == 1) & has_down) | ((core == 0) & has_up))
        def _():
            for i in range(2):
                remote(
                    src_at(i, pl.ds(0, cols)), dst_at(pl.ds(0, cols)), edge_sems[0].at[i], edge_sems[1].at[0], sec, row
                ).wait_send()

    def input_parts(src, m):
        return (
            lambda i, r=pl.ds(0, strip): src.at[m, :, r, channels(i)],
            lambda r: inp.at[m, :, r, :],
            (pi_s.at[m], pi_r.at[m]),
            (ie_s.at[m], ie_r.at[m]),
        )

    mask_parts = (
        lambda i, r=pl.ds(0, strip): mask_own.at[:, :, r, :],
        lambda r: mask_v.at[:, :, r, :],
        (mp_s, mp_r),
        (me_s, me_r),
    )

    @pl.when(first)
    def _():
        for m in range(batches):
            start_argument(*input_parts(images, m))

    @pl.when(last)
    def _():
        for m in range(batches):
            start_argument(*input_parts(cotangent, m))

    @pl.when(decoder)
    def _():
        start_argument(*mask_parts)

    def affine_sends():
        return (
            remote(gains, gain_prev, gp_s.at[0], gp_r.at[0], sec + 1, row),
            remote(shifts, shift_prev, gp_s.at[1], gp_r.at[1], sec + 1, row),
        )

    @pl.when(sec < sections - 1)
    def _():
        for copy in affine_sends():
            copy.start()

    def block_sends(src, src_from, dst, send, recv, m, s):
        def body(i):
            return remote(
                src.at[m, i, pl.ds(src_from, px), :], dst.at[m, i, centre, :], send.at[m, i], recv.at[m, i], s, row
            )

        def edge(e, src_row, dst_row, i):
            return remote(
                src.at[m, :, pl.ds(src_from + src_row, cols), :], dst.at[m, :, pl.ds(dst_row, cols), :],
                send.at[m, 2 + e], recv.at[m, 2 + e], s, i,
            )

        return body, lambda: edge(0, px - cols, 0, row + 2), lambda: edge(1, 0, cols + px, row - 2)

    def each_edge(parts, act):
        _, to_down, to_up = parts

        @pl.when(has_down)
        def _():
            act(to_down())

        @pl.when(has_up)
        def _():
            act(to_up())

    def edges_arrived(parts):
        _, to_down, to_up = parts

        @pl.when(has_up)
        def _():
            to_down().wait_recv()

        @pl.when(has_down)
        def _():
            to_up().wait_recv()

    def send_block(parts):
        each_edge(parts, start)
        for i in range(2):
            parts[0](i).start()

    def block_sent(parts):
        each_edge(parts, sent)
        for i in range(2):
            parts[0](i).wait_send()

    def start(copy):
        copy.start()

    def sent(copy):
        copy.wait_send()

    def came(copy):
        copy.wait_recv()

    def z_sends(m, s):
        return block_sends(zown, cols, zin, fz_s, fz_r, m, s)

    def own_edges(m):
        return block_sends(zown, cols, zown, oe_s, oe_r, m, sec)

    def dy_sends(m, s):
        return block_sends(dyout, 0, dyin, bz_s, bz_r, m, s)

    def stats_each(src, dst, send, recv, m, s, same, act):
        def one(d, carry):
            q = chip + d
            q = jnp.where(q >= chips, q - chips, q)
            act(remote(src.at[m], dst.at[m, chip], send.at[m, d], recv.at[m, d], s, 2 * q + core))
            return carry
        lax.fori_loop(1 if same else 0, chips, one, 0)

    def start_stats(src, dst, send, recv, m, s, same):
        stats_each(src, dst, send, recv, m, s, same, start)
        if same:
            dst[m, chip] = src[m]

    def wait_stats(src, dst, send, recv, m, same):
        stats_each(src, dst, send, recv, m, sec, same, came)

    down_stats = (stat_out, zin_stat, fs_s, fs_r)
    same_stats = (stat_out, own_stat, os_s, os_r)
    back_stats = (sums_out, dy_stat, bs_s, bs_r)
    seed_stats = (seed_sums, dy_stat, ls_s, bs_r)

    def join(stats_ref, m):
        means, squares = stats_ref[m, :, 0, :], stats_ref[m, :, 1, :]
        mean = jnp.sum(means, 0, keepdims=True) / float(chips)
        off = means - mean
        var = (jnp.sum(squares, 0, keepdims=True) + local * jnp.sum(off * off, 0, keepdims=True)) / total
        at = (jnp.maximum(chip - 1, 0), chip, jnp.minimum(chip + 1, chips - 1))
        return lax.rsqrt(var + EPSILON), [stats_ref[m, i, pl.ds(0, 1), :] - mean for i in at]

    def kind(g):
        return 0 if g == 0 else 2 if g == groups - 1 else 1

    def inside(g, values):
        if kind(g) == 1:
            return values
        return jnp.where(has_up if kind(g) == 0 else has_down, values, jnp.zeros_like(values))

    def group(g):
        return pl.ds(g * cols, cols)

    column = lax.broadcasted_iota(jnp.int32, (1, cols, half), 1)

    def taps_joined(parts, left, right):
        def moved(values, by, edge):
            turned = pltpu.roll(values, by % (2 * px), 0).reshape(2 * px // cols, cols, half)
            return jnp.where(column == edge, 0.0, turned).reshape(2 * px, half)
        return parts[1] + moved(parts[left], 1, 0) + moved(parts[right], -1, cols - 1)

    def pass_on(operand, send, recv, m, i):
        return remote(operand.at[m, core, i], operand.at[m, core, i], send.at[m, i], recv.at[m, i], sec, partner)

    def products(operand, w, m, h, r_at):
        def one(c):
            acc = jnp.zeros((2 * px, half), F32)
            for r in range(3):
                left = operand[m, h, :, pl.ds(r_at(r) * cols, px), :].reshape(2 * px, half)
                acc += jnp.dot(left, w[h, 3 * r + c], preferred_element_type=F32)
            return acc
        return one

    def convolve(operand, w, send, recv, m, r_at, before_second=None):
        mine_first = products(operand, w, m, core, r_at)
        for c in range(3):
            product_v[c] = mine_first(c)
        for i in range(2):
            pass_on(operand, send, recv, m, i).wait_recv()
        if before_second is not None:
            before_second()
        then = products(operand, w, m, 1 - core, r_at)
        return [product_v[c] + then(c) for c in range(3)]

    def turned_copy(m, q):
        src = ut_own.at[m, pl.ds(pl.multiple_of((q // 2) * block, block), block), :]
        return src, ut_all.at[m, core, chip]


    def turned_each(m, act):
        def one(d, carry):
            q = chip + d
            q = jnp.where(q >= chips, q - chips, q)
            its_team = q // 2
            nearest = 2 * its_team + jnp.where(chip > q, 1, 0)

            @pl.when((its_team == team) | (q == nearest))
            def _():
                src, dst = turned_copy(m, q)
                act(remote(src, dst, ut_s.at[m, d], ut_r.at[m, d], sec, 2 * q + core))
            return carry
        lax.fori_loop(1, chips, one, 0)

    def entry_for(p):
        return (p // 2 != team) & (jnp.where(p > chip, 1, 0) == chip % 2)

    def turned_arrived(m):
        def one(d, carry):
            p = chip - d
            p = jnp.where(p < 0, p + chips, p)

            @pl.when(jnp.logical_not(entry_for(p)))
            def _():
                piece = ut_all.at[m, core, p]
                remote(piece, piece, ut_s.at[m, d], ut_r.at[m, d], sec, row).wait_recv()
            return carry
        lax.fori_loop(1, chips, one, 0)

    def turned_onward(m, act, arrive):
        other = chip + 1 - 2 * (chip % 2)

        def one(d, carry):
            p = chip - d
            p = jnp.where(p < 0, p + chips, p)

            @pl.when(entry_for(p))
            def _():
                piece = ut_all.at[m, core, p]
                if arrive:
                    remote(piece, piece, ut_s.at[m, d], ut_r.at[m, d], sec, row).wait_recv()
                there = other - p
                there = jnp.where(there < 0, there + chips, there)
                act(remote(piece, piece, uw_s.at[m, d], ut_r.at[m, there], sec, 2 * other + core))

            return carry
        lax.fori_loop(1, chips, one, 0)

    def turn_inputs(m):
        for h in range(2):
            ut_own[m, pl.ds(h * half, half), :] = ub[m, h, core, centre, :].T
        mine_at = pl.ds(pl.multiple_of(team * block, block), block)
        ut_all[m, core, chip] = ut_own[m, mine_at, :]

    def send_turned(m):
        turn_inputs(m)
        turned_each(m, start)

    def turned_relay(m):
        return remote(ut_all.at[m, core], ut_all.at[m, core], uf_s.at[m], uf_r.at[m], sec, partner)

    def relay_turned(m):
        turned_arrived(m)
        turned_relay(m).start()

    def relay_all():
        def one(m, carry):
            relay_turned(m)
            return carry
        lax.fori_loop(0, batches, one, 0)

    def dz_copy(m, i):
        src = dzb.at[m, (i % 4) // 2, core, centre, pl.ds(pl.multiple_of(i % 2 * lanes, lanes), lanes)]
        dst = dz_all.at[m, core, pl.ds(pl.multiple_of(cols + chip * px, cols), px), :]
        return src, dst

    def dz_each(m, act):
        def one(d, carry):
            i = row + d
            i = jnp.where(i >= strips, i - strips, i)
            src, dst = dz_copy(m, i)
            act(remote(src, dst, dz_s.at[m, d], dz_r.at[m, d], sec, i))
            return carry
        lax.fori_loop(1, strips, one, 0)

    def send_dz(m):
        dz_each(m, start)
        dz_all[m, core, pl.ds(pl.multiple_of(cols + chip * px, cols), px), :] = dzb[
            m, seat // 2, core, centre, pl.ds(pl.multiple_of(seat % 2 * lanes, lanes), lanes)
        ]

    def gather_taps(m):
        dz_each(m, came)
        relayed = ut_all.at[m, 1 - core]
        pltpu.make_async_copy(relayed, relayed, uf_r.at[m]).wait()
        rows = dz_all.shape[2]
        edge = lax.broadcasted_iota(jnp.int32, (1, cols, lanes), 1)
        for i in range(2):
            values = dz_all[m, i].astype(F32)
            for c, by, gone in ((0, rows - 1, cols - 1), (2, 1, 0)):
                turned = pltpu.roll(values, by, 0).reshape(rows // cols, cols, lanes)
                turned = jnp.where(edge == gone, 0.0, turned).reshape(rows, lanes)
                dz_taps[i, :, pl.ds(c * lanes, lanes)] = turned.astype(BF16)
            dz_taps[i, :, pl.ds(lanes, lanes)] = dz_all[m, i]

    def kernel_row(m, r):
        part = jnp.zeros((block, 3 * lanes), F32)
        for i in range(2):
            left = jnp.concatenate([ut_all[m, i, q] for q in range(chips)], axis=1)
            part += jnp.dot(
                left, dz_taps[i, pl.ds((2 - r) * cols, px * (strips // 2)), :], preferred_element_type=F32
            )
        return part

    def add_gradients(m):
        gather_taps(m)
        for r in range(3):
            acc_v[r] = acc_v[r] + kernel_row(m, r)

    def forward(m):
        @pl.when(first)
        def _():
            in_copy(images, m).wait()
            argument_arrived(*input_parts(images, m))
            for i in range(2):
                for g in range(groups):
                    ub[m, core, i, group(g), :] = inside(g, inp[m, i, group(g), :])
                pass_on(ub, ux_s, ux_r, m, i).start()

        @pl.when(sec > 0)
        def _():
            @pl.when(m == 0)
            def _():
                for copy in affine_sends():
                    copy.wait_recv()

                @pl.when(decoder)
                def _():
                    argument_arrived(*mask_parts)

            wait_stats(*down_stats, m, False)
            inv, offs = join(zin_stat, m)
            prev_coef[m, pl.ds(0, 1), :] = inv
            prev_coef[m, pl.ds(1, 1), :] = offs[1]
            slant = 0.5 * inv * gain_prev[:, channels(core)]
            level = [slant * off + 0.5 * shift_prev[:, channels(core)] for off in offs]
            sends = z_sends(m, sec)
            edges_arrived(sends)
            for i in range(2):
                sends[0](i).wait_recv()
                for g in range(groups):
                    gate = jnp.concatenate([mask_v[m, i, group(g), :].astype(F32)] * (half // 128), axis=1)
                    halved = zin[m, i, group(g), :].astype(F32) * slant + level[kind(g)]
                    turn = jnp.tanh(halved)
                    bent = halved * turn
                    ub[m, core, i, group(g), :] = inside(g, ((halved + bent) * gate).astype(BF16))
                    if kind(g) == 1:
                        slope_prev[m, i, pl.ds((g - 1) * cols, cols), :] = (0.5 + 0.5 * turn) * (1.0 + halved - bent)
                pass_on(ub, ux_s, ux_r, m, i).start()

        @pl.when(m == 0)
        def _():
            for copy in w_copies():
                copy.wait()

        conv = taps_joined(convolve(ub, w_v, ux_s, ux_r, m, lambda r: r), 0, 2)
        mean = jnp.sum(conv, 0, keepdims=True) / local
        conv = conv - mean
        stat_out[m, pl.ds(0, 1), :] = mean
        stat_out[m, pl.ds(1, 1), :] = jnp.sum(conv * conv, 0, keepdims=True)
        zown[m, :, centre, :] = conv.reshape(2, px, half).astype(BF16)

        @pl.when(sec < sections - 1)
        def _():
            start_stats(*down_stats, m, sec + 1, False)
            send_block(z_sends(m, sec + 1))

        start_stats(*same_stats, m, sec, True)
        each_edge(own_edges(m), start)

    def finish(m):
        wait_stats(*same_stats, m, True)
        inv, offs = join(own_stat, m)
        scale = inv * gains[:, channels(core)]
        own_coef[m, pl.ds(0, 1), :] = inv
        own_coef[m, pl.ds(1, 1), :] = scale
        for e in range(3):
            own_coef[m, pl.ds(2 + e, 1), :] = offs[e]
        slant = 0.5 * scale
        level = [slant * off + 0.5 * shifts[:, channels(core)] for off in offs]
        edges_arrived(own_edges(m))

        @pl.when(last)
        def _():
            in_copy(cotangent, m).wait()
            argument_arrived(*input_parts(cotangent, m))
            sums = jnp.zeros((cols, half), F32)
            cross = jnp.zeros((cols, half), F32)
            for i in range(2):
                for g in range(groups):
                    z = zown[m, i, group(g), :].astype(F32)
                    halved = z * slant + level[kind(g)]
                    turn = jnp.tanh(halved)
                    bent = halved * turn
                    dy = inp[m, i, group(g), :].astype(F32) * ((0.5 + 0.5 * turn) * (1.0 + halved - bent))
                    dyin[m, i, group(g), :] = dy.astype(BF16)
                    if kind(g) == 1:
                        out_v[m, i, pl.ds((g - 1) * cols, cols), :] = (halved + bent).astype(BF16)
                        sums += dy
                        cross += dy * z
            one = jnp.sum(sums, 0, keepdims=True)
            cross = jnp.sum(cross, 0, keepdims=True)
            seed_sums[m, pl.ds(0, 1), :] = one
            seed_sums[m, pl.ds(1, 1), :] = inv * (cross + offs[1] * one)
            start_stats(*seed_stats, m, sec, True)

        @pl.when(jnp.logical_not(last))
        def _():
            for i in range(2):
                for g in range(1, groups - 1):
                    halved = zown[m, i, group(g), :].astype(F32) * slant + level[1]
                    out_v[m, i, pl.ds((g - 1) * cols, cols), :] = (halved + halved * jnp.tanh(halved)).astype(BF16)

        for copy in result_copies(out_v, outs, out_sem, po_s, po_r, m):
            copy.start()

    def result_copies(src, dst, sem, send, recv, m):
        here, there = pl.multiple_of(strip * core, cols), pl.multiple_of(strip * (1 - core), cols)
        place = dst.at[m, :, :, channels(core)]
        return (
            pltpu.make_async_copy(src.at[m, :, pl.ds(here, strip), :], place, sem.at[m]),
            remote(src.at[m, :, pl.ds(there, strip), :], place, send.at[m], recv.at[m], sec, partner),
        )

    def backward(m):
        @pl.when(last)
        def _():
            wait_stats(*seed_stats, m, True)

        @pl.when(jnp.logical_not(last))
        def _():
            wait_stats(*back_stats, m, False)

        first_sum = jnp.sum(dy_stat[m, :, 0, :], 0, keepdims=True)
        cross_sum = jnp.sum(dy_stat[m, :, 1, :], 0, keepdims=True)
        sums_v[core, pl.ds(0, 1), :] = sums_v[core, pl.ds(0, 1), :] + first_sum
        sums_v[core, pl.ds(1, 1), :] = sums_v[core, pl.ds(1, 1), :] + cross_sum
        inv = own_coef[m, pl.ds(0, 1), :]
        scale = own_coef[m, pl.ds(1, 1), :]
        tilt = scale * inv * (cross_sum / total)
        base = [scale * (first_sum / total) + tilt * own_coef[m, pl.ds(2 + e, 1), :] for e in range(3)]
        sends = dy_sends(m, sec)

        @pl.when(jnp.logical_not(last))
        def _():
            edges_arrived(sends)

        for i in range(2):
            @pl.when(jnp.logical_not(last))
            def _():
                sends[0](i).wait_recv()

            for g in range(groups):
                dz = dyin[m, i, group(g), :].astype(F32) * scale
                dz = dz - zown[m, i, group(g), :].astype(F32) * tilt - base[kind(g)]
                dzb[m, core, i, group(g), :] = inside(g, dz.astype(BF16))
            pass_on(dzb, dx_s, dx_r, m, i).start()

        def early():
            @pl.when(first)
            def _():
                send_dz(m)

        gate = jnp.concatenate([mask_v[m, :, centre, :].astype(F32)] * (half // 128), axis=2)
        conv = taps_joined(convolve(dzb, wt_v, dx_s, dx_r, m, lambda r: 2 - r, early), 2, 0)
        du = (conv.reshape(2, px, half) * gate).astype(BF16)
        gin_v[m] = du

        @pl.when(sec > 0)
        def _():
            dy = du.astype(F32) * slope_prev[m]
            dyout[m] = dy.astype(BF16)
            one = jnp.sum(dy.reshape(2 * px, half), 0, keepdims=True)
            cross = jnp.sum((dy * zin[m, :, centre, :].astype(F32)).reshape(2 * px, half), 0, keepdims=True)
            sums_out[m, pl.ds(0, 1), :] = one
            sums_out[m, pl.ds(1, 1), :] = prev_coef[m, pl.ds(0, 1), :] * (cross + prev_coef[m, pl.ds(1, 1), :] * one)
            start_stats(*back_stats, m, sec - 1, False)
            send_block(dy_sends(m, sec - 1))

        for copy in result_copies(gin_v, grads_in, gin_sem, pg_s, pg_r, m):
            copy.start()

        @pl.when((sec > 0) & (sec < sections - 1))
        def _():
            send_dz(m)

    def turn_weights():
        for copy in wt_copies():
            copy.wait()

        def one(i, carry):
            for h in range(2):
                wt_v[h, i] = wt_v[h, i].T
            return carry
        lax.fori_loop(0, 9, one, 0)

    @pl.when(late)
    def _():
        turn_weights()

    def step(t, carry):
        ahead = t - sec
        behind = t - (2 * sections - 1 - sec)

        @pl.when((ahead >= 0) & (ahead < batches))
        def _():
            forward(ahead)

        @pl.when(late & (ahead >= 0) & (ahead < batches))
        def _():
            send_turned(ahead)

        @pl.when(jnp.logical_not(late) & (ahead == batches))
        def _():
            def turned(m, carry):
                send_turned(m)
                return carry
            lax.fori_loop(0, batches, turned, 0)
            turn_weights()

        @pl.when(jnp.logical_not(late) & (ahead == batches + 1))
        def _():
            def onward(m, carry):
                turned_onward(m, start, True)
                return carry
            lax.fori_loop(0, batches, onward, 0)

        @pl.when(first & (ahead == batches + 2))
        def _():
            relay_all()

        done = ahead - jnp.where(last, 0, 1)

        @pl.when((behind >= 0) & (behind < batches))
        def _():
            backward(behind)

        @pl.when((done >= 0) & (done < batches))
        def _():
            finish(done)

        @pl.when(late & (ahead >= 1) & (ahead <= batches))
        def _():
            turned_onward(ahead - 1, start, True)

        return carry

    lax.fori_loop(0, 2 * sections - 1 + batches, step, 0)

    remote(sums_v.at[core], sums_v.at[core], sv_s, sv_r, sec, partner).start()

    @pl.when(last)
    def _():
        def send(m, carry):
            send_dz(m)
            return carry

        lax.fori_loop(0, batches, send, 0)

    @pl.when(jnp.logical_not(first))
    def _():
        relay_all()

    def add(m, carry):
        add_gradients(m)
        return carry

    lax.fori_loop(0, batches - 1, add, 0)

    def swap(r, d):
        other = (seat + d) % 4
        return remote(
            swap_out.at[r, pl.ds(pl.multiple_of(other * share, share), share), :], swap_in.at[r, 4 - d - 1],
            sw_s.at[r, d - 1], sw_r.at[r, 4 - d - 1], sec, 4 * team + other,
        )

    gather_taps(batches - 1)
    for r in range(3):
        part = acc_v[r] + kernel_row(batches - 1, r)
        acc_v[r] = part
        swap_out[r] = part.astype(BF16)
        for d in range(1, 4):
            swap(r, d).start()

    def dw_copy(r):
        return pltpu.make_async_copy(dw_v.at[r], weight_grad.at[r], dw_sem.at[r])

    own_rows = pl.ds(pl.multiple_of(seat * share, share), share)
    for r in range(3):
        for c in range(3):
            dw_v[r, c, :, pl.ds(pl.multiple_of(seat * lanes, lanes), lanes)] = acc_v[r, own_rows, pl.ds(c * lanes, lanes)]
        for d in range(1, 4):
            swap(r, 4 - d).wait_recv()
            source = (seat + d) % 4
            for c in range(3):
                dw_v[r, c, :, pl.ds(pl.multiple_of(source * lanes, lanes), lanes)] = swap_in[
                    r, d - 1, :, pl.ds(c * lanes, lanes)
                ].astype(F32)
        dw_copy(r).start()

    for r in range(3):
        dw_copy(r).wait()
        for d in range(1, 4):
            swap(r, d).wait_send()

    @pl.when(decoder)
    def _():
        argument_sent(*mask_parts)

    @pl.when(sec < sections - 1)
    def _():
        for copy in affine_sends():
            copy.wait_send()

    def sums_copy():
        return remote(sums_v.at[core], sums_v.at[core], sv_s, sv_r, sec, partner)

    sums_copy().wait_recv()
    sums_copy().wait_send()
    for h in range(2):
        shift_sum[:, pl.ds(h * half, half)] = sums_v[h, pl.ds(0, 1), :]
        gain_sum[:, pl.ds(h * half, half)] = sums_v[h, pl.ds(1, 1), :]

    def drain(m, carry):
        for src, dst, sems in ((out_v, outs, (out_sem, po_s, po_r)), (gin_v, grads_in, (gin_sem, pg_s, pg_r))):
            here, there = result_copies(src, dst, *sems, m)
            here.wait()
            there.wait_send()
            remote(
                src.at[m, :, pl.ds(0, strip), :], dst.at[m, :, :, channels(1 - core)], sems[1].at[m], sems[2].at[m],
                sec, partner,
            ).wait_recv()

        turned_each(m, sent)
        turned_onward(m, sent, False)
        turned_relay(m).wait_send()
        dz_each(m, sent)
        for i in range(2):
            pass_on(ub, ux_s, ux_r, m, i).wait_send()
            pass_on(dzb, dx_s, dx_r, m, i).wait_send()

        @pl.when(first)
        def _():
            argument_sent(*input_parts(images, m))

        @pl.when(last)
        def _():
            argument_sent(*input_parts(cotangent, m))
            stats_each(*seed_stats, m, sec, True, sent)

        @pl.when(sec < sections - 1)
        def _():
            stats_each(*down_stats, m, sec + 1, False, sent)
            block_sent(z_sends(m, sec + 1))

        stats_each(*same_stats, m, sec, True, sent)
        each_edge(own_edges(m), sent)

        @pl.when(sec > 0)
        def _():
            stats_each(*back_stats, m, sec - 1, False, sent)
            block_sent(dy_sends(m, sec - 1))

        return carry

    lax.fori_loop(0, batches, drain, 0)


def settle(*refs):
    count = (len(refs) - 2) // 3
    sources, targets, stages = refs[:count], refs[count : 2 * count], refs[2 * count : 3 * count]
    moves = []
    for src, dst, stage in zip(sources, targets, stages):
        if len(src.shape) == 2:
            moves.append((src, dst, stage))
        else:
            moves += [(src.at[i], dst.at[i], stage.at[i]) for i in range(src.shape[0])]
    ins = [pltpu.make_async_copy(src, stage, refs[-2].at[i]) for i, (src, dst, stage) in enumerate(moves)]
    outs = [pltpu.make_async_copy(stage, dst, refs[-1].at[i]) for i, (src, dst, stage) in enumerate(moves)]
    for copy in ins:
        copy.start()
    for come, go in zip(ins, outs):
        come.wait()
        go.start()
    for copy in outs:
        copy.wait()


def body(images, switches, conv_weights, gains, shifts, cotangent):
    sections = lax.axis_size("section")
    strips = lax.axis_size("rows")
    batches, pictures, strip_rows, cols, ch = images.shape
    strip = strip_rows * cols
    px = 2 * strip
    tall = px + 2 * cols
    anywhere = pl.BlockSpec(memory_space=pl.ANY)
    vmem = pl.BlockSpec(memory_space=pltpu.VMEM)
    dma = pltpu.SemaphoreType.DMA
    flops = 3 * 2 * 9 * ch * ch * batches * px
    share = ch // strips
    chips = strips // 2
    outs, grads_in, weight_grad, gain_sum, shift_sum = pl.pallas_call(
        functools.partial(kernel, sections, strips, cols),
        out_shape=(
            jax.ShapeDtypeStruct((batches, pictures, strip, ch), BF16),
            jax.ShapeDtypeStruct((batches, pictures, strip, ch), BF16),
            jax.ShapeDtypeStruct((3, 3, share, ch), F32),
            jax.ShapeDtypeStruct((1, ch), F32),
            jax.ShapeDtypeStruct((1, ch), F32),
        ),
        in_specs=[anywhere, anywhere, anywhere, vmem, vmem, vmem],
        out_specs=(anywhere, anywhere, anywhere, vmem, vmem),
        scratch_shapes=[
            pltpu.VMEM((2, 9, ch // 2, ch // 2), BF16),
            pltpu.VMEM((2, 9, ch // 2, ch // 2), BF16),
            pltpu.VMEM((batches, 2, tall, ch // 2), BF16),
            pltpu.VMEM((batches, 2, strip, 128), BF16),
            pltpu.VMEM((batches, 2, tall, 128), BF16),
            pltpu.VMEM((1, ch), F32),
            pltpu.VMEM((1, ch), F32),
            pltpu.VMEM((batches, 2, tall, ch // 2), BF16),
            pltpu.VMEM((batches, chips, 2, ch // 2), F32),
            pltpu.VMEM((batches, 2, tall, ch // 2), BF16),
            pltpu.VMEM((batches, chips, 2, ch // 2), F32),
            pltpu.VMEM((batches, 2, 2, tall, ch // 2), BF16),
            pltpu.VMEM((batches, 2, px, ch // 2), F32),
            pltpu.VMEM((batches, 2, ch // 2), F32),
            pltpu.VMEM((batches, 8, ch // 2), F32),
            pltpu.VMEM((batches, 2, tall, ch // 2), BF16),
            pltpu.VMEM((batches, chips, 2, ch // 2), F32),
            pltpu.VMEM((batches, 2, 2, tall, ch // 2), BF16),
            pltpu.VMEM((batches, 2, px, ch // 2), BF16),
            pltpu.VMEM((3, 2 * px, ch // 2), F32),
            pltpu.VMEM((2, 2, ch // 2), F32),
            pltpu.VMEM((batches, 2, ch // 2), F32),
            pltpu.VMEM((batches, 2, ch // 2), F32),
            pltpu.VMEM((batches, 2, ch // 2), F32),
            pltpu.VMEM((batches, 2, px, ch // 2), BF16),
            pltpu.VMEM((batches, 2, px, ch // 2), BF16),
            pltpu.VMEM((batches, ch, px), BF16),
            pltpu.VMEM((batches, 2, strips // 2, 4 * share, px), BF16),
            pltpu.VMEM((batches, 2, px * strips // 2 + 2 * cols, ch // 4), BF16),
            pltpu.VMEM((2, px * strips // 2 + 2 * cols, 3 * ch // 4), BF16),
            pltpu.VMEM((3, 4 * share, 3 * ch // 4), F32),
            pltpu.VMEM((3, 4 * share, 3 * ch // 4), BF16),
            pltpu.VMEM((3, 3, share, 3 * ch // 4), BF16),
            pltpu.VMEM((3, 3, share, ch), F32),
            dma((2,)), dma((2,)),
            dma((batches,)),
            dma((batches,)), dma((batches,)),
            dma((batches, 2)), dma((batches, 2)),
            dma, dma,
            dma((2,)), dma((2,)),
            dma((2,)), dma((2,)),
            dma((batches, 2)), dma((batches, 2)),
            dma((batches, 2)), dma((batches, 2)),
            dma, dma,
            dma((batches, 4)), dma((batches, 4)),
            dma((batches, chips)), dma((batches, chips)),
            dma((batches, 4)), dma((batches, 4)),
            dma((batches, chips)), dma((batches, chips)),
            dma((batches, 4)), dma((batches, 4)),
            dma((batches, chips)), dma((batches, chips)),
            dma((batches, chips)),
            dma((batches,)), dma((batches,)), dma((batches,)),
            dma((batches,)), dma((batches,)), dma((batches,)),
            dma((batches, chips)), dma((batches, chips)), dma((batches, chips)),
            dma((batches,)), dma((batches,)),
            dma((batches, strips)), dma((batches, strips)),
            dma((3, 3)), dma((3, 3)),
            dma((3,)),
        ],
        compiler_params=pltpu.CompilerParams(
            collective_id=0, has_side_effects=True, vmem_limit_bytes=56 * 2**20
        ),
        cost_estimate=pl.CostEstimate(
            flops=flops, bytes_accessed=2 * 9 * ch * ch * 2, transcendentals=0
        ),
    )(
        images.reshape(batches, pictures, strip, ch),
        cotangent.reshape(batches, pictures, strip, ch),
        conv_weights.reshape(9, ch, ch),
        gains,
        shifts,
        switches.reshape(-1, switches.shape[-1]),
    )
    results = (outs, grads_in, weight_grad, gain_sum, shift_sum)
    outs, grads_in, weight_grad, gain_sum, shift_sum = pl.pallas_call(
        settle,
        out_shape=tuple(jax.ShapeDtypeStruct(r.shape, r.dtype) for r in results),
        in_specs=[anywhere] * 5,
        out_specs=(anywhere,) * 5,
        scratch_shapes=[pltpu.VMEM(r.shape, r.dtype) for r in results] + [dma((2 * batches + 5,))] * 2,
        compiler_params=pltpu.CompilerParams(vmem_limit_bytes=60 * 2**20),
    )(*results)
    shape = (1, batches, pictures, strip_rows, cols, ch)
    return (outs.reshape(shape), grads_in.reshape(shape), weight_grad[None], gain_sum, shift_sum)


def solution(mesh):
    return jax.shard_map(
        body,
        mesh=mesh,
        in_specs=(
            P(None, None, "rows", None, None),
            P(None, None, "rows", None),
            P("section", None, None, None, None),
            P("section", None),
            P("section", None),
            P(None, None, "rows", None, None),
        ),
        out_specs=(
            P("section", None, None, "rows", None, None),
            P("section", None, None, "rows", None, None),
            P("section", None, None, "rows", None),
            P("section", None),
            P("section", None),
        ),
        check_vma=False,
    )
```

```python
import functools

import jax
import jax.numpy as jnp
from jax import lax
from jax.experimental import pallas as pl
from jax.experimental.pallas import tpu as pltpu
from jax.sharding import PartitionSpec as P

EPSILON = 1e-05
MESH = pl.DeviceIdType.MESH
BF16 = jnp.bfloat16
F32 = jnp.float32


def kernel(
    sections, strips, cols,
    images, cotangent, weights, gains, shifts, switches,
    outs, grads_in, weight_grad, gain_sum, shift_sum,
    w_v, wt_v, inp, mask_own, mask_v, gain_prev, shift_prev, zin, zin_stat, zown, own_stat, ub, slope_prev,
    prev_coef, own_coef, dyin, dy_stat, dzb, dyout, product_v, sums_v, stat_out, sums_out, seed_sums, out_v, gin_v,
    ut_own, ut_all, dz_all, dz_taps, acc_v, swap_out, swap_in, dw_v,
    w_sem, wt_sem, in_sem, pi_s, pi_r, ie_s, ie_r, mp_s, mp_r, me_s, me_r, gp_s, gp_r,
    ux_s, ux_r, dx_s, dx_r, sv_s, sv_r,
    fz_s, fz_r, fs_s, fs_r, oe_s, oe_r, os_s, os_r, bz_s, bz_r, bs_s, bs_r, ls_s,
    out_sem, po_s, po_r, gin_sem, pg_s, pg_r,
    ut_s, ut_r, uw_s, uf_s, uf_r, dz_s, dz_r, sw_s, sw_r, dw_sem,
):
    sec = lax.axis_index("section")
    row = lax.axis_index("rows")
    batches, _, tall, half = inp.shape
    ch = 2 * half
    px = tall - 2 * cols
    strip = px // 2
    groups = tall // cols
    chips = strips // 2
    local = float(2 * px)
    total = local * chips
    first, last, decoder = sec == 0, sec == sections - 1, sec == sections // 2
    late = sec >= sections // 2
    core = row % 2
    partner = row + 1 - 2 * core
    has_up, has_down = row >= 2, row < strips - 2
    centre = pl.ds(cols, px)
    chip = row // 2
    team, seat = row // 4, row % 4
    lanes = dz_all.shape[3]
    block = ut_all.shape[3]
    share = block // 4
    mine = pl.multiple_of(cols + strip * core, cols)

    def channels(h):
        return pl.ds(pl.multiple_of(h * half, half), half)

    def w_copies():
        return [
            pltpu.make_async_copy(weights.at[:, channels(h), channels(core)], w_v.at[h], w_sem.at[h]) for h in range(2)
        ]

    def wt_copies():
        return [
            pltpu.make_async_copy(weights.at[:, channels(core), channels(h)], wt_v.at[h], wt_sem.at[h]) for h in range(2)
        ]

    def in_copy(src, m):
        return pltpu.make_async_copy(src.at[m, :, :, channels(core)], inp.at[m, :, pl.ds(mine, strip), :], in_sem.at[m])

    for copy in w_copies() + wt_copies():
        copy.start()

    @pl.when(first)
    def _():
        for m in range(batches):
            in_copy(images, m).start()

    @pl.when(last)
    def _():
        for m in range(batches):
            in_copy(cotangent, m).start()

    barrier = pltpu.get_barrier_semaphore()
    for s in range(sections):
        @pl.when((sec >= s - 1) & (sec <= s + 1))
        def _():
            def greet(i, carry):
                @pl.when((s != sec) | (i != row))
                def _():
                    pl.semaphore_signal(barrier, inc=1, device_id=(jnp.int32(s), i), device_id_type=MESH)
                return carry
            lax.fori_loop(0, strips, greet, 0)

    acc_v[...] = jnp.zeros_like(acc_v)
    sums_v[...] = jnp.zeros_like(sums_v)

    for m in range(batches):
        for i in range(2):
            for at in (0, dz_all.shape[2] - cols):
                dz_all[m, i, pl.ds(at, cols), :] = jnp.zeros((cols, lanes), BF16)

    @pl.when(decoder)
    def _():
        wide = cols // 2
        windows_at = lax.broadcasted_iota(jnp.int32, (cols, wide), 1)
        places = lax.broadcasted_iota(jnp.int32, (cols, wide), 0)
        pick = (lax.shift_right_logical(places, 1) == windows_at).astype(F32)
        table = lax.dot_general(
            pick, switches[...].astype(F32), (((1,), (1,)), ((), ())), preferred_element_type=F32
        )
        odd = jnp.bitwise_and(lax.broadcasted_iota(jnp.int32, (cols, 128), 0), 1).astype(F32)
        windows = strip // cols // 2
        for m in range(batches):
            for i in range(2):
                for w in range(windows):
                    at = (m * 2 + i) * windows + w
                    value = jnp.broadcast_to(table[:, at : at + 1], (cols, 128))
                    for p in range(2):
                        hit = (jnp.abs(value - (2.0 * p + odd)) < 0.5).astype(F32).astype(BF16)
                        mask_own[m, i, pl.ds((2 * w + p) * cols, cols), :] = hit
        for m in range(batches):
            mask_v[m, :, pl.ds(mine, strip), :] = mask_own[m]

    @pl.when(jnp.logical_not(decoder))
    def _():
        mask_v[...] = jnp.ones_like(mask_v)

    near = 1 + jnp.where(sec > 0, 1, 0) + jnp.where(sec < sections - 1, 1, 0)
    pl.semaphore_wait(barrier, near * strips - 1)

    def remote(src, dst, send, recv, s, i):
        return pltpu.make_async_remote_copy(
            src_ref=src, dst_ref=dst, send_sem=send, recv_sem=recv, device_id=(s, i), device_id_type=MESH
        )

    def to_partner(src_at, dst_at, send, recv):
        return remote(src_at(1 - core), dst_at(pl.ds(mine, strip)), send, recv, sec, partner)

    def start_argument(src_at, dst_at, pair_sems, edge_sems):
        to_partner(src_at, dst_at, *pair_sems).start()

        @pl.when((core == 1) & has_down)
        def _():
            for i in range(2):
                remote(
                    src_at(i, pl.ds(strip - cols, cols)), dst_at(pl.ds(0, cols)),
                    edge_sems[0].at[i], edge_sems[1].at[0], sec, row + 1 + i,
                ).start()

        @pl.when((core == 0) & has_up)
        def _():
            for i in range(2):
                remote(
                    src_at(i, pl.ds(0, cols)), dst_at(pl.ds(cols + px, cols)),
                    edge_sems[0].at[i], edge_sems[1].at[1], sec, row - 2 + i,
                ).start()

    def argument_arrived(src_at, dst_at, pair_sems, edge_sems):
        to_partner(src_at, dst_at, *pair_sems).wait_recv()

        @pl.when(has_up)
        def _():
            remote(
                src_at(0, pl.ds(0, cols)), dst_at(pl.ds(0, cols)), edge_sems[0].at[0], edge_sems[1].at[0], sec, row
            ).wait_recv()

        @pl.when(has_down)
        def _():
            remote(
                src_at(0, pl.ds(0, cols)), dst_at(pl.ds(cols + px, cols)), edge_sems[0].at[0], edge_sems[1].at[1],
                sec, row,
            ).wait_recv()

    def argument_sent(src_at, dst_at, pair_sems, edge_sems):
        to_partner(src_at, dst_at, *pair_sems).wait_send()

        @pl.when(((core == 1) & has_down) | ((core == 0) & has_up))
        def _():
            for i in range(2):
                remote(
                    src_at(i, pl.ds(0, cols)), dst_at(pl.ds(0, cols)), edge_sems[0].at[i], edge_sems[1].at[0], sec, row
                ).wait_send()

    def input_parts(src, m):
        return (
            lambda i, r=pl.ds(0, strip): src.at[m, :, r, channels(i)],
            lambda r: inp.at[m, :, r, :],
            (pi_s.at[m], pi_r.at[m]),
            (ie_s.at[m], ie_r.at[m]),
        )

    mask_parts = (
        lambda i, r=pl.ds(0, strip): mask_own.at[:, :, r, :],
        lambda r: mask_v.at[:, :, r, :],
        (mp_s, mp_r),
        (me_s, me_r),
    )

    @pl.when(first)
    def _():
        for m in range(batches):
            start_argument(*input_parts(images, m))

    @pl.when(last)
    def _():
        for m in range(batches):
            start_argument(*input_parts(cotangent, m))

    @pl.when(decoder)
    def _():
        start_argument(*mask_parts)

    def affine_sends():
        return (
            remote(gains, gain_prev, gp_s.at[0], gp_r.at[0], sec + 1, row),
            remote(shifts, shift_prev, gp_s.at[1], gp_r.at[1], sec + 1, row),
        )

    @pl.when(sec < sections - 1)
    def _():
        for copy in affine_sends():
            copy.start()

    def block_sends(src, src_from, dst, send, recv, m, s):
        def body(i):
            return remote(
                src.at[m, i, pl.ds(src_from, px), :], dst.at[m, i, centre, :], send.at[m, i], recv.at[m, i], s, row
            )

        def edge(e, src_row, dst_row, i):
            return remote(
                src.at[m, :, pl.ds(src_from + src_row, cols), :], dst.at[m, :, pl.ds(dst_row, cols), :],
                send.at[m, 2 + e], recv.at[m, 2 + e], s, i,
            )

        return body, lambda: edge(0, px - cols, 0, row + 2), lambda: edge(1, 0, cols + px, row - 2)

    def each_edge(parts, act):
        _, to_down, to_up = parts

        @pl.when(has_down)
        def _():
            act(to_down())

        @pl.when(has_up)
        def _():
            act(to_up())

    def edges_arrived(parts):
        _, to_down, to_up = parts

        @pl.when(has_up)
        def _():
            to_down().wait_recv()

        @pl.when(has_down)
        def _():
            to_up().wait_recv()

    def send_block(parts):
        each_edge(parts, start)
        for i in range(2):
            parts[0](i).start()

    def block_sent(parts):
        each_edge(parts, sent)
        for i in range(2):
            parts[0](i).wait_send()

    def start(copy):
        copy.start()

    def sent(copy):
        copy.wait_send()

    def came(copy):
        copy.wait_recv()

    def z_sends(m, s):
        return block_sends(zown, cols, zin, fz_s, fz_r, m, s)

    def own_edges(m):
        return block_sends(zown, cols, zown, oe_s, oe_r, m, sec)

    def dy_sends(m, s):
        return block_sends(dyout, 0, dyin, bz_s, bz_r, m, s)

    def stats_each(src, dst, send, recv, m, s, same, act):
        def one(d, carry):
            q = chip + d
            q = jnp.where(q >= chips, q - chips, q)
            act(remote(src.at[m], dst.at[m, chip], send.at[m, d], recv.at[m, d], s, 2 * q + core))
            return carry
        lax.fori_loop(1 if same else 0, chips, one, 0)

    def start_stats(src, dst, send, recv, m, s, same):
        stats_each(src, dst, send, recv, m, s, same, start)
        if same:
            dst[m, chip] = src[m]

    def wait_stats(src, dst, send, recv, m, same):
        stats_each(src, dst, send, recv, m, sec, same, came)

    down_stats = (stat_out, zin_stat, fs_s, fs_r)
    same_stats = (stat_out, own_stat, os_s, os_r)
    back_stats = (sums_out, dy_stat, bs_s, bs_r)
    seed_stats = (seed_sums, dy_stat, ls_s, bs_r)

    def join(stats_ref, m):
        means, squares = stats_ref[m, :, 0, :], stats_ref[m, :, 1, :]
        mean = jnp.sum(means, 0, keepdims=True) / float(chips)
        off = means - mean
        var = (jnp.sum(squares, 0, keepdims=True) + local * jnp.sum(off * off, 0, keepdims=True)) / total
        at = (jnp.maximum(chip - 1, 0), chip, jnp.minimum(chip + 1, chips - 1))
        return lax.rsqrt(var + EPSILON), [stats_ref[m, i, pl.ds(0, 1), :] - mean for i in at]

    def kind(g):
        return 0 if g == 0 else 2 if g == groups - 1 else 1

    def inside(g, values):
        if kind(g) == 1:
            return values
        return jnp.where(has_up if kind(g) == 0 else has_down, values, jnp.zeros_like(values))

    def group(g):
        return pl.ds(g * cols, cols)

    column = lax.broadcasted_iota(jnp.int32, (1, cols, half), 1)

    def taps_joined(parts, left, right):
        def moved(values, by, edge):
            turned = pltpu.roll(values, by % (2 * px), 0).reshape(2 * px // cols, cols, half)
            return jnp.where(column == edge, 0.0, turned).reshape(2 * px, half)
        return parts[1] + moved(parts[left], 1, 0) + moved(parts[right], -1, cols - 1)

    def pass_on(operand, send, recv, m, i):
        return remote(operand.at[m, core, i], operand.at[m, core, i], send.at[m, i], recv.at[m, i], sec, partner)

    def products(operand, w, m, h, r_at):
        def one(c):
            acc = jnp.zeros((2 * px, half), F32)
            for r in range(3):
                left = operand[m, h, :, pl.ds(r_at(r) * cols, px), :].reshape(2 * px, half)
                acc += jnp.dot(left, w[h, 3 * r + c], preferred_element_type=F32)
            return acc
        return one

    def convolve(operand, w, send, recv, m, r_at, before_second=None):
        mine_first = products(operand, w, m, core, r_at)
        for c in range(3):
            product_v[c] = mine_first(c)
        for i in range(2):
            pass_on(operand, send, recv, m, i).wait_recv()
        if before_second is not None:
            before_second()
        then = products(operand, w, m, 1 - core, r_at)
        return [product_v[c] + then(c) for c in range(3)]

    def turned_copy(m, q):
        src = ut_own.at[m, pl.ds(pl.multiple_of((q // 2) * block, block), block), :]
        return src, ut_all.at[m, core, chip]


    def turned_each(m, act):
        def one(d, carry):
            q = chip + d
            q = jnp.where(q >= chips, q - chips, q)
            its_team = q // 2
            nearest = 2 * its_team + jnp.where(chip > q, 1, 0)

            @pl.when((its_team == team) | (q == nearest))
            def _():
                src, dst = turned_copy(m, q)
                act(remote(src, dst, ut_s.at[m, d], ut_r.at[m, d], sec, 2 * q + core))
            return carry
        lax.fori_loop(1, chips, one, 0)

    def entry_for(p):
        return (p // 2 != team) & (jnp.where(p > chip, 1, 0) == chip % 2)

    def turned_arrived(m):
        def one(d, carry):
            p = chip - d
            p = jnp.where(p < 0, p + chips, p)

            @pl.when(jnp.logical_not(entry_for(p)))
            def _():
                piece = ut_all.at[m, core, p]
                remote(piece, piece, ut_s.at[m, d], ut_r.at[m, d], sec, row).wait_recv()
            return carry
        lax.fori_loop(1, chips, one, 0)

    def turned_onward(m, act, arrive):
        other = chip + 1 - 2 * (chip % 2)

        def one(d, carry):
            p = chip - d
            p = jnp.where(p < 0, p + chips, p)

            @pl.when(entry_for(p))
            def _():
                piece = ut_all.at[m, core, p]
                if arrive:
                    remote(piece, piece, ut_s.at[m, d], ut_r.at[m, d], sec, row).wait_recv()
                there = other - p
                there = jnp.where(there < 0, there + chips, there)
                act(remote(piece, piece, uw_s.at[m, d], ut_r.at[m, there], sec, 2 * other + core))

            return carry
        lax.fori_loop(1, chips, one, 0)

    def turn_inputs(m):
        for h in range(2):
            ut_own[m, pl.ds(h * half, half), :] = ub[m, h, core, centre, :].T
        mine_at = pl.ds(pl.multiple_of(team * block, block), block)
        ut_all[m, core, chip] = ut_own[m, mine_at, :]

    def send_turned(m):
        turn_inputs(m)
        turned_each(m, start)

    def turned_relay(m):
        return remote(ut_all.at[m, core], ut_all.at[m, core], uf_s.at[m], uf_r.at[m], sec, partner)

    def relay_turned(m):
        turned_arrived(m)
        turned_relay(m).start()

    def pass_on_all():
        def one(m, carry):
            turned_onward(m, start, True)
            return carry
        lax.fori_loop(0, batches, one, 0)

    def relay_all():
        def one(m, carry):
            relay_turned(m)
            return carry
        lax.fori_loop(0, batches, one, 0)

    def dz_copy(m, i):
        src = dzb.at[m, (i % 4) // 2, core, centre, pl.ds(pl.multiple_of(i % 2 * lanes, lanes), lanes)]
        dst = dz_all.at[m, core, pl.ds(pl.multiple_of(cols + chip * px, cols), px), :]
        return src, dst

    def dz_each(m, act):
        def one(d, carry):
            i = row + d
            i = jnp.where(i >= strips, i - strips, i)
            src, dst = dz_copy(m, i)
            act(remote(src, dst, dz_s.at[m, d], dz_r.at[m, d], sec, i))
            return carry
        lax.fori_loop(1, strips, one, 0)

    def send_dz(m):
        dz_each(m, start)
        dz_all[m, core, pl.ds(pl.multiple_of(cols + chip * px, cols), px), :] = dzb[
            m, seat // 2, core, centre, pl.ds(pl.multiple_of(seat % 2 * lanes, lanes), lanes)
        ]

    def gather_taps(m):
        dz_each(m, came)
        relayed = ut_all.at[m, 1 - core]
        pltpu.make_async_copy(relayed, relayed, uf_r.at[m]).wait()
        rows = dz_all.shape[2]
        edge = lax.broadcasted_iota(jnp.int32, (1, cols, lanes), 1)
        for i in range(2):
            values = dz_all[m, i].astype(F32)
            for c, by, gone in ((0, rows - 1, cols - 1), (2, 1, 0)):
                turned = pltpu.roll(values, by, 0).reshape(rows // cols, cols, lanes)
                turned = jnp.where(edge == gone, 0.0, turned).reshape(rows, lanes)
                dz_taps[i, :, pl.ds(c * lanes, lanes)] = turned.astype(BF16)
            dz_taps[i, :, pl.ds(lanes, lanes)] = dz_all[m, i]

    def kernel_row(m, r):
        part = jnp.zeros((block, 3 * lanes), F32)
        for i in range(2):
            left = jnp.concatenate([ut_all[m, i, q] for q in range(chips)], axis=1)
            part += jnp.dot(
                left, dz_taps[i, pl.ds((2 - r) * cols, px * (strips // 2)), :], preferred_element_type=F32
            )
        return part

    def add_gradients(m):
        gather_taps(m)
        for r in range(3):
            acc_v[r] = acc_v[r] + kernel_row(m, r)

    def forward(m):
        @pl.when(first)
        def _():
            in_copy(images, m).wait()
            argument_arrived(*input_parts(images, m))
            for i in range(2):
                for g in range(groups):
                    ub[m, core, i, group(g), :] = inside(g, inp[m, i, group(g), :])
                pass_on(ub, ux_s, ux_r, m, i).start()

        @pl.when(sec > 0)
        def _():
            @pl.when(m == 0)
            def _():
                for copy in affine_sends():
                    copy.wait_recv()

                @pl.when(decoder)
                def _():
                    argument_arrived(*mask_parts)

            wait_stats(*down_stats, m, False)
            inv, offs = join(zin_stat, m)
            prev_coef[m, pl.ds(0, 1), :] = inv
            prev_coef[m, pl.ds(1, 1), :] = offs[1]
            slant = 0.5 * inv * gain_prev[:, channels(core)]
            level = [slant * off + 0.5 * shift_prev[:, channels(core)] for off in offs]
            sends = z_sends(m, sec)
            edges_arrived(sends)
            for i in range(2):
                sends[0](i).wait_recv()
                for g in range(groups):
                    gate = jnp.concatenate([mask_v[m, i, group(g), :].astype(F32)] * (half // 128), axis=1)
                    halved = zin[m, i, group(g), :].astype(F32) * slant + level[kind(g)]
                    turn = jnp.tanh(halved)
                    bent = halved * turn
                    ub[m, core, i, group(g), :] = inside(g, ((halved + bent) * gate).astype(BF16))
                    if kind(g) == 1:
                        slope_prev[m, i, pl.ds((g - 1) * cols, cols), :] = (0.5 + 0.5 * turn) * (1.0 + halved - bent)
                pass_on(ub, ux_s, ux_r, m, i).start()

        @pl.when(m == 0)
        def _():
            for copy in w_copies():
                copy.wait()

        conv = taps_joined(convolve(ub, w_v, ux_s, ux_r, m, lambda r: r), 0, 2)
        mean = jnp.sum(conv, 0, keepdims=True) / local
        conv = conv - mean
        stat_out[m, pl.ds(0, 1), :] = mean
        stat_out[m, pl.ds(1, 1), :] = jnp.sum(conv * conv, 0, keepdims=True)
        zown[m, :, centre, :] = conv.reshape(2, px, half).astype(BF16)

        @pl.when(sec < sections - 1)
        def _():
            start_stats(*down_stats, m, sec + 1, False)
            send_block(z_sends(m, sec + 1))

        start_stats(*same_stats, m, sec, True)
        each_edge(own_edges(m), start)

    def finish(m):
        wait_stats(*same_stats, m, True)
        inv, offs = join(own_stat, m)
        scale = inv * gains[:, channels(core)]
        own_coef[m, pl.ds(0, 1), :] = inv
        own_coef[m, pl.ds(1, 1), :] = scale
        for e in range(3):
            own_coef[m, pl.ds(2 + e, 1), :] = offs[e]
        slant = 0.5 * scale
        level = [slant * off + 0.5 * shifts[:, channels(core)] for off in offs]
        edges_arrived(own_edges(m))

        @pl.when(last)
        def _():
            in_copy(cotangent, m).wait()
            argument_arrived(*input_parts(cotangent, m))
            sums = jnp.zeros((cols, half), F32)
            cross = jnp.zeros((cols, half), F32)
            for i in range(2):
                for g in range(groups):
                    z = zown[m, i, group(g), :].astype(F32)
                    halved = z * slant + level[kind(g)]
                    turn = jnp.tanh(halved)
                    bent = halved * turn
                    dy = inp[m, i, group(g), :].astype(F32) * ((0.5 + 0.5 * turn) * (1.0 + halved - bent))
                    dyin[m, i, group(g), :] = dy.astype(BF16)
                    if kind(g) == 1:
                        out_v[m, i, pl.ds((g - 1) * cols, cols), :] = (halved + bent).astype(BF16)
                        sums += dy
                        cross += dy * z
            one = jnp.sum(sums, 0, keepdims=True)
            cross = jnp.sum(cross, 0, keepdims=True)
            seed_sums[m, pl.ds(0, 1), :] = one
            seed_sums[m, pl.ds(1, 1), :] = inv * (cross + offs[1] * one)
            start_stats(*seed_stats, m, sec, True)

        @pl.when(jnp.logical_not(last))
        def _():
            for i in range(2):
                for g in range(1, groups - 1):
                    halved = zown[m, i, group(g), :].astype(F32) * slant + level[1]
                    out_v[m, i, pl.ds((g - 1) * cols, cols), :] = (halved + halved * jnp.tanh(halved)).astype(BF16)

        for copy in result_copies(out_v, outs, out_sem, po_s, po_r, m):
            copy.start()

    def result_copies(src, dst, sem, send, recv, m):
        here, there = pl.multiple_of(strip * core, cols), pl.multiple_of(strip * (1 - core), cols)
        place = dst.at[m, :, :, channels(core)]
        return (
            pltpu.make_async_copy(src.at[m, :, pl.ds(here, strip), :], place, sem.at[m]),
            remote(src.at[m, :, pl.ds(there, strip), :], place, send.at[m], recv.at[m], sec, partner),
        )

    def backward(m):
        @pl.when(last)
        def _():
            wait_stats(*seed_stats, m, True)

        @pl.when(jnp.logical_not(last))
        def _():
            wait_stats(*back_stats, m, False)

        first_sum = jnp.sum(dy_stat[m, :, 0, :], 0, keepdims=True)
        cross_sum = jnp.sum(dy_stat[m, :, 1, :], 0, keepdims=True)
        sums_v[core, pl.ds(0, 1), :] = sums_v[core, pl.ds(0, 1), :] + first_sum
        sums_v[core, pl.ds(1, 1), :] = sums_v[core, pl.ds(1, 1), :] + cross_sum
        inv = own_coef[m, pl.ds(0, 1), :]
        scale = own_coef[m, pl.ds(1, 1), :]
        tilt = scale * inv * (cross_sum / total)
        base = [scale * (first_sum / total) + tilt * own_coef[m, pl.ds(2 + e, 1), :] for e in range(3)]
        sends = dy_sends(m, sec)

        @pl.when(jnp.logical_not(last))
        def _():
            edges_arrived(sends)

        for i in range(2):
            @pl.when(jnp.logical_not(last))
            def _():
                sends[0](i).wait_recv()

            for g in range(groups):
                dz = dyin[m, i, group(g), :].astype(F32) * scale
                dz = dz - zown[m, i, group(g), :].astype(F32) * tilt - base[kind(g)]
                dzb[m, core, i, group(g), :] = inside(g, dz.astype(BF16))
            pass_on(dzb, dx_s, dx_r, m, i).start()

        def early():
            @pl.when(first)
            def _():
                send_dz(m)

        gate = jnp.concatenate([mask_v[m, :, centre, :].astype(F32)] * (half // 128), axis=2)
        conv = taps_joined(convolve(dzb, wt_v, dx_s, dx_r, m, lambda r: 2 - r, early), 2, 0)
        du = (conv.reshape(2, px, half) * gate).astype(BF16)
        gin_v[m] = du

        @pl.when(sec > 0)
        def _():
            dy = du.astype(F32) * slope_prev[m]
            dyout[m] = dy.astype(BF16)
            one = jnp.sum(dy.reshape(2 * px, half), 0, keepdims=True)
            cross = jnp.sum((dy * zin[m, :, centre, :].astype(F32)).reshape(2 * px, half), 0, keepdims=True)
            sums_out[m, pl.ds(0, 1), :] = one
            sums_out[m, pl.ds(1, 1), :] = prev_coef[m, pl.ds(0, 1), :] * (cross + prev_coef[m, pl.ds(1, 1), :] * one)
            start_stats(*back_stats, m, sec - 1, False)
            send_block(dy_sends(m, sec - 1))

        for copy in result_copies(gin_v, grads_in, gin_sem, pg_s, pg_r, m):
            copy.start()

        @pl.when((sec > 0) & (sec < sections - 1))
        def _():
            send_dz(m)

    def turn_weights():
        for copy in wt_copies():
            copy.wait()

        def one(i, carry):
            for h in range(2):
                wt_v[h, i] = wt_v[h, i].T
            return carry
        lax.fori_loop(0, 9, one, 0)

    @pl.when(late)
    def _():
        turn_weights()

    def step(t, carry):
        ahead = t - sec
        behind = t - (2 * sections - 1 - sec)

        @pl.when((ahead >= 0) & (ahead < batches))
        def _():
            forward(ahead)

        @pl.when(late & (ahead >= 0) & (ahead < batches))
        def _():
            send_turned(ahead)

        @pl.when(jnp.logical_not(late) & (ahead == batches))
        def _():
            def turned(m, carry):
                send_turned(m)
                return carry
            lax.fori_loop(0, batches, turned, 0)
            turn_weights()

        @pl.when(jnp.logical_not(late) & (ahead == batches + 1))
        def _():
            pass_on_all()

        @pl.when(first & (ahead == batches + 2))
        def _():
            relay_all()

        done = ahead - jnp.where(last, 0, 1)

        @pl.when((behind >= 0) & (behind < batches))
        def _():
            backward(behind)

        @pl.when((done >= 0) & (done < batches))
        def _():
            finish(done)

        return carry

    lax.fori_loop(0, 2 * sections - 1 + batches, step, 0)

    remote(sums_v.at[core], sums_v.at[core], sv_s, sv_r, sec, partner).start()

    @pl.when(last)
    def _():
        def send(m, carry):
            send_dz(m)
            return carry

        lax.fori_loop(0, batches, send, 0)

    @pl.when(late)
    def _():
        pass_on_all()

    @pl.when(jnp.logical_not(first))
    def _():
        relay_all()

    def add(m, carry):
        add_gradients(m)
        return carry

    lax.fori_loop(0, batches - 1, add, 0)

    def swap(r, d):
        other = (seat + d) % 4
        return remote(
            swap_out.at[r, pl.ds(pl.multiple_of(other * share, share), share), :], swap_in.at[r, 4 - d - 1],
            sw_s.at[r, d - 1], sw_r.at[r, 4 - d - 1], sec, 4 * team + other,
        )

    gather_taps(batches - 1)
    for r in range(3):
        part = acc_v[r] + kernel_row(batches - 1, r)
        acc_v[r] = part
        swap_out[r] = part.astype(BF16)
        for d in range(1, 4):
            swap(r, d).start()

    def dw_copy(r):
        return pltpu.make_async_copy(dw_v.at[r], weight_grad.at[r], dw_sem.at[r])

    own_rows = pl.ds(pl.multiple_of(seat * share, share), share)
    for r in range(3):
        for c in range(3):
            dw_v[r, c, :, pl.ds(pl.multiple_of(seat * lanes, lanes), lanes)] = acc_v[r, own_rows, pl.ds(c * lanes, lanes)]
        for d in range(1, 4):
            swap(r, 4 - d).wait_recv()
            source = (seat + d) % 4
            for c in range(3):
                dw_v[r, c, :, pl.ds(pl.multiple_of(source * lanes, lanes), lanes)] = swap_in[
                    r, d - 1, :, pl.ds(c * lanes, lanes)
                ].astype(F32)
        dw_copy(r).start()

    for r in range(3):
        dw_copy(r).wait()
        for d in range(1, 4):
            swap(r, d).wait_send()

    @pl.when(decoder)
    def _():
        argument_sent(*mask_parts)

    @pl.when(sec < sections - 1)
    def _():
        for copy in affine_sends():
            copy.wait_send()

    def sums_copy():
        return remote(sums_v.at[core], sums_v.at[core], sv_s, sv_r, sec, partner)

    sums_copy().wait_recv()
    sums_copy().wait_send()
    for h in range(2):
        shift_sum[:, pl.ds(h * half, half)] = sums_v[h, pl.ds(0, 1), :]
        gain_sum[:, pl.ds(h * half, half)] = sums_v[h, pl.ds(1, 1), :]

    def drain(m, carry):
        for src, dst, sems in ((out_v, outs, (out_sem, po_s, po_r)), (gin_v, grads_in, (gin_sem, pg_s, pg_r))):
            here, there = result_copies(src, dst, *sems, m)
            here.wait()
            there.wait_send()
            remote(
                src.at[m, :, pl.ds(0, strip), :], dst.at[m, :, :, channels(1 - core)], sems[1].at[m], sems[2].at[m],
                sec, partner,
            ).wait_recv()

        turned_each(m, sent)
        turned_onward(m, sent, False)
        turned_relay(m).wait_send()
        dz_each(m, sent)
        for i in range(2):
            pass_on(ub, ux_s, ux_r, m, i).wait_send()
            pass_on(dzb, dx_s, dx_r, m, i).wait_send()

        @pl.when(first)
        def _():
            argument_sent(*input_parts(images, m))

        @pl.when(last)
        def _():
            argument_sent(*input_parts(cotangent, m))
            stats_each(*seed_stats, m, sec, True, sent)

        @pl.when(sec < sections - 1)
        def _():
            stats_each(*down_stats, m, sec + 1, False, sent)
            block_sent(z_sends(m, sec + 1))

        stats_each(*same_stats, m, sec, True, sent)
        each_edge(own_edges(m), sent)

        @pl.when(sec > 0)
        def _():
            stats_each(*back_stats, m, sec - 1, False, sent)
            block_sent(dy_sends(m, sec - 1))

        return carry

    lax.fori_loop(0, batches, drain, 0)


def settle(*refs):
    count = (len(refs) - 2) // 3
    sources, targets, stages = refs[:count], refs[count : 2 * count], refs[2 * count : 3 * count]
    moves = []
    for src, dst, stage in zip(sources, targets, stages):
        if len(src.shape) == 2:
            moves.append((src, dst, stage))
        else:
            moves += [(src.at[i], dst.at[i], stage.at[i]) for i in range(src.shape[0])]
    ins = [pltpu.make_async_copy(src, stage, refs[-2].at[i]) for i, (src, dst, stage) in enumerate(moves)]
    outs = [pltpu.make_async_copy(stage, dst, refs[-1].at[i]) for i, (src, dst, stage) in enumerate(moves)]
    for copy in ins:
        copy.start()
    for come, go in zip(ins, outs):
        come.wait()
        go.start()
    for copy in outs:
        copy.wait()


def body(images, switches, conv_weights, gains, shifts, cotangent):
    sections = lax.axis_size("section")
    strips = lax.axis_size("rows")
    batches, pictures, strip_rows, cols, ch = images.shape
    strip = strip_rows * cols
    px = 2 * strip
    tall = px + 2 * cols
    anywhere = pl.BlockSpec(memory_space=pl.ANY)
    vmem = pl.BlockSpec(memory_space=pltpu.VMEM)
    dma = pltpu.SemaphoreType.DMA
    flops = 3 * 2 * 9 * ch * ch * batches * px
    share = ch // strips
    chips = strips // 2
    outs, grads_in, weight_grad, gain_sum, shift_sum = pl.pallas_call(
        functools.partial(kernel, sections, strips, cols),
        out_shape=(
            jax.ShapeDtypeStruct((batches, pictures, strip, ch), BF16),
            jax.ShapeDtypeStruct((batches, pictures, strip, ch), BF16),
            jax.ShapeDtypeStruct((3, 3, share, ch), F32),
            jax.ShapeDtypeStruct((1, ch), F32),
            jax.ShapeDtypeStruct((1, ch), F32),
        ),
        in_specs=[anywhere, anywhere, anywhere, vmem, vmem, vmem],
        out_specs=(anywhere, anywhere, anywhere, vmem, vmem),
        scratch_shapes=[
            pltpu.VMEM((2, 9, ch // 2, ch // 2), BF16),
            pltpu.VMEM((2, 9, ch // 2, ch // 2), BF16),
            pltpu.VMEM((batches, 2, tall, ch // 2), BF16),
            pltpu.VMEM((batches, 2, strip, 128), BF16),
            pltpu.VMEM((batches, 2, tall, 128), BF16),
            pltpu.VMEM((1, ch), F32),
            pltpu.VMEM((1, ch), F32),
            pltpu.VMEM((batches, 2, tall, ch // 2), BF16),
            pltpu.VMEM((batches, chips, 2, ch // 2), F32),
            pltpu.VMEM((batches, 2, tall, ch // 2), BF16),
            pltpu.VMEM((batches, chips, 2, ch // 2), F32),
            pltpu.VMEM((batches, 2, 2, tall, ch // 2), BF16),
            pltpu.VMEM((batches, 2, px, ch // 2), F32),
            pltpu.VMEM((batches, 2, ch // 2), F32),
            pltpu.VMEM((batches, 8, ch // 2), F32),
            pltpu.VMEM((batches, 2, tall, ch // 2), BF16),
            pltpu.VMEM((batches, chips, 2, ch // 2), F32),
            pltpu.VMEM((batches, 2, 2, tall, ch // 2), BF16),
            pltpu.VMEM((batches, 2, px, ch // 2), BF16),
            pltpu.VMEM((3, 2 * px, ch // 2), F32),
            pltpu.VMEM((2, 2, ch // 2), F32),
            pltpu.VMEM((batches, 2, ch // 2), F32),
            pltpu.VMEM((batches, 2, ch // 2), F32),
            pltpu.VMEM((batches, 2, ch // 2), F32),
            pltpu.VMEM((batches, 2, px, ch // 2), BF16),
            pltpu.VMEM((batches, 2, px, ch // 2), BF16),
            pltpu.VMEM((batches, ch, px), BF16),
            pltpu.VMEM((batches, 2, strips // 2, 4 * share, px), BF16),
            pltpu.VMEM((batches, 2, px * strips // 2 + 2 * cols, ch // 4), BF16),
            pltpu.VMEM((2, px * strips // 2 + 2 * cols, 3 * ch // 4), BF16),
            pltpu.VMEM((3, 4 * share, 3 * ch // 4), F32),
            pltpu.VMEM((3, 4 * share, 3 * ch // 4), BF16),
            pltpu.VMEM((3, 3, share, 3 * ch // 4), BF16),
            pltpu.VMEM((3, 3, share, ch), F32),
            dma((2,)), dma((2,)),
            dma((batches,)),
            dma((batches,)), dma((batches,)),
            dma((batches, 2)), dma((batches, 2)),
            dma, dma,
            dma((2,)), dma((2,)),
            dma((2,)), dma((2,)),
            dma((batches, 2)), dma((batches, 2)),
            dma((batches, 2)), dma((batches, 2)),
            dma, dma,
            dma((batches, 4)), dma((batches, 4)),
            dma((batches, chips)), dma((batches, chips)),
            dma((batches, 4)), dma((batches, 4)),
            dma((batches, chips)), dma((batches, chips)),
            dma((batches, 4)), dma((batches, 4)),
            dma((batches, chips)), dma((batches, chips)),
            dma((batches, chips)),
            dma((batches,)), dma((batches,)), dma((batches,)),
            dma((batches,)), dma((batches,)), dma((batches,)),
            dma((batches, chips)), dma((batches, chips)), dma((batches, chips)),
            dma((batches,)), dma((batches,)),
            dma((batches, strips)), dma((batches, strips)),
            dma((3, 3)), dma((3, 3)),
            dma((3,)),
        ],
        compiler_params=pltpu.CompilerParams(
            collective_id=0, has_side_effects=True, vmem_limit_bytes=56 * 2**20
        ),
        cost_estimate=pl.CostEstimate(
            flops=flops, bytes_accessed=2 * 9 * ch * ch * 2, transcendentals=0
        ),
    )(
        images.reshape(batches, pictures, strip, ch),
        cotangent.reshape(batches, pictures, strip, ch),
        conv_weights.reshape(9, ch, ch),
        gains,
        shifts,
        switches.reshape(-1, switches.shape[-1]),
    )
    results = (outs, grads_in, weight_grad, gain_sum, shift_sum)
    outs, grads_in, weight_grad, gain_sum, shift_sum = pl.pallas_call(
        settle,
        out_shape=tuple(jax.ShapeDtypeStruct(r.shape, r.dtype) for r in results),
        in_specs=[anywhere] * 5,
        out_specs=(anywhere,) * 5,
        scratch_shapes=[pltpu.VMEM(r.shape, r.dtype) for r in results] + [dma((2 * batches + 5,))] * 2,
        compiler_params=pltpu.CompilerParams(vmem_limit_bytes=60 * 2**20),
    )(*results)
    shape = (1, batches, pictures, strip_rows, cols, ch)
    return (outs.reshape(shape), grads_in.reshape(shape), weight_grad[None], gain_sum, shift_sum)


def solution(mesh):
    return jax.shard_map(
        body,
        mesh=mesh,
        in_specs=(
            P(None, None, "rows", None, None),
            P(None, None, "rows", None),
            P("section", None, None, None, None),
            P("section", None),
            P("section", None),
            P(None, None, "rows", None, None),
        ),
        out_specs=(
            P("section", None, None, "rows", None, None),
            P("section", None, None, "rows", None, None),
            P("section", None, None, "rows", None),
            P("section", None),
            P("section", None),
        ),
        check_vma=False,
    )
```

```python
import functools

import jax
import jax.numpy as jnp
from jax import lax
from jax.experimental import pallas as pl
from jax.experimental.pallas import tpu as pltpu
from jax.sharding import PartitionSpec as P

EPSILON = 1e-05
MESH = pl.DeviceIdType.MESH
BF16 = jnp.bfloat16
F32 = jnp.float32


def kernel(
    sections, strips, cols,
    images, cotangent, weights, gains, shifts, switches,
    outs, grads_in, weight_grad, gain_sum, shift_sum,
    w_v, wt_v, inp, mask_own, mask_v, gain_prev, shift_prev, zin, zin_stat, zown, own_stat, ub, slope_prev,
    prev_coef, own_coef, dyin, dy_stat, dzb, dyout, product_v, sums_v, stat_out, sums_out, seed_sums, out_v, gin_v,
    ut_own, ut_all, dz_all, dz_taps, acc_v, swap_out, swap_in, dw_v,
    w_sem, wt_sem, in_sem, pi_s, pi_r, ie_s, ie_r, mp_s, mp_r, me_s, me_r, gp_s, gp_r,
    ux_s, ux_r, dx_s, dx_r, sv_s, sv_r,
    fz_s, fz_r, fs_s, fs_r, oe_s, oe_r, os_s, os_r, bz_s, bz_r, bs_s, bs_r, ls_s,
    out_sem, po_s, po_r, gin_sem, pg_s, pg_r,
    ut_s, ut_r, uw_s, uf_s, uf_r, dz_s, dz_r, sw_s, sw_r, dw_sem,
):
    sec = lax.axis_index("section")
    row = lax.axis_index("rows")
    batches, _, tall, half = inp.shape
    ch = 2 * half
    px = tall - 2 * cols
    strip = px // 2
    groups = tall // cols
    chips = strips // 2
    local = float(px)
    total = 2.0 * local * chips
    first, last, decoder = sec == 0, sec == sections - 1, sec == sections // 2
    late = sec >= sections // 2
    core = row % 2
    partner = row + 1 - 2 * core
    has_up, has_down = row >= 2, row < strips - 2
    centre = pl.ds(cols, px)
    chip = row // 2
    team, seat = row // 4, row % 4
    lanes = dz_all.shape[3]
    block = ut_all.shape[3]
    share = block // 4
    mine = pl.multiple_of(cols + strip * core, cols)

    def channels(h):
        return pl.ds(pl.multiple_of(h * half, half), half)

    def w_copies():
        return [
            pltpu.make_async_copy(weights.at[:, channels(h), channels(core)], w_v.at[h], w_sem.at[h]) for h in range(2)
        ]

    def wt_copies():
        return [
            pltpu.make_async_copy(weights.at[:, channels(core), channels(h)], wt_v.at[h], wt_sem.at[h]) for h in range(2)
        ]

    def in_copy(src, m):
        return pltpu.make_async_copy(src.at[m, :, :, channels(core)], inp.at[m, :, pl.ds(mine, strip), :], in_sem.at[m])

    for copy in w_copies() + wt_copies():
        copy.start()

    @pl.when(first)
    def _():
        for m in range(batches):
            in_copy(images, m).start()

    @pl.when(last)
    def _():
        for m in range(batches):
            in_copy(cotangent, m).start()

    barrier = pltpu.get_barrier_semaphore()
    for s in range(sections):
        @pl.when((sec >= s - 1) & (sec <= s + 1))
        def _():
            def greet(i, carry):
                @pl.when((s != sec) | (i != row))
                def _():
                    pl.semaphore_signal(barrier, inc=1, device_id=(jnp.int32(s), i), device_id_type=MESH)
                return carry
            lax.fori_loop(0, strips, greet, 0)

    acc_v[...] = jnp.zeros_like(acc_v)
    sums_v[...] = jnp.zeros_like(sums_v)

    for m in range(batches):
        for i in range(2):
            for at in (0, dz_all.shape[2] - cols):
                dz_all[m, i, pl.ds(at, cols), :] = jnp.zeros((cols, lanes), BF16)

    @pl.when(decoder)
    def _():
        wide = cols // 2
        windows_at = lax.broadcasted_iota(jnp.int32, (cols, wide), 1)
        places = lax.broadcasted_iota(jnp.int32, (cols, wide), 0)
        pick = (lax.shift_right_logical(places, 1) == windows_at).astype(F32)
        table = lax.dot_general(
            pick, switches[...].astype(F32), (((1,), (1,)), ((), ())), preferred_element_type=F32
        )
        odd = jnp.bitwise_and(lax.broadcasted_iota(jnp.int32, (cols, 128), 0), 1).astype(F32)
        windows = strip // cols // 2
        for m in range(batches):
            for i in range(2):
                for w in range(windows):
                    at = (m * 2 + i) * windows + w
                    value = jnp.broadcast_to(table[:, at : at + 1], (cols, 128))
                    for p in range(2):
                        hit = (jnp.abs(value - (2.0 * p + odd)) < 0.5).astype(F32).astype(BF16)
                        mask_own[m, i, pl.ds((2 * w + p) * cols, cols), :] = hit
        for m in range(batches):
            mask_v[m, :, pl.ds(mine, strip), :] = mask_own[m]

    @pl.when(jnp.logical_not(decoder))
    def _():
        mask_v[...] = jnp.ones_like(mask_v)

    near = 1 + jnp.where(sec > 0, 1, 0) + jnp.where(sec < sections - 1, 1, 0)
    pl.semaphore_wait(barrier, near * strips - 1)

    def remote(src, dst, send, recv, s, i):
        return pltpu.make_async_remote_copy(
            src_ref=src, dst_ref=dst, send_sem=send, recv_sem=recv, device_id=(s, i), device_id_type=MESH
        )

    def to_partner(src_at, dst_at, send, recv):
        return remote(src_at(1 - core), dst_at(pl.ds(mine, strip)), send, recv, sec, partner)

    def start_argument(src_at, dst_at, pair_sems, edge_sems):
        to_partner(src_at, dst_at, *pair_sems).start()

        @pl.when((core == 1) & has_down)
        def _():
            for i in range(2):
                remote(
                    src_at(i, pl.ds(strip - cols, cols)), dst_at(pl.ds(0, cols)),
                    edge_sems[0].at[i], edge_sems[1].at[0], sec, row + 1 + i,
                ).start()

        @pl.when((core == 0) & has_up)
        def _():
            for i in range(2):
                remote(
                    src_at(i, pl.ds(0, cols)), dst_at(pl.ds(cols + px, cols)),
                    edge_sems[0].at[i], edge_sems[1].at[1], sec, row - 2 + i,
                ).start()

    def argument_arrived(src_at, dst_at, pair_sems, edge_sems):
        to_partner(src_at, dst_at, *pair_sems).wait_recv()

        @pl.when(has_up)
        def _():
            remote(
                src_at(0, pl.ds(0, cols)), dst_at(pl.ds(0, cols)), edge_sems[0].at[0], edge_sems[1].at[0], sec, row
            ).wait_recv()

        @pl.when(has_down)
        def _():
            remote(
                src_at(0, pl.ds(0, cols)), dst_at(pl.ds(cols + px, cols)), edge_sems[0].at[0], edge_sems[1].at[1],
                sec, row,
            ).wait_recv()

    def argument_sent(src_at, dst_at, pair_sems, edge_sems):
        to_partner(src_at, dst_at, *pair_sems).wait_send()

        @pl.when(((core == 1) & has_down) | ((core == 0) & has_up))
        def _():
            for i in range(2):
                remote(
                    src_at(i, pl.ds(0, cols)), dst_at(pl.ds(0, cols)), edge_sems[0].at[i], edge_sems[1].at[0], sec, row
                ).wait_send()

    def input_parts(src, m):
        return (
            lambda i, r=pl.ds(0, strip): src.at[m, :, r, channels(i)],
            lambda r: inp.at[m, :, r, :],
            (pi_s.at[m], pi_r.at[m]),
            (ie_s.at[m], ie_r.at[m]),
        )

    mask_parts = (
        lambda i, r=pl.ds(0, strip): mask_own.at[:, :, r, :],
        lambda r: mask_v.at[:, :, r, :],
        (mp_s, mp_r),
        (me_s, me_r),
    )

    @pl.when(first)
    def _():
        for m in range(batches):
            start_argument(*input_parts(images, m))

    @pl.when(last)
    def _():
        for m in range(batches):
            start_argument(*input_parts(cotangent, m))

    @pl.when(decoder)
    def _():
        start_argument(*mask_parts)

    def affine_sends():
        return (
            remote(gains, gain_prev, gp_s.at[0], gp_r.at[0], sec + 1, row),
            remote(shifts, shift_prev, gp_s.at[1], gp_r.at[1], sec + 1, row),
        )

    @pl.when(sec < sections - 1)
    def _():
        for copy in affine_sends():
            copy.start()

    def block_sends(src, src_from, dst, send, recv, m, s):
        def piece(k, src_row, dst_row, rows, to):
            def one(i):
                return remote(
                    src.at[m, i, pl.ds(src_from + src_row, rows), :], dst.at[m, i, pl.ds(dst_row, rows), :],
                    send.at[m, k, i], recv.at[m, k, i], s, to,
                )
            return one

        return (
            piece(0, 0, cols, px, row), piece(1, px - cols, 0, cols, row + 2), piece(2, 0, cols + px, cols, row - 2)
        )

    def each_edge(parts, i, act):
        _, to_down, to_up = parts

        @pl.when(has_down)
        def _():
            act(to_down(i))

        @pl.when(has_up)
        def _():
            act(to_up(i))

    def edges_arrived(parts, i):
        _, to_down, to_up = parts

        @pl.when(has_up)
        def _():
            to_down(i).wait_recv()

        @pl.when(has_down)
        def _():
            to_up(i).wait_recv()

    def send_block(parts, i):
        each_edge(parts, i, start)
        parts[0](i).start()

    def block_sent(parts):
        for i in range(2):
            each_edge(parts, i, sent)
            parts[0](i).wait_send()

    def start(copy):
        copy.start()

    def sent(copy):
        copy.wait_send()

    def came(copy):
        copy.wait_recv()

    def z_sends(m, s):
        return block_sends(zown, cols, zin, fz_s, fz_r, m, s)

    def own_edges(m):
        return block_sends(zown, cols, zown, oe_s, oe_r, m, sec)

    def dy_sends(m, s):
        return block_sends(dyout, 0, dyin, bz_s, bz_r, m, s)

    def stats_each(src, dst, send, recv, m, s, same, act):
        def one(d, carry):
            q = chip + d
            q = jnp.where(q >= chips, q - chips, q)
            act(remote(src.at[m], dst.at[m, chip], send.at[m, d], recv.at[m, d], s, 2 * q + core))
            return carry
        lax.fori_loop(1 if same else 0, chips, one, 0)

    def start_stats(src, dst, send, recv, m, s, same):
        stats_each(src, dst, send, recv, m, s, same, start)
        if same:
            dst[m, chip] = src[m]

    def wait_stats(src, dst, send, recv, m, same):
        stats_each(src, dst, send, recv, m, sec, same, came)

    down_stats = (stat_out, zin_stat, fs_s, fs_r)
    same_stats = (stat_out, own_stat, os_s, os_r)
    back_stats = (sums_out, dy_stat, bs_s, bs_r)
    seed_stats = (seed_sums, dy_stat, ls_s, bs_r)

    def join(stats_ref, m):
        means = stats_ref[m, :, 0, :], stats_ref[m, :, 1, :]
        mean = jnp.sum(means[0] + means[1], 0, keepdims=True) / (2.0 * chips)
        off = [part - mean for part in means]
        squares = jnp.sum(stats_ref[m, :, 2, :] + stats_ref[m, :, 3, :], 0, keepdims=True)
        apart = jnp.sum(off[0] * off[0] + off[1] * off[1], 0, keepdims=True)
        at = (jnp.maximum(chip - 1, 0), chip, jnp.minimum(chip + 1, chips - 1))
        offs = [[stats_ref[m, q, pl.ds(i, 1), :] - mean for q in at] for i in range(2)]
        return lax.rsqrt((squares + local * apart) / total + EPSILON), offs

    def kind(g):
        return 0 if g == 0 else 2 if g == groups - 1 else 1

    def inside(g, values):
        if kind(g) == 1:
            return values
        return jnp.where(has_up if kind(g) == 0 else has_down, values, jnp.zeros_like(values))

    def group(g):
        return pl.ds(g * cols, cols)

    column = lax.broadcasted_iota(jnp.int32, (1, cols, half), 1)

    def taps_joined(parts, left, right):
        rows = parts[0].shape[0]

        def moved(values, by, edge):
            turned = pltpu.roll(values, by % rows, 0).reshape(rows // cols, cols, half)
            return jnp.where(column == edge, 0.0, turned).reshape(rows, half)
        return parts[1] + moved(parts[left], 1, 0) + moved(parts[right], -1, cols - 1)

    def pass_on(operand, send, recv, m, i):
        return remote(operand.at[m, core, i], operand.at[m, core, i], send.at[m, i], recv.at[m, i], sec, partner)

    def products(operand, w, m, h, r_at, images_at):
        rows = images_at.size * px

        def one(c):
            acc = jnp.zeros((rows, half), F32)
            for r in range(3):
                left = operand[m, h, images_at, pl.ds(r_at(r) * cols, px), :].reshape(rows, half)
                acc += jnp.dot(left, w[h, 3 * r + c], preferred_element_type=F32)
            return acc
        return one

    def convolve(operand, w, send, recv, m, r_at, left, right, prepare, use, between=None):
        def part(images_at, wait_for):
            rows = pl.ds(0, images_at.size * px)
            mine_first = products(operand, w, m, core, r_at, images_at)
            for c in range(3):
                product_v[c, rows, :] = mine_first(c)
            for i in wait_for:
                pass_on(operand, send, recv, m, i).wait_recv()
            if between is not None:
                between()
            then = products(operand, w, m, 1 - core, r_at, images_at)
            return taps_joined([product_v[c, rows, :] + then(c) for c in range(3)], left, right)

        def ready(i):
            prepare(i)
            pass_on(operand, send, recv, m, i).start()

        def together():
            for i in range(2):
                ready(i)
            whole = part(pl.ds(0, 2), range(2))
            for i in range(2):
                use(i, whole[i * px : (i + 1) * px])

        def apart():
            for i in range(2):
                ready(i)
                use(i, part(pl.ds(i, 1), [i]))

        return together, apart

    def turned_copy(m, q):
        src = ut_own.at[m, pl.ds(pl.multiple_of((q // 2) * block, block), block), :]
        return src, ut_all.at[m, core, chip]


    def turned_each(m, act):
        def one(d, carry):
            q = chip + d
            q = jnp.where(q >= chips, q - chips, q)
            its_team = q // 2
            nearest = 2 * its_team + jnp.where(chip > q, 1, 0)

            @pl.when((its_team == team) | (q == nearest))
            def _():
                src, dst = turned_copy(m, q)
                act(remote(src, dst, ut_s.at[m, d], ut_r.at[m, d], sec, 2 * q + core))
            return carry
        lax.fori_loop(1, chips, one, 0)

    def entry_for(p):
        return (p // 2 != team) & (jnp.where(p > chip, 1, 0) == chip % 2)

    def turned_arrived(m):
        def one(d, carry):
            p = chip - d
            p = jnp.where(p < 0, p + chips, p)

            @pl.when(jnp.logical_not(entry_for(p)))
            def _():
                piece = ut_all.at[m, core, p]
                remote(piece, piece, ut_s.at[m, d], ut_r.at[m, d], sec, row).wait_recv()
            return carry
        lax.fori_loop(1, chips, one, 0)

    def turned_onward(m, act, arrive):
        other = chip + 1 - 2 * (chip % 2)

        def one(d, carry):
            p = chip - d
            p = jnp.where(p < 0, p + chips, p)

            @pl.when(entry_for(p))
            def _():
                piece = ut_all.at[m, core, p]
                if arrive:
                    remote(piece, piece, ut_s.at[m, d], ut_r.at[m, d], sec, row).wait_recv()
                there = other - p
                there = jnp.where(there < 0, there + chips, there)
                act(remote(piece, piece, uw_s.at[m, d], ut_r.at[m, there], sec, 2 * other + core))

            return carry
        lax.fori_loop(1, chips, one, 0)

    def turn_inputs(m):
        for h in range(2):
            ut_own[m, pl.ds(h * half, half), :] = ub[m, h, core, centre, :].T
        mine_at = pl.ds(pl.multiple_of(team * block, block), block)
        ut_all[m, core, chip] = ut_own[m, mine_at, :]

    def send_turned(m):
        turn_inputs(m)
        turned_each(m, start)

    def turned_relay(m):
        return remote(ut_all.at[m, core], ut_all.at[m, core], uf_s.at[m], uf_r.at[m], sec, partner)

    def relay_turned(m):
        turned_arrived(m)
        turned_relay(m).start()

    def relay_all():
        def one(m, carry):
            relay_turned(m)
            return carry
        lax.fori_loop(0, batches, one, 0)

    def dz_copy(m, i):
        src = dzb.at[m, (i % 4) // 2, core, centre, pl.ds(pl.multiple_of(i % 2 * lanes, lanes), lanes)]
        dst = dz_all.at[m, core, pl.ds(pl.multiple_of(cols + chip * px, cols), px), :]
        return src, dst

    def dz_each(m, act):
        def one(d, carry):
            i = row + d
            i = jnp.where(i >= strips, i - strips, i)
            src, dst = dz_copy(m, i)
            act(remote(src, dst, dz_s.at[m, d], dz_r.at[m, d], sec, i))
            return carry
        lax.fori_loop(1, strips, one, 0)

    def send_dz(m):
        dz_each(m, start)
        dz_all[m, core, pl.ds(pl.multiple_of(cols + chip * px, cols), px), :] = dzb[
            m, seat // 2, core, centre, pl.ds(pl.multiple_of(seat % 2 * lanes, lanes), lanes)
        ]

    def gather_taps(m):
        dz_each(m, came)
        relayed = ut_all.at[m, 1 - core]
        pltpu.make_async_copy(relayed, relayed, uf_r.at[m]).wait()
        rows = dz_all.shape[2]
        edge = lax.broadcasted_iota(jnp.int32, (1, cols, lanes), 1)
        for i in range(2):
            values = dz_all[m, i].astype(F32)
            for c, by, gone in ((0, rows - 1, cols - 1), (2, 1, 0)):
                turned = pltpu.roll(values, by, 0).reshape(rows // cols, cols, lanes)
                turned = jnp.where(edge == gone, 0.0, turned).reshape(rows, lanes)
                dz_taps[i, :, pl.ds(c * lanes, lanes)] = turned.astype(BF16)
            dz_taps[i, :, pl.ds(lanes, lanes)] = dz_all[m, i]

    def kernel_row(m, r):
        part = jnp.zeros((block, 3 * lanes), F32)
        for i in range(2):
            left = jnp.concatenate([ut_all[m, i, q] for q in range(chips)], axis=1)
            part += jnp.dot(
                left, dz_taps[i, pl.ds((2 - r) * cols, px * (strips // 2)), :], preferred_element_type=F32
            )
        return part

    def add_gradients(m):
        gather_taps(m)
        for r in range(3):
            acc_v[r] = acc_v[r] + kernel_row(m, r)

    def forward(m):
        def prepare_first(i):
            for g in range(groups):
                ub[m, core, i, group(g), :] = inside(g, inp[m, i, group(g), :])

        def prepare_later(i):
            sends = z_sends(m, sec)
            inv = prev_coef[m, pl.ds(0, 1), :]
            slant = 0.5 * inv * gain_prev[:, channels(core)]
            shift = 0.5 * shift_prev[:, channels(core)]
            level = [slant * prev_coef[m, pl.ds(1 + 3 * i + e, 1), :] + shift for e in range(3)]
            edges_arrived(sends, i)
            sends[0](i).wait_recv()
            for g in range(groups):
                gate = jnp.concatenate([mask_v[m, i, group(g), :].astype(F32)] * (half // 128), axis=1)
                halved = zin[m, i, group(g), :].astype(F32) * slant + level[kind(g)]
                turn = jnp.tanh(halved)
                bent = halved * turn
                ub[m, core, i, group(g), :] = inside(g, ((halved + bent) * gate).astype(BF16))
                if kind(g) == 1:
                    slope_prev[m, i, pl.ds((g - 1) * cols, cols), :] = (0.5 + 0.5 * turn) * (1.0 + halved - bent)

        def prepare(i):
            @pl.when(first)
            def _():
                prepare_first(i)

            @pl.when(sec > 0)
            def _():
                prepare_later(i)

        def use(i, conv):
            mean = jnp.sum(conv, 0, keepdims=True) / local
            conv = conv - mean
            stat_out[m, pl.ds(i, 1), :] = mean
            stat_out[m, pl.ds(2 + i, 1), :] = jnp.sum(conv * conv, 0, keepdims=True)
            zown[m, i, centre, :] = conv.astype(BF16)

            @pl.when(sec < sections - 1)
            def _():
                if i == 1:
                    start_stats(*down_stats, m, sec + 1, False)
                send_block(z_sends(m, sec + 1), i)

        @pl.when(first)
        def _():
            in_copy(images, m).wait()
            argument_arrived(*input_parts(images, m))

        @pl.when(sec > 0)
        def _():
            @pl.when(m == 0)
            def _():
                for copy in affine_sends():
                    copy.wait_recv()

                @pl.when(decoder)
                def _():
                    argument_arrived(*mask_parts)

            wait_stats(*down_stats, m, False)
            inv, offs = join(zin_stat, m)
            for e, value in enumerate((inv, *offs[0], *offs[1])):
                prev_coef[m, pl.ds(e, 1), :] = value

        @pl.when(m == 0)
        def _():
            for copy in w_copies():
                copy.wait()

        together, apart = convolve(ub, w_v, ux_s, ux_r, m, lambda r: r, 0, 2, prepare, use)

        @pl.when(last)
        def _():
            together()

        @pl.when(jnp.logical_not(last))
        def _():
            apart()

        start_stats(*same_stats, m, sec, True)
        for i in range(2):
            each_edge(own_edges(m), i, start)

    def finish(m):
        wait_stats(*same_stats, m, True)
        inv, offs = join(own_stat, m)
        scale = inv * gains[:, channels(core)]
        for e, value in enumerate((inv, scale, *offs[0], *offs[1])):
            own_coef[m, pl.ds(e, 1), :] = value
        slant = 0.5 * scale
        shift = 0.5 * shifts[:, channels(core)]
        level = [[slant * off + shift for off in part] for part in offs]
        for i in range(2):
            edges_arrived(own_edges(m), i)

        @pl.when(last)
        def _():
            in_copy(cotangent, m).wait()
            argument_arrived(*input_parts(cotangent, m))
            ones, crosses = [], []
            for i in range(2):
                sums = jnp.zeros((cols, half), F32)
                cross = jnp.zeros((cols, half), F32)
                for g in range(groups):
                    z = zown[m, i, group(g), :].astype(F32)
                    halved = z * slant + level[i][kind(g)]
                    turn = jnp.tanh(halved)
                    bent = halved * turn
                    dy = inp[m, i, group(g), :].astype(F32) * ((0.5 + 0.5 * turn) * (1.0 + halved - bent))
                    dyin[m, i, group(g), :] = dy.astype(BF16)
                    if kind(g) == 1:
                        out_v[m, i, pl.ds((g - 1) * cols, cols), :] = (halved + bent).astype(BF16)
                        sums += dy
                        cross += dy * z
                one = jnp.sum(sums, 0, keepdims=True)
                ones.append(one)
                crosses.append(jnp.sum(cross, 0, keepdims=True) + offs[i][1] * one)
            seed_sums[m, pl.ds(0, 1), :] = ones[0] + ones[1]
            seed_sums[m, pl.ds(1, 1), :] = inv * (crosses[0] + crosses[1])
            start_stats(*seed_stats, m, sec, True)

        @pl.when(jnp.logical_not(last))
        def _():
            for i in range(2):
                for g in range(1, groups - 1):
                    halved = zown[m, i, group(g), :].astype(F32) * slant + level[i][1]
                    out_v[m, i, pl.ds((g - 1) * cols, cols), :] = (halved + halved * jnp.tanh(halved)).astype(BF16)

        for copy in result_copies(out_v, outs, out_sem, po_s, po_r, m):
            copy.start()

    def result_copies(src, dst, sem, send, recv, m):
        here, there = pl.multiple_of(strip * core, cols), pl.multiple_of(strip * (1 - core), cols)
        place = dst.at[m, :, :, channels(core)]
        return (
            pltpu.make_async_copy(src.at[m, :, pl.ds(here, strip), :], place, sem.at[m]),
            remote(src.at[m, :, pl.ds(there, strip), :], place, send.at[m], recv.at[m], sec, partner),
        )

    def backward(m):
        @pl.when(last)
        def _():
            wait_stats(*seed_stats, m, True)

        @pl.when(jnp.logical_not(last))
        def _():
            wait_stats(*back_stats, m, False)

        first_sum = jnp.sum(dy_stat[m, :, 0, :], 0, keepdims=True)
        cross_sum = jnp.sum(dy_stat[m, :, 1, :], 0, keepdims=True)
        sums_v[core, pl.ds(0, 1), :] = sums_v[core, pl.ds(0, 1), :] + first_sum
        sums_v[core, pl.ds(1, 1), :] = sums_v[core, pl.ds(1, 1), :] + cross_sum

        def prepare(i):
            inv = own_coef[m, pl.ds(0, 1), :]
            scale = own_coef[m, pl.ds(1, 1), :]
            tilt = scale * inv * (cross_sum / total)
            base = [scale * (first_sum / total) + tilt * own_coef[m, pl.ds(2 + 3 * i + e, 1), :] for e in range(3)]
            sends = dy_sends(m, sec)

            @pl.when(jnp.logical_not(last))
            def _():
                edges_arrived(sends, i)
                sends[0](i).wait_recv()

            for g in range(groups):
                dz = dyin[m, i, group(g), :].astype(F32) * scale
                dz = dz - zown[m, i, group(g), :].astype(F32) * tilt - base[kind(g)]
                dzb[m, core, i, group(g), :] = inside(g, dz.astype(BF16))

        def between():
            @pl.when(first)
            def _():
                send_dz(m)

        def use(i, conv):
            gate = jnp.concatenate([mask_v[m, i, centre, :].astype(F32)] * (half // 128), axis=1)
            du = (conv * gate).astype(BF16)
            gin_v[m, i] = du

            @pl.when(sec > 0)
            def _():
                dy = du.astype(F32) * slope_prev[m, i]
                dyout[m, i] = dy.astype(BF16)
                one = jnp.sum(dy, 0, keepdims=True)
                cross = jnp.sum(dy * zin[m, i, centre, :].astype(F32), 0, keepdims=True)
                cross = prev_coef[m, pl.ds(0, 1), :] * (cross + prev_coef[m, pl.ds(2 + 3 * i, 1), :] * one)
                if i == 1:
                    one = one + sums_out[m, pl.ds(0, 1), :]
                    cross = cross + sums_out[m, pl.ds(1, 1), :]
                sums_out[m, pl.ds(0, 1), :] = one
                sums_out[m, pl.ds(1, 1), :] = cross
                if i == 1:
                    start_stats(*back_stats, m, sec - 1, False)
                send_block(dy_sends(m, sec - 1), i)

        together, _ = convolve(dzb, wt_v, dx_s, dx_r, m, lambda r: 2 - r, 2, 0, prepare, use, between)
        _, apart = convolve(dzb, wt_v, dx_s, dx_r, m, lambda r: 2 - r, 2, 0, prepare, use)

        @pl.when(first | last)
        def _():
            together()

        @pl.when((sec > 0) & (sec < sections - 1))
        def _():
            apart()

        for copy in result_copies(gin_v, grads_in, gin_sem, pg_s, pg_r, m):
            copy.start()

        @pl.when((sec > 0) & (sec < sections - 1))
        def _():
            send_dz(m)

    def turn_weights():
        for copy in wt_copies():
            copy.wait()

        def one(i, carry):
            for h in range(2):
                wt_v[h, i] = wt_v[h, i].T
            return carry
        lax.fori_loop(0, 9, one, 0)

    @pl.when(late)
    def _():
        turn_weights()

    def step(t, carry):
        ahead = t - sec
        behind = t - (2 * sections - 1 - sec)

        @pl.when((ahead >= 0) & (ahead < batches))
        def _():
            forward(ahead)

        @pl.when(late & (ahead >= 0) & (ahead < batches))
        def _():
            send_turned(ahead)

        @pl.when(jnp.logical_not(late) & (ahead == batches))
        def _():
            def turned(m, carry):
                send_turned(m)
                return carry
            lax.fori_loop(0, batches, turned, 0)
            turn_weights()

        @pl.when(jnp.logical_not(late) & (ahead == batches + 1))
        def _():
            def onward(m, carry):
                turned_onward(m, start, True)
                return carry
            lax.fori_loop(0, batches, onward, 0)

        @pl.when(first & (ahead == batches + 2))
        def _():
            relay_all()

        done = ahead - jnp.where(last, 0, 1)

        @pl.when((behind >= 0) & (behind < batches))
        def _():
            backward(behind)

        @pl.when((done >= 0) & (done < batches))
        def _():
            finish(done)

        @pl.when(late & (ahead >= 1) & (ahead <= batches))
        def _():
            turned_onward(ahead - 1, start, True)

        return carry

    lax.fori_loop(0, 2 * sections - 1 + batches, step, 0)

    remote(sums_v.at[core], sums_v.at[core], sv_s, sv_r, sec, partner).start()

    @pl.when(last)
    def _():
        def send(m, carry):
            send_dz(m)
            return carry

        lax.fori_loop(0, batches, send, 0)

    @pl.when(jnp.logical_not(first))
    def _():
        relay_all()

    def add(m, carry):
        add_gradients(m)
        return carry

    lax.fori_loop(0, batches - 1, add, 0)

    def swap(r, d):
        other = (seat + d) % 4
        return remote(
            swap_out.at[r, pl.ds(pl.multiple_of(other * share, share), share), :], swap_in.at[r, 4 - d - 1],
            sw_s.at[r, d - 1], sw_r.at[r, 4 - d - 1], sec, 4 * team + other,
        )

    gather_taps(batches - 1)
    for r in range(3):
        part = acc_v[r] + kernel_row(batches - 1, r)
        acc_v[r] = part
        swap_out[r] = part.astype(BF16)
        for d in range(1, 4):
            swap(r, d).start()

    def dw_copy(r):
        return pltpu.make_async_copy(dw_v.at[r], weight_grad.at[r], dw_sem.at[r])

    own_rows = pl.ds(pl.multiple_of(seat * share, share), share)
    for r in range(3):
        for c in range(3):
            dw_v[r, c, :, pl.ds(pl.multiple_of(seat * lanes, lanes), lanes)] = acc_v[r, own_rows, pl.ds(c * lanes, lanes)]
        for d in range(1, 4):
            swap(r, 4 - d).wait_recv()
            source = (seat + d) % 4
            for c in range(3):
                dw_v[r, c, :, pl.ds(pl.multiple_of(source * lanes, lanes), lanes)] = swap_in[
                    r, d - 1, :, pl.ds(c * lanes, lanes)
                ].astype(F32)
        dw_copy(r).start()

    for r in range(3):
        dw_copy(r).wait()
        for d in range(1, 4):
            swap(r, d).wait_send()

    @pl.when(decoder)
    def _():
        argument_sent(*mask_parts)

    @pl.when(sec < sections - 1)
    def _():
        for copy in affine_sends():
            copy.wait_send()

    def sums_copy():
        return remote(sums_v.at[core], sums_v.at[core], sv_s, sv_r, sec, partner)

    sums_copy().wait_recv()
    sums_copy().wait_send()
    for h in range(2):
        shift_sum[:, pl.ds(h * half, half)] = sums_v[h, pl.ds(0, 1), :]
        gain_sum[:, pl.ds(h * half, half)] = sums_v[h, pl.ds(1, 1), :]

    def drain(m, carry):
        for src, dst, sems in ((out_v, outs, (out_sem, po_s, po_r)), (gin_v, grads_in, (gin_sem, pg_s, pg_r))):
            here, there = result_copies(src, dst, *sems, m)
            here.wait()
            there.wait_send()
            remote(
                src.at[m, :, pl.ds(0, strip), :], dst.at[m, :, :, channels(1 - core)], sems[1].at[m], sems[2].at[m],
                sec, partner,
            ).wait_recv()

        turned_each(m, sent)
        turned_onward(m, sent, False)
        turned_relay(m).wait_send()
        dz_each(m, sent)
        for i in range(2):
            pass_on(ub, ux_s, ux_r, m, i).wait_send()
            pass_on(dzb, dx_s, dx_r, m, i).wait_send()

        @pl.when(first)
        def _():
            argument_sent(*input_parts(images, m))

        @pl.when(last)
        def _():
            argument_sent(*input_parts(cotangent, m))
            stats_each(*seed_stats, m, sec, True, sent)

        @pl.when(sec < sections - 1)
        def _():
            stats_each(*down_stats, m, sec + 1, False, sent)
            block_sent(z_sends(m, sec + 1))

        stats_each(*same_stats, m, sec, True, sent)
        for i in range(2):
            each_edge(own_edges(m), i, sent)

        @pl.when(sec > 0)
        def _():
            stats_each(*back_stats, m, sec - 1, False, sent)
            block_sent(dy_sends(m, sec - 1))

        return carry

    lax.fori_loop(0, batches, drain, 0)


def settle(*refs):
    count = (len(refs) - 2) // 3
    sources, targets, stages = refs[:count], refs[count : 2 * count], refs[2 * count : 3 * count]
    moves = []
    for src, dst, stage in zip(sources, targets, stages):
        if len(src.shape) == 2:
            moves.append((src, dst, stage))
        else:
            moves += [(src.at[i], dst.at[i], stage.at[i]) for i in range(src.shape[0])]
    ins = [pltpu.make_async_copy(src, stage, refs[-2].at[i]) for i, (src, dst, stage) in enumerate(moves)]
    outs = [pltpu.make_async_copy(stage, dst, refs[-1].at[i]) for i, (src, dst, stage) in enumerate(moves)]
    for copy in ins:
        copy.start()
    for come, go in zip(ins, outs):
        come.wait()
        go.start()
    for copy in outs:
        copy.wait()


def body(images, switches, conv_weights, gains, shifts, cotangent):
    sections = lax.axis_size("section")
    strips = lax.axis_size("rows")
    batches, pictures, strip_rows, cols, ch = images.shape
    strip = strip_rows * cols
    px = 2 * strip
    tall = px + 2 * cols
    anywhere = pl.BlockSpec(memory_space=pl.ANY)
    vmem = pl.BlockSpec(memory_space=pltpu.VMEM)
    dma = pltpu.SemaphoreType.DMA
    flops = 3 * 2 * 9 * ch * ch * batches * px
    share = ch // strips
    chips = strips // 2
    outs, grads_in, weight_grad, gain_sum, shift_sum = pl.pallas_call(
        functools.partial(kernel, sections, strips, cols),
        out_shape=(
            jax.ShapeDtypeStruct((batches, pictures, strip, ch), BF16),
            jax.ShapeDtypeStruct((batches, pictures, strip, ch), BF16),
            jax.ShapeDtypeStruct((3, 3, share, ch), F32),
            jax.ShapeDtypeStruct((1, ch), F32),
            jax.ShapeDtypeStruct((1, ch), F32),
        ),
        in_specs=[anywhere, anywhere, anywhere, vmem, vmem, vmem],
        out_specs=(anywhere, anywhere, anywhere, vmem, vmem),
        scratch_shapes=[
            pltpu.VMEM((2, 9, ch // 2, ch // 2), BF16),
            pltpu.VMEM((2, 9, ch // 2, ch // 2), BF16),
            pltpu.VMEM((batches, 2, tall, ch // 2), BF16),
            pltpu.VMEM((batches, 2, strip, 128), BF16),
            pltpu.VMEM((batches, 2, tall, 128), BF16),
            pltpu.VMEM((1, ch), F32),
            pltpu.VMEM((1, ch), F32),
            pltpu.VMEM((batches, 2, tall, ch // 2), BF16),
            pltpu.VMEM((batches, chips, 4, ch // 2), F32),
            pltpu.VMEM((batches, 2, tall, ch // 2), BF16),
            pltpu.VMEM((batches, chips, 4, ch // 2), F32),
            pltpu.VMEM((batches, 2, 2, tall, ch // 2), BF16),
            pltpu.VMEM((batches, 2, px, ch // 2), F32),
            pltpu.VMEM((batches, 8, ch // 2), F32),
            pltpu.VMEM((batches, 8, ch // 2), F32),
            pltpu.VMEM((batches, 2, tall, ch // 2), BF16),
            pltpu.VMEM((batches, chips, 2, ch // 2), F32),
            pltpu.VMEM((batches, 2, 2, tall, ch // 2), BF16),
            pltpu.VMEM((batches, 2, px, ch // 2), BF16),
            pltpu.VMEM((3, 2 * px, ch // 2), F32),
            pltpu.VMEM((2, 2, ch // 2), F32),
            pltpu.VMEM((batches, 4, ch // 2), F32),
            pltpu.VMEM((batches, 2, ch // 2), F32),
            pltpu.VMEM((batches, 2, ch // 2), F32),
            pltpu.VMEM((batches, 2, px, ch // 2), BF16),
            pltpu.VMEM((batches, 2, px, ch // 2), BF16),
            pltpu.VMEM((batches, ch, px), BF16),
            pltpu.VMEM((batches, 2, strips // 2, 4 * share, px), BF16),
            pltpu.VMEM((batches, 2, px * strips // 2 + 2 * cols, ch // 4), BF16),
            pltpu.VMEM((2, px * strips // 2 + 2 * cols, 3 * ch // 4), BF16),
            pltpu.VMEM((3, 4 * share, 3 * ch // 4), F32),
            pltpu.VMEM((3, 4 * share, 3 * ch // 4), BF16),
            pltpu.VMEM((3, 3, share, 3 * ch // 4), BF16),
            pltpu.VMEM((3, 3, share, ch), F32),
            dma((2,)), dma((2,)),
            dma((batches,)),
            dma((batches,)), dma((batches,)),
            dma((batches, 2)), dma((batches, 2)),
            dma, dma,
            dma((2,)), dma((2,)),
            dma((2,)), dma((2,)),
            dma((batches, 2)), dma((batches, 2)),
            dma((batches, 2)), dma((batches, 2)),
            dma, dma,
            dma((batches, 3, 2)), dma((batches, 3, 2)),
            dma((batches, chips)), dma((batches, chips)),
            dma((batches, 3, 2)), dma((batches, 3, 2)),
            dma((batches, chips)), dma((batches, chips)),
            dma((batches, 3, 2)), dma((batches, 3, 2)),
            dma((batches, chips)), dma((batches, chips)),
            dma((batches, chips)),
            dma((batches,)), dma((batches,)), dma((batches,)),
            dma((batches,)), dma((batches,)), dma((batches,)),
            dma((batches, chips)), dma((batches, chips)), dma((batches, chips)),
            dma((batches,)), dma((batches,)),
            dma((batches, strips)), dma((batches, strips)),
            dma((3, 3)), dma((3, 3)),
            dma((3,)),
        ],
        compiler_params=pltpu.CompilerParams(
            collective_id=0, has_side_effects=True, vmem_limit_bytes=56 * 2**20
        ),
        cost_estimate=pl.CostEstimate(
            flops=flops, bytes_accessed=2 * 9 * ch * ch * 2, transcendentals=0
        ),
    )(
        images.reshape(batches, pictures, strip, ch),
        cotangent.reshape(batches, pictures, strip, ch),
        conv_weights.reshape(9, ch, ch),
        gains,
        shifts,
        switches.reshape(-1, switches.shape[-1]),
    )
    results = (outs, grads_in, weight_grad, gain_sum, shift_sum)
    outs, grads_in, weight_grad, gain_sum, shift_sum = pl.pallas_call(
        settle,
        out_shape=tuple(jax.ShapeDtypeStruct(r.shape, r.dtype) for r in results),
        in_specs=[anywhere] * 5,
        out_specs=(anywhere,) * 5,
        scratch_shapes=[pltpu.VMEM(r.shape, r.dtype) for r in results] + [dma((2 * batches + 5,))] * 2,
        compiler_params=pltpu.CompilerParams(vmem_limit_bytes=60 * 2**20),
    )(*results)
    shape = (1, batches, pictures, strip_rows, cols, ch)
    return (outs.reshape(shape), grads_in.reshape(shape), weight_grad[None], gain_sum, shift_sum)


def solution(mesh):
    return jax.shard_map(
        body,
        mesh=mesh,
        in_specs=(
            P(None, None, "rows", None, None),
            P(None, None, "rows", None),
            P("section", None, None, None, None),
            P("section", None),
            P("section", None),
            P(None, None, "rows", None, None),
        ),
        out_specs=(
            P("section", None, None, "rows", None, None),
            P("section", None, None, "rows", None, None),
            P("section", None, None, "rows", None),
            P("section", None),
            P("section", None),
        ),
        check_vma=False,
    )
```

```python
import functools

import jax
import jax.numpy as jnp
from jax import lax
from jax.experimental import pallas as pl
from jax.experimental.pallas import tpu as pltpu
from jax.sharding import PartitionSpec as P

EPSILON = 1e-05
MESH = pl.DeviceIdType.MESH
BF16 = jnp.bfloat16
F32 = jnp.float32


def kernel(
    sections, strips, cols,
    images, cotangent, weights, gains, shifts, switches,
    outs, grads_in, weight_grad, gain_sum, shift_sum,
    w_v, wt_v, inp, mask_own, mask_v, gain_prev, shift_prev, zin, zin_stat, zown, own_stat, ub, slope_prev,
    prev_coef, own_coef, dyin, dy_stat, dzb, dyout, product_v, sums_v, stat_out, sums_out, seed_sums, out_v, gin_v,
    ut_own, ut_all, dz_all, dz_taps, acc_v, swap_out, swap_in, dw_v,
    w_sem, wt_sem, in_sem, pi_s, pi_r, ie_s, ie_r, mp_s, mp_r, me_s, me_r, gp_s, gp_r,
    ux_s, ux_r, dx_s, dx_r, sv_s, sv_r,
    fz_s, fz_r, fs_s, fs_r, oe_s, oe_r, os_s, os_r, bz_s, bz_r, bs_s, bs_r, ls_s,
    out_sem, po_s, po_r, gin_sem, pg_s, pg_r,
    ut_s, ut_r, uw_s, uf_s, uf_r, dz_s, dz_r, sw_s, sw_r, dw_sem,
):
    sec = lax.axis_index("section")
    row = lax.axis_index("rows")
    batches, _, tall, half = inp.shape
    ch = 2 * half
    px = tall - 2 * cols
    strip = px // 2
    groups = tall // cols
    chips = strips // 2
    local = float(px)
    total = 2.0 * local * chips
    first, last, decoder = sec == 0, sec == sections - 1, sec == sections // 2
    late = sec >= sections // 2
    core = row % 2
    partner = row + 1 - 2 * core
    has_up, has_down = row >= 2, row < strips - 2
    centre = pl.ds(cols, px)
    chip = row // 2
    team, seat = row // 4, row % 4
    lanes = dz_all.shape[3]
    block = ut_all.shape[3]
    share = block // 4
    mine = pl.multiple_of(cols + strip * core, cols)

    def channels(h):
        return pl.ds(pl.multiple_of(h * half, half), half)

    def w_copies():
        return [
            pltpu.make_async_copy(weights.at[:, channels(h), channels(core)], w_v.at[h], w_sem.at[h]) for h in range(2)
        ]

    def wt_copies():
        return [
            pltpu.make_async_copy(weights.at[:, channels(core), channels(h)], wt_v.at[h], wt_sem.at[h]) for h in range(2)
        ]

    def in_copy(src, m):
        return pltpu.make_async_copy(src.at[m, :, :, channels(core)], inp.at[m, :, pl.ds(mine, strip), :], in_sem.at[m])

    for copy in w_copies() + wt_copies():
        copy.start()

    @pl.when(first)
    def _():
        for m in range(batches):
            in_copy(images, m).start()

    @pl.when(last)
    def _():
        for m in range(batches):
            in_copy(cotangent, m).start()

    barrier = pltpu.get_barrier_semaphore()
    for s in range(sections):
        @pl.when((sec >= s - 1) & (sec <= s + 1))
        def _():
            def greet(i, carry):
                @pl.when((s != sec) | (i != row))
                def _():
                    pl.semaphore_signal(barrier, inc=1, device_id=(jnp.int32(s), i), device_id_type=MESH)
                return carry
            lax.fori_loop(0, strips, greet, 0)

    acc_v[...] = jnp.zeros_like(acc_v)
    sums_v[...] = jnp.zeros_like(sums_v)

    for m in range(batches):
        for i in range(2):
            for at in (0, dz_all.shape[2] - cols):
                dz_all[m, i, pl.ds(at, cols), :] = jnp.zeros((cols, lanes), BF16)

    @pl.when(decoder)
    def _():
        wide = cols // 2
        windows_at = lax.broadcasted_iota(jnp.int32, (cols, wide), 1)
        places = lax.broadcasted_iota(jnp.int32, (cols, wide), 0)
        pick = (lax.shift_right_logical(places, 1) == windows_at).astype(F32)
        table = lax.dot_general(
            pick, switches[...].astype(F32), (((1,), (1,)), ((), ())), preferred_element_type=F32
        )
        odd = jnp.bitwise_and(lax.broadcasted_iota(jnp.int32, (cols, 128), 0), 1).astype(F32)
        windows = strip // cols // 2
        for m in range(batches):
            for i in range(2):
                for w in range(windows):
                    at = (m * 2 + i) * windows + w
                    value = jnp.broadcast_to(table[:, at : at + 1], (cols, 128))
                    for p in range(2):
                        hit = (jnp.abs(value - (2.0 * p + odd)) < 0.5).astype(F32).astype(BF16)
                        mask_own[m, i, pl.ds((2 * w + p) * cols, cols), :] = hit
        for m in range(batches):
            mask_v[m, :, pl.ds(mine, strip), :] = mask_own[m]

    @pl.when(jnp.logical_not(decoder))
    def _():
        mask_v[...] = jnp.ones_like(mask_v)

    near = 1 + jnp.where(sec > 0, 1, 0) + jnp.where(sec < sections - 1, 1, 0)
    pl.semaphore_wait(barrier, near * strips - 1)

    def remote(src, dst, send, recv, s, i):
        return pltpu.make_async_remote_copy(
            src_ref=src, dst_ref=dst, send_sem=send, recv_sem=recv, device_id=(s, i), device_id_type=MESH
        )

    def to_partner(src_at, dst_at, send, recv):
        return remote(src_at(1 - core), dst_at(pl.ds(mine, strip)), send, recv, sec, partner)

    def start_argument(src_at, dst_at, pair_sems, edge_sems):
        to_partner(src_at, dst_at, *pair_sems).start()

        @pl.when((core == 1) & has_down)
        def _():
            for i in range(2):
                remote(
                    src_at(i, pl.ds(strip - cols, cols)), dst_at(pl.ds(0, cols)),
                    edge_sems[0].at[i], edge_sems[1].at[0], sec, row + 1 + i,
                ).start()

        @pl.when((core == 0) & has_up)
        def _():
            for i in range(2):
                remote(
                    src_at(i, pl.ds(0, cols)), dst_at(pl.ds(cols + px, cols)),
                    edge_sems[0].at[i], edge_sems[1].at[1], sec, row - 2 + i,
                ).start()

    def argument_arrived(src_at, dst_at, pair_sems, edge_sems):
        to_partner(src_at, dst_at, *pair_sems).wait_recv()

        @pl.when(has_up)
        def _():
            remote(
                src_at(0, pl.ds(0, cols)), dst_at(pl.ds(0, cols)), edge_sems[0].at[0], edge_sems[1].at[0], sec, row
            ).wait_recv()

        @pl.when(has_down)
        def _():
            remote(
                src_at(0, pl.ds(0, cols)), dst_at(pl.ds(cols + px, cols)), edge_sems[0].at[0], edge_sems[1].at[1],
                sec, row,
            ).wait_recv()

    def argument_sent(src_at, dst_at, pair_sems, edge_sems):
        to_partner(src_at, dst_at, *pair_sems).wait_send()

        @pl.when(((core == 1) & has_down) | ((core == 0) & has_up))
        def _():
            for i in range(2):
                remote(
                    src_at(i, pl.ds(0, cols)), dst_at(pl.ds(0, cols)), edge_sems[0].at[i], edge_sems[1].at[0], sec, row
                ).wait_send()

    def input_parts(src, m):
        return (
            lambda i, r=pl.ds(0, strip): src.at[m, :, r, channels(i)],
            lambda r: inp.at[m, :, r, :],
            (pi_s.at[m], pi_r.at[m]),
            (ie_s.at[m], ie_r.at[m]),
        )

    mask_parts = (
        lambda i, r=pl.ds(0, strip): mask_own.at[:, :, r, :],
        lambda r: mask_v.at[:, :, r, :],
        (mp_s, mp_r),
        (me_s, me_r),
    )

    @pl.when(first)
    def _():
        for m in range(batches):
            start_argument(*input_parts(images, m))

    @pl.when(last)
    def _():
        for m in range(batches):
            start_argument(*input_parts(cotangent, m))

    @pl.when(decoder)
    def _():
        start_argument(*mask_parts)

    def affine_sends():
        return (
            remote(gains, gain_prev, gp_s.at[0], gp_r.at[0], sec + 1, row),
            remote(shifts, shift_prev, gp_s.at[1], gp_r.at[1], sec + 1, row),
        )

    @pl.when(sec < sections - 1)
    def _():
        for copy in affine_sends():
            copy.start()

    def block_sends(src, src_from, dst, send, recv, m, s):
        def piece(k, src_row, dst_row, rows, to):
            def one(i):
                return remote(
                    src.at[m, i, pl.ds(src_from + src_row, rows), :], dst.at[m, i, pl.ds(dst_row, rows), :],
                    send.at[m, k, i], recv.at[m, k, i], s, to,
                )
            return one

        return (
            piece(0, 0, cols, px, row), piece(1, px - cols, 0, cols, row + 2), piece(2, 0, cols + px, cols, row - 2)
        )

    def each_edge(parts, i, act):
        _, to_down, to_up = parts

        @pl.when(has_down)
        def _():
            act(to_down(i))

        @pl.when(has_up)
        def _():
            act(to_up(i))

    def edges_arrived(parts, i):
        _, to_down, to_up = parts

        @pl.when(has_up)
        def _():
            to_down(i).wait_recv()

        @pl.when(has_down)
        def _():
            to_up(i).wait_recv()

    def send_block(parts, i):
        each_edge(parts, i, start)
        parts[0](i).start()

    def block_sent(parts):
        for i in range(2):
            each_edge(parts, i, sent)
            parts[0](i).wait_send()

    def start(copy):
        copy.start()

    def sent(copy):
        copy.wait_send()

    def came(copy):
        copy.wait_recv()

    def z_sends(m, s):
        return block_sends(zown, cols, zin, fz_s, fz_r, m, s)

    def own_edges(m):
        return block_sends(zown, cols, zown, oe_s, oe_r, m, sec)

    def dy_sends(m, s):
        return block_sends(dyout, 0, dyin, bz_s, bz_r, m, s)

    def stats_each(src, dst, send, recv, m, s, same, act):
        def one(d, carry):
            q = chip + d
            q = jnp.where(q >= chips, q - chips, q)
            act(remote(src.at[m], dst.at[m, chip], send.at[m, d], recv.at[m, d], s, 2 * q + core))
            return carry
        lax.fori_loop(1 if same else 0, chips, one, 0)

    def start_stats(src, dst, send, recv, m, s, same):
        stats_each(src, dst, send, recv, m, s, same, start)
        if same:
            dst[m, chip] = src[m]

    def wait_stats(src, dst, send, recv, m, same):
        stats_each(src, dst, send, recv, m, sec, same, came)

    down_stats = (stat_out, zin_stat, fs_s, fs_r)
    same_stats = (stat_out, own_stat, os_s, os_r)
    back_stats = (sums_out, dy_stat, bs_s, bs_r)
    seed_stats = (seed_sums, dy_stat, ls_s, bs_r)

    def join(stats_ref, m):
        means = stats_ref[m, :, 0, :], stats_ref[m, :, 1, :]
        mean = jnp.sum(means[0] + means[1], 0, keepdims=True) / (2.0 * chips)
        off = [part - mean for part in means]
        squares = jnp.sum(stats_ref[m, :, 2, :] + stats_ref[m, :, 3, :], 0, keepdims=True)
        apart = jnp.sum(off[0] * off[0] + off[1] * off[1], 0, keepdims=True)
        at = (jnp.maximum(chip - 1, 0), chip, jnp.minimum(chip + 1, chips - 1))
        offs = [[stats_ref[m, q, pl.ds(i, 1), :] - mean for q in at] for i in range(2)]
        return lax.rsqrt((squares + local * apart) / total + EPSILON), offs

    def kind(g):
        return 0 if g == 0 else 2 if g == groups - 1 else 1

    def inside(g, values):
        if kind(g) == 1:
            return values
        return jnp.where(has_up if kind(g) == 0 else has_down, values, jnp.zeros_like(values))

    def group(g):
        return pl.ds(g * cols, cols)

    column = lax.broadcasted_iota(jnp.int32, (1, cols, half), 1)

    def taps_joined(parts, left, right):
        rows = parts[0].shape[0]

        def moved(values, by, edge):
            turned = pltpu.roll(values, by % rows, 0).reshape(rows // cols, cols, half)
            return jnp.where(column == edge, 0.0, turned).reshape(rows, half)
        return parts[1] + moved(parts[left], 1, 0) + moved(parts[right], -1, cols - 1)

    def pass_on(operand, send, recv, m, i):
        return remote(operand.at[m, core, i], operand.at[m, core, i], send.at[m, i], recv.at[m, i], sec, partner)

    def products(operand, w, m, h, r_at, images_at):
        rows = images_at.size * px

        def one(c):
            acc = jnp.zeros((rows, half), F32)
            for r in range(3):
                left = operand[m, h, images_at, pl.ds(r_at(r) * cols, px), :].reshape(rows, half)
                acc += jnp.dot(left, w[h, 3 * r + c], preferred_element_type=F32)
            return acc
        return one

    def convolve(operand, w, send, recv, m, r_at, left, right, prepare, use, after=lambda i: None):
        def part(images_at, wait_for):
            rows = pl.ds(0, images_at.size * px)
            mine_first = products(operand, w, m, core, r_at, images_at)
            for c in range(3):
                product_v[c, rows, :] = mine_first(c)
            for i in wait_for:
                pass_on(operand, send, recv, m, i).wait_recv()
            then = products(operand, w, m, 1 - core, r_at, images_at)
            return taps_joined([product_v[c, rows, :] + then(c) for c in range(3)], left, right)

        def ready(i):
            prepare(i)
            pass_on(operand, send, recv, m, i).start()
            after(i)

        def together():
            for i in range(2):
                ready(i)
            whole = part(pl.ds(0, 2), range(2))
            for i in range(2):
                use(i, whole[i * px : (i + 1) * px])

        def apart():
            for i in range(2):
                ready(i)
                use(i, part(pl.ds(i, 1), [i]))

        return together, apart

    def turned_copy(m, q):
        src = ut_own.at[m, pl.ds(pl.multiple_of((q // 2) * block, block), block), :]
        return src, ut_all.at[m, core, chip]


    def turned_each(m, act):
        def one(d, carry):
            q = chip + d
            q = jnp.where(q >= chips, q - chips, q)
            its_team = q // 2
            nearest = 2 * its_team + jnp.where(chip > q, 1, 0)

            @pl.when((its_team == team) | (q == nearest))
            def _():
                src, dst = turned_copy(m, q)
                act(remote(src, dst, ut_s.at[m, d], ut_r.at[m, d], sec, 2 * q + core))
            return carry
        lax.fori_loop(1, chips, one, 0)

    def entry_for(p):
        return (p // 2 != team) & (jnp.where(p > chip, 1, 0) == chip % 2)

    def turned_arrived(m):
        def one(d, carry):
            p = chip - d
            p = jnp.where(p < 0, p + chips, p)

            @pl.when(jnp.logical_not(entry_for(p)))
            def _():
                piece = ut_all.at[m, core, p]
                remote(piece, piece, ut_s.at[m, d], ut_r.at[m, d], sec, row).wait_recv()
            return carry
        lax.fori_loop(1, chips, one, 0)

    def turned_onward(m, act, arrive):
        other = chip + 1 - 2 * (chip % 2)

        def one(d, carry):
            p = chip - d
            p = jnp.where(p < 0, p + chips, p)

            @pl.when(entry_for(p))
            def _():
                piece = ut_all.at[m, core, p]
                if arrive:
                    remote(piece, piece, ut_s.at[m, d], ut_r.at[m, d], sec, row).wait_recv()
                there = other - p
                there = jnp.where(there < 0, there + chips, there)
                act(remote(piece, piece, uw_s.at[m, d], ut_r.at[m, there], sec, 2 * other + core))

            return carry
        lax.fori_loop(1, chips, one, 0)

    def turn_inputs(m):
        for h in range(2):
            ut_own[m, pl.ds(h * half, half), :] = ub[m, h, core, centre, :].T
        mine_at = pl.ds(pl.multiple_of(team * block, block), block)
        ut_all[m, core, chip] = ut_own[m, mine_at, :]

    def send_turned(m):
        turn_inputs(m)
        turned_each(m, start)

    def turned_relay(m):
        return remote(ut_all.at[m, core], ut_all.at[m, core], uf_s.at[m], uf_r.at[m], sec, partner)

    def relay_turned(m):
        turned_arrived(m)
        turned_relay(m).start()

    def pass_on_all():
        def one(m, carry):
            turned_onward(m, start, True)
            return carry
        lax.fori_loop(0, batches, one, 0)

    def relay_all():
        def one(m, carry):
            relay_turned(m)
            return carry
        lax.fori_loop(0, batches, one, 0)

    def dz_piece(m, i, k):
        src = dzb.at[m, core, i, centre, pl.ds(pl.multiple_of(k * lanes, lanes), lanes)]
        return src, dz_all.at[m, i, pl.ds(pl.multiple_of(cols + chip * px, cols), px), :]

    def dz_each(m, i, act):
        def one(e, carry):
            q = team + e
            q = 2 * jnp.where(q >= chips // 2, q - chips // 2, q) + core
            for k in range(2):
                @pl.when((q != chip) | (k != core))
                def _():
                    src, dst = dz_piece(m, i, k)
                    act(remote(src, dst, dz_s.at[m, i, 2 * e + k], dz_r.at[m, i, chip], sec, 2 * q + k))
            return carry
        lax.fori_loop(0, chips // 2, one, 0)

    def send_dz(m, i):
        dz_each(m, i, start)

        @pl.when(chip % 2 == core)
        def _():
            dz_all[m, i, pl.ds(pl.multiple_of(cols + chip * px, cols), px), :] = dzb[
                m, core, i, centre, pl.ds(pl.multiple_of(core * lanes, lanes), lanes)
            ]

    def dz_arrived(m):
        for i in range(2):
            def one(p, carry):
                @pl.when((p != chip) | (chip % 2 != core))
                def _():
                    piece = dz_all.at[m, i, pl.ds(cols, px), :]
                    remote(piece, piece, dz_s.at[m, i, 0], dz_r.at[m, i, p], sec, row).wait_recv()
                return carry
            lax.fori_loop(0, chips, one, 0)

    def gather_taps(m):
        dz_arrived(m)
        relayed = ut_all.at[m, 1 - core]
        pltpu.make_async_copy(relayed, relayed, uf_r.at[m]).wait()
        rows = dz_all.shape[2]
        edge = lax.broadcasted_iota(jnp.int32, (1, cols, lanes), 1)
        for i in range(2):
            values = dz_all[m, i].astype(F32)
            for c, by, gone in ((0, rows - 1, cols - 1), (2, 1, 0)):
                turned = pltpu.roll(values, by, 0).reshape(rows // cols, cols, lanes)
                turned = jnp.where(edge == gone, 0.0, turned).reshape(rows, lanes)
                dz_taps[i, :, pl.ds(c * lanes, lanes)] = turned.astype(BF16)
            dz_taps[i, :, pl.ds(lanes, lanes)] = dz_all[m, i]

    def kernel_row(m, r):
        part = jnp.zeros((block, 3 * lanes), F32)
        for i in range(2):
            left = jnp.concatenate([ut_all[m, i, q] for q in range(chips)], axis=1)
            part += jnp.dot(
                left, dz_taps[i, pl.ds((2 - r) * cols, px * (strips // 2)), :], preferred_element_type=F32
            )
        return part

    def add_gradients(m):
        gather_taps(m)
        for r in range(3):
            acc_v[r] = acc_v[r] + kernel_row(m, r)

    def forward(m):
        def prepare_first(i):
            for g in range(groups):
                ub[m, core, i, group(g), :] = inside(g, inp[m, i, group(g), :])

        def prepare_later(i):
            sends = z_sends(m, sec)
            inv = prev_coef[m, pl.ds(0, 1), :]
            slant = 0.5 * inv * gain_prev[:, channels(core)]
            shift = 0.5 * shift_prev[:, channels(core)]
            level = [slant * prev_coef[m, pl.ds(1 + 3 * i + e, 1), :] + shift for e in range(3)]
            edges_arrived(sends, i)
            sends[0](i).wait_recv()
            for g in range(groups):
                gate = jnp.concatenate([mask_v[m, i, group(g), :].astype(F32)] * (half // 128), axis=1)
                halved = zin[m, i, group(g), :].astype(F32) * slant + level[kind(g)]
                turn = jnp.tanh(halved)
                bent = halved * turn
                ub[m, core, i, group(g), :] = inside(g, ((halved + bent) * gate).astype(BF16))
                if kind(g) == 1:
                    slope_prev[m, i, pl.ds((g - 1) * cols, cols), :] = (0.5 + 0.5 * turn) * (1.0 + halved - bent)

        def prepare(i):
            @pl.when(first)
            def _():
                prepare_first(i)

            @pl.when(sec > 0)
            def _():
                prepare_later(i)

        def use(i, conv):
            mean = jnp.sum(conv, 0, keepdims=True) / local
            conv = conv - mean
            stat_out[m, pl.ds(i, 1), :] = mean
            stat_out[m, pl.ds(2 + i, 1), :] = jnp.sum(conv * conv, 0, keepdims=True)
            zown[m, i, centre, :] = conv.astype(BF16)

            @pl.when(sec < sections - 1)
            def _():
                if i == 1:
                    start_stats(*down_stats, m, sec + 1, False)
                send_block(z_sends(m, sec + 1), i)

        @pl.when(first)
        def _():
            in_copy(images, m).wait()
            argument_arrived(*input_parts(images, m))

        @pl.when(sec > 0)
        def _():
            @pl.when(m == 0)
            def _():
                for copy in affine_sends():
                    copy.wait_recv()

                @pl.when(decoder)
                def _():
                    argument_arrived(*mask_parts)

            wait_stats(*down_stats, m, False)
            inv, offs = join(zin_stat, m)
            for e, value in enumerate((inv, *offs[0], *offs[1])):
                prev_coef[m, pl.ds(e, 1), :] = value

        @pl.when(m == 0)
        def _():
            for copy in w_copies():
                copy.wait()

        together, apart = convolve(ub, w_v, ux_s, ux_r, m, lambda r: r, 0, 2, prepare, use)

        @pl.when(last)
        def _():
            together()

        @pl.when(jnp.logical_not(last))
        def _():
            apart()

        start_stats(*same_stats, m, sec, True)
        for i in range(2):
            each_edge(own_edges(m), i, start)

    def finish(m):
        wait_stats(*same_stats, m, True)
        inv, offs = join(own_stat, m)
        scale = inv * gains[:, channels(core)]
        for e, value in enumerate((inv, scale, *offs[0], *offs[1])):
            own_coef[m, pl.ds(e, 1), :] = value
        slant = 0.5 * scale
        shift = 0.5 * shifts[:, channels(core)]
        level = [[slant * off + shift for off in part] for part in offs]
        for i in range(2):
            edges_arrived(own_edges(m), i)

        @pl.when(last)
        def _():
            in_copy(cotangent, m).wait()
            argument_arrived(*input_parts(cotangent, m))
            ones, crosses = [], []
            for i in range(2):
                sums = jnp.zeros((cols, half), F32)
                cross = jnp.zeros((cols, half), F32)
                for g in range(groups):
                    z = zown[m, i, group(g), :].astype(F32)
                    halved = z * slant + level[i][kind(g)]
                    turn = jnp.tanh(halved)
                    bent = halved * turn
                    dy = inp[m, i, group(g), :].astype(F32) * ((0.5 + 0.5 * turn) * (1.0 + halved - bent))
                    dyin[m, i, group(g), :] = dy.astype(BF16)
                    if kind(g) == 1:
                        out_v[m, i, pl.ds((g - 1) * cols, cols), :] = (halved + bent).astype(BF16)
                        sums += dy
                        cross += dy * z
                one = jnp.sum(sums, 0, keepdims=True)
                ones.append(one)
                crosses.append(jnp.sum(cross, 0, keepdims=True) + offs[i][1] * one)
            seed_sums[m, pl.ds(0, 1), :] = ones[0] + ones[1]
            seed_sums[m, pl.ds(1, 1), :] = inv * (crosses[0] + crosses[1])
            start_stats(*seed_stats, m, sec, True)

        @pl.when(jnp.logical_not(last))
        def _():
            for i in range(2):
                for g in range(1, groups - 1):
                    halved = zown[m, i, group(g), :].astype(F32) * slant + level[i][1]
                    out_v[m, i, pl.ds((g - 1) * cols, cols), :] = (halved + halved * jnp.tanh(halved)).astype(BF16)

        for copy in result_copies(out_v, outs, out_sem, po_s, po_r, m):
            copy.start()

    def result_copies(src, dst, sem, send, recv, m):
        here, there = pl.multiple_of(strip * core, cols), pl.multiple_of(strip * (1 - core), cols)
        place = dst.at[m, :, :, channels(core)]
        return (
            pltpu.make_async_copy(src.at[m, :, pl.ds(here, strip), :], place, sem.at[m]),
            remote(src.at[m, :, pl.ds(there, strip), :], place, send.at[m], recv.at[m], sec, partner),
        )

    def backward(m):
        @pl.when(last)
        def _():
            wait_stats(*seed_stats, m, True)

        @pl.when(jnp.logical_not(last))
        def _():
            wait_stats(*back_stats, m, False)

        first_sum = jnp.sum(dy_stat[m, :, 0, :], 0, keepdims=True)
        cross_sum = jnp.sum(dy_stat[m, :, 1, :], 0, keepdims=True)
        sums_v[core, pl.ds(0, 1), :] = sums_v[core, pl.ds(0, 1), :] + first_sum
        sums_v[core, pl.ds(1, 1), :] = sums_v[core, pl.ds(1, 1), :] + cross_sum

        def prepare(i):
            inv = own_coef[m, pl.ds(0, 1), :]
            scale = own_coef[m, pl.ds(1, 1), :]
            tilt = scale * inv * (cross_sum / total)
            base = [scale * (first_sum / total) + tilt * own_coef[m, pl.ds(2 + 3 * i + e, 1), :] for e in range(3)]
            sends = dy_sends(m, sec)

            @pl.when(jnp.logical_not(last))
            def _():
                edges_arrived(sends, i)
                sends[0](i).wait_recv()

            for g in range(groups):
                dz = dyin[m, i, group(g), :].astype(F32) * scale
                dz = dz - zown[m, i, group(g), :].astype(F32) * tilt - base[kind(g)]
                dzb[m, core, i, group(g), :] = inside(g, dz.astype(BF16))

        def then(i):
            @pl.when(first)
            def _():
                send_dz(m, i)

        def use(i, conv):
            gate = jnp.concatenate([mask_v[m, i, centre, :].astype(F32)] * (half // 128), axis=1)
            du = (conv * gate).astype(BF16)
            gin_v[m, i] = du

            @pl.when(sec > 0)
            def _():
                dy = du.astype(F32) * slope_prev[m, i]
                dyout[m, i] = dy.astype(BF16)
                one = jnp.sum(dy, 0, keepdims=True)
                cross = jnp.sum(dy * zin[m, i, centre, :].astype(F32), 0, keepdims=True)
                cross = prev_coef[m, pl.ds(0, 1), :] * (cross + prev_coef[m, pl.ds(2 + 3 * i, 1), :] * one)
                if i == 1:
                    one = one + sums_out[m, pl.ds(0, 1), :]
                    cross = cross + sums_out[m, pl.ds(1, 1), :]
                sums_out[m, pl.ds(0, 1), :] = one
                sums_out[m, pl.ds(1, 1), :] = cross
                if i == 1:
                    start_stats(*back_stats, m, sec - 1, False)
                send_block(dy_sends(m, sec - 1), i)

        together, apart = convolve(dzb, wt_v, dx_s, dx_r, m, lambda r: 2 - r, 2, 0, prepare, use, then)

        @pl.when(first | last)
        def _():
            together()

        @pl.when((sec > 0) & (sec < sections - 1))
        def _():
            apart()

        for copy in result_copies(gin_v, grads_in, gin_sem, pg_s, pg_r, m):
            copy.start()

        @pl.when((sec > 0) & (sec < sections - 1))
        def _():
            for i in range(2):
                send_dz(m, i)

    def turn_weights():
        for copy in wt_copies():
            copy.wait()

        def one(i, carry):
            for h in range(2):
                wt_v[h, i] = wt_v[h, i].T
            return carry
        lax.fori_loop(0, 9, one, 0)

    @pl.when(late)
    def _():
        turn_weights()

    def step(t, carry):
        ahead = t - sec
        behind = t - (2 * sections - 1 - sec)

        @pl.when((ahead >= 0) & (ahead < batches))
        def _():
            forward(ahead)

        @pl.when(late & (ahead >= 0) & (ahead < batches))
        def _():
            send_turned(ahead)

        @pl.when(jnp.logical_not(late) & (ahead == batches))
        def _():
            def turned(m, carry):
                send_turned(m)
                return carry
            lax.fori_loop(0, batches, turned, 0)
            turn_weights()

        @pl.when(jnp.logical_not(late) & (ahead == batches + 1))
        def _():
            pass_on_all()

        @pl.when(first & (ahead == batches + 2))
        def _():
            relay_all()

        done = ahead - jnp.where(last, 0, 1)

        @pl.when((behind >= 0) & (behind < batches))
        def _():
            backward(behind)

        @pl.when((done >= 0) & (done < batches))
        def _():
            finish(done)

        @pl.when(last & (ahead >= 1) & (ahead <= batches))
        def _():
            turned_onward(ahead - 1, start, True)

        return carry

    lax.fori_loop(0, 2 * sections - 1 + batches, step, 0)

    remote(sums_v.at[core], sums_v.at[core], sv_s, sv_r, sec, partner).start()

    @pl.when(last)
    def _():
        def send(m, carry):
            for i in range(2):
                send_dz(m, i)
            return carry

        lax.fori_loop(0, batches, send, 0)

    @pl.when(late & jnp.logical_not(last))
    def _():
        pass_on_all()

    @pl.when(jnp.logical_not(first))
    def _():
        relay_all()

    def add(m, carry):
        add_gradients(m)
        return carry

    lax.fori_loop(0, batches - 1, add, 0)

    def swap(r, d):
        other = (seat + d) % 4
        return remote(
            swap_out.at[r, pl.ds(pl.multiple_of(other * share, share), share), :], swap_in.at[r, 4 - d - 1],
            sw_s.at[r, d - 1], sw_r.at[r, 4 - d - 1], sec, 4 * team + other,
        )

    gather_taps(batches - 1)
    for r in range(3):
        part = acc_v[r] + kernel_row(batches - 1, r)
        acc_v[r] = part
        swap_out[r] = part.astype(BF16)
        for d in range(1, 4):
            swap(r, d).start()

    def dw_copy(r):
        return pltpu.make_async_copy(dw_v.at[r], weight_grad.at[r], dw_sem.at[r])

    own_rows = pl.ds(pl.multiple_of(seat * share, share), share)
    for r in range(3):
        for c in range(3):
            dw_v[r, c, :, pl.ds(pl.multiple_of(seat * lanes, lanes), lanes)] = acc_v[r, own_rows, pl.ds(c * lanes, lanes)]
        for d in range(1, 4):
            swap(r, 4 - d).wait_recv()
            source = (seat + d) % 4
            for c in range(3):
                dw_v[r, c, :, pl.ds(pl.multiple_of(source * lanes, lanes), lanes)] = swap_in[
                    r, d - 1, :, pl.ds(c * lanes, lanes)
                ].astype(F32)
        dw_copy(r).start()

    for r in range(3):
        dw_copy(r).wait()
        for d in range(1, 4):
            swap(r, d).wait_send()

    @pl.when(decoder)
    def _():
        argument_sent(*mask_parts)

    @pl.when(sec < sections - 1)
    def _():
        for copy in affine_sends():
            copy.wait_send()

    def sums_copy():
        return remote(sums_v.at[core], sums_v.at[core], sv_s, sv_r, sec, partner)

    sums_copy().wait_recv()
    sums_copy().wait_send()
    for h in range(2):
        shift_sum[:, pl.ds(h * half, half)] = sums_v[h, pl.ds(0, 1), :]
        gain_sum[:, pl.ds(h * half, half)] = sums_v[h, pl.ds(1, 1), :]

    def drain(m, carry):
        for src, dst, sems in ((out_v, outs, (out_sem, po_s, po_r)), (gin_v, grads_in, (gin_sem, pg_s, pg_r))):
            here, there = result_copies(src, dst, *sems, m)
            here.wait()
            there.wait_send()
            remote(
                src.at[m, :, pl.ds(0, strip), :], dst.at[m, :, :, channels(1 - core)], sems[1].at[m], sems[2].at[m],
                sec, partner,
            ).wait_recv()

        turned_each(m, sent)
        turned_onward(m, sent, False)
        turned_relay(m).wait_send()
        for i in range(2):
            dz_each(m, i, sent)
        for i in range(2):
            pass_on(ub, ux_s, ux_r, m, i).wait_send()
            pass_on(dzb, dx_s, dx_r, m, i).wait_send()

        @pl.when(first)
        def _():
            argument_sent(*input_parts(images, m))

        @pl.when(last)
        def _():
            argument_sent(*input_parts(cotangent, m))
            stats_each(*seed_stats, m, sec, True, sent)

        @pl.when(sec < sections - 1)
        def _():
            stats_each(*down_stats, m, sec + 1, False, sent)
            block_sent(z_sends(m, sec + 1))

        stats_each(*same_stats, m, sec, True, sent)
        for i in range(2):
            each_edge(own_edges(m), i, sent)

        @pl.when(sec > 0)
        def _():
            stats_each(*back_stats, m, sec - 1, False, sent)
            block_sent(dy_sends(m, sec - 1))

        return carry

    lax.fori_loop(0, batches, drain, 0)


def settle(*refs):
    count = (len(refs) - 2) // 3
    sources, targets, stages = refs[:count], refs[count : 2 * count], refs[2 * count : 3 * count]
    moves = []
    for src, dst, stage in zip(sources, targets, stages):
        if len(src.shape) == 2:
            moves.append((src, dst, stage))
        else:
            moves += [(src.at[i], dst.at[i], stage.at[i]) for i in range(src.shape[0])]
    ins = [pltpu.make_async_copy(src, stage, refs[-2].at[i]) for i, (src, dst, stage) in enumerate(moves)]
    outs = [pltpu.make_async_copy(stage, dst, refs[-1].at[i]) for i, (src, dst, stage) in enumerate(moves)]
    for copy in ins:
        copy.start()
    for come, go in zip(ins, outs):
        come.wait()
        go.start()
    for copy in outs:
        copy.wait()


def body(images, switches, conv_weights, gains, shifts, cotangent):
    sections = lax.axis_size("section")
    strips = lax.axis_size("rows")
    batches, pictures, strip_rows, cols, ch = images.shape
    strip = strip_rows * cols
    px = 2 * strip
    tall = px + 2 * cols
    anywhere = pl.BlockSpec(memory_space=pl.ANY)
    vmem = pl.BlockSpec(memory_space=pltpu.VMEM)
    dma = pltpu.SemaphoreType.DMA
    flops = 3 * 2 * 9 * ch * ch * batches * px
    share = ch // strips
    chips = strips // 2
    outs, grads_in, weight_grad, gain_sum, shift_sum = pl.pallas_call(
        functools.partial(kernel, sections, strips, cols),
        out_shape=(
            jax.ShapeDtypeStruct((batches, pictures, strip, ch), BF16),
            jax.ShapeDtypeStruct((batches, pictures, strip, ch), BF16),
            jax.ShapeDtypeStruct((3, 3, share, ch), F32),
            jax.ShapeDtypeStruct((1, ch), F32),
            jax.ShapeDtypeStruct((1, ch), F32),
        ),
        in_specs=[anywhere, anywhere, anywhere, vmem, vmem, vmem],
        out_specs=(anywhere, anywhere, anywhere, vmem, vmem),
        scratch_shapes=[
            pltpu.VMEM((2, 9, ch // 2, ch // 2), BF16),
            pltpu.VMEM((2, 9, ch // 2, ch // 2), BF16),
            pltpu.VMEM((batches, 2, tall, ch // 2), BF16),
            pltpu.VMEM((batches, 2, strip, 128), BF16),
            pltpu.VMEM((batches, 2, tall, 128), BF16),
            pltpu.VMEM((1, ch), F32),
            pltpu.VMEM((1, ch), F32),
            pltpu.VMEM((batches, 2, tall, ch // 2), BF16),
            pltpu.VMEM((batches, chips, 4, ch // 2), F32),
            pltpu.VMEM((batches, 2, tall, ch // 2), BF16),
            pltpu.VMEM((batches, chips, 4, ch // 2), F32),
            pltpu.VMEM((batches, 2, 2, tall, ch // 2), BF16),
            pltpu.VMEM((batches, 2, px, ch // 2), F32),
            pltpu.VMEM((batches, 8, ch // 2), F32),
            pltpu.VMEM((batches, 8, ch // 2), F32),
            pltpu.VMEM((batches, 2, tall, ch // 2), BF16),
            pltpu.VMEM((batches, chips, 2, ch // 2), F32),
            pltpu.VMEM((batches, 2, 2, tall, ch // 2), BF16),
            pltpu.VMEM((batches, 2, px, ch // 2), BF16),
            pltpu.VMEM((3, 2 * px, ch // 2), F32),
            pltpu.VMEM((2, 2, ch // 2), F32),
            pltpu.VMEM((batches, 4, ch // 2), F32),
            pltpu.VMEM((batches, 2, ch // 2), F32),
            pltpu.VMEM((batches, 2, ch // 2), F32),
            pltpu.VMEM((batches, 2, px, ch // 2), BF16),
            pltpu.VMEM((batches, 2, px, ch // 2), BF16),
            pltpu.VMEM((batches, ch, px), BF16),
            pltpu.VMEM((batches, 2, strips // 2, 4 * share, px), BF16),
            pltpu.VMEM((batches, 2, px * strips // 2 + 2 * cols, ch // 4), BF16),
            pltpu.VMEM((2, px * strips // 2 + 2 * cols, 3 * ch // 4), BF16),
            pltpu.VMEM((3, 4 * share, 3 * ch // 4), F32),
            pltpu.VMEM((3, 4 * share, 3 * ch // 4), BF16),
            pltpu.VMEM((3, 3, share, 3 * ch // 4), BF16),
            pltpu.VMEM((3, 3, share, ch), F32),
            dma((2,)), dma((2,)),
            dma((batches,)),
            dma((batches,)), dma((batches,)),
            dma((batches, 2)), dma((batches, 2)),
            dma, dma,
            dma((2,)), dma((2,)),
            dma((2,)), dma((2,)),
            dma((batches, 2)), dma((batches, 2)),
            dma((batches, 2)), dma((batches, 2)),
            dma, dma,
            dma((batches, 3, 2)), dma((batches, 3, 2)),
            dma((batches, chips)), dma((batches, chips)),
            dma((batches, 3, 2)), dma((batches, 3, 2)),
            dma((batches, chips)), dma((batches, chips)),
            dma((batches, 3, 2)), dma((batches, 3, 2)),
            dma((batches, chips)), dma((batches, chips)),
            dma((batches, chips)),
            dma((batches,)), dma((batches,)), dma((batches,)),
            dma((batches,)), dma((batches,)), dma((batches,)),
            dma((batches, chips)), dma((batches, chips)), dma((batches, chips)),
            dma((batches,)), dma((batches,)),
            dma((batches, 2, chips)), dma((batches, 2, chips)),
            dma((3, 3)), dma((3, 3)),
            dma((3,)),
        ],
        compiler_params=pltpu.CompilerParams(
            collective_id=0, has_side_effects=True, vmem_limit_bytes=56 * 2**20
        ),
        cost_estimate=pl.CostEstimate(
            flops=flops, bytes_accessed=2 * 9 * ch * ch * 2, transcendentals=0
        ),
    )(
        images.reshape(batches, pictures, strip, ch),
        cotangent.reshape(batches, pictures, strip, ch),
        conv_weights.reshape(9, ch, ch),
        gains,
        shifts,
        switches.reshape(-1, switches.shape[-1]),
    )
    results = (outs, grads_in, weight_grad, gain_sum, shift_sum)
    outs, grads_in, weight_grad, gain_sum, shift_sum = pl.pallas_call(
        settle,
        out_shape=tuple(jax.ShapeDtypeStruct(r.shape, r.dtype) for r in results),
        in_specs=[anywhere] * 5,
        out_specs=(anywhere,) * 5,
        scratch_shapes=[pltpu.VMEM(r.shape, r.dtype) for r in results] + [dma((2 * batches + 5,))] * 2,
        compiler_params=pltpu.CompilerParams(vmem_limit_bytes=60 * 2**20),
    )(*results)
    shape = (1, batches, pictures, strip_rows, cols, ch)
    return (outs.reshape(shape), grads_in.reshape(shape), weight_grad[None], gain_sum, shift_sum)


def solution(mesh):
    return jax.shard_map(
        body,
        mesh=mesh,
        in_specs=(
            P(None, None, "rows", None, None),
            P(None, None, "rows", None),
            P("section", None, None, None, None),
            P("section", None),
            P("section", None),
            P(None, None, "rows", None, None),
        ),
        out_specs=(
            P("section", None, None, "rows", None, None),
            P("section", None, None, "rows", None, None),
            P("section", None, None, "rows", None),
            P("section", None),
            P("section", None),
        ),
        check_vma=False,
    )
```

```python
import functools

import jax
import jax.numpy as jnp
from jax import lax
from jax.experimental import pallas as pl
from jax.experimental.pallas import tpu as pltpu
from jax.sharding import PartitionSpec as P

EPSILON = 1e-05
MESH = pl.DeviceIdType.MESH
BF16 = jnp.bfloat16
F32 = jnp.float32


def kernel(
    sections, strips, cols,
    images, cotangent, weights, gains, shifts, switches,
    outs, grads_in, own_part, other_parts, gain_sum, shift_sum,
    w_v, wt_v, inp, mask_own, mask_v, gain_prev, shift_prev, zin, zin_stat, zown, own_stat, ub, slope_prev,
    prev_coef, own_coef, dyin, dy_stat, dzb, dyout, product_v, sums_v, stat_out, sums_out, seed_sums, out_v, gin_v,
    ut_own, ut_all, dz_all, dz_taps, acc_v, swap_out,
    w_sem, wt_sem, in_sem, pi_s, pi_r, ie_s, ie_r, mp_s, mp_r, me_s, me_r, gp_s, gp_r,
    ux_s, ux_r, dx_s, dx_r, sv_s, sv_r,
    fz_s, fz_r, fs_s, fs_r, oe_s, oe_r, os_s, os_r, bz_s, bz_r, bs_s, bs_r, ls_s,
    out_sem, po_s, po_r, gin_sem, pg_s, pg_r,
    ut_s, ut_r, uw_s, uf_s, uf_r, dz_s, dz_r, sw_s, sw_r, dw_sem,
):
    sec = lax.axis_index("section")
    row = lax.axis_index("rows")
    batches, _, tall, half = inp.shape
    ch = 2 * half
    px = tall - 2 * cols
    strip = px // 2
    groups = tall // cols
    chips = strips // 2
    local = float(px)
    total = 2.0 * local * chips
    first, last, decoder = sec == 0, sec == sections - 1, sec == sections // 2
    late = sec >= sections // 2
    core = row % 2
    partner = row + 1 - 2 * core
    has_up, has_down = row >= 2, row < strips - 2
    centre = pl.ds(cols, px)
    chip = row // 2
    team, seat = row // 4, row % 4
    lanes = dz_all.shape[3]
    block = ut_all.shape[3]
    share = block // 4
    mine = pl.multiple_of(cols + strip * core, cols)

    def channels(h):
        return pl.ds(pl.multiple_of(h * half, half), half)

    def w_copies():
        return [
            pltpu.make_async_copy(weights.at[:, channels(h), channels(core)], w_v.at[h], w_sem.at[h]) for h in range(2)
        ]

    def wt_copies():
        return [
            pltpu.make_async_copy(weights.at[:, channels(core), channels(h)], wt_v.at[h], wt_sem.at[h]) for h in range(2)
        ]

    def in_copy(src, m):
        return pltpu.make_async_copy(src.at[m, :, :, channels(core)], inp.at[m, :, pl.ds(mine, strip), :], in_sem.at[m])

    for copy in w_copies() + wt_copies():
        copy.start()

    @pl.when(first)
    def _():
        for m in range(batches):
            in_copy(images, m).start()

    @pl.when(last)
    def _():
        for m in range(batches):
            in_copy(cotangent, m).start()

    barrier = pltpu.get_barrier_semaphore()
    for s in range(sections):
        @pl.when((sec >= s - 1) & (sec <= s + 1))
        def _():
            def greet(i, carry):
                @pl.when((s != sec) | (i != row))
                def _():
                    pl.semaphore_signal(barrier, inc=1, device_id=(jnp.int32(s), i), device_id_type=MESH)
                return carry
            lax.fori_loop(0, strips, greet, 0)

    acc_v[...] = jnp.zeros_like(acc_v)
    sums_v[...] = jnp.zeros_like(sums_v)

    for m in range(batches):
        for i in range(2):
            for at in (0, dz_all.shape[2] - cols):
                dz_all[m, i, pl.ds(at, cols), :] = jnp.zeros((cols, lanes), BF16)

    @pl.when(decoder)
    def _():
        wide = cols // 2
        windows_at = lax.broadcasted_iota(jnp.int32, (cols, wide), 1)
        places = lax.broadcasted_iota(jnp.int32, (cols, wide), 0)
        pick = (lax.shift_right_logical(places, 1) == windows_at).astype(F32)
        table = lax.dot_general(
            pick, switches[...].astype(F32), (((1,), (1,)), ((), ())), preferred_element_type=F32
        )
        odd = jnp.bitwise_and(lax.broadcasted_iota(jnp.int32, (cols, 128), 0), 1).astype(F32)
        windows = strip // cols // 2
        for m in range(batches):
            for i in range(2):
                for w in range(windows):
                    at = (m * 2 + i) * windows + w
                    value = jnp.broadcast_to(table[:, at : at + 1], (cols, 128))
                    for p in range(2):
                        hit = (jnp.abs(value - (2.0 * p + odd)) < 0.5).astype(F32).astype(BF16)
                        mask_own[m, i, pl.ds((2 * w + p) * cols, cols), :] = hit
        for m in range(batches):
            mask_v[m, :, pl.ds(mine, strip), :] = mask_own[m]

    @pl.when(jnp.logical_not(decoder))
    def _():
        mask_v[...] = jnp.ones_like(mask_v)

    near = 1 + jnp.where(sec > 0, 1, 0) + jnp.where(sec < sections - 1, 1, 0)
    pl.semaphore_wait(barrier, near * strips - 1)

    def remote(src, dst, send, recv, s, i):
        return pltpu.make_async_remote_copy(
            src_ref=src, dst_ref=dst, send_sem=send, recv_sem=recv, device_id=(s, i), device_id_type=MESH
        )

    def to_partner(src_at, dst_at, send, recv):
        return remote(src_at(1 - core), dst_at(pl.ds(mine, strip)), send, recv, sec, partner)

    def start_argument(src_at, dst_at, pair_sems, edge_sems):
        to_partner(src_at, dst_at, *pair_sems).start()

        @pl.when((core == 1) & has_down)
        def _():
            for i in range(2):
                remote(
                    src_at(i, pl.ds(strip - cols, cols)), dst_at(pl.ds(0, cols)),
                    edge_sems[0].at[i], edge_sems[1].at[0], sec, row + 1 + i,
                ).start()

        @pl.when((core == 0) & has_up)
        def _():
            for i in range(2):
                remote(
                    src_at(i, pl.ds(0, cols)), dst_at(pl.ds(cols + px, cols)),
                    edge_sems[0].at[i], edge_sems[1].at[1], sec, row - 2 + i,
                ).start()

    def argument_arrived(src_at, dst_at, pair_sems, edge_sems):
        to_partner(src_at, dst_at, *pair_sems).wait_recv()

        @pl.when(has_up)
        def _():
            remote(
                src_at(0, pl.ds(0, cols)), dst_at(pl.ds(0, cols)), edge_sems[0].at[0], edge_sems[1].at[0], sec, row
            ).wait_recv()

        @pl.when(has_down)
        def _():
            remote(
                src_at(0, pl.ds(0, cols)), dst_at(pl.ds(cols + px, cols)), edge_sems[0].at[0], edge_sems[1].at[1],
                sec, row,
            ).wait_recv()

    def argument_sent(src_at, dst_at, pair_sems, edge_sems):
        to_partner(src_at, dst_at, *pair_sems).wait_send()

        @pl.when(((core == 1) & has_down) | ((core == 0) & has_up))
        def _():
            for i in range(2):
                remote(
                    src_at(i, pl.ds(0, cols)), dst_at(pl.ds(0, cols)), edge_sems[0].at[i], edge_sems[1].at[0], sec, row
                ).wait_send()

    def input_parts(src, m):
        return (
            lambda i, r=pl.ds(0, strip): src.at[m, :, r, channels(i)],
            lambda r: inp.at[m, :, r, :],
            (pi_s.at[m], pi_r.at[m]),
            (ie_s.at[m], ie_r.at[m]),
        )

    mask_parts = (
        lambda i, r=pl.ds(0, strip): mask_own.at[:, :, r, :],
        lambda r: mask_v.at[:, :, r, :],
        (mp_s, mp_r),
        (me_s, me_r),
    )

    @pl.when(first)
    def _():
        for m in range(batches):
            start_argument(*input_parts(images, m))

    @pl.when(last)
    def _():
        for m in range(batches):
            start_argument(*input_parts(cotangent, m))

    @pl.when(decoder)
    def _():
        start_argument(*mask_parts)

    def affine_sends():
        return (
            remote(gains, gain_prev, gp_s.at[0], gp_r.at[0], sec + 1, row),
            remote(shifts, shift_prev, gp_s.at[1], gp_r.at[1], sec + 1, row),
        )

    @pl.when(sec < sections - 1)
    def _():
        for copy in affine_sends():
            copy.start()

    def block_sends(src, src_from, dst, send, recv, m, s):
        def piece(k, src_row, dst_row, rows, to):
            def one(i):
                return remote(
                    src.at[m, i, pl.ds(src_from + src_row, rows), :], dst.at[m, i, pl.ds(dst_row, rows), :],
                    send.at[m, k, i], recv.at[m, k, i], s, to,
                )
            return one

        return (
            piece(0, 0, cols, px, row), piece(1, px - cols, 0, cols, row + 2), piece(2, 0, cols + px, cols, row - 2)
        )

    def each_edge(parts, i, act):
        _, to_down, to_up = parts

        @pl.when(has_down)
        def _():
            act(to_down(i))

        @pl.when(has_up)
        def _():
            act(to_up(i))

    def edges_arrived(parts, i):
        _, to_down, to_up = parts

        @pl.when(has_up)
        def _():
            to_down(i).wait_recv()

        @pl.when(has_down)
        def _():
            to_up(i).wait_recv()

    def send_block(parts, i):
        each_edge(parts, i, start)
        parts[0](i).start()

    def block_sent(parts):
        for i in range(2):
            each_edge(parts, i, sent)
            parts[0](i).wait_send()

    def start(copy):
        copy.start()

    def sent(copy):
        copy.wait_send()

    def came(copy):
        copy.wait_recv()

    def z_sends(m, s):
        return block_sends(zown, cols, zin, fz_s, fz_r, m, s)

    def own_edges(m):
        return block_sends(zown, cols, zown, oe_s, oe_r, m, sec)

    def dy_sends(m, s):
        return block_sends(dyout, 0, dyin, bz_s, bz_r, m, s)

    def stats_each(src, dst, send, recv, m, s, same, act):
        def one(d, carry):
            q = chip + d
            q = jnp.where(q >= chips, q - chips, q)
            act(remote(src.at[m], dst.at[m, chip], send.at[m, d], recv.at[m, d], s, 2 * q + core))
            return carry
        lax.fori_loop(1 if same else 0, chips, one, 0)

    def start_stats(src, dst, send, recv, m, s, same):
        stats_each(src, dst, send, recv, m, s, same, start)
        if same:
            dst[m, chip] = src[m]

    def wait_stats(src, dst, send, recv, m, same):
        stats_each(src, dst, send, recv, m, sec, same, came)

    down_stats = (stat_out, zin_stat, fs_s, fs_r)
    same_stats = (stat_out, own_stat, os_s, os_r)
    back_stats = (sums_out, dy_stat, bs_s, bs_r)
    seed_stats = (seed_sums, dy_stat, ls_s, bs_r)

    def join(stats_ref, m):
        means = stats_ref[m, :, 0, :], stats_ref[m, :, 1, :]
        mean = jnp.sum(means[0] + means[1], 0, keepdims=True) / (2.0 * chips)
        off = [part - mean for part in means]
        squares = jnp.sum(stats_ref[m, :, 2, :] + stats_ref[m, :, 3, :], 0, keepdims=True)
        apart = jnp.sum(off[0] * off[0] + off[1] * off[1], 0, keepdims=True)
        at = (jnp.maximum(chip - 1, 0), chip, jnp.minimum(chip + 1, chips - 1))
        offs = [[stats_ref[m, q, pl.ds(i, 1), :] - mean for q in at] for i in range(2)]
        return lax.rsqrt((squares + local * apart) / total + EPSILON), offs

    def kind(g):
        return 0 if g == 0 else 2 if g == groups - 1 else 1

    def inside(g, values):
        if kind(g) == 1:
            return values
        return jnp.where(has_up if kind(g) == 0 else has_down, values, jnp.zeros_like(values))

    def group(g):
        return pl.ds(g * cols, cols)

    column = lax.broadcasted_iota(jnp.int32, (1, cols, half), 1)

    def taps_joined(parts, left, right):
        rows = parts[0].shape[0]

        def moved(values, by, edge):
            turned = pltpu.roll(values, by % rows, 0).reshape(rows // cols, cols, half)
            return jnp.where(column == edge, 0.0, turned).reshape(rows, half)
        return parts[1] + moved(parts[left], 1, 0) + moved(parts[right], -1, cols - 1)

    def pass_on(operand, send, recv, m, i):
        return remote(operand.at[m, core, i], operand.at[m, core, i], send.at[m, i], recv.at[m, i], sec, partner)

    def products(operand, w, m, h, r_at, images_at):
        rows = images_at.size * px

        def one(c):
            acc = jnp.zeros((rows, half), F32)
            for r in range(3):
                left = operand[m, h, images_at, pl.ds(r_at(r) * cols, px), :].reshape(rows, half)
                acc += jnp.dot(left, w[h, 3 * r + c], preferred_element_type=F32)
            return acc
        return one

    def convolve(operand, w, send, recv, m, r_at, left, right, prepare, use, after=lambda i: None):
        def part(images_at, wait_for):
            rows = pl.ds(0, images_at.size * px)
            mine_first = products(operand, w, m, core, r_at, images_at)
            for c in range(3):
                product_v[c, rows, :] = mine_first(c)
            for i in wait_for:
                pass_on(operand, send, recv, m, i).wait_recv()
            then = products(operand, w, m, 1 - core, r_at, images_at)
            return taps_joined([product_v[c, rows, :] + then(c) for c in range(3)], left, right)

        def ready(i):
            prepare(i)
            pass_on(operand, send, recv, m, i).start()
            after(i)

        def together():
            for i in range(2):
                ready(i)
            whole = part(pl.ds(0, 2), range(2))
            for i in range(2):
                use(i, whole[i * px : (i + 1) * px])

        def apart():
            for i in range(2):
                ready(i)
                use(i, part(pl.ds(i, 1), [i]))

        return together, apart

    def turned_copy(m, q):
        src = ut_own.at[m, pl.ds(pl.multiple_of((q // 2) * block, block), block), :]
        return src, ut_all.at[m, core, chip]


    def turned_each(m, act):
        def one(d, carry):
            q = chip + d
            q = jnp.where(q >= chips, q - chips, q)
            its_team = q // 2
            nearest = 2 * its_team + jnp.where(chip > q, 1, 0)

            @pl.when((its_team == team) | (q == nearest))
            def _():
                src, dst = turned_copy(m, q)
                act(remote(src, dst, ut_s.at[m, d], ut_r.at[m, d], sec, 2 * q + core))
            return carry
        lax.fori_loop(1, chips, one, 0)

    def entry_for(p):
        return (p // 2 != team) & (jnp.where(p > chip, 1, 0) == chip % 2)

    def turned_arrived(m):
        def one(d, carry):
            p = chip - d
            p = jnp.where(p < 0, p + chips, p)

            @pl.when(jnp.logical_not(entry_for(p)))
            def _():
                piece = ut_all.at[m, core, p]
                remote(piece, piece, ut_s.at[m, d], ut_r.at[m, d], sec, row).wait_recv()
            return carry
        lax.fori_loop(1, chips, one, 0)

    def turned_onward(m, act, arrive):
        other = chip + 1 - 2 * (chip % 2)

        def one(d, carry):
            p = chip - d
            p = jnp.where(p < 0, p + chips, p)

            @pl.when(entry_for(p))
            def _():
                piece = ut_all.at[m, core, p]
                if arrive:
                    remote(piece, piece, ut_s.at[m, d], ut_r.at[m, d], sec, row).wait_recv()
                there = other - p
                there = jnp.where(there < 0, there + chips, there)
                act(remote(piece, piece, uw_s.at[m, d], ut_r.at[m, there], sec, 2 * other + core))

            return carry
        lax.fori_loop(1, chips, one, 0)

    def turn_inputs(m):
        for h in range(2):
            ut_own[m, pl.ds(h * half, half), :] = ub[m, h, core, centre, :].T
        mine_at = pl.ds(pl.multiple_of(team * block, block), block)
        ut_all[m, core, chip] = ut_own[m, mine_at, :]

    def send_turned(m):
        turn_inputs(m)
        turned_each(m, start)

    def turned_relay(m):
        return remote(ut_all.at[m, core], ut_all.at[m, core], uf_s.at[m], uf_r.at[m], sec, partner)

    def relay_turned(m):
        turned_arrived(m)
        turned_relay(m).start()

    def pass_on_from(begin):
        def one(m, carry):
            turned_onward(m, start, True)
            return carry
        lax.fori_loop(begin, batches, one, 0)

    def relay_all():
        def one(m, carry):
            relay_turned(m)
            return carry
        lax.fori_loop(0, batches, one, 0)

    def dz_piece(m, i, k):
        src = dzb.at[m, core, i, centre, pl.ds(pl.multiple_of(k * lanes, lanes), lanes)]
        return src, dz_all.at[m, i, pl.ds(pl.multiple_of(cols + chip * px, cols), px), :]

    def dz_each(m, i, act):
        def one(e, carry):
            q = team + e
            q = 2 * jnp.where(q >= chips // 2, q - chips // 2, q) + core
            for k in range(2):
                @pl.when((q != chip) | (k != core))
                def _():
                    src, dst = dz_piece(m, i, k)
                    act(remote(src, dst, dz_s.at[m, i, 2 * e + k], dz_r.at[m, i, chip], sec, 2 * q + k))
            return carry
        lax.fori_loop(0, chips // 2, one, 0)

    def send_dz(m, i):
        dz_each(m, i, start)

        @pl.when(chip % 2 == core)
        def _():
            dz_all[m, i, pl.ds(pl.multiple_of(cols + chip * px, cols), px), :] = dzb[
                m, core, i, centre, pl.ds(pl.multiple_of(core * lanes, lanes), lanes)
            ]

    def dz_arrived(m):
        for i in range(2):
            def one(p, carry):
                @pl.when((p != chip) | (chip % 2 != core))
                def _():
                    piece = dz_all.at[m, i, pl.ds(cols, px), :]
                    remote(piece, piece, dz_s.at[m, i, 0], dz_r.at[m, i, p], sec, row).wait_recv()
                return carry
            lax.fori_loop(0, chips, one, 0)

    def gather_taps(m):
        dz_arrived(m)
        relayed = ut_all.at[m, 1 - core]
        pltpu.make_async_copy(relayed, relayed, uf_r.at[m]).wait()
        rows = dz_all.shape[2]
        edge = lax.broadcasted_iota(jnp.int32, (1, cols, lanes), 1)
        for i in range(2):
            values = dz_all[m, i].astype(F32)
            for c, by, gone in ((0, rows - 1, cols - 1), (2, 1, 0)):
                turned = pltpu.roll(values, by, 0).reshape(rows // cols, cols, lanes)
                turned = jnp.where(edge == gone, 0.0, turned).reshape(rows, lanes)
                dz_taps[i, :, pl.ds(c * lanes, lanes)] = turned.astype(BF16)
            dz_taps[i, :, pl.ds(lanes, lanes)] = dz_all[m, i]

    def kernel_row(m, r):
        part = jnp.zeros((block, 3 * lanes), F32)
        for i in range(2):
            left = jnp.concatenate([ut_all[m, i, q] for q in range(chips)], axis=1)
            part += jnp.dot(
                left, dz_taps[i, pl.ds((2 - r) * cols, px * (strips // 2)), :], preferred_element_type=F32
            )
        return part

    def add_gradients(m):
        gather_taps(m)
        for r in range(3):
            acc_v[r] = acc_v[r] + kernel_row(m, r)

    def forward(m):
        def prepare_first(i):
            for g in range(groups):
                ub[m, core, i, group(g), :] = inside(g, inp[m, i, group(g), :])

        def prepare_later(i):
            sends = z_sends(m, sec)
            inv = prev_coef[m, pl.ds(0, 1), :]
            slant = 0.5 * inv * gain_prev[:, channels(core)]
            shift = 0.5 * shift_prev[:, channels(core)]
            level = [slant * prev_coef[m, pl.ds(1 + 3 * i + e, 1), :] + shift for e in range(3)]
            edges_arrived(sends, i)
            sends[0](i).wait_recv()
            for g in range(groups):
                gate = jnp.concatenate([mask_v[m, i, group(g), :].astype(F32)] * (half // 128), axis=1)
                halved = zin[m, i, group(g), :].astype(F32) * slant + level[kind(g)]
                turn = jnp.tanh(halved)
                bent = halved * turn
                ub[m, core, i, group(g), :] = inside(g, ((halved + bent) * gate).astype(BF16))
                if kind(g) == 1:
                    slope_prev[m, i, pl.ds((g - 1) * cols, cols), :] = (0.5 + 0.5 * turn) * (1.0 + halved - bent)

        def prepare(i):
            @pl.when(first)
            def _():
                prepare_first(i)

            @pl.when(sec > 0)
            def _():
                prepare_later(i)

        def use(i, conv):
            mean = jnp.sum(conv, 0, keepdims=True) / local
            conv = conv - mean
            stat_out[m, pl.ds(i, 1), :] = mean
            stat_out[m, pl.ds(2 + i, 1), :] = jnp.sum(conv * conv, 0, keepdims=True)
            zown[m, i, centre, :] = conv.astype(BF16)

            @pl.when(sec < sections - 1)
            def _():
                if i == 1:
                    start_stats(*down_stats, m, sec + 1, False)
                send_block(z_sends(m, sec + 1), i)

        @pl.when(first)
        def _():
            in_copy(images, m).wait()
            argument_arrived(*input_parts(images, m))

        @pl.when(sec > 0)
        def _():
            @pl.when(m == 0)
            def _():
                for copy in affine_sends():
                    copy.wait_recv()

                @pl.when(decoder)
                def _():
                    argument_arrived(*mask_parts)

            wait_stats(*down_stats, m, False)
            inv, offs = join(zin_stat, m)
            for e, value in enumerate((inv, *offs[0], *offs[1])):
                prev_coef[m, pl.ds(e, 1), :] = value

        @pl.when(m == 0)
        def _():
            for copy in w_copies():
                copy.wait()

        together, apart = convolve(ub, w_v, ux_s, ux_r, m, lambda r: r, 0, 2, prepare, use)

        @pl.when(last)
        def _():
            together()

        @pl.when(jnp.logical_not(last))
        def _():
            apart()

        start_stats(*same_stats, m, sec, True)
        for i in range(2):
            each_edge(own_edges(m), i, start)

    def finish(m):
        wait_stats(*same_stats, m, True)
        inv, offs = join(own_stat, m)
        scale = inv * gains[:, channels(core)]
        for e, value in enumerate((inv, scale, *offs[0], *offs[1])):
            own_coef[m, pl.ds(e, 1), :] = value
        slant = 0.5 * scale
        shift = 0.5 * shifts[:, channels(core)]
        level = [[slant * off + shift for off in part] for part in offs]
        for i in range(2):
            edges_arrived(own_edges(m), i)

        @pl.when(last)
        def _():
            in_copy(cotangent, m).wait()
            argument_arrived(*input_parts(cotangent, m))
            ones, crosses = [], []
            for i in range(2):
                sums = jnp.zeros((cols, half), F32)
                cross = jnp.zeros((cols, half), F32)
                for g in range(groups):
                    z = zown[m, i, group(g), :].astype(F32)
                    halved = z * slant + level[i][kind(g)]
                    turn = jnp.tanh(halved)
                    bent = halved * turn
                    dy = inp[m, i, group(g), :].astype(F32) * ((0.5 + 0.5 * turn) * (1.0 + halved - bent))
                    dyin[m, i, group(g), :] = dy.astype(BF16)
                    if kind(g) == 1:
                        out_v[m, i, pl.ds((g - 1) * cols, cols), :] = (halved + bent).astype(BF16)
                        sums += dy
                        cross += dy * z
                one = jnp.sum(sums, 0, keepdims=True)
                ones.append(one)
                crosses.append(jnp.sum(cross, 0, keepdims=True) + offs[i][1] * one)
            seed_sums[m, pl.ds(0, 1), :] = ones[0] + ones[1]
            seed_sums[m, pl.ds(1, 1), :] = inv * (crosses[0] + crosses[1])
            start_stats(*seed_stats, m, sec, True)

        @pl.when(jnp.logical_not(last))
        def _():
            for i in range(2):
                for g in range(1, groups - 1):
                    halved = zown[m, i, group(g), :].astype(F32) * slant + level[i][1]
                    out_v[m, i, pl.ds((g - 1) * cols, cols), :] = (halved + halved * jnp.tanh(halved)).astype(BF16)

        for copy in result_copies(out_v, outs, out_sem, po_s, po_r, m):
            copy.start()

    def result_copies(src, dst, sem, send, recv, m):
        here, there = pl.multiple_of(strip * core, cols), pl.multiple_of(strip * (1 - core), cols)
        place = dst.at[m, :, :, channels(core)]
        return (
            pltpu.make_async_copy(src.at[m, :, pl.ds(here, strip), :], place, sem.at[m]),
            remote(src.at[m, :, pl.ds(there, strip), :], place, send.at[m], recv.at[m], sec, partner),
        )

    def backward(m):
        @pl.when(last)
        def _():
            wait_stats(*seed_stats, m, True)

        @pl.when(jnp.logical_not(last))
        def _():
            wait_stats(*back_stats, m, False)

        first_sum = jnp.sum(dy_stat[m, :, 0, :], 0, keepdims=True)
        cross_sum = jnp.sum(dy_stat[m, :, 1, :], 0, keepdims=True)
        sums_v[core, pl.ds(0, 1), :] = sums_v[core, pl.ds(0, 1), :] + first_sum
        sums_v[core, pl.ds(1, 1), :] = sums_v[core, pl.ds(1, 1), :] + cross_sum

        def prepare(i):
            inv = own_coef[m, pl.ds(0, 1), :]
            scale = own_coef[m, pl.ds(1, 1), :]
            tilt = scale * inv * (cross_sum / total)
            base = [scale * (first_sum / total) + tilt * own_coef[m, pl.ds(2 + 3 * i + e, 1), :] for e in range(3)]
            sends = dy_sends(m, sec)

            @pl.when(jnp.logical_not(last))
            def _():
                edges_arrived(sends, i)
                sends[0](i).wait_recv()

            for g in range(groups):
                dz = dyin[m, i, group(g), :].astype(F32) * scale
                dz = dz - zown[m, i, group(g), :].astype(F32) * tilt - base[kind(g)]
                dzb[m, core, i, group(g), :] = inside(g, dz.astype(BF16))

        def then(i):
            @pl.when(first)
            def _():
                send_dz(m, i)

        def use(i, conv):
            gate = jnp.concatenate([mask_v[m, i, centre, :].astype(F32)] * (half // 128), axis=1)
            du = (conv * gate).astype(BF16)
            gin_v[m, i] = du

            @pl.when(sec > 0)
            def _():
                dy = du.astype(F32) * slope_prev[m, i]
                dyout[m, i] = dy.astype(BF16)
                one = jnp.sum(dy, 0, keepdims=True)
                cross = jnp.sum(dy * zin[m, i, centre, :].astype(F32), 0, keepdims=True)
                cross = prev_coef[m, pl.ds(0, 1), :] * (cross + prev_coef[m, pl.ds(2 + 3 * i, 1), :] * one)
                if i == 1:
                    one = one + sums_out[m, pl.ds(0, 1), :]
                    cross = cross + sums_out[m, pl.ds(1, 1), :]
                sums_out[m, pl.ds(0, 1), :] = one
                sums_out[m, pl.ds(1, 1), :] = cross
                if i == 1:
                    start_stats(*back_stats, m, sec - 1, False)
                send_block(dy_sends(m, sec - 1), i)

        together, apart = convolve(dzb, wt_v, dx_s, dx_r, m, lambda r: 2 - r, 2, 0, prepare, use, then)

        whole = first | (last & (m < batches - 1))

        @pl.when(whole)
        def _():
            together()

        @pl.when(jnp.logical_not(whole))
        def _():
            apart()

        for copy in result_copies(gin_v, grads_in, gin_sem, pg_s, pg_r, m):
            copy.start()

        @pl.when(((sec > 0) & (sec < sections - 1)) | (last & (m == 0)))
        def _():
            for i in range(2):
                send_dz(m, i)

    def turn_weights():
        for copy in wt_copies():
            copy.wait()

        def one(i, carry):
            for h in range(2):
                wt_v[h, i] = wt_v[h, i].T
            return carry
        lax.fori_loop(0, 9, one, 0)

    @pl.when(late)
    def _():
        turn_weights()

    def step(t, carry):
        ahead = t - sec
        behind = t - (2 * sections - 1 - sec)

        @pl.when((ahead >= 0) & (ahead < batches))
        def _():
            forward(ahead)

        @pl.when(late & (ahead >= 0) & (ahead < batches))
        def _():
            send_turned(ahead)

        @pl.when(jnp.logical_not(late) & (ahead == batches))
        def _():
            def turned(m, carry):
                send_turned(m)
                return carry
            lax.fori_loop(0, batches, turned, 0)
            turn_weights()

        @pl.when(jnp.logical_not(late) & (ahead == batches + 1))
        def _():
            pass_on_from(0)

        @pl.when(first & (ahead == batches + 2))
        def _():
            relay_all()

        done = ahead - jnp.where(last, 0, 1)

        @pl.when((behind >= 0) & (behind < batches))
        def _():
            backward(behind)

        @pl.when((done >= 0) & (done < batches))
        def _():
            finish(done)

        @pl.when(late & (ahead >= 1) & (ahead <= jnp.where(last, batches, batches // 2)))
        def _():
            turned_onward(ahead - 1, start, True)

        return carry

    lax.fori_loop(0, 2 * sections - 1 + batches, step, 0)

    remote(sums_v.at[core], sums_v.at[core], sv_s, sv_r, sec, partner).start()

    @pl.when(last)
    def _():
        def send(m, carry):
            for i in range(2):
                send_dz(m, i)
            return carry

        lax.fori_loop(1, batches, send, 0)

    @pl.when(late & jnp.logical_not(last))
    def _():
        pass_on_from(batches // 2)

    @pl.when(jnp.logical_not(first))
    def _():
        relay_all()

    def add(m, carry):
        add_gradients(m)
        return carry

    lax.fori_loop(0, batches - 1, add, 0)

    def swap(r, d):
        other = (seat + d) % 4
        return remote(
            swap_out.at[r, pl.ds(pl.multiple_of(other * share, share), share), :], other_parts.at[4 - d - 1, r],
            sw_s.at[r, d - 1], sw_r.at[r, 4 - d - 1], sec, 4 * team + other,
        )

    def own_copy(r):
        return pltpu.make_async_copy(
            acc_v.at[r, pl.ds(pl.multiple_of(seat * share, share), share), :], own_part.at[r], dw_sem.at[r]
        )

    gather_taps(batches - 1)
    for r in range(3):
        part = acc_v[r] + kernel_row(batches - 1, r)
        acc_v[r] = part
        swap_out[r] = part.astype(BF16)
        for d in range(1, 4):
            swap(r, d).start()
        own_copy(r).start()

    for r in range(3):
        own_copy(r).wait()
        for d in range(1, 4):
            swap(r, d).wait_send()
            swap(r, d).wait_recv()

    @pl.when(decoder)
    def _():
        argument_sent(*mask_parts)

    @pl.when(sec < sections - 1)
    def _():
        for copy in affine_sends():
            copy.wait_send()

    def sums_copy():
        return remote(sums_v.at[core], sums_v.at[core], sv_s, sv_r, sec, partner)

    sums_copy().wait_recv()
    sums_copy().wait_send()
    for h in range(2):
        shift_sum[:, pl.ds(h * half, half)] = sums_v[h, pl.ds(0, 1), :]
        gain_sum[:, pl.ds(h * half, half)] = sums_v[h, pl.ds(1, 1), :]

    def drain(m, carry):
        for src, dst, sems in ((out_v, outs, (out_sem, po_s, po_r)), (gin_v, grads_in, (gin_sem, pg_s, pg_r))):
            here, there = result_copies(src, dst, *sems, m)
            here.wait()
            there.wait_send()
            remote(
                src.at[m, :, pl.ds(0, strip), :], dst.at[m, :, :, channels(1 - core)], sems[1].at[m], sems[2].at[m],
                sec, partner,
            ).wait_recv()

        turned_each(m, sent)
        turned_onward(m, sent, False)
        turned_relay(m).wait_send()
        for i in range(2):
            dz_each(m, i, sent)
        for i in range(2):
            pass_on(ub, ux_s, ux_r, m, i).wait_send()
            pass_on(dzb, dx_s, dx_r, m, i).wait_send()

        @pl.when(first)
        def _():
            argument_sent(*input_parts(images, m))

        @pl.when(last)
        def _():
            argument_sent(*input_parts(cotangent, m))
            stats_each(*seed_stats, m, sec, True, sent)

        @pl.when(sec < sections - 1)
        def _():
            stats_each(*down_stats, m, sec + 1, False, sent)
            block_sent(z_sends(m, sec + 1))

        stats_each(*same_stats, m, sec, True, sent)
        for i in range(2):
            each_edge(own_edges(m), i, sent)

        @pl.when(sec > 0)
        def _():
            stats_each(*back_stats, m, sec - 1, False, sent)
            block_sent(dy_sends(m, sec - 1))

        return carry

    lax.fori_loop(0, batches, drain, 0)


def settle(outs, grads_in, gain_sum, shift_sum, own, others, *refs):
    targets, stages, (own_v, others_v, whole, in_sem, out_sem) = refs[:5], refs[5:9], refs[9:]
    moves = []
    for src, dst, stage in zip((outs, grads_in, gain_sum, shift_sum), targets[:4], stages):
        if len(src.shape) == 2:
            moves.append((src, dst, stage))
        else:
            moves += [(src.at[i], dst.at[i], stage.at[i]) for i in range(src.shape[0])]
    count = len(moves)
    parts = [pltpu.make_async_copy(own, own_v, in_sem.at[count])]
    parts += [pltpu.make_async_copy(others.at[d], others_v.at[d], in_sem.at[count + 1 + d]) for d in range(3)]
    ins = [pltpu.make_async_copy(src, stage, in_sem.at[i]) for i, (src, dst, stage) in enumerate(moves)]
    outs = [pltpu.make_async_copy(stage, dst, out_sem.at[i]) for i, (src, dst, stage) in enumerate(moves)]
    rows = [pltpu.make_async_copy(whole.at[r], targets[4].at[r], out_sem.at[count + r]) for r in range(3)]
    for copy in parts + ins:
        copy.start()
    for copy in parts:
        copy.wait()
    seat = lax.axis_index("rows") % 4
    lanes = whole.shape[3] // 4
    for r in range(3):
        for d in range(4):
            at = pl.ds(pl.multiple_of(((seat + d) % 4) * lanes, lanes), lanes)
            for c in range(3):
                part = pl.ds(c * lanes, lanes)
                whole[r, c, :, at] = own_v[r, :, part] if d == 0 else others_v[d - 1, r, :, part].astype(F32)
        rows[r].start()
    for come, go in zip(ins, outs):
        come.wait()
        go.start()
    for copy in outs + rows:
        copy.wait()


def body(images, switches, conv_weights, gains, shifts, cotangent):
    sections = lax.axis_size("section")
    strips = lax.axis_size("rows")
    batches, pictures, strip_rows, cols, ch = images.shape
    strip = strip_rows * cols
    px = 2 * strip
    tall = px + 2 * cols
    anywhere = pl.BlockSpec(memory_space=pl.ANY)
    vmem = pl.BlockSpec(memory_space=pltpu.VMEM)
    dma = pltpu.SemaphoreType.DMA
    flops = 3 * 2 * 9 * ch * ch * batches * px
    share = ch // strips
    chips = strips // 2
    outs, grads_in, own, others, gain_sum, shift_sum = pl.pallas_call(
        functools.partial(kernel, sections, strips, cols),
        out_shape=(
            jax.ShapeDtypeStruct((batches, pictures, strip, ch), BF16),
            jax.ShapeDtypeStruct((batches, pictures, strip, ch), BF16),
            jax.ShapeDtypeStruct((3, share, 3 * ch // 4), F32),
            jax.ShapeDtypeStruct((3, 3, share, 3 * ch // 4), BF16),
            jax.ShapeDtypeStruct((1, ch), F32),
            jax.ShapeDtypeStruct((1, ch), F32),
        ),
        in_specs=[anywhere, anywhere, anywhere, vmem, vmem, vmem],
        out_specs=(anywhere,) * 4 + (vmem, vmem),
        scratch_shapes=[
            pltpu.VMEM((2, 9, ch // 2, ch // 2), BF16),
            pltpu.VMEM((2, 9, ch // 2, ch // 2), BF16),
            pltpu.VMEM((batches, 2, tall, ch // 2), BF16),
            pltpu.VMEM((batches, 2, strip, 128), BF16),
            pltpu.VMEM((batches, 2, tall, 128), BF16),
            pltpu.VMEM((1, ch), F32),
            pltpu.VMEM((1, ch), F32),
            pltpu.VMEM((batches, 2, tall, ch // 2), BF16),
            pltpu.VMEM((batches, chips, 4, ch // 2), F32),
            pltpu.VMEM((batches, 2, tall, ch // 2), BF16),
            pltpu.VMEM((batches, chips, 4, ch // 2), F32),
            pltpu.VMEM((batches, 2, 2, tall, ch // 2), BF16),
            pltpu.VMEM((batches, 2, px, ch // 2), F32),
            pltpu.VMEM((batches, 8, ch // 2), F32),
            pltpu.VMEM((batches, 8, ch // 2), F32),
            pltpu.VMEM((batches, 2, tall, ch // 2), BF16),
            pltpu.VMEM((batches, chips, 2, ch // 2), F32),
            pltpu.VMEM((batches, 2, 2, tall, ch // 2), BF16),
            pltpu.VMEM((batches, 2, px, ch // 2), BF16),
            pltpu.VMEM((3, 2 * px, ch // 2), F32),
            pltpu.VMEM((2, 2, ch // 2), F32),
            pltpu.VMEM((batches, 4, ch // 2), F32),
            pltpu.VMEM((batches, 2, ch // 2), F32),
            pltpu.VMEM((batches, 2, ch // 2), F32),
            pltpu.VMEM((batches, 2, px, ch // 2), BF16),
            pltpu.VMEM((batches, 2, px, ch // 2), BF16),
            pltpu.VMEM((batches, ch, px), BF16),
            pltpu.VMEM((batches, 2, strips // 2, 4 * share, px), BF16),
            pltpu.VMEM((batches, 2, px * strips // 2 + 2 * cols, ch // 4), BF16),
            pltpu.VMEM((2, px * strips // 2 + 2 * cols, 3 * ch // 4), BF16),
            pltpu.VMEM((3, 4 * share, 3 * ch // 4), F32),
            pltpu.VMEM((3, 4 * share, 3 * ch // 4), BF16),
            dma((2,)), dma((2,)),
            dma((batches,)),
            dma((batches,)), dma((batches,)),
            dma((batches, 2)), dma((batches, 2)),
            dma, dma,
            dma((2,)), dma((2,)),
            dma((2,)), dma((2,)),
            dma((batches, 2)), dma((batches, 2)),
            dma((batches, 2)), dma((batches, 2)),
            dma, dma,
            dma((batches, 3, 2)), dma((batches, 3, 2)),
            dma((batches, chips)), dma((batches, chips)),
            dma((batches, 3, 2)), dma((batches, 3, 2)),
            dma((batches, chips)), dma((batches, chips)),
            dma((batches, 3, 2)), dma((batches, 3, 2)),
            dma((batches, chips)), dma((batches, chips)),
            dma((batches, chips)),
            dma((batches,)), dma((batches,)), dma((batches,)),
            dma((batches,)), dma((batches,)), dma((batches,)),
            dma((batches, chips)), dma((batches, chips)), dma((batches, chips)),
            dma((batches,)), dma((batches,)),
            dma((batches, 2, chips)), dma((batches, 2, chips)),
            dma((3, 3)), dma((3, 3)),
            dma((3,)),
        ],
        compiler_params=pltpu.CompilerParams(
            collective_id=0, has_side_effects=True, vmem_limit_bytes=56 * 2**20
        ),
        cost_estimate=pl.CostEstimate(
            flops=flops, bytes_accessed=2 * 9 * ch * ch * 2, transcendentals=0
        ),
    )(
        images.reshape(batches, pictures, strip, ch),
        cotangent.reshape(batches, pictures, strip, ch),
        conv_weights.reshape(9, ch, ch),
        gains,
        shifts,
        switches.reshape(-1, switches.shape[-1]),
    )
    results = (outs, grads_in, gain_sum, shift_sum)
    whole = jax.ShapeDtypeStruct((3, 3, share, ch), F32)
    outs, grads_in, gain_sum, shift_sum, weight_grad = pl.pallas_call(
        settle,
        out_shape=tuple(jax.ShapeDtypeStruct(r.shape, r.dtype) for r in results) + (whole,),
        in_specs=[anywhere] * 6,
        out_specs=(anywhere,) * 5,
        scratch_shapes=[pltpu.VMEM(r.shape, r.dtype) for r in results]
        + [
            pltpu.VMEM(own.shape, F32),
            pltpu.VMEM(others.shape, BF16),
            pltpu.VMEM(whole.shape, F32),
            dma((2 * batches + 6,)),
            dma((2 * batches + 5,)),
        ],
        compiler_params=pltpu.CompilerParams(vmem_limit_bytes=60 * 2**20),
    )(*results, own, others)
    shape = (1, batches, pictures, strip_rows, cols, ch)
    return (outs.reshape(shape), grads_in.reshape(shape), weight_grad[None], gain_sum, shift_sum)


def solution(mesh):
    return jax.shard_map(
        body,
        mesh=mesh,
        in_specs=(
            P(None, None, "rows", None, None),
            P(None, None, "rows", None),
            P("section", None, None, None, None),
            P("section", None),
            P("section", None),
            P(None, None, "rows", None, None),
        ),
        out_specs=(
            P("section", None, None, "rows", None, None),
            P("section", None, None, "rows", None, None),
            P("section", None, None, "rows", None),
            P("section", None),
            P("section", None),
        ),
        check_vma=False,
    )
```

```python
import functools

import jax
import jax.numpy as jnp
from jax import lax
from jax.experimental import pallas as pl
from jax.experimental.pallas import tpu as pltpu
from jax.sharding import PartitionSpec as P

EPSILON = 1e-05
MESH = pl.DeviceIdType.MESH
BF16 = jnp.bfloat16
F32 = jnp.float32


def kernel(
    sections, strips, cols,
    images, cotangent, weights, gains, shifts, switches,
    outs, grads_in, own_part, other_parts, gain_sum, shift_sum,
    w_v, wt_v, inp, mask_own, mask_v, gain_prev, shift_prev, zin, zin_stat, zown, own_stat, ub, slope_prev,
    prev_coef, own_coef, dyin, dy_stat, dzb, dyout, product_v, sums_v, stat_out, sums_out, seed_sums, out_v, gin_v,
    ut_own, ut_all, dz_all, dz_taps, acc_v, swap_out,
    w_sem, wt_sem, in_sem, pi_s, pi_r, ie_s, ie_r, mp_s, mp_r, me_s, me_r, gp_s, gp_r,
    ux_s, ux_r, dx_s, dx_r, sv_s, sv_r,
    fz_s, fz_r, fs_s, fs_r, oe_s, oe_r, os_s, os_r, bz_s, bz_r, bs_s, bs_r, ls_s,
    out_sem, po_s, po_r, gin_sem, pg_s, pg_r,
    ut_s, ut_r, uw_s, uf_s, uf_r, dz_s, dz_r, sw_s, sw_r, dw_sem,
):
    sec = lax.axis_index("section")
    row = lax.axis_index("rows")
    batches, _, tall, half = inp.shape
    ch = 2 * half
    px = tall - 2 * cols
    strip = px // 2
    groups = tall // cols
    chips = strips // 2
    local = float(px)
    total = 2.0 * local * chips
    first, last, decoder = sec == 0, sec == sections - 1, sec == sections // 2
    late = sec >= sections // 2
    core = row % 2
    partner = row + 1 - 2 * core
    has_up, has_down = row >= 2, row < strips - 2
    centre = pl.ds(cols, px)
    chip = row // 2
    team, seat = row // 4, row % 4
    lanes = dz_all.shape[3]
    block = ut_all.shape[3]
    share = block // 4
    mine = pl.multiple_of(cols + strip * core, cols)

    def channels(h):
        return pl.ds(pl.multiple_of(h * half, half), half)

    def w_copies():
        return [
            pltpu.make_async_copy(weights.at[:, channels(h), channels(core)], w_v.at[h], w_sem.at[h]) for h in range(2)
        ]

    def wt_copies():
        return [
            pltpu.make_async_copy(weights.at[:, channels(core), channels(h)], wt_v.at[h], wt_sem.at[h]) for h in range(2)
        ]

    def in_copy(src, m):
        return pltpu.make_async_copy(src.at[m, :, :, channels(core)], inp.at[m, :, pl.ds(mine, strip), :], in_sem.at[m])

    for copy in w_copies() + wt_copies():
        copy.start()

    @pl.when(first)
    def _():
        for m in range(batches):
            in_copy(images, m).start()

    @pl.when(last)
    def _():
        for m in range(batches):
            in_copy(cotangent, m).start()

    barrier = pltpu.get_barrier_semaphore()
    for s in range(sections):
        @pl.when((sec >= s - 1) & (sec <= s + 1))
        def _():
            def greet(i, carry):
                @pl.when((s != sec) | (i != row))
                def _():
                    pl.semaphore_signal(barrier, inc=1, device_id=(jnp.int32(s), i), device_id_type=MESH)
                return carry
            lax.fori_loop(0, strips, greet, 0)

    acc_v[...] = jnp.zeros_like(acc_v)
    sums_v[...] = jnp.zeros_like(sums_v)

    for m in range(batches):
        for i in range(2):
            for at in (0, dz_all.shape[2] - cols):
                dz_all[m, i, pl.ds(at, cols), :] = jnp.zeros((cols, lanes), BF16)

    @pl.when(decoder)
    def _():
        wide = cols // 2
        windows_at = lax.broadcasted_iota(jnp.int32, (cols, wide), 1)
        places = lax.broadcasted_iota(jnp.int32, (cols, wide), 0)
        pick = (lax.shift_right_logical(places, 1) == windows_at).astype(F32)
        table = lax.dot_general(
            pick, switches[...].astype(F32), (((1,), (1,)), ((), ())), preferred_element_type=F32
        )
        odd = jnp.bitwise_and(lax.broadcasted_iota(jnp.int32, (cols, 128), 0), 1).astype(F32)
        windows = strip // cols // 2
        for m in range(batches):
            for i in range(2):
                for w in range(windows):
                    at = (m * 2 + i) * windows + w
                    value = jnp.broadcast_to(table[:, at : at + 1], (cols, 128))
                    for p in range(2):
                        hit = (jnp.abs(value - (2.0 * p + odd)) < 0.5).astype(F32).astype(BF16)
                        mask_own[m, i, pl.ds((2 * w + p) * cols, cols), :] = hit
        for m in range(batches):
            mask_v[m, :, pl.ds(mine, strip), :] = mask_own[m]

    @pl.when(jnp.logical_not(decoder))
    def _():
        mask_v[...] = jnp.ones_like(mask_v)

    near = 1 + jnp.where(sec > 0, 1, 0) + jnp.where(sec < sections - 1, 1, 0)
    pl.semaphore_wait(barrier, near * strips - 1)

    def remote(src, dst, send, recv, s, i):
        return pltpu.make_async_remote_copy(
            src_ref=src, dst_ref=dst, send_sem=send, recv_sem=recv, device_id=(s, i), device_id_type=MESH
        )

    def to_partner(src_at, dst_at, send, recv):
        return remote(src_at(1 - core), dst_at(pl.ds(mine, strip)), send, recv, sec, partner)

    def start_argument(src_at, dst_at, pair_sems, edge_sems):
        to_partner(src_at, dst_at, *pair_sems).start()

        @pl.when((core == 1) & has_down)
        def _():
            for i in range(2):
                remote(
                    src_at(i, pl.ds(strip - cols, cols)), dst_at(pl.ds(0, cols)),
                    edge_sems[0].at[i], edge_sems[1].at[0], sec, row + 1 + i,
                ).start()

        @pl.when((core == 0) & has_up)
        def _():
            for i in range(2):
                remote(
                    src_at(i, pl.ds(0, cols)), dst_at(pl.ds(cols + px, cols)),
                    edge_sems[0].at[i], edge_sems[1].at[1], sec, row - 2 + i,
                ).start()

    def argument_arrived(src_at, dst_at, pair_sems, edge_sems):
        to_partner(src_at, dst_at, *pair_sems).wait_recv()

        @pl.when(has_up)
        def _():
            remote(
                src_at(0, pl.ds(0, cols)), dst_at(pl.ds(0, cols)), edge_sems[0].at[0], edge_sems[1].at[0], sec, row
            ).wait_recv()

        @pl.when(has_down)
        def _():
            remote(
                src_at(0, pl.ds(0, cols)), dst_at(pl.ds(cols + px, cols)), edge_sems[0].at[0], edge_sems[1].at[1],
                sec, row,
            ).wait_recv()

    def argument_sent(src_at, dst_at, pair_sems, edge_sems):
        to_partner(src_at, dst_at, *pair_sems).wait_send()

        @pl.when(((core == 1) & has_down) | ((core == 0) & has_up))
        def _():
            for i in range(2):
                remote(
                    src_at(i, pl.ds(0, cols)), dst_at(pl.ds(0, cols)), edge_sems[0].at[i], edge_sems[1].at[0], sec, row
                ).wait_send()

    def input_parts(src, m):
        return (
            lambda i, r=pl.ds(0, strip): src.at[m, :, r, channels(i)],
            lambda r: inp.at[m, :, r, :],
            (pi_s.at[m], pi_r.at[m]),
            (ie_s.at[m], ie_r.at[m]),
        )

    mask_parts = (
        lambda i, r=pl.ds(0, strip): mask_own.at[:, :, r, :],
        lambda r: mask_v.at[:, :, r, :],
        (mp_s, mp_r),
        (me_s, me_r),
    )

    @pl.when(first)
    def _():
        for m in range(batches):
            start_argument(*input_parts(images, m))

    @pl.when(last)
    def _():
        for m in range(batches):
            start_argument(*input_parts(cotangent, m))

    @pl.when(decoder)
    def _():
        start_argument(*mask_parts)

    def affine_sends():
        return (
            remote(gains, gain_prev, gp_s.at[0], gp_r.at[0], sec + 1, row),
            remote(shifts, shift_prev, gp_s.at[1], gp_r.at[1], sec + 1, row),
        )

    @pl.when(sec < sections - 1)
    def _():
        for copy in affine_sends():
            copy.start()

    def block_sends(src, src_from, dst, send, recv, m, s):
        def piece(k, src_row, dst_row, rows, to):
            def one(i):
                return remote(
                    src.at[m, i, pl.ds(src_from + src_row, rows), :], dst.at[m, i, pl.ds(dst_row, rows), :],
                    send.at[m, k, i], recv.at[m, k, i], s, to,
                )
            return one

        return (
            piece(0, 0, cols, px, row), piece(1, px - cols, 0, cols, row + 2), piece(2, 0, cols + px, cols, row - 2)
        )

    def each_edge(parts, i, act):
        _, to_down, to_up = parts

        @pl.when(has_down)
        def _():
            act(to_down(i))

        @pl.when(has_up)
        def _():
            act(to_up(i))

    def edges_arrived(parts, i):
        _, to_down, to_up = parts

        @pl.when(has_up)
        def _():
            to_down(i).wait_recv()

        @pl.when(has_down)
        def _():
            to_up(i).wait_recv()

    def send_block(parts, i):
        each_edge(parts, i, start)
        parts[0](i).start()

    def block_sent(parts):
        for i in range(2):
            each_edge(parts, i, sent)
            parts[0](i).wait_send()

    def start(copy):
        copy.start()

    def sent(copy):
        copy.wait_send()

    def came(copy):
        copy.wait_recv()

    def z_sends(m, s):
        return block_sends(zown, cols, zin, fz_s, fz_r, m, s)

    def own_edges(m):
        return block_sends(zown, cols, zown, oe_s, oe_r, m, sec)

    def dy_sends(m, s):
        return block_sends(dyout, 0, dyin, bz_s, bz_r, m, s)

    def stats_each(src, dst, send, recv, m, s, same, act):
        def one(d, carry):
            q = chip + d
            q = jnp.where(q >= chips, q - chips, q)
            act(remote(src.at[m], dst.at[m, chip], send.at[m, d], recv.at[m, d], s, 2 * q + core))
            return carry
        lax.fori_loop(1 if same else 0, chips, one, 0)

    def start_stats(src, dst, send, recv, m, s, same):
        stats_each(src, dst, send, recv, m, s, same, start)
        if same:
            dst[m, chip] = src[m]

    def wait_stats(src, dst, send, recv, m, same):
        stats_each(src, dst, send, recv, m, sec, same, came)

    down_stats = (stat_out, zin_stat, fs_s, fs_r)
    same_stats = (stat_out, own_stat, os_s, os_r)
    back_stats = (sums_out, dy_stat, bs_s, bs_r)
    seed_stats = (seed_sums, dy_stat, ls_s, bs_r)

    def join(stats_ref, m):
        means = stats_ref[m, :, 0, :], stats_ref[m, :, 1, :]
        mean = jnp.sum(means[0] + means[1], 0, keepdims=True) / (2.0 * chips)
        off = [part - mean for part in means]
        squares = jnp.sum(stats_ref[m, :, 2, :] + stats_ref[m, :, 3, :], 0, keepdims=True)
        apart = jnp.sum(off[0] * off[0] + off[1] * off[1], 0, keepdims=True)
        at = (jnp.maximum(chip - 1, 0), chip, jnp.minimum(chip + 1, chips - 1))
        offs = [[stats_ref[m, q, pl.ds(i, 1), :] - mean for q in at] for i in range(2)]
        return lax.rsqrt((squares + local * apart) / total + EPSILON), offs

    def kind(g):
        return 0 if g == 0 else 2 if g == groups - 1 else 1

    def inside(g, values):
        if kind(g) == 1:
            return values
        return jnp.where(has_up if kind(g) == 0 else has_down, values, jnp.zeros_like(values))

    def group(g):
        return pl.ds(g * cols, cols)

    column = lax.broadcasted_iota(jnp.int32, (1, cols, half), 1)

    def taps_joined(parts, left, right):
        rows = parts[0].shape[0]

        def moved(values, by, edge):
            turned = pltpu.roll(values, by % rows, 0).reshape(rows // cols, cols, half)
            return jnp.where(column == edge, 0.0, turned).reshape(rows, half)
        return parts[1] + moved(parts[left], 1, 0) + moved(parts[right], -1, cols - 1)

    def pass_on(operand, send, recv, m, i):
        return remote(operand.at[m, core, i], operand.at[m, core, i], send.at[m, i], recv.at[m, i], sec, partner)

    def products(operand, w, m, h, r_at, images_at):
        rows = images_at.size * px

        def one(c):
            acc = jnp.zeros((rows, half), F32)
            for r in range(3):
                left = operand[m, h, images_at, pl.ds(r_at(r) * cols, px), :].reshape(rows, half)
                acc += jnp.dot(left, w[h, 3 * r + c], preferred_element_type=F32)
            return acc
        return one

    def convolve(operand, w, send, recv, m, r_at, left, right, prepare, use, after=lambda i: None):
        def part(images_at, wait_for):
            rows = pl.ds(0, images_at.size * px)
            mine_first = products(operand, w, m, core, r_at, images_at)
            for c in range(3):
                product_v[c, rows, :] = mine_first(c)
            for i in wait_for:
                pass_on(operand, send, recv, m, i).wait_recv()
            then = products(operand, w, m, 1 - core, r_at, images_at)
            return taps_joined([product_v[c, rows, :] + then(c) for c in range(3)], left, right)

        def ready(i):
            prepare(i)
            pass_on(operand, send, recv, m, i).start()
            after(i)

        def together():
            for i in range(2):
                ready(i)
            whole = part(pl.ds(0, 2), range(2))
            for i in range(2):
                use(i, whole[i * px : (i + 1) * px])

        def apart():
            for i in range(2):
                ready(i)
                use(i, part(pl.ds(i, 1), [i]))

        return together, apart

    def turned_copy(m, q):
        src = ut_own.at[m, pl.ds(pl.multiple_of((q // 2) * block, block), block), :]
        return src, ut_all.at[m, core, chip]


    def turned_each(m, act):
        def one(d, carry):
            q = chip + d
            q = jnp.where(q >= chips, q - chips, q)
            its_team = q // 2
            nearest = 2 * its_team + jnp.where(chip > q, 1, 0)

            @pl.when((its_team == team) | (q == nearest))
            def _():
                src, dst = turned_copy(m, q)
                act(remote(src, dst, ut_s.at[m, d], ut_r.at[m, d], sec, 2 * q + core))
            return carry
        lax.fori_loop(1, chips, one, 0)

    def entry_for(p):
        return (p // 2 != team) & (jnp.where(p > chip, 1, 0) == chip % 2)

    def turned_arrived(m):
        def one(d, carry):
            p = chip - d
            p = jnp.where(p < 0, p + chips, p)

            @pl.when(jnp.logical_not(entry_for(p)))
            def _():
                piece = ut_all.at[m, core, p]
                remote(piece, piece, ut_s.at[m, d], ut_r.at[m, d], sec, row).wait_recv()
            return carry
        lax.fori_loop(1, chips, one, 0)

    def turned_onward(m, act, arrive):
        other = chip + 1 - 2 * (chip % 2)

        def one(d, carry):
            p = chip - d
            p = jnp.where(p < 0, p + chips, p)

            @pl.when(entry_for(p))
            def _():
                piece = ut_all.at[m, core, p]
                if arrive:
                    remote(piece, piece, ut_s.at[m, d], ut_r.at[m, d], sec, row).wait_recv()
                there = other - p
                there = jnp.where(there < 0, there + chips, there)
                act(remote(piece, piece, uw_s.at[m, d], ut_r.at[m, there], sec, 2 * other + core))

            return carry
        lax.fori_loop(1, chips, one, 0)

    def turn_inputs(m):
        for h in range(2):
            ut_own[m, pl.ds(h * half, half), :] = ub[m, h, core, centre, :].T
        mine_at = pl.ds(pl.multiple_of(team * block, block), block)
        ut_all[m, core, chip] = ut_own[m, mine_at, :]

    def send_turned(m):
        turn_inputs(m)
        turned_each(m, start)

    def turned_relay(m):
        return remote(ut_all.at[m, core], ut_all.at[m, core], uf_s.at[m], uf_r.at[m], sec, partner)

    def relay_turned(m):
        turned_arrived(m)
        turned_relay(m).start()

    def pass_on_from(begin):
        def one(m, carry):
            turned_onward(m, start, True)
            return carry
        lax.fori_loop(begin, batches, one, 0)

    def relay_all():
        def one(m, carry):
            relay_turned(m)
            return carry
        lax.fori_loop(0, batches, one, 0)

    def dz_piece(m, i, k):
        src = dzb.at[m, core, i, centre, pl.ds(pl.multiple_of(k * lanes, lanes), lanes)]
        return src, dz_all.at[m, i, pl.ds(pl.multiple_of(cols + chip * px, cols), px), :]

    def dz_each(m, i, act):
        def one(e, carry):
            q = team + e
            q = 2 * jnp.where(q >= chips // 2, q - chips // 2, q) + core
            for k in range(2):
                @pl.when((q != chip) | (k != core))
                def _():
                    src, dst = dz_piece(m, i, k)
                    act(remote(src, dst, dz_s.at[m, i, 2 * e + k], dz_r.at[m, i, chip], sec, 2 * q + k))
            return carry
        lax.fori_loop(0, chips // 2, one, 0)

    def send_dz(m, i):
        dz_each(m, i, start)

        @pl.when(chip % 2 == core)
        def _():
            dz_all[m, i, pl.ds(pl.multiple_of(cols + chip * px, cols), px), :] = dzb[
                m, core, i, centre, pl.ds(pl.multiple_of(core * lanes, lanes), lanes)
            ]

    def dz_arrived(m):
        for i in range(2):
            def one(p, carry):
                @pl.when((p != chip) | (chip % 2 != core))
                def _():
                    piece = dz_all.at[m, i, pl.ds(cols, px), :]
                    remote(piece, piece, dz_s.at[m, i, 0], dz_r.at[m, i, p], sec, row).wait_recv()
                return carry
            lax.fori_loop(0, chips, one, 0)

    def gather_taps(m):
        dz_arrived(m)
        relayed = ut_all.at[m, 1 - core]
        pltpu.make_async_copy(relayed, relayed, uf_r.at[m]).wait()
        rows = dz_all.shape[2]
        edge = lax.broadcasted_iota(jnp.int32, (1, cols, lanes), 1)
        for i in range(2):
            values = dz_all[m, i].astype(F32)
            for c, by, gone in ((0, rows - 1, cols - 1), (2, 1, 0)):
                turned = pltpu.roll(values, by, 0).reshape(rows // cols, cols, lanes)
                turned = jnp.where(edge == gone, 0.0, turned).reshape(rows, lanes)
                dz_taps[i, :, pl.ds(c * lanes, lanes)] = turned.astype(BF16)
            dz_taps[i, :, pl.ds(lanes, lanes)] = dz_all[m, i]

    def kernel_row(m, r):
        part = jnp.zeros((block, 3 * lanes), F32)
        for i in range(2):
            left = jnp.concatenate([ut_all[m, i, q] for q in range(chips)], axis=1)
            part += jnp.dot(
                left, dz_taps[i, pl.ds((2 - r) * cols, px * (strips // 2)), :], preferred_element_type=F32
            )
        return part

    def add_gradients(m):
        gather_taps(m)
        for r in range(3):
            acc_v[r] = acc_v[r] + kernel_row(m, r)

    def forward(m):
        def prepare_first(i):
            for g in range(groups):
                ub[m, core, i, group(g), :] = inside(g, inp[m, i, group(g), :])

        def prepare_later(i):
            sends = z_sends(m, sec)
            inv = prev_coef[m, pl.ds(0, 1), :]
            slant = 0.5 * inv * gain_prev[:, channels(core)]
            shift = 0.5 * shift_prev[:, channels(core)]
            level = [slant * prev_coef[m, pl.ds(1 + 3 * i + e, 1), :] + shift for e in range(3)]
            edges_arrived(sends, i)
            sends[0](i).wait_recv()
            for g in range(groups):
                gate = jnp.concatenate([mask_v[m, i, group(g), :].astype(F32)] * (half // 128), axis=1)
                halved = zin[m, i, group(g), :].astype(F32) * slant + level[kind(g)]
                turn = jnp.tanh(halved)
                bent = halved * turn
                ub[m, core, i, group(g), :] = inside(g, ((halved + bent) * gate).astype(BF16))
                if kind(g) == 1:
                    slope_prev[m, i, pl.ds((g - 1) * cols, cols), :] = (0.5 + 0.5 * turn) * (1.0 + halved - bent)

        def prepare(i):
            @pl.when(first)
            def _():
                prepare_first(i)

            @pl.when(sec > 0)
            def _():
                prepare_later(i)

        def use(i, conv):
            mean = jnp.sum(conv, 0, keepdims=True) / local
            conv = conv - mean
            stat_out[m, pl.ds(i, 1), :] = mean
            stat_out[m, pl.ds(2 + i, 1), :] = jnp.sum(conv * conv, 0, keepdims=True)
            zown[m, i, centre, :] = conv.astype(BF16)

            @pl.when(sec < sections - 1)
            def _():
                if i == 1:
                    start_stats(*down_stats, m, sec + 1, False)
                send_block(z_sends(m, sec + 1), i)

        @pl.when(first)
        def _():
            in_copy(images, m).wait()
            argument_arrived(*input_parts(images, m))

        @pl.when(sec > 0)
        def _():
            @pl.when(m == 0)
            def _():
                for copy in affine_sends():
                    copy.wait_recv()

                @pl.when(decoder)
                def _():
                    argument_arrived(*mask_parts)

            wait_stats(*down_stats, m, False)
            inv, offs = join(zin_stat, m)
            for e, value in enumerate((inv, *offs[0], *offs[1])):
                prev_coef[m, pl.ds(e, 1), :] = value

        @pl.when(m == 0)
        def _():
            for copy in w_copies():
                copy.wait()

        together, apart = convolve(ub, w_v, ux_s, ux_r, m, lambda r: r, 0, 2, prepare, use)

        @pl.when(last)
        def _():
            together()

        @pl.when(jnp.logical_not(last))
        def _():
            apart()

        start_stats(*same_stats, m, sec, True)
        for i in range(2):
            each_edge(own_edges(m), i, start)

    def finish(m):
        wait_stats(*same_stats, m, True)
        inv, offs = join(own_stat, m)
        scale = inv * gains[:, channels(core)]
        for e, value in enumerate((inv, scale, *offs[0], *offs[1])):
            own_coef[m, pl.ds(e, 1), :] = value
        slant = 0.5 * scale
        shift = 0.5 * shifts[:, channels(core)]
        level = [[slant * off + shift for off in part] for part in offs]
        for i in range(2):
            edges_arrived(own_edges(m), i)

        @pl.when(last)
        def _():
            in_copy(cotangent, m).wait()
            argument_arrived(*input_parts(cotangent, m))
            ones, crosses = [], []
            for i in range(2):
                sums = jnp.zeros((cols, half), F32)
                cross = jnp.zeros((cols, half), F32)
                for g in range(groups):
                    z = zown[m, i, group(g), :].astype(F32)
                    halved = z * slant + level[i][kind(g)]
                    turn = jnp.tanh(halved)
                    bent = halved * turn
                    dy = inp[m, i, group(g), :].astype(F32) * ((0.5 + 0.5 * turn) * (1.0 + halved - bent))
                    dyin[m, i, group(g), :] = dy.astype(BF16)
                    if kind(g) == 1:
                        out_v[m, i, pl.ds((g - 1) * cols, cols), :] = (halved + bent).astype(BF16)
                        sums += dy
                        cross += dy * z
                one = jnp.sum(sums, 0, keepdims=True)
                ones.append(one)
                crosses.append(jnp.sum(cross, 0, keepdims=True) + offs[i][1] * one)
            seed_sums[m, pl.ds(0, 1), :] = ones[0] + ones[1]
            seed_sums[m, pl.ds(1, 1), :] = inv * (crosses[0] + crosses[1])
            start_stats(*seed_stats, m, sec, True)

        @pl.when(jnp.logical_not(last))
        def _():
            for i in range(2):
                for g in range(1, groups - 1):
                    halved = zown[m, i, group(g), :].astype(F32) * slant + level[i][1]
                    out_v[m, i, pl.ds((g - 1) * cols, cols), :] = (halved + halved * jnp.tanh(halved)).astype(BF16)

        for copy in result_copies(out_v, outs, out_sem, po_s, po_r, m):
            copy.start()

    def result_copies(src, dst, sem, send, recv, m):
        here, there = pl.multiple_of(strip * core, cols), pl.multiple_of(strip * (1 - core), cols)
        place = dst.at[m, :, :, channels(core)]
        return (
            pltpu.make_async_copy(src.at[m, :, pl.ds(here, strip), :], place, sem.at[m]),
            remote(src.at[m, :, pl.ds(there, strip), :], place, send.at[m], recv.at[m], sec, partner),
        )

    def backward(m):
        @pl.when(last)
        def _():
            wait_stats(*seed_stats, m, True)

        @pl.when(jnp.logical_not(last))
        def _():
            wait_stats(*back_stats, m, False)

        first_sum = jnp.sum(dy_stat[m, :, 0, :], 0, keepdims=True)
        cross_sum = jnp.sum(dy_stat[m, :, 1, :], 0, keepdims=True)
        sums_v[core, pl.ds(0, 1), :] = sums_v[core, pl.ds(0, 1), :] + first_sum
        sums_v[core, pl.ds(1, 1), :] = sums_v[core, pl.ds(1, 1), :] + cross_sum

        def prepare(i):
            inv = own_coef[m, pl.ds(0, 1), :]
            scale = own_coef[m, pl.ds(1, 1), :]
            tilt = scale * inv * (cross_sum / total)
            base = [scale * (first_sum / total) + tilt * own_coef[m, pl.ds(2 + 3 * i + e, 1), :] for e in range(3)]
            sends = dy_sends(m, sec)

            @pl.when(jnp.logical_not(last))
            def _():
                edges_arrived(sends, i)
                sends[0](i).wait_recv()

            for g in range(groups):
                dz = dyin[m, i, group(g), :].astype(F32) * scale
                dz = dz - zown[m, i, group(g), :].astype(F32) * tilt - base[kind(g)]
                dzb[m, core, i, group(g), :] = inside(g, dz.astype(BF16))

        def then(i):
            @pl.when(first)
            def _():
                send_dz(m, i)

        def use(i, conv):
            gate = jnp.concatenate([mask_v[m, i, centre, :].astype(F32)] * (half // 128), axis=1)
            du = (conv * gate).astype(BF16)
            gin_v[m, i] = du

            @pl.when(sec > 0)
            def _():
                dy = du.astype(F32) * slope_prev[m, i]
                dyout[m, i] = dy.astype(BF16)
                one = jnp.sum(dy, 0, keepdims=True)
                cross = jnp.sum(dy * zin[m, i, centre, :].astype(F32), 0, keepdims=True)
                cross = prev_coef[m, pl.ds(0, 1), :] * (cross + prev_coef[m, pl.ds(2 + 3 * i, 1), :] * one)
                if i == 1:
                    one = one + sums_out[m, pl.ds(0, 1), :]
                    cross = cross + sums_out[m, pl.ds(1, 1), :]
                sums_out[m, pl.ds(0, 1), :] = one
                sums_out[m, pl.ds(1, 1), :] = cross
                if i == 1:
                    start_stats(*back_stats, m, sec - 1, False)
                send_block(dy_sends(m, sec - 1), i)

        together, apart = convolve(dzb, wt_v, dx_s, dx_r, m, lambda r: 2 - r, 2, 0, prepare, use, then)

        whole = first | (last & (m < batches - 1))

        @pl.when(whole)
        def _():
            together()

        @pl.when(jnp.logical_not(whole))
        def _():
            apart()

        for copy in result_copies(gin_v, grads_in, gin_sem, pg_s, pg_r, m):
            copy.start()

        @pl.when((sec > 0) & (sec < sections - 1))
        def _():
            for i in range(2):
                send_dz(m, i)

    def turn_weights():
        for copy in wt_copies():
            copy.wait()

        def one(i, carry):
            for h in range(2):
                wt_v[h, i] = wt_v[h, i].T
            return carry
        lax.fori_loop(0, 9, one, 0)

    @pl.when(late)
    def _():
        turn_weights()

    def step(t, carry):
        ahead = t - sec
        behind = t - (2 * sections - 1 - sec)

        @pl.when((ahead >= 0) & (ahead < batches))
        def _():
            forward(ahead)

        @pl.when(late & (ahead >= 0) & (ahead < batches))
        def _():
            send_turned(ahead)

        @pl.when(jnp.logical_not(late) & (ahead == batches))
        def _():
            def turned(m, carry):
                send_turned(m)
                return carry
            lax.fori_loop(0, batches, turned, 0)
            turn_weights()

        @pl.when(jnp.logical_not(late) & (ahead == batches + 1))
        def _():
            pass_on_from(0)

        @pl.when(first & (ahead == batches + 2))
        def _():
            relay_all()

        done = ahead - jnp.where(last, 0, 1)

        @pl.when((behind >= 0) & (behind < batches))
        def _():
            backward(behind)

        @pl.when((done >= 0) & (done < batches))
        def _():
            finish(done)

        @pl.when(last & (ahead >= 1) & (ahead <= batches))
        def _():
            turned_onward(ahead - 1, start, True)

        return carry

    lax.fori_loop(0, 2 * sections - 1 + batches, step, 0)

    remote(sums_v.at[core], sums_v.at[core], sv_s, sv_r, sec, partner).start()

    @pl.when(last)
    def _():
        def send(m, carry):
            for i in range(2):
                send_dz(m, i)
            return carry

        lax.fori_loop(0, batches, send, 0)

    @pl.when(late & jnp.logical_not(last))
    def _():
        pass_on_from(0)

    @pl.when(jnp.logical_not(first))
    def _():
        relay_all()

    def add(m, carry):
        add_gradients(m)
        return carry

    lax.fori_loop(0, batches - 1, add, 0)

    def swap(r, d):
        other = (seat + d) % 4
        return remote(
            swap_out.at[r, pl.ds(pl.multiple_of(other * share, share), share), :], other_parts.at[4 - d - 1, r],
            sw_s.at[r, d - 1], sw_r.at[r, 4 - d - 1], sec, 4 * team + other,
        )

    def own_copy(r):
        return pltpu.make_async_copy(
            acc_v.at[r, pl.ds(pl.multiple_of(seat * share, share), share), :], own_part.at[r], dw_sem.at[r]
        )

    gather_taps(batches - 1)
    for r in range(3):
        part = acc_v[r] + kernel_row(batches - 1, r)
        acc_v[r] = part
        swap_out[r] = part.astype(BF16)
        for d in range(1, 4):
            swap(r, d).start()
        own_copy(r).start()

    for r in range(3):
        own_copy(r).wait()
        for d in range(1, 4):
            swap(r, d).wait_send()
            swap(r, d).wait_recv()

    @pl.when(decoder)
    def _():
        argument_sent(*mask_parts)

    @pl.when(sec < sections - 1)
    def _():
        for copy in affine_sends():
            copy.wait_send()

    def sums_copy():
        return remote(sums_v.at[core], sums_v.at[core], sv_s, sv_r, sec, partner)

    sums_copy().wait_recv()
    sums_copy().wait_send()
    for h in range(2):
        shift_sum[:, pl.ds(h * half, half)] = sums_v[h, pl.ds(0, 1), :]
        gain_sum[:, pl.ds(h * half, half)] = sums_v[h, pl.ds(1, 1), :]

    def drain(m, carry):
        for src, dst, sems in ((out_v, outs, (out_sem, po_s, po_r)), (gin_v, grads_in, (gin_sem, pg_s, pg_r))):
            here, there = result_copies(src, dst, *sems, m)
            here.wait()
            there.wait_send()
            remote(
                src.at[m, :, pl.ds(0, strip), :], dst.at[m, :, :, channels(1 - core)], sems[1].at[m], sems[2].at[m],
                sec, partner,
            ).wait_recv()

        turned_each(m, sent)
        turned_onward(m, sent, False)
        turned_relay(m).wait_send()
        for i in range(2):
            dz_each(m, i, sent)
        for i in range(2):
            pass_on(ub, ux_s, ux_r, m, i).wait_send()
            pass_on(dzb, dx_s, dx_r, m, i).wait_send()

        @pl.when(first)
        def _():
            argument_sent(*input_parts(images, m))

        @pl.when(last)
        def _():
            argument_sent(*input_parts(cotangent, m))
            stats_each(*seed_stats, m, sec, True, sent)

        @pl.when(sec < sections - 1)
        def _():
            stats_each(*down_stats, m, sec + 1, False, sent)
            block_sent(z_sends(m, sec + 1))

        stats_each(*same_stats, m, sec, True, sent)
        for i in range(2):
            each_edge(own_edges(m), i, sent)

        @pl.when(sec > 0)
        def _():
            stats_each(*back_stats, m, sec - 1, False, sent)
            block_sent(dy_sends(m, sec - 1))

        return carry

    lax.fori_loop(0, batches, drain, 0)


def settle(outs, grads_in, gain_sum, shift_sum, own, others, *refs):
    targets, stages, (own_v, others_v, whole, in_sem, out_sem) = refs[:5], refs[5:9], refs[9:]
    moves = []
    for src, dst, stage in zip((outs, grads_in, gain_sum, shift_sum), targets[:4], stages):
        if len(src.shape) == 2:
            moves.append((src, dst, stage))
        else:
            moves += [(src.at[i], dst.at[i], stage.at[i]) for i in range(src.shape[0])]
    count = len(moves)
    parts = [pltpu.make_async_copy(own, own_v, in_sem.at[count])]
    parts += [pltpu.make_async_copy(others.at[d], others_v.at[d], in_sem.at[count + 1 + d]) for d in range(3)]
    ins = [pltpu.make_async_copy(src, stage, in_sem.at[i]) for i, (src, dst, stage) in enumerate(moves)]
    outs = [pltpu.make_async_copy(stage, dst, out_sem.at[i]) for i, (src, dst, stage) in enumerate(moves)]
    rows = [pltpu.make_async_copy(whole.at[r], targets[4].at[r], out_sem.at[count + r]) for r in range(3)]
    for copy in parts + ins:
        copy.start()
    for copy in parts:
        copy.wait()
    seat = lax.axis_index("rows") % 4
    lanes = whole.shape[3] // 4
    for r in range(3):
        for d in range(4):
            at = pl.ds(pl.multiple_of(((seat + d) % 4) * lanes, lanes), lanes)
            for c in range(3):
                part = pl.ds(c * lanes, lanes)
                whole[r, c, :, at] = own_v[r, :, part] if d == 0 else others_v[d - 1, r, :, part].astype(F32)
        rows[r].start()
    for come, go in zip(ins, outs):
        come.wait()
        go.start()
    for copy in outs + rows:
        copy.wait()


def body(images, switches, conv_weights, gains, shifts, cotangent):
    sections = lax.axis_size("section")
    strips = lax.axis_size("rows")
    batches, pictures, strip_rows, cols, ch = images.shape
    strip = strip_rows * cols
    px = 2 * strip
    tall = px + 2 * cols
    anywhere = pl.BlockSpec(memory_space=pl.ANY)
    vmem = pl.BlockSpec(memory_space=pltpu.VMEM)
    dma = pltpu.SemaphoreType.DMA
    flops = 3 * 2 * 9 * ch * ch * batches * px
    share = ch // strips
    chips = strips // 2
    outs, grads_in, own, others, gain_sum, shift_sum = pl.pallas_call(
        functools.partial(kernel, sections, strips, cols),
        out_shape=(
            jax.ShapeDtypeStruct((batches, pictures, strip, ch), BF16),
            jax.ShapeDtypeStruct((batches, pictures, strip, ch), BF16),
            jax.ShapeDtypeStruct((3, share, 3 * ch // 4), F32),
            jax.ShapeDtypeStruct((3, 3, share, 3 * ch // 4), BF16),
            jax.ShapeDtypeStruct((1, ch), F32),
            jax.ShapeDtypeStruct((1, ch), F32),
        ),
        in_specs=[anywhere, anywhere, anywhere, vmem, vmem, vmem],
        out_specs=(anywhere,) * 4 + (vmem, vmem),
        scratch_shapes=[
            pltpu.VMEM((2, 9, ch // 2, ch // 2), BF16),
            pltpu.VMEM((2, 9, ch // 2, ch // 2), BF16),
            pltpu.VMEM((batches, 2, tall, ch // 2), BF16),
            pltpu.VMEM((batches, 2, strip, 128), BF16),
            pltpu.VMEM((batches, 2, tall, 128), BF16),
            pltpu.VMEM((1, ch), F32),
            pltpu.VMEM((1, ch), F32),
            pltpu.VMEM((batches, 2, tall, ch // 2), BF16),
            pltpu.VMEM((batches, chips, 4, ch // 2), F32),
            pltpu.VMEM((batches, 2, tall, ch // 2), BF16),
            pltpu.VMEM((batches, chips, 4, ch // 2), F32),
            pltpu.VMEM((batches, 2, 2, tall, ch // 2), BF16),
            pltpu.VMEM((batches, 2, px, ch // 2), F32),
            pltpu.VMEM((batches, 8, ch // 2), F32),
            pltpu.VMEM((batches, 8, ch // 2), F32),
            pltpu.VMEM((batches, 2, tall, ch // 2), BF16),
            pltpu.VMEM((batches, chips, 2, ch // 2), F32),
            pltpu.VMEM((batches, 2, 2, tall, ch // 2), BF16),
            pltpu.VMEM((batches, 2, px, ch // 2), BF16),
            pltpu.VMEM((3, 2 * px, ch // 2), F32),
            pltpu.VMEM((2, 2, ch // 2), F32),
            pltpu.VMEM((batches, 4, ch // 2), F32),
            pltpu.VMEM((batches, 2, ch // 2), F32),
            pltpu.VMEM((batches, 2, ch // 2), F32),
            pltpu.VMEM((batches, 2, px, ch // 2), BF16),
            pltpu.VMEM((batches, 2, px, ch // 2), BF16),
            pltpu.VMEM((batches, ch, px), BF16),
            pltpu.VMEM((batches, 2, strips // 2, 4 * share, px), BF16),
            pltpu.VMEM((batches, 2, px * strips // 2 + 2 * cols, ch // 4), BF16),
            pltpu.VMEM((2, px * strips // 2 + 2 * cols, 3 * ch // 4), BF16),
            pltpu.VMEM((3, 4 * share, 3 * ch // 4), F32),
            pltpu.VMEM((3, 4 * share, 3 * ch // 4), BF16),
            dma((2,)), dma((2,)),
            dma((batches,)),
            dma((batches,)), dma((batches,)),
            dma((batches, 2)), dma((batches, 2)),
            dma, dma,
            dma((2,)), dma((2,)),
            dma((2,)), dma((2,)),
            dma((batches, 2)), dma((batches, 2)),
            dma((batches, 2)), dma((batches, 2)),
            dma, dma,
            dma((batches, 3, 2)), dma((batches, 3, 2)),
            dma((batches, chips)), dma((batches, chips)),
            dma((batches, 3, 2)), dma((batches, 3, 2)),
            dma((batches, chips)), dma((batches, chips)),
            dma((batches, 3, 2)), dma((batches, 3, 2)),
            dma((batches, chips)), dma((batches, chips)),
            dma((batches, chips)),
            dma((batches,)), dma((batches,)), dma((batches,)),
            dma((batches,)), dma((batches,)), dma((batches,)),
            dma((batches, chips)), dma((batches, chips)), dma((batches, chips)),
            dma((batches,)), dma((batches,)),
            dma((batches, 2, chips)), dma((batches, 2, chips)),
            dma((3, 3)), dma((3, 3)),
            dma((3,)),
        ],
        compiler_params=pltpu.CompilerParams(
            collective_id=0, has_side_effects=True, vmem_limit_bytes=56 * 2**20
        ),
        cost_estimate=pl.CostEstimate(
            flops=flops, bytes_accessed=2 * 9 * ch * ch * 2, transcendentals=0
        ),
    )(
        images.reshape(batches, pictures, strip, ch),
        cotangent.reshape(batches, pictures, strip, ch),
        conv_weights.reshape(9, ch, ch),
        gains,
        shifts,
        switches.reshape(-1, switches.shape[-1]),
    )
    results = (outs, grads_in, gain_sum, shift_sum)
    whole = jax.ShapeDtypeStruct((3, 3, share, ch), F32)
    outs, grads_in, gain_sum, shift_sum, weight_grad = pl.pallas_call(
        settle,
        out_shape=tuple(jax.ShapeDtypeStruct(r.shape, r.dtype) for r in results) + (whole,),
        in_specs=[anywhere] * 6,
        out_specs=(anywhere,) * 5,
        scratch_shapes=[pltpu.VMEM(r.shape, r.dtype) for r in results]
        + [
            pltpu.VMEM(own.shape, F32),
            pltpu.VMEM(others.shape, BF16),
            pltpu.VMEM(whole.shape, F32),
            dma((2 * batches + 6,)),
            dma((2 * batches + 5,)),
        ],
        compiler_params=pltpu.CompilerParams(vmem_limit_bytes=60 * 2**20),
    )(*results, own, others)
    shape = (1, batches, pictures, strip_rows, cols, ch)
    return (outs.reshape(shape), grads_in.reshape(shape), weight_grad[None], gain_sum, shift_sum)


def solution(mesh):
    return jax.shard_map(
        body,
        mesh=mesh,
        in_specs=(
            P(None, None, "rows", None, None),
            P(None, None, "rows", None),
            P("section", None, None, None, None),
            P("section", None),
            P("section", None),
            P(None, None, "rows", None, None),
        ),
        out_specs=(
            P("section", None, None, "rows", None, None),
            P("section", None, None, "rows", None, None),
            P("section", None, None, "rows", None),
            P("section", None),
            P("section", None),
        ),
        check_vma=False,
    )
```

```python
import functools

import jax
import jax.numpy as jnp
from jax import lax
from jax.experimental import pallas as pl
from jax.experimental.pallas import tpu as pltpu
from jax.sharding import PartitionSpec as P

EPSILON = 1e-05
MESH = pl.DeviceIdType.MESH
BF16 = jnp.bfloat16
F32 = jnp.float32


def kernel(
    sections, strips, cols,
    images, cotangent, weights, gains, shifts, switches,
    outs, grads_in, own_part, other_parts, gain_sum, shift_sum,
    w_v, wt_v, inp, mask_own, mask_v, gain_prev, shift_prev, zin, zin_stat, zown, own_stat, ub, slope_prev,
    prev_coef, own_coef, dyin, dy_stat, dzb, dyout, product_v, sums_v, stat_out, sums_out, seed_sums, out_v, gin_v,
    ut_own, ut_all, dz_all, dz_taps, acc_v, swap_out,
    w_sem, wt_sem, in_sem, pi_s, pi_r, ie_s, ie_r, mp_s, mp_r, me_s, me_r, gp_s, gp_r,
    ux_s, ux_r, dx_s, dx_r, sv_s, sv_r,
    fz_s, fz_r, fs_s, fs_r, oe_s, oe_r, os_s, os_r, bz_s, bz_r, bs_s, bs_r, ls_s,
    out_sem, po_s, po_r, gin_sem, pg_s, pg_r,
    ut_s, ut_r, uw_s, uf_s, uf_r, dz_s, dz_r, sw_s, sw_r, dw_sem,
):
    sec = lax.axis_index("section")
    row = lax.axis_index("rows")
    batches, _, tall, half = inp.shape
    ch = 2 * half
    px = tall - 2 * cols
    strip = px // 2
    groups = tall // cols
    chips = strips // 2
    local = float(px)
    total = 2.0 * local * chips
    first, last, decoder = sec == 0, sec == sections - 1, sec == sections // 2
    late = sec >= sections // 2
    core = row % 2
    partner = row + 1 - 2 * core
    has_up, has_down = row >= 2, row < strips - 2
    centre = pl.ds(cols, px)
    chip = row // 2
    team, seat = row // 4, row % 4
    lanes = dz_all.shape[3]
    block = ut_all.shape[3]
    share = block // 4
    mine = pl.multiple_of(cols + strip * core, cols)

    def channels(h):
        return pl.ds(pl.multiple_of(h * half, half), half)

    def w_copies():
        return [
            pltpu.make_async_copy(weights.at[:, channels(h), channels(core)], w_v.at[h], w_sem.at[h]) for h in range(2)
        ]

    def wt_copies():
        return [
            pltpu.make_async_copy(weights.at[:, channels(core), channels(h)], wt_v.at[h], wt_sem.at[h]) for h in range(2)
        ]

    def in_copy(src, m):
        return pltpu.make_async_copy(src.at[m, :, :, channels(core)], inp.at[m, :, pl.ds(mine, strip), :], in_sem.at[m])

    for copy in w_copies() + wt_copies():
        copy.start()

    @pl.when(first)
    def _():
        for m in range(batches):
            in_copy(images, m).start()

    @pl.when(last)
    def _():
        for m in range(batches):
            in_copy(cotangent, m).start()

    barrier = pltpu.get_barrier_semaphore()
    for s in range(sections):
        @pl.when((sec >= s - 1) & (sec <= s + 1))
        def _():
            def greet(i, carry):
                @pl.when((s != sec) | (i != row))
                def _():
                    pl.semaphore_signal(barrier, inc=1, device_id=(jnp.int32(s), i), device_id_type=MESH)
                return carry
            lax.fori_loop(0, strips, greet, 0)

    acc_v[...] = jnp.zeros_like(acc_v)
    sums_v[...] = jnp.zeros_like(sums_v)

    for m in range(batches):
        for i in range(2):
            for at in (0, dz_all.shape[2] - cols):
                dz_all[m, i, pl.ds(at, cols), :] = jnp.zeros((cols, lanes), BF16)

    @pl.when(decoder)
    def _():
        wide = cols // 2
        windows_at = lax.broadcasted_iota(jnp.int32, (cols, wide), 1)
        places = lax.broadcasted_iota(jnp.int32, (cols, wide), 0)
        pick = (lax.shift_right_logical(places, 1) == windows_at).astype(F32)
        table = lax.dot_general(
            pick, switches[...].astype(F32), (((1,), (1,)), ((), ())), preferred_element_type=F32
        )
        odd = jnp.bitwise_and(lax.broadcasted_iota(jnp.int32, (cols, 128), 0), 1).astype(F32)
        windows = strip // cols // 2
        for m in range(batches):
            for i in range(2):
                for w in range(windows):
                    at = (m * 2 + i) * windows + w
                    value = jnp.broadcast_to(table[:, at : at + 1], (cols, 128))
                    for p in range(2):
                        hit = (jnp.abs(value - (2.0 * p + odd)) < 0.5).astype(F32).astype(BF16)
                        mask_own[m, i, pl.ds((2 * w + p) * cols, cols), :] = hit
        for m in range(batches):
            mask_v[m, :, pl.ds(mine, strip), :] = mask_own[m]

    @pl.when(jnp.logical_not(decoder))
    def _():
        mask_v[...] = jnp.ones_like(mask_v)

    near = 1 + jnp.where(sec > 0, 1, 0) + jnp.where(sec < sections - 1, 1, 0)
    pl.semaphore_wait(barrier, near * strips - 1)

    def remote(src, dst, send, recv, s, i):
        return pltpu.make_async_remote_copy(
            src_ref=src, dst_ref=dst, send_sem=send, recv_sem=recv, device_id=(s, i), device_id_type=MESH
        )

    def to_partner(src_at, dst_at, send, recv):
        return remote(src_at(1 - core), dst_at(pl.ds(mine, strip)), send, recv, sec, partner)

    def start_argument(src_at, dst_at, pair_sems, edge_sems):
        to_partner(src_at, dst_at, *pair_sems).start()

        @pl.when((core == 1) & has_down)
        def _():
            for i in range(2):
                remote(
                    src_at(i, pl.ds(strip - cols, cols)), dst_at(pl.ds(0, cols)),
                    edge_sems[0].at[i], edge_sems[1].at[0], sec, row + 1 + i,
                ).start()

        @pl.when((core == 0) & has_up)
        def _():
            for i in range(2):
                remote(
                    src_at(i, pl.ds(0, cols)), dst_at(pl.ds(cols + px, cols)),
                    edge_sems[0].at[i], edge_sems[1].at[1], sec, row - 2 + i,
                ).start()

    def argument_arrived(src_at, dst_at, pair_sems, edge_sems):
        to_partner(src_at, dst_at, *pair_sems).wait_recv()

        @pl.when(has_up)
        def _():
            remote(
                src_at(0, pl.ds(0, cols)), dst_at(pl.ds(0, cols)), edge_sems[0].at[0], edge_sems[1].at[0], sec, row
            ).wait_recv()

        @pl.when(has_down)
        def _():
            remote(
                src_at(0, pl.ds(0, cols)), dst_at(pl.ds(cols + px, cols)), edge_sems[0].at[0], edge_sems[1].at[1],
                sec, row,
            ).wait_recv()

    def argument_sent(src_at, dst_at, pair_sems, edge_sems):
        to_partner(src_at, dst_at, *pair_sems).wait_send()

        @pl.when(((core == 1) & has_down) | ((core == 0) & has_up))
        def _():
            for i in range(2):
                remote(
                    src_at(i, pl.ds(0, cols)), dst_at(pl.ds(0, cols)), edge_sems[0].at[i], edge_sems[1].at[0], sec, row
                ).wait_send()

    def input_parts(src, m):
        return (
            lambda i, r=pl.ds(0, strip): src.at[m, :, r, channels(i)],
            lambda r: inp.at[m, :, r, :],
            (pi_s.at[m], pi_r.at[m]),
            (ie_s.at[m], ie_r.at[m]),
        )

    mask_parts = (
        lambda i, r=pl.ds(0, strip): mask_own.at[:, :, r, :],
        lambda r: mask_v.at[:, :, r, :],
        (mp_s, mp_r),
        (me_s, me_r),
    )

    @pl.when(first)
    def _():
        for m in range(batches):
            start_argument(*input_parts(images, m))

    @pl.when(last)
    def _():
        for m in range(batches):
            start_argument(*input_parts(cotangent, m))

    @pl.when(decoder)
    def _():
        start_argument(*mask_parts)

    def affine_sends():
        return (
            remote(gains, gain_prev, gp_s.at[0], gp_r.at[0], sec + 1, row),
            remote(shifts, shift_prev, gp_s.at[1], gp_r.at[1], sec + 1, row),
        )

    @pl.when(sec < sections - 1)
    def _():
        for copy in affine_sends():
            copy.start()

    def block_sends(src, src_from, dst, send, recv, m, s):
        def piece(k, src_row, dst_row, rows, to):
            def one(i):
                return remote(
                    src.at[m, i, pl.ds(src_from + src_row, rows), :], dst.at[m, i, pl.ds(dst_row, rows), :],
                    send.at[m, k, i], recv.at[m, k, i], s, to,
                )
            return one

        return (
            piece(0, 0, cols, px, row), piece(1, px - cols, 0, cols, row + 2), piece(2, 0, cols + px, cols, row - 2)
        )

    def each_edge(parts, i, act):
        _, to_down, to_up = parts

        @pl.when(has_down)
        def _():
            act(to_down(i))

        @pl.when(has_up)
        def _():
            act(to_up(i))

    def edges_arrived(parts, i):
        _, to_down, to_up = parts

        @pl.when(has_up)
        def _():
            to_down(i).wait_recv()

        @pl.when(has_down)
        def _():
            to_up(i).wait_recv()

    def send_block(parts, i):
        each_edge(parts, i, start)
        parts[0](i).start()

    def block_sent(parts):
        for i in range(2):
            each_edge(parts, i, sent)
            parts[0](i).wait_send()

    def start(copy):
        copy.start()

    def sent(copy):
        copy.wait_send()

    def came(copy):
        copy.wait_recv()

    def z_sends(m, s):
        return block_sends(zown, cols, zin, fz_s, fz_r, m, s)

    def own_edges(m):
        return block_sends(zown, cols, zown, oe_s, oe_r, m, sec)

    def dy_sends(m, s):
        return block_sends(dyout, 0, dyin, bz_s, bz_r, m, s)

    def stats_each(src, dst, send, recv, m, s, same, act):
        def one(d, carry):
            q = chip + d
            q = jnp.where(q >= chips, q - chips, q)
            act(remote(src.at[m], dst.at[m, chip], send.at[m, d], recv.at[m, d], s, 2 * q + core))
            return carry
        lax.fori_loop(1 if same else 0, chips, one, 0)

    def start_stats(src, dst, send, recv, m, s, same):
        stats_each(src, dst, send, recv, m, s, same, start)
        if same:
            dst[m, chip] = src[m]

    def wait_stats(src, dst, send, recv, m, same):
        stats_each(src, dst, send, recv, m, sec, same, came)

    down_stats = (stat_out, zin_stat, fs_s, fs_r)
    same_stats = (stat_out, own_stat, os_s, os_r)
    back_stats = (sums_out, dy_stat, bs_s, bs_r)
    seed_stats = (seed_sums, dy_stat, ls_s, bs_r)

    def join(stats_ref, m):
        means = stats_ref[m, :, 0, :], stats_ref[m, :, 1, :]
        mean = jnp.sum(means[0] + means[1], 0, keepdims=True) / (2.0 * chips)
        off = [part - mean for part in means]
        squares = jnp.sum(stats_ref[m, :, 2, :] + stats_ref[m, :, 3, :], 0, keepdims=True)
        apart = jnp.sum(off[0] * off[0] + off[1] * off[1], 0, keepdims=True)
        at = (jnp.maximum(chip - 1, 0), chip, jnp.minimum(chip + 1, chips - 1))
        offs = [[stats_ref[m, q, pl.ds(i, 1), :] - mean for q in at] for i in range(2)]
        return lax.rsqrt((squares + local * apart) / total + EPSILON), offs

    def kind(g):
        return 0 if g == 0 else 2 if g == groups - 1 else 1

    def inside(g, values):
        if kind(g) == 1:
            return values
        return jnp.where(has_up if kind(g) == 0 else has_down, values, jnp.zeros_like(values))

    def group(g):
        return pl.ds(g * cols, cols)

    column = lax.broadcasted_iota(jnp.int32, (1, cols, half), 1)

    def taps_joined(parts, left, right):
        rows = parts[0].shape[0]

        def moved(values, by, edge):
            turned = pltpu.roll(values, by % rows, 0).reshape(rows // cols, cols, half)
            return jnp.where(column == edge, 0.0, turned).reshape(rows, half)
        return parts[1] + moved(parts[left], 1, 0) + moved(parts[right], -1, cols - 1)

    def pass_on(operand, send, recv, m, i):
        return remote(operand.at[m, core, i], operand.at[m, core, i], send.at[m, i], recv.at[m, i], sec, partner)

    def products(operand, w, m, h, r_at, images_at):
        rows = images_at.size * px

        def one(c):
            acc = jnp.zeros((rows, half), F32)
            for r in range(3):
                left = operand[m, h, images_at, pl.ds(r_at(r) * cols, px), :].reshape(rows, half)
                acc += jnp.dot(left, w[h, 3 * r + c], preferred_element_type=F32)
            return acc
        return one

    def convolve(operand, w, send, recv, m, r_at, left, right, prepare, use, after=lambda i: None):
        def part(images_at, wait_for):
            rows = pl.ds(0, images_at.size * px)
            mine_first = products(operand, w, m, core, r_at, images_at)
            for c in range(3):
                product_v[c, rows, :] = mine_first(c)
            for i in wait_for:
                pass_on(operand, send, recv, m, i).wait_recv()
            then = products(operand, w, m, 1 - core, r_at, images_at)
            return taps_joined([product_v[c, rows, :] + then(c) for c in range(3)], left, right)

        def ready(i):
            prepare(i)
            pass_on(operand, send, recv, m, i).start()
            after(i)

        def together():
            for i in range(2):
                ready(i)
            whole = part(pl.ds(0, 2), range(2))
            for i in range(2):
                use(i, whole[i * px : (i + 1) * px])

        def apart():
            for i in range(2):
                ready(i)
                use(i, part(pl.ds(i, 1), [i]))

        return together, apart

    def turned_copy(m, q):
        src = ut_own.at[m, pl.ds(pl.multiple_of((q // 2) * block, block), block), :]
        return src, ut_all.at[m, core, chip]


    def turned_each(m, act):
        def one(d, carry):
            q = chip + d
            q = jnp.where(q >= chips, q - chips, q)
            its_team = q // 2
            nearest = 2 * its_team + jnp.where(chip > q, 1, 0)

            @pl.when((its_team == team) | (q == nearest))
            def _():
                src, dst = turned_copy(m, q)
                act(remote(src, dst, ut_s.at[m, d], ut_r.at[m, d], sec, 2 * q + core))
            return carry
        lax.fori_loop(1, chips, one, 0)

    def entry_for(p):
        return (p // 2 != team) & (jnp.where(p > chip, 1, 0) == chip % 2)

    def turned_arrived(m):
        def one(d, carry):
            p = chip - d
            p = jnp.where(p < 0, p + chips, p)

            @pl.when(jnp.logical_not(entry_for(p)))
            def _():
                piece = ut_all.at[m, core, p]
                remote(piece, piece, ut_s.at[m, d], ut_r.at[m, d], sec, row).wait_recv()
            return carry
        lax.fori_loop(1, chips, one, 0)

    def turned_onward(m, act, arrive):
        other = chip + 1 - 2 * (chip % 2)

        def one(d, carry):
            p = chip - d
            p = jnp.where(p < 0, p + chips, p)

            @pl.when(entry_for(p))
            def _():
                piece = ut_all.at[m, core, p]
                if arrive:
                    remote(piece, piece, ut_s.at[m, d], ut_r.at[m, d], sec, row).wait_recv()
                there = other - p
                there = jnp.where(there < 0, there + chips, there)
                act(remote(piece, piece, uw_s.at[m, d], ut_r.at[m, there], sec, 2 * other + core))

            return carry
        lax.fori_loop(1, chips, one, 0)

    def turn_inputs(m):
        for h in range(2):
            ut_own[m, pl.ds(h * half, half), :] = ub[m, h, core, centre, :].T
        mine_at = pl.ds(pl.multiple_of(team * block, block), block)
        ut_all[m, core, chip] = ut_own[m, mine_at, :]

    def send_turned(m):
        turn_inputs(m)
        turned_each(m, start)

    def turned_relay(m):
        return remote(ut_all.at[m, core], ut_all.at[m, core], uf_s.at[m], uf_r.at[m], sec, partner)

    def relay_turned(m):
        turned_arrived(m)
        turned_relay(m).start()

    def pass_on_from(begin):
        def one(m, carry):
            turned_onward(m, start, True)
            return carry
        lax.fori_loop(begin, batches, one, 0)

    def relay_all():
        def one(m, carry):
            relay_turned(m)
            return carry
        lax.fori_loop(0, batches, one, 0)

    def dz_piece(m, i, k):
        src = dzb.at[m, core, i, centre, pl.ds(pl.multiple_of(k * lanes, lanes), lanes)]
        return src, dz_all.at[m, i, pl.ds(pl.multiple_of(cols + chip * px, cols), px), :]

    def dz_each(m, i, act):
        def one(e, carry):
            q = team + e
            q = 2 * jnp.where(q >= chips // 2, q - chips // 2, q) + core
            for k in range(2):
                @pl.when((q != chip) | (k != core))
                def _():
                    src, dst = dz_piece(m, i, k)
                    act(remote(src, dst, dz_s.at[m, i, 2 * e + k], dz_r.at[m, i, chip], sec, 2 * q + k))
            return carry
        lax.fori_loop(0, chips // 2, one, 0)

    def send_dz(m, i):
        dz_each(m, i, start)

        @pl.when(chip % 2 == core)
        def _():
            dz_all[m, i, pl.ds(pl.multiple_of(cols + chip * px, cols), px), :] = dzb[
                m, core, i, centre, pl.ds(pl.multiple_of(core * lanes, lanes), lanes)
            ]

    def dz_arrived(m):
        for i in range(2):
            def one(p, carry):
                @pl.when((p != chip) | (chip % 2 != core))
                def _():
                    piece = dz_all.at[m, i, pl.ds(cols, px), :]
                    remote(piece, piece, dz_s.at[m, i, 0], dz_r.at[m, i, p], sec, row).wait_recv()
                return carry
            lax.fori_loop(0, chips, one, 0)

    def gather_taps(m):
        dz_arrived(m)
        relayed = ut_all.at[m, 1 - core]
        pltpu.make_async_copy(relayed, relayed, uf_r.at[m]).wait()
        rows = dz_all.shape[2]
        edge = lax.broadcasted_iota(jnp.int32, (1, cols, lanes), 1)
        for i in range(2):
            values = dz_all[m, i].astype(F32)
            for c, by, gone in ((0, rows - 1, cols - 1), (2, 1, 0)):
                turned = pltpu.roll(values, by, 0).reshape(rows // cols, cols, lanes)
                turned = jnp.where(edge == gone, 0.0, turned).reshape(rows, lanes)
                dz_taps[i, :, pl.ds(c * lanes, lanes)] = turned.astype(BF16)
            dz_taps[i, :, pl.ds(lanes, lanes)] = dz_all[m, i]

    def kernel_row(m, r):
        part = jnp.zeros((block, 3 * lanes), F32)
        for i in range(2):
            left = jnp.concatenate([ut_all[m, i, q] for q in range(chips)], axis=1)
            part += jnp.dot(
                left, dz_taps[i, pl.ds((2 - r) * cols, px * (strips // 2)), :], preferred_element_type=F32
            )
        return part

    def add_gradients(m):
        gather_taps(m)
        for r in range(3):
            acc_v[r] = acc_v[r] + kernel_row(m, r)

    def forward(m):
        def prepare_first(i):
            for g in range(groups):
                ub[m, core, i, group(g), :] = inside(g, inp[m, i, group(g), :])

        def prepare_later(i):
            sends = z_sends(m, sec)
            inv = prev_coef[m, pl.ds(0, 1), :]
            slant = 0.5 * inv * gain_prev[:, channels(core)]
            shift = 0.5 * shift_prev[:, channels(core)]
            level = [slant * prev_coef[m, pl.ds(1 + 3 * i + e, 1), :] + shift for e in range(3)]
            edges_arrived(sends, i)
            sends[0](i).wait_recv()
            for g in range(groups):
                gate = jnp.concatenate([mask_v[m, i, group(g), :].astype(F32)] * (half // 128), axis=1)
                halved = zin[m, i, group(g), :].astype(F32) * slant + level[kind(g)]
                turn = jnp.tanh(halved)
                bent = halved * turn
                ub[m, core, i, group(g), :] = inside(g, ((halved + bent) * gate).astype(BF16))
                if kind(g) == 1:
                    slope_prev[m, i, pl.ds((g - 1) * cols, cols), :] = (0.5 + 0.5 * turn) * (1.0 + halved - bent)

        def prepare(i):
            @pl.when(first)
            def _():
                prepare_first(i)

            @pl.when(sec > 0)
            def _():
                prepare_later(i)

        def use(i, conv):
            mean = jnp.sum(conv, 0, keepdims=True) / local
            conv = conv - mean
            stat_out[m, pl.ds(i, 1), :] = mean
            stat_out[m, pl.ds(2 + i, 1), :] = jnp.sum(conv * conv, 0, keepdims=True)
            zown[m, i, centre, :] = conv.astype(BF16)

            @pl.when(sec < sections - 1)
            def _():
                if i == 1:
                    start_stats(*down_stats, m, sec + 1, False)
                send_block(z_sends(m, sec + 1), i)

        @pl.when(first)
        def _():
            in_copy(images, m).wait()
            argument_arrived(*input_parts(images, m))

        @pl.when(sec > 0)
        def _():
            @pl.when(m == 0)
            def _():
                for copy in affine_sends():
                    copy.wait_recv()

                @pl.when(decoder)
                def _():
                    argument_arrived(*mask_parts)

            wait_stats(*down_stats, m, False)
            inv, offs = join(zin_stat, m)
            for e, value in enumerate((inv, *offs[0], *offs[1])):
                prev_coef[m, pl.ds(e, 1), :] = value

        @pl.when(m == 0)
        def _():
            for copy in w_copies():
                copy.wait()

        together, apart = convolve(ub, w_v, ux_s, ux_r, m, lambda r: r, 0, 2, prepare, use)

        @pl.when(last)
        def _():
            together()

        @pl.when(jnp.logical_not(last))
        def _():
            apart()

        start_stats(*same_stats, m, sec, True)
        for i in range(2):
            each_edge(own_edges(m), i, start)

    def finish(m):
        wait_stats(*same_stats, m, True)
        inv, offs = join(own_stat, m)
        scale = inv * gains[:, channels(core)]
        for e, value in enumerate((inv, scale, *offs[0], *offs[1])):
            own_coef[m, pl.ds(e, 1), :] = value
        slant = 0.5 * scale
        shift = 0.5 * shifts[:, channels(core)]
        level = [[slant * off + shift for off in part] for part in offs]
        for i in range(2):
            edges_arrived(own_edges(m), i)

        @pl.when(last)
        def _():
            in_copy(cotangent, m).wait()
            argument_arrived(*input_parts(cotangent, m))
            ones, crosses = [], []
            for i in range(2):
                sums = jnp.zeros((cols, half), F32)
                cross = jnp.zeros((cols, half), F32)
                for g in range(groups):
                    z = zown[m, i, group(g), :].astype(F32)
                    halved = z * slant + level[i][kind(g)]
                    turn = jnp.tanh(halved)
                    bent = halved * turn
                    dy = inp[m, i, group(g), :].astype(F32) * ((0.5 + 0.5 * turn) * (1.0 + halved - bent))
                    dyin[m, i, group(g), :] = dy.astype(BF16)
                    if kind(g) == 1:
                        out_v[m, i, pl.ds((g - 1) * cols, cols), :] = (halved + bent).astype(BF16)
                        sums += dy
                        cross += dy * z
                one = jnp.sum(sums, 0, keepdims=True)
                ones.append(one)
                crosses.append(jnp.sum(cross, 0, keepdims=True) + offs[i][1] * one)
            seed_sums[m, pl.ds(0, 1), :] = ones[0] + ones[1]
            seed_sums[m, pl.ds(1, 1), :] = inv * (crosses[0] + crosses[1])
            start_stats(*seed_stats, m, sec, True)

        @pl.when(jnp.logical_not(last))
        def _():
            for i in range(2):
                for g in range(1, groups - 1):
                    halved = zown[m, i, group(g), :].astype(F32) * slant + level[i][1]
                    out_v[m, i, pl.ds((g - 1) * cols, cols), :] = (halved + halved * jnp.tanh(halved)).astype(BF16)

        for copy in result_copies(out_v, outs, out_sem, po_s, po_r, m):
            copy.start()

    def result_copies(src, dst, sem, send, recv, m):
        here, there = pl.multiple_of(strip * core, cols), pl.multiple_of(strip * (1 - core), cols)
        place = dst.at[m, :, :, channels(core)]
        return (
            pltpu.make_async_copy(src.at[m, :, pl.ds(here, strip), :], place, sem.at[m]),
            remote(src.at[m, :, pl.ds(there, strip), :], place, send.at[m], recv.at[m], sec, partner),
        )

    def backward(m):
        @pl.when(last)
        def _():
            wait_stats(*seed_stats, m, True)

        @pl.when(jnp.logical_not(last))
        def _():
            wait_stats(*back_stats, m, False)

        first_sum = jnp.sum(dy_stat[m, :, 0, :], 0, keepdims=True)
        cross_sum = jnp.sum(dy_stat[m, :, 1, :], 0, keepdims=True)
        sums_v[core, pl.ds(0, 1), :] = sums_v[core, pl.ds(0, 1), :] + first_sum
        sums_v[core, pl.ds(1, 1), :] = sums_v[core, pl.ds(1, 1), :] + cross_sum

        def prepare(i):
            inv = own_coef[m, pl.ds(0, 1), :]
            scale = own_coef[m, pl.ds(1, 1), :]
            tilt = scale * inv * (cross_sum / total)
            base = [scale * (first_sum / total) + tilt * own_coef[m, pl.ds(2 + 3 * i + e, 1), :] for e in range(3)]
            sends = dy_sends(m, sec)

            @pl.when(jnp.logical_not(last))
            def _():
                edges_arrived(sends, i)
                sends[0](i).wait_recv()

            for g in range(groups):
                dz = dyin[m, i, group(g), :].astype(F32) * scale
                dz = dz - zown[m, i, group(g), :].astype(F32) * tilt - base[kind(g)]
                dzb[m, core, i, group(g), :] = inside(g, dz.astype(BF16))

        def then(i):
            @pl.when(first)
            def _():
                send_dz(m, i)

        def use(i, conv):
            gate = jnp.concatenate([mask_v[m, i, centre, :].astype(F32)] * (half // 128), axis=1)
            du = (conv * gate).astype(BF16)
            gin_v[m, i] = du

            @pl.when(sec > 0)
            def _():
                dy = du.astype(F32) * slope_prev[m, i]
                dyout[m, i] = dy.astype(BF16)
                one = jnp.sum(dy, 0, keepdims=True)
                cross = jnp.sum(dy * zin[m, i, centre, :].astype(F32), 0, keepdims=True)
                cross = prev_coef[m, pl.ds(0, 1), :] * (cross + prev_coef[m, pl.ds(2 + 3 * i, 1), :] * one)
                if i == 1:
                    one = one + sums_out[m, pl.ds(0, 1), :]
                    cross = cross + sums_out[m, pl.ds(1, 1), :]
                sums_out[m, pl.ds(0, 1), :] = one
                sums_out[m, pl.ds(1, 1), :] = cross
                if i == 1:
                    start_stats(*back_stats, m, sec - 1, False)
                send_block(dy_sends(m, sec - 1), i)

        together, apart = convolve(dzb, wt_v, dx_s, dx_r, m, lambda r: 2 - r, 2, 0, prepare, use, then)

        whole = first | (last & (m < batches - 1))

        @pl.when(whole)
        def _():
            together()

        @pl.when(jnp.logical_not(whole))
        def _():
            apart()

        for copy in result_copies(gin_v, grads_in, gin_sem, pg_s, pg_r, m):
            copy.start()

        @pl.when((sec > 0) & (sec < sections - 1))
        def _():
            for i in range(2):
                send_dz(m, i)

    def turn_weights():
        for copy in wt_copies():
            copy.wait()

        def one(i, carry):
            for h in range(2):
                wt_v[h, i] = wt_v[h, i].T
            return carry
        lax.fori_loop(0, 9, one, 0)

    @pl.when(late)
    def _():
        turn_weights()

    def step(t, carry):
        ahead = t - sec
        behind = t - (2 * sections - 1 - sec)

        @pl.when((ahead >= 0) & (ahead < batches))
        def _():
            forward(ahead)

        @pl.when(late & (ahead >= 0) & (ahead < batches))
        def _():
            send_turned(ahead)

        @pl.when(jnp.logical_not(late) & (ahead == batches))
        def _():
            def turned(m, carry):
                send_turned(m)
                return carry
            lax.fori_loop(0, batches, turned, 0)
            turn_weights()

        @pl.when(jnp.logical_not(late) & (ahead == batches + 1))
        def _():
            pass_on_from(0)

        @pl.when(first & (ahead == batches + 2))
        def _():
            relay_all()

        done = ahead - jnp.where(last, 0, 1)

        @pl.when((behind >= 0) & (behind < batches))
        def _():
            backward(behind)

        @pl.when((done >= 0) & (done < batches))
        def _():
            finish(done)

        @pl.when(last & (ahead >= 1) & (ahead <= batches))
        def _():
            turned_onward(ahead - 1, start, True)

        return carry

    lax.fori_loop(0, 2 * sections - 1 + batches, step, 0)

    remote(sums_v.at[core], sums_v.at[core], sv_s, sv_r, sec, partner).start()

    @pl.when(last)
    def _():
        def send(m, carry):
            for i in range(2):
                send_dz(m, i)
            return carry

        lax.fori_loop(0, batches, send, 0)

    @pl.when(late & jnp.logical_not(last))
    def _():
        pass_on_from(0)

    def relay_and_add(m, carry):
        @pl.when(jnp.logical_not(first))
        def _():
            relay_turned(m)

        @pl.when(m >= 1)
        def _():
            add_gradients(m - 1)

        return carry

    lax.fori_loop(0, batches, relay_and_add, 0)

    def swap(r, d):
        other = (seat + d) % 4
        return remote(
            swap_out.at[r, pl.ds(pl.multiple_of(other * share, share), share), :], other_parts.at[4 - d - 1, r],
            sw_s.at[r, d - 1], sw_r.at[r, 4 - d - 1], sec, 4 * team + other,
        )

    def own_copy(r):
        return pltpu.make_async_copy(
            acc_v.at[r, pl.ds(pl.multiple_of(seat * share, share), share), :], own_part.at[r], dw_sem.at[r]
        )

    gather_taps(batches - 1)
    for r in range(3):
        part = acc_v[r] + kernel_row(batches - 1, r)
        acc_v[r] = part
        swap_out[r] = part.astype(BF16)
        for d in range(1, 4):
            swap(r, d).start()
        own_copy(r).start()

    for r in range(3):
        own_copy(r).wait()
        for d in range(1, 4):
            swap(r, d).wait_send()
            swap(r, d).wait_recv()

    @pl.when(decoder)
    def _():
        argument_sent(*mask_parts)

    @pl.when(sec < sections - 1)
    def _():
        for copy in affine_sends():
            copy.wait_send()

    def sums_copy():
        return remote(sums_v.at[core], sums_v.at[core], sv_s, sv_r, sec, partner)

    sums_copy().wait_recv()
    sums_copy().wait_send()
    for h in range(2):
        shift_sum[:, pl.ds(h * half, half)] = sums_v[h, pl.ds(0, 1), :]
        gain_sum[:, pl.ds(h * half, half)] = sums_v[h, pl.ds(1, 1), :]

    def drain(m, carry):
        for src, dst, sems in ((out_v, outs, (out_sem, po_s, po_r)), (gin_v, grads_in, (gin_sem, pg_s, pg_r))):
            here, there = result_copies(src, dst, *sems, m)
            here.wait()
            there.wait_send()
            remote(
                src.at[m, :, pl.ds(0, strip), :], dst.at[m, :, :, channels(1 - core)], sems[1].at[m], sems[2].at[m],
                sec, partner,
            ).wait_recv()

        turned_each(m, sent)
        turned_onward(m, sent, False)
        turned_relay(m).wait_send()
        for i in range(2):
            dz_each(m, i, sent)
        for i in range(2):
            pass_on(ub, ux_s, ux_r, m, i).wait_send()
            pass_on(dzb, dx_s, dx_r, m, i).wait_send()

        @pl.when(first)
        def _():
            argument_sent(*input_parts(images, m))

        @pl.when(last)
        def _():
            argument_sent(*input_parts(cotangent, m))
            stats_each(*seed_stats, m, sec, True, sent)

        @pl.when(sec < sections - 1)
        def _():
            stats_each(*down_stats, m, sec + 1, False, sent)
            block_sent(z_sends(m, sec + 1))

        stats_each(*same_stats, m, sec, True, sent)
        for i in range(2):
            each_edge(own_edges(m), i, sent)

        @pl.when(sec > 0)
        def _():
            stats_each(*back_stats, m, sec - 1, False, sent)
            block_sent(dy_sends(m, sec - 1))

        return carry

    lax.fori_loop(0, batches, drain, 0)


def settle(outs, grads_in, gain_sum, shift_sum, own, others, *refs):
    targets, stages, (own_v, others_v, whole, in_sem, out_sem) = refs[:5], refs[5:9], refs[9:]
    moves = []
    for src, dst, stage in zip((outs, grads_in, gain_sum, shift_sum), targets[:4], stages):
        if len(src.shape) == 2:
            moves.append((src, dst, stage))
        else:
            moves += [(src.at[i], dst.at[i], stage.at[i]) for i in range(src.shape[0])]
    count = len(moves)
    parts = [pltpu.make_async_copy(own, own_v, in_sem.at[count])]
    parts += [pltpu.make_async_copy(others.at[d], others_v.at[d], in_sem.at[count + 1 + d]) for d in range(3)]
    ins = [pltpu.make_async_copy(src, stage, in_sem.at[i]) for i, (src, dst, stage) in enumerate(moves)]
    outs = [pltpu.make_async_copy(stage, dst, out_sem.at[i]) for i, (src, dst, stage) in enumerate(moves)]
    rows = [pltpu.make_async_copy(whole.at[r], targets[4].at[r], out_sem.at[count + r]) for r in range(3)]
    for copy in parts + ins:
        copy.start()
    for copy in parts:
        copy.wait()
    seat = lax.axis_index("rows") % 4
    lanes = whole.shape[3] // 4
    for r in range(3):
        for d in range(4):
            at = pl.ds(pl.multiple_of(((seat + d) % 4) * lanes, lanes), lanes)
            for c in range(3):
                part = pl.ds(c * lanes, lanes)
                whole[r, c, :, at] = own_v[r, :, part] if d == 0 else others_v[d - 1, r, :, part].astype(F32)
        rows[r].start()
    for come, go in zip(ins, outs):
        come.wait()
        go.start()
    for copy in outs + rows:
        copy.wait()


def body(images, switches, conv_weights, gains, shifts, cotangent):
    sections = lax.axis_size("section")
    strips = lax.axis_size("rows")
    batches, pictures, strip_rows, cols, ch = images.shape
    strip = strip_rows * cols
    px = 2 * strip
    tall = px + 2 * cols
    anywhere = pl.BlockSpec(memory_space=pl.ANY)
    vmem = pl.BlockSpec(memory_space=pltpu.VMEM)
    dma = pltpu.SemaphoreType.DMA
    flops = 3 * 2 * 9 * ch * ch * batches * px
    share = ch // strips
    chips = strips // 2
    outs, grads_in, own, others, gain_sum, shift_sum = pl.pallas_call(
        functools.partial(kernel, sections, strips, cols),
        out_shape=(
            jax.ShapeDtypeStruct((batches, pictures, strip, ch), BF16),
            jax.ShapeDtypeStruct((batches, pictures, strip, ch), BF16),
            jax.ShapeDtypeStruct((3, share, 3 * ch // 4), F32),
            jax.ShapeDtypeStruct((3, 3, share, 3 * ch // 4), BF16),
            jax.ShapeDtypeStruct((1, ch), F32),
            jax.ShapeDtypeStruct((1, ch), F32),
        ),
        in_specs=[anywhere, anywhere, anywhere, vmem, vmem, vmem],
        out_specs=(anywhere,) * 4 + (vmem, vmem),
        scratch_shapes=[
            pltpu.VMEM((2, 9, ch // 2, ch // 2), BF16),
            pltpu.VMEM((2, 9, ch // 2, ch // 2), BF16),
            pltpu.VMEM((batches, 2, tall, ch // 2), BF16),
            pltpu.VMEM((batches, 2, strip, 128), BF16),
            pltpu.VMEM((batches, 2, tall, 128), BF16),
            pltpu.VMEM((1, ch), F32),
            pltpu.VMEM((1, ch), F32),
            pltpu.VMEM((batches, 2, tall, ch // 2), BF16),
            pltpu.VMEM((batches, chips, 4, ch // 2), F32),
            pltpu.VMEM((batches, 2, tall, ch // 2), BF16),
            pltpu.VMEM((batches, chips, 4, ch // 2), F32),
            pltpu.VMEM((batches, 2, 2, tall, ch // 2), BF16),
            pltpu.VMEM((batches, 2, px, ch // 2), F32),
            pltpu.VMEM((batches, 8, ch // 2), F32),
            pltpu.VMEM((batches, 8, ch // 2), F32),
            pltpu.VMEM((batches, 2, tall, ch // 2), BF16),
            pltpu.VMEM((batches, chips, 2, ch // 2), F32),
            pltpu.VMEM((batches, 2, 2, tall, ch // 2), BF16),
            pltpu.VMEM((batches, 2, px, ch // 2), BF16),
            pltpu.VMEM((3, 2 * px, ch // 2), F32),
            pltpu.VMEM((2, 2, ch // 2), F32),
            pltpu.VMEM((batches, 4, ch // 2), F32),
            pltpu.VMEM((batches, 2, ch // 2), F32),
            pltpu.VMEM((batches, 2, ch // 2), F32),
            pltpu.VMEM((batches, 2, px, ch // 2), BF16),
            pltpu.VMEM((batches, 2, px, ch // 2), BF16),
            pltpu.VMEM((batches, ch, px), BF16),
            pltpu.VMEM((batches, 2, strips // 2, 4 * share, px), BF16),
            pltpu.VMEM((batches, 2, px * strips // 2 + 2 * cols, ch // 4), BF16),
            pltpu.VMEM((2, px * strips // 2 + 2 * cols, 3 * ch // 4), BF16),
            pltpu.VMEM((3, 4 * share, 3 * ch // 4), F32),
            pltpu.VMEM((3, 4 * share, 3 * ch // 4), BF16),
            dma((2,)), dma((2,)),
            dma((batches,)),
            dma((batches,)), dma((batches,)),
            dma((batches, 2)), dma((batches, 2)),
            dma, dma,
            dma((2,)), dma((2,)),
            dma((2,)), dma((2,)),
            dma((batches, 2)), dma((batches, 2)),
            dma((batches, 2)), dma((batches, 2)),
            dma, dma,
            dma((batches, 3, 2)), dma((batches, 3, 2)),
            dma((batches, chips)), dma((batches, chips)),
            dma((batches, 3, 2)), dma((batches, 3, 2)),
            dma((batches, chips)), dma((batches, chips)),
            dma((batches, 3, 2)), dma((batches, 3, 2)),
            dma((batches, chips)), dma((batches, chips)),
            dma((batches, chips)),
            dma((batches,)), dma((batches,)), dma((batches,)),
            dma((batches,)), dma((batches,)), dma((batches,)),
            dma((batches, chips)), dma((batches, chips)), dma((batches, chips)),
            dma((batches,)), dma((batches,)),
            dma((batches, 2, chips)), dma((batches, 2, chips)),
            dma((3, 3)), dma((3, 3)),
            dma((3,)),
        ],
        compiler_params=pltpu.CompilerParams(
            collective_id=0, has_side_effects=True, vmem_limit_bytes=56 * 2**20
        ),
        cost_estimate=pl.CostEstimate(
            flops=flops, bytes_accessed=2 * 9 * ch * ch * 2, transcendentals=0
        ),
    )(
        images.reshape(batches, pictures, strip, ch),
        cotangent.reshape(batches, pictures, strip, ch),
        conv_weights.reshape(9, ch, ch),
        gains,
        shifts,
        switches.reshape(-1, switches.shape[-1]),
    )
    results = (outs, grads_in, gain_sum, shift_sum)
    whole = jax.ShapeDtypeStruct((3, 3, share, ch), F32)
    outs, grads_in, gain_sum, shift_sum, weight_grad = pl.pallas_call(
        settle,
        out_shape=tuple(jax.ShapeDtypeStruct(r.shape, r.dtype) for r in results) + (whole,),
        in_specs=[anywhere] * 6,
        out_specs=(anywhere,) * 5,
        scratch_shapes=[pltpu.VMEM(r.shape, r.dtype) for r in results]
        + [
            pltpu.VMEM(own.shape, F32),
            pltpu.VMEM(others.shape, BF16),
            pltpu.VMEM(whole.shape, F32),
            dma((2 * batches + 6,)),
            dma((2 * batches + 5,)),
        ],
        compiler_params=pltpu.CompilerParams(vmem_limit_bytes=60 * 2**20),
    )(*results, own, others)
    shape = (1, batches, pictures, strip_rows, cols, ch)
    return (outs.reshape(shape), grads_in.reshape(shape), weight_grad[None], gain_sum, shift_sum)


def solution(mesh):
    return jax.shard_map(
        body,
        mesh=mesh,
        in_specs=(
            P(None, None, "rows", None, None),
            P(None, None, "rows", None),
            P("section", None, None, None, None),
            P("section", None),
            P("section", None),
            P(None, None, "rows", None, None),
        ),
        out_specs=(
            P("section", None, None, "rows", None, None),
            P("section", None, None, "rows", None, None),
            P("section", None, None, "rows", None),
            P("section", None),
            P("section", None),
        ),
        check_vma=False,
    )
```

```python
import functools

import jax
import jax.numpy as jnp
from jax import lax
from jax.experimental import pallas as pl
from jax.experimental.pallas import tpu as pltpu
from jax.sharding import PartitionSpec as P

EPSILON = 1e-05
MESH = pl.DeviceIdType.MESH
BF16 = jnp.bfloat16
F32 = jnp.float32


def kernel(
    sections, strips, cols,
    images, cotangent, weights, gains, shifts, switches,
    outs, grads_in, own_part, other_parts, gain_sum, shift_sum,
    w_v, wt_v, inp, mask_own, mask_v, gain_prev, shift_prev, zin, zin_stat, zown, own_stat, ub, slope_prev,
    prev_coef, own_coef, dyin, dy_stat, dzb, dyout, product_v, sums_v, stat_out, sums_out, seed_sums, out_v, gin_v,
    ut_own, ut_all, dz_all, dz_taps, acc_v, swap_out,
    w_sem, wt_sem, in_sem, pi_s, pi_r, ie_s, ie_r, mp_s, mp_r, me_s, me_r, gp_s, gp_r,
    ux_s, ux_r, dx_s, dx_r, sv_s, sv_r,
    fz_s, fz_r, fs_s, fs_r, oe_s, oe_r, os_s, os_r, bz_s, bz_r, bs_s, bs_r, ls_s,
    out_sem, po_s, po_r, gin_sem, pg_s, pg_r,
    ut_s, ut_r, uw_s, uf_s, uf_r, dz_s, dz_r, sw_s, sw_r, dw_sem,
):
    sec = lax.axis_index("section")
    row = lax.axis_index("rows")
    batches, _, tall, half = inp.shape
    ch = 2 * half
    px = tall - 2 * cols
    strip = px // 2
    groups = tall // cols
    chips = strips // 2
    local = float(px)
    total = 2.0 * local * chips
    first, last, decoder = sec == 0, sec == sections - 1, sec == sections // 2
    late = sec >= sections // 2
    core = row % 2
    partner = row + 1 - 2 * core
    has_up, has_down = row >= 2, row < strips - 2
    centre = pl.ds(cols, px)
    chip = row // 2
    team, seat = row // 4, row % 4
    lanes = dz_all.shape[3]
    block = ut_all.shape[3]
    share = block // 4
    mine = pl.multiple_of(cols + strip * core, cols)

    def channels(h):
        return pl.ds(pl.multiple_of(h * half, half), half)

    def w_copies():
        return [
            pltpu.make_async_copy(weights.at[:, channels(h), channels(core)], w_v.at[h], w_sem.at[h]) for h in range(2)
        ]

    def wt_copies():
        return [
            pltpu.make_async_copy(weights.at[:, channels(core), channels(h)], wt_v.at[h], wt_sem.at[h]) for h in range(2)
        ]

    def in_copy(src, m):
        return pltpu.make_async_copy(src.at[m, :, :, channels(core)], inp.at[m, :, pl.ds(mine, strip), :], in_sem.at[m])

    for copy in w_copies() + wt_copies():
        copy.start()

    @pl.when(first)
    def _():
        for m in range(batches):
            in_copy(images, m).start()

    @pl.when(last)
    def _():
        for m in range(batches):
            in_copy(cotangent, m).start()

    barrier = pltpu.get_barrier_semaphore()
    for s in range(sections):
        @pl.when((sec >= s - 1) & (sec <= s + 1))
        def _():
            def greet(i, carry):
                @pl.when((s != sec) | (i != row))
                def _():
                    pl.semaphore_signal(barrier, inc=1, device_id=(jnp.int32(s), i), device_id_type=MESH)
                return carry
            lax.fori_loop(0, strips, greet, 0)

    acc_v[...] = jnp.zeros_like(acc_v)
    sums_v[...] = jnp.zeros_like(sums_v)

    for m in range(batches):
        for i in range(2):
            for at in (0, dz_all.shape[2] - cols):
                dz_all[m, i, pl.ds(at, cols), :] = jnp.zeros((cols, lanes), BF16)

    @pl.when(decoder)
    def _():
        wide = cols // 2
        windows_at = lax.broadcasted_iota(jnp.int32, (cols, wide), 1)
        places = lax.broadcasted_iota(jnp.int32, (cols, wide), 0)
        pick = (lax.shift_right_logical(places, 1) == windows_at).astype(F32)
        table = lax.dot_general(
            pick, switches[...].astype(F32), (((1,), (1,)), ((), ())), preferred_element_type=F32
        )
        odd = jnp.bitwise_and(lax.broadcasted_iota(jnp.int32, (cols, 128), 0), 1).astype(F32)
        windows = strip // cols // 2
        for m in range(batches):
            for i in range(2):
                for w in range(windows):
                    at = (m * 2 + i) * windows + w
                    value = jnp.broadcast_to(table[:, at : at + 1], (cols, 128))
                    for p in range(2):
                        hit = (jnp.abs(value - (2.0 * p + odd)) < 0.5).astype(F32).astype(BF16)
                        mask_own[m, i, pl.ds((2 * w + p) * cols, cols), :] = hit
        for m in range(batches):
            mask_v[m, :, pl.ds(mine, strip), :] = mask_own[m]

    @pl.when(jnp.logical_not(decoder))
    def _():
        mask_v[...] = jnp.ones_like(mask_v)

    near = 1 + jnp.where(sec > 0, 1, 0) + jnp.where(sec < sections - 1, 1, 0)
    pl.semaphore_wait(barrier, near * strips - 1)

    def remote(src, dst, send, recv, s, i):
        return pltpu.make_async_remote_copy(
            src_ref=src, dst_ref=dst, send_sem=send, recv_sem=recv, device_id=(s, i), device_id_type=MESH
        )

    def to_partner(src_at, dst_at, send, recv):
        return remote(src_at(1 - core), dst_at(pl.ds(mine, strip)), send, recv, sec, partner)

    def start_argument(src_at, dst_at, pair_sems, edge_sems):
        to_partner(src_at, dst_at, *pair_sems).start()

        @pl.when((core == 1) & has_down)
        def _():
            for i in range(2):
                remote(
                    src_at(i, pl.ds(strip - cols, cols)), dst_at(pl.ds(0, cols)),
                    edge_sems[0].at[i], edge_sems[1].at[0], sec, row + 1 + i,
                ).start()

        @pl.when((core == 0) & has_up)
        def _():
            for i in range(2):
                remote(
                    src_at(i, pl.ds(0, cols)), dst_at(pl.ds(cols + px, cols)),
                    edge_sems[0].at[i], edge_sems[1].at[1], sec, row - 2 + i,
                ).start()

    def argument_arrived(src_at, dst_at, pair_sems, edge_sems):
        to_partner(src_at, dst_at, *pair_sems).wait_recv()

        @pl.when(has_up)
        def _():
            remote(
                src_at(0, pl.ds(0, cols)), dst_at(pl.ds(0, cols)), edge_sems[0].at[0], edge_sems[1].at[0], sec, row
            ).wait_recv()

        @pl.when(has_down)
        def _():
            remote(
                src_at(0, pl.ds(0, cols)), dst_at(pl.ds(cols + px, cols)), edge_sems[0].at[0], edge_sems[1].at[1],
                sec, row,
            ).wait_recv()

    def argument_sent(src_at, dst_at, pair_sems, edge_sems):
        to_partner(src_at, dst_at, *pair_sems).wait_send()

        @pl.when(((core == 1) & has_down) | ((core == 0) & has_up))
        def _():
            for i in range(2):
                remote(
                    src_at(i, pl.ds(0, cols)), dst_at(pl.ds(0, cols)), edge_sems[0].at[i], edge_sems[1].at[0], sec, row
                ).wait_send()

    def input_parts(src, m):
        return (
            lambda i, r=pl.ds(0, strip): src.at[m, :, r, channels(i)],
            lambda r: inp.at[m, :, r, :],
            (pi_s.at[m], pi_r.at[m]),
            (ie_s.at[m], ie_r.at[m]),
        )

    mask_parts = (
        lambda i, r=pl.ds(0, strip): mask_own.at[:, :, r, :],
        lambda r: mask_v.at[:, :, r, :],
        (mp_s, mp_r),
        (me_s, me_r),
    )

    @pl.when(first)
    def _():
        for m in range(batches):
            start_argument(*input_parts(images, m))

    @pl.when(last)
    def _():
        for m in range(batches):
            start_argument(*input_parts(cotangent, m))

    @pl.when(decoder)
    def _():
        start_argument(*mask_parts)

    def affine_sends():
        return (
            remote(gains, gain_prev, gp_s.at[0], gp_r.at[0], sec + 1, row),
            remote(shifts, shift_prev, gp_s.at[1], gp_r.at[1], sec + 1, row),
        )

    @pl.when(sec < sections - 1)
    def _():
        for copy in affine_sends():
            copy.start()

    def block_sends(src, src_from, dst, send, recv, m, s):
        def piece(k, src_row, dst_row, rows, to):
            def one(i):
                return remote(
                    src.at[m, i, pl.ds(src_from + src_row, rows), :], dst.at[m, i, pl.ds(dst_row, rows), :],
                    send.at[m, k, i], recv.at[m, k, i], s, to,
                )
            return one

        return (
            piece(0, 0, cols, px, row), piece(1, px - cols, 0, cols, row + 2), piece(2, 0, cols + px, cols, row - 2)
        )

    def each_edge(parts, i, act):
        _, to_down, to_up = parts

        @pl.when(has_down)
        def _():
            act(to_down(i))

        @pl.when(has_up)
        def _():
            act(to_up(i))

    def edges_arrived(parts, i):
        _, to_down, to_up = parts

        @pl.when(has_up)
        def _():
            to_down(i).wait_recv()

        @pl.when(has_down)
        def _():
            to_up(i).wait_recv()

    def send_block(parts, i):
        each_edge(parts, i, start)
        parts[0](i).start()

    def block_sent(parts):
        for i in range(2):
            each_edge(parts, i, sent)
            parts[0](i).wait_send()

    def start(copy):
        copy.start()

    def sent(copy):
        copy.wait_send()

    def came(copy):
        copy.wait_recv()

    def z_sends(m, s):
        return block_sends(zown, cols, zin, fz_s, fz_r, m, s)

    def own_edges(m):
        return block_sends(zown, cols, zown, oe_s, oe_r, m, sec)

    def dy_sends(m, s):
        return block_sends(dyout, 0, dyin, bz_s, bz_r, m, s)

    def stats_each(src, dst, send, recv, m, s, same, act):
        def one(d, carry):
            q = chip + d
            q = jnp.where(q >= chips, q - chips, q)
            act(remote(src.at[m], dst.at[m, chip], send.at[m, d], recv.at[m, d], s, 2 * q + core))
            return carry
        lax.fori_loop(1 if same else 0, chips, one, 0)

    def start_stats(src, dst, send, recv, m, s, same):
        stats_each(src, dst, send, recv, m, s, same, start)
        if same:
            dst[m, chip] = src[m]

    def wait_stats(src, dst, send, recv, m, same):
        stats_each(src, dst, send, recv, m, sec, same, came)

    down_stats = (stat_out, zin_stat, fs_s, fs_r)
    same_stats = (stat_out, own_stat, os_s, os_r)
    back_stats = (sums_out, dy_stat, bs_s, bs_r)
    seed_stats = (seed_sums, dy_stat, ls_s, bs_r)

    def join(stats_ref, m):
        means = stats_ref[m, :, 0, :], stats_ref[m, :, 1, :]
        mean = jnp.sum(means[0] + means[1], 0, keepdims=True) / (2.0 * chips)
        off = [part - mean for part in means]
        squares = jnp.sum(stats_ref[m, :, 2, :] + stats_ref[m, :, 3, :], 0, keepdims=True)
        apart = jnp.sum(off[0] * off[0] + off[1] * off[1], 0, keepdims=True)
        at = (jnp.maximum(chip - 1, 0), chip, jnp.minimum(chip + 1, chips - 1))
        offs = [[stats_ref[m, q, pl.ds(i, 1), :] - mean for q in at] for i in range(2)]
        return lax.rsqrt((squares + local * apart) / total + EPSILON), offs

    def kind(g):
        return 0 if g == 0 else 2 if g == groups - 1 else 1

    def inside(g, values):
        if kind(g) == 1:
            return values
        return jnp.where(has_up if kind(g) == 0 else has_down, values, jnp.zeros_like(values))

    def group(g):
        return pl.ds(g * cols, cols)

    column = lax.broadcasted_iota(jnp.int32, (1, cols, half), 1)

    def taps_joined(parts, left, right):
        rows = parts[0].shape[0]

        def moved(values, by, edge):
            turned = pltpu.roll(values, by % rows, 0).reshape(rows // cols, cols, half)
            return jnp.where(column == edge, 0.0, turned).reshape(rows, half)
        return parts[1] + moved(parts[left], 1, 0) + moved(parts[right], -1, cols - 1)

    def pass_on(operand, send, recv, m, i):
        return remote(operand.at[m, core, i], operand.at[m, core, i], send.at[m, i], recv.at[m, i], sec, partner)

    def products(operand, w, m, h, r_at, images_at):
        rows = images_at.size * px

        def one(c):
            acc = jnp.zeros((rows, half), F32)
            for r in range(3):
                left = operand[m, h, images_at, pl.ds(r_at(r) * cols, px), :].reshape(rows, half)
                acc += jnp.dot(left, w[h, 3 * r + c], preferred_element_type=F32)
            return acc
        return one

    def convolve(operand, w, send, recv, m, r_at, left, right, prepare, use, after=lambda i: None):
        def part(images_at, wait_for):
            rows = pl.ds(0, images_at.size * px)
            mine_first = products(operand, w, m, core, r_at, images_at)
            for c in range(3):
                product_v[c, rows, :] = mine_first(c)
            for i in wait_for:
                pass_on(operand, send, recv, m, i).wait_recv()
            then = products(operand, w, m, 1 - core, r_at, images_at)
            return taps_joined([product_v[c, rows, :] + then(c) for c in range(3)], left, right)

        def ready(i):
            prepare(i)
            pass_on(operand, send, recv, m, i).start()
            after(i)

        def together():
            for i in range(2):
                ready(i)
            whole = part(pl.ds(0, 2), range(2))
            for i in range(2):
                use(i, whole[i * px : (i + 1) * px])

        def apart():
            for i in range(2):
                ready(i)
                use(i, part(pl.ds(i, 1), [i]))

        return together, apart

    def turned_copy(m, q):
        src = ut_own.at[m, pl.ds(pl.multiple_of((q // 2) * block, block), block), :]
        return src, ut_all.at[m, core, chip]


    def turned_each(m, act):
        def one(d, carry):
            q = chip + d
            q = jnp.where(q >= chips, q - chips, q)
            its_team = q // 2
            nearest = 2 * its_team + jnp.where(chip > q, 1, 0)

            @pl.when((its_team == team) | (q == nearest))
            def _():
                src, dst = turned_copy(m, q)
                act(remote(src, dst, ut_s.at[m, d], ut_r.at[m, d], sec, 2 * q + core))
            return carry
        lax.fori_loop(1, chips, one, 0)

    def entry_for(p):
        return (p // 2 != team) & (jnp.where(p > chip, 1, 0) == chip % 2)

    def turned_arrived(m):
        def one(d, carry):
            p = chip - d
            p = jnp.where(p < 0, p + chips, p)

            @pl.when(jnp.logical_not(entry_for(p)))
            def _():
                piece = ut_all.at[m, core, p]
                remote(piece, piece, ut_s.at[m, d], ut_r.at[m, d], sec, row).wait_recv()
            return carry
        lax.fori_loop(1, chips, one, 0)

    def turned_onward(m, act, arrive):
        other = chip + 1 - 2 * (chip % 2)

        def one(d, carry):
            p = chip - d
            p = jnp.where(p < 0, p + chips, p)

            @pl.when(entry_for(p))
            def _():
                piece = ut_all.at[m, core, p]
                if arrive:
                    remote(piece, piece, ut_s.at[m, d], ut_r.at[m, d], sec, row).wait_recv()
                there = other - p
                there = jnp.where(there < 0, there + chips, there)
                act(remote(piece, piece, uw_s.at[m, d], ut_r.at[m, there], sec, 2 * other + core))

            return carry
        lax.fori_loop(1, chips, one, 0)

    def turn_inputs(m):
        for h in range(2):
            ut_own[m, pl.ds(h * half, half), :] = ub[m, h, core, centre, :].T
        mine_at = pl.ds(pl.multiple_of(team * block, block), block)
        ut_all[m, core, chip] = ut_own[m, mine_at, :]

    def send_turned(m):
        turn_inputs(m)
        turned_each(m, start)

    def turned_relay(m):
        return remote(ut_all.at[m, core], ut_all.at[m, core], uf_s.at[m], uf_r.at[m], sec, partner)

    def relay_turned(m):
        turned_arrived(m)
        turned_relay(m).start()

    def pass_on_from(begin):
        def one(m, carry):
            turned_onward(m, start, True)
            return carry
        lax.fori_loop(begin, batches, one, 0)

    def relay_all():
        def one(m, carry):
            relay_turned(m)
            return carry
        lax.fori_loop(0, batches, one, 0)

    def dz_piece(m, i, k):
        src = dzb.at[m, core, i, centre, pl.ds(pl.multiple_of(k * lanes, lanes), lanes)]
        return src, dz_all.at[m, i, pl.ds(pl.multiple_of(cols + chip * px, cols), px), :]

    def dz_each(m, i, act):
        def one(e, carry):
            q = team + e
            q = 2 * jnp.where(q >= chips // 2, q - chips // 2, q) + core
            for k in range(2):
                @pl.when((q != chip) | (k != core))
                def _():
                    src, dst = dz_piece(m, i, k)
                    act(remote(src, dst, dz_s.at[m, i, 2 * e + k], dz_r.at[m, i, chip], sec, 2 * q + k))
            return carry
        lax.fori_loop(0, chips // 2, one, 0)

    def send_dz(m, i):
        dz_each(m, i, start)

        @pl.when(chip % 2 == core)
        def _():
            dz_all[m, i, pl.ds(pl.multiple_of(cols + chip * px, cols), px), :] = dzb[
                m, core, i, centre, pl.ds(pl.multiple_of(core * lanes, lanes), lanes)
            ]

    def dz_arrived(m):
        for i in range(2):
            def one(p, carry):
                @pl.when((p != chip) | (chip % 2 != core))
                def _():
                    piece = dz_all.at[m, i, pl.ds(cols, px), :]
                    remote(piece, piece, dz_s.at[m, i, 0], dz_r.at[m, i, p], sec, row).wait_recv()
                return carry
            lax.fori_loop(0, chips, one, 0)

    def gather_taps(m):
        dz_arrived(m)
        relayed = ut_all.at[m, 1 - core]
        pltpu.make_async_copy(relayed, relayed, uf_r.at[m]).wait()
        rows = dz_all.shape[2]
        edge = lax.broadcasted_iota(jnp.int32, (1, cols, lanes), 1)
        for i in range(2):
            values = dz_all[m, i].astype(F32)
            for c, by, gone in ((0, rows - 1, cols - 1), (2, 1, 0)):
                turned = pltpu.roll(values, by, 0).reshape(rows // cols, cols, lanes)
                turned = jnp.where(edge == gone, 0.0, turned).reshape(rows, lanes)
                dz_taps[i, :, pl.ds(c * lanes, lanes)] = turned.astype(BF16)
            dz_taps[i, :, pl.ds(lanes, lanes)] = dz_all[m, i]

    def kernel_row(m, r):
        part = jnp.zeros((block, 3 * lanes), F32)
        for i in range(2):
            left = jnp.concatenate([ut_all[m, i, q] for q in range(chips)], axis=1)
            part += jnp.dot(
                left, dz_taps[i, pl.ds((2 - r) * cols, px * (strips // 2)), :], preferred_element_type=F32
            )
        return part

    def add_gradients(m):
        gather_taps(m)
        for r in range(3):
            acc_v[r] = acc_v[r] + kernel_row(m, r)

    def forward(m):
        def prepare_first(i):
            for g in range(groups):
                ub[m, core, i, group(g), :] = inside(g, inp[m, i, group(g), :])

        def prepare_later(i):
            sends = z_sends(m, sec)
            inv = prev_coef[m, pl.ds(0, 1), :]
            slant = 0.5 * inv * gain_prev[:, channels(core)]
            shift = 0.5 * shift_prev[:, channels(core)]
            level = [slant * prev_coef[m, pl.ds(1 + 3 * i + e, 1), :] + shift for e in range(3)]
            edges_arrived(sends, i)
            sends[0](i).wait_recv()
            for g in range(groups):
                gate = jnp.concatenate([mask_v[m, i, group(g), :].astype(F32)] * (half // 128), axis=1)
                halved = zin[m, i, group(g), :].astype(F32) * slant + level[kind(g)]
                turn = jnp.tanh(halved)
                bent = halved * turn
                ub[m, core, i, group(g), :] = inside(g, ((halved + bent) * gate).astype(BF16))
                if kind(g) == 1:
                    slope_prev[m, i, pl.ds((g - 1) * cols, cols), :] = (0.5 + 0.5 * turn) * (1.0 + halved - bent)

        def prepare(i):
            @pl.when(first)
            def _():
                prepare_first(i)

            @pl.when(sec > 0)
            def _():
                prepare_later(i)

        def use(i, conv):
            mean = jnp.sum(conv, 0, keepdims=True) / local
            conv = conv - mean
            stat_out[m, pl.ds(i, 1), :] = mean
            stat_out[m, pl.ds(2 + i, 1), :] = jnp.sum(conv * conv, 0, keepdims=True)
            zown[m, i, centre, :] = conv.astype(BF16)

            @pl.when(sec < sections - 1)
            def _():
                if i == 1:
                    start_stats(*down_stats, m, sec + 1, False)
                send_block(z_sends(m, sec + 1), i)

        @pl.when(first)
        def _():
            in_copy(images, m).wait()
            argument_arrived(*input_parts(images, m))

        @pl.when(sec > 0)
        def _():
            @pl.when(m == 0)
            def _():
                for copy in affine_sends():
                    copy.wait_recv()

                @pl.when(decoder)
                def _():
                    argument_arrived(*mask_parts)

            wait_stats(*down_stats, m, False)
            inv, offs = join(zin_stat, m)
            for e, value in enumerate((inv, *offs[0], *offs[1])):
                prev_coef[m, pl.ds(e, 1), :] = value

        @pl.when(m == 0)
        def _():
            for copy in w_copies():
                copy.wait()

        together, apart = convolve(ub, w_v, ux_s, ux_r, m, lambda r: r, 0, 2, prepare, use)

        @pl.when(last)
        def _():
            together()

        @pl.when(jnp.logical_not(last))
        def _():
            apart()

        start_stats(*same_stats, m, sec, True)
        for i in range(2):
            each_edge(own_edges(m), i, start)

    def finish(m):
        wait_stats(*same_stats, m, True)
        inv, offs = join(own_stat, m)
        scale = inv * gains[:, channels(core)]
        for e, value in enumerate((inv, scale, *offs[0], *offs[1])):
            own_coef[m, pl.ds(e, 1), :] = value
        slant = 0.5 * scale
        shift = 0.5 * shifts[:, channels(core)]
        level = [[slant * off + shift for off in part] for part in offs]
        for i in range(2):
            edges_arrived(own_edges(m), i)

        @pl.when(last)
        def _():
            in_copy(cotangent, m).wait()
            argument_arrived(*input_parts(cotangent, m))
            ones, crosses = [], []
            for i in range(2):
                sums = jnp.zeros((cols, half), F32)
                cross = jnp.zeros((cols, half), F32)
                for g in range(groups):
                    z = zown[m, i, group(g), :].astype(F32)
                    halved = z * slant + level[i][kind(g)]
                    turn = jnp.tanh(halved)
                    bent = halved * turn
                    dy = inp[m, i, group(g), :].astype(F32) * ((0.5 + 0.5 * turn) * (1.0 + halved - bent))
                    dyin[m, i, group(g), :] = dy.astype(BF16)
                    if kind(g) == 1:
                        out_v[m, i, pl.ds((g - 1) * cols, cols), :] = (halved + bent).astype(BF16)
                        sums += dy
                        cross += dy * z
                one = jnp.sum(sums, 0, keepdims=True)
                ones.append(one)
                crosses.append(jnp.sum(cross, 0, keepdims=True) + offs[i][1] * one)
            seed_sums[m, pl.ds(0, 1), :] = ones[0] + ones[1]
            seed_sums[m, pl.ds(1, 1), :] = inv * (crosses[0] + crosses[1])
            start_stats(*seed_stats, m, sec, True)

        @pl.when(jnp.logical_not(last))
        def _():
            for i in range(2):
                for g in range(1, groups - 1):
                    halved = zown[m, i, group(g), :].astype(F32) * slant + level[i][1]
                    out_v[m, i, pl.ds((g - 1) * cols, cols), :] = (halved + halved * jnp.tanh(halved)).astype(BF16)

        for copy in result_copies(out_v, outs, out_sem, po_s, po_r, m):
            copy.start()

    def result_copies(src, dst, sem, send, recv, m):
        here, there = pl.multiple_of(strip * core, cols), pl.multiple_of(strip * (1 - core), cols)
        place = dst.at[m, :, :, channels(core)]
        return (
            pltpu.make_async_copy(src.at[m, :, pl.ds(here, strip), :], place, sem.at[m]),
            remote(src.at[m, :, pl.ds(there, strip), :], place, send.at[m], recv.at[m], sec, partner),
        )

    def backward(m):
        @pl.when(last)
        def _():
            wait_stats(*seed_stats, m, True)

        @pl.when(jnp.logical_not(last))
        def _():
            wait_stats(*back_stats, m, False)

        first_sum = jnp.sum(dy_stat[m, :, 0, :], 0, keepdims=True)
        cross_sum = jnp.sum(dy_stat[m, :, 1, :], 0, keepdims=True)
        sums_v[core, pl.ds(0, 1), :] = sums_v[core, pl.ds(0, 1), :] + first_sum
        sums_v[core, pl.ds(1, 1), :] = sums_v[core, pl.ds(1, 1), :] + cross_sum

        def prepare(i):
            inv = own_coef[m, pl.ds(0, 1), :]
            scale = own_coef[m, pl.ds(1, 1), :]
            tilt = scale * inv * (cross_sum / total)
            base = [scale * (first_sum / total) + tilt * own_coef[m, pl.ds(2 + 3 * i + e, 1), :] for e in range(3)]
            sends = dy_sends(m, sec)

            @pl.when(jnp.logical_not(last))
            def _():
                edges_arrived(sends, i)
                sends[0](i).wait_recv()

            for g in range(groups):
                dz = dyin[m, i, group(g), :].astype(F32) * scale
                dz = dz - zown[m, i, group(g), :].astype(F32) * tilt - base[kind(g)]
                dzb[m, core, i, group(g), :] = inside(g, dz.astype(BF16))

        def then(i):
            @pl.when(first)
            def _():
                send_dz(m, i)

        def use(i, conv):
            gate = jnp.concatenate([mask_v[m, i, centre, :].astype(F32)] * (half // 128), axis=1)
            du = (conv * gate).astype(BF16)
            gin_v[m, i] = du

            @pl.when(sec > 0)
            def _():
                dy = du.astype(F32) * slope_prev[m, i]
                dyout[m, i] = dy.astype(BF16)
                one = jnp.sum(dy, 0, keepdims=True)
                cross = jnp.sum(dy * zin[m, i, centre, :].astype(F32), 0, keepdims=True)
                cross = prev_coef[m, pl.ds(0, 1), :] * (cross + prev_coef[m, pl.ds(2 + 3 * i, 1), :] * one)
                if i == 1:
                    one = one + sums_out[m, pl.ds(0, 1), :]
                    cross = cross + sums_out[m, pl.ds(1, 1), :]
                sums_out[m, pl.ds(0, 1), :] = one
                sums_out[m, pl.ds(1, 1), :] = cross
                if i == 1:
                    start_stats(*back_stats, m, sec - 1, False)
                send_block(dy_sends(m, sec - 1), i)

        together, apart = convolve(dzb, wt_v, dx_s, dx_r, m, lambda r: 2 - r, 2, 0, prepare, use, then)

        whole = first | (last & (m < batches - 1))

        @pl.when(whole)
        def _():
            together()

        @pl.when(jnp.logical_not(whole))
        def _():
            apart()

        for copy in result_copies(gin_v, grads_in, gin_sem, pg_s, pg_r, m):
            copy.start()

        @pl.when((sec > 0) & (sec < sections - 1))
        def _():
            for i in range(2):
                send_dz(m, i)

    def turn_weights():
        for copy in wt_copies():
            copy.wait()

        def one(i, carry):
            for h in range(2):
                wt_v[h, i] = wt_v[h, i].T
            return carry
        lax.fori_loop(0, 9, one, 0)

    @pl.when(late)
    def _():
        turn_weights()

    def step(t, carry):
        ahead = t - sec
        behind = t - (2 * sections - 1 - sec)

        @pl.when((ahead >= 0) & (ahead < batches))
        def _():
            forward(ahead)

        @pl.when(late & (ahead >= 0) & (ahead < batches))
        def _():
            send_turned(ahead)

        @pl.when(jnp.logical_not(late) & (ahead == batches))
        def _():
            def turned(m, carry):
                send_turned(m)
                return carry
            lax.fori_loop(0, batches, turned, 0)
            turn_weights()

        @pl.when(jnp.logical_not(late) & (ahead == batches + 1))
        def _():
            pass_on_from(0)

        @pl.when(first & (ahead == batches + 2))
        def _():
            relay_all()

        done = ahead - jnp.where(last, 0, 1)

        @pl.when((behind >= 0) & (behind < batches))
        def _():
            backward(behind)

        @pl.when(late & jnp.logical_not(last) & (behind == batches - 2))
        def _():
            turned_onward(0, start, True)

        @pl.when((done >= 0) & (done < batches))
        def _():
            finish(done)

        @pl.when(last & (ahead >= 1) & (ahead <= batches))
        def _():
            turned_onward(ahead - 1, start, True)

        return carry

    lax.fori_loop(0, 2 * sections - 1 + batches, step, 0)

    remote(sums_v.at[core], sums_v.at[core], sv_s, sv_r, sec, partner).start()

    @pl.when(last)
    def _():
        def send(m, carry):
            for i in range(2):
                send_dz(m, i)
            return carry

        lax.fori_loop(0, batches, send, 0)

    @pl.when(late & jnp.logical_not(last))
    def _():
        pass_on_from(1)

    def relay_and_add(m, carry):
        @pl.when(jnp.logical_not(first))
        def _():
            relay_turned(m)

        @pl.when(m >= 1)
        def _():
            add_gradients(m - 1)

        return carry

    lax.fori_loop(0, batches, relay_and_add, 0)

    def swap(r, d):
        other = (seat + d) % 4
        return remote(
            swap_out.at[r, pl.ds(pl.multiple_of(other * share, share), share), :], other_parts.at[4 - d - 1, r],
            sw_s.at[r, d - 1], sw_r.at[r, 4 - d - 1], sec, 4 * team + other,
        )

    def own_copy(r):
        return pltpu.make_async_copy(
            acc_v.at[r, pl.ds(pl.multiple_of(seat * share, share), share), :], own_part.at[r], dw_sem.at[r]
        )

    gather_taps(batches - 1)
    for r in range(3):
        part = acc_v[r] + kernel_row(batches - 1, r)
        acc_v[r] = part
        swap_out[r] = part.astype(BF16)
        for d in range(1, 4):
            swap(r, d).start()
        own_copy(r).start()

    for r in range(3):
        own_copy(r).wait()
        for d in range(1, 4):
            swap(r, d).wait_send()
            swap(r, d).wait_recv()

    @pl.when(decoder)
    def _():
        argument_sent(*mask_parts)

    @pl.when(sec < sections - 1)
    def _():
        for copy in affine_sends():
            copy.wait_send()

    def sums_copy():
        return remote(sums_v.at[core], sums_v.at[core], sv_s, sv_r, sec, partner)

    sums_copy().wait_recv()
    sums_copy().wait_send()
    for h in range(2):
        shift_sum[:, pl.ds(h * half, half)] = sums_v[h, pl.ds(0, 1), :]
        gain_sum[:, pl.ds(h * half, half)] = sums_v[h, pl.ds(1, 1), :]

    def drain(m, carry):
        for src, dst, sems in ((out_v, outs, (out_sem, po_s, po_r)), (gin_v, grads_in, (gin_sem, pg_s, pg_r))):
            here, there = result_copies(src, dst, *sems, m)
            here.wait()
            there.wait_send()
            remote(
                src.at[m, :, pl.ds(0, strip), :], dst.at[m, :, :, channels(1 - core)], sems[1].at[m], sems[2].at[m],
                sec, partner,
            ).wait_recv()

        turned_each(m, sent)
        turned_onward(m, sent, False)
        turned_relay(m).wait_send()
        for i in range(2):
            dz_each(m, i, sent)
        for i in range(2):
            pass_on(ub, ux_s, ux_r, m, i).wait_send()
            pass_on(dzb, dx_s, dx_r, m, i).wait_send()

        @pl.when(first)
        def _():
            argument_sent(*input_parts(images, m))

        @pl.when(last)
        def _():
            argument_sent(*input_parts(cotangent, m))
            stats_each(*seed_stats, m, sec, True, sent)

        @pl.when(sec < sections - 1)
        def _():
            stats_each(*down_stats, m, sec + 1, False, sent)
            block_sent(z_sends(m, sec + 1))

        stats_each(*same_stats, m, sec, True, sent)
        for i in range(2):
            each_edge(own_edges(m), i, sent)

        @pl.when(sec > 0)
        def _():
            stats_each(*back_stats, m, sec - 1, False, sent)
            block_sent(dy_sends(m, sec - 1))

        return carry

    lax.fori_loop(0, batches, drain, 0)


def settle(outs, grads_in, gain_sum, shift_sum, own, others, *refs):
    targets, stages, (own_v, others_v, whole, in_sem, out_sem) = refs[:5], refs[5:9], refs[9:]
    moves = []
    for src, dst, stage in zip((outs, grads_in, gain_sum, shift_sum), targets[:4], stages):
        if len(src.shape) == 2:
            moves.append((src, dst, stage))
        else:
            moves += [(src.at[i], dst.at[i], stage.at[i]) for i in range(src.shape[0])]
    count = len(moves)
    parts = [pltpu.make_async_copy(own, own_v, in_sem.at[count])]
    parts += [pltpu.make_async_copy(others.at[d], others_v.at[d], in_sem.at[count + 1 + d]) for d in range(3)]
    ins = [pltpu.make_async_copy(src, stage, in_sem.at[i]) for i, (src, dst, stage) in enumerate(moves)]
    outs = [pltpu.make_async_copy(stage, dst, out_sem.at[i]) for i, (src, dst, stage) in enumerate(moves)]
    rows = [pltpu.make_async_copy(whole.at[r], targets[4].at[r], out_sem.at[count + r]) for r in range(3)]
    for copy in parts + ins:
        copy.start()
    for copy in parts:
        copy.wait()
    seat = lax.axis_index("rows") % 4
    lanes = whole.shape[3] // 4
    for r in range(3):
        for d in range(4):
            at = pl.ds(pl.multiple_of(((seat + d) % 4) * lanes, lanes), lanes)
            for c in range(3):
                part = pl.ds(c * lanes, lanes)
                whole[r, c, :, at] = own_v[r, :, part] if d == 0 else others_v[d - 1, r, :, part].astype(F32)
        rows[r].start()
    for come, go in zip(ins, outs):
        come.wait()
        go.start()
    for copy in outs + rows:
        copy.wait()


def body(images, switches, conv_weights, gains, shifts, cotangent):
    sections = lax.axis_size("section")
    strips = lax.axis_size("rows")
    batches, pictures, strip_rows, cols, ch = images.shape
    strip = strip_rows * cols
    px = 2 * strip
    tall = px + 2 * cols
    anywhere = pl.BlockSpec(memory_space=pl.ANY)
    vmem = pl.BlockSpec(memory_space=pltpu.VMEM)
    dma = pltpu.SemaphoreType.DMA
    flops = 3 * 2 * 9 * ch * ch * batches * px
    share = ch // strips
    chips = strips // 2
    outs, grads_in, own, others, gain_sum, shift_sum = pl.pallas_call(
        functools.partial(kernel, sections, strips, cols),
        out_shape=(
            jax.ShapeDtypeStruct((batches, pictures, strip, ch), BF16),
            jax.ShapeDtypeStruct((batches, pictures, strip, ch), BF16),
            jax.ShapeDtypeStruct((3, share, 3 * ch // 4), F32),
            jax.ShapeDtypeStruct((3, 3, share, 3 * ch // 4), BF16),
            jax.ShapeDtypeStruct((1, ch), F32),
            jax.ShapeDtypeStruct((1, ch), F32),
        ),
        in_specs=[anywhere, anywhere, anywhere, vmem, vmem, vmem],
        out_specs=(anywhere,) * 4 + (vmem, vmem),
        scratch_shapes=[
            pltpu.VMEM((2, 9, ch // 2, ch // 2), BF16),
            pltpu.VMEM((2, 9, ch // 2, ch // 2), BF16),
            pltpu.VMEM((batches, 2, tall, ch // 2), BF16),
            pltpu.VMEM((batches, 2, strip, 128), BF16),
            pltpu.VMEM((batches, 2, tall, 128), BF16),
            pltpu.VMEM((1, ch), F32),
            pltpu.VMEM((1, ch), F32),
            pltpu.VMEM((batches, 2, tall, ch // 2), BF16),
            pltpu.VMEM((batches, chips, 4, ch // 2), F32),
            pltpu.VMEM((batches, 2, tall, ch // 2), BF16),
            pltpu.VMEM((batches, chips, 4, ch // 2), F32),
            pltpu.VMEM((batches, 2, 2, tall, ch // 2), BF16),
            pltpu.VMEM((batches, 2, px, ch // 2), F32),
            pltpu.VMEM((batches, 8, ch // 2), F32),
            pltpu.VMEM((batches, 8, ch // 2), F32),
            pltpu.VMEM((batches, 2, tall, ch // 2), BF16),
            pltpu.VMEM((batches, chips, 2, ch // 2), F32),
            pltpu.VMEM((batches, 2, 2, tall, ch // 2), BF16),
            pltpu.VMEM((batches, 2, px, ch // 2), BF16),
            pltpu.VMEM((3, 2 * px, ch // 2), F32),
            pltpu.VMEM((2, 2, ch // 2), F32),
            pltpu.VMEM((batches, 4, ch // 2), F32),
            pltpu.VMEM((batches, 2, ch // 2), F32),
            pltpu.VMEM((batches, 2, ch // 2), F32),
            pltpu.VMEM((batches, 2, px, ch // 2), BF16),
            pltpu.VMEM((batches, 2, px, ch // 2), BF16),
            pltpu.VMEM((batches, ch, px), BF16),
            pltpu.VMEM((batches, 2, strips // 2, 4 * share, px), BF16),
            pltpu.VMEM((batches, 2, px * strips // 2 + 2 * cols, ch // 4), BF16),
            pltpu.VMEM((2, px * strips // 2 + 2 * cols, 3 * ch // 4), BF16),
            pltpu.VMEM((3, 4 * share, 3 * ch // 4), F32),
            pltpu.VMEM((3, 4 * share, 3 * ch // 4), BF16),
            dma((2,)), dma((2,)),
            dma((batches,)),
            dma((batches,)), dma((batches,)),
            dma((batches, 2)), dma((batches, 2)),
            dma, dma,
            dma((2,)), dma((2,)),
            dma((2,)), dma((2,)),
            dma((batches, 2)), dma((batches, 2)),
            dma((batches, 2)), dma((batches, 2)),
            dma, dma,
            dma((batches, 3, 2)), dma((batches, 3, 2)),
            dma((batches, chips)), dma((batches, chips)),
            dma((batches, 3, 2)), dma((batches, 3, 2)),
            dma((batches, chips)), dma((batches, chips)),
            dma((batches, 3, 2)), dma((batches, 3, 2)),
            dma((batches, chips)), dma((batches, chips)),
            dma((batches, chips)),
            dma((batches,)), dma((batches,)), dma((batches,)),
            dma((batches,)), dma((batches,)), dma((batches,)),
            dma((batches, chips)), dma((batches, chips)), dma((batches, chips)),
            dma((batches,)), dma((batches,)),
            dma((batches, 2, chips)), dma((batches, 2, chips)),
            dma((3, 3)), dma((3, 3)),
            dma((3,)),
        ],
        compiler_params=pltpu.CompilerParams(
            collective_id=0, has_side_effects=True, vmem_limit_bytes=56 * 2**20
        ),
        cost_estimate=pl.CostEstimate(
            flops=flops, bytes_accessed=2 * 9 * ch * ch * 2, transcendentals=0
        ),
    )(
        images.reshape(batches, pictures, strip, ch),
        cotangent.reshape(batches, pictures, strip, ch),
        conv_weights.reshape(9, ch, ch),
        gains,
        shifts,
        switches.reshape(-1, switches.shape[-1]),
    )
    results = (outs, grads_in, gain_sum, shift_sum)
    whole = jax.ShapeDtypeStruct((3, 3, share, ch), F32)
    outs, grads_in, gain_sum, shift_sum, weight_grad = pl.pallas_call(
        settle,
        out_shape=tuple(jax.ShapeDtypeStruct(r.shape, r.dtype) for r in results) + (whole,),
        in_specs=[anywhere] * 6,
        out_specs=(anywhere,) * 5,
        scratch_shapes=[pltpu.VMEM(r.shape, r.dtype) for r in results]
        + [
            pltpu.VMEM(own.shape, F32),
            pltpu.VMEM(others.shape, BF16),
            pltpu.VMEM(whole.shape, F32),
            dma((2 * batches + 6,)),
            dma((2 * batches + 5,)),
        ],
        compiler_params=pltpu.CompilerParams(vmem_limit_bytes=60 * 2**20),
    )(*results, own, others)
    shape = (1, batches, pictures, strip_rows, cols, ch)
    return (outs.reshape(shape), grads_in.reshape(shape), weight_grad[None], gain_sum, shift_sum)


def solution(mesh):
    return jax.shard_map(
        body,
        mesh=mesh,
        in_specs=(
            P(None, None, "rows", None, None),
            P(None, None, "rows", None),
            P("section", None, None, None, None),
            P("section", None),
            P("section", None),
            P(None, None, "rows", None, None),
        ),
        out_specs=(
            P("section", None, None, "rows", None, None),
            P("section", None, None, "rows", None, None),
            P("section", None, None, "rows", None),
            P("section", None),
            P("section", None),
        ),
        check_vma=False,
    )
```
